32 devices in a mesh: dp: 8 (over z, y), seq: 4 (over x, core).
Axes of the slice: x: 2, y: 2, z: 4, core: 2. Of those that a mesh axis runs over, the one named last changes fastest.
Arguments:
- activations: bfloat16 [8, 1280, 512], P('dp', 'seq'), may hold values from -6 to 6
- encoder_attention_norm_gain: bfloat16 [512], P('seq'), may hold values from 0.5 to 1.5
- encoder_attention_norm_bias: bfloat16 [512], P('seq'), may hold values from -3 to 3
- encoder_query_key_value_weight: bfloat16 [512, 1536], P('seq'), may hold values from -0.25 to 0.25
- encoder_attention_output_weight: bfloat16 [512, 512], P('seq'), may hold values from -1 to 1
- encoder_attention_layer_scale: bfloat16 [512], P('seq'), may hold values from 0.5 to 1.5
- encoder_forward_norm_gain: bfloat16 [512], P('seq'), may hold values from 0.5 to 1.5
- encoder_forward_norm_bias: bfloat16 [512], P('seq'), may hold values from -3 to 3
- encoder_forward_input_weight: bfloat16 [512, 2048], P('seq'), may hold values from -0.25 to 0.25
- encoder_forward_output_weight: bfloat16 [2048, 512], P('seq'), may hold values from -0.125 to 0.125
- encoder_forward_layer_scale: bfloat16 [512], P('seq'), may hold values from 0.5 to 1.5
- strided_convolution_weight: bfloat16 [4, 512, 512], P(None, 'seq'), may hold values from -0.125 to 0.125
- strided_convolution_bias: bfloat16 [512], P('seq'), may hold values from -3 to 3
- quantizer_input_weight: bfloat16 [512, 256], P('seq'), may hold values from -0.25 to 0.25
- codebook: bfloat16 [8, 2048, 256], P(None, 'seq'), may hold values from -1.796875 to 1.796875
- quantizer_output_weight: bfloat16 [256, 512], P(None, 'seq'), may hold values from -0.375 to 0.375
- transposed_convolution_weight: bfloat16 [4, 512, 512], P(None, 'seq'), may hold values from -0.1875 to 0.1875
- transposed_convolution_bias: bfloat16 [512], P('seq'), may hold values from -3 to 3
- decoder_attention_norm_gain: bfloat16 [512], P('seq'), may hold values from 0.5 to 1.5
- decoder_attention_norm_bias: bfloat16 [512], P('seq'), may hold values from -3 to 3
- decoder_query_key_value_weight: bfloat16 [512, 1536], P('seq'), may hold values from -0.25 to 0.25
- decoder_attention_output_weight: bfloat16 [512, 512], P('seq'), may hold values from -1 to 1
- decoder_attention_layer_scale: bfloat16 [512], P('seq'), may hold values from 0.5 to 1.5
- decoder_forward_norm_gain: bfloat16 [512], P('seq'), may hold values from 0.5 to 1.5
- decoder_forward_norm_bias: bfloat16 [512], P('seq'), may hold values from -3 to 3
- decoder_forward_input_weight: bfloat16 [512, 2048], P('seq'), may hold values from -0.25 to 0.25
- decoder_forward_output_weight: bfloat16 [2048, 512], P('seq'), may hold values from -0.125 to 0.125
- decoder_forward_layer_scale: bfloat16 [512], P('seq'), may hold values from 0.5 to 1.5
- cotangent: bfloat16 [8, 1280, 512], P('dp', 'seq'), may hold values from -6 to 6
- frame_segment_index: int32 [8, 1280], P('dp'), may hold values from 0 to 1, as said below
- frame_code_index: int32 [8, 640, 8], P('dp', 'seq'), may hold values from 0 to 2047
- replace_code_mask: int32 [8, 2048], replicated, may hold values 0 or 1
- replacing_batch_position: int32 [8, 2048], replicated, may hold values from 0 to 5119
- code_usage_average: float32 [8, 2048], P(None, ('dp', 'seq')), may hold values from 0.25 to 2
- code_latent_sum_average: float32 [8, 2048, 256], P(None, ('dp', 'seq')), may hold values from -6 to 6
Outputs:
- output: bfloat16 [8, 1280, 512], P('dp', 'seq')
- activations_grad: bfloat16 [8, 1280, 512], P('dp', 'seq')
- grad_encoder_gain_one: float32 [512], P(('dp', 'seq'))
- grad_encoder_bias_one: float32 [512], P(('dp', 'seq'))
- grad_encoder_in_proj: float32 [512, 1536], P(('dp', 'seq'))
- grad_encoder_out_proj: float32 [512, 512], P(('dp', 'seq'))
- grad_encoder_scale_one: float32 [512], P(('dp', 'seq'))
- grad_encoder_gain_two: float32 [512], P(('dp', 'seq'))
- grad_encoder_bias_two: float32 [512], P(('dp', 'seq'))
- grad_encoder_linear_one: float32 [512, 2048], P(('dp', 'seq'))
- grad_encoder_linear_two: float32 [2048, 512], P(('dp', 'seq'))
- grad_encoder_scale_two: float32 [512], P(('dp', 'seq'))
- grad_downsample_weight: float32 [4, 512, 512], P(None, ('dp', 'seq'))
- grad_downsample_bias: float32 [512], P(('dp', 'seq'))
- grad_latent_in: float32 [512, 256], P(('dp', 'seq'))
- grad_latent_out: float32 [256, 512], P(None, ('dp', 'seq'))
- grad_upsample_weight: float32 [4, 512, 512], P(None, ('dp', 'seq'))
- grad_upsample_bias: float32 [512], P(('dp', 'seq'))
- grad_decoder_gain_one: float32 [512], P(('dp', 'seq'))
- grad_decoder_bias_one: float32 [512], P(('dp', 'seq'))
- grad_decoder_in_proj: float32 [512, 1536], P(('dp', 'seq'))
- grad_decoder_out_proj: float32 [512, 512], P(('dp', 'seq'))
- grad_decoder_scale_one: float32 [512], P(('dp', 'seq'))
- grad_decoder_gain_two: float32 [512], P(('dp', 'seq'))
- grad_decoder_bias_two: float32 [512], P(('dp', 'seq'))
- grad_decoder_linear_one: float32 [512, 2048], P(('dp', 'seq'))
- grad_decoder_linear_two: float32 [2048, 512], P(('dp', 'seq'))
- grad_decoder_scale_two: float32 [512], P(('dp', 'seq'))
- new_cluster_size: float32 [8, 2048], P(None, ('dp', 'seq'))
- new_embed_sum: float32 [8, 2048, 256], P(None, ('dp', 'seq'))
- new_codebook: float32 [8, 2048, 256], P(None, ('dp', 'seq'))
The draws below stay inside these ranges and needn't reach their ends.
Inputs may be any that keep to these rules, and one draw needn't show every extreme that they name: `frame_segment_index`: each row is segment 0 up to some frame after its first and segment 1 from that frame on; in each aligned block of 1 row one row turns to segment 1 within its first 160 frames. `replacing_batch_position`: a flat position row * 640 + frame in the whole batch.
All inputs are finite; a program needn't handle non-finite values.
Results may differ from the reference program's by a relative error of at most 0.024.
Values may be sent and summed in bfloat16 or wider, within the bound.
No kernel may reach another device: no remote copies, remote signals or barrier semaphores. Data moves between devices by JAX's collectives and lax.ppermute only.
A program may use at most 256 MiB of HBM per device.

```python
import math
from functools import partial
import jax
import jax.numpy as jnp
from jax import lax

MODEL_DIMENSION = 512
HEADS = 8
HEAD_DIM = 64
FF = 2048
CONTEXT = 250
LEVELS = 8
CODES = 2048
LATENT = 256
ROW_DEV = 1
FRAMES_DEV = 320
ROWS = 8
SEQ_LEN = 1280
CODEC_LEN = 640


def draw_frame_segment_index(key, part):
    key = jax.random.fold_in(key, 11)
    first_key, second_key, third_key = jax.random.split(key, 3)
    cut_frames = jax.random.randint(first_key, (ROWS,), 1, SEQ_LEN)
    early_cut = jax.random.randint(third_key, (ROWS,), 1, FRAMES_DEV // 2)
    picked = jax.random.randint(second_key, (ROWS // ROW_DEV,), 0, ROW_DEV)
    early_row = jnp.arange(ROWS) % ROW_DEV == jnp.repeat(picked, ROW_DEV)
    cut_frames = jnp.where(early_row, early_cut, cut_frames)
    return (jnp.arange(SEQ_LEN)[None, :] >= cut_frames[:, None]).astype(jnp.int32)


def place_ends(array, stream_key, low, top_value):
    index_at = [jax.random.randint(jax.random.fold_in(stream_key, axis), (), 0, length) for axis, length in enumerate(array.shape)]
    widest = array.shape.index(max(array.shape))
    neighbour = index_at[:widest] + [(index_at[widest] + 1) % array.shape[widest]] + index_at[widest + 1:]
    return array.at[tuple(index_at)].set(low).at[tuple(neighbour)].set(top_value)


def level_of(own_key, extent, pieces, smallest, largest):
    loudness, own = 1.0, jax.random.fold_in(own_key, 6)
    for axis_at, blocks in pieces:
        draws = jnp.exp(jax.random.uniform(jax.random.fold_in(own, axis_at), (blocks,), jnp.float32, smallest / len(pieces), largest / len(pieces)))
        loudness = loudness * jnp.repeat(draws, extent[axis_at] // blocks).reshape([-1 if axis == axis_at else 1 for axis in range(len(extent))])
    return loudness


def gaussian(stream_key, shape, scale, bound, cuts=(), kind=jnp.bfloat16):
    array = scale * jax.random.normal(stream_key, shape, jnp.float32)
    if cuts:
        array = array * level_of(stream_key, shape, cuts, -0.22, 0.18)
    return jnp.clip(array, -bound, bound).astype(kind)


def setup_inputs(seed: int = 0) -> dict:
    streams_of = jax.random.split(jax.random.key(seed), 36)
    activations = gaussian(streams_of[0], (ROWS, SEQ_LEN, MODEL_DIMENSION), 1.0, 6.0, ((0, 8), (1, 4)))
    encoder_attention_norm_gain = jnp.clip(1.0 + 0.1 * jax.random.normal(streams_of[1], (MODEL_DIMENSION,), jnp.float32), 0.5, 1.5).astype(jnp.bfloat16)
    encoder_attention_norm_bias = gaussian(streams_of[2], (MODEL_DIMENSION,), 0.5, 3.0, ((0, 4),))
    encoder_query_key_value_weight = gaussian(streams_of[3], (MODEL_DIMENSION, 3 * MODEL_DIMENSION), MODEL_DIMENSION ** -0.5, 0.25, ((0, 4),))
    encoder_attention_output_weight = gaussian(streams_of[4], (MODEL_DIMENSION, MODEL_DIMENSION), (MODEL_DIMENSION // 16) ** -0.5, 1.0, ((0, 4),))
    encoder_attention_layer_scale = jnp.clip(1.0 + 0.1 * jax.random.normal(streams_of[5], (MODEL_DIMENSION,), jnp.float32), 0.5, 1.5).astype(jnp.bfloat16)
    encoder_forward_norm_gain = jnp.clip(1.0 + 0.1 * jax.random.normal(streams_of[6], (MODEL_DIMENSION,), jnp.float32), 0.5, 1.5).astype(jnp.bfloat16)
    encoder_forward_norm_bias = gaussian(streams_of[7], (MODEL_DIMENSION,), 0.5, 3.0, ((0, 4),))
    encoder_forward_input_weight = gaussian(streams_of[8], (MODEL_DIMENSION, FF), MODEL_DIMENSION ** -0.5, 0.25, ((0, 4),))
    encoder_forward_output_weight = gaussian(streams_of[9], (FF, MODEL_DIMENSION), FF ** -0.5, 0.125, ((0, 4),))
    encoder_forward_layer_scale = jnp.clip(1.0 + 0.1 * jax.random.normal(streams_of[10], (MODEL_DIMENSION,), jnp.float32), 0.5, 1.5).astype(jnp.bfloat16)
    strided_convolution_weight = gaussian(streams_of[11], (4, MODEL_DIMENSION, MODEL_DIMENSION), (4 * MODEL_DIMENSION) ** -0.5, 0.125, ((1, 4),))
    strided_convolution_bias = gaussian(streams_of[12], (MODEL_DIMENSION,), 0.5, 3.0, ((0, 4),))
    quantizer_input_weight = gaussian(streams_of[13], (MODEL_DIMENSION, LATENT), MODEL_DIMENSION ** -0.5, 0.25, ((0, 4),))
    codebook = gaussian(streams_of[14], (LEVELS, CODES, LATENT), 0.3, 1.796875, ((1, 4),))
    quantizer_output_weight = gaussian(streams_of[15], (LATENT, MODEL_DIMENSION), LATENT ** -0.5, 0.375, ((1, 4),))
    transposed_convolution_weight = gaussian(streams_of[16], (4, MODEL_DIMENSION, MODEL_DIMENSION), (2 * MODEL_DIMENSION) ** -0.5, 0.1875, ((1, 4),))
    transposed_convolution_bias = gaussian(streams_of[17], (MODEL_DIMENSION,), 0.5, 3.0, ((0, 4),))
    decoder_attention_norm_gain = jnp.clip(1.0 + 0.1 * jax.random.normal(streams_of[18], (MODEL_DIMENSION,), jnp.float32), 0.5, 1.5).astype(jnp.bfloat16)
    decoder_attention_norm_bias = gaussian(streams_of[19], (MODEL_DIMENSION,), 0.5, 3.0, ((0, 4),))
    decoder_query_key_value_weight = gaussian(streams_of[20], (MODEL_DIMENSION, 3 * MODEL_DIMENSION), MODEL_DIMENSION ** -0.5, 0.25, ((0, 4),))
    decoder_attention_output_weight = gaussian(streams_of[21], (MODEL_DIMENSION, MODEL_DIMENSION), (MODEL_DIMENSION // 16) ** -0.5, 1.0, ((0, 4),))
    decoder_attention_layer_scale = jnp.clip(1.0 + 0.1 * jax.random.normal(streams_of[22], (MODEL_DIMENSION,), jnp.float32), 0.5, 1.5).astype(jnp.bfloat16)
    decoder_forward_norm_gain = jnp.clip(1.0 + 0.1 * jax.random.normal(streams_of[23], (MODEL_DIMENSION,), jnp.float32), 0.5, 1.5).astype(jnp.bfloat16)
    decoder_forward_norm_bias = gaussian(streams_of[24], (MODEL_DIMENSION,), 0.5, 3.0, ((0, 4),))
    decoder_forward_input_weight = gaussian(streams_of[25], (MODEL_DIMENSION, FF), MODEL_DIMENSION ** -0.5, 0.25, ((0, 4),))
    decoder_forward_output_weight = gaussian(streams_of[26], (FF, MODEL_DIMENSION), FF ** -0.5, 0.125, ((0, 4),))
    decoder_forward_layer_scale = jnp.clip(1.0 + 0.1 * jax.random.normal(streams_of[27], (MODEL_DIMENSION,), jnp.float32), 0.5, 1.5).astype(jnp.bfloat16)
    cotangent = gaussian(streams_of[28], (ROWS, SEQ_LEN, MODEL_DIMENSION), 1.0, 6.0, ((0, 8), (1, 4)))
    frame_segment_index = draw_frame_segment_index(jax.random.fold_in(streams_of[35], 71), 0)
    frame_code_index = place_ends(jax.random.randint(streams_of[30], (ROWS, CODEC_LEN, LEVELS), 0, CODES), jax.random.fold_in(streams_of[30], 1), 0, CODES - 1).astype(jnp.int32)
    replace_code_mask = place_ends((jax.random.randint(streams_of[31], (LEVELS, CODES), 0, 16) < 1).astype(jnp.int32), jax.random.fold_in(streams_of[31], 1), 0, 1)
    replacing_batch_position = place_ends(jax.random.randint(streams_of[32], (LEVELS, CODES), 0, ROWS * CODEC_LEN), jax.random.fold_in(streams_of[32], 1), 0, (ROWS * CODEC_LEN) - 1).astype(jnp.int32)
    code_usage_average = jnp.clip(jnp.exp(math.log(2.0) - 2.0794415 * jax.random.uniform(streams_of[33], (LEVELS, CODES), jnp.float32) ** level_of(streams_of[33], (LEVELS, CODES), ((1, 32),), -0.2, 0.2)), 0.25, 2.0)
    code_latent_sum_average = gaussian(streams_of[34], (LEVELS, CODES, LATENT), 1.0, 6.0, ((1, 32),), jnp.float32)
    return dict(activations=activations, encoder_attention_norm_gain=encoder_attention_norm_gain, encoder_attention_norm_bias=encoder_attention_norm_bias, encoder_query_key_value_weight=encoder_query_key_value_weight, encoder_attention_output_weight=encoder_attention_output_weight, encoder_attention_layer_scale=encoder_attention_layer_scale, encoder_forward_norm_gain=encoder_forward_norm_gain, encoder_forward_norm_bias=encoder_forward_norm_bias, encoder_forward_input_weight=encoder_forward_input_weight, encoder_forward_output_weight=encoder_forward_output_weight, encoder_forward_layer_scale=encoder_forward_layer_scale, strided_convolution_weight=strided_convolution_weight, strided_convolution_bias=strided_convolution_bias, quantizer_input_weight=quantizer_input_weight, codebook=codebook, quantizer_output_weight=quantizer_output_weight, transposed_convolution_weight=transposed_convolution_weight, transposed_convolution_bias=transposed_convolution_bias, decoder_attention_norm_gain=decoder_attention_norm_gain, decoder_attention_norm_bias=decoder_attention_norm_bias, decoder_query_key_value_weight=decoder_query_key_value_weight, decoder_attention_output_weight=decoder_attention_output_weight, decoder_attention_layer_scale=decoder_attention_layer_scale, decoder_forward_norm_gain=decoder_forward_norm_gain, decoder_forward_norm_bias=decoder_forward_norm_bias, decoder_forward_input_weight=decoder_forward_input_weight, decoder_forward_output_weight=decoder_forward_output_weight, decoder_forward_layer_scale=decoder_forward_layer_scale, cotangent=cotangent, frame_segment_index=frame_segment_index, frame_code_index=frame_code_index, replace_code_mask=replace_code_mask, replacing_batch_position=replacing_batch_position, code_usage_average=code_usage_average, code_latent_sum_average=code_latent_sum_average)


norm_eps = 1e-05
ema_decay = 0.9
highest = lax.Precision.HIGHEST

@jax.custom_vjp
def low(v):
    return lax.optimization_barrier(v.astype(jnp.bfloat16)).astype(jnp.float32)

@jax.custom_vjp
def low_back(v):
    return v

def low_keep(v):
    return (low(v), None)

def low_pass(kept, grad):
    return (grad,)

def back_keep(v):
    return (v, None)

def back_low(kept, grad):
    return (low(grad),)
low.defvjp(low_keep, low_pass)
low_back.defvjp(back_keep, back_low)

def product(equation, left, right):
    return jnp.einsum(equation, left, right, precision=highest)

def layer_norm(stream, norm_gain, offset):
    center = stream - lax.optimization_barrier(jnp.mean(stream, -1, keepdims=True))
    variance = lax.optimization_barrier(jnp.mean(center * center, -1, keepdims=True))
    return center * lax.rsqrt(variance + norm_eps) * norm_gain + offset

def rotate(tensor, cos_table, sin_table):
    half_dim = tensor.shape[-1] // 2
    first_half = tensor[..., :half_dim]
    second = tensor[..., half_dim:]
    return jnp.concatenate([first_half * cos_table - second * sin_table, first_half * sin_table + second * cos_table], -1)

def layer(params, stream, visible, cos_table, sin_table):
    gain_one, bias_one, in_proj, out_proj, scale_one, gain_two, bias_two, linear_one, linear_two, scale_two = params
    batch_rows = stream.shape[0]
    normed = low(layer_norm(stream, gain_one, bias_one))
    mixed_proj = low_back(product('rfd,de->rfe', normed, in_proj))
    head_parts = mixed_proj.reshape(batch_rows, SEQ_LEN, 3, HEADS, HEAD_DIM)
    queries = low(rotate(head_parts[:, :, 0], cos_table, sin_table))
    key_rows = low(rotate(head_parts[:, :, 1], cos_table, sin_table))
    values = low(head_parts[:, :, 2])
    scores = low_back(product('rqhd,rkhd->rhqk', queries, key_rows) * HEAD_DIM ** (-0.5))
    weights = low(jax.nn.softmax(jnp.where(visible, scores, -jnp.inf), axis=-1))
    attended = low(low_back(product('rhqk,rkhd->rqhd', weights, values))).reshape(batch_rows, SEQ_LEN, MODEL_DIMENSION)
    branch = low_back(product('rfd,de->rfe', attended, out_proj))
    stream = stream + scale_one * branch
    normed = low(layer_norm(stream, gain_two, bias_two))
    hidden = low_back(product('rfd,de->rfe', normed, linear_one))
    hidden = low(jax.nn.gelu(hidden, approximate=False))
    branch = low_back(product('rfe,ed->rfd', hidden, linear_two))
    return stream + scale_two * branch

def encode(params, stream, visible, cos_table, sin_table):
    stream = layer(params[:10], stream, visible, cos_table, sin_table)
    down_weight, down_bias, project_in = params[10:13]
    batch_rows = stream.shape[0]
    padded = jnp.concatenate([jnp.zeros((batch_rows, 2, MODEL_DIMENSION), stream.dtype), low(stream)], 1)
    frame_pairs = padded.reshape(batch_rows, CODEC_LEN + 1, 2 * MODEL_DIMENSION)
    windows = jnp.concatenate([frame_pairs[:, :-1], frame_pairs[:, 1:]], -1)
    reduced = low(low_back(product('rti,io->rto', windows, down_weight.reshape(4 * MODEL_DIMENSION, MODEL_DIMENSION)) + down_bias))
    return low_back(product('rto,ol->rtl', reduced, project_in))

def decode(params, quantized, visible, cos_table, sin_table):
    project_out, up_weight, up_bias = params[:3]
    batch_rows = quantized.shape[0]
    restored = low(low_back(product('rtl,ld->rtd', low(quantized), project_out)))
    shifted = jnp.concatenate([jnp.zeros((batch_rows, 1, MODEL_DIMENSION), restored.dtype), restored[:, :-1]], 1)
    joined = jnp.concatenate([restored, shifted], -1)
    matrix = up_weight.reshape(2, 2, MODEL_DIMENSION, MODEL_DIMENSION).transpose(0, 2, 1, 3).reshape(2 * MODEL_DIMENSION, 2 * MODEL_DIMENSION)
    stream = low_back(product('rti,io->rto', joined, matrix)).reshape(batch_rows, SEQ_LEN, MODEL_DIMENSION) + up_bias
    return layer(params[3:], stream, visible, cos_table, sin_table)

def reference(activations, encoder_attention_norm_gain, encoder_attention_norm_bias, encoder_query_key_value_weight, encoder_attention_output_weight, encoder_attention_layer_scale, encoder_forward_norm_gain, encoder_forward_norm_bias, encoder_forward_input_weight, encoder_forward_output_weight, encoder_forward_layer_scale, strided_convolution_weight, strided_convolution_bias, quantizer_input_weight, codebook, quantizer_output_weight, transposed_convolution_weight, transposed_convolution_bias, decoder_attention_norm_gain, decoder_attention_norm_bias, decoder_query_key_value_weight, decoder_attention_output_weight, decoder_attention_layer_scale, decoder_forward_norm_gain, decoder_forward_norm_bias, decoder_forward_input_weight, decoder_forward_output_weight, decoder_forward_layer_scale, cotangent, frame_segment_index, frame_code_index, replace_code_mask, replacing_batch_position, code_usage_average, code_latent_sum_average):
    encoder_parameters = (encoder_attention_norm_gain.astype(jnp.float32), encoder_attention_norm_bias.astype(jnp.float32), encoder_query_key_value_weight.astype(jnp.float32), encoder_attention_output_weight.astype(jnp.float32), encoder_attention_layer_scale.astype(jnp.float32), encoder_forward_norm_gain.astype(jnp.float32), encoder_forward_norm_bias.astype(jnp.float32), encoder_forward_input_weight.astype(jnp.float32), encoder_forward_output_weight.astype(jnp.float32), encoder_forward_layer_scale.astype(jnp.float32), strided_convolution_weight.astype(jnp.float32), strided_convolution_bias.astype(jnp.float32), quantizer_input_weight.astype(jnp.float32))
    decoder_params = (quantizer_output_weight.astype(jnp.float32), transposed_convolution_weight.astype(jnp.float32), transposed_convolution_bias.astype(jnp.float32), decoder_attention_norm_gain.astype(jnp.float32), decoder_attention_norm_bias.astype(jnp.float32), decoder_query_key_value_weight.astype(jnp.float32), decoder_attention_output_weight.astype(jnp.float32), decoder_attention_layer_scale.astype(jnp.float32), decoder_forward_norm_gain.astype(jnp.float32), decoder_forward_norm_bias.astype(jnp.float32), decoder_forward_input_weight.astype(jnp.float32), decoder_forward_output_weight.astype(jnp.float32), decoder_forward_layer_scale.astype(jnp.float32))
    book_values = codebook.astype(jnp.float32)
    half_dim = HEAD_DIM // 2
    frequency = jnp.power(10000.0, -jnp.arange(half_dim, dtype=jnp.float32) / half_dim)
    positions = jnp.arange(SEQ_LEN, dtype=jnp.int32)
    angles = positions.astype(jnp.float32)[:, None] * frequency[None, :]
    cos_table = jnp.cos(angles)[:, None, :]
    sin_table = jnp.sin(angles)[:, None, :]
    causal = (positions[None, :] <= positions[:, None]) & (positions[:, None] - positions[None, :] < CONTEXT)
    place_row = replacing_batch_position // CODEC_LEN
    place_local = place_row % ROW_DEV * CODEC_LEN + replacing_batch_position % CODEC_LEN
    segment_codes = partial(jax.ops.segment_sum, num_segments=CODES)
    groups = ROWS // ROW_DEV

    def group_step(running, group_data):
        grads_encoder, grads_decoder, code_sums, counts, chosen = running
        group_index, stream, upstream, segments, code_block = group_data
        visible = causal[None, None] & (segments[:, None, :, None] == segments[:, None, None, :])
        latent, encoder_back = jax.vjp(partial(encode, visible=visible, cos_table=cos_table, sin_table=sin_table), encoder_parameters, stream.astype(jnp.float32))
        flat_codes = code_block.reshape(ROW_DEV * CODEC_LEN, LEVELS)
        remaining = latent.reshape(ROW_DEV * CODEC_LEN, LATENT)
        quantized = jnp.zeros_like(remaining)
        residuals = []
        for level_index in range(LEVELS):
            residuals.append(remaining)
            code_rows = jnp.take(book_values[level_index], flat_codes[:, level_index], axis=0)
            remaining = remaining - code_rows
            quantized = quantized + code_rows
        residuals = jnp.stack(residuals)
        code_sums = code_sums + jax.vmap(segment_codes)(residuals, flat_codes.T)
        counts = counts + jax.vmap(segment_codes)(jnp.ones(flat_codes.T.shape, residuals.dtype), flat_codes.T)
        found_rows = jax.vmap(partial(jnp.take, axis=0))(residuals, place_local)
        chosen = chosen + jnp.where((place_row // ROW_DEV == group_index)[:, :, None], found_rows, 0.0)
        output, decoder_back = jax.vjp(partial(decode, visible=visible, cos_table=cos_table, sin_table=sin_table), decoder_params, quantized.reshape(ROW_DEV, CODEC_LEN, LATENT))
        grad_decoder, grad_quantized = decoder_back(upstream.astype(jnp.float32))
        grad_encoder, grad_stream = encoder_back(grad_quantized)
        grads_encoder = jax.tree.map(jnp.add, grads_encoder, grad_encoder)
        grads_decoder = jax.tree.map(jnp.add, grads_decoder, grad_decoder)
        return ((grads_encoder, grads_decoder, code_sums, counts, chosen), (output.astype(jnp.bfloat16), grad_stream.astype(jnp.bfloat16)))
    initial = (jax.tree.map(jnp.zeros_like, encoder_parameters), jax.tree.map(jnp.zeros_like, decoder_params), jnp.zeros((LEVELS, CODES, LATENT), jnp.float32), jnp.zeros((LEVELS, CODES), jnp.float32), jnp.zeros((LEVELS, CODES, LATENT), jnp.float32))
    inputs = (jnp.arange(groups, dtype=jnp.int32), activations.reshape(groups, ROW_DEV, SEQ_LEN, MODEL_DIMENSION), cotangent.reshape(groups, ROW_DEV, SEQ_LEN, MODEL_DIMENSION), frame_segment_index.reshape(groups, ROW_DEV, SEQ_LEN), frame_code_index.reshape(groups, ROW_DEV, CODEC_LEN, LEVELS))
    finals, blocks = lax.scan(group_step, initial, inputs)
    grads_encoder, grads_decoder, code_sums, counts, chosen = finals
    output = blocks[0].reshape(ROWS, SEQ_LEN, MODEL_DIMENSION)
    activations_grad = blocks[1].reshape(ROWS, SEQ_LEN, MODEL_DIMENSION)
    dead_flag = (replace_code_mask == 1)[:, :, None]
    new_cluster_size = ema_decay * code_usage_average + (1.0 - ema_decay) * counts
    new_embed_sum = jnp.where(dead_flag, chosen * new_cluster_size[:, :, None], ema_decay * code_latent_sum_average + (1.0 - ema_decay) * code_sums)
    new_codebook = new_embed_sum / new_cluster_size[:, :, None]
    return (output, activations_grad, grads_encoder[0], grads_encoder[1], grads_encoder[2], grads_encoder[3], grads_encoder[4], grads_encoder[5], grads_encoder[6], grads_encoder[7], grads_encoder[8], grads_encoder[9], grads_encoder[10], grads_encoder[11], grads_encoder[12], grads_decoder[0], grads_decoder[1], grads_decoder[2], grads_decoder[3], grads_decoder[4], grads_decoder[5], grads_decoder[6], grads_decoder[7], grads_decoder[8], grads_decoder[9], grads_decoder[10], grads_decoder[11], grads_decoder[12], new_cluster_size, new_embed_sum, new_codebook)
```

```python
import jax
import jax.numpy as jnp
from jax import lax
from jax.sharding import PartitionSpec as P

HEADS = 8
HEAD_DIM = 64
CONTEXT = 250


norm_eps = 1e-05
ema_decay = 0.9


def shifted_2(block, axis, distance):
    devices = range(lax.axis_size(axis))
    route = [(i - distance, i) for i in devices if i - distance in devices]
    return lax.ppermute(block, axis, route)


def exact_gelu(value):
    return jax.nn.gelu(value, approximate=False)


def norm_forward(stream, norm_gain, offset):
    center = stream - jnp.mean(stream, -1, keepdims=True)
    scaled = lax.rsqrt(jnp.mean(center * center, -1, keepdims=True) + norm_eps)
    normal = center * scaled
    return (normal * norm_gain + offset, normal, scaled)


def norm_backward(upstream, normal, scaled, norm_gain):
    inner = upstream * norm_gain
    result = scaled * (
        inner
        - jnp.mean(inner, -1, keepdims=True)
        - normal * jnp.mean(inner * normal, -1, keepdims=True)
    )
    return (result, jnp.sum(upstream * normal, (0, 1)), jnp.sum(upstream, (0, 1)))


def rotate(tensor, cos_table, sin_table, forward):
    half_dim = tensor.shape[-1] // 2
    first_half = tensor[..., :half_dim]
    second = tensor[..., half_dim:]
    if forward:
        return jnp.concatenate(
            [
                first_half * cos_table - second * sin_table,
                first_half * sin_table + second * cos_table,
            ],
            -1,
        )
    return jnp.concatenate(
        [first_half * cos_table + second * sin_table, second * cos_table - first_half * sin_table],
        -1,
    )


def layer_forward(stream, params, visible, cos_table, sin_table):
    (
        gain_one,
        bias_one,
        in_proj,
        out_proj,
        scale_one,
        gain_two,
        bias_two,
        linear_one,
        linear_two,
        scale_two,
    ) = params
    batch_rows, local_frames, model_width = stream.shape
    normed, normal_one, scaled_one = norm_forward(stream, gain_one, bias_one)
    normed_low = normed.astype(jnp.bfloat16)
    mixed_proj = jnp.einsum("rfd,de->rfe", normed_low, in_proj, preferred_element_type=jnp.float32)
    head_parts = mixed_proj.reshape(batch_rows, local_frames, 3, HEADS, HEAD_DIM)
    queries = rotate(head_parts[:, :, 0], cos_table, sin_table, True).astype(jnp.bfloat16)
    keys_low = (
        rotate(head_parts[:, :, 1], cos_table, sin_table, True)
        .astype(jnp.bfloat16)
        .reshape(batch_rows, local_frames, model_width)
    )
    values_low = (
        head_parts[:, :, 2].astype(jnp.bfloat16).reshape(batch_rows, local_frames, model_width)
    )
    earlier_keys, earlier_values = shifted_2((keys_low, values_low), "seq", 1)
    total_frames = 2 * local_frames
    all_keys = jnp.concatenate([earlier_keys, keys_low], 1).reshape(
        batch_rows, total_frames, HEADS, HEAD_DIM
    )
    all_values = jnp.concatenate([earlier_values, values_low], 1).reshape(
        batch_rows, total_frames, HEADS, HEAD_DIM
    )
    scores = jnp.einsum(
        "rqhd,rkhd->rhqk", queries, all_keys, preferred_element_type=jnp.float32
    ) * HEAD_DIM ** (-0.5)
    masked = jnp.where(visible, scores, -jnp.inf)
    largest = jnp.max(masked, -1, keepdims=True)
    exponent = jnp.exp(masked - largest)
    totals = jnp.sum(exponent, -1, keepdims=True)
    attention = exponent / totals
    log_total = largest + jnp.log(totals)
    attended = jnp.einsum(
        "rhqk,rkhd->rqhd",
        attention.astype(jnp.bfloat16),
        all_values,
        preferred_element_type=jnp.float32,
    )
    attended = attended.reshape(batch_rows, local_frames, model_width).astype(jnp.bfloat16)
    branch = jnp.einsum("rfd,de->rfe", attended, out_proj, preferred_element_type=jnp.float32)
    middle = stream + scale_one * branch
    normed_two, normal_two, scaled_two = norm_forward(middle, gain_two, bias_two)
    normed_two_low = normed_two.astype(jnp.bfloat16)
    hidden = jnp.einsum(
        "rfd,de->rfe", normed_two_low, linear_one, preferred_element_type=jnp.float32
    )
    active = exact_gelu(hidden).astype(jnp.bfloat16)
    second_branch = jnp.einsum(
        "rfe,ed->rfd", active, linear_two, preferred_element_type=jnp.float32
    )
    result = middle + scale_two * second_branch
    kept = (
        normal_one,
        scaled_one,
        normed_low,
        queries,
        all_keys,
        all_values,
        log_total,
        attended,
        branch,
        normal_two,
        scaled_two,
        normed_two_low,
        hidden,
        active,
        second_branch,
    )
    return (result, kept)


def layer_backward(upstream, kept, params, visible, cos_table, sin_table):
    (
        gain_one,
        bias_one,
        in_proj,
        out_proj,
        scale_one,
        gain_two,
        bias_two,
        linear_one,
        linear_two,
        scale_two,
    ) = params
    (
        normal_one,
        scaled_one,
        normed_low,
        queries,
        all_keys,
        all_values,
        log_total,
        attended,
        branch,
        normal_two,
        scaled_two,
        normed_two_low,
        hidden,
        active,
        second_branch,
    ) = kept
    batch_rows, local_frames, model_width = upstream.shape
    total_frames = all_keys.shape[1]
    head_scale = HEAD_DIM ** (-0.5)
    grad_scale_two = jnp.sum(upstream * second_branch, (0, 1))
    second_low = (upstream * scale_two).astype(jnp.bfloat16)
    grad_linear_two = jnp.einsum(
        "rfe,rfd->ed", active, second_low, preferred_element_type=jnp.float32
    )
    grad_active = jnp.einsum(
        "rfd,ed->rfe", second_low, linear_two, preferred_element_type=jnp.float32
    )
    grad_hidden = jax.vjp(exact_gelu, hidden)[1](grad_active)[0].astype(jnp.bfloat16)
    grad_linear_one = jnp.einsum(
        "rfd,rfe->de", normed_two_low, grad_hidden, preferred_element_type=jnp.float32
    )
    grad_normed_two = jnp.einsum(
        "rfe,de->rfd", grad_hidden, linear_one, preferred_element_type=jnp.float32
    )
    from_norm_two, grad_gain_two, grad_bias_two = norm_backward(
        grad_normed_two, normal_two, scaled_two, gain_two
    )
    grad_middle = upstream + from_norm_two
    grad_scale_one = jnp.sum(grad_middle * branch, (0, 1))
    branch_low = (grad_middle * scale_one).astype(jnp.bfloat16)
    grad_out_proj = jnp.einsum(
        "rfd,rfe->de", attended, branch_low, preferred_element_type=jnp.float32
    )
    grad_attended = jnp.einsum(
        "rfe,de->rfd", branch_low, out_proj, preferred_element_type=jnp.float32
    )
    grad_attended = grad_attended.astype(jnp.bfloat16).reshape(
        batch_rows, local_frames, HEADS, HEAD_DIM
    )
    scores = (
        jnp.einsum("rqhd,rkhd->rhqk", queries, all_keys, preferred_element_type=jnp.float32)
        * head_scale
    )
    attention = jnp.where(visible, jnp.exp(scores - log_total), 0.0)
    grad_attention = jnp.einsum(
        "rqhd,rkhd->rhqk", grad_attended, all_values, preferred_element_type=jnp.float32
    )
    grad_values_all = jnp.einsum(
        "rhqk,rqhd->rkhd",
        attention.astype(jnp.bfloat16),
        grad_attended,
        preferred_element_type=jnp.float32,
    )
    grad_scores = (
        attention * (grad_attention - jnp.sum(attention * grad_attention, -1, keepdims=True))
    ).astype(jnp.bfloat16)
    grad_queries = (
        jnp.einsum("rhqk,rkhd->rqhd", grad_scores, all_keys, preferred_element_type=jnp.float32)
        * head_scale
    )
    grad_keys_all = (
        jnp.einsum("rhqk,rqhd->rkhd", grad_scores, queries, preferred_element_type=jnp.float32)
        * head_scale
    )
    grad_keys_all = grad_keys_all.reshape(batch_rows, total_frames, model_width)
    grad_values_all = grad_values_all.reshape(batch_rows, total_frames, model_width)
    later_keys, later_values = (
        shifted_2(grad_keys_all[:, :local_frames].astype(jnp.bfloat16), "seq", -1).astype(
            jnp.float32
        ),
        shifted_2(grad_values_all[:, :local_frames].astype(jnp.bfloat16), "seq", -1).astype(
            jnp.float32
        ),
    )
    grad_keys = grad_keys_all[:, local_frames:] + later_keys
    grad_values = grad_values_all[:, local_frames:] + later_values
    grad_mixed = jnp.stack(
        [
            rotate(grad_queries, cos_table, sin_table, False),
            rotate(
                grad_keys.reshape(batch_rows, local_frames, HEADS, HEAD_DIM),
                cos_table,
                sin_table,
                False,
            ),
            grad_values.reshape(batch_rows, local_frames, HEADS, HEAD_DIM),
        ],
        2,
    )
    grad_mixed = grad_mixed.reshape(batch_rows, local_frames, 3 * model_width).astype(jnp.bfloat16)
    grad_in_proj = jnp.einsum(
        "rfd,rfe->de", normed_low, grad_mixed, preferred_element_type=jnp.float32
    )
    grad_normed = jnp.einsum("rfe,de->rfd", grad_mixed, in_proj, preferred_element_type=jnp.float32)
    from_norm_one, grad_gain_one, grad_bias_one = norm_backward(
        grad_normed, normal_one, scaled_one, gain_one
    )
    grads = (
        grad_gain_one,
        grad_bias_one,
        grad_in_proj,
        grad_out_proj,
        grad_scale_one,
        grad_gain_two,
        grad_bias_two,
        grad_linear_one,
        grad_linear_two,
        grad_scale_two,
    )
    return (grad_middle + from_norm_one, grads)


def local(
    activations,
    encoder_attention_norm_gain,
    encoder_attention_norm_bias,
    encoder_query_key_value_weight,
    encoder_attention_output_weight,
    encoder_attention_layer_scale,
    encoder_forward_norm_gain,
    encoder_forward_norm_bias,
    encoder_forward_input_weight,
    encoder_forward_output_weight,
    encoder_forward_layer_scale,
    strided_convolution_weight,
    strided_convolution_bias,
    quantizer_input_weight,
    codebook,
    quantizer_output_weight,
    transposed_convolution_weight,
    transposed_convolution_bias,
    decoder_attention_norm_gain,
    decoder_attention_norm_bias,
    decoder_query_key_value_weight,
    decoder_attention_output_weight,
    decoder_attention_layer_scale,
    decoder_forward_norm_gain,
    decoder_forward_norm_bias,
    decoder_forward_input_weight,
    decoder_forward_output_weight,
    decoder_forward_layer_scale,
    cotangent,
    frame_segment_index,
    frame_code_index,
    replace_code_mask,
    replacing_batch_position,
    code_usage_average,
    code_latent_sum_average,
):
    batch_rows, local_frames, model_width = activations.shape
    seq_index = lax.axis_index("seq")
    seq_count = lax.axis_size("seq")
    dp_index = lax.axis_index("dp")
    dp_count = lax.axis_size("dp")
    half_frames = local_frames // 2
    level_count = frame_code_index.shape[2]

    frame_total = batch_rows * half_frames
    own_codes = frame_code_index.reshape(frame_total, level_count)
    row_codes = lax.all_gather(own_codes, "seq", axis=0, tiled=False)
    book_share = codebook.shape[1]
    vectors = jnp.stack(
        [
            encoder_attention_norm_gain,
            encoder_attention_norm_bias,
            encoder_attention_layer_scale,
            encoder_forward_norm_gain,
            encoder_forward_norm_bias,
            encoder_forward_layer_scale,
            strided_convolution_bias,
            transposed_convolution_bias,
            decoder_attention_norm_gain,
            decoder_attention_norm_bias,
            decoder_attention_layer_scale,
            decoder_forward_norm_gain,
            decoder_forward_norm_bias,
            decoder_forward_layer_scale,
        ]
    )
    vectors = lax.all_gather(vectors, "seq", axis=1, tiled=True)

    def flat_taps(taps):
        return taps.transpose(1, 0, 2).reshape(taps.shape[1], -1)

    def gather_together(*shares):
        joined_share = jnp.concatenate(shares, 1)
        whole = lax.all_gather(joined_share, "seq", axis=0, tiled=True)
        edges = [0]
        for share in shares:
            edges.append(edges[-1] + share.shape[1])
        return [whole[:, low:high] for low, high in zip(edges[:-1], edges[1:])]

    latent_out_t, up_flat, dec_in = gather_together(
        quantizer_output_weight.T,
        flat_taps(transposed_convolution_weight),
        decoder_query_key_value_weight,
    )
    dec_out, dec_l1 = gather_together(
        decoder_attention_output_weight, decoder_forward_input_weight
    )
    dec_l2 = lax.all_gather(decoder_forward_output_weight, "seq", axis=0, tiled=True)
    enc_in, enc_out = gather_together(
        encoder_query_key_value_weight, encoder_attention_output_weight
    )
    enc_l1, down_flat, latent_in_full = gather_together(
        encoder_forward_input_weight,
        flat_taps(strided_convolution_weight),
        quantizer_input_weight,
    )
    enc_l2 = lax.all_gather(encoder_forward_output_weight, "seq", axis=0, tiled=True)
    encoder_parameters = (
        vectors[0], vectors[1], enc_in, enc_out, vectors[2],
        vectors[3], vectors[4], enc_l1, enc_l2, vectors[5],
    )
    decoder_params = (
        vectors[8], vectors[9], dec_in, dec_out, vectors[10],
        vectors[11], vectors[12], dec_l1, dec_l2, vectors[13],
    )
    down_bias_full = vectors[6]
    up_bias_full = vectors[7]

    local_code = row_codes - seq_index * book_share
    picks = (
        local_code[..., None] == jnp.arange(book_share, dtype=jnp.int32)
    ).astype(jnp.bfloat16)
    part_rows = jnp.einsum(
        "stlc,lcd->stld", picks, codebook, preferred_element_type=jnp.float32
    )
    part_quantized = jnp.sum(part_rows, 2)
    quantized = lax.psum_scatter(part_quantized, "seq", scatter_dimension=0, tiled=False)
    code_rows = lax.psum_scatter(
        part_rows.astype(jnp.bfloat16), "seq", scatter_dimension=0, tiled=False
    ).astype(jnp.float32)

    query_pos = seq_index * local_frames + jnp.arange(local_frames, dtype=jnp.int32)
    key_pos = (seq_index - 1) * local_frames + jnp.arange(2 * local_frames, dtype=jnp.int32)
    causal = (
        (key_pos[None, :] >= 0)
        & (key_pos[None, :] <= query_pos[:, None])
        & (query_pos[:, None] - key_pos[None, :] < CONTEXT)
    )
    own_segments = lax.dynamic_slice_in_dim(
        frame_segment_index, seq_index * local_frames, local_frames, 1
    )
    padded_segments = jnp.concatenate(
        [jnp.full((batch_rows, local_frames), -1, jnp.int32), frame_segment_index], 1
    )
    key_segments = lax.dynamic_slice_in_dim(
        padded_segments, seq_index * local_frames, 2 * local_frames, 1
    )
    visible = causal[None, None] & (
        own_segments[:, None, :, None] == key_segments[:, None, None, :]
    )
    half_dim = HEAD_DIM // 2
    frequency = jnp.power(10000.0, -jnp.arange(half_dim, dtype=jnp.float32) / half_dim)
    angles = query_pos.astype(jnp.float32)[:, None] * frequency[None, :]
    cos_table = jnp.cos(angles)[:, None, :]
    sin_table = jnp.sin(angles)[:, None, :]

    quantized_low = quantized.reshape(batch_rows, half_frames, -1).astype(jnp.bfloat16)
    restored = jnp.einsum(
        "rtl,dl->rtd", quantized_low, latent_out_t, preferred_element_type=jnp.float32
    ).astype(jnp.bfloat16)
    previous = shifted_2(restored[:, half_frames - 1 :], "seq", 1)
    shifted = jnp.concatenate([previous, restored[:, :-1]], 1)
    joined = jnp.concatenate([restored, shifted], -1)
    up_matrix = jnp.concatenate(
        [up_flat[:, : 2 * model_width], up_flat[:, 2 * model_width :]], 0
    )
    upsampled = (
        jnp.einsum("rti,io->rto", joined, up_matrix, preferred_element_type=jnp.float32).reshape(
            batch_rows, local_frames, model_width
        )
        + up_bias_full
    )
    decoded, kept_decoder = layer_forward(upsampled, decoder_params, visible, cos_table, sin_table)
    output = decoded.astype(jnp.bfloat16)

    grad_upsampled, grads_decoder = layer_backward(
        cotangent.astype(jnp.float32), kept_decoder, decoder_params, visible, cos_table, sin_table
    )

    def reduce_together(*parts):
        block = jnp.concatenate([part.astype(jnp.bfloat16) for part in parts], 1)
        width = block.shape[1]
        rows = block.shape[0] // (dp_count * seq_count)
        block = block.reshape(dp_count, seq_count, rows, width).transpose(1, 0, 2, 3)
        block = lax.psum_scatter(block, "seq", scatter_dimension=0, tiled=False)
        block = lax.psum_scatter(block, "dp", scatter_dimension=0, tiled=False)
        block = block.astype(jnp.float32)
        edges = [0]
        for part in parts:
            edges.append(edges[-1] + part.shape[1])
        return [block[:, low:high] for low, high in zip(edges[:-1], edges[1:])]

    shares = dp_count * seq_count

    def fold_rows(grad):
        rows = model_width // shares
        return (
            grad.reshape(shares, -1, rows, model_width)
            .transpose(0, 2, 1, 3)
            .reshape(model_width, -1)
        )

    def unfold_rows(block):
        rows = model_width // shares
        return block.reshape(rows, -1, model_width).transpose(1, 0, 2).reshape(-1, model_width)

    dec_l1_grad, dec_l2_grad = reduce_together(grads_decoder[7], fold_rows(grads_decoder[8]))
    dec_in_grad, dec_out_grad = reduce_together(grads_decoder[2], grads_decoder[3])

    grad_up_bias = jnp.sum(grad_upsampled, (0, 1))
    grad_up_low = grad_upsampled.reshape(batch_rows, half_frames, 2 * model_width).astype(
        jnp.bfloat16
    )
    grad_up_matrix = jnp.einsum(
        "rti,rto->io", joined, grad_up_low, preferred_element_type=jnp.float32
    )
    grad_up_flat = jnp.concatenate(
        [grad_up_matrix[:model_width], grad_up_matrix[model_width:]], 1
    )
    grad_joined = jnp.einsum(
        "rto,io->rti", grad_up_low, up_matrix, preferred_element_type=jnp.float32
    )
    from_next = shifted_2(grad_joined[:, :1, model_width:], "seq", -1)
    grad_restored = grad_joined[:, :, :model_width] + jnp.concatenate(
        [grad_joined[:, 1:, model_width:], from_next], 1
    )
    grad_restored_low = grad_restored.astype(jnp.bfloat16)
    grad_latent_out_t = jnp.einsum(
        "rtl,rtd->dl", quantized_low, grad_restored_low, preferred_element_type=jnp.float32
    )
    grad_latent_low = jnp.einsum(
        "rtd,dl->rtl", grad_restored_low, latent_out_t, preferred_element_type=jnp.float32
    ).astype(jnp.bfloat16)

    encoded, kept_encoder = layer_forward(
        activations.astype(jnp.float32), encoder_parameters, visible, cos_table, sin_table
    )
    encoded_low = encoded.astype(jnp.bfloat16)
    rim_frames = shifted_2(encoded_low[:, local_frames - 2 :], "seq", 1)
    padded = jnp.concatenate([rim_frames, encoded_low], 1)
    frame_pairs = padded.reshape(batch_rows, half_frames + 1, 2 * model_width)
    windows = jnp.concatenate([frame_pairs[:, :-1], frame_pairs[:, 1:]], -1)
    down_matrix = (
        down_flat.reshape(model_width, 4, model_width)
        .transpose(1, 0, 2)
        .reshape(4 * model_width, model_width)
    )
    reduced = (
        jnp.einsum("rti,io->rto", windows, down_matrix, preferred_element_type=jnp.float32)
        + down_bias_full
    )
    reduced_low = reduced.astype(jnp.bfloat16)
    latent = jnp.einsum(
        "rto,ol->rtl", reduced_low, latent_in_full, preferred_element_type=jnp.float32
    )

    remaining = latent.reshape(frame_total, latent.shape[2])
    residuals = []
    for level_index in range(level_count):
        residuals.append(remaining)
        remaining = remaining - code_rows[:, level_index]
    residuals = jnp.stack(residuals).astype(jnp.bfloat16)
    row_residuals = lax.all_gather(residuals, "seq", axis=1, tiled=True)
    code_total = replace_code_mask.shape[1]
    code_share = code_usage_average.shape[1]
    group_frames = frame_total * seq_count
    dead_flag = replace_code_mask == 1

    def seq_part(array):
        return lax.dynamic_index_in_dim(
            array.reshape(level_count, dp_count, seq_count, code_share), seq_index, 2, False
        ).reshape(level_count, dp_count * code_share)

    part_dead = seq_part(replace_code_mask) == 1
    part_place = seq_part(replacing_batch_position) - 0
    codec_total = half_frames * seq_count
    place_row = part_place // codec_total
    place_frame = part_place % codec_total
    place_local = (
        (place_frame // half_frames) * frame_total
        + (place_row % batch_rows) * half_frames
        + place_frame % half_frames
    )
    place_local = jnp.where(place_row // batch_rows == dp_index, place_local, -1)
    part_code = seq_part(
        jnp.broadcast_to(jnp.arange(code_total, dtype=jnp.int32), (level_count, code_total))
    )
    flat_row_codes = row_codes.reshape(group_frames, level_count).T
    used = part_code[:, :, None] == flat_row_codes[:, None, :]
    placed_at = place_local[:, :, None] == jnp.arange(group_frames, dtype=jnp.int32)
    counts = jnp.sum(used.astype(jnp.float32), 2)
    selects = jnp.where(part_dead[:, :, None], placed_at, used).astype(jnp.bfloat16)
    combined = jnp.einsum(
        "lct,ltd->lcd", selects, row_residuals, preferred_element_type=jnp.float32
    ).astype(jnp.bfloat16)
    latent_width = combined.shape[2]
    summed = lax.psum_scatter(
        combined.reshape(level_count, dp_count, code_share, latent_width).transpose(1, 0, 2, 3),
        "dp", scatter_dimension=0, tiled=False,
    ).astype(jnp.float32)
    counted = lax.psum_scatter(
        counts.reshape(level_count, dp_count, code_share).transpose(1, 0, 2),
        "dp", scatter_dimension=0, tiled=False,
    )
    owner_flag = lax.dynamic_slice_in_dim(
        dead_flag, lax.axis_index(("dp", "seq")) * code_share, code_share, 1
    )
    new_cluster_size = ema_decay * code_usage_average + (1.0 - ema_decay) * counted
    new_embed_sum = jnp.where(
        owner_flag[:, :, None],
        summed * new_cluster_size[:, :, None],
        ema_decay * code_latent_sum_average + (1.0 - ema_decay) * summed,
    )
    new_codebook = new_embed_sum / new_cluster_size[:, :, None]

    grad_latent_in = jnp.einsum(
        "rtd,rtl->dl", reduced_low, grad_latent_low, preferred_element_type=jnp.float32
    )
    grad_reduced_low = jnp.einsum(
        "rtl,dl->rtd", grad_latent_low, latent_in_full, preferred_element_type=jnp.float32
    ).astype(jnp.bfloat16)
    grad_down_bias = jnp.sum(grad_reduced_low.astype(jnp.float32), (0, 1))
    grad_down_weight = jnp.einsum(
        "rti,rto->io", windows, grad_reduced_low, preferred_element_type=jnp.float32
    )
    grad_down_flat = (
        grad_down_weight.reshape(4, model_width, model_width)
        .transpose(1, 0, 2)
        .reshape(model_width, 4 * model_width)
    )
    mid_grads = reduce_together(grad_up_flat, grad_latent_out_t, grad_down_flat, grad_latent_in)
    grad_windows = jnp.einsum(
        "rto,io->rti", grad_reduced_low, down_matrix, preferred_element_type=jnp.float32
    )
    zero_pair = jnp.zeros((batch_rows, 1, 2 * model_width), jnp.float32)
    grad_pairs = jnp.concatenate(
        [grad_windows[:, :, : 2 * model_width], zero_pair], 1
    ) + jnp.concatenate([zero_pair, grad_windows[:, :, 2 * model_width :]], 1)
    grad_padded = grad_pairs.reshape(batch_rows, local_frames + 2, model_width)
    from_right = shifted_2(grad_padded[:, :2], "seq", -1)
    grad_encoded = grad_padded[:, 2:] + jnp.concatenate(
        [jnp.zeros((batch_rows, local_frames - 2, model_width), jnp.float32), from_right], 1
    )
    grad_activations, grads_encoder = layer_backward(
        grad_encoded, kept_encoder, encoder_parameters, visible, cos_table, sin_table
    )
    activations_grad = grad_activations.astype(jnp.bfloat16)
    enc_l1_grad, enc_l2_grad = reduce_together(grads_encoder[7], fold_rows(grads_encoder[8]))
    vector_grads = jnp.stack(
        [grads_encoder[i] for i in (0, 1, 4, 5, 6, 9)]
        + [grad_down_bias, grad_up_bias]
        + [grads_decoder[i] for i in (0, 1, 4, 5, 6, 9)],
        1,
    )
    vector_grads = jnp.pad(vector_grads, ((0, 0), (0, 128 - vector_grads.shape[1])))
    enc_in_grad, enc_out_grad, vector_share = reduce_together(
        grads_encoder[2], grads_encoder[3], vector_grads
    )
    vec = vector_share.T
    taps = lambda block: block.reshape(-1, 4, model_width).transpose(1, 0, 2)
    return (
        output,
        activations_grad,
        vec[0],
        vec[1],
        enc_in_grad,
        enc_out_grad,
        vec[2],
        vec[3],
        vec[4],
        enc_l1_grad,
        unfold_rows(enc_l2_grad),
        vec[5],
        taps(mid_grads[2]),
        vec[6],
        mid_grads[3],
        mid_grads[1].T,
        taps(mid_grads[0]),
        vec[7],
        vec[8],
        vec[9],
        dec_in_grad,
        dec_out_grad,
        vec[10],
        vec[11],
        vec[12],
        dec_l1_grad,
        unfold_rows(dec_l2_grad),
        vec[13],
        new_cluster_size,
        new_embed_sum,
        new_codebook,
    )


def solution(mesh):
    placed = (
        P("dp", "seq", None),
        P("seq"),
        P("seq"),
        P("seq", None),
        P("seq", None),
        P("seq"),
        P("seq"),
        P("seq"),
        P("seq", None),
        P("seq", None),
        P("seq"),
        P(None, "seq", None),
        P("seq"),
        P("seq", None),
        P(None, "seq", None),
        P(None, "seq"),
        P(None, "seq", None),
        P("seq"),
        P("seq"),
        P("seq"),
        P("seq", None),
        P("seq", None),
        P("seq"),
        P("seq"),
        P("seq"),
        P("seq", None),
        P("seq", None),
        P("seq"),
        P("dp", "seq", None),
        P("dp", None),
        P("dp", "seq", None),
        P(),
        P(),
        P(None, ("dp", "seq")),
        P(None, ("dp", "seq"), None),
    )
    return jax.shard_map(
        local,
        mesh=mesh,
        in_specs=placed,
        out_specs=(
            P("dp", "seq", None),
            P("dp", "seq", None),
            P(("dp", "seq")),
            P(("dp", "seq")),
            P(("dp", "seq"), None),
            P(("dp", "seq"), None),
            P(("dp", "seq")),
            P(("dp", "seq")),
            P(("dp", "seq")),
            P(("dp", "seq"), None),
            P(("dp", "seq"), None),
            P(("dp", "seq")),
            P(None, ("dp", "seq"), None),
            P(("dp", "seq")),
            P(("dp", "seq"), None),
            P(None, ("dp", "seq")),
            P(None, ("dp", "seq"), None),
            P(("dp", "seq")),
            P(("dp", "seq")),
            P(("dp", "seq")),
            P(("dp", "seq"), None),
            P(("dp", "seq"), None),
            P(("dp", "seq")),
            P(("dp", "seq")),
            P(("dp", "seq")),
            P(("dp", "seq"), None),
            P(("dp", "seq"), None),
            P(("dp", "seq")),
            P(None, ("dp", "seq")),
            P(None, ("dp", "seq"), None),
            P(None, ("dp", "seq"), None),
        ),
        check_vma=False,
    )
```

```python
import jax
import jax.numpy as jnp
from jax import lax
from jax.sharding import PartitionSpec as P

HEADS = 8
HEAD_DIM = 64
CONTEXT = 250


DP = ("hi", "lo")
SEQ = ("x", "core")

norm_eps = 1e-05
ema_decay = 0.9


def shifted_2(block, axis, distance):
    devices = range(lax.axis_size(axis))
    route = [(i - distance, i) for i in devices if i - distance in devices]
    return lax.ppermute(block, axis, route)


def halve(block, dim, axis):
    mine = lax.axis_index(axis)
    sent = lax.dynamic_index_in_dim(block, 1 - mine, dim, False)
    kept = lax.dynamic_index_in_dim(block, mine, dim, False)
    got = lax.ppermute(sent, axis, [(0, 1), (1, 0)])
    return (kept.astype(jnp.float32) + got.astype(jnp.float32)).astype(block.dtype)


def sum_over_hi(block):
    parts = lax.all_to_all(block, "hi", 0, 0, tiled=True)
    return jnp.sum(parts.astype(jnp.float32), 0)


def exact_gelu(value):
    return jax.nn.gelu(value, approximate=False)


def norm_forward(stream, norm_gain, offset):
    center = stream - jnp.mean(stream, -1, keepdims=True)
    scaled = lax.rsqrt(jnp.mean(center * center, -1, keepdims=True) + norm_eps)
    normal = center * scaled
    return (normal * norm_gain + offset, normal, scaled)


def norm_backward(upstream, normal, scaled, norm_gain):
    inner = upstream * norm_gain
    result = scaled * (
        inner
        - jnp.mean(inner, -1, keepdims=True)
        - normal * jnp.mean(inner * normal, -1, keepdims=True)
    )
    return (result, jnp.sum(upstream * normal, (0, 1)), jnp.sum(upstream, (0, 1)))


def rotate(tensor, cos_table, sin_table, forward):
    half_dim = tensor.shape[-1] // 2
    first_half = tensor[..., :half_dim]
    second = tensor[..., half_dim:]
    if forward:
        return jnp.concatenate(
            [
                first_half * cos_table - second * sin_table,
                first_half * sin_table + second * cos_table,
            ],
            -1,
        )
    return jnp.concatenate(
        [first_half * cos_table + second * sin_table, second * cos_table - first_half * sin_table],
        -1,
    )


def layer_forward(stream, params, visible, cos_table, sin_table):
    (
        gain_one,
        bias_one,
        in_proj,
        out_proj,
        scale_one,
        gain_two,
        bias_two,
        linear_one,
        linear_two,
        scale_two,
    ) = params
    batch_rows, local_frames, model_width = stream.shape
    normed, normal_one, scaled_one = norm_forward(stream, gain_one, bias_one)
    normed_low = normed.astype(jnp.bfloat16)
    mixed_proj = jnp.einsum("rfd,de->rfe", normed_low, in_proj, preferred_element_type=jnp.float32)
    head_parts = mixed_proj.reshape(batch_rows, local_frames, 3, HEADS, HEAD_DIM)
    queries = rotate(head_parts[:, :, 0], cos_table, sin_table, True).astype(jnp.bfloat16)
    keys_low = (
        rotate(head_parts[:, :, 1], cos_table, sin_table, True)
        .astype(jnp.bfloat16)
        .reshape(batch_rows, local_frames, model_width)
    )
    values_low = (
        head_parts[:, :, 2].astype(jnp.bfloat16).reshape(batch_rows, local_frames, model_width)
    )
    earlier_keys, earlier_values = shifted_2((keys_low, values_low), SEQ, 1)
    total_frames = 2 * local_frames
    all_keys = jnp.concatenate([earlier_keys, keys_low], 1).reshape(
        batch_rows, total_frames, HEADS, HEAD_DIM
    )
    all_values = jnp.concatenate([earlier_values, values_low], 1).reshape(
        batch_rows, total_frames, HEADS, HEAD_DIM
    )
    scores = jnp.einsum(
        "rqhd,rkhd->rhqk", queries, all_keys, preferred_element_type=jnp.float32
    ) * HEAD_DIM ** (-0.5)
    masked = jnp.where(visible, scores, -jnp.inf)
    largest = jnp.max(masked, -1, keepdims=True)
    exponent = jnp.exp(masked - largest)
    totals = jnp.sum(exponent, -1, keepdims=True)
    attention = exponent / totals
    log_total = largest + jnp.log(totals)
    attended = jnp.einsum(
        "rhqk,rkhd->rqhd",
        attention.astype(jnp.bfloat16),
        all_values,
        preferred_element_type=jnp.float32,
    )
    attended = attended.reshape(batch_rows, local_frames, model_width).astype(jnp.bfloat16)
    branch = jnp.einsum("rfd,de->rfe", attended, out_proj, preferred_element_type=jnp.float32)
    middle = stream + scale_one * branch
    normed_two, normal_two, scaled_two = norm_forward(middle, gain_two, bias_two)
    normed_two_low = normed_two.astype(jnp.bfloat16)
    hidden = jnp.einsum(
        "rfd,de->rfe", normed_two_low, linear_one, preferred_element_type=jnp.float32
    )
    active = exact_gelu(hidden).astype(jnp.bfloat16)
    second_branch = jnp.einsum(
        "rfe,ed->rfd", active, linear_two, preferred_element_type=jnp.float32
    )
    result = middle + scale_two * second_branch
    kept = (
        normal_one,
        scaled_one,
        normed_low,
        queries,
        all_keys,
        all_values,
        log_total,
        attended,
        branch,
        normal_two,
        scaled_two,
        normed_two_low,
        hidden,
        active,
        second_branch,
    )
    return (result, kept)


def layer_backward(upstream, kept, params, visible, cos_table, sin_table):
    (
        gain_one,
        bias_one,
        in_proj,
        out_proj,
        scale_one,
        gain_two,
        bias_two,
        linear_one,
        linear_two,
        scale_two,
    ) = params
    (
        normal_one,
        scaled_one,
        normed_low,
        queries,
        all_keys,
        all_values,
        log_total,
        attended,
        branch,
        normal_two,
        scaled_two,
        normed_two_low,
        hidden,
        active,
        second_branch,
    ) = kept
    batch_rows, local_frames, model_width = upstream.shape
    total_frames = all_keys.shape[1]
    head_scale = HEAD_DIM ** (-0.5)
    grad_scale_two = jnp.sum(upstream * second_branch, (0, 1))
    second_low = (upstream * scale_two).astype(jnp.bfloat16)
    grad_linear_two = jnp.einsum(
        "rfe,rfd->ed", active, second_low, preferred_element_type=jnp.float32
    )
    grad_active = jnp.einsum(
        "rfd,ed->rfe", second_low, linear_two, preferred_element_type=jnp.float32
    )
    grad_hidden = jax.vjp(exact_gelu, hidden)[1](grad_active)[0].astype(jnp.bfloat16)
    grad_linear_one = jnp.einsum(
        "rfd,rfe->de", normed_two_low, grad_hidden, preferred_element_type=jnp.float32
    )
    grad_normed_two = jnp.einsum(
        "rfe,de->rfd", grad_hidden, linear_one, preferred_element_type=jnp.float32
    )
    from_norm_two, grad_gain_two, grad_bias_two = norm_backward(
        grad_normed_two, normal_two, scaled_two, gain_two
    )
    grad_middle = upstream + from_norm_two
    grad_scale_one = jnp.sum(grad_middle * branch, (0, 1))
    branch_low = (grad_middle * scale_one).astype(jnp.bfloat16)
    grad_out_proj = jnp.einsum(
        "rfd,rfe->de", attended, branch_low, preferred_element_type=jnp.float32
    )
    grad_attended = jnp.einsum(
        "rfe,de->rfd", branch_low, out_proj, preferred_element_type=jnp.float32
    )
    grad_attended = grad_attended.astype(jnp.bfloat16).reshape(
        batch_rows, local_frames, HEADS, HEAD_DIM
    )
    scores = (
        jnp.einsum("rqhd,rkhd->rhqk", queries, all_keys, preferred_element_type=jnp.float32)
        * head_scale
    )
    attention = jnp.where(visible, jnp.exp(scores - log_total), 0.0)
    grad_attention = jnp.einsum(
        "rqhd,rkhd->rhqk", grad_attended, all_values, preferred_element_type=jnp.float32
    )
    grad_values_all = jnp.einsum(
        "rhqk,rqhd->rkhd",
        attention.astype(jnp.bfloat16),
        grad_attended,
        preferred_element_type=jnp.float32,
    )
    grad_scores = (
        attention * (grad_attention - jnp.sum(attention * grad_attention, -1, keepdims=True))
    ).astype(jnp.bfloat16)
    grad_queries = (
        jnp.einsum("rhqk,rkhd->rqhd", grad_scores, all_keys, preferred_element_type=jnp.float32)
        * head_scale
    )
    grad_keys_all = (
        jnp.einsum("rhqk,rqhd->rkhd", grad_scores, queries, preferred_element_type=jnp.float32)
        * head_scale
    )
    grad_keys_all = grad_keys_all.reshape(batch_rows, total_frames, model_width)
    grad_values_all = grad_values_all.reshape(batch_rows, total_frames, model_width)
    later_keys, later_values = (
        shifted_2(grad_keys_all[:, :local_frames].astype(jnp.bfloat16), SEQ, -1).astype(
            jnp.float32
        ),
        shifted_2(grad_values_all[:, :local_frames].astype(jnp.bfloat16), SEQ, -1).astype(
            jnp.float32
        ),
    )
    grad_keys = grad_keys_all[:, local_frames:] + later_keys
    grad_values = grad_values_all[:, local_frames:] + later_values
    grad_mixed = jnp.stack(
        [
            rotate(grad_queries, cos_table, sin_table, False),
            rotate(
                grad_keys.reshape(batch_rows, local_frames, HEADS, HEAD_DIM),
                cos_table,
                sin_table,
                False,
            ),
            grad_values.reshape(batch_rows, local_frames, HEADS, HEAD_DIM),
        ],
        2,
    )
    grad_mixed = grad_mixed.reshape(batch_rows, local_frames, 3 * model_width).astype(jnp.bfloat16)
    grad_in_proj = jnp.einsum(
        "rfd,rfe->de", normed_low, grad_mixed, preferred_element_type=jnp.float32
    )
    grad_normed = jnp.einsum("rfe,de->rfd", grad_mixed, in_proj, preferred_element_type=jnp.float32)
    from_norm_one, grad_gain_one, grad_bias_one = norm_backward(
        grad_normed, normal_one, scaled_one, gain_one
    )
    grads = (
        grad_gain_one,
        grad_bias_one,
        grad_in_proj,
        grad_out_proj,
        grad_scale_one,
        grad_gain_two,
        grad_bias_two,
        grad_linear_one,
        grad_linear_two,
        grad_scale_two,
    )
    return (grad_middle + from_norm_one, grads)


def local(
    activations,
    encoder_attention_norm_gain,
    encoder_attention_norm_bias,
    encoder_query_key_value_weight,
    encoder_attention_output_weight,
    encoder_attention_layer_scale,
    encoder_forward_norm_gain,
    encoder_forward_norm_bias,
    encoder_forward_input_weight,
    encoder_forward_output_weight,
    encoder_forward_layer_scale,
    strided_convolution_weight,
    strided_convolution_bias,
    quantizer_input_weight,
    codebook,
    quantizer_output_weight,
    transposed_convolution_weight,
    transposed_convolution_bias,
    decoder_attention_norm_gain,
    decoder_attention_norm_bias,
    decoder_query_key_value_weight,
    decoder_attention_output_weight,
    decoder_attention_layer_scale,
    decoder_forward_norm_gain,
    decoder_forward_norm_bias,
    decoder_forward_input_weight,
    decoder_forward_output_weight,
    decoder_forward_layer_scale,
    cotangent,
    frame_segment_index,
    frame_code_index,
    replace_code_mask,
    replacing_batch_position,
    code_usage_average,
    code_latent_sum_average,
):
    batch_rows, local_frames, model_width = activations.shape
    seq_index = lax.axis_index(SEQ)
    seq_count = lax.axis_size(SEQ)
    dp_index = lax.axis_index(DP)
    dp_count = lax.axis_size(DP)
    half_frames = local_frames // 2
    level_count = frame_code_index.shape[2]

    frame_total = batch_rows * half_frames
    own_codes = frame_code_index.reshape(frame_total, level_count)
    row_codes = lax.all_gather(own_codes, SEQ, axis=0, tiled=False)
    book_share = codebook.shape[1]
    vectors = jnp.stack(
        [
            encoder_attention_norm_gain,
            encoder_attention_norm_bias,
            encoder_attention_layer_scale,
            encoder_forward_norm_gain,
            encoder_forward_norm_bias,
            encoder_forward_layer_scale,
            strided_convolution_bias,
            transposed_convolution_bias,
            decoder_attention_norm_gain,
            decoder_attention_norm_bias,
            decoder_attention_layer_scale,
            decoder_forward_norm_gain,
            decoder_forward_norm_bias,
            decoder_forward_layer_scale,
        ]
    )
    vectors = lax.all_gather(vectors, SEQ, axis=1, tiled=True)

    def flat_taps(taps):
        return taps.transpose(1, 0, 2).reshape(taps.shape[1], -1)

    def gather_together(*shares):
        joined_share = jnp.concatenate(shares, 1)
        whole = lax.all_gather(joined_share, SEQ, axis=0, tiled=True)
        edges = [0]
        for share in shares:
            edges.append(edges[-1] + share.shape[1])
        return [whole[:, low:high] for low, high in zip(edges[:-1], edges[1:])]

    latent_out_t, up_flat, dec_in = gather_together(
        quantizer_output_weight.T,
        flat_taps(transposed_convolution_weight),
        decoder_query_key_value_weight,
    )
    dec_out, dec_l1 = gather_together(
        decoder_attention_output_weight, decoder_forward_input_weight
    )
    dec_l2 = lax.all_gather(decoder_forward_output_weight, SEQ, axis=0, tiled=True)
    enc_in, enc_out = gather_together(
        encoder_query_key_value_weight, encoder_attention_output_weight
    )
    enc_l1, down_flat, latent_in_full = gather_together(
        encoder_forward_input_weight,
        flat_taps(strided_convolution_weight),
        quantizer_input_weight,
    )
    enc_l2 = lax.all_gather(encoder_forward_output_weight, SEQ, axis=0, tiled=True)
    encoder_parameters = (
        vectors[0], vectors[1], enc_in, enc_out, vectors[2],
        vectors[3], vectors[4], enc_l1, enc_l2, vectors[5],
    )
    decoder_params = (
        vectors[8], vectors[9], dec_in, dec_out, vectors[10],
        vectors[11], vectors[12], dec_l1, dec_l2, vectors[13],
    )
    down_bias_full = vectors[6]
    up_bias_full = vectors[7]

    local_code = row_codes - seq_index * book_share
    picks = (
        local_code[..., None] == jnp.arange(book_share, dtype=jnp.int32)
    ).astype(jnp.bfloat16)
    part_rows = jnp.einsum(
        "stlc,lcd->stld", picks, codebook, preferred_element_type=jnp.float32
    )
    part_quantized = jnp.sum(part_rows, 2).reshape(2, 2, frame_total, -1)
    quantized = halve(halve(part_quantized, 1, "core"), 0, "x")
    part_rows = part_rows.astype(jnp.bfloat16).reshape(2, 2, frame_total * level_count, -1)
    code_rows = (
        halve(halve(part_rows, 1, "core"), 0, "x")
        .reshape(frame_total, level_count, -1)
        .astype(jnp.float32)
    )

    query_pos = seq_index * local_frames + jnp.arange(local_frames, dtype=jnp.int32)
    key_pos = (seq_index - 1) * local_frames + jnp.arange(2 * local_frames, dtype=jnp.int32)
    causal = (
        (key_pos[None, :] >= 0)
        & (key_pos[None, :] <= query_pos[:, None])
        & (query_pos[:, None] - key_pos[None, :] < CONTEXT)
    )
    own_segments = lax.dynamic_slice_in_dim(
        frame_segment_index, seq_index * local_frames, local_frames, 1
    )
    padded_segments = jnp.concatenate(
        [jnp.full((batch_rows, local_frames), -1, jnp.int32), frame_segment_index], 1
    )
    key_segments = lax.dynamic_slice_in_dim(
        padded_segments, seq_index * local_frames, 2 * local_frames, 1
    )
    visible = causal[None, None] & (
        own_segments[:, None, :, None] == key_segments[:, None, None, :]
    )
    half_dim = HEAD_DIM // 2
    frequency = jnp.power(10000.0, -jnp.arange(half_dim, dtype=jnp.float32) / half_dim)
    angles = query_pos.astype(jnp.float32)[:, None] * frequency[None, :]
    cos_table = jnp.cos(angles)[:, None, :]
    sin_table = jnp.sin(angles)[:, None, :]

    quantized_low = quantized.reshape(batch_rows, half_frames, -1).astype(jnp.bfloat16)
    restored = jnp.einsum(
        "rtl,dl->rtd", quantized_low, latent_out_t, preferred_element_type=jnp.float32
    ).astype(jnp.bfloat16)
    previous = shifted_2(restored[:, half_frames - 1 :], SEQ, 1)
    shifted = jnp.concatenate([previous, restored[:, :-1]], 1)
    joined = jnp.concatenate([restored, shifted], -1)
    up_matrix = jnp.concatenate(
        [up_flat[:, : 2 * model_width], up_flat[:, 2 * model_width :]], 0
    )
    upsampled = (
        jnp.einsum("rti,io->rto", joined, up_matrix, preferred_element_type=jnp.float32).reshape(
            batch_rows, local_frames, model_width
        )
        + up_bias_full
    )
    decoded, kept_decoder = layer_forward(upsampled, decoder_params, visible, cos_table, sin_table)
    output = decoded.astype(jnp.bfloat16)

    grad_upsampled, grads_decoder = layer_backward(
        cotangent.astype(jnp.float32), kept_decoder, decoder_params, visible, cos_table, sin_table
    )

    def reduce_together(*parts):
        block = jnp.concatenate([part.astype(jnp.bfloat16) for part in parts], 1)
        width = block.shape[1]
        rows = block.shape[0] // (dp_count * seq_count)
        block = block.reshape(dp_count // 2, 2, 2, 2, rows, width)
        block = halve(halve(halve(block, 3, "core"), 2, "x"), 1, "lo")
        block = sum_over_hi(block)
        edges = [0]
        for part in parts:
            edges.append(edges[-1] + part.shape[1])
        return [block[:, low:high] for low, high in zip(edges[:-1], edges[1:])]

    shares = dp_count * seq_count

    def fold_rows(grad):
        rows = model_width // shares
        return (
            grad.reshape(shares, -1, rows, model_width)
            .transpose(0, 2, 1, 3)
            .reshape(model_width, -1)
        )

    def unfold_rows(block):
        rows = model_width // shares
        return block.reshape(rows, -1, model_width).transpose(1, 0, 2).reshape(-1, model_width)

    dec_l1_grad, dec_l2_grad = reduce_together(grads_decoder[7], fold_rows(grads_decoder[8]))

    grad_up_bias = jnp.sum(grad_upsampled, (0, 1))
    grad_up_low = grad_upsampled.reshape(batch_rows, half_frames, 2 * model_width).astype(
        jnp.bfloat16
    )
    grad_up_matrix = jnp.einsum(
        "rti,rto->io", joined, grad_up_low, preferred_element_type=jnp.float32
    )
    grad_up_flat = jnp.concatenate(
        [grad_up_matrix[:model_width], grad_up_matrix[model_width:]], 1
    )
    grad_joined = jnp.einsum(
        "rto,io->rti", grad_up_low, up_matrix, preferred_element_type=jnp.float32
    )
    from_next = shifted_2(grad_joined[:, :1, model_width:], SEQ, -1)
    grad_restored = grad_joined[:, :, :model_width] + jnp.concatenate(
        [grad_joined[:, 1:, model_width:], from_next], 1
    )
    grad_restored_low = grad_restored.astype(jnp.bfloat16)
    grad_latent_out_t = jnp.einsum(
        "rtl,rtd->dl", quantized_low, grad_restored_low, preferred_element_type=jnp.float32
    )
    grad_latent_low = jnp.einsum(
        "rtd,dl->rtl", grad_restored_low, latent_out_t, preferred_element_type=jnp.float32
    ).astype(jnp.bfloat16)

    dec_in_grad, dec_out_grad, up_grad, latent_out_grad = reduce_together(
        grads_decoder[2], grads_decoder[3], grad_up_flat, grad_latent_out_t
    )

    encoded, kept_encoder = layer_forward(
        activations.astype(jnp.float32), encoder_parameters, visible, cos_table, sin_table
    )
    encoded_low = encoded.astype(jnp.bfloat16)
    rim_frames = shifted_2(encoded_low[:, local_frames - 2 :], SEQ, 1)
    padded = jnp.concatenate([rim_frames, encoded_low], 1)
    frame_pairs = padded.reshape(batch_rows, half_frames + 1, 2 * model_width)
    windows = jnp.concatenate([frame_pairs[:, :-1], frame_pairs[:, 1:]], -1)
    down_matrix = (
        down_flat.reshape(model_width, 4, model_width)
        .transpose(1, 0, 2)
        .reshape(4 * model_width, model_width)
    )
    reduced = (
        jnp.einsum("rti,io->rto", windows, down_matrix, preferred_element_type=jnp.float32)
        + down_bias_full
    )
    reduced_low = reduced.astype(jnp.bfloat16)
    latent = jnp.einsum(
        "rto,ol->rtl", reduced_low, latent_in_full, preferred_element_type=jnp.float32
    )

    remaining = latent.reshape(frame_total, latent.shape[2])
    residuals = []
    for level_index in range(level_count):
        residuals.append(remaining)
        remaining = remaining - code_rows[:, level_index]
    residuals = jnp.stack(residuals).astype(jnp.bfloat16)
    row_residuals = lax.all_gather(residuals, SEQ, axis=1, tiled=True)
    code_total = replace_code_mask.shape[1]
    code_share = code_usage_average.shape[1]
    group_frames = frame_total * seq_count
    dead_flag = replace_code_mask == 1

    def seq_part(array):
        return lax.dynamic_index_in_dim(
            array.reshape(level_count, dp_count, seq_count, code_share), seq_index, 2, False
        ).reshape(level_count, dp_count * code_share)

    part_dead = seq_part(replace_code_mask) == 1
    part_place = seq_part(replacing_batch_position) - 0
    codec_total = half_frames * seq_count
    place_row = part_place // codec_total
    place_frame = part_place % codec_total
    place_local = (
        (place_frame // half_frames) * frame_total
        + (place_row % batch_rows) * half_frames
        + place_frame % half_frames
    )
    place_local = jnp.where(place_row // batch_rows == dp_index, place_local, -1)
    part_code = seq_part(
        jnp.broadcast_to(jnp.arange(code_total, dtype=jnp.int32), (level_count, code_total))
    )
    flat_row_codes = row_codes.reshape(group_frames, level_count).T
    used = part_code[:, :, None] == flat_row_codes[:, None, :]
    placed_at = place_local[:, :, None] == jnp.arange(group_frames, dtype=jnp.int32)
    counts = jnp.sum(used.astype(jnp.float32), 2)
    selects = jnp.where(part_dead[:, :, None], placed_at, used).astype(jnp.bfloat16)
    combined = jnp.einsum(
        "lct,ltd->lcd", selects, row_residuals, preferred_element_type=jnp.float32
    ).astype(jnp.bfloat16)
    latent_width = combined.shape[2]
    high_digit = jnp.floor(counts * (1.0 / 128.0))
    digits = jnp.stack([high_digit, counts - 128.0 * high_digit])
    digits = digits.reshape(2, level_count, dp_count, code_share).transpose(2, 0, 1, 3)
    digits = digits.reshape(dp_count, -1).astype(jnp.bfloat16)
    digit_total = digits.shape[1]
    digits = jnp.pad(digits, ((0, 0), (0, -digit_total % (16 * latent_width))))
    digits = digits.reshape(dp_count, -1, latent_width)
    combined = (
        combined.reshape(level_count, dp_count, code_share, latent_width)
        .transpose(1, 0, 2, 3)
        .reshape(dp_count, -1, latent_width)
    )
    sum_rows = combined.shape[1]
    combined = jnp.concatenate([combined, digits], 1)
    combined = combined.reshape(dp_count // 2, 2, -1, latent_width)
    combined = sum_over_hi(halve(combined, 1, "lo"))
    summed = combined[:sum_rows].reshape(level_count, code_share, latent_width)
    digits = combined[sum_rows:].reshape(-1)[:digit_total].reshape(2, level_count, code_share)
    counted = 128.0 * digits[0] + digits[1]
    owner_flag = lax.dynamic_slice_in_dim(
        dead_flag, lax.axis_index(DP + SEQ) * code_share, code_share, 1
    )
    new_cluster_size = ema_decay * code_usage_average + (1.0 - ema_decay) * counted
    new_embed_sum = jnp.where(
        owner_flag[:, :, None],
        summed * new_cluster_size[:, :, None],
        ema_decay * code_latent_sum_average + (1.0 - ema_decay) * summed,
    )
    new_codebook = new_embed_sum / new_cluster_size[:, :, None]

    grad_latent_in = jnp.einsum(
        "rtd,rtl->dl", reduced_low, grad_latent_low, preferred_element_type=jnp.float32
    )
    grad_reduced_low = jnp.einsum(
        "rtl,dl->rtd", grad_latent_low, latent_in_full, preferred_element_type=jnp.float32
    ).astype(jnp.bfloat16)
    grad_down_bias = jnp.sum(grad_reduced_low.astype(jnp.float32), (0, 1))
    grad_down_weight = jnp.einsum(
        "rti,rto->io", windows, grad_reduced_low, preferred_element_type=jnp.float32
    )
    grad_down_flat = (
        grad_down_weight.reshape(4, model_width, model_width)
        .transpose(1, 0, 2)
        .reshape(model_width, 4 * model_width)
    )
    grad_windows = jnp.einsum(
        "rto,io->rti", grad_reduced_low, down_matrix, preferred_element_type=jnp.float32
    )
    zero_pair = jnp.zeros((batch_rows, 1, 2 * model_width), jnp.float32)
    grad_pairs = jnp.concatenate(
        [grad_windows[:, :, : 2 * model_width], zero_pair], 1
    ) + jnp.concatenate([zero_pair, grad_windows[:, :, 2 * model_width :]], 1)
    grad_padded = grad_pairs.reshape(batch_rows, local_frames + 2, model_width)
    from_right = shifted_2(grad_padded[:, :2], SEQ, -1)
    grad_encoded = grad_padded[:, 2:] + jnp.concatenate(
        [jnp.zeros((batch_rows, local_frames - 2, model_width), jnp.float32), from_right], 1
    )
    grad_activations, grads_encoder = layer_backward(
        grad_encoded, kept_encoder, encoder_parameters, visible, cos_table, sin_table
    )
    activations_grad = grad_activations.astype(jnp.bfloat16)
    down_grad, latent_in_grad, enc_l1_grad, enc_l2_grad = reduce_together(
        grad_down_flat, grad_latent_in, grads_encoder[7], fold_rows(grads_encoder[8])
    )
    vector_grads = jnp.stack(
        [grads_encoder[i] for i in (0, 1, 4, 5, 6, 9)]
        + [grad_down_bias, grad_up_bias]
        + [grads_decoder[i] for i in (0, 1, 4, 5, 6, 9)],
        1,
    )
    vector_grads = jnp.pad(vector_grads, ((0, 0), (0, 128 - vector_grads.shape[1])))
    enc_in_grad, enc_out_grad, vector_share = reduce_together(
        grads_encoder[2], grads_encoder[3], vector_grads
    )
    vec = vector_share.T
    taps = lambda block: block.reshape(-1, 4, model_width).transpose(1, 0, 2)
    return (
        output,
        activations_grad,
        vec[0],
        vec[1],
        enc_in_grad,
        enc_out_grad,
        vec[2],
        vec[3],
        vec[4],
        enc_l1_grad,
        unfold_rows(enc_l2_grad),
        vec[5],
        taps(down_grad),
        vec[6],
        latent_in_grad,
        latent_out_grad.T,
        taps(up_grad),
        vec[7],
        vec[8],
        vec[9],
        dec_in_grad,
        dec_out_grad,
        vec[10],
        vec[11],
        vec[12],
        dec_l1_grad,
        unfold_rows(dec_l2_grad),
        vec[13],
        new_cluster_size,
        new_embed_sum,
        new_codebook,
    )


def solution(mesh):
    grid = mesh.devices
    mesh = jax.sharding.Mesh(
        grid.reshape(grid.shape[0] // 2, 2, grid.shape[1] // 2, 2), ("hi", "lo", "x", "core")
    )
    placed = (
        P(DP, SEQ, None),
        P(SEQ),
        P(SEQ),
        P(SEQ, None),
        P(SEQ, None),
        P(SEQ),
        P(SEQ),
        P(SEQ),
        P(SEQ, None),
        P(SEQ, None),
        P(SEQ),
        P(None, SEQ, None),
        P(SEQ),
        P(SEQ, None),
        P(None, SEQ, None),
        P(None, SEQ),
        P(None, SEQ, None),
        P(SEQ),
        P(SEQ),
        P(SEQ),
        P(SEQ, None),
        P(SEQ, None),
        P(SEQ),
        P(SEQ),
        P(SEQ),
        P(SEQ, None),
        P(SEQ, None),
        P(SEQ),
        P(DP, SEQ, None),
        P(DP, None),
        P(DP, SEQ, None),
        P(),
        P(),
        P(None, DP + SEQ),
        P(None, DP + SEQ, None),
    )
    return jax.shard_map(
        local,
        mesh=mesh,
        in_specs=placed,
        out_specs=(
            P(DP, SEQ, None),
            P(DP, SEQ, None),
            P(DP + SEQ),
            P(DP + SEQ),
            P(DP + SEQ, None),
            P(DP + SEQ, None),
            P(DP + SEQ),
            P(DP + SEQ),
            P(DP + SEQ),
            P(DP + SEQ, None),
            P(DP + SEQ, None),
            P(DP + SEQ),
            P(None, DP + SEQ, None),
            P(DP + SEQ),
            P(DP + SEQ, None),
            P(None, DP + SEQ),
            P(None, DP + SEQ, None),
            P(DP + SEQ),
            P(DP + SEQ),
            P(DP + SEQ),
            P(DP + SEQ, None),
            P(DP + SEQ, None),
            P(DP + SEQ),
            P(DP + SEQ),
            P(DP + SEQ),
            P(DP + SEQ, None),
            P(DP + SEQ, None),
            P(DP + SEQ),
            P(None, DP + SEQ),
            P(None, DP + SEQ, None),
            P(None, DP + SEQ, None),
        ),
        check_vma=False,
    )
```

```python
from functools import partial

import jax
import jax.numpy as jnp
from jax import lax
from jax.experimental import pallas as pl
from jax.experimental.pallas import tpu as pltpu
from jax.sharding import PartitionSpec as P

HEADS = 8
HEAD_DIM = 64
CONTEXT = 250
HALO = 256
CODE_HALO = HALO // 2 + 16
EXTRA = 16
QUERIES = 64
GROUP = 4
WINDOW = HALO + QUERIES
VMEM_LIMIT = 44 * 1024 * 1024
DP = ("hi", "lo")
SEQ = ("x", "core")

norm_eps = 1e-05
ema_decay = 0.9
bf16 = jnp.bfloat16
f32 = jnp.float32


def mm(a, b):
    return jnp.dot(a, b, preferred_element_type=f32)


def mm_nt(a, b):
    return lax.dot_general(a, b, (((1,), (1,)), ((), ())), preferred_element_type=f32)


def mm_tn(a, b):
    return lax.dot_general(a, b, (((0,), (0,)), ((), ())), preferred_element_type=f32)


def normalize(stream):
    center = stream - jnp.mean(stream, -1, keepdims=True)
    scaled = lax.rsqrt(jnp.mean(center * center, -1, keepdims=True) + norm_eps)
    return center * scaled, scaled


def norm_backward(upstream, normal, scaled, gain):
    inner = upstream * gain
    return scaled * (
        inner
        - jnp.mean(inner, -1, keepdims=True)
        - normal * jnp.mean(inner * normal, -1, keepdims=True)
    )


def column_sum(value):
    return jnp.sum(value, 0, keepdims=True)


def interleave(even, odd, scr):
    tiles, rows, _ = scr.shape
    for tile in range(tiles):
        cols = slice(tile * 128, (tile + 1) * 128)
        scr[tile, pl.ds(0, rows // 2, stride=2), :] = even[:, cols]
        scr[tile, pl.ds(1, rows // 2, stride=2), :] = odd[:, cols]
    return jnp.concatenate([scr[tile] for tile in range(tiles)], 1)


def split_rows(value, scr):
    tiles, rows, _ = scr.shape
    for tile in range(tiles):
        scr[tile] = value[:, tile * 128 : (tile + 1) * 128]
    even = [scr[tile, pl.ds(0, rows // 2, stride=2), :] for tile in range(tiles)]
    odd = [scr[tile, pl.ds(1, rows // 2, stride=2), :] for tile in range(tiles)]
    return jnp.concatenate(even, 1), jnp.concatenate(odd, 1)


def first_half():
    lane = lax.broadcasted_iota(jnp.int32, (1, 128), 1)
    return lane % HEAD_DIM < HEAD_DIM // 2


def rotate(tile, cos, sin):
    swapped = jnp.where(first_half(), pltpu.roll(tile, 96, 1), pltpu.roll(tile, 32, 1))
    return tile * cos + swapped * sin


def head_lanes():
    lane = lax.broadcasted_iota(jnp.int32, (1, GROUP * HEAD_DIM), 1) // HEAD_DIM
    return [(lane == head) for head in range(GROUP)]


def stack_heads(block, lanes):
    return jnp.concatenate([block * mask.astype(bf16) for mask in lanes], 0)


def unstack_heads(block, lanes):
    rows = block.shape[0] // GROUP
    out = block[:rows]
    for head in range(1, GROUP):
        out = jnp.where(lanes[head], block[head * rows : (head + 1) * rows], out)
    return out


def lowest_key(query, cut):
    low = jnp.maximum(query - (CONTEXT - 1), 0)
    return jnp.where(query >= cut, jnp.maximum(low, cut), low)


def attend(q_ref, k_ref, v_ref, att_ref, sc_ref, rows, first_query, first_key, keys, at_row):
    start, cut = sc_ref[0], sc_ref[1]
    query = start + first_query + lax.broadcasted_iota(jnp.int32, (rows, 1), 0)
    low = lowest_key(query, cut)
    key = start + first_key + lax.broadcasted_iota(jnp.int32, (rows, keys), 1)
    mask = (key <= query) & (key >= low)
    mask = jnp.concatenate([mask] * GROUP, 0)
    lanes = head_lanes()
    key_row = first_key + HALO
    for group in range(HEADS // GROUP):
        cols = slice(group * GROUP * HEAD_DIM, (group + 1) * GROUP * HEAD_DIM)
        stacked = stack_heads(q_ref[at_row : at_row + rows, cols], lanes)
        scores = mm_nt(stacked, k_ref[key_row : key_row + keys, cols]) * HEAD_DIM ** (-0.5)
        scores = jnp.where(mask, scores, -1e30)
        exponent = jnp.exp(scores - jnp.max(scores, -1, keepdims=True))
        weights = exponent * (1.0 / jnp.sum(exponent, -1, keepdims=True))
        mixed = mm(weights.astype(bf16), v_ref[key_row : key_row + keys, cols])
        att_ref[at_row : at_row + rows, cols] = unstack_heads(mixed, lanes).astype(bf16)


def front(x, vec_ref, base, w_in, cos_ref, sin_ref, sc_ref, n1_ref, q_ref, k_ref, v_ref, att_ref,
          extra):
    width = x.shape[1]
    normal, _ = normalize(x)
    low = (normal * vec_ref[base : base + 1] + vec_ref[base + 1 : base + 2]).astype(bf16)
    n1_ref[...] = low[HALO:]
    skip = HALO - extra
    queries = mm(low[skip:], w_in[:, :width])
    keys = mm(low, w_in[:, width : 2 * width])
    for at in range(0, width, 128):
        q_ref[:, at : at + 128] = rotate(
            queries[:, at : at + 128], cos_ref[skip:], sin_ref[skip:]
        ).astype(bf16)
        k_ref[:, at : at + 128] = rotate(keys[:, at : at + 128], cos_ref[...], sin_ref[...]).astype(
            bf16
        )
    v_ref[...] = mm(low, w_in[:, 2 * width :]).astype(bf16)
    frames = x.shape[0] - HALO
    if extra:
        attend(q_ref, k_ref, v_ref, att_ref, sc_ref, extra, -extra, -HALO, HALO, 0)
    for first in range(0, frames, QUERIES):
        attend(
            q_ref, k_ref, v_ref, att_ref, sc_ref, QUERIES, first, first - HALO, WINDOW,
            extra + first,
        )


def decoder_front_kernel(sc_ref, qz_ref, w_ref, vec_ref, cos_ref, sin_ref,
                         x_ref, restored_ref, n1_ref, q_ref, k_ref, v_ref, att_ref,
                         w_vmem, x_scr, sem):
    width = x_ref.shape[1]
    copy = pltpu.make_async_copy(w_ref, w_vmem, sem)
    copy.start()
    copy.wait()
    latent = qz_ref.shape[1]
    restored = mm_nt(qz_ref[...], w_vmem[:, :latent]).astype(bf16)
    restored_ref[...] = restored[CODE_HALO - 16 :]
    both = mm(restored, w_vmem[:, latent : latent + 4 * width])
    bias = vec_ref[7:8]
    now = both[16:, : 2 * width]
    before = pltpu.roll(both[:, 2 * width :], 1, 0)[16:]
    total = now + before
    x = interleave(total[:, :width] + bias, total[:, width:] + bias, x_scr)
    x_ref[...] = x[HALO:]
    w_in = w_vmem.at[:, latent + 4 * width :]
    front(x, vec_ref, 8, w_in, cos_ref, sin_ref, sc_ref, n1_ref, q_ref, k_ref, v_ref,
          att_ref, 0)


def encoder_front_kernel(sc_ref, halo_ref, x_ref, w_ref, vec_ref, cos_ref, sin_ref,
                         n1_ref, q_ref, k_ref, v_ref, att_ref, w_vmem, sem):
    width = x_ref.shape[1]
    copy = pltpu.make_async_copy(w_ref.at[:, : 3 * width], w_vmem, sem)
    copy.start()
    x = jnp.concatenate([halo_ref[...], x_ref[...]], 0).astype(f32)
    copy.wait()
    front(x, vec_ref, 0, w_vmem, cos_ref, sin_ref, sc_ref, n1_ref, q_ref, k_ref, v_ref, att_ref,
          EXTRA)


def gelu_both(hidden):
    share = 0.5 * (1.0 + lax.erf(hidden * 0.7071067811865476))
    density = jnp.exp(-0.5 * hidden * hidden) * 0.3989422804014327
    return hidden * share, share + hidden * density


def l2_rows(w, at, chunk, width):
    rows = width // 4
    return jnp.concatenate(
        [
            w[chunk * rows : (chunk + 1) * rows, at + g * width : at + (g + 1) * width]
            for g in range(4)
        ],
        0,
    )


def forward_kernel(base, extra, at, att_ref, x_ref, g_ref, w_ref, vec_ref,
                   out_ref, gmid_ref, datt_ref, n2_ref, active_ref, dh_ref, dtwo_ref, done_ref,
                   vg_ref, w_vmem, h_scr, slope_scr, mid_scr, act_scr, sems):
    width = x_ref.shape[1]
    frames = g_ref.shape[0]
    hidden_total = 4 * width
    parts = ((0, width), (width, width + hidden_total), (width + hidden_total, width + 2 * hidden_total))
    copies = []
    for i, (low, high) in enumerate(parts):
        copies.append(
            pltpu.make_async_copy(
                w_ref.at[:, at + low : at + high], w_vmem.at[:, low:high], sems.at[i]
            )
        )
        copies[-1].start()
    scale_one = vec_ref[base + 2 : base + 3]
    gain_two = vec_ref[base + 3 : base + 4]
    bias_two = vec_ref[base + 4 : base + 5]
    scale_two = vec_ref[base + 5 : base + 6]
    copies[0].wait()
    branch = mm(att_ref[...], w_vmem[:, :width])
    middle = x_ref[...].astype(f32) + scale_one * branch
    mid_scr[...] = middle
    normal, scaled = normalize(middle)
    n2 = (normal * gain_two + bias_two).astype(bf16)
    n2_ref[...] = n2[extra:]
    copies[1].wait()
    l1_at, l2_at = width, width + hidden_total
    rows = x_ref.shape[0]
    second = None
    for chunk in range(4):
        cols = slice(chunk * width, (chunk + 1) * width)
        h_scr[...] = mm(n2, w_vmem[:, l1_at + chunk * width : l1_at + (chunk + 1) * width])

        def body(i, _):
            at_row = pl.multiple_of(i * 16, 16)
            here = pl.ds(at_row, 16)
            act, slope = gelu_both(h_scr[here, :])
            act_scr[here, cols] = act.astype(bf16)
            slope_scr[here, cols] = slope
            return 0

        lax.fori_loop(0, rows // 16, body, 0)
        if chunk == 0:
            copies[2].wait()
        part = mm(act_scr[:, cols], l2_rows(w_vmem, l2_at, chunk, width))
        second = part if second is None else second + part
    active_ref[...] = act_scr[extra:, :]
    out_ref[...] = (mid_scr[...] + scale_two * second).astype(bf16)

    g = g_ref[...].astype(f32)
    vg_ref[3:4, :] = column_sum(g * second[extra:])
    d_two = (g * scale_two).astype(bf16)
    dtwo_ref[...] = d_two
    e = None
    for chunk in range(4):
        cols = slice(chunk * width, (chunk + 1) * width)
        d_active = mm_nt(d_two, l2_rows(w_vmem, l2_at, chunk, width))
        dh_ref[:, cols] = (d_active * slope_scr[extra:, cols]).astype(bf16)
        part = mm_nt(
            dh_ref[:, cols], w_vmem[:, l1_at + chunk * width : l1_at + (chunk + 1) * width]
        )
        e = part if e is None else e + part
    normal, scaled = normal[extra:], scaled[extra:]
    vg_ref[1:2, :] = column_sum(e * normal)
    vg_ref[2:3, :] = column_sum(e)
    g_mid = g + norm_backward(e, normal, scaled, gain_two)
    gmid_ref[...] = g_mid
    vg_ref[0:1, :] = column_sum(g_mid * branch[extra:])
    d_one = (g_mid * scale_one).astype(bf16)
    done_ref[...] = d_one
    datt_ref[...] = mm_nt(d_one, w_vmem[:, :width]).astype(bf16)


def attention_backward_kernel(extra, sc_ref, q_ref, k_ref, v_ref, do_ref,
                              dq_ref, dk_ref, dv_ref, dkh_ref, dvh_ref, dk_scr, dv_scr):
    start, cut = sc_ref[0], sc_ref[1]
    frames = do_ref.shape[0]
    lanes = head_lanes()
    scale = HEAD_DIM ** (-0.5)
    dk_scr[...] = jnp.zeros_like(dk_scr)
    dv_scr[...] = jnp.zeros_like(dv_scr)
    wide = GROUP * QUERIES
    for first in range(0, frames, QUERIES):
        lane = lax.broadcasted_iota(jnp.int32, (1, wide), 1) % QUERIES
        query = start + first + lane
        low = lowest_key(query, cut)
        key = start + first - HALO + lax.broadcasted_iota(jnp.int32, (WINDOW, wide), 0)
        mask = (key <= query) & (key >= low)
        for group in range(HEADS // GROUP):
            cols = slice(group * GROUP * HEAD_DIM, (group + 1) * GROUP * HEAD_DIM)
            qs = stack_heads(q_ref[extra + first : extra + first + QUERIES, cols], lanes)
            ds = stack_heads(do_ref[first : first + QUERIES, cols], lanes)
            kw = k_ref[first : first + WINDOW, cols]
            vw = v_ref[first : first + WINDOW, cols]
            scores = jnp.where(mask, mm_nt(kw, qs) * scale, -1e30)
            exponent = jnp.exp(scores - jnp.max(scores, 0, keepdims=True))
            probs = exponent * (1.0 / jnp.sum(exponent, 0, keepdims=True))
            d_probs = mm_nt(vw, ds)
            mean = jnp.sum(probs * d_probs, 0, keepdims=True)
            d_scores = (probs * (d_probs - mean)).astype(bf16)
            dk_scr[first : first + WINDOW, cols] += mm(d_scores, qs)
            dv_scr[first : first + WINDOW, cols] += mm(probs.astype(bf16), ds)
            dq_ref[first : first + QUERIES, cols] = (
                unstack_heads(mm_tn(d_scores, kw), lanes) * scale
            )
    dk_ref[...] = dk_scr[HALO:] * scale
    dv_ref[...] = dv_scr[HALO:]
    dkh_ref[...] = (dk_scr[:HALO] * scale).astype(bf16)
    dvh_ref[...] = dv_scr[:HALO].astype(bf16)


class Packer:
    def __init__(self, core, refs, shares):
        self.core, self.refs, self.shares = core, refs, shares

    def put(self, value, at, step=1, phase=0, block0=0):
        if len(self.refs) == 1:
            if step == 1:
                self.refs[0][:, at : at + value.shape[1]] = value.astype(bf16)
            return
        send, keep = self.refs
        cols = slice(at, at + value.shape[1])
        rows = 16
        hi = self.shares // 8
        blocks = value.shape[0] // (rows * step)
        for pair in range(blocks // 2):
            even = value[(2 * pair * step + phase) * rows :][:rows]
            odd = value[((2 * pair + 1) * step + phase) * rows :][:rows]
            block = (block0 + 2 * pair) // 2
            x, lo, high = block % 2, (block // 2) % 2, block // 4
            at_row = ((x * 2 + lo) * hi + high) * rows
            first = self.core == 0
            keep[at_row : at_row + rows, cols] = jnp.where(first, even, odd).astype(bf16)
            send[at_row : at_row + rows, cols] = jnp.where(first, odd, even).astype(bf16)

    def put_l2(self, value, at, chunk, width):
        if len(self.refs) == 1:
            cols = slice(at + chunk * width, at + (chunk + 1) * width)
            self.refs[0][:, cols] = value.astype(bf16)
            return
        for phase in range(4):
            self.put(value, at + phase * width, 4, phase, chunk * width // 64)


def weight_gradients_kernel(extra, shares, sc_ref, n2_ref, active_ref, dh_ref, dtwo_ref, att_ref,
                            done_ref, *rest):
    refs = rest
    width = n2_ref.shape[1]
    pack = Packer(sc_ref[2], refs, shares)
    for chunk in range(4):
        cols = slice(chunk * width, (chunk + 1) * width)
        pack.put(mm_tn(n2_ref[...], dh_ref[:, cols]), chunk * width)
        pack.put_l2(mm_tn(active_ref[:, cols], dtwo_ref[...]), 4 * width, chunk, width)
    pack.put(mm_tn(att_ref[extra:, :], done_ref[...]), 8 * width)


def encoder_weight_gradients_kernel(extra, shares, sc_ref, n2_ref, active_ref, dh_ref, dtwo_ref,
                                    att_ref, done_ref, win_ref, dred_ref, red_ref, dlat_ref, *rest):
    width = n2_ref.shape[1]
    weight_gradients_kernel(
        extra, shares, sc_ref, n2_ref, active_ref, dh_ref, dtwo_ref, att_ref, done_ref, *rest
    )
    pack = Packer(sc_ref[2], rest, shares)
    d_reduced = dred_ref[...]
    for tap in range(4):
        pack.put(mm_tn(win_ref[tap], d_reduced), (9 + tap) * width)
    pack.put(mm_tn(red_ref[...], dlat_ref[...]), 13 * width)


def layer_input_gradient(extra_rows, base, dq_ref, dk_ref, dv_ref, dkh_ref, dvh_ref, x, gmid_ref,
                         w_in, vec_ref, cos_ref, sin_ref, dmix_ref, vg_ref):
    frames, width = dq_ref.shape
    later = frames - HALO
    cos, sin = cos_ref[HALO:], -sin_ref[HALO:]
    for at in range(0, width, 128):
        cols = slice(at, at + 128)
        dmix_ref[:, cols] = rotate(dq_ref[:, cols], cos, sin).astype(bf16)
        keys = dk_ref[:, cols]
        keys = jnp.concatenate([keys[:later], keys[later:] + dkh_ref[:, cols].astype(f32)], 0)
        dmix_ref[:, width + at : width + at + 128] = rotate(keys, cos, sin).astype(bf16)
        values = dv_ref[:, cols]
        values = jnp.concatenate([values[:later], values[later:] + dvh_ref[:, cols].astype(f32)], 0)
        dmix_ref[:, 2 * width + at : 2 * width + at + 128] = values.astype(bf16)
    d_normed = mm_nt(dmix_ref[...], w_in[...])
    normal, scaled = normalize(x)
    vg_ref[0:1, :] = column_sum(d_normed * normal)
    vg_ref[1:2, :] = column_sum(d_normed)
    return gmid_ref[...] + norm_backward(d_normed, normal, scaled, vec_ref[base : base + 1])


def decoder_back_kernel(at, sc_ref, dq_ref, dk_ref, dv_ref, dkh_ref, dvh_ref, x_ref, gmid_ref, w_ref,
                        vec_ref, cos_ref, sin_ref, dup_ref, dmix_ref, vg_ref, w_vmem, sem):
    copy = pltpu.make_async_copy(w_ref.at[:, at : at + w_vmem.shape[1]], w_vmem, sem)
    copy.start()
    copy.wait()
    grad = layer_input_gradient(
        0, 8, dq_ref, dk_ref, dv_ref, dkh_ref, dvh_ref, x_ref[...], gmid_ref, w_vmem, vec_ref,
        cos_ref, sin_ref, dmix_ref, vg_ref,
    )
    vg_ref[2:3, :] = column_sum(grad)
    dup_ref[...] = grad.astype(bf16)


def encoder_back_kernel(shares, sc_ref, dq_ref, dk_ref, dv_ref, dkh_ref, dvh_ref, x_ref, gmid_ref,
                        w_ref, vec_ref, cos_ref, sin_ref, n1_ref, vgs_ref, grad_ref, *rest):
    refs, (w_vmem, dmix_scr, vg_scr, all_scr, sem) = rest[:-5], rest[-5:]
    width = x_ref.shape[1]
    copy = pltpu.make_async_copy(w_ref.at[:, : w_vmem.shape[1]], w_vmem, sem)
    copy.start()
    copy.wait()
    grad = layer_input_gradient(
        0, 0, dq_ref, dk_ref, dv_ref, dkh_ref, dvh_ref, x_ref[...].astype(f32), gmid_ref, w_vmem,
        vec_ref, cos_ref, sin_ref, dmix_scr, vg_scr,
    )
    grad_ref[...] = grad.astype(bf16)
    pack = Packer(sc_ref[2], refs, shares)
    for part in range(3):
        cols = slice(part * width, (part + 1) * width)
        pack.put(mm_tn(n1_ref[...], dmix_scr[:, cols]), part * width)
    all_scr[...] = jnp.zeros_like(all_scr)
    all_scr[0:2, :] = vg_scr[0:2, :]
    all_scr[2:6, :] = vgs_ref[0:4, :]
    all_scr[6:7, :] = vgs_ref[16:17, :]
    all_scr[7:8, :] = vgs_ref[26:27, :]
    all_scr[8:10, :] = vgs_ref[24:26, :]
    all_scr[10:14, :] = vgs_ref[8:12, :]
    pack.put(all_scr[...].T, 3 * width)


def middle_kernel(shares, sc_ref, dup_ref, next_ref, dmix_ref, n1_ref, restored_ref, qz_ref, w_ref,
                  we_ref, denc_ref, dred_ref, dlat_ref, vg_ref, *rest):
    refs, (up_vmem, down_vmem, frame_scr, sems) = rest[:-4], rest[-4:]
    frames, width = dup_ref.shape
    latent = qz_ref.shape[1]
    codec = frames // 2
    copies = [
        pltpu.make_async_copy(w_ref.at[:, : latent + 4 * width], up_vmem, sems.at[0]),
        pltpu.make_async_copy(
            we_ref.at[:, 12 * width : 16 * width + latent], down_vmem, sems.at[1]
        ),
    ]
    for copy in copies:
        copy.start()
    pairs = codec + 16
    even, odd = split_rows(
        jnp.concatenate([dup_ref[...], next_ref[...]], 0).astype(f32), frame_scr
    )
    both = jnp.concatenate([even, odd], 1).astype(bf16)
    copies[0].wait()
    up = up_vmem[:, latent : latent + 4 * width]
    here = mm_nt(both, up[:, : 2 * width])
    later = mm_nt(both, up[:, 2 * width :])
    d_restored = (here + pltpu.roll(later, pairs - 1, 0)).astype(bf16)
    d_latent = mm(d_restored, up_vmem[:, :latent]).astype(bf16)
    copies[1].wait()
    d_reduced = mm_nt(d_latent, down_vmem[:, 4 * width :]).astype(bf16)
    dlat_ref[...] = d_latent[:codec]
    dred_ref[...] = d_reduced[:codec]
    vg_ref[0:1, :] = column_sum(d_reduced[:codec].astype(f32))
    taps = [mm_nt(d_reduced, down_vmem[:, tap * width : (tap + 1) * width]) for tap in range(4)]
    denc_ref[...] = interleave(
        taps[2] + pltpu.roll(taps[0], pairs - 1, 0),
        taps[3] + pltpu.roll(taps[1], pairs - 1, 0),
        frame_scr,
    )[:frames]

    pack = Packer(sc_ref[2], refs, shares)
    for part in range(3):
        cols = slice(part * width, (part + 1) * width)
        pack.put(mm_tn(n1_ref[...], dmix_ref[:, cols]), part * width)
    restored = restored_ref[...]
    own_pairs = both[:codec]
    before = pltpu.roll(restored.astype(f32), 1, 0)[16:].astype(bf16)
    pack.put(mm_tn(restored[16:], own_pairs[:, :width]), 3 * width)
    pack.put(mm_tn(restored[16:], own_pairs[:, width:]), 4 * width)
    pack.put(mm_tn(before, own_pairs[:, :width]), 5 * width)
    pack.put(mm_tn(before, own_pairs[:, width:]), 6 * width)
    pack.put(mm_tn(d_restored[:codec], qz_ref[CODE_HALO:, :]), 7 * width)


def latent_kernel(sc_ref, enc_ref, rows_ref, w_ref, vec_ref, res_ref, win_ref, red_ref,
                  w_vmem, frame_scr, sem):
    total, width = enc_ref.shape
    codec = (total - EXTRA) // 2
    copy = pltpu.make_async_copy(w_ref.at[:, 12 * width : 12 * width + w_vmem.shape[1]], w_vmem, sem)
    copy.start()
    inside = (sc_ref[0] > 0).astype(f32)
    rim = enc_ref[:EXTRA].astype(f32) * inside
    skip = EXTRA // 2
    even, odd = split_rows(jnp.concatenate([rim, enc_ref[EXTRA:].astype(f32)], 0), frame_scr)
    win_ref[0] = pltpu.roll(even, 1, 0)[skip:].astype(bf16)
    win_ref[1] = pltpu.roll(odd, 1, 0)[skip:].astype(bf16)
    win_ref[2] = even[skip:].astype(bf16)
    win_ref[3] = odd[skip:].astype(bf16)
    copy.wait()
    reduced = vec_ref[6:7]
    for tap in range(4):
        reduced = reduced + mm(win_ref[tap], w_vmem[:, tap * width : (tap + 1) * width])
    reduced = reduced.astype(bf16)
    red_ref[...] = reduced
    remaining = mm(reduced, w_vmem[:, 4 * width :])
    for level in range(rows_ref.shape[0]):
        res_ref[level] = remaining.astype(bf16)
        remaining = remaining - rows_ref[level].astype(f32)


def lookup_kernel(sc_ref, codes_ref, book_ref, qsend_ref, qkeep_ref, rsend_ref, rkeep_ref, q_scr):
    levels, share, latent = book_ref.shape
    total = codes_ref.shape[0]
    codec = total // 4
    base = sc_ref[3]
    core = sc_ref[2]
    entry = lax.broadcasted_iota(jnp.int32, (1, share), 1)
    for level in range(levels):
        picks = (codes_ref[:, level : level + 1] - base == entry).astype(f32).astype(bf16)
        found = mm(picks, book_ref[level])
        q_scr[CODE_HALO:] = found if level == 0 else q_scr[CODE_HALO:] + found
        for x in range(2):
            even = found[(2 * x) * codec :][:codec]
            odd = found[(2 * x + 1) * codec :][:codec]
            rkeep_ref[x, level] = jnp.where(core == 0, even, odd).astype(bf16)
            rsend_ref[x, level] = jnp.where(core == 0, odd, even).astype(bf16)
    q_scr[:CODE_HALO] = jnp.zeros((CODE_HALO, latent), f32)
    for x in range(2):
        even = q_scr[(2 * x) * codec : (2 * x + 1) * codec + CODE_HALO]
        odd = q_scr[(2 * x + 1) * codec : (2 * x + 2) * codec + CODE_HALO]
        qkeep_ref[x] = jnp.where(core == 0, even, odd)
        qsend_ref[x] = jnp.where(core == 0, odd, even)


def collect_kernel(share, sc_ref, res_ref, codes_ref, entry_ref, dead_ref, place_ref,
                   send_ref, keep_ref, cnt_scr):
    levels = codes_ref.shape[0]
    parts, _, codec, latent = res_ref.shape
    total = codes_ref.shape[1]
    lo = sc_ref[4]
    high = send_ref.shape[0]
    frame = lax.broadcasted_iota(jnp.int32, (1, total), 1)
    ones = jnp.ones((16, total), bf16)
    for level in range(levels):
        used = (entry_ref[:, level : level + 1] == codes_ref[level : level + 1, :]).astype(f32)
        placed = (place_ref[:, level : level + 1] == frame).astype(f32)
        select = jnp.where(dead_ref[:, level : level + 1] == 1, placed, used).astype(bf16)
        rows = jnp.concatenate([res_ref[part, level] for part in range(parts)], 0)
        sums = mm(select, rows)
        cnt_scr[level : level + 1, :] = mm_nt(ones, used.astype(bf16))[0:1]
        at = slice(level * share, (level + 1) * share)
        for h in range(high):
            even = sums[(2 * h) * share :][:share]
            odd = sums[(2 * h + 1) * share :][:share]
            keep_ref[h, at, :] = jnp.where(lo == 0, even, odd).astype(bf16)
            send_ref[h, at, :] = jnp.where(lo == 0, odd, even).astype(bf16)
    counts = cnt_scr[...]
    upper = jnp.floor(counts * (1.0 / 128.0))
    digits = jnp.concatenate([upper, counts - 128.0 * upper], 0)
    tail = slice(levels * share, levels * share + 2 * levels)
    for h in range(high):
        even = digits[:, (2 * h) * share : (2 * h + 1) * share]
        odd = digits[:, (2 * h + 1) * share : (2 * h + 2) * share]
        keep_ref[h, tail, :] = jnp.zeros((2 * levels, latent), bf16)
        send_ref[h, tail, :] = jnp.zeros((2 * levels, latent), bf16)
        keep_ref[h, tail, :share] = jnp.where(lo == 0, even, odd).astype(bf16)
        send_ref[h, tail, :share] = jnp.where(lo == 0, odd, even).astype(bf16)


def call(kernel, outs, spaces, scratch, flops, args):
    where = {"s": pltpu.SMEM, "v": pltpu.VMEM, "a": pl.ANY}
    size = sum(o.size * o.dtype.itemsize for o in outs) + sum(a.size * a.dtype.itemsize for a in args)
    return pl.pallas_call(
        kernel,
        out_shape=outs,
        in_specs=[pl.BlockSpec(memory_space=where[s]) for s in spaces],
        out_specs=[pl.BlockSpec(memory_space=pltpu.VMEM) for _ in outs],
        scratch_shapes=scratch,
        compiler_params=pltpu.CompilerParams(vmem_limit_bytes=VMEM_LIMIT),
        cost_estimate=pl.CostEstimate(flops=flops, bytes_accessed=size, transcendentals=0),
    )(*args)


def shape(dims, dtype=f32):
    return jax.ShapeDtypeStruct(dims, dtype)


def halve(block, dim, axis):
    mine = lax.axis_index(axis)
    sent = lax.dynamic_index_in_dim(block, 1 - mine, dim, False)
    kept = lax.dynamic_index_in_dim(block, mine, dim, False)
    got = lax.ppermute(sent, axis, [(0, 1), (1, 0)])
    return (kept.astype(f32) + got.astype(f32)).astype(block.dtype)


def swap_add(send, keep, axis):
    got = lax.ppermute(send, axis, [(0, 1), (1, 0)])
    return (keep.astype(f32) + got.astype(f32)).astype(keep.dtype)


def sum_over_hi(block):
    parts = lax.all_to_all(block, "hi", 0, 0, tiled=True)
    return jnp.sum(parts.astype(f32), 0)


def shifted(block, distance):
    devices = range(lax.axis_size(SEQ))
    route = [(i - distance, i) for i in devices if i - distance in devices]
    return lax.ppermute(block, SEQ, route)


def packed_outs(width_total, width, shares):
    if width // shares % 16 == 0:
        return [shape((width // 2, width_total), bf16)] * 2
    return [shape((width, width_total), bf16)]


def reduce_packed(parts, shares, l2_at=None):
    if len(parts) == 2:
        send, keep = parts
        total = keep.shape[1]
        block = swap_add(send, keep, "core")
        block = block.reshape(2, 2, shares // 8, -1, total)
        block = halve(halve(block, 0, "x"), 0, "lo")
        return sum_over_hi(block)
    (block,) = parts
    width, total = block.shape
    rows = width // shares
    if l2_at is not None:
        full = [block[:, l2_at + i * width : l2_at + (i + 1) * width] for i in range(4)]
        full = jnp.concatenate(full, 0).reshape(shares, 4, rows, width)
        full = full.transpose(0, 2, 1, 3).reshape(width, 4 * width)
        block = jnp.concatenate([block[:, :l2_at], full, block[:, l2_at + 4 * width :]], 1)
    block = block.reshape(shares // 8, 2, 2, 2, rows, total)
    block = halve(halve(halve(block, 3, "core"), 2, "x"), 1, "lo")
    return sum_over_hi(block)


def local(
    activations,
    encoder_attention_norm_gain,
    encoder_attention_norm_bias,
    encoder_query_key_value_weight,
    encoder_attention_output_weight,
    encoder_attention_layer_scale,
    encoder_forward_norm_gain,
    encoder_forward_norm_bias,
    encoder_forward_input_weight,
    encoder_forward_output_weight,
    encoder_forward_layer_scale,
    strided_convolution_weight,
    strided_convolution_bias,
    quantizer_input_weight,
    codebook,
    quantizer_output_weight,
    transposed_convolution_weight,
    transposed_convolution_bias,
    decoder_attention_norm_gain,
    decoder_attention_norm_bias,
    decoder_query_key_value_weight,
    decoder_attention_output_weight,
    decoder_attention_layer_scale,
    decoder_forward_norm_gain,
    decoder_forward_norm_bias,
    decoder_forward_input_weight,
    decoder_forward_output_weight,
    decoder_forward_layer_scale,
    cotangent,
    frame_segment_index,
    frame_code_index,
    replace_code_mask,
    replacing_batch_position,
    code_usage_average,
    code_latent_sum_average,
):
    batch_rows, frames, width = activations.shape
    assert batch_rows == 1
    seq_index = lax.axis_index(SEQ)
    seq_count = lax.axis_size(SEQ)
    dp_index = lax.axis_index(DP)
    dp_count = lax.axis_size(DP)
    shares = dp_count * seq_count
    codec = frames // 2
    levels = frame_code_index.shape[2]
    latent = codebook.shape[2]
    book_share = codebook.shape[1]
    core_index = lax.axis_index("core")

    cut = jnp.sum((frame_segment_index[0] == 0).astype(jnp.int32))
    scalars = jnp.stack(
        [
            seq_index * frames,
            cut,
            core_index,
            seq_index * book_share,
            lax.axis_index("lo"),
        ]
    ).astype(jnp.int32)

    row_codes = lax.all_gather(frame_code_index[0], SEQ, axis=0, tiled=True)

    def flat_taps(taps):
        return taps.transpose(1, 0, 2).reshape(taps.shape[1], -1)

    first_pack = jnp.concatenate(
        [
            quantizer_output_weight.T,
            flat_taps(transposed_convolution_weight),
            decoder_query_key_value_weight,
        ],
        1,
    )
    dec_one = lax.all_gather(first_pack, SEQ, axis=0, tiled=True)
    first_pack, out_share, l1_share, l2_share = lax.optimization_barrier(
        (
            first_pack,
            decoder_attention_output_weight,
            decoder_forward_input_weight,
            decoder_forward_output_weight,
        )
    )

    def fold_l2(share):
        return share.reshape(4, -1, width).transpose(1, 0, 2).reshape(-1, 4 * width)

    second_pack = jnp.concatenate([out_share, l1_share, fold_l2(l2_share)], 1)
    dec_two = lax.all_gather(second_pack, SEQ, axis=0, tiled=True)
    vectors = jnp.stack(
        [
            encoder_attention_norm_gain,
            encoder_attention_norm_bias,
            encoder_attention_layer_scale,
            encoder_forward_norm_gain,
            encoder_forward_norm_bias,
            encoder_forward_layer_scale,
            strided_convolution_bias,
            transposed_convolution_bias,
            decoder_attention_norm_gain,
            decoder_attention_norm_bias,
            decoder_attention_layer_scale,
            decoder_forward_norm_gain,
            decoder_forward_norm_bias,
            decoder_forward_layer_scale,
        ]
    )
    vectors = jnp.pad(vectors, ((0, 2), (0, 0)))
    vectors = lax.all_gather(vectors, SEQ, axis=1, tiled=True).astype(f32)
    second_pack, in_share, down_share = lax.optimization_barrier(
        (second_pack, encoder_query_key_value_weight, strided_convolution_weight)
    )
    third_pack = jnp.concatenate(
        [
            in_share,
            encoder_attention_output_weight,
            encoder_forward_input_weight,
            fold_l2(encoder_forward_output_weight),
            flat_taps(down_share),
            quantizer_input_weight,
        ],
        1,
    )
    enc_all = lax.all_gather(third_pack, SEQ, axis=0, tiled=True)

    positions = seq_index * frames - HALO + jnp.arange(HALO + frames, dtype=jnp.int32)
    half_dim = HEAD_DIM // 2
    frequency = jnp.power(10000.0, -jnp.arange(half_dim, dtype=f32) / half_dim)
    angles = positions.astype(f32)[:, None] * frequency[None, :]
    cos, sin = jnp.cos(angles), jnp.sin(angles)
    cos_table = jnp.concatenate([cos] * 4, 1)
    sin_table = jnp.concatenate([-sin, sin, -sin, sin], 1)
    activation_halo = shifted(activations[0, frames - HALO :], 1)

    window = codec + CODE_HALO
    qsend, qkeep, rsend, rkeep = call(
        lookup_kernel,
        [shape((2, window, latent))] * 2 + [shape((2, levels, codec, latent), bf16)] * 2,
        "svv",
        [pltpu.VMEM((CODE_HALO + codec * seq_count, latent), f32)],
        2 * codec * seq_count * levels * book_share * latent,
        (scalars, row_codes, codebook),
    )
    quantized = halve(swap_add(qsend, qkeep, "core"), 0, "x").astype(bf16)

    total_frames = HALO + frames
    layer_flops = 2 * total_frames * width * 3 * width

    d_x, restored, d_n1, d_q, d_k, d_v, d_att = call(
        decoder_front_kernel,
        [
            shape((frames, width)),
            shape((codec + 16, width), bf16),
            shape((frames, width), bf16),
            shape((frames, width), bf16),
            shape((total_frames, width), bf16),
            shape((total_frames, width), bf16),
            shape((frames, width), bf16),
        ],
        "svavvv",
        [
            pltpu.VMEM((width, dec_one.shape[1]), bf16),
            pltpu.VMEM((width // 128, total_frames, 128), f32),
            pltpu.SemaphoreType.DMA,
        ],
        2 * layer_flops,
        (scalars, quantized, dec_one, vectors, cos_table, sin_table),
    )

    def feed_forward(base, extra, at, att, x, g, weights):
        rows = frames + extra
        return call(
            partial(forward_kernel, base, extra, at),
            [
                shape((rows, width), bf16),
                shape((frames, width)),
                shape((frames, width), bf16),
                shape((frames, width), bf16),
                shape((frames, 4 * width), bf16),
                shape((frames, 4 * width), bf16),
                shape((frames, width), bf16),
                shape((frames, width), bf16),
                shape((8, width)),
            ],
            "vvvav",
            [
                pltpu.VMEM((width, 9 * width), bf16),
                pltpu.VMEM((rows, width), f32),
                pltpu.VMEM((rows, 4 * width), f32),
                pltpu.VMEM((rows, width), f32),
                pltpu.VMEM((rows, 4 * width), bf16),
                pltpu.SemaphoreType.DMA((3,)),
            ],
            2 * frames * width * width * 18,
            (att, x, g, weights, vectors),
        )

    def attention_backward(extra, q, k, v, do):
        return call(
            partial(attention_backward_kernel, extra),
            [shape((frames, width))] * 3 + [shape((HALO, width), bf16)] * 2,
            "svvvv",
            [pltpu.VMEM((total_frames, width), f32)] * 2,
            layer_flops,
            (scalars, q, k, v, do),
        )

    (output, d_gmid, d_datt, d_n2, d_active, d_dh, d_dtwo, d_done, d_vg_two) = feed_forward(
        8, 0, 0, d_att, d_x, cotangent[0], dec_two
    )
    d_dq, d_dk, d_dv, d_dkh, d_dvh = attention_backward(0, d_q, d_k, d_v, d_datt)
    d_dkh, d_dvh = shifted(d_dkh, -1), shifted(d_dvh, -1)
    group_a = call(
        partial(weight_gradients_kernel, 0, shares),
        packed_outs(9 * width, width, shares),
        "svvvvvv",
        [],
        2 * frames * width * width * 9,
        (scalars, d_n2, d_active, d_dh, d_dtwo, d_att, d_done),
    )
    grads_a = reduce_packed(group_a, shares, 4 * width)
    in_at = latent + 4 * width
    d_up, d_mixed, d_vg_one = call(
        partial(decoder_back_kernel, in_at),
        [shape((frames, width), bf16), shape((frames, 3 * width), bf16), shape((8, width))],
        "svvvvvvvavvv",
        [pltpu.VMEM((width, 3 * width), bf16), pltpu.SemaphoreType.DMA],
        layer_flops,
        (scalars, d_dq, d_dk, d_dv, d_dkh, d_dvh, d_x, d_gmid, dec_one, vectors, cos_table, sin_table),
    )
    d_up_next = shifted(d_up[:32], -1)

    e_n1, e_q, e_k, e_v, e_att = call(
        encoder_front_kernel,
        [
            shape((frames, width), bf16),
            shape((frames + EXTRA, width), bf16),
            shape((total_frames, width), bf16),
            shape((total_frames, width), bf16),
            shape((frames + EXTRA, width), bf16),
        ],
        "svvavvv",
        [pltpu.VMEM((width, 3 * width), bf16), pltpu.SemaphoreType.DMA],
        2 * layer_flops,
        (scalars, activation_halo, activations[0], enc_all, vectors, cos_table, sin_table),
    )

    middle_outs = call(
        partial(middle_kernel, shares),
        [
            shape((frames, width)),
            shape((codec, width), bf16),
            shape((codec, latent), bf16),
            shape((8, width)),
        ]
        + packed_outs(7 * width + latent, width, shares),
        "svvvvvvaa",
        [
            pltpu.VMEM((width, latent + 4 * width), bf16),
            pltpu.VMEM((width, latent + 4 * width), bf16),
            pltpu.VMEM((width // 128, frames + 32, 128), f32),
            pltpu.SemaphoreType.DMA((2,)),
        ],
        2 * codec * width * width * 20,
        (scalars, d_up, d_up_next, d_mixed, d_n1, restored, quantized, dec_one, enc_all),
    )
    d_encoded, d_reduced, d_latent, m_vg = middle_outs[:4]
    grads_b = reduce_packed(middle_outs[4:], shares)

    e_x = jnp.concatenate([activation_halo[HALO - EXTRA :], activations[0]], 0)
    (encoded, e_gmid, e_datt, e_n2, e_active, e_dh, e_dtwo, e_done, e_vg_two) = feed_forward(
        0, EXTRA, 3 * width, e_att, e_x, d_encoded, enc_all
    )
    code_rows = halve(swap_add(rsend, rkeep, "core"), 0, "x")
    residuals, windows, reduced = call(
        latent_kernel,
        [
            shape((levels, codec, latent), bf16),
            shape((4, codec, width), bf16),
            shape((codec, width), bf16),
        ],
        "svvav",
        [
            pltpu.VMEM((width, 4 * width + latent), bf16),
            pltpu.VMEM((width // 128, frames + EXTRA, 128), f32),
            pltpu.SemaphoreType.DMA,
        ],
        2 * codec * width * width * 5,
        (scalars, encoded, code_rows, enc_all, vectors),
    )
    e_dq, e_dk, e_dv, e_dkh, e_dvh = attention_backward(EXTRA, e_q, e_k, e_v, e_datt)
    e_dkh, e_dvh = shifted(e_dkh, -1), shifted(e_dvh, -1)
    group_c = call(
        partial(encoder_weight_gradients_kernel, EXTRA, shares),
        packed_outs(13 * width + latent, width, shares),
        "svvvvvvvvvv",
        [],
        2 * frames * width * width * 12,
        (
            scalars, e_n2, e_active, e_dh, e_dtwo, e_att, e_done,
            windows, d_reduced, reduced, d_latent,
        ),
    )
    grads_c = reduce_packed(group_c, shares, 4 * width)
    vector_grads = jnp.concatenate([e_vg_two, d_vg_two, m_vg, d_vg_one], 0)
    back_outs = call(
        partial(encoder_back_kernel, shares),
        [shape((frames, width), bf16)] + packed_outs(3 * width + 128, width, shares),
        "svvvvvvvavvvvv",
        [
            pltpu.VMEM((width, 3 * width), bf16),
            pltpu.VMEM((frames, 3 * width), bf16),
            pltpu.VMEM((8, width), f32),
            pltpu.VMEM((128, width), f32),
            pltpu.SemaphoreType.DMA,
        ],
        layer_flops,
        (
            scalars, e_dq, e_dk, e_dv, e_dkh, e_dvh, activations[0], e_gmid, enc_all, vectors,
            cos_table, sin_table, e_n1, vector_grads,
        ),
    )
    grads_d = reduce_packed(back_outs[1:], shares)

    row_residuals = lax.all_gather(residuals, SEQ, axis=0, tiled=False)
    code_total = replace_code_mask.shape[1]
    code_share = code_usage_average.shape[1]
    row_frames = codec * seq_count
    dead_flag = replace_code_mask == 1

    def seq_part(array):
        return lax.dynamic_index_in_dim(
            array.reshape(levels, dp_count, seq_count, code_share), seq_index, 2, False
        ).reshape(levels, dp_count * code_share)

    part_dead = seq_part(replace_code_mask)
    part_place = seq_part(replacing_batch_position)
    part_place = jnp.where(part_place // row_frames == dp_index, part_place % row_frames, -1)
    part_code = seq_part(
        jnp.broadcast_to(jnp.arange(code_total, dtype=jnp.int32), (levels, code_total))
    )
    if code_share % 16 == 0:
        tail_rows = levels * code_share
        csend, ckeep = call(
            partial(collect_kernel, code_share),
            [shape((dp_count // 2, tail_rows + 2 * levels, latent), bf16)] * 2,
            "svvvvv",
            [pltpu.VMEM((levels, dp_count * code_share), f32)],
            2 * levels * row_frames * dp_count * code_share * latent,
            (scalars, row_residuals, row_codes.T, part_code.T, part_dead.T, part_place.T),
        )
        combined = sum_over_hi(swap_add(csend, ckeep, "lo"))
        summed = combined[:tail_rows].reshape(levels, code_share, latent)
        digits = combined[tail_rows:, :code_share]
        counted = 128.0 * digits[:levels] + digits[levels:]
    else:
        flat_res = row_residuals.transpose(1, 0, 2, 3).reshape(levels, row_frames, latent)
        used = part_code[:, :, None] == row_codes.T[:, None, :]
        placed = part_place[:, :, None] == jnp.arange(row_frames, dtype=jnp.int32)
        counts = jnp.sum(used.astype(f32), 2).reshape(levels, dp_count, code_share)
        selects = jnp.where(part_dead[:, :, None] == 1, placed, used).astype(bf16)
        sums = jnp.einsum("lct,ltd->lcd", selects, flat_res, preferred_element_type=f32)
        sums = sums.astype(bf16).reshape(levels, dp_count, code_share, latent)
        summed = lax.psum_scatter(sums, DP, scatter_dimension=1, tiled=False).astype(f32)
        counted = lax.psum_scatter(counts, DP, scatter_dimension=1, tiled=False)
    owner_flag = lax.dynamic_slice_in_dim(
        dead_flag, lax.axis_index(DP + SEQ) * code_share, code_share, 1
    )
    new_cluster_size = ema_decay * code_usage_average + (1.0 - ema_decay) * counted
    new_embed_sum = jnp.where(
        owner_flag[:, :, None],
        summed * new_cluster_size[:, :, None],
        ema_decay * code_latent_sum_average + (1.0 - ema_decay) * summed,
    )
    new_codebook = new_embed_sum / new_cluster_size[:, :, None]

    def columns(block, at, count):
        return block[:, at * width : (at + count) * width]

    def taps(block):
        return block.reshape(-1, 4, width).transpose(1, 0, 2)

    def unfold(block):
        return block.reshape(-1, 4, width).transpose(1, 0, 2).reshape(-1, width)

    vec = grads_d[:, 3 * width : 3 * width + 16].T
    return (
        output[None],
        back_outs[0][None],
        vec[0],
        vec[1],
        columns(grads_d, 0, 3),
        columns(grads_c, 8, 1),
        vec[2],
        vec[3],
        vec[4],
        columns(grads_c, 0, 4),
        unfold(columns(grads_c, 4, 4)),
        vec[5],
        taps(columns(grads_c, 9, 4)),
        vec[6],
        grads_c[:, 13 * width :],
        grads_b[:, 7 * width :].T,
        taps(columns(grads_b, 3, 4)),
        vec[7],
        vec[8],
        vec[9],
        columns(grads_b, 0, 3),
        columns(grads_a, 8, 1),
        vec[10],
        vec[11],
        vec[12],
        columns(grads_a, 0, 4),
        unfold(columns(grads_a, 4, 4)),
        vec[13],
        new_cluster_size,
        new_embed_sum,
        new_codebook,
    )


def solution(mesh):
    grid = mesh.devices
    mesh = jax.sharding.Mesh(
        grid.reshape(grid.shape[0] // 2, 2, grid.shape[1] // 2, 2), ("hi", "lo", "x", "core")
    )
    placed = (
        P(DP, SEQ, None),
        P(SEQ),
        P(SEQ),
        P(SEQ, None),
        P(SEQ, None),
        P(SEQ),
        P(SEQ),
        P(SEQ),
        P(SEQ, None),
        P(SEQ, None),
        P(SEQ),
        P(None, SEQ, None),
        P(SEQ),
        P(SEQ, None),
        P(None, SEQ, None),
        P(None, SEQ),
        P(None, SEQ, None),
        P(SEQ),
        P(SEQ),
        P(SEQ),
        P(SEQ, None),
        P(SEQ, None),
        P(SEQ),
        P(SEQ),
        P(SEQ),
        P(SEQ, None),
        P(SEQ, None),
        P(SEQ),
        P(DP, SEQ, None),
        P(DP, None),
        P(DP, SEQ, None),
        P(),
        P(),
        P(None, DP + SEQ),
        P(None, DP + SEQ, None),
    )
    return jax.shard_map(
        local,
        mesh=mesh,
        in_specs=placed,
        out_specs=(
            P(DP, SEQ, None),
            P(DP, SEQ, None),
            P(DP + SEQ),
            P(DP + SEQ),
            P(DP + SEQ, None),
            P(DP + SEQ, None),
            P(DP + SEQ),
            P(DP + SEQ),
            P(DP + SEQ),
            P(DP + SEQ, None),
            P(DP + SEQ, None),
            P(DP + SEQ),
            P(None, DP + SEQ, None),
            P(DP + SEQ),
            P(DP + SEQ, None),
            P(None, DP + SEQ),
            P(None, DP + SEQ, None),
            P(DP + SEQ),
            P(DP + SEQ),
            P(DP + SEQ),
            P(DP + SEQ, None),
            P(DP + SEQ, None),
            P(DP + SEQ),
            P(DP + SEQ),
            P(DP + SEQ),
            P(DP + SEQ, None),
            P(DP + SEQ, None),
            P(DP + SEQ),
            P(None, DP + SEQ),
            P(None, DP + SEQ, None),
            P(None, DP + SEQ, None),
        ),
        check_vma=False,
    )
```

```python
from functools import partial

import jax
import jax.numpy as jnp
from jax import lax
from jax.experimental import pallas as pl
from jax.experimental.pallas import tpu as pltpu
from jax.sharding import PartitionSpec as P

HEADS = 8
HEAD_DIM = 64
CONTEXT = 250
HALO = 256
CODE_HALO = HALO // 2 + 16
EXTRA = 16
QUERIES = 64
GROUP = 4
WINDOW = HALO + QUERIES
VMEM_LIMIT = 32 * 1024 * 1024
ORDER_A = ("lo", "x", "hi")
ORDER_B = ("hi", "lo", "x")
ORDER_C = ("x", "lo", "hi")
ORDER_D = ("lo", "x", "hi")
DP = ("hi", "lo")
SEQ = ("x", "core")

norm_eps = 1e-05
ema_decay = 0.9
bf16 = jnp.bfloat16
f32 = jnp.float32


PIECES = 6


def fetch(sc_ref, pieces, at, width, dst, sems, first=0):
    copies = []
    base = 8 if len(pieces) == 6 else 14
    for i, piece in enumerate(pieces):
        rows = piece.shape[0]
        row = pl.multiple_of(sc_ref[base + i], 64)
        copies.append(
            pltpu.make_async_copy(
                piece.at[:, at : at + width], dst.at[pl.ds(row, rows), :], sems.at[first + i]
            )
        )
        copies[-1].start()
    return copies


def split_refs(refs, counts):
    groups = []
    for count in counts:
        groups.append(refs[:count])
        refs = refs[count:]
    return groups, refs


def wait_all(copies):
    for copy in copies:
        copy.wait()


def mm(a, b):
    return jnp.dot(a, b, preferred_element_type=f32)


def mm_nt(a, b):
    return lax.dot_general(a, b, (((1,), (1,)), ((), ())), preferred_element_type=f32)


def mm_tn(a, b):
    return lax.dot_general(a, b, (((0,), (0,)), ((), ())), preferred_element_type=f32)


def normalize(stream):
    center = stream - jnp.mean(stream, -1, keepdims=True)
    scaled = lax.rsqrt(jnp.mean(center * center, -1, keepdims=True) + norm_eps)
    return center * scaled, scaled


def norm_backward(upstream, normal, scaled, gain):
    inner = upstream * gain
    return scaled * (
        inner
        - jnp.mean(inner, -1, keepdims=True)
        - normal * jnp.mean(inner * normal, -1, keepdims=True)
    )


def column_sum(value):
    return jnp.sum(value, 0, keepdims=True)


def interleave(even, odd, scr):
    tiles, rows, _ = scr.shape
    for tile in range(tiles):
        cols = slice(tile * 128, (tile + 1) * 128)
        scr[tile, pl.ds(0, rows // 2, stride=2), :] = even[:, cols]
        scr[tile, pl.ds(1, rows // 2, stride=2), :] = odd[:, cols]
    return jnp.concatenate([scr[tile] for tile in range(tiles)], 1)


def split_rows(value, scr):
    tiles, rows, _ = scr.shape
    for tile in range(tiles):
        scr[tile] = value[:, tile * 128 : (tile + 1) * 128]
    even = [scr[tile, pl.ds(0, rows // 2, stride=2), :] for tile in range(tiles)]
    odd = [scr[tile, pl.ds(1, rows // 2, stride=2), :] for tile in range(tiles)]
    return jnp.concatenate(even, 1), jnp.concatenate(odd, 1)


def first_half():
    lane = lax.broadcasted_iota(jnp.int32, (1, 128), 1)
    return lane % HEAD_DIM < HEAD_DIM // 2


def rotate(tile, cos, sin):
    swapped = jnp.where(first_half(), pltpu.roll(tile, 96, 1), pltpu.roll(tile, 32, 1))
    return tile * cos + swapped * sin


def head_lanes():
    lane = lax.broadcasted_iota(jnp.int32, (1, GROUP * HEAD_DIM), 1) // HEAD_DIM
    return [(lane == head) for head in range(GROUP)]


def stack_heads(block, lanes):
    return jnp.concatenate([block * mask.astype(bf16) for mask in lanes], 0)


def unstack_heads(block, lanes):
    rows = block.shape[0] // GROUP
    out = block[:rows]
    for head in range(1, GROUP):
        out = jnp.where(lanes[head], block[head * rows : (head + 1) * rows], out)
    return out


def lowest_key(query, cut):
    low = jnp.maximum(query - (CONTEXT - 1), 0)
    return jnp.where(query >= cut, jnp.maximum(low, cut), low)


def attend(q_ref, k_ref, v_ref, att_ref, sc_ref, rows, first_query, first_key, keys, at_row):
    start, cut = sc_ref[0], sc_ref[1]
    query = start + first_query + lax.broadcasted_iota(jnp.int32, (rows, 1), 0)
    low = lowest_key(query, cut)
    key = start + first_key + lax.broadcasted_iota(jnp.int32, (rows, keys), 1)
    mask = (key <= query) & (key >= low)
    mask = jnp.concatenate([mask] * GROUP, 0)
    lanes = head_lanes()
    key_row = first_key + HALO
    for group in range(HEADS // GROUP):
        cols = slice(group * GROUP * HEAD_DIM, (group + 1) * GROUP * HEAD_DIM)
        stacked = stack_heads(q_ref[at_row : at_row + rows, cols], lanes)
        scores = mm_nt(stacked, k_ref[key_row : key_row + keys, cols]) * HEAD_DIM ** (-0.5)
        scores = jnp.where(mask, scores, -1e30)
        exponent = jnp.exp(scores - jnp.max(scores, -1, keepdims=True))
        weights = exponent * (1.0 / jnp.sum(exponent, -1, keepdims=True))
        mixed = mm(weights.astype(bf16), v_ref[key_row : key_row + keys, cols])
        att_ref[at_row : at_row + rows, cols] = unstack_heads(mixed, lanes).astype(bf16)


def front(x, vec_ref, base, w_in, cos_ref, sin_ref, sc_ref, n1_ref, q_ref, k_ref, v_ref, att_ref,
          extra):
    width = x.shape[1]
    normal, _ = normalize(x)
    low = (normal * vec_ref[base : base + 1] + vec_ref[base + 1 : base + 2]).astype(bf16)
    n1_ref[...] = low[HALO:]
    skip = HALO - extra
    queries = mm(low[skip:], w_in[:, :width])
    keys = mm(low, w_in[:, width : 2 * width])
    for at in range(0, width, 128):
        q_ref[:, at : at + 128] = rotate(
            queries[:, at : at + 128], cos_ref[skip:], sin_ref[skip:]
        ).astype(bf16)
        k_ref[:, at : at + 128] = rotate(keys[:, at : at + 128], cos_ref[...], sin_ref[...]).astype(
            bf16
        )
    v_ref[...] = mm(low, w_in[:, 2 * width :]).astype(bf16)
    frames = x.shape[0] - HALO
    if extra:
        attend(q_ref, k_ref, v_ref, att_ref, sc_ref, extra, -extra, -HALO, HALO, 0)
    for first in range(0, frames, QUERIES):
        attend(
            q_ref, k_ref, v_ref, att_ref, sc_ref, QUERIES, first, first - HALO, WINDOW,
            extra + first,
        )


def decoder_front_kernel(sc_ref, *refs):
    pieces, refs = refs[:PIECES], refs[PIECES:]
    (qz_ref, vec_ref, cos_ref, sin_ref, x_ref, restored_ref, n1_ref, q_ref, k_ref, v_ref, att_ref,
     w_vmem, x_scr, sems) = refs
    width = x_ref.shape[1]
    wait_all(fetch(sc_ref, pieces, 0, w_vmem.shape[1], w_vmem, sems))
    latent = qz_ref.shape[1]
    restored = mm_nt(qz_ref[...], w_vmem[:, :latent]).astype(bf16)
    restored_ref[...] = restored[CODE_HALO - 16 :]
    both = mm(restored, w_vmem[:, latent : latent + 4 * width])
    bias = vec_ref[7:8]
    now = both[16:, : 2 * width]
    before = pltpu.roll(both[:, 2 * width :], 1, 0)[16:]
    total = now + before
    x = interleave(total[:, :width] + bias, total[:, width:] + bias, x_scr)
    x_ref[...] = x[HALO:]
    w_in = w_vmem.at[:, latent + 4 * width :]
    front(x, vec_ref, 8, w_in, cos_ref, sin_ref, sc_ref, n1_ref, q_ref, k_ref, v_ref,
          att_ref, 0)


def encoder_front_kernel(sc_ref, *refs):
    (pieces,), refs = split_refs(refs, (4,))
    (halo_ref, x_ref, vec_ref, cos_ref, sin_ref, n1_ref, q_ref, k_ref, v_ref, att_ref,
     w_vmem, sems) = refs
    width = x_ref.shape[1]
    copies = fetch(sc_ref, pieces, 0, 3 * width, w_vmem, sems)
    x = jnp.concatenate([halo_ref[...], x_ref[...]], 0).astype(f32)
    wait_all(copies)
    front(x, vec_ref, 0, w_vmem, cos_ref, sin_ref, sc_ref, n1_ref, q_ref, k_ref, v_ref, att_ref,
          EXTRA)


def gelu_both(hidden):
    share = 0.5 * (1.0 + lax.erf(hidden * 0.7071067811865476))
    density = jnp.exp(-0.5 * hidden * hidden) * 0.3989422804014327
    return hidden * share, share + hidden * density


def l2_rows(w, at, chunk, width):
    rows = width // 4
    return jnp.concatenate(
        [
            w[chunk * rows : (chunk + 1) * rows, at + g * width : at + (g + 1) * width]
            for g in range(4)
        ],
        0,
    )


def forward_kernel(base, extra, counts, plan, sc_ref, *refs):
    groups, refs = split_refs(refs, counts)
    (att_ref, x_ref, g_ref, vec_ref,
     out_ref, gmid_ref, datt_ref, n2_ref, active_ref, dh_ref, dtwo_ref, done_ref, vg_ref,
     w_vmem, h_scr, slope_scr, mid_scr, act_scr, sems) = refs
    width = x_ref.shape[1]
    hidden_total = 4 * width
    parts = (
        (0, width),
        (width, width + hidden_total),
        (width + hidden_total, width + 2 * hidden_total),
    )
    copies = [
        fetch(
            sc_ref, groups[plan[i][0]], plan[i][1], high - low, w_vmem.at[:, low:high], sems,
            PIECES * i,
        )
        for i, (low, high) in enumerate(parts)
    ]
    scale_one = vec_ref[base + 2 : base + 3]
    gain_two = vec_ref[base + 3 : base + 4]
    bias_two = vec_ref[base + 4 : base + 5]
    scale_two = vec_ref[base + 5 : base + 6]
    wait_all(copies[0])
    branch = mm(att_ref[...], w_vmem[:, :width])
    middle = x_ref[...].astype(f32) + scale_one * branch
    mid_scr[...] = middle
    normal, scaled = normalize(middle)
    n2 = (normal * gain_two + bias_two).astype(bf16)
    n2_ref[...] = n2[extra:]
    wait_all(copies[1])
    l1_at, l2_at = width, width + hidden_total
    rows = x_ref.shape[0]
    second = None
    for chunk in range(4):
        cols = slice(chunk * width, (chunk + 1) * width)
        h_scr[...] = mm(n2, w_vmem[:, l1_at + chunk * width : l1_at + (chunk + 1) * width])

        def body(i, _):
            at_row = pl.multiple_of(i * 16, 16)
            here = pl.ds(at_row, 16)
            act, slope = gelu_both(h_scr[here, :])
            act_scr[here, cols] = act.astype(bf16)
            slope_scr[here, cols] = slope
            return 0

        lax.fori_loop(0, rows // 16, body, 0)
        if chunk == 0:
            wait_all(copies[2])
        part = mm(act_scr[:, cols], l2_rows(w_vmem, l2_at, chunk, width))
        second = part if second is None else second + part
    active_ref[...] = act_scr[extra:, :]
    out_ref[...] = (mid_scr[...] + scale_two * second).astype(bf16)

    g = g_ref[...].astype(f32)
    vg_ref[3:4, :] = column_sum(g * second[extra:])
    d_two = (g * scale_two).astype(bf16)
    dtwo_ref[...] = d_two
    e = None
    for chunk in range(4):
        cols = slice(chunk * width, (chunk + 1) * width)
        d_active = mm_nt(d_two, l2_rows(w_vmem, l2_at, chunk, width))
        dh_ref[:, cols] = (d_active * slope_scr[extra:, cols]).astype(bf16)
        part = mm_nt(
            dh_ref[:, cols], w_vmem[:, l1_at + chunk * width : l1_at + (chunk + 1) * width]
        )
        e = part if e is None else e + part
    normal, scaled = normal[extra:], scaled[extra:]
    vg_ref[1:2, :] = column_sum(e * normal)
    vg_ref[2:3, :] = column_sum(e)
    g_mid = g + norm_backward(e, normal, scaled, gain_two)
    gmid_ref[...] = g_mid
    vg_ref[0:1, :] = column_sum(g_mid * branch[extra:])
    d_one = (g_mid * scale_one).astype(bf16)
    done_ref[...] = d_one
    datt_ref[...] = mm_nt(d_one, w_vmem[:, :width]).astype(bf16)


def attention_backward_kernel(extra, sc_ref, q_ref, k_ref, v_ref, do_ref,
                              dq_ref, dk_ref, dv_ref, dkh_ref, dvh_ref, dk_scr, dv_scr):
    start, cut = sc_ref[0], sc_ref[1]
    frames = do_ref.shape[0]
    lanes = head_lanes()
    scale = HEAD_DIM ** (-0.5)
    dk_scr[...] = jnp.zeros_like(dk_scr)
    dv_scr[...] = jnp.zeros_like(dv_scr)
    wide = GROUP * QUERIES
    for first in range(0, frames, QUERIES):
        lane = lax.broadcasted_iota(jnp.int32, (1, wide), 1) % QUERIES
        query = start + first + lane
        low = lowest_key(query, cut)
        key = start + first - HALO + lax.broadcasted_iota(jnp.int32, (WINDOW, wide), 0)
        mask = (key <= query) & (key >= low)
        for group in range(HEADS // GROUP):
            cols = slice(group * GROUP * HEAD_DIM, (group + 1) * GROUP * HEAD_DIM)
            qs = stack_heads(q_ref[extra + first : extra + first + QUERIES, cols], lanes)
            ds = stack_heads(do_ref[first : first + QUERIES, cols], lanes)
            kw = k_ref[first : first + WINDOW, cols]
            vw = v_ref[first : first + WINDOW, cols]
            scores = jnp.where(mask, mm_nt(kw, qs) * scale, -1e30)
            exponent = jnp.exp(scores - jnp.max(scores, 0, keepdims=True))
            probs = exponent * (1.0 / jnp.sum(exponent, 0, keepdims=True))
            d_probs = mm_nt(vw, ds)
            mean = jnp.sum(probs * d_probs, 0, keepdims=True)
            d_scores = (probs * (d_probs - mean)).astype(bf16)
            dk_scr[first : first + WINDOW, cols] += mm(d_scores, qs)
            dv_scr[first : first + WINDOW, cols] += mm(probs.astype(bf16), ds)
            dq_ref[first : first + QUERIES, cols] = (
                unstack_heads(mm_tn(d_scores, kw), lanes) * scale
            )
    dk_ref[...] = dk_scr[HALO:] * scale
    dv_ref[...] = dv_scr[HALO:]
    dkh_ref[...] = (dk_scr[:HALO] * scale).astype(bf16)
    dvh_ref[...] = dv_scr[:HALO].astype(bf16)


class Packer:
    def __init__(self, core, refs, shares, order):
        self.core, self.refs, self.shares, self.order = core, refs, shares, order

    def put(self, value, at, step=1, phase=0, block0=0):
        if len(self.refs) == 1:
            if step == 1:
                self.refs[0][:, at : at + value.shape[1]] = value.astype(bf16)
            return
        send, keep = self.refs
        cols = slice(at, at + value.shape[1])
        rows = 16
        hi = self.shares // 8
        blocks = value.shape[0] // (rows * step)
        for pair in range(blocks // 2):
            even = value[(2 * pair * step + phase) * rows :][:rows]
            odd = value[((2 * pair + 1) * step + phase) * rows :][:rows]
            block = (block0 + 2 * pair) // 2
            place = {"x": (block % 2, 2), "lo": (block // 2 % 2, 2), "hi": (block // 4, hi)}
            at_row = 0
            for axis in self.order:
                at_row = at_row * place[axis][1] + place[axis][0]
            at_row = at_row * rows
            first = self.core == 0
            keep[at_row : at_row + rows, cols] = jnp.where(first, even, odd).astype(bf16)
            send[at_row : at_row + rows, cols] = jnp.where(first, odd, even).astype(bf16)

    def put_l2(self, value, at, chunk, width):
        if len(self.refs) == 1:
            cols = slice(at + chunk * width, at + (chunk + 1) * width)
            self.refs[0][:, cols] = value.astype(bf16)
            return
        for phase in range(4):
            self.put(value, at + phase * width, 4, phase, chunk * width // 64)


def weight_gradients_kernel(extra, shares, order, sc_ref, n2_ref, active_ref, dh_ref, dtwo_ref,
                            *rest):
    att_ref = None
    if not extra:
        att_ref, done_ref, *rest = rest
    width = n2_ref.shape[1]
    pack = Packer(sc_ref[2], rest, shares, order)
    for chunk in range(4):
        cols = slice(chunk * width, (chunk + 1) * width)
        pack.put(mm_tn(n2_ref[...], dh_ref[:, cols]), chunk * width)
        pack.put_l2(mm_tn(active_ref[:, cols], dtwo_ref[...]), 4 * width, chunk, width)
    if att_ref is not None:
        pack.put(mm_tn(att_ref[...], done_ref[...]), 8 * width)


def layer_input_gradient(extra_rows, base, dq_ref, dk_ref, dv_ref, dkh_ref, dvh_ref, x, gmid_ref,
                         w_in, vec_ref, cos_ref, sin_ref, dmix_ref, vg_ref):
    frames, width = dq_ref.shape
    later = frames - HALO
    cos, sin = cos_ref[HALO:], -sin_ref[HALO:]
    for at in range(0, width, 128):
        cols = slice(at, at + 128)
        dmix_ref[:, cols] = rotate(dq_ref[:, cols], cos, sin).astype(bf16)
        keys = dk_ref[:, cols]
        keys = jnp.concatenate([keys[:later], keys[later:] + dkh_ref[:, cols].astype(f32)], 0)
        dmix_ref[:, width + at : width + at + 128] = rotate(keys, cos, sin).astype(bf16)
        values = dv_ref[:, cols]
        values = jnp.concatenate([values[:later], values[later:] + dvh_ref[:, cols].astype(f32)], 0)
        dmix_ref[:, 2 * width + at : 2 * width + at + 128] = values.astype(bf16)
    d_normed = mm_nt(dmix_ref[...], w_in[...])
    normal, scaled = normalize(x)
    vg_ref[0:1, :] = column_sum(d_normed * normal)
    vg_ref[1:2, :] = column_sum(d_normed)
    return gmid_ref[...] + norm_backward(d_normed, normal, scaled, vec_ref[base : base + 1])


def decoder_back_kernel(at, sc_ref, *refs):
    pieces, refs = refs[:PIECES], refs[PIECES:]
    (dq_ref, dk_ref, dv_ref, dkh_ref, dvh_ref, x_ref, gmid_ref, vec_ref, cos_ref, sin_ref,
     dup_ref, dmix_ref, vg_ref, w_vmem, sems) = refs
    wait_all(fetch(sc_ref, pieces, at, w_vmem.shape[1], w_vmem, sems))
    grad = layer_input_gradient(
        0, 8, dq_ref, dk_ref, dv_ref, dkh_ref, dvh_ref, x_ref[...], gmid_ref, w_vmem, vec_ref,
        cos_ref, sin_ref, dmix_ref, vg_ref,
    )
    vg_ref[2:3, :] = column_sum(grad)
    dup_ref[...] = grad.astype(bf16)


def encoder_back_kernel(shares, sc_ref, *refs):
    (pieces,), refs = split_refs(refs, (4,))
    (dq_ref, dk_ref, dv_ref, dkh_ref, dvh_ref, x_ref, gmid_ref, vec_ref, cos_ref, sin_ref, n1_ref,
     vgs_ref, att_ref, done_ref, win_ref, dred_ref, red_ref, dlat_ref, grad_ref, *rest) = refs
    refs, (w_vmem, dmix_scr, vg_scr, all_scr, sems) = rest[:-5], rest[-5:]
    width = x_ref.shape[1]
    wait_all(fetch(sc_ref, pieces, 0, w_vmem.shape[1], w_vmem, sems))
    grad = layer_input_gradient(
        0, 0, dq_ref, dk_ref, dv_ref, dkh_ref, dvh_ref, x_ref[...].astype(f32), gmid_ref, w_vmem,
        vec_ref, cos_ref, sin_ref, dmix_scr, vg_scr,
    )
    grad_ref[...] = grad.astype(bf16)
    pack = Packer(sc_ref[2], refs, shares, ORDER_D)
    for part in range(3):
        cols = slice(part * width, (part + 1) * width)
        pack.put(mm_tn(n1_ref[...], dmix_scr[:, cols]), part * width)
    all_scr[...] = jnp.zeros_like(all_scr)
    all_scr[0:2, :] = vg_scr[0:2, :]
    all_scr[2:6, :] = vgs_ref[0:4, :]
    all_scr[6:7, :] = vgs_ref[16:17, :]
    all_scr[7:8, :] = vgs_ref[26:27, :]
    all_scr[8:10, :] = vgs_ref[24:26, :]
    all_scr[10:14, :] = vgs_ref[8:12, :]
    pack.put(mm_tn(att_ref[EXTRA:, :], done_ref[...]), 3 * width)
    d_reduced = dred_ref[...]
    for tap in range(4):
        pack.put(mm_tn(win_ref[tap], d_reduced), (4 + tap) * width)
    pack.put(mm_tn(red_ref[...], dlat_ref[...]), 8 * width)
    pack.put(all_scr[...].T, 8 * width + dlat_ref.shape[1])


def middle_kernel(shares, sc_ref, *refs):
    (pieces, more), refs = split_refs(refs, (6, 4))
    (dup_ref, next_ref, dmix_ref, n1_ref, restored_ref, qz_ref,
     denc_ref, dred_ref, dlat_ref, vg_ref, *rest) = refs
    refs, (up_vmem, down_vmem, frame_scr, sems) = rest[:-4], rest[-4:]
    frames, width = dup_ref.shape
    latent = qz_ref.shape[1]
    codec = frames // 2
    copies = [
        fetch(sc_ref, pieces, 0, latent + 4 * width, up_vmem, sems),
        fetch(sc_ref, more, 0, 4 * width + latent, down_vmem, sems, PIECES),
    ]
    pairs = codec + 16
    even, odd = split_rows(
        jnp.concatenate([dup_ref[...], next_ref[...]], 0).astype(f32), frame_scr
    )
    both = jnp.concatenate([even, odd], 1).astype(bf16)
    wait_all(copies[0])
    up = up_vmem[:, latent : latent + 4 * width]
    here = mm_nt(both, up[:, : 2 * width])
    later = mm_nt(both, up[:, 2 * width :])
    d_restored = (here + pltpu.roll(later, pairs - 1, 0)).astype(bf16)
    d_latent = mm(d_restored, up_vmem[:, :latent]).astype(bf16)
    wait_all(copies[1])
    d_reduced = mm_nt(d_latent, down_vmem[:, 4 * width :]).astype(bf16)
    dlat_ref[...] = d_latent[:codec]
    dred_ref[...] = d_reduced[:codec]
    vg_ref[0:1, :] = column_sum(d_reduced[:codec].astype(f32))
    taps = [mm_nt(d_reduced, down_vmem[:, tap * width : (tap + 1) * width]) for tap in range(4)]
    denc_ref[...] = interleave(
        taps[2] + pltpu.roll(taps[0], pairs - 1, 0),
        taps[3] + pltpu.roll(taps[1], pairs - 1, 0),
        frame_scr,
    )[:frames]

    pack = Packer(sc_ref[2], refs, shares, ORDER_B)
    for part in range(3):
        cols = slice(part * width, (part + 1) * width)
        pack.put(mm_tn(n1_ref[...], dmix_ref[:, cols]), part * width)
    restored = restored_ref[...]
    own_pairs = both[:codec]
    before = pltpu.roll(restored.astype(f32), 1, 0)[16:].astype(bf16)
    pack.put(mm_tn(restored[16:], own_pairs[:, :width]), 3 * width)
    pack.put(mm_tn(restored[16:], own_pairs[:, width:]), 4 * width)
    pack.put(mm_tn(before, own_pairs[:, :width]), 5 * width)
    pack.put(mm_tn(before, own_pairs[:, width:]), 6 * width)
    pack.put(mm_tn(d_restored[:codec], qz_ref[CODE_HALO:, :]), 7 * width)


def latent_kernel(sc_ref, *refs):
    (pieces,), refs = split_refs(refs, (4,))
    (enc_ref, rows_ref, vec_ref, res_ref, win_ref, red_ref, w_vmem, frame_scr, sems) = refs
    total, width = enc_ref.shape
    copies = fetch(sc_ref, pieces, 0, w_vmem.shape[1], w_vmem, sems)
    inside = (sc_ref[0] > 0).astype(f32)
    rim = enc_ref[:EXTRA].astype(f32) * inside
    skip = EXTRA // 2
    even, odd = split_rows(jnp.concatenate([rim, enc_ref[EXTRA:].astype(f32)], 0), frame_scr)
    win_ref[0] = pltpu.roll(even, 1, 0)[skip:].astype(bf16)
    win_ref[1] = pltpu.roll(odd, 1, 0)[skip:].astype(bf16)
    win_ref[2] = even[skip:].astype(bf16)
    win_ref[3] = odd[skip:].astype(bf16)
    wait_all(copies)
    reduced = vec_ref[6:7]
    for tap in range(4):
        reduced = reduced + mm(win_ref[tap], w_vmem[:, tap * width : (tap + 1) * width])
    reduced = reduced.astype(bf16)
    red_ref[...] = reduced
    remaining = mm(reduced, w_vmem[:, 4 * width :])
    for level in range(rows_ref.shape[0]):
        res_ref[level] = remaining.astype(bf16)
        remaining = remaining - rows_ref[level].astype(f32)


def lookup_kernel(sc_ref, codes_ref, book_ref, qsend_ref, qkeep_ref, rsend_ref, rkeep_ref, q_scr):
    levels, share, latent = book_ref.shape
    total = codes_ref.shape[0]
    codec = total // 4
    base = sc_ref[3]
    core = sc_ref[2]
    entry = lax.broadcasted_iota(jnp.int32, (1, share), 1)
    for level in range(levels):
        picks = (codes_ref[:, level : level + 1] - base == entry).astype(f32).astype(bf16)
        found = mm(picks, book_ref[level])
        q_scr[CODE_HALO:] = found if level == 0 else q_scr[CODE_HALO:] + found
        for x in range(2):
            even = found[(2 * x) * codec :][:codec]
            odd = found[(2 * x + 1) * codec :][:codec]
            rkeep_ref[x, level] = jnp.where(core == 0, even, odd).astype(bf16)
            rsend_ref[x, level] = jnp.where(core == 0, odd, even).astype(bf16)
    q_scr[:CODE_HALO] = jnp.zeros((CODE_HALO, latent), f32)
    for x in range(2):
        even = q_scr[(2 * x) * codec : (2 * x + 1) * codec + CODE_HALO]
        odd = q_scr[(2 * x + 1) * codec : (2 * x + 2) * codec + CODE_HALO]
        qkeep_ref[x] = jnp.where(core == 0, even, odd)
        qsend_ref[x] = jnp.where(core == 0, odd, even)


def collect_kernel(share, sc_ref, own_ref, x_ref, core_ref, far_ref, frame_ref, codes_ref, entry_ref,
                   dead_ref, place_ref, send_ref, keep_ref, cnt_scr):
    levels = codes_ref.shape[0]
    latent = own_ref.shape[2]
    total = codes_ref.shape[1]
    lo = sc_ref[4]
    high = send_ref.shape[0]
    frame = frame_ref[0:1, :]
    ones = jnp.ones((16, total), bf16)
    for level in range(levels):
        used = (entry_ref[:, level : level + 1] == codes_ref[level : level + 1, :]).astype(f32)
        placed = (place_ref[:, level : level + 1] == frame).astype(f32)
        select = jnp.where(dead_ref[:, level : level + 1] == 1, placed, used).astype(bf16)
        rows = jnp.concatenate([ref[level] for ref in (own_ref, x_ref, core_ref, far_ref)], 0)
        sums = mm(select, rows)
        cnt_scr[level : level + 1, :] = mm_nt(ones, used.astype(bf16))[0:1]
        at = slice(level * share, (level + 1) * share)
        for h in range(high):
            even = sums[(2 * h) * share :][:share]
            odd = sums[(2 * h + 1) * share :][:share]
            keep_ref[h, at, :] = jnp.where(lo == 0, even, odd).astype(bf16)
            send_ref[h, at, :] = jnp.where(lo == 0, odd, even).astype(bf16)
    counts = cnt_scr[...]
    upper = jnp.floor(counts * (1.0 / 128.0))
    digits = jnp.concatenate([upper, counts - 128.0 * upper], 0)
    tail = slice(levels * share, levels * share + 2 * levels)
    for h in range(high):
        even = digits[:, (2 * h) * share : (2 * h + 1) * share]
        odd = digits[:, (2 * h + 1) * share : (2 * h + 2) * share]
        keep_ref[h, tail, :] = jnp.zeros((2 * levels, latent), bf16)
        send_ref[h, tail, :] = jnp.zeros((2 * levels, latent), bf16)
        keep_ref[h, tail, :share] = jnp.where(lo == 0, even, odd).astype(bf16)
        send_ref[h, tail, :share] = jnp.where(lo == 0, odd, even).astype(bf16)


def call(kernel, outs, spaces, scratch, args):
    title = getattr(kernel, "func", kernel).__name__
    where = {"s": pltpu.SMEM, "v": pltpu.VMEM, "a": pl.ANY}
    return pl.pallas_call(
        kernel,
        name=title,
        out_shape=outs,
        in_specs=[pl.BlockSpec(memory_space=where[s]) for s in spaces],
        out_specs=[pl.BlockSpec(memory_space=pltpu.VMEM) for _ in outs],
        scratch_shapes=scratch,
        compiler_params=pltpu.CompilerParams(vmem_limit_bytes=VMEM_LIMIT),
        cost_estimate=pl.CostEstimate(flops=1, bytes_accessed=1, transcendentals=0),
    )(*args)


def shape(dims, dtype=f32):
    return jax.ShapeDtypeStruct(dims, dtype)


def halve(block, dim, axis):
    mine = lax.axis_index(axis)
    sent = lax.dynamic_index_in_dim(block, 1 - mine, dim, False)
    kept = lax.dynamic_index_in_dim(block, mine, dim, False)
    got = lax.ppermute(sent, axis, [(0, 1), (1, 0)])
    return (kept.astype(f32) + got.astype(f32)).astype(block.dtype)


def swap_add(send, keep, axis):
    got = lax.ppermute(send, axis, [(0, 1), (1, 0)])
    return (keep.astype(f32) + got.astype(f32)).astype(keep.dtype)


def sum_over_hi(block):
    parts = lax.all_to_all(block, "hi", 0, 0, tiled=True)
    return jnp.sum(parts.astype(f32), 0)


def shifted(block, distance):
    devices = range(lax.axis_size(SEQ))
    route = [(i - distance, i) for i in devices if i - distance in devices]
    return lax.ppermute(block, SEQ, route)


def packed_outs(width_total, width, shares):
    if width // shares % 16 == 0:
        return [shape((width // 2, width_total), bf16)] * 2
    return [shape((width, width_total), bf16)]


def swap(block, axis):
    return lax.ppermute(block, axis, [(0, 1), (1, 0)])


def tie(*values):
    return lax.optimization_barrier(values)


def near_half(share):
    rows = share.shape[0] // 2
    half = lax.dynamic_slice_in_dim(share, lax.axis_index("lo") * rows, rows, 0)
    return swap(half, "x")


def spread(share, near):
    far = swap(near, "lo")
    return [share, near, far, swap(share, "core"), swap(near, "core"), swap(far, "core")]


def spread_whole(share, near):
    return [share, near, swap(share, "core"), swap(near, "core")]


def unfolded_rows(block, shares, l2_at):
    width = block.shape[0]
    full = [block[:, l2_at + i * width : l2_at + (i + 1) * width] for i in range(4)]
    full = jnp.concatenate(full, 0).reshape(shares, 4, width // shares, width)
    full = full.transpose(0, 2, 1, 3).reshape(width, 4 * width)
    return jnp.concatenate([block[:, :l2_at], full, block[:, l2_at + 4 * width :]], 1)


def first_sum(parts, shares, order, l2_at=None):
    if len(parts) == 2:
        return swap_add(*parts, "core")
    (block,) = parts
    if l2_at is not None:
        block = unfolded_rows(block, shares, l2_at)
    width, total = block.shape
    block = block.reshape(shares // 8, 2, 2, 2, width // shares, total)
    block = halve(block, 3, "core")
    places = [("hi", "lo", "x").index(axis) for axis in order]
    return block.transpose(*places, 3, 4).reshape(width // 2, total)


def next_sum(block, axis):
    rows, total = block.shape
    return halve(block.reshape(2, rows // 2, total), 0, axis)


def last_sum(block, high):
    return sum_over_hi(block.reshape(high, -1, block.shape[1]))


def local(
    activations,
    encoder_attention_norm_gain,
    encoder_attention_norm_bias,
    encoder_query_key_value_weight,
    encoder_attention_output_weight,
    encoder_attention_layer_scale,
    encoder_forward_norm_gain,
    encoder_forward_norm_bias,
    encoder_forward_input_weight,
    encoder_forward_output_weight,
    encoder_forward_layer_scale,
    strided_convolution_weight,
    strided_convolution_bias,
    quantizer_input_weight,
    codebook,
    quantizer_output_weight,
    transposed_convolution_weight,
    transposed_convolution_bias,
    decoder_attention_norm_gain,
    decoder_attention_norm_bias,
    decoder_query_key_value_weight,
    decoder_attention_output_weight,
    decoder_attention_layer_scale,
    decoder_forward_norm_gain,
    decoder_forward_norm_bias,
    decoder_forward_input_weight,
    decoder_forward_output_weight,
    decoder_forward_layer_scale,
    cotangent,
    frame_segment_index,
    frame_code_index,
    replace_code_mask,
    replacing_batch_position,
    code_usage_average,
    code_latent_sum_average,
):
    batch_rows, frames, width = activations.shape
    assert batch_rows == 1
    seq_index = lax.axis_index(SEQ)
    seq_count = lax.axis_size(SEQ)
    dp_index = lax.axis_index(DP)
    dp_count = lax.axis_size(DP)
    shares = dp_count * seq_count
    codec = frames // 2
    levels = frame_code_index.shape[2]
    latent = codebook.shape[2]
    book_share = codebook.shape[1]
    core_index = lax.axis_index("core")

    x_index, lo_index = lax.axis_index("x"), lax.axis_index("lo")
    rows_share = width // seq_count

    row_codes = lax.all_gather(frame_code_index[0], SEQ, axis=0, tiled=False)
    cut = jnp.sum((frame_segment_index[0] == 0).astype(jnp.int32))
    order = [2 * x_index + core_index, 2 * (1 - x_index) + core_index]
    order += [2 * x_index + 1 - core_index, 2 * (1 - x_index) + 1 - core_index]
    half_rows = rows_share // 2
    near, far = lo_index * half_rows, (1 - lo_index) * half_rows
    scalars = jnp.stack(
        [
            seq_index * frames,
            cut,
            core_index,
            seq_index * book_share,
            lo_index,
            seq_index,
            seq_index,
            seq_index,
            order[0] * rows_share,
            order[1] * rows_share + near,
            order[1] * rows_share + far,
            order[2] * rows_share,
            order[3] * rows_share + near,
            order[3] * rows_share + far,
            order[0] * rows_share,
            order[1] * rows_share,
            order[2] * rows_share,
            order[3] * rows_share,
        ]
    ).astype(jnp.int32)

    def flat_taps(taps):
        return taps.transpose(1, 0, 2).reshape(taps.shape[1], -1)

    first_pack = jnp.concatenate(
        [
            quantizer_output_weight.T,
            flat_taps(transposed_convolution_weight),
            decoder_query_key_value_weight,
        ],
        1,
    )
    near_one = near_half(first_pack)
    dec_one = spread(first_pack, near_one)
    out_share, l1_share, l2_share = (
        decoder_attention_output_weight,
        decoder_forward_input_weight,
        decoder_forward_output_weight,
    )

    def fold_l2(share):
        return share.reshape(4, -1, width).transpose(1, 0, 2).reshape(-1, 4 * width)

    second_pack = jnp.concatenate([out_share, l1_share, fold_l2(l2_share)], 1)
    second_pack, near_one = tie(second_pack, near_one)
    near_two = near_half(second_pack)
    dec_two = spread(second_pack, near_two)
    vectors = jnp.stack(
        [
            encoder_attention_norm_gain,
            encoder_attention_norm_bias,
            encoder_attention_layer_scale,
            encoder_forward_norm_gain,
            encoder_forward_norm_bias,
            encoder_forward_layer_scale,
            strided_convolution_bias,
            transposed_convolution_bias,
            decoder_attention_norm_gain,
            decoder_attention_norm_bias,
            decoder_attention_layer_scale,
            decoder_forward_norm_gain,
            decoder_forward_norm_bias,
            decoder_forward_layer_scale,
        ]
    )
    vectors = jnp.pad(vectors, ((0, 2), (0, 0)))
    vectors = lax.all_gather(vectors, SEQ, axis=1, tiled=True).astype(f32)
    pack_in = jnp.concatenate(
        [encoder_query_key_value_weight, encoder_attention_output_weight], 1
    )
    pack_down = jnp.concatenate(
        [flat_taps(strided_convolution_weight), quantizer_input_weight], 1
    )
    pack_l1 = encoder_forward_input_weight
    pack_l2 = fold_l2(encoder_forward_output_weight)
    pack_in, near_two = tie(pack_in, near_two)
    near_in = swap(pack_in, "x")

    positions = seq_index * frames - HALO + jnp.arange(HALO + frames, dtype=jnp.int32)
    half_dim = HEAD_DIM // 2
    frequency = jnp.power(10000.0, -jnp.arange(half_dim, dtype=f32) / half_dim)
    angles = positions.astype(f32)[:, None] * frequency[None, :]
    cos, sin = jnp.cos(angles), jnp.sin(angles)
    cos_table = jnp.concatenate([cos] * 4, 1)
    sin_table = jnp.concatenate([-sin, sin, -sin, sin], 1)
    activation_halo = shifted(activations[0, frames - HALO :], 1)

    window = codec + CODE_HALO
    qsend, qkeep, rsend, rkeep = call(
        lookup_kernel,
        [shape((2, window, latent))] * 2 + [shape((2, levels, codec, latent), bf16)] * 2,
        "svv",
        [pltpu.VMEM((CODE_HALO + codec * seq_count, latent), f32)],
        (scalars, row_codes.reshape(-1, levels), codebook),
    )
    quantized = halve(swap_add(qsend, qkeep, "core"), 0, "x").astype(bf16)

    code_total = replace_code_mask.shape[1]
    code_share = code_usage_average.shape[1]
    row_frames = codec * seq_count
    dead_flag = replace_code_mask == 1

    def seq_part(array):
        return lax.dynamic_index_in_dim(
            array.reshape(levels, dp_count, seq_count, code_share), seq_index, 2, False
        ).reshape(levels, dp_count * code_share)

    part_dead = seq_part(replace_code_mask)
    part_place = seq_part(replacing_batch_position)
    part_place = jnp.where(part_place // row_frames == dp_index, part_place % row_frames, -1)
    part_code = seq_part(
        jnp.broadcast_to(jnp.arange(code_total, dtype=jnp.int32), (levels, code_total))
    )
    relative_codes = jnp.concatenate([row_codes[i] for i in order], 0).T
    relative_frames = jnp.concatenate(
        [i * codec + jnp.arange(codec, dtype=jnp.int32) for i in order]
    )[None]
    entry_t, dead_t, place_t = part_code.T, part_dead.T, part_place.T
    e_x = jnp.concatenate([activation_halo[HALO - EXTRA :], activations[0]], 0)
    (quantized, cos_table, sin_table, entry_t, dead_t, place_t, relative_codes, relative_frames, e_x,
     dead_flag) = tie(
        quantized, cos_table, sin_table, entry_t, dead_t, place_t, relative_codes, relative_frames,
        e_x, dead_flag
    )

    total_frames = HALO + frames

    d_x, restored, d_n1, d_q, d_k, d_v, d_att = call(
        decoder_front_kernel,
        [
            shape((frames, width)),
            shape((codec + 16, width), bf16),
            shape((frames, width), bf16),
            shape((frames, width), bf16),
            shape((total_frames, width), bf16),
            shape((total_frames, width), bf16),
            shape((frames, width), bf16),
        ],
        "s" + "a" * PIECES + "vvvv",
        [
            pltpu.VMEM((width, first_pack.shape[1]), bf16),
            pltpu.VMEM((width // 128, total_frames, 128), f32),
            pltpu.SemaphoreType.DMA((PIECES,)),
        ],
        (scalars, *dec_one, quantized, vectors, cos_table, sin_table),
    )

    d_att, near_in, pack_down = tie(d_att, near_in, pack_down)
    near_down = swap(pack_down, "x")

    def feed_forward(base, extra, att, x, g, weights, plan):
        rows = frames + extra
        return call(
            partial(forward_kernel, base, extra, tuple(len(w) for w in weights), plan),
            [
                shape((rows, width), bf16),
                shape((frames, width)),
                shape((frames, width), bf16),
                shape((frames, width), bf16),
                shape((frames, 4 * width), bf16),
                shape((frames, 4 * width), bf16),
                shape((frames, width), bf16),
                shape((frames, width), bf16),
                shape((8, width)),
            ],
            "s" + "a" * sum(len(w) for w in weights) + "vvvv",
            [
                pltpu.VMEM((width, 9 * width), bf16),
                pltpu.VMEM((rows, width), f32),
                pltpu.VMEM((rows, 4 * width), f32),
                pltpu.VMEM((rows, width), f32),
                pltpu.VMEM((rows, 4 * width), bf16),
                pltpu.SemaphoreType.DMA((3 * PIECES,)),
            ],
            (scalars, *sum(weights, []), att, x, g, vectors),
        )

    def attention_backward(extra, q, k, v, do):
        return call(
            partial(attention_backward_kernel, extra),
            [shape((frames, width))] * 3 + [shape((HALO, width), bf16)] * 2,
            "svvvv",
            [pltpu.VMEM((total_frames, width), f32)] * 2,
            (scalars, q, k, v, do),
        )

    (output, d_gmid, d_datt, d_n2, d_active, d_dh, d_dtwo, d_done, d_vg_two) = feed_forward(
        8, 0, d_att, d_x, cotangent[0], [dec_two], ((0, 0), (0, width), (0, 5 * width))
    )
    d_datt, near_down, pack_l1 = tie(d_datt, near_down, pack_l1)
    near_l1 = swap(pack_l1, "x")
    enc_down = spread_whole(pack_down, near_down)
    d_dq, d_dk, d_dv, d_dkh, d_dvh = attention_backward(0, d_q, d_k, d_v, d_datt)
    d_n2, d_dkh, d_dvh = tie(d_n2, d_dkh, d_dvh)
    d_dkh, d_dvh = shifted(d_dkh, -1), shifted(d_dvh, -1)
    group_a = call(
        partial(weight_gradients_kernel, 0, shares, ORDER_A),
        packed_outs(9 * width, width, shares),
        "svvvvvv",
        [],
        (scalars, d_n2, d_active, d_dh, d_dtwo, d_att, d_done),
    )
    d_dq, near_l1, pack_l2, *group_a = tie(d_dq, near_l1, pack_l2, *group_a)
    near_l2 = swap(pack_l2, "x")
    enc_l1 = spread_whole(pack_l1, near_l1)
    a_sum = first_sum(group_a, shares, ORDER_A, 4 * width)
    in_at = latent + 4 * width
    d_up, d_mixed, d_vg_one = call(
        partial(decoder_back_kernel, in_at),
        [shape((frames, width), bf16), shape((frames, 3 * width), bf16), shape((8, width))],
        "s" + "a" * PIECES + "v" * 10,
        [pltpu.VMEM((width, 3 * width), bf16), pltpu.SemaphoreType.DMA((PIECES,))],
        (
            scalars, *dec_one, d_dq, d_dk, d_dv, d_dkh, d_dvh, d_x, d_gmid, vectors, cos_table,
            sin_table,
        ),
    )
    d_up_next = shifted(d_up[:32], -1)

    enc_in = spread_whole(pack_in, near_in)
    activation_halo, a_sum, d_up = tie(activation_halo, a_sum, d_up)
    e_n1, e_q, e_k, e_v, e_att = call(
        encoder_front_kernel,
        [
            shape((frames, width), bf16),
            shape((frames + EXTRA, width), bf16),
            shape((total_frames, width), bf16),
            shape((total_frames, width), bf16),
            shape((frames + EXTRA, width), bf16),
        ],
        "s" + "a" * 4 + "vvvvv",
        [pltpu.VMEM((width, 3 * width), bf16), pltpu.SemaphoreType.DMA((PIECES,))],
        (scalars, *enc_in, activation_halo, activations[0], vectors, cos_table, sin_table),
    )

    d_mixed, e_n1, near_l2 = tie(d_mixed, e_n1, near_l2)
    enc_l2 = spread_whole(pack_l2, near_l2)
    middle_outs = call(
        partial(middle_kernel, shares),
        [
            shape((frames, width)),
            shape((codec, width), bf16),
            shape((codec, latent), bf16),
            shape((8, width)),
        ]
        + packed_outs(7 * width + latent, width, shares),
        "s" + "a" * 10 + "v" * 6,
        [
            pltpu.VMEM((width, latent + 4 * width), bf16),
            pltpu.VMEM((width, latent + 4 * width), bf16),
            pltpu.VMEM((width // 128, frames + 32, 128), f32),
            pltpu.SemaphoreType.DMA((2 * PIECES,)),
        ],
        (
            scalars, *dec_one, *enc_down, d_up, d_up_next, d_mixed, d_n1, restored, quantized,
        ),
    )
    d_encoded, d_reduced, d_latent, m_vg = middle_outs[:4]
    b_sum = first_sum(middle_outs[4:], shares, ORDER_B)
    a_sum = next_sum(a_sum, ORDER_A[0])

    (encoded, e_gmid, e_datt, e_n2, e_active, e_dh, e_dtwo, e_done, e_vg_two) = feed_forward(
        0, EXTRA, e_att, e_x, d_encoded, [enc_in, enc_l1, enc_l2],
        ((0, 3 * width), (1, 0), (2, 0)),
    )
    code_rows = halve(swap_add(rsend, rkeep, "core"), 0, "x")
    encoded, b_sum = tie(encoded, b_sum)
    residuals, windows, reduced = call(
        latent_kernel,
        [
            shape((levels, codec, latent), bf16),
            shape((4, codec, width), bf16),
            shape((codec, width), bf16),
        ],
        "s" + "a" * 4 + "vvv",
        [
            pltpu.VMEM((width, 4 * width + latent), bf16),
            pltpu.VMEM((width // 128, frames + EXTRA, 128), f32),
            pltpu.SemaphoreType.DMA((PIECES,)),
        ],
        (scalars, *enc_down, encoded, code_rows, vectors),
    )
    e_datt, a_sum, residuals = tie(e_datt, a_sum, residuals)
    e_dq, e_dk, e_dv, e_dkh, e_dvh = attention_backward(EXTRA, e_q, e_k, e_v, e_datt)
    e_n2, e_dkh, e_dvh = tie(e_n2, e_dkh, e_dvh)
    e_dkh, e_dvh = shifted(e_dkh, -1), shifted(e_dvh, -1)
    group_c = call(
        partial(weight_gradients_kernel, EXTRA, shares, ORDER_C),
        packed_outs(8 * width, width, shares),
        "svvvv",
        [],
        (scalars, e_n2, e_active, e_dh, e_dtwo),
    )
    e_dq, *group_c = tie(e_dq, *group_c)
    c_sum = first_sum(group_c, shares, ORDER_C, 4 * width)
    a_sum = next_sum(a_sum, ORDER_A[1])
    vector_grads = jnp.concatenate([e_vg_two, d_vg_two, m_vg, d_vg_one], 0)
    back_outs = call(
        partial(encoder_back_kernel, shares),
        [shape((frames, width), bf16)] + packed_outs(8 * width + latent + 128, width, shares),
        "s" + "a" * 4 + "v" * 18,
        [
            pltpu.VMEM((width, 3 * width), bf16),
            pltpu.VMEM((frames, 3 * width), bf16),
            pltpu.VMEM((8, width), f32),
            pltpu.VMEM((128, width), f32),
            pltpu.SemaphoreType.DMA((PIECES,)),
        ],
        (
            scalars, *enc_in, e_dq, e_dk, e_dv, e_dkh, e_dvh, activations[0], e_gmid, vectors,
            cos_table, sin_table, e_n1, vector_grads, e_att, e_done, windows, d_reduced, reduced,
            d_latent,
        ),
    )
    high = shares // 8
    d_sum = first_sum(back_outs[1:], shares, ORDER_D)
    b_sum = last_sum(b_sum, high).astype(bf16)
    grads_a = last_sum(a_sum, high)
    c_sum = next_sum(c_sum, ORDER_C[0])
    d_sum = next_sum(d_sum, ORDER_D[0])
    b_sum = next_sum(b_sum, ORDER_B[1])
    c_sum = next_sum(c_sum, ORDER_C[1])
    d_sum = next_sum(d_sum, ORDER_D[1])
    grads_b = next_sum(b_sum, ORDER_B[2]).astype(f32)
    grads_c = last_sum(c_sum, high)
    grads_d = last_sum(d_sum, high)

    near_res = swap(residuals, "x")
    res_pieces = [residuals, near_res, swap(residuals, "core"), swap(near_res, "core")]
    if code_share % 16 == 0:
        tail_rows = levels * code_share
        csend, ckeep = call(
            partial(collect_kernel, code_share),
            [shape((dp_count // 2, tail_rows + 2 * levels, latent), bf16)] * 2,
            "s" + "v" * 9,
            [pltpu.VMEM((levels, dp_count * code_share), f32)],
            (scalars, *res_pieces, relative_frames, relative_codes, entry_t, dead_t, place_t),
        )
        combined = sum_over_hi(swap_add(csend, ckeep, "lo"))
        summed = combined[:tail_rows].reshape(levels, code_share, latent)
        digits = combined[tail_rows:, :code_share]
        counted = 128.0 * digits[:levels] + digits[levels:]
    else:
        flat_res = jnp.concatenate(res_pieces, 1)
        used = part_code[:, :, None] == relative_codes[:, None, :]
        placed = part_place[:, :, None] == relative_frames[None]
        counts = jnp.sum(used.astype(f32), 2).reshape(levels, dp_count, code_share)
        selects = jnp.where(part_dead[:, :, None] == 1, placed, used).astype(bf16)
        sums = jnp.einsum("lct,ltd->lcd", selects, flat_res, preferred_element_type=f32)
        sums = sums.astype(bf16).reshape(levels, dp_count, code_share, latent)
        summed = lax.psum_scatter(sums, DP, scatter_dimension=1, tiled=False).astype(f32)
        counted = lax.psum_scatter(counts, DP, scatter_dimension=1, tiled=False)
    owner_flag = lax.dynamic_slice_in_dim(
        dead_flag, lax.axis_index(DP + SEQ) * code_share, code_share, 1
    )
    new_cluster_size = ema_decay * code_usage_average + (1.0 - ema_decay) * counted
    new_embed_sum = jnp.where(
        owner_flag[:, :, None],
        summed * new_cluster_size[:, :, None],
        ema_decay * code_latent_sum_average + (1.0 - ema_decay) * summed,
    )
    new_codebook = new_embed_sum / new_cluster_size[:, :, None]

    def columns(block, at, count):
        return block[:, at * width : (at + count) * width]

    def taps(block):
        return block.reshape(-1, 4, width).transpose(1, 0, 2)

    def unfold(block):
        return block.reshape(-1, 4, width).transpose(1, 0, 2).reshape(-1, width)

    vec_at = 8 * width + latent
    vec = grads_d[:, vec_at : vec_at + 16].T
    return (
        output[None],
        back_outs[0][None],
        vec[0],
        vec[1],
        columns(grads_d, 0, 3),
        columns(grads_d, 3, 1),
        vec[2],
        vec[3],
        vec[4],
        columns(grads_c, 0, 4),
        unfold(columns(grads_c, 4, 4)),
        vec[5],
        taps(columns(grads_d, 4, 4)),
        vec[6],
        grads_d[:, 8 * width : 8 * width + latent],
        grads_b[:, 7 * width :].T,
        taps(columns(grads_b, 3, 4)),
        vec[7],
        vec[8],
        vec[9],
        columns(grads_b, 0, 3),
        columns(grads_a, 8, 1),
        vec[10],
        vec[11],
        vec[12],
        columns(grads_a, 0, 4),
        unfold(columns(grads_a, 4, 4)),
        vec[13],
        new_cluster_size,
        new_embed_sum,
        new_codebook,
    )


def solution(mesh):
    grid = mesh.devices
    mesh = jax.sharding.Mesh(
        grid.reshape(grid.shape[0] // 2, 2, grid.shape[1] // 2, 2), ("hi", "lo", "x", "core")
    )
    placed = (
        P(DP, SEQ, None),
        P(SEQ),
        P(SEQ),
        P(SEQ, None),
        P(SEQ, None),
        P(SEQ),
        P(SEQ),
        P(SEQ),
        P(SEQ, None),
        P(SEQ, None),
        P(SEQ),
        P(None, SEQ, None),
        P(SEQ),
        P(SEQ, None),
        P(None, SEQ, None),
        P(None, SEQ),
        P(None, SEQ, None),
        P(SEQ),
        P(SEQ),
        P(SEQ),
        P(SEQ, None),
        P(SEQ, None),
        P(SEQ),
        P(SEQ),
        P(SEQ),
        P(SEQ, None),
        P(SEQ, None),
        P(SEQ),
        P(DP, SEQ, None),
        P(DP, None),
        P(DP, SEQ, None),
        P(),
        P(),
        P(None, DP + SEQ),
        P(None, DP + SEQ, None),
    )
    return jax.shard_map(
        local,
        mesh=mesh,
        in_specs=placed,
        out_specs=(
            P(DP, SEQ, None),
            P(DP, SEQ, None),
            P(DP + SEQ),
            P(DP + SEQ),
            P(DP + SEQ, None),
            P(DP + SEQ, None),
            P(DP + SEQ),
            P(DP + SEQ),
            P(DP + SEQ),
            P(DP + SEQ, None),
            P(DP + SEQ, None),
            P(DP + SEQ),
            P(None, DP + SEQ, None),
            P(DP + SEQ),
            P(DP + SEQ, None),
            P(None, DP + SEQ),
            P(None, DP + SEQ, None),
            P(DP + SEQ),
            P(DP + SEQ),
            P(DP + SEQ),
            P(DP + SEQ, None),
            P(DP + SEQ, None),
            P(DP + SEQ),
            P(DP + SEQ),
            P(DP + SEQ),
            P(DP + SEQ, None),
            P(DP + SEQ, None),
            P(DP + SEQ),
            P(None, DP + SEQ),
            P(None, DP + SEQ, None),
            P(None, DP + SEQ, None),
        ),
        check_vma=False,
    )
```

```python
from functools import partial

import jax
import jax.numpy as jnp
from jax import lax
from jax.experimental import pallas as pl
from jax.experimental.pallas import tpu as pltpu
from jax.sharding import PartitionSpec as P

HEADS = 8
HEAD_DIM = 64
CONTEXT = 250
HALO = 256
CODE_HALO = HALO // 2 + 16
EXTRA = 16
QUERIES = 64
GROUP = 4
WINDOW = HALO + QUERIES
VMEM_LIMIT = 56 * 1024 * 1024
ORDER_A = ("hi", "lo", "x")
ORDER_B = ("lo", "x", "hi")
ORDER_C = ("x", "lo", "hi")
ORDER_D = ("lo", "x", "hi")
DP = ("hi", "lo")
SEQ = ("x", "core")

norm_eps = 1e-05
ema_decay = 0.9
bf16 = jnp.bfloat16
f32 = jnp.float32


PIECES = 6


def fetch(sc_ref, pieces, at, width, dst, sems, first=0):
    copies = []
    base = 8 if len(pieces) == 6 else 14
    for i, piece in enumerate(pieces):
        rows = piece.shape[0]
        row = pl.multiple_of(sc_ref[base + i], 64)
        copies.append(
            pltpu.make_async_copy(
                piece.at[:, at : at + width], dst.at[pl.ds(row, rows), :], sems.at[first + i]
            )
        )
        copies[-1].start()
    return copies


def split_refs(refs, counts):
    groups = []
    for count in counts:
        groups.append(refs[:count])
        refs = refs[count:]
    return groups, refs


def wait_all(copies):
    for copy in copies:
        copy.wait()


def mm(a, b):
    return jnp.dot(a, b, preferred_element_type=f32)


def mm_nt(a, b):
    return lax.dot_general(a, b, (((1,), (1,)), ((), ())), preferred_element_type=f32)


def mm_tn(a, b):
    return lax.dot_general(a, b, (((0,), (0,)), ((), ())), preferred_element_type=f32)


def normalize(stream):
    center = stream - jnp.mean(stream, -1, keepdims=True)
    scaled = lax.rsqrt(jnp.mean(center * center, -1, keepdims=True) + norm_eps)
    return center * scaled, scaled


def norm_backward(upstream, normal, scaled, gain):
    inner = upstream * gain
    return scaled * (
        inner
        - jnp.mean(inner, -1, keepdims=True)
        - normal * jnp.mean(inner * normal, -1, keepdims=True)
    )


def column_sum(value):
    return jnp.sum(value, 0, keepdims=True)


def interleave(even, odd, scr):
    tiles, rows, _ = scr.shape
    for tile in range(tiles):
        cols = slice(tile * 128, (tile + 1) * 128)
        scr[tile, pl.ds(0, rows // 2, stride=2), :] = even[:, cols]
        scr[tile, pl.ds(1, rows // 2, stride=2), :] = odd[:, cols]
    return jnp.concatenate([scr[tile] for tile in range(tiles)], 1)


def split_rows(value, scr):
    tiles, rows, _ = scr.shape
    for tile in range(tiles):
        scr[tile] = value[:, tile * 128 : (tile + 1) * 128]
    even = [scr[tile, pl.ds(0, rows // 2, stride=2), :] for tile in range(tiles)]
    odd = [scr[tile, pl.ds(1, rows // 2, stride=2), :] for tile in range(tiles)]
    return jnp.concatenate(even, 1), jnp.concatenate(odd, 1)


def first_half():
    lane = lax.broadcasted_iota(jnp.int32, (1, 128), 1)
    return lane % HEAD_DIM < HEAD_DIM // 2


def rotate(tile, cos, sin):
    swapped = jnp.where(first_half(), pltpu.roll(tile, 96, 1), pltpu.roll(tile, 32, 1))
    return tile * cos + swapped * sin


def head_lanes():
    lane = lax.broadcasted_iota(jnp.int32, (1, GROUP * HEAD_DIM), 1) // HEAD_DIM
    return [(lane == head) for head in range(GROUP)]


def stack_heads(block, lanes):
    return jnp.concatenate([block * mask.astype(bf16) for mask in lanes], 0)


def unstack_heads(block, lanes):
    rows = block.shape[0] // GROUP
    out = block[:rows]
    for head in range(1, GROUP):
        out = jnp.where(lanes[head], block[head * rows : (head + 1) * rows], out)
    return out


def lowest_key(query, cut):
    low = jnp.maximum(query - (CONTEXT - 1), 0)
    return jnp.where(query >= cut, jnp.maximum(low, cut), low)


def attend(q_ref, k_ref, v_ref, att_ref, sc_ref, rows, first_query, first_key, keys, at_row):
    start, cut = sc_ref[0], sc_ref[1]
    query = start + first_query + lax.broadcasted_iota(jnp.int32, (rows, 1), 0)
    low = lowest_key(query, cut)
    key = start + first_key + lax.broadcasted_iota(jnp.int32, (rows, keys), 1)
    mask = (key <= query) & (key >= low)
    mask = jnp.concatenate([mask] * GROUP, 0)
    lanes = head_lanes()
    key_row = first_key + HALO
    for group in range(HEADS // GROUP):
        cols = slice(group * GROUP * HEAD_DIM, (group + 1) * GROUP * HEAD_DIM)
        stacked = stack_heads(q_ref[at_row : at_row + rows, cols], lanes)
        scores = mm_nt(stacked, k_ref[key_row : key_row + keys, cols]) * HEAD_DIM ** (-0.5)
        scores = jnp.where(mask, scores, -1e30)
        exponent = jnp.exp(scores - jnp.max(scores, -1, keepdims=True))
        weights = exponent * (1.0 / jnp.sum(exponent, -1, keepdims=True))
        mixed = mm(weights.astype(bf16), v_ref[key_row : key_row + keys, cols])
        att_ref[at_row : at_row + rows, cols] = unstack_heads(mixed, lanes).astype(bf16)


def front(x, vec_ref, base, w_in, cos_ref, sin_ref, sc_ref, n1_ref, q_ref, k_ref, v_ref, att_ref,
          extra):
    width = x.shape[1]
    normal, _ = normalize(x)
    low = (normal * vec_ref[base : base + 1] + vec_ref[base + 1 : base + 2]).astype(bf16)
    n1_ref[...] = low[HALO:]
    skip = HALO - extra
    queries = mm(low[skip:], w_in[:, :width])
    keys = mm(low, w_in[:, width : 2 * width])
    for at in range(0, width, 128):
        q_ref[:, at : at + 128] = rotate(
            queries[:, at : at + 128], cos_ref[skip:], sin_ref[skip:]
        ).astype(bf16)
        k_ref[:, at : at + 128] = rotate(keys[:, at : at + 128], cos_ref[...], sin_ref[...]).astype(
            bf16
        )
    v_ref[...] = mm(low, w_in[:, 2 * width :]).astype(bf16)
    frames = x.shape[0] - HALO
    if extra:
        attend(q_ref, k_ref, v_ref, att_ref, sc_ref, extra, -extra, -HALO, HALO, 0)
    for first in range(0, frames, QUERIES):
        attend(
            q_ref, k_ref, v_ref, att_ref, sc_ref, QUERIES, first, first - HALO, WINDOW,
            extra + first,
        )


def decoder_front_kernel(sc_ref, *refs):
    pieces, refs = refs[:PIECES], refs[PIECES:]
    (qz_ref, vec_ref, cos_ref, sin_ref, x_ref, restored_ref, n1_ref, q_ref, k_ref, v_ref, att_ref,
     w_vmem, x_scr, sems) = refs
    width = x_ref.shape[1]
    wait_all(fetch(sc_ref, pieces, 0, w_vmem.shape[1], w_vmem, sems))
    latent = qz_ref.shape[1]
    restored = mm_nt(qz_ref[...], w_vmem[:, :latent]).astype(bf16)
    restored_ref[...] = restored[CODE_HALO - 16 :]
    both = mm(restored, w_vmem[:, latent : latent + 4 * width])
    bias = vec_ref[7:8]
    now = both[16:, : 2 * width]
    before = pltpu.roll(both[:, 2 * width :], 1, 0)[16:]
    total = now + before
    x = interleave(total[:, :width] + bias, total[:, width:] + bias, x_scr)
    x_ref[...] = x[HALO:]
    w_in = w_vmem.at[:, latent + 4 * width :]
    front(x, vec_ref, 8, w_in, cos_ref, sin_ref, sc_ref, n1_ref, q_ref, k_ref, v_ref,
          att_ref, 0)


def encoder_front_kernel(sc_ref, *refs):
    (pieces,), refs = split_refs(refs, (4,))
    (halo_ref, x_ref, vec_ref, cos_ref, sin_ref, n1_ref, q_ref, k_ref, v_ref, att_ref,
     w_vmem, sems) = refs
    width = x_ref.shape[1]
    copies = fetch(sc_ref, pieces, 0, 3 * width, w_vmem, sems)
    x = jnp.concatenate([halo_ref[...], x_ref[...]], 0).astype(f32)
    wait_all(copies)
    front(x, vec_ref, 0, w_vmem, cos_ref, sin_ref, sc_ref, n1_ref, q_ref, k_ref, v_ref, att_ref,
          EXTRA)


def gelu_both(hidden):
    share = 0.5 * (1.0 + lax.erf(hidden * 0.7071067811865476))
    density = jnp.exp(-0.5 * hidden * hidden) * 0.3989422804014327
    return hidden * share, share + hidden * density


def l2_rows(w, at, chunk, width):
    rows = width // 4
    return jnp.concatenate(
        [
            w[chunk * rows : (chunk + 1) * rows, at + g * width : at + (g + 1) * width]
            for g in range(4)
        ],
        0,
    )


def forward_kernel(base, extra, counts, plan, sc_ref, *refs):
    groups, refs = split_refs(refs, counts)
    halo_ref, refs = (refs[0], refs[1:]) if extra else (None, refs)
    (att_ref, x_ref, g_ref, vec_ref, q_ref, k_ref, v_ref,
     out_ref, gmid_ref, n2_ref, active_ref, dh_ref, dtwo_ref, done_ref, vg_ref,
     dq_ref, dk_ref, dv_ref, dkh_ref, dvh_ref,
     w_vmem, h_scr, slope_scr, mid_scr, act_scr, datt_scr, dk_scr, dv_scr, sems) = refs
    frames, width = x_ref.shape
    hidden_total = 4 * width
    parts = (
        (0, width),
        (width, width + hidden_total),
        (width + hidden_total, width + 2 * hidden_total),
    )
    copies = [
        fetch(
            sc_ref, groups[plan[i][0]], plan[i][1], high - low, w_vmem.at[:, low:high], sems,
            PIECES * i,
        )
        for i, (low, high) in enumerate(parts)
    ]
    scale_one = vec_ref[base + 2 : base + 3]
    gain_two = vec_ref[base + 3 : base + 4]
    bias_two = vec_ref[base + 4 : base + 5]
    scale_two = vec_ref[base + 5 : base + 6]
    wait_all(copies[0])
    branch = mm(att_ref[...], w_vmem[:, :width])
    stream = x_ref[...].astype(f32)
    if extra:
        stream = jnp.concatenate([halo_ref[HALO - extra :, :].astype(f32), stream], 0)
    middle = stream + scale_one * branch
    mid_scr[...] = middle
    normal, scaled = normalize(middle)
    n2 = (normal * gain_two + bias_two).astype(bf16)
    n2_ref[...] = n2[extra:]
    wait_all(copies[1])
    l1_at, l2_at = width, width + hidden_total
    rows = frames + extra
    second = None
    for chunk in range(4):
        cols = slice(chunk * width, (chunk + 1) * width)
        h_scr[...] = mm(n2, w_vmem[:, l1_at + chunk * width : l1_at + (chunk + 1) * width])

        def body(i, _):
            at_row = pl.multiple_of(i * 16, 16)
            here = pl.ds(at_row, 16)
            act, slope = gelu_both(h_scr[here, :])
            act_scr[here, cols] = act.astype(bf16)
            slope_scr[here, cols] = slope
            return 0

        lax.fori_loop(0, rows // 16, body, 0)
        if chunk == 0:
            wait_all(copies[2])
        part = mm(act_scr[:, cols], l2_rows(w_vmem, l2_at, chunk, width))
        second = part if second is None else second + part
    active_ref[...] = act_scr[extra:, :]
    out_ref[...] = (mid_scr[...] + scale_two * second).astype(bf16)

    g = g_ref[...].astype(f32)
    vg_ref[3:4, :] = column_sum(g * second[extra:])
    d_two = (g * scale_two).astype(bf16)
    dtwo_ref[...] = d_two
    e = None
    for chunk in range(4):
        cols = slice(chunk * width, (chunk + 1) * width)
        d_active = mm_nt(d_two, l2_rows(w_vmem, l2_at, chunk, width))
        dh_ref[:, cols] = (d_active * slope_scr[extra:, cols]).astype(bf16)
        part = mm_nt(
            dh_ref[:, cols], w_vmem[:, l1_at + chunk * width : l1_at + (chunk + 1) * width]
        )
        e = part if e is None else e + part
    dh_ref.flush()
    normal, scaled = normal[extra:], scaled[extra:]
    vg_ref[1:2, :] = column_sum(e * normal)
    vg_ref[2:3, :] = column_sum(e)
    g_mid = g + norm_backward(e, normal, scaled, gain_two)
    gmid_ref[...] = g_mid
    vg_ref[0:1, :] = column_sum(g_mid * branch[extra:])
    d_one = (g_mid * scale_one).astype(bf16)
    done_ref[...] = d_one
    datt_scr[...] = mm_nt(d_one, w_vmem[:, :width]).astype(bf16)
    attention_backward(
        extra, sc_ref, q_ref, k_ref, v_ref, datt_scr, dq_ref, dk_ref, dv_ref, dkh_ref, dvh_ref,
        dk_scr, dv_scr,
    )


def attention_backward(extra, sc_ref, q_ref, k_ref, v_ref, do_ref,
                       dq_ref, dk_ref, dv_ref, dkh_ref, dvh_ref, dk_scr, dv_scr):
    start, cut = sc_ref[0], sc_ref[1]
    frames = do_ref.shape[0]
    lanes = head_lanes()
    scale = HEAD_DIM ** (-0.5)
    dk_scr[...] = jnp.zeros_like(dk_scr)
    dv_scr[...] = jnp.zeros_like(dv_scr)
    wide = GROUP * QUERIES
    for first in range(0, frames, QUERIES):
        lane = lax.broadcasted_iota(jnp.int32, (1, wide), 1) % QUERIES
        query = start + first + lane
        low = lowest_key(query, cut)
        key = start + first - HALO + lax.broadcasted_iota(jnp.int32, (WINDOW, wide), 0)
        mask = (key <= query) & (key >= low)
        for group in range(HEADS // GROUP):
            cols = slice(group * GROUP * HEAD_DIM, (group + 1) * GROUP * HEAD_DIM)
            qs = stack_heads(q_ref[extra + first : extra + first + QUERIES, cols], lanes)
            ds = stack_heads(do_ref[first : first + QUERIES, cols], lanes)
            kw = k_ref[first : first + WINDOW, cols]
            vw = v_ref[first : first + WINDOW, cols]
            scores = jnp.where(mask, mm_nt(kw, qs) * scale, -1e30)
            exponent = jnp.exp(scores - jnp.max(scores, 0, keepdims=True))
            probs = exponent * (1.0 / jnp.sum(exponent, 0, keepdims=True))
            d_probs = mm_nt(vw, ds)
            mean = jnp.sum(probs * d_probs, 0, keepdims=True)
            d_scores = (probs * (d_probs - mean)).astype(bf16)
            dk_scr[first : first + WINDOW, cols] += mm(d_scores, qs)
            dv_scr[first : first + WINDOW, cols] += mm(probs.astype(bf16), ds)
            dq_ref[first : first + QUERIES, cols] = (
                unstack_heads(mm_tn(d_scores, kw), lanes) * scale
            )
    dq_ref.flush()
    dkh_ref[...] = (dk_scr[:HALO] * scale).astype(bf16)
    dvh_ref[...] = dv_scr[:HALO].astype(bf16)
    dk_ref[...] = dk_scr[HALO:] * scale
    dv_ref[...] = dv_scr[HALO:]


class Packer:
    def __init__(self, core, refs, shares, order):
        self.core, self.refs, self.shares, self.order = core, refs, shares, order

    def flush(self, upto):
        for ref in self.refs:
            ref.flush(upto)

    def put(self, value, at, step=1, phase=0, block0=0):
        if len(self.refs) == 1:
            if step == 1:
                self.refs[0][:, at : at + value.shape[1]] = value.astype(bf16)
            return
        send, keep = self.refs
        cols = slice(at, at + value.shape[1])
        rows = 16
        hi = self.shares // 8
        blocks = value.shape[0] // (rows * step)
        for pair in range(blocks // 2):
            even = value[(2 * pair * step + phase) * rows :][:rows]
            odd = value[((2 * pair + 1) * step + phase) * rows :][:rows]
            block = (block0 + 2 * pair) // 2
            place = {"x": (block % 2, 2), "lo": (block // 2 % 2, 2), "hi": (block // 4, hi)}
            at_row = 0
            for axis in self.order:
                at_row = at_row * place[axis][1] + place[axis][0]
            at_row = at_row * rows
            first = self.core == 0
            keep[at_row : at_row + rows, cols] = jnp.where(first, even, odd).astype(bf16)
            send[at_row : at_row + rows, cols] = jnp.where(first, odd, even).astype(bf16)

    def put_l2(self, value, at, chunk, width):
        if len(self.refs) == 1:
            cols = slice(at + chunk * width, at + (chunk + 1) * width)
            self.refs[0][:, cols] = value.astype(bf16)
            return
        for phase in range(4):
            self.put(value, at + phase * width, 4, phase, chunk * width // 64)


def weight_gradients_kernel(extra, shares, order, sc_ref, n2_ref, active_ref, dh_ref, dtwo_ref,
                            *rest):
    att_ref = None
    if not extra:
        att_ref, done_ref, *rest = rest
    width = n2_ref.shape[1]
    pack = Packer(sc_ref[2], rest, shares, order)
    for chunk in range(4):
        cols = slice(chunk * width, (chunk + 1) * width)
        pack.put_l2(mm_tn(active_ref[:, cols], dtwo_ref[...]), 0, chunk, width)
    pack.flush(4 * width)
    for chunk in range(4):
        cols = slice(chunk * width, (chunk + 1) * width)
        pack.put(mm_tn(n2_ref[...], dh_ref[:, cols]), (4 + chunk) * width)
        pack.flush((5 + chunk) * width)
    if att_ref is not None:
        pack.put(mm_tn(att_ref[...], done_ref[...]), 8 * width)


def layer_input_gradient(extra_rows, base, dq_ref, dk_ref, dv_ref, dkh_ref, dvh_ref, x, gmid_ref,
                         w_in, vec_ref, cos_ref, sin_ref, dmix_ref, vg_ref):
    frames, width = dq_ref.shape
    later = frames - HALO
    cos, sin = cos_ref[HALO:], -sin_ref[HALO:]
    for at in range(0, width, 128):
        cols = slice(at, at + 128)
        dmix_ref[:, cols] = rotate(dq_ref[:, cols], cos, sin).astype(bf16)
        keys = dk_ref[:, cols]
        keys = jnp.concatenate([keys[:later], keys[later:] + dkh_ref[:, cols].astype(f32)], 0)
        dmix_ref[:, width + at : width + at + 128] = rotate(keys, cos, sin).astype(bf16)
        values = dv_ref[:, cols]
        values = jnp.concatenate([values[:later], values[later:] + dvh_ref[:, cols].astype(f32)], 0)
        dmix_ref[:, 2 * width + at : 2 * width + at + 128] = values.astype(bf16)
    d_normed = mm_nt(dmix_ref[...], w_in[...])
    normal, scaled = normalize(x)
    vg_ref[0:1, :] = column_sum(d_normed * normal)
    vg_ref[1:2, :] = column_sum(d_normed)
    return gmid_ref[...] + norm_backward(d_normed, normal, scaled, vec_ref[base : base + 1])


def decoder_back_kernel(at, sc_ref, *refs):
    pieces, refs = refs[:PIECES], refs[PIECES:]
    (dq_ref, dk_ref, dv_ref, dkh_ref, dvh_ref, x_ref, gmid_ref, vec_ref, cos_ref, sin_ref,
     dup_ref, dmix_ref, vg_ref, w_vmem, sems) = refs
    wait_all(fetch(sc_ref, pieces, at, w_vmem.shape[1], w_vmem, sems))
    grad = layer_input_gradient(
        0, 8, dq_ref, dk_ref, dv_ref, dkh_ref, dvh_ref, x_ref[...], gmid_ref, w_vmem, vec_ref,
        cos_ref, sin_ref, dmix_ref, vg_ref,
    )
    vg_ref[2:3, :] = column_sum(grad)
    dup_ref[...] = grad.astype(bf16)


def encoder_back_kernel(shares, sc_ref, *refs):
    (pieces,), refs = split_refs(refs, (4,))
    (dq_ref, dk_ref, dv_ref, dkh_ref, dvh_ref, x_ref, gmid_ref, vec_ref, cos_ref, sin_ref, n1_ref,
     vgs_ref, att_ref, done_ref, win_ref, dred_ref, red_ref, dlat_ref, grad_ref, *rest) = refs
    refs, (w_vmem, dmix_scr, vg_scr, all_scr, sems) = rest[:-5], rest[-5:]
    width = x_ref.shape[1]
    wait_all(fetch(sc_ref, pieces, 0, w_vmem.shape[1], w_vmem, sems))
    grad = layer_input_gradient(
        0, 0, dq_ref, dk_ref, dv_ref, dkh_ref, dvh_ref, x_ref[...].astype(f32), gmid_ref, w_vmem,
        vec_ref, cos_ref, sin_ref, dmix_scr, vg_scr,
    )
    grad_ref[...] = grad.astype(bf16)
    pack = Packer(sc_ref[2], refs, shares, ORDER_D)
    for part in range(3):
        cols = slice(part * width, (part + 1) * width)
        pack.put(mm_tn(n1_ref[...], dmix_scr[:, cols]), part * width)
    all_scr[...] = jnp.zeros_like(all_scr)
    all_scr[0:2, :] = vg_scr[0:2, :]
    all_scr[2:6, :] = vgs_ref[0:4, :]
    all_scr[6:7, :] = vgs_ref[16:17, :]
    all_scr[7:8, :] = vgs_ref[26:27, :]
    all_scr[8:10, :] = vgs_ref[24:26, :]
    all_scr[10:14, :] = vgs_ref[8:12, :]
    pack.put(mm_tn(att_ref[EXTRA:, :], done_ref[...]), 3 * width)
    d_reduced = dred_ref[...]
    for tap in range(4):
        pack.put(mm_tn(win_ref[tap], d_reduced), (4 + tap) * width)
    pack.put(mm_tn(red_ref[...], dlat_ref[...]), 8 * width)
    pack.put(all_scr[...].T, 8 * width + dlat_ref.shape[1])


def middle_kernel(shares, sc_ref, *refs):
    (pieces, more), refs = split_refs(refs, (6, 4))
    (dup_ref, next_ref, dmix_ref, n1_ref, restored_ref, qz_ref,
     denc_ref, dred_ref, dlat_ref, vg_ref, *rest) = refs
    refs, (up_vmem, down_vmem, frame_scr, sems) = rest[:-4], rest[-4:]
    frames, width = dup_ref.shape
    latent = qz_ref.shape[1]
    codec = frames // 2
    copies = [
        fetch(sc_ref, pieces, 0, latent + 4 * width, up_vmem, sems),
        fetch(sc_ref, more, 0, 4 * width + latent, down_vmem, sems, PIECES),
    ]
    pairs = codec + 16
    even, odd = split_rows(
        jnp.concatenate([dup_ref[...], next_ref[...]], 0).astype(f32), frame_scr
    )
    both = jnp.concatenate([even, odd], 1).astype(bf16)
    wait_all(copies[0])
    up = up_vmem[:, latent : latent + 4 * width]
    here = mm_nt(both, up[:, : 2 * width])
    later = mm_nt(both, up[:, 2 * width :])
    d_restored = (here + pltpu.roll(later, pairs - 1, 0)).astype(bf16)
    d_latent = mm(d_restored, up_vmem[:, :latent]).astype(bf16)
    wait_all(copies[1])
    d_reduced = mm_nt(d_latent, down_vmem[:, 4 * width :]).astype(bf16)
    dlat_ref[...] = d_latent[:codec]
    dred_ref[...] = d_reduced[:codec]
    vg_ref[0:1, :] = column_sum(d_reduced[:codec].astype(f32))
    taps = [mm_nt(d_reduced, down_vmem[:, tap * width : (tap + 1) * width]) for tap in range(4)]
    denc_ref[...] = interleave(
        taps[2] + pltpu.roll(taps[0], pairs - 1, 0),
        taps[3] + pltpu.roll(taps[1], pairs - 1, 0),
        frame_scr,
    )[:frames]

    pack = Packer(sc_ref[2], refs, shares, ORDER_B)
    for part in range(3):
        cols = slice(part * width, (part + 1) * width)
        pack.put(mm_tn(n1_ref[...], dmix_ref[:, cols]), part * width)
    restored = restored_ref[...]
    own_pairs = both[:codec]
    before = pltpu.roll(restored.astype(f32), 1, 0)[16:].astype(bf16)
    pack.put(mm_tn(restored[16:], own_pairs[:, :width]), 3 * width)
    pack.put(mm_tn(restored[16:], own_pairs[:, width:]), 4 * width)
    pack.put(mm_tn(before, own_pairs[:, :width]), 5 * width)
    pack.put(mm_tn(before, own_pairs[:, width:]), 6 * width)
    pack.put(mm_tn(d_restored[:codec], qz_ref[CODE_HALO:, :]), 7 * width)


def latent_kernel(sc_ref, *refs):
    (pieces,), refs = split_refs(refs, (4,))
    (enc_ref, rows_ref, vec_ref, res_ref, win_ref, red_ref, w_vmem, frame_scr, sems) = refs
    total, width = enc_ref.shape
    copies = fetch(sc_ref, pieces, 0, w_vmem.shape[1], w_vmem, sems)
    inside = (sc_ref[0] > 0).astype(f32)
    rim = enc_ref[:EXTRA].astype(f32) * inside
    skip = EXTRA // 2
    even, odd = split_rows(jnp.concatenate([rim, enc_ref[EXTRA:].astype(f32)], 0), frame_scr)
    win_ref[0] = pltpu.roll(even, 1, 0)[skip:].astype(bf16)
    win_ref[1] = pltpu.roll(odd, 1, 0)[skip:].astype(bf16)
    win_ref[2] = even[skip:].astype(bf16)
    win_ref[3] = odd[skip:].astype(bf16)
    wait_all(copies)
    reduced = vec_ref[6:7]
    for tap in range(4):
        reduced = reduced + mm(win_ref[tap], w_vmem[:, tap * width : (tap + 1) * width])
    reduced = reduced.astype(bf16)
    red_ref[...] = reduced
    remaining = mm(reduced, w_vmem[:, 4 * width :])
    for level in range(rows_ref.shape[0]):
        res_ref[level] = remaining.astype(bf16)
        remaining = remaining - rows_ref[level].astype(f32)


def lookup_kernel(sc_ref, codes_ref, book_ref, qsend_ref, qkeep_ref, rsend_ref, rkeep_ref, q_scr):
    levels, share, latent = book_ref.shape
    total = codes_ref.shape[0]
    codec = total // 4
    base = sc_ref[3]
    core = sc_ref[2]
    entry = lax.broadcasted_iota(jnp.int32, (1, share), 1)
    for level in range(levels):
        picks = (codes_ref[:, level : level + 1] - base == entry).astype(f32).astype(bf16)
        found = mm(picks, book_ref[level])
        q_scr[CODE_HALO:] = found if level == 0 else q_scr[CODE_HALO:] + found
        for x in range(2):
            even = found[(2 * x) * codec :][:codec]
            odd = found[(2 * x + 1) * codec :][:codec]
            rkeep_ref[x, level] = jnp.where(core == 0, even, odd).astype(bf16)
            rsend_ref[x, level] = jnp.where(core == 0, odd, even).astype(bf16)
    q_scr[:CODE_HALO] = jnp.zeros((CODE_HALO, latent), f32)
    for x in range(2):
        even = q_scr[(2 * x) * codec : (2 * x + 1) * codec + CODE_HALO]
        odd = q_scr[(2 * x + 1) * codec : (2 * x + 2) * codec + CODE_HALO]
        qkeep_ref[x] = jnp.where(core == 0, even, odd)
        qsend_ref[x] = jnp.where(core == 0, odd, even)


def collect_kernel(share, sc_ref, own_ref, x_ref, core_ref, far_ref, frame_ref, codes_ref, entry_ref,
                   dead_ref, place_ref, send_ref, keep_ref, cnt_scr):
    levels = codes_ref.shape[0]
    latent = own_ref.shape[2]
    total = codes_ref.shape[1]
    lo = sc_ref[4]
    high = send_ref.shape[0]
    frame = frame_ref[0:1, :]
    ones = jnp.ones((16, total), bf16)
    for level in range(levels):
        used = (entry_ref[:, level : level + 1] == codes_ref[level : level + 1, :]).astype(f32)
        placed = (place_ref[:, level : level + 1] == frame).astype(f32)
        select = jnp.where(dead_ref[:, level : level + 1] == 1, placed, used).astype(bf16)
        rows = jnp.concatenate([ref[level] for ref in (own_ref, x_ref, core_ref, far_ref)], 0)
        sums = mm(select, rows)
        cnt_scr[level : level + 1, :] = mm_nt(ones, used.astype(bf16))[0:1]
        at = slice(level * share, (level + 1) * share)
        for h in range(high):
            even = sums[(2 * h) * share :][:share]
            odd = sums[(2 * h + 1) * share :][:share]
            keep_ref[h, at, :] = jnp.where(lo == 0, even, odd).astype(bf16)
            send_ref[h, at, :] = jnp.where(lo == 0, odd, even).astype(bf16)
    counts = cnt_scr[...]
    upper = jnp.floor(counts * (1.0 / 128.0))
    digits = jnp.concatenate([upper, counts - 128.0 * upper], 0)
    tail = slice(levels * share, levels * share + 2 * levels)
    for h in range(high):
        even = digits[:, (2 * h) * share : (2 * h + 1) * share]
        odd = digits[:, (2 * h + 1) * share : (2 * h + 2) * share]
        keep_ref[h, tail, :] = jnp.zeros((2 * levels, latent), bf16)
        send_ref[h, tail, :] = jnp.zeros((2 * levels, latent), bf16)
        keep_ref[h, tail, :share] = jnp.where(lo == 0, even, odd).astype(bf16)
        send_ref[h, tail, :share] = jnp.where(lo == 0, odd, even).astype(bf16)


class Source:
    def __init__(self, ref, copy):
        self.ref, self.copy, self.shape = ref, copy, ref.shape
        copy.start()

    def ready(self):
        if self.copy is not None:
            self.copy.wait()
            self.copy = None

    def __getitem__(self, index):
        self.ready()
        return self.ref[index]


class Result:
    def __init__(self, ref, out, sems):
        self.ref, self.out, self.sems, self.shape = ref, out, sems, ref.shape
        self.sent, self.copies = 0, []

    def __getitem__(self, index):
        return self.ref[index]

    def __setitem__(self, index, value):
        self.ref[index] = value
        if index is Ellipsis:
            self.flush()

    def flush(self, upto=None):
        last = self.shape[-1]
        upto = last if upto is None else upto
        if upto <= self.sent:
            return
        src, dst = self.ref, self.out
        if (self.sent, upto) != (0, last):
            where = (slice(None),) * (len(self.shape) - 1) + (slice(self.sent, upto),)
            src, dst = src.at[where], dst.at[where]
        self.copies.append(pltpu.make_async_copy(src, dst, self.sems.at[len(self.copies)]))
        self.copies[-1].start()
        self.sent = upto


FLUSHES = 8


def call(kernel, outs, spaces, scratch, args):
    where = {"s": pltpu.SMEM, "v": pl.ANY, "a": pl.ANY}
    title = getattr(kernel, "func", kernel).__name__
    brought = [i for i, space in enumerate(spaces) if space == "v"]

    def body(*refs):
        ins, refs = list(refs[: len(args)]), refs[len(args) :]
        results, refs = refs[: len(outs)], refs[len(outs) :]
        mine, refs = refs[: len(scratch)], refs[len(scratch) :]
        in_bufs, refs = refs[: len(brought)], refs[len(brought) :]
        out_bufs, (in_sems, out_sems) = refs[: len(outs)], refs[len(outs) :]
        for n, i in enumerate(brought):
            ins[i] = Source(in_bufs[n], pltpu.make_async_copy(ins[i], in_bufs[n], in_sems.at[n]))
        results = [
            Result(buf, out, out_sems.at[n])
            for n, (buf, out) in enumerate(zip(out_bufs, results))
        ]
        kernel(*ins, *results, *mine)
        for result in results:
            result.flush()
        for i in brought:
            ins[i].ready()
        for result in results:
            for copy in result.copies:
                copy.wait()

    return pl.pallas_call(
        body,
        name=title,
        out_shape=outs,
        in_specs=[pl.BlockSpec(memory_space=where[s]) for s in spaces],
        out_specs=[pl.BlockSpec(memory_space=pl.ANY) for _ in outs],
        scratch_shapes=scratch
        + [pltpu.VMEM(args[i].shape, args[i].dtype) for i in brought]
        + [pltpu.VMEM(o.shape, o.dtype) for o in outs]
        + [
            pltpu.SemaphoreType.DMA((max(1, len(brought)),)),
            pltpu.SemaphoreType.DMA((len(outs), FLUSHES)),
        ],
        compiler_params=pltpu.CompilerParams(vmem_limit_bytes=VMEM_LIMIT),
        cost_estimate=pl.CostEstimate(flops=1, bytes_accessed=1, transcendentals=0),
    )(*args)


def shape(dims, dtype=f32):
    return jax.ShapeDtypeStruct(dims, dtype)


def halve(block, dim, axis):
    mine = lax.axis_index(axis)
    sent = lax.dynamic_index_in_dim(block, 1 - mine, dim, False)
    kept = lax.dynamic_index_in_dim(block, mine, dim, False)
    got = lax.ppermute(sent, axis, [(0, 1), (1, 0)])
    return (kept.astype(f32) + got.astype(f32)).astype(block.dtype)


def swap_add(send, keep, axis):
    got = lax.ppermute(send, axis, [(0, 1), (1, 0)])
    return (keep.astype(f32) + got.astype(f32)).astype(keep.dtype)


def sum_over_hi(block):
    parts = lax.all_to_all(block, "hi", 0, 0, tiled=True)
    return jnp.sum(parts.astype(f32), 0)


def shifted(block, distance):
    devices = range(lax.axis_size(SEQ))
    route = [(i - distance, i) for i in devices if i - distance in devices]
    return lax.ppermute(block, SEQ, route)


def packed_outs(width_total, width, shares):
    if width // shares % 16 == 0:
        return [shape((width // 2, width_total), bf16)] * 2
    return [shape((width, width_total), bf16)]


def swap(block, axis):
    return lax.ppermute(block, axis, [(0, 1), (1, 0)])


def tie(*values):
    return lax.optimization_barrier(values)


def near_half(share):
    rows = share.shape[0] // 2
    half = lax.dynamic_slice_in_dim(share, lax.axis_index("lo") * rows, rows, 0)
    return swap(half, "x")


def spread(share, near):
    far = swap(near, "lo")
    return [share, near, far, swap(share, "core"), swap(near, "core"), swap(far, "core")]


def spread_whole(share, near):
    return [share, near, swap(share, "core"), swap(near, "core")]


def unfolded_rows(block, shares, l2_at):
    width = block.shape[0]
    full = [block[:, l2_at + i * width : l2_at + (i + 1) * width] for i in range(4)]
    full = jnp.concatenate(full, 0).reshape(shares, 4, width // shares, width)
    full = full.transpose(0, 2, 1, 3).reshape(width, 4 * width)
    return jnp.concatenate([block[:, :l2_at], full, block[:, l2_at + 4 * width :]], 1)


def first_sum(parts, shares, order, l2_at=None):
    if len(parts) == 2:
        return swap_add(*parts, "core")
    (block,) = parts
    if l2_at is not None:
        block = unfolded_rows(block, shares, l2_at)
    width, total = block.shape
    block = block.reshape(shares // 8, 2, 2, 2, width // shares, total)
    block = halve(block, 3, "core")
    places = [("hi", "lo", "x").index(axis) for axis in order]
    return block.transpose(*places, 3, 4).reshape(width // 2, total)


def next_sum(block, axis):
    rows, total = block.shape
    return halve(block.reshape(2, rows // 2, total), 0, axis)


def last_sum(block, high):
    return sum_over_hi(block.reshape(high, -1, block.shape[1]))


def local(
    activations,
    encoder_attention_norm_gain,
    encoder_attention_norm_bias,
    encoder_query_key_value_weight,
    encoder_attention_output_weight,
    encoder_attention_layer_scale,
    encoder_forward_norm_gain,
    encoder_forward_norm_bias,
    encoder_forward_input_weight,
    encoder_forward_output_weight,
    encoder_forward_layer_scale,
    strided_convolution_weight,
    strided_convolution_bias,
    quantizer_input_weight,
    codebook,
    quantizer_output_weight,
    transposed_convolution_weight,
    transposed_convolution_bias,
    decoder_attention_norm_gain,
    decoder_attention_norm_bias,
    decoder_query_key_value_weight,
    decoder_attention_output_weight,
    decoder_attention_layer_scale,
    decoder_forward_norm_gain,
    decoder_forward_norm_bias,
    decoder_forward_input_weight,
    decoder_forward_output_weight,
    decoder_forward_layer_scale,
    cotangent,
    frame_segment_index,
    frame_code_index,
    replace_code_mask,
    replacing_batch_position,
    code_usage_average,
    code_latent_sum_average,
):
    batch_rows, frames, width = activations.shape
    assert batch_rows == 1
    seq_index = lax.axis_index(SEQ)
    seq_count = lax.axis_size(SEQ)
    dp_index = lax.axis_index(DP)
    dp_count = lax.axis_size(DP)
    shares = dp_count * seq_count
    codec = frames // 2
    levels = frame_code_index.shape[2]
    latent = codebook.shape[2]
    book_share = codebook.shape[1]
    core_index = lax.axis_index("core")

    x_index, lo_index = lax.axis_index("x"), lax.axis_index("lo")
    rows_share = width // seq_count

    vectors = jnp.stack(
        [
            encoder_attention_norm_gain,
            encoder_attention_norm_bias,
            encoder_attention_layer_scale,
            encoder_forward_norm_gain,
            encoder_forward_norm_bias,
            encoder_forward_layer_scale,
            strided_convolution_bias,
            transposed_convolution_bias,
            decoder_attention_norm_gain,
            decoder_attention_norm_bias,
            decoder_attention_layer_scale,
            decoder_forward_norm_gain,
            decoder_forward_norm_bias,
            decoder_forward_layer_scale,
        ]
    )
    vectors = jnp.pad(vectors, ((0, 2), (0, 0)))
    small = jnp.concatenate(
        [frame_code_index.reshape(-1).astype(f32), vectors.reshape(-1).astype(f32)]
    )
    small = lax.all_gather(small, SEQ, axis=0, tiled=False)
    code_count = codec * levels
    row_codes = small[:, :code_count].astype(jnp.int32).reshape(seq_count, codec, levels)
    vectors = small[:, code_count:].reshape(seq_count, 16, -1).transpose(1, 0, 2).reshape(16, width)
    cut = jnp.sum((frame_segment_index[0] == 0).astype(jnp.int32))
    order = [2 * x_index + core_index, 2 * (1 - x_index) + core_index]
    order += [2 * x_index + 1 - core_index, 2 * (1 - x_index) + 1 - core_index]
    half_rows = rows_share // 2
    near, far = lo_index * half_rows, (1 - lo_index) * half_rows
    scalars = jnp.stack(
        [
            seq_index * frames,
            cut,
            core_index,
            seq_index * book_share,
            lo_index,
            seq_index,
            seq_index,
            seq_index,
            order[0] * rows_share,
            order[1] * rows_share + near,
            order[1] * rows_share + far,
            order[2] * rows_share,
            order[3] * rows_share + near,
            order[3] * rows_share + far,
            order[0] * rows_share,
            order[1] * rows_share,
            order[2] * rows_share,
            order[3] * rows_share,
        ]
    ).astype(jnp.int32)

    def flat_taps(taps):
        return taps.transpose(1, 0, 2).reshape(taps.shape[1], -1)

    first_pack = jnp.concatenate(
        [
            quantizer_output_weight.T,
            flat_taps(transposed_convolution_weight),
            decoder_query_key_value_weight,
        ],
        1,
    )
    near_one = near_half(first_pack)
    dec_one = spread(first_pack, near_one)
    out_share, l1_share, l2_share = (
        decoder_attention_output_weight,
        decoder_forward_input_weight,
        decoder_forward_output_weight,
    )

    def fold_l2(share):
        return share.reshape(4, -1, width).transpose(1, 0, 2).reshape(-1, 4 * width)

    second_pack = jnp.concatenate([out_share, l1_share, fold_l2(l2_share)], 1)
    near_two = near_half(second_pack)
    dec_two = spread(second_pack, near_two)
    pack_in = jnp.concatenate(
        [encoder_query_key_value_weight, encoder_attention_output_weight], 1
    )
    pack_down = jnp.concatenate(
        [flat_taps(strided_convolution_weight), quantizer_input_weight], 1
    )
    pack_l1 = encoder_forward_input_weight
    pack_l2 = fold_l2(encoder_forward_output_weight)

    positions = seq_index * frames - HALO + jnp.arange(HALO + frames, dtype=jnp.int32)
    half_dim = HEAD_DIM // 2
    frequency = jnp.power(10000.0, -jnp.arange(half_dim, dtype=f32) / half_dim)
    angles = positions.astype(f32)[:, None] * frequency[None, :]
    cos, sin = jnp.cos(angles), jnp.sin(angles)
    cos_table = jnp.concatenate([cos] * 4, 1)
    sin_table = jnp.concatenate([-sin, sin, -sin, sin], 1)
    activation_halo = shifted(activations[0, frames - HALO :], 1)

    window = codec + CODE_HALO
    qsend, qkeep, rsend, rkeep = call(
        lookup_kernel,
        [shape((2, window, latent))] * 2 + [shape((2, levels, codec, latent), bf16)] * 2,
        "svv",
        [pltpu.VMEM((CODE_HALO + codec * seq_count, latent), f32)],
        (scalars, row_codes.reshape(-1, levels), codebook),
    )
    quantized = halve(swap_add(qsend, qkeep, "core"), 0, "x").astype(bf16)

    code_total = replace_code_mask.shape[1]
    code_share = code_usage_average.shape[1]
    row_frames = codec * seq_count
    dead_flag = replace_code_mask == 1

    def seq_part(array):
        return lax.dynamic_index_in_dim(
            array.reshape(levels, dp_count, seq_count, code_share), seq_index, 2, False
        ).reshape(levels, dp_count * code_share)

    part_dead = seq_part(replace_code_mask)
    part_place = seq_part(replacing_batch_position)
    part_place = jnp.where(part_place // row_frames == dp_index, part_place % row_frames, -1)
    part_code = seq_part(
        jnp.broadcast_to(jnp.arange(code_total, dtype=jnp.int32), (levels, code_total))
    )
    relative_codes = jnp.concatenate([row_codes[i] for i in order], 0).T
    relative_frames = jnp.concatenate(
        [i * codec + jnp.arange(codec, dtype=jnp.int32) for i in order]
    )[None]
    entry_t, dead_t, place_t = part_code.T, part_dead.T, part_place.T
    (quantized, cos_table, sin_table, entry_t, dead_t, place_t, relative_codes, relative_frames,
     dead_flag) = tie(
        quantized, cos_table, sin_table, entry_t, dead_t, place_t, relative_codes, relative_frames,
        dead_flag
    )

    pack_in, quantized = tie(pack_in, quantized)
    near_in = swap(pack_in, "x")
    total_frames = HALO + frames

    d_x, restored, d_n1, d_q, d_k, d_v, d_att = call(
        decoder_front_kernel,
        [
            shape((frames, width)),
            shape((codec + 16, width), bf16),
            shape((frames, width), bf16),
            shape((frames, width), bf16),
            shape((total_frames, width), bf16),
            shape((total_frames, width), bf16),
            shape((frames, width), bf16),
        ],
        "s" + "a" * PIECES + "vvvv",
        [
            pltpu.VMEM((width, first_pack.shape[1]), bf16),
            pltpu.VMEM((width // 128, total_frames, 128), f32),
            pltpu.SemaphoreType.DMA((PIECES,)),
        ],
        (scalars, *dec_one, quantized, vectors, cos_table, sin_table),
    )

    d_att, near_in, pack_down = tie(d_att, near_in, pack_down)
    near_down = swap(pack_down, "x")

    def feed_forward(base, extra, inputs, weights, plan):
        rows = frames + extra
        return call(
            partial(forward_kernel, base, extra, tuple(len(w) for w in weights), plan),
            [
                shape((rows, width), bf16),
                shape((frames, width)),
                shape((frames, width), bf16),
                shape((frames, 4 * width), bf16),
                shape((frames, 4 * width), bf16),
                shape((frames, width), bf16),
                shape((frames, width), bf16),
                shape((8, width)),
            ]
            + [shape((frames, width))] * 3
            + [shape((HALO, width), bf16)] * 2,
            "s" + "a" * sum(len(w) for w in weights) + "v" * len(inputs),
            [
                pltpu.VMEM((width, 9 * width), bf16),
                pltpu.VMEM((rows, width), f32),
                pltpu.VMEM((rows, 4 * width), f32),
                pltpu.VMEM((rows, width), f32),
                pltpu.VMEM((rows, 4 * width), bf16),
                pltpu.VMEM((frames, width), bf16),
                pltpu.VMEM((total_frames, width), f32),
                pltpu.VMEM((total_frames, width), f32),
                pltpu.SemaphoreType.DMA((3 * PIECES,)),
            ],
            (scalars, *sum(weights, []), *inputs),
        )

    (output, d_gmid, d_n2, d_active, d_dh, d_dtwo, d_done, d_vg_two, d_dq, d_dk, d_dv, d_dkh,
     d_dvh) = feed_forward(
        8, 0, (d_att, d_x, cotangent[0], vectors, d_q, d_k, d_v), [dec_two],
        ((0, 0), (0, width), (0, 5 * width)),
    )
    d_n2, near_down, pack_l1 = tie(d_n2, near_down, pack_l1)
    near_l1 = swap(pack_l1, "x")
    enc_down = spread_whole(pack_down, near_down)
    d_n2, d_dkh, d_dvh = tie(d_n2, d_dkh, d_dvh)
    d_dkh, d_dvh = shifted(d_dkh, -1), shifted(d_dvh, -1)
    group_a = call(
        partial(weight_gradients_kernel, 0, shares, ORDER_A),
        packed_outs(9 * width, width, shares),
        "svvvvvv",
        [],
        (scalars, d_n2, d_active, d_dh, d_dtwo, d_att, d_done),
    )
    d_dq, near_l1, pack_l2, *group_a = tie(d_dq, near_l1, pack_l2, *group_a)
    near_l2 = swap(pack_l2, "x")
    enc_l1 = spread_whole(pack_l1, near_l1)
    a_sum = first_sum(group_a, shares, ORDER_A, 0)
    in_at = latent + 4 * width
    d_up, d_mixed, d_vg_one = call(
        partial(decoder_back_kernel, in_at),
        [shape((frames, width), bf16), shape((frames, 3 * width), bf16), shape((8, width))],
        "s" + "a" * PIECES + "v" * 10,
        [pltpu.VMEM((width, 3 * width), bf16), pltpu.SemaphoreType.DMA((PIECES,))],
        (
            scalars, *dec_one, d_dq, d_dk, d_dv, d_dkh, d_dvh, d_x, d_gmid, vectors, cos_table,
            sin_table,
        ),
    )
    d_up_next = shifted(d_up[:32], -1)

    enc_in = spread_whole(pack_in, near_in)
    a_sum, d_up, e_input = tie(a_sum, d_up, activations[0])
    e_n1, e_q, e_k, e_v, e_att = call(
        encoder_front_kernel,
        [
            shape((frames, width), bf16),
            shape((frames + EXTRA, width), bf16),
            shape((total_frames, width), bf16),
            shape((total_frames, width), bf16),
            shape((frames + EXTRA, width), bf16),
        ],
        "s" + "a" * 4 + "vvvvv",
        [pltpu.VMEM((width, 3 * width), bf16), pltpu.SemaphoreType.DMA((PIECES,))],
        (scalars, *enc_in, activation_halo, e_input, vectors, cos_table, sin_table),
    )

    d_mixed, e_n1, near_l2 = tie(d_mixed, e_n1, near_l2)
    enc_l2 = spread_whole(pack_l2, near_l2)
    middle_outs = call(
        partial(middle_kernel, shares),
        [
            shape((frames, width)),
            shape((codec, width), bf16),
            shape((codec, latent), bf16),
            shape((8, width)),
        ]
        + packed_outs(7 * width + latent, width, shares),
        "s" + "a" * 10 + "v" * 6,
        [
            pltpu.VMEM((width, latent + 4 * width), bf16),
            pltpu.VMEM((width, latent + 4 * width), bf16),
            pltpu.VMEM((width // 128, frames + 32, 128), f32),
            pltpu.SemaphoreType.DMA((2 * PIECES,)),
        ],
        (
            scalars, *dec_one, *enc_down, d_up, d_up_next, d_mixed, d_n1, restored, quantized,
        ),
    )
    d_encoded, d_reduced, d_latent, m_vg = middle_outs[:4]
    b_sum = first_sum(middle_outs[4:], shares, ORDER_B)
    high = shares // 8
    a_sum = last_sum(a_sum, high).astype(bf16)

    (encoded, e_gmid, e_n2, e_active, e_dh, e_dtwo, e_done, e_vg_two, e_dq, e_dk, e_dv, e_dkh,
     e_dvh) = feed_forward(
        0, EXTRA,
        (activation_halo, e_att, activations[0], d_encoded, vectors, e_q, e_k, e_v),
        [enc_in, enc_l1, enc_l2], ((0, 3 * width), (1, 0), (2, 0)),
    )
    e_n2, e_dkh, e_dvh = tie(e_n2, e_dkh, e_dvh)
    e_dkh, e_dvh = shifted(e_dkh, -1), shifted(e_dvh, -1)
    group_c = call(
        partial(weight_gradients_kernel, EXTRA, shares, ORDER_C),
        packed_outs(8 * width, width, shares),
        "svvvv",
        [],
        (scalars, e_n2, e_active, e_dh, e_dtwo),
    )
    encoded, *group_c = tie(encoded, *group_c)
    c_sum = first_sum(group_c, shares, ORDER_C, 0)
    code_rows = halve(swap_add(rsend, rkeep, "core"), 0, "x")
    encoded, b_sum = tie(encoded, b_sum)
    residuals, windows, reduced = call(
        latent_kernel,
        [
            shape((levels, codec, latent), bf16),
            shape((4, codec, width), bf16),
            shape((codec, width), bf16),
        ],
        "s" + "a" * 4 + "vvv",
        [
            pltpu.VMEM((width, 4 * width + latent), bf16),
            pltpu.VMEM((width // 128, frames + EXTRA, 128), f32),
            pltpu.SemaphoreType.DMA((PIECES,)),
        ],
        (scalars, *enc_down, encoded, code_rows, vectors),
    )
    e_dq, residuals = tie(e_dq, residuals)
    vector_grads = jnp.concatenate([e_vg_two, d_vg_two, m_vg, d_vg_one], 0)
    back_outs = call(
        partial(encoder_back_kernel, shares),
        [shape((frames, width), bf16)] + packed_outs(8 * width + latent + 128, width, shares),
        "s" + "a" * 4 + "v" * 18,
        [
            pltpu.VMEM((width, 3 * width), bf16),
            pltpu.VMEM((frames, 3 * width), bf16),
            pltpu.VMEM((8, width), f32),
            pltpu.VMEM((128, width), f32),
            pltpu.SemaphoreType.DMA((PIECES,)),
        ],
        (
            scalars, *enc_in, e_dq, e_dk, e_dv, e_dkh, e_dvh, activations[0], e_gmid, vectors,
            cos_table, sin_table, e_n1, vector_grads, e_att, e_done, windows, d_reduced, reduced,
            d_latent,
        ),
    )
    d_sum = first_sum(back_outs[1:], shares, ORDER_D)
    b_sum = next_sum(b_sum, ORDER_B[0])
    c_sum = next_sum(c_sum, ORDER_C[0])
    d_sum = next_sum(d_sum, ORDER_D[0])
    a_sum = next_sum(a_sum, ORDER_A[1])
    b_sum = next_sum(b_sum, ORDER_B[1])
    c_sum = next_sum(c_sum, ORDER_C[1])
    d_sum = next_sum(d_sum, ORDER_D[1])
    grads_a = next_sum(a_sum, ORDER_A[2]).astype(f32)
    grads_b = last_sum(b_sum, high)
    both = last_sum(jnp.concatenate([c_sum, d_sum], 1), high)
    grads_c, grads_d = both[:, : c_sum.shape[1]], both[:, c_sum.shape[1] :]

    near_res = swap(residuals, "x")
    res_pieces = [residuals, near_res, swap(residuals, "core"), swap(near_res, "core")]
    if code_share % 16 == 0:
        tail_rows = levels * code_share
        csend, ckeep = call(
            partial(collect_kernel, code_share),
            [shape((dp_count // 2, tail_rows + 2 * levels, latent), bf16)] * 2,
            "s" + "v" * 9,
            [pltpu.VMEM((levels, dp_count * code_share), f32)],
            (scalars, *res_pieces, relative_frames, relative_codes, entry_t, dead_t, place_t),
        )
        combined = sum_over_hi(swap_add(csend, ckeep, "lo"))
        summed = combined[:tail_rows].reshape(levels, code_share, latent)
        digits = combined[tail_rows:, :code_share]
        counted = 128.0 * digits[:levels] + digits[levels:]
    else:
        flat_res = jnp.concatenate(res_pieces, 1)
        used = part_code[:, :, None] == relative_codes[:, None, :]
        placed = part_place[:, :, None] == relative_frames[None]
        counts = jnp.sum(used.astype(f32), 2).reshape(levels, dp_count, code_share)
        selects = jnp.where(part_dead[:, :, None] == 1, placed, used).astype(bf16)
        sums = jnp.einsum("lct,ltd->lcd", selects, flat_res, preferred_element_type=f32)
        sums = sums.astype(bf16).reshape(levels, dp_count, code_share, latent)
        summed = lax.psum_scatter(sums, DP, scatter_dimension=1, tiled=False).astype(f32)
        counted = lax.psum_scatter(counts, DP, scatter_dimension=1, tiled=False)
    owner_flag = lax.dynamic_slice_in_dim(
        dead_flag, lax.axis_index(DP + SEQ) * code_share, code_share, 1
    )
    new_cluster_size = ema_decay * code_usage_average + (1.0 - ema_decay) * counted
    new_embed_sum = jnp.where(
        owner_flag[:, :, None],
        summed * new_cluster_size[:, :, None],
        ema_decay * code_latent_sum_average + (1.0 - ema_decay) * summed,
    )
    new_codebook = new_embed_sum / new_cluster_size[:, :, None]

    def columns(block, at, count):
        return block[:, at * width : (at + count) * width]

    def taps(block):
        return block.reshape(-1, 4, width).transpose(1, 0, 2)

    def unfold(block):
        return block.reshape(-1, 4, width).transpose(1, 0, 2).reshape(-1, width)

    vec_at = 8 * width + latent
    vec = grads_d[:, vec_at : vec_at + 16].T
    return (
        output[None],
        back_outs[0][None],
        vec[0],
        vec[1],
        columns(grads_d, 0, 3),
        columns(grads_d, 3, 1),
        vec[2],
        vec[3],
        vec[4],
        columns(grads_c, 4, 4),
        unfold(columns(grads_c, 0, 4)),
        vec[5],
        taps(columns(grads_d, 4, 4)),
        vec[6],
        grads_d[:, 8 * width : 8 * width + latent],
        grads_b[:, 7 * width :].T,
        taps(columns(grads_b, 3, 4)),
        vec[7],
        vec[8],
        vec[9],
        columns(grads_b, 0, 3),
        columns(grads_a, 8, 1),
        vec[10],
        vec[11],
        vec[12],
        columns(grads_a, 4, 4),
        unfold(columns(grads_a, 0, 4)),
        vec[13],
        new_cluster_size,
        new_embed_sum,
        new_codebook,
    )


def solution(mesh):
    grid = mesh.devices
    mesh = jax.sharding.Mesh(
        grid.reshape(grid.shape[0] // 2, 2, grid.shape[1] // 2, 2), ("hi", "lo", "x", "core")
    )
    placed = (
        P(DP, SEQ, None),
        P(SEQ),
        P(SEQ),
        P(SEQ, None),
        P(SEQ, None),
        P(SEQ),
        P(SEQ),
        P(SEQ),
        P(SEQ, None),
        P(SEQ, None),
        P(SEQ),
        P(None, SEQ, None),
        P(SEQ),
        P(SEQ, None),
        P(None, SEQ, None),
        P(None, SEQ),
        P(None, SEQ, None),
        P(SEQ),
        P(SEQ),
        P(SEQ),
        P(SEQ, None),
        P(SEQ, None),
        P(SEQ),
        P(SEQ),
        P(SEQ),
        P(SEQ, None),
        P(SEQ, None),
        P(SEQ),
        P(DP, SEQ, None),
        P(DP, None),
        P(DP, SEQ, None),
        P(),
        P(),
        P(None, DP + SEQ),
        P(None, DP + SEQ, None),
    )
    return jax.shard_map(
        local,
        mesh=mesh,
        in_specs=placed,
        out_specs=(
            P(DP, SEQ, None),
            P(DP, SEQ, None),
            P(DP + SEQ),
            P(DP + SEQ),
            P(DP + SEQ, None),
            P(DP + SEQ, None),
            P(DP + SEQ),
            P(DP + SEQ),
            P(DP + SEQ),
            P(DP + SEQ, None),
            P(DP + SEQ, None),
            P(DP + SEQ),
            P(None, DP + SEQ, None),
            P(DP + SEQ),
            P(DP + SEQ, None),
            P(None, DP + SEQ),
            P(None, DP + SEQ, None),
            P(DP + SEQ),
            P(DP + SEQ),
            P(DP + SEQ),
            P(DP + SEQ, None),
            P(DP + SEQ, None),
            P(DP + SEQ),
            P(DP + SEQ),
            P(DP + SEQ),
            P(DP + SEQ, None),
            P(DP + SEQ, None),
            P(DP + SEQ),
            P(None, DP + SEQ),
            P(None, DP + SEQ, None),
            P(None, DP + SEQ, None),
        ),
        check_vma=False,
    )
```

```python
from functools import partial

import jax
import jax.numpy as jnp
from jax import lax
from jax.experimental import pallas as pl
from jax.experimental.pallas import tpu as pltpu
from jax.sharding import PartitionSpec as P

HEADS = 8
HEAD_DIM = 64
CONTEXT = 250
HALO = 256
CODE_HALO = HALO // 2 + 16
EXTRA = 16
QUERIES = 64
GROUP = 4
WINDOW = HALO + QUERIES
VMEM_LIMIT = 26 * 1024 * 1024
ORDER_A = ("lo", "x", "hi")
ORDER_B = ("hi", "lo", "x")
ORDER_C_ONE = ("x", "lo", "hi")
ORDER_C_TWO = ("lo", "x", "hi")
ORDER_D = ("lo", "x", "hi")
DP = ("hi", "lo")
SEQ = ("x", "core")

norm_eps = 1e-05
ema_decay = 0.9
bf16 = jnp.bfloat16
f32 = jnp.float32


PIECES = 4


def fetch(sc_ref, pieces, at, width, dst, sems, first=0):
    copies = []
    for i, piece in enumerate(pieces):
        rows = piece.shape[0]
        row = pl.multiple_of(sc_ref[8 + i], 128)
        copies.append(
            pltpu.make_async_copy(
                piece.at[:, at : at + width], dst.at[pl.ds(row, rows), :], sems.at[first + i]
            )
        )
        copies[-1].start()
    return copies


def split_refs(refs, counts):
    groups = []
    for count in counts:
        groups.append(refs[:count])
        refs = refs[count:]
    return groups, refs


def wait_all(copies):
    for copy in copies:
        copy.wait()


def mm(a, b):
    return jnp.dot(a, b, preferred_element_type=f32)


def mm_nt(a, b):
    return lax.dot_general(a, b, (((1,), (1,)), ((), ())), preferred_element_type=f32)


def mm_tn(a, b):
    return lax.dot_general(a, b, (((0,), (0,)), ((), ())), preferred_element_type=f32)


def normalize(stream):
    center = stream - jnp.mean(stream, -1, keepdims=True)
    scaled = lax.rsqrt(jnp.mean(center * center, -1, keepdims=True) + norm_eps)
    return center * scaled, scaled


def norm_backward(upstream, normal, scaled, gain):
    inner = upstream * gain
    return scaled * (
        inner
        - jnp.mean(inner, -1, keepdims=True)
        - normal * jnp.mean(inner * normal, -1, keepdims=True)
    )


def column_sum(value):
    return jnp.sum(value, 0, keepdims=True)


def interleave(even, odd, scr):
    tiles, rows, _ = scr.shape
    for tile in range(tiles):
        cols = slice(tile * 128, (tile + 1) * 128)
        scr[tile, pl.ds(0, rows // 2, stride=2), :] = even[:, cols]
        scr[tile, pl.ds(1, rows // 2, stride=2), :] = odd[:, cols]
    return jnp.concatenate([scr[tile] for tile in range(tiles)], 1)


def split_rows(value, scr):
    tiles, rows, _ = scr.shape
    for tile in range(tiles):
        scr[tile] = value[:, tile * 128 : (tile + 1) * 128]
    even = [scr[tile, pl.ds(0, rows // 2, stride=2), :] for tile in range(tiles)]
    odd = [scr[tile, pl.ds(1, rows // 2, stride=2), :] for tile in range(tiles)]
    return jnp.concatenate(even, 1), jnp.concatenate(odd, 1)


def first_half():
    lane = lax.broadcasted_iota(jnp.int32, (1, 128), 1)
    return lane % HEAD_DIM < HEAD_DIM // 2


def rotate(tile, cos, sin):
    swapped = jnp.where(first_half(), pltpu.roll(tile, 96, 1), pltpu.roll(tile, 32, 1))
    return tile * cos + swapped * sin


def head_lanes():
    lane = lax.broadcasted_iota(jnp.int32, (1, GROUP * HEAD_DIM), 1) // HEAD_DIM
    return [(lane == head) for head in range(GROUP)]


def stack_heads(block, lanes):
    return jnp.concatenate([block * mask.astype(bf16) for mask in lanes], 0)


def unstack_heads(block, lanes):
    rows = block.shape[0] // GROUP
    out = block[:rows]
    for head in range(1, GROUP):
        out = jnp.where(lanes[head], block[head * rows : (head + 1) * rows], out)
    return out


def lowest_key(query, cut):
    low = jnp.maximum(query - (CONTEXT - 1), 0)
    return jnp.where(query >= cut, jnp.maximum(low, cut), low)


def attend(q_ref, k_ref, v_ref, att_ref, sc_ref, rows, first_query, first_key, keys, at_row):
    start, cut = sc_ref[0], sc_ref[1]
    query = start + first_query + lax.broadcasted_iota(jnp.int32, (rows, 1), 0)
    low = lowest_key(query, cut)
    key = start + first_key + lax.broadcasted_iota(jnp.int32, (rows, keys), 1)
    mask = (key <= query) & (key >= low)
    mask = jnp.concatenate([mask] * GROUP, 0)
    lanes = head_lanes()
    key_row = first_key + HALO
    for group in range(HEADS // GROUP):
        cols = slice(group * GROUP * HEAD_DIM, (group + 1) * GROUP * HEAD_DIM)
        stacked = stack_heads(q_ref[at_row : at_row + rows, cols], lanes)
        scores = mm_nt(stacked, k_ref[key_row : key_row + keys, cols]) * HEAD_DIM ** (-0.5)
        scores = jnp.where(mask, scores, -1e30)
        exponent = jnp.exp(scores - jnp.max(scores, -1, keepdims=True))
        weights = exponent * (1.0 / jnp.sum(exponent, -1, keepdims=True))
        mixed = mm(weights.astype(bf16), v_ref[key_row : key_row + keys, cols])
        att_ref[at_row : at_row + rows, cols] = unstack_heads(mixed, lanes).astype(bf16)


def front(x, vec_ref, base, w_in, cos_ref, sin_ref, sc_ref, n1_ref, q_ref, k_ref, v_ref, att_ref,
          extra):
    width = x.shape[1]
    normal, _ = normalize(x)
    low = (normal * vec_ref[base : base + 1] + vec_ref[base + 1 : base + 2]).astype(bf16)
    n1_ref[...] = low[HALO:]
    skip = HALO - extra
    queries = mm(low[skip:], w_in[:, :width])
    keys = mm(low, w_in[:, width : 2 * width])
    for at in range(0, width, 128):
        q_ref[:, at : at + 128] = rotate(
            queries[:, at : at + 128], cos_ref[skip:], sin_ref[skip:]
        ).astype(bf16)
        k_ref[:, at : at + 128] = rotate(keys[:, at : at + 128], cos_ref[...], sin_ref[...]).astype(
            bf16
        )
    v_ref[...] = mm(low, w_in[:, 2 * width :]).astype(bf16)
    frames = x.shape[0] - HALO
    if extra:
        attend(q_ref, k_ref, v_ref, att_ref, sc_ref, extra, -extra, -HALO, HALO, 0)
    for first in range(0, frames, QUERIES):
        attend(
            q_ref, k_ref, v_ref, att_ref, sc_ref, QUERIES, first, first - HALO, WINDOW,
            extra + first,
        )


def decoder_front_kernel(sc_ref, *refs):
    pieces, refs = refs[:PIECES], refs[PIECES:]
    (qz_ref, vec_ref, cos_ref, sin_ref, x_ref, restored_ref, n1_ref, q_ref, k_ref, v_ref, att_ref,
     w_vmem, x_scr, sems) = refs
    width = x_ref.shape[1]
    wait_all(fetch(sc_ref, pieces, 0, w_vmem.shape[1], w_vmem, sems))
    latent = qz_ref.shape[1]
    restored = mm_nt(qz_ref[...], w_vmem[:, :latent]).astype(bf16)
    restored_ref[...] = restored[CODE_HALO - 16 :]
    both = mm(restored, w_vmem[:, latent : latent + 4 * width])
    bias = vec_ref[7:8]
    now = both[16:, : 2 * width]
    before = pltpu.roll(both[:, 2 * width :], 1, 0)[16:]
    total = now + before
    x = interleave(total[:, :width] + bias, total[:, width:] + bias, x_scr)
    x_ref[...] = x[HALO:]
    w_in = w_vmem.at[:, latent + 4 * width :]
    front(x, vec_ref, 8, w_in, cos_ref, sin_ref, sc_ref, n1_ref, q_ref, k_ref, v_ref,
          att_ref, 0)


def encoder_front_kernel(sc_ref, *refs):
    (pieces,), refs = split_refs(refs, (4,))
    (halo_ref, x_ref, vec_ref, cos_ref, sin_ref, n1_ref, q_ref, k_ref, v_ref, att_ref,
     w_vmem, sems) = refs
    width = x_ref.shape[1]
    copies = fetch(sc_ref, pieces, 0, 3 * width, w_vmem, sems)
    x = jnp.concatenate([halo_ref[...], x_ref[...]], 0).astype(f32)
    wait_all(copies)
    front(x, vec_ref, 0, w_vmem, cos_ref, sin_ref, sc_ref, n1_ref, q_ref, k_ref, v_ref, att_ref,
          EXTRA)


def gelu_both(hidden):
    share = 0.5 * (1.0 + lax.erf(hidden * 0.7071067811865476))
    density = jnp.exp(-0.5 * hidden * hidden) * 0.3989422804014327
    return hidden * share, share + hidden * density


def l2_rows(w, at, chunk, width):
    rows = width // 4
    return jnp.concatenate(
        [
            w[chunk * rows : (chunk + 1) * rows, at + g * width : at + (g + 1) * width]
            for g in range(4)
        ],
        0,
    )


def fetch_layer(sc_ref, groups, plan, width, w_vmem, sems):
    edges = (0, width, 5 * width, 9 * width)
    return [
        fetch(
            sc_ref, groups[plan[i][0]], plan[i][1], high - low, w_vmem.at[:, low:high], sems,
            PIECES * i,
        )
        for i, (low, high) in enumerate(zip(edges[:-1], edges[1:]))
    ]


def ff_forward(base, extra, copies, w_vmem, att_ref, stream, vec_ref, out_ref, n2_ref, active_ref,
               slope_ref, mid_ref, second_ref, h_scr, act_scr):
    rows, width = stream.shape
    scale_one = vec_ref[base + 2 : base + 3]
    gain_two = vec_ref[base + 3 : base + 4]
    bias_two = vec_ref[base + 4 : base + 5]
    scale_two = vec_ref[base + 5 : base + 6]
    wait_all(copies[0])
    middle = stream + scale_one * mm(att_ref[...], w_vmem[:, :width])
    mid_ref[...] = middle[extra:]
    normal, _ = normalize(middle)
    n2 = (normal * gain_two + bias_two).astype(bf16)
    n2_ref[...] = n2[extra:]
    wait_all(copies[1])
    l1_at, l2_at = width, 5 * width
    second = None
    for chunk in range(4):
        cols = slice(chunk * width, (chunk + 1) * width)
        h_scr[...] = mm(n2, w_vmem[:, l1_at + chunk * width : l1_at + (chunk + 1) * width])
        if extra:
            act, _ = gelu_both(h_scr[:extra, :])
            act_scr[:extra, cols] = act.astype(bf16)

        def body(i, _):
            at_row = pl.multiple_of(i * 16, 16)
            act, slope = gelu_both(h_scr[pl.ds(at_row + extra, 16), :])
            act_scr[pl.ds(at_row + extra, 16), cols] = act.astype(bf16)
            slope_ref[pl.ds(at_row, 16), cols] = slope
            return 0

        lax.fori_loop(0, (rows - extra) // 16, body, 0)
        if chunk == 0:
            wait_all(copies[2])
        part = mm(act_scr[:, cols], l2_rows(w_vmem, l2_at, chunk, width))
        second = part if second is None else second + part
    active_ref[...] = act_scr[extra:, :]
    second_ref[...] = second[extra:]
    out_ref[...] = (middle + scale_two * second).astype(bf16)


def ff_backward(base, extra, w_vmem, att_ref, g, vec_ref, slope_ref, mid_ref, second_ref, gmid_ref,
                dh_ref, dtwo_ref, done_ref, vg_ref, datt_scr):
    width = g.shape[1]
    scale_one = vec_ref[base + 2 : base + 3]
    gain_two = vec_ref[base + 3 : base + 4]
    scale_two = vec_ref[base + 5 : base + 6]
    l1_at, l2_at = width, 5 * width
    vg_ref[3:4, :] = column_sum(g * second_ref[...])
    d_two = (g * scale_two).astype(bf16)
    dtwo_ref[...] = d_two
    e = None
    for chunk in range(4):
        cols = slice(chunk * width, (chunk + 1) * width)
        d_active = mm_nt(d_two, l2_rows(w_vmem, l2_at, chunk, width))
        dh_ref[:, cols] = (d_active * slope_ref[:, cols]).astype(bf16)
        part = mm_nt(
            dh_ref[:, cols], w_vmem[:, l1_at + chunk * width : l1_at + (chunk + 1) * width]
        )
        e = part if e is None else e + part
    normal, scaled = normalize(mid_ref[...])
    vg_ref[1:2, :] = column_sum(e * normal)
    vg_ref[2:3, :] = column_sum(e)
    g_mid = g + norm_backward(e, normal, scaled, gain_two)
    gmid_ref[...] = g_mid
    vg_ref[0:1, :] = column_sum(g_mid * mm(att_ref[extra:, :], w_vmem[:, :width]))
    d_one = (g_mid * scale_one).astype(bf16)
    done_ref[...] = d_one
    datt_scr[...] = mm_nt(d_one, w_vmem[:, :width]).astype(bf16)


def decoder_layer_kernel(plan, sc_ref, *refs):
    (pieces,), refs = split_refs(refs, (4,))
    (att_ref, x_ref, g_ref, vec_ref, q_ref, k_ref, v_ref,
     out_ref, n2_ref, active_ref, gmid_ref, dh_ref, dtwo_ref, done_ref, vg_ref,
     dq_ref, dk_ref, dv_ref, dkh_ref, dvh_ref,
     w_vmem, h_scr, act_scr, slope_scr, mid_scr, second_scr, datt_scr, dk_scr, dv_scr, sems) = refs
    width = x_ref.shape[1]
    copies = fetch_layer(sc_ref, (pieces,), plan, width, w_vmem, sems)
    ff_forward(8, 0, copies, w_vmem, att_ref, x_ref[...], vec_ref, out_ref, n2_ref, active_ref,
               slope_scr, mid_scr, second_scr, h_scr, act_scr)
    ff_backward(8, 0, w_vmem, att_ref, g_ref[...].astype(f32), vec_ref, slope_scr, mid_scr,
                second_scr, gmid_ref, dh_ref, dtwo_ref, done_ref, vg_ref, datt_scr)
    attention_backward(0, sc_ref, q_ref, k_ref, v_ref, datt_scr, dq_ref, dk_ref, dv_ref, dkh_ref,
                       dvh_ref, dk_scr, dv_scr)


def encoder_forward_kernel(plan, sc_ref, *refs):
    groups, refs = split_refs(refs, (4, 4))
    (halo_ref, x_ref, att_ref, vec_ref,
     out_ref, n2_ref, active_ref, slope_ref, mid_ref, second_ref,
     w_vmem, h_scr, act_scr, sems) = refs
    width = x_ref.shape[1]
    copies = fetch_layer(sc_ref, groups, plan, width, w_vmem, sems)
    stream = jnp.concatenate([halo_ref[HALO - EXTRA :, :], x_ref[...]], 0).astype(f32)
    ff_forward(0, EXTRA, copies, w_vmem, att_ref, stream, vec_ref, out_ref, n2_ref, active_ref,
               slope_ref, mid_ref, second_ref, h_scr, act_scr)


def encoder_backward_kernel(plan, sc_ref, *refs):
    groups, refs = split_refs(refs, (4, 4))
    (att_ref, g_ref, vec_ref, slope_ref, mid_ref, second_ref, q_ref, k_ref, v_ref,
     gmid_ref, dh_ref, dtwo_ref, done_ref, vg_ref, dq_ref, dk_ref, dv_ref, dkh_ref, dvh_ref,
     w_vmem, datt_scr, dk_scr, dv_scr, sems) = refs
    width = g_ref.shape[1]
    for copies in fetch_layer(sc_ref, groups, plan, width, w_vmem, sems):
        wait_all(copies)
    ff_backward(0, EXTRA, w_vmem, att_ref, g_ref[...], vec_ref, slope_ref, mid_ref, second_ref,
                gmid_ref, dh_ref, dtwo_ref, done_ref, vg_ref, datt_scr)
    attention_backward(EXTRA, sc_ref, q_ref, k_ref, v_ref, datt_scr, dq_ref, dk_ref, dv_ref,
                       dkh_ref, dvh_ref, dk_scr, dv_scr)


def attention_backward(extra, sc_ref, q_ref, k_ref, v_ref, do_ref,
                       dq_ref, dk_ref, dv_ref, dkh_ref, dvh_ref, dk_scr, dv_scr):
    start, cut = sc_ref[0], sc_ref[1]
    frames = do_ref.shape[0]
    lanes = head_lanes()
    scale = HEAD_DIM ** (-0.5)
    dk_scr[...] = jnp.zeros_like(dk_scr)
    dv_scr[...] = jnp.zeros_like(dv_scr)
    wide = GROUP * QUERIES
    for first in range(0, frames, QUERIES):
        lane = lax.broadcasted_iota(jnp.int32, (1, wide), 1) % QUERIES
        query = start + first + lane
        low = lowest_key(query, cut)
        key = start + first - HALO + lax.broadcasted_iota(jnp.int32, (WINDOW, wide), 0)
        mask = (key <= query) & (key >= low)
        for group in range(HEADS // GROUP):
            cols = slice(group * GROUP * HEAD_DIM, (group + 1) * GROUP * HEAD_DIM)
            qs = stack_heads(q_ref[extra + first : extra + first + QUERIES, cols], lanes)
            ds = stack_heads(do_ref[first : first + QUERIES, cols], lanes)
            kw = k_ref[first : first + WINDOW, cols]
            vw = v_ref[first : first + WINDOW, cols]
            scores = jnp.where(mask, mm_nt(kw, qs) * scale, -1e30)
            exponent = jnp.exp(scores - jnp.max(scores, 0, keepdims=True))
            probs = exponent * (1.0 / jnp.sum(exponent, 0, keepdims=True))
            d_probs = mm_nt(vw, ds)
            mean = jnp.sum(probs * d_probs, 0, keepdims=True)
            d_scores = (probs * (d_probs - mean)).astype(bf16)
            dk_scr[first : first + WINDOW, cols] += mm(d_scores, qs)
            dv_scr[first : first + WINDOW, cols] += mm(probs.astype(bf16), ds)
            dq_ref[first : first + QUERIES, cols] = (
                unstack_heads(mm_tn(d_scores, kw), lanes) * scale
            )
    dkh_ref[...] = (dk_scr[:HALO] * scale).astype(bf16)
    dvh_ref[...] = dv_scr[:HALO].astype(bf16)
    dk_ref[...] = dk_scr[HALO:] * scale
    dv_ref[...] = dv_scr[HALO:]


class Packer:
    def __init__(self, core, refs, shares, order):
        self.core, self.refs, self.shares, self.order = core, refs, shares, order

    def put(self, value, at, step=1, phase=0, block0=0):
        if len(self.refs) == 1:
            if step == 1:
                self.refs[0][:, at : at + value.shape[1]] = value.astype(bf16)
            return
        send, keep = self.refs
        cols = slice(at, at + value.shape[1])
        rows = 16
        hi = self.shares // 8
        blocks = value.shape[0] // (rows * step)
        for pair in range(blocks // 2):
            even = value[(2 * pair * step + phase) * rows :][:rows]
            odd = value[((2 * pair + 1) * step + phase) * rows :][:rows]
            block = (block0 + 2 * pair) // 2
            place = {"x": (block % 2, 2), "lo": (block // 2 % 2, 2), "hi": (block // 4, hi)}
            at_row = 0
            for axis in self.order:
                at_row = at_row * place[axis][1] + place[axis][0]
            at_row = at_row * rows
            first = self.core == 0
            keep[at_row : at_row + rows, cols] = jnp.where(first, even, odd).astype(bf16)
            send[at_row : at_row + rows, cols] = jnp.where(first, odd, even).astype(bf16)

    def put_l2(self, value, at, chunk, width):
        if len(self.refs) == 1:
            cols = slice(at + chunk * width, at + (chunk + 1) * width)
            self.refs[0][:, cols] = value.astype(bf16)
            return
        for phase in range(4):
            self.put(value, at + phase * width, 4, phase, chunk * width // 64)


def linear_gradients(pack, n2_ref, active_ref, dh_ref, dtwo_ref):
    width = n2_ref.shape[1]
    for chunk in range(4):
        cols = slice(chunk * width, (chunk + 1) * width)
        pack.put_l2(mm_tn(active_ref[:, cols], dtwo_ref[...]), 0, chunk, width)
        pack.put(mm_tn(n2_ref[...], dh_ref[:, cols]), (4 + chunk) * width)


def decoder_gradients_kernel(shares, sc_ref, n2_ref, active_ref, dh_ref, dtwo_ref, att_ref, done_ref,
                             *refs):
    pack = Packer(sc_ref[2], refs, shares, ORDER_A)
    linear_gradients(pack, n2_ref, active_ref, dh_ref, dtwo_ref)
    pack.put(mm_tn(att_ref[...], done_ref[...]), 8 * n2_ref.shape[1])


def encoder_gradients_kernel(shares, sc_ref, n2_ref, active_ref, dh_ref, dtwo_ref, att_ref, done_ref,
                             win_ref, dred_ref, red_ref, dlat_ref, *refs):
    width = n2_ref.shape[1]
    half = len(refs) // 2
    linear_gradients(
        Packer(sc_ref[2], refs[:half], shares, ORDER_C_ONE), n2_ref, active_ref, dh_ref, dtwo_ref
    )
    pack = Packer(sc_ref[2], refs[half:], shares, ORDER_C_TWO)
    d_reduced = dred_ref[...]
    for tap in range(4):
        pack.put(mm_tn(win_ref[tap], d_reduced), tap * width)
    pack.put(mm_tn(att_ref[EXTRA:, :], done_ref[...]), 4 * width)
    pack.put(mm_tn(red_ref[...], dlat_ref[...]), 5 * width)


def layer_input_gradient(extra_rows, base, dq_ref, dk_ref, dv_ref, dkh_ref, dvh_ref, x, gmid_ref,
                         w_in, vec_ref, cos_ref, sin_ref, dmix_ref, vg_ref):
    frames, width = dq_ref.shape
    later = frames - HALO
    cos, sin = cos_ref[HALO:], -sin_ref[HALO:]
    for at in range(0, width, 128):
        cols = slice(at, at + 128)
        dmix_ref[:, cols] = rotate(dq_ref[:, cols], cos, sin).astype(bf16)
        keys = dk_ref[:, cols]
        keys = jnp.concatenate([keys[:later], keys[later:] + dkh_ref[:, cols].astype(f32)], 0)
        dmix_ref[:, width + at : width + at + 128] = rotate(keys, cos, sin).astype(bf16)
        values = dv_ref[:, cols]
        values = jnp.concatenate([values[:later], values[later:] + dvh_ref[:, cols].astype(f32)], 0)
        dmix_ref[:, 2 * width + at : 2 * width + at + 128] = values.astype(bf16)
    d_normed = mm_nt(dmix_ref[...], w_in[...])
    normal, scaled = normalize(x)
    vg_ref[0:1, :] = column_sum(d_normed * normal)
    vg_ref[1:2, :] = column_sum(d_normed)
    return gmid_ref[...] + norm_backward(d_normed, normal, scaled, vec_ref[base : base + 1])


def decoder_back_kernel(at, sc_ref, *refs):
    pieces, refs = refs[:PIECES], refs[PIECES:]
    (dq_ref, dk_ref, dv_ref, dkh_ref, dvh_ref, x_ref, gmid_ref, vec_ref, cos_ref, sin_ref,
     dup_ref, dmix_ref, vg_ref, w_vmem, sems) = refs
    wait_all(fetch(sc_ref, pieces, at, w_vmem.shape[1], w_vmem, sems))
    grad = layer_input_gradient(
        0, 8, dq_ref, dk_ref, dv_ref, dkh_ref, dvh_ref, x_ref[...], gmid_ref, w_vmem, vec_ref,
        cos_ref, sin_ref, dmix_ref, vg_ref,
    )
    vg_ref[2:3, :] = column_sum(grad)
    dup_ref[...] = grad.astype(bf16)


def encoder_back_kernel(shares, sc_ref, *refs):
    (pieces,), refs = split_refs(refs, (4,))
    (dq_ref, dk_ref, dv_ref, dkh_ref, dvh_ref, x_ref, gmid_ref, vec_ref, cos_ref, sin_ref, n1_ref,
     vgs_ref, grad_ref, *rest) = refs
    refs, (w_vmem, dmix_scr, vg_scr, all_scr, sems) = rest[:-5], rest[-5:]
    width = x_ref.shape[1]
    wait_all(fetch(sc_ref, pieces, 0, w_vmem.shape[1], w_vmem, sems))
    grad = layer_input_gradient(
        0, 0, dq_ref, dk_ref, dv_ref, dkh_ref, dvh_ref, x_ref[...].astype(f32), gmid_ref, w_vmem,
        vec_ref, cos_ref, sin_ref, dmix_scr, vg_scr,
    )
    grad_ref[...] = grad.astype(bf16)
    pack = Packer(sc_ref[2], refs, shares, ORDER_D)
    for part in range(3):
        cols = slice(part * width, (part + 1) * width)
        pack.put(mm_tn(n1_ref[...], dmix_scr[:, cols]), part * width)
    all_scr[...] = jnp.zeros_like(all_scr)
    all_scr[0:2, :] = vg_scr[0:2, :]
    all_scr[2:6, :] = vgs_ref[0:4, :]
    all_scr[6:7, :] = vgs_ref[16:17, :]
    all_scr[7:8, :] = vgs_ref[26:27, :]
    all_scr[8:10, :] = vgs_ref[24:26, :]
    all_scr[10:14, :] = vgs_ref[8:12, :]
    pack.put(all_scr[...].T, 3 * width)


def middle_kernel(shares, sc_ref, *refs):
    (pieces, more), refs = split_refs(refs, (4, 4))
    (dup_ref, next_ref, dmix_ref, n1_ref, restored_ref, qz_ref,
     denc_ref, dred_ref, dlat_ref, vg_ref, *rest) = refs
    refs, (up_vmem, down_vmem, frame_scr, sems) = rest[:-4], rest[-4:]
    frames, width = dup_ref.shape
    latent = qz_ref.shape[1]
    codec = frames // 2
    copies = [
        fetch(sc_ref, pieces, 0, latent + 4 * width, up_vmem, sems),
        fetch(sc_ref, more, 4 * width, 4 * width + latent, down_vmem, sems, PIECES),
    ]
    pairs = codec + 16
    even, odd = split_rows(
        jnp.concatenate([dup_ref[...], next_ref[...]], 0).astype(f32), frame_scr
    )
    both = jnp.concatenate([even, odd], 1).astype(bf16)
    wait_all(copies[0])
    up = up_vmem[:, latent : latent + 4 * width]
    here = mm_nt(both, up[:, : 2 * width])
    later = mm_nt(both, up[:, 2 * width :])
    d_restored = (here + pltpu.roll(later, pairs - 1, 0)).astype(bf16)
    d_latent = mm(d_restored, up_vmem[:, :latent]).astype(bf16)
    wait_all(copies[1])
    d_reduced = mm_nt(d_latent, down_vmem[:, 4 * width :]).astype(bf16)
    dlat_ref[...] = d_latent[:codec]
    dred_ref[...] = d_reduced[:codec]
    vg_ref[0:1, :] = column_sum(d_reduced[:codec].astype(f32))
    taps = [mm_nt(d_reduced, down_vmem[:, tap * width : (tap + 1) * width]) for tap in range(4)]
    denc_ref[...] = interleave(
        taps[2] + pltpu.roll(taps[0], pairs - 1, 0),
        taps[3] + pltpu.roll(taps[1], pairs - 1, 0),
        frame_scr,
    )[:frames]

    pack = Packer(sc_ref[2], refs, shares, ORDER_B)
    for part in range(3):
        cols = slice(part * width, (part + 1) * width)
        pack.put(mm_tn(n1_ref[...], dmix_ref[:, cols]), part * width)
    restored = restored_ref[...]
    own_pairs = both[:codec]
    before = pltpu.roll(restored.astype(f32), 1, 0)[16:].astype(bf16)
    pack.put(mm_tn(restored[16:], own_pairs[:, :width]), 3 * width)
    pack.put(mm_tn(restored[16:], own_pairs[:, width:]), 4 * width)
    pack.put(mm_tn(before, own_pairs[:, :width]), 5 * width)
    pack.put(mm_tn(before, own_pairs[:, width:]), 6 * width)
    pack.put(mm_tn(d_restored[:codec], qz_ref[CODE_HALO:, :]), 7 * width)


def latent_kernel(sc_ref, *refs):
    (pieces,), refs = split_refs(refs, (4,))
    (enc_ref, rows_ref, vec_ref, res_ref, win_ref, red_ref, w_vmem, frame_scr, sems) = refs
    total, width = enc_ref.shape
    copies = fetch(sc_ref, pieces, 4 * width, w_vmem.shape[1], w_vmem, sems)
    inside = (sc_ref[0] > 0).astype(f32)
    rim = enc_ref[:EXTRA].astype(f32) * inside
    skip = EXTRA // 2
    even, odd = split_rows(jnp.concatenate([rim, enc_ref[EXTRA:].astype(f32)], 0), frame_scr)
    win_ref[0] = pltpu.roll(even, 1, 0)[skip:].astype(bf16)
    win_ref[1] = pltpu.roll(odd, 1, 0)[skip:].astype(bf16)
    win_ref[2] = even[skip:].astype(bf16)
    win_ref[3] = odd[skip:].astype(bf16)
    wait_all(copies)
    reduced = vec_ref[6:7]
    for tap in range(4):
        reduced = reduced + mm(win_ref[tap], w_vmem[:, tap * width : (tap + 1) * width])
    reduced = reduced.astype(bf16)
    red_ref[...] = reduced
    remaining = mm(reduced, w_vmem[:, 4 * width :])
    for level in range(rows_ref.shape[0]):
        res_ref[level] = remaining.astype(bf16)
        remaining = remaining - rows_ref[level].astype(f32)


def lookup_kernel(sc_ref, codes_ref, book_ref, qsend_ref, qkeep_ref, rsend_ref, rkeep_ref, q_scr):
    levels, share, latent = book_ref.shape
    total = codes_ref.shape[0]
    codec = total // 4
    base = sc_ref[3]
    core = sc_ref[2]
    entry = lax.broadcasted_iota(jnp.int32, (1, share), 1)
    for level in range(levels):
        picks = (codes_ref[:, level : level + 1] - base == entry).astype(f32).astype(bf16)
        found = mm(picks, book_ref[level])
        q_scr[CODE_HALO:] = found if level == 0 else q_scr[CODE_HALO:] + found
        for x in range(2):
            even = found[(2 * x) * codec :][:codec]
            odd = found[(2 * x + 1) * codec :][:codec]
            rkeep_ref[x, level] = jnp.where(core == 0, even, odd).astype(bf16)
            rsend_ref[x, level] = jnp.where(core == 0, odd, even).astype(bf16)
    q_scr[:CODE_HALO] = jnp.zeros((CODE_HALO, latent), f32)
    for x in range(2):
        even = q_scr[(2 * x) * codec : (2 * x + 1) * codec + CODE_HALO]
        odd = q_scr[(2 * x + 1) * codec : (2 * x + 2) * codec + CODE_HALO]
        qkeep_ref[x] = jnp.where(core == 0, even, odd)
        qsend_ref[x] = jnp.where(core == 0, odd, even)


def collect_kernel(share, sc_ref, own_ref, x_ref, core_ref, far_ref, frame_ref, codes_ref, entry_ref,
                   dead_ref, place_ref, send_ref, keep_ref, cnt_scr):
    levels = codes_ref.shape[0]
    latent = own_ref.shape[2]
    total = codes_ref.shape[1]
    lo = sc_ref[4]
    high = send_ref.shape[0]
    frame = frame_ref[0:1, :]
    ones = jnp.ones((16, total), bf16)
    for level in range(levels):
        used = (entry_ref[:, level : level + 1] == codes_ref[level : level + 1, :]).astype(f32)
        placed = (place_ref[:, level : level + 1] == frame).astype(f32)
        select = jnp.where(dead_ref[:, level : level + 1] == 1, placed, used).astype(bf16)
        rows = jnp.concatenate([ref[level] for ref in (own_ref, x_ref, core_ref, far_ref)], 0)
        sums = mm(select, rows)
        cnt_scr[level : level + 1, :] = mm_nt(ones, used.astype(bf16))[0:1]
        at = slice(level * share, (level + 1) * share)
        for h in range(high):
            even = sums[(2 * h) * share :][:share]
            odd = sums[(2 * h + 1) * share :][:share]
            keep_ref[h, at, :] = jnp.where(lo == 0, even, odd).astype(bf16)
            send_ref[h, at, :] = jnp.where(lo == 0, odd, even).astype(bf16)
    counts = cnt_scr[...]
    upper = jnp.floor(counts * (1.0 / 128.0))
    digits = jnp.concatenate([upper, counts - 128.0 * upper], 0)
    tail = slice(levels * share, levels * share + 2 * levels)
    for h in range(high):
        even = digits[:, (2 * h) * share : (2 * h + 1) * share]
        odd = digits[:, (2 * h + 1) * share : (2 * h + 2) * share]
        keep_ref[h, tail, :] = jnp.zeros((2 * levels, latent), bf16)
        send_ref[h, tail, :] = jnp.zeros((2 * levels, latent), bf16)
        keep_ref[h, tail, :share] = jnp.where(lo == 0, even, odd).astype(bf16)
        send_ref[h, tail, :share] = jnp.where(lo == 0, odd, even).astype(bf16)


def call(kernel, outs, spaces, scratch, args, micros):
    where = {"s": pltpu.SMEM, "v": pltpu.VMEM, "h": pltpu.HBM}
    title = getattr(kernel, "func", kernel).__name__
    return pl.pallas_call(
        kernel,
        name=title,
        out_shape=outs,
        in_specs=[pl.BlockSpec(memory_space=where[s]) for s in spaces],
        out_specs=[pl.BlockSpec(memory_space=pltpu.VMEM) for _ in outs],
        scratch_shapes=scratch,
        compiler_params=pltpu.CompilerParams(vmem_limit_bytes=VMEM_LIMIT),
        cost_estimate=pl.CostEstimate(
            flops=int(micros * 1.1e9), bytes_accessed=1, transcendentals=0
        ),
    )(*args)


def shape(dims, dtype=f32):
    return jax.ShapeDtypeStruct(dims, dtype)


def halve(block, dim, axis, after=None):
    mine = lax.axis_index(axis)
    sent = lax.dynamic_index_in_dim(block, 1 - mine, dim, False)
    kept = lax.dynamic_index_in_dim(block, mine, dim, False)
    got = lax.ppermute(sent, axis, [(0, 1), (1, 0)])
    if after is not None:
        got, _ = tie(got, after)
    return (kept.astype(f32) + got.astype(f32)).astype(block.dtype)


def swap_add(send, keep, axis):
    got = lax.ppermute(send, axis, [(0, 1), (1, 0)])
    return (keep.astype(f32) + got.astype(f32)).astype(keep.dtype)


def sum_over_hi(block):
    parts = lax.all_to_all(block, "hi", 0, 0, tiled=True)
    return jnp.sum(parts.astype(f32), 0)


def shifted(block, distance):
    devices = range(lax.axis_size(SEQ))
    route = [(i - distance, i) for i in devices if i - distance in devices]
    return lax.ppermute(block, SEQ, route)


def packed_outs(width_total, width, shares):
    if width // shares % 16 == 0:
        return [shape((width // 2, width_total), bf16)] * 2
    return [shape((width, width_total), bf16)]


def swap(block, axis):
    return lax.ppermute(block, axis, [(0, 1), (1, 0)])


def tie(*values):
    return lax.optimization_barrier(values)


def spread(share, near):
    return [share, near, swap(share, "core"), swap(near, "core")]


def unfolded_rows(block, shares, l2_at):
    width = block.shape[0]
    full = [block[:, l2_at + i * width : l2_at + (i + 1) * width] for i in range(4)]
    full = jnp.concatenate(full, 0).reshape(shares, 4, width // shares, width)
    full = full.transpose(0, 2, 1, 3).reshape(width, 4 * width)
    return jnp.concatenate([block[:, :l2_at], full, block[:, l2_at + 4 * width :]], 1)


def first_sum(parts, shares, order, l2_at=None):
    if len(parts) == 2:
        return swap_add(*parts, "core")
    (block,) = parts
    if l2_at is not None:
        block = unfolded_rows(block, shares, l2_at)
    width, total = block.shape
    block = block.reshape(shares // 8, 2, 2, 2, width // shares, total)
    block = halve(block, 3, "core")
    places = [("hi", "lo", "x").index(axis) for axis in order]
    return block.transpose(*places, 3, 4).reshape(width // 2, total)


def next_sum(block, axis, after=None):
    rows, total = block.shape
    return halve(block.reshape(2, rows // 2, total), 0, axis, after)


def last_sum(block, high):
    return sum_over_hi(block.reshape(high, -1, block.shape[1]))


def local(
    activations,
    encoder_attention_norm_gain,
    encoder_attention_norm_bias,
    encoder_query_key_value_weight,
    encoder_attention_output_weight,
    encoder_attention_layer_scale,
    encoder_forward_norm_gain,
    encoder_forward_norm_bias,
    encoder_forward_input_weight,
    encoder_forward_output_weight,
    encoder_forward_layer_scale,
    strided_convolution_weight,
    strided_convolution_bias,
    quantizer_input_weight,
    codebook,
    quantizer_output_weight,
    transposed_convolution_weight,
    transposed_convolution_bias,
    decoder_attention_norm_gain,
    decoder_attention_norm_bias,
    decoder_query_key_value_weight,
    decoder_attention_output_weight,
    decoder_attention_layer_scale,
    decoder_forward_norm_gain,
    decoder_forward_norm_bias,
    decoder_forward_input_weight,
    decoder_forward_output_weight,
    decoder_forward_layer_scale,
    cotangent,
    frame_segment_index,
    frame_code_index,
    replace_code_mask,
    replacing_batch_position,
    code_usage_average,
    code_latent_sum_average,
):
    batch_rows, frames, width = activations.shape
    assert batch_rows == 1
    seq_index = lax.axis_index(SEQ)
    seq_count = lax.axis_size(SEQ)
    dp_index = lax.axis_index(DP)
    dp_count = lax.axis_size(DP)
    shares = dp_count * seq_count
    codec = frames // 2
    levels = frame_code_index.shape[2]
    latent = codebook.shape[2]
    book_share = codebook.shape[1]
    core_index = lax.axis_index("core")

    x_index, lo_index = lax.axis_index("x"), lax.axis_index("lo")
    rows_share = width // seq_count
    high = shares // 8
    total_frames = HALO + frames
    code_total = replace_code_mask.shape[1]
    code_share = code_usage_average.shape[1]
    row_frames = codec * seq_count

    vectors = jnp.stack(
        [
            encoder_attention_norm_gain,
            encoder_attention_norm_bias,
            encoder_attention_layer_scale,
            encoder_forward_norm_gain,
            encoder_forward_norm_bias,
            encoder_forward_layer_scale,
            strided_convolution_bias,
            transposed_convolution_bias,
            decoder_attention_norm_gain,
            decoder_attention_norm_bias,
            decoder_attention_layer_scale,
            decoder_forward_norm_gain,
            decoder_forward_norm_bias,
            decoder_forward_layer_scale,
        ]
    )
    vectors = jnp.pad(vectors, ((0, 2), (0, 0)))
    small = jnp.concatenate(
        [frame_code_index.reshape(-1).astype(f32), vectors.reshape(-1).astype(f32)]
    )
    small = lax.all_gather(small, SEQ, axis=0, tiled=False)
    code_count = codec * levels
    row_codes = small[:, :code_count].astype(jnp.int32).reshape(seq_count, codec, levels)
    vectors = small[:, code_count:].reshape(seq_count, 16, -1).transpose(1, 0, 2).reshape(16, width)
    order = [2 * x_index + core_index, 2 * (1 - x_index) + core_index]
    order += [2 * x_index + 1 - core_index, 2 * (1 - x_index) + 1 - core_index]
    cut = jnp.sum((frame_segment_index[0] == 0).astype(jnp.int32))
    scalars = jnp.stack(
        [
            seq_index * frames,
            cut,
            core_index,
            seq_index * book_share,
            lo_index,
            seq_index,
            seq_index,
            seq_index,
        ]
        + [place * rows_share for place in order]
    ).astype(jnp.int32)

    def flat_taps(taps):
        return taps.transpose(1, 0, 2).reshape(taps.shape[1], -1)

    def fold_l2(share):
        return share.reshape(4, -1, width).transpose(1, 0, 2).reshape(-1, 4 * width)

    dec_one = jnp.concatenate(
        [
            quantizer_output_weight.T,
            flat_taps(transposed_convolution_weight),
            decoder_query_key_value_weight,
        ],
        1,
    )
    dec_two = jnp.concatenate(
        [
            decoder_attention_output_weight,
            decoder_forward_input_weight,
            fold_l2(decoder_forward_output_weight),
        ],
        1,
    )
    enc_one = jnp.concatenate(
        [
            encoder_query_key_value_weight,
            encoder_attention_output_weight,
            flat_taps(strided_convolution_weight),
            quantizer_input_weight,
        ],
        1,
    )
    enc_two = jnp.concatenate(
        [encoder_forward_input_weight, fold_l2(encoder_forward_output_weight)], 1
    )
    dec_one, small = tie(dec_one, small)
    dec_one = spread(dec_one, swap(dec_one, "x"))
    activation_halo = shifted(activations[0, frames - HALO :], 1)

    window = codec + CODE_HALO
    qsend, qkeep, rsend, rkeep = call(
        lookup_kernel,
        [shape((2, window, latent))] * 2 + [shape((2, levels, codec, latent), bf16)] * 2,
        "svv",
        [pltpu.VMEM((CODE_HALO + codec * seq_count, latent), f32)],
        (scalars, row_codes.reshape(-1, levels), codebook),
        4,
    )
    quantized = halve(swap_add(qsend, qkeep, "core"), 0, "x").astype(bf16)

    positions = seq_index * frames - HALO + jnp.arange(total_frames, dtype=jnp.int32)
    half_dim = HEAD_DIM // 2
    frequency = jnp.power(10000.0, -jnp.arange(half_dim, dtype=f32) / half_dim)
    angles = positions.astype(f32)[:, None] * frequency[None, :]
    cos, sin = jnp.cos(angles), jnp.sin(angles)
    cos_table = jnp.concatenate([cos] * 4, 1)
    sin_table = jnp.concatenate([-sin, sin, -sin, sin], 1)
    dead_flag = replace_code_mask == 1

    def seq_part(array):
        return lax.dynamic_index_in_dim(
            array.reshape(levels, dp_count, seq_count, code_share), seq_index, 2, False
        ).reshape(levels, dp_count * code_share)

    part_dead = seq_part(replace_code_mask)
    part_place = seq_part(replacing_batch_position)
    part_place = jnp.where(part_place // row_frames == dp_index, part_place % row_frames, -1)
    part_code = seq_part(
        jnp.broadcast_to(jnp.arange(code_total, dtype=jnp.int32), (levels, code_total))
    )
    owner_flag = lax.dynamic_slice_in_dim(
        dead_flag, lax.axis_index(DP + SEQ) * code_share, code_share, 1
    )
    relative_codes = jnp.concatenate([row_codes[i] for i in order], 0).T
    relative_frames = jnp.concatenate(
        [i * codec + jnp.arange(codec, dtype=jnp.int32) for i in order]
    )[None]
    entry_t, dead_t, place_t = part_code.T, part_dead.T, part_place.T
    code_rows = swap_add(rsend, rkeep, "core")
    (quantized, cos_table, sin_table, entry_t, dead_t, place_t, relative_codes, relative_frames,
     owner_flag, dec_two, enc_one, enc_two, code_rows) = tie(
        quantized, cos_table, sin_table, entry_t, dead_t, place_t, relative_codes, relative_frames,
        owner_flag, dec_two, enc_one, enc_two, code_rows,
    )
    near_two = swap(dec_two, "x")
    dec_two = spread(dec_two, near_two)

    d_x, restored, d_n1, d_q, d_k, d_v, d_att = call(
        decoder_front_kernel,
        [
            shape((frames, width)),
            shape((codec + 16, width), bf16),
            shape((frames, width), bf16),
            shape((frames, width), bf16),
            shape((total_frames, width), bf16),
            shape((total_frames, width), bf16),
            shape((frames, width), bf16),
        ],
        "shhhhvvvv",
        [
            pltpu.VMEM((width, latent + 7 * width), bf16),
            pltpu.VMEM((width // 128, total_frames, 128), f32),
            pltpu.SemaphoreType.DMA((PIECES,)),
        ],
        (scalars, *dec_one, quantized, vectors, cos_table, sin_table),
        8,
    )
    enc_one, near_two, d_att = tie(enc_one, near_two, d_att)
    near_three = swap(enc_one, "x")
    layer_scratch = [
        pltpu.VMEM((frames, width), bf16),
        pltpu.VMEM((total_frames, width), f32),
        pltpu.VMEM((total_frames, width), f32),
        pltpu.SemaphoreType.DMA((3 * PIECES,)),
    ]
    forward_outs = [shape((frames, width), bf16), shape((frames, 4 * width), bf16)]
    kept_outs = [shape((frames, 4 * width)), shape((frames, width)), shape((frames, width))]
    backward_outs = [
        shape((frames, width)),
        shape((frames, 4 * width), bf16),
        shape((frames, width), bf16),
        shape((frames, width), bf16),
        shape((8, width)),
        shape((frames, width)),
        shape((frames, width)),
        shape((frames, width)),
        shape((HALO, width), bf16),
        shape((HALO, width), bf16),
    ]
    weights_scratch = pltpu.VMEM((width, 9 * width), bf16)
    (output, d_n2, d_active, d_gmid, d_dh, d_dtwo, d_done, d_vg_two, d_dq, d_dk, d_dv, d_dkh,
     d_dvh) = call(
        partial(decoder_layer_kernel, ((0, 0), (0, width), (0, 5 * width))),
        [shape((frames, width), bf16)] + forward_outs + backward_outs,
        "shhhhvvvvvvv",
        [
            weights_scratch,
            pltpu.VMEM((frames, width), f32),
            pltpu.VMEM((frames, 4 * width), bf16),
            pltpu.VMEM((frames, 4 * width), f32),
            pltpu.VMEM((frames, width), f32),
            pltpu.VMEM((frames, width), f32),
        ]
        + layer_scratch,
        (scalars, *dec_two, d_att, d_x, cotangent[0], vectors, d_q, d_k, d_v),
        14,
    )
    enc_two, near_three, d_n2, d_dkh, d_dvh = tie(enc_two, near_three, d_n2, d_dkh, d_dvh)
    near_four = swap(enc_two, "x")
    enc_one = spread(enc_one, near_three)
    d_dkh, d_dvh = shifted(d_dkh, -1), shifted(d_dvh, -1)
    group_a = call(
        partial(decoder_gradients_kernel, shares),
        packed_outs(9 * width, width, shares),
        "svvvvvv",
        [],
        (scalars, d_n2, d_active, d_dh, d_dtwo, d_att, d_done),
        5,
    )
    d_dq, *group_a = tie(d_dq, *group_a)
    a_sum = first_sum(group_a, shares, ORDER_A, 0)
    d_up, d_mixed, d_vg_one = call(
        partial(decoder_back_kernel, latent + 4 * width),
        [shape((frames, width), bf16), shape((frames, 3 * width), bf16), shape((8, width))],
        "shhhh" + "v" * 10,
        [pltpu.VMEM((width, 3 * width), bf16), pltpu.SemaphoreType.DMA((PIECES,))],
        (
            scalars, *dec_one, d_dq, d_dk, d_dv, d_dkh, d_dvh, d_x, d_gmid, vectors, cos_table,
            sin_table,
        ),
        4,
    )
    d_up_next = shifted(d_up[:32], -1)

    a_sum, d_up, e_input = tie(a_sum, d_up, activations[0])
    e_n1, e_q, e_k, e_v, e_att = call(
        encoder_front_kernel,
        [
            shape((frames, width), bf16),
            shape((frames + EXTRA, width), bf16),
            shape((total_frames, width), bf16),
            shape((total_frames, width), bf16),
            shape((frames + EXTRA, width), bf16),
        ],
        "shhhhvvvvv",
        [pltpu.VMEM((width, 3 * width), bf16), pltpu.SemaphoreType.DMA((PIECES,))],
        (scalars, *enc_one, activation_halo, e_input, vectors, cos_table, sin_table),
        7,
    )

    d_mixed, e_n1 = tie(d_mixed, e_n1)
    middle_outs = call(
        partial(middle_kernel, shares),
        [
            shape((frames, width)),
            shape((codec, width), bf16),
            shape((codec, latent), bf16),
            shape((8, width)),
        ]
        + packed_outs(7 * width + latent, width, shares),
        "shhhhhhhh" + "v" * 6,
        [
            pltpu.VMEM((width, latent + 4 * width), bf16),
            pltpu.VMEM((width, latent + 4 * width), bf16),
            pltpu.VMEM((width // 128, frames + 32, 128), f32),
            pltpu.SemaphoreType.DMA((2 * PIECES,)),
        ],
        (scalars, *dec_one, *enc_one, d_up, d_up_next, d_mixed, d_n1, restored, quantized),
        7,
    )
    d_encoded, d_reduced, d_latent, m_vg = middle_outs[:4]
    b_sum = first_sum(middle_outs[4:], shares, ORDER_B)

    code_rows, near_four = tie(code_rows, near_four)
    enc_two = spread(enc_two, near_four)
    code_rows = halve(code_rows, 0, "x")
    e_att, d_encoded = tie(e_att, d_encoded)
    enc_plan = ((0, 3 * width), (1, 0), (1, 4 * width))
    rows = frames + EXTRA
    encoded, e_n2, e_active, e_slope, e_mid, e_second = call(
        partial(encoder_forward_kernel, enc_plan),
        [shape((rows, width), bf16)] + forward_outs + kept_outs,
        "shhhhhhhhvvvv",
        [
            weights_scratch,
            pltpu.VMEM((rows, width), f32),
            pltpu.VMEM((rows, 4 * width), bf16),
            pltpu.SemaphoreType.DMA((3 * PIECES,)),
        ],
        (scalars, *enc_one, *enc_two, activation_halo, e_input, e_att, vectors),
        6,
    )
    a_sum = next_sum(a_sum, ORDER_A[0])
    encoded, b_sum, a_sum = tie(encoded, b_sum, a_sum)
    b_sum = last_sum(b_sum, high).astype(bf16)
    residuals, windows, reduced = call(
        latent_kernel,
        [
            shape((levels, codec, latent), bf16),
            shape((4, codec, width), bf16),
            shape((codec, width), bf16),
        ],
        "shhhhvvv",
        [
            pltpu.VMEM((width, 4 * width + latent), bf16),
            pltpu.VMEM((width // 128, frames + EXTRA, 128), f32),
            pltpu.SemaphoreType.DMA((PIECES,)),
        ],
        (scalars, *enc_one, encoded, code_rows, vectors),
        3,
    )
    near_res = swap(residuals, "x")
    res_pieces = [residuals, near_res, swap(residuals, "core"), swap(near_res, "core")]

    d_encoded, _ = tie(d_encoded, residuals)
    (e_gmid, e_dh, e_dtwo, e_done, e_vg_two, e_dq, e_dk, e_dv, e_dkh, e_dvh) = call(
        partial(encoder_backward_kernel, enc_plan),
        backward_outs,
        "shhhhhhhh" + "v" * 9,
        [weights_scratch] + layer_scratch,
        (
            scalars, *enc_one, *enc_two, e_att, d_encoded, vectors, e_slope, e_mid, e_second,
            e_q, e_k, e_v,
        ),
        11,
    )
    e_dkh, e_dvh = shifted(e_dkh, -1), shifted(e_dvh, -1)
    c_outs = packed_outs(8 * width, width, shares)
    group_c = call(
        partial(encoder_gradients_kernel, shares),
        c_outs + packed_outs(5 * width + latent, width, shares),
        "s" + "v" * 10,
        [],
        (
            scalars, e_n2, e_active, e_dh, e_dtwo, e_att, e_done, windows, d_reduced, reduced,
            d_latent,
        ),
        6,
    )
    c_one = first_sum(group_c[: len(c_outs)], shares, ORDER_C_ONE, 0)
    c_two = first_sum(group_c[len(c_outs) :], shares, ORDER_C_TWO)
    a_sum = next_sum(a_sum, ORDER_A[1])

    if code_share % 16 == 0:
        tail_rows = levels * code_share
        csend, ckeep = call(
            partial(collect_kernel, code_share),
            [shape((dp_count // 2, tail_rows + 2 * levels, latent), bf16)] * 2,
            "s" + "v" * 9,
            [pltpu.VMEM((levels, dp_count * code_share), f32)],
            (scalars, *res_pieces, relative_frames, relative_codes, entry_t, dead_t, place_t),
            6,
        )
        e_dq, csend, c_one, c_two, a_sum = tie(e_dq, csend, c_one, c_two, a_sum)
    vector_grads = jnp.concatenate([e_vg_two, d_vg_two, m_vg, d_vg_one], 0)
    grad_outs = call(
        partial(encoder_back_kernel, shares),
        [shape((frames, width), bf16)] + packed_outs(3 * width + 128, width, shares),
        "shhhh" + "v" * 12,
        [
            pltpu.VMEM((width, 3 * width), bf16),
            pltpu.VMEM((frames, 3 * width), bf16),
            pltpu.VMEM((8, width), f32),
            pltpu.VMEM((128, width), f32),
            pltpu.SemaphoreType.DMA((PIECES,)),
        ],
        (
            scalars, *enc_one, e_dq, e_dk, e_dv, e_dkh, e_dvh, e_input, e_gmid, vectors,
            cos_table, sin_table, e_n1, vector_grads,
        ),
        5,
    )
    activations_grad = grad_outs[0]

    d_sum = first_sum(grad_outs[1:], shares, ORDER_D)
    c_two = next_sum(c_two, ORDER_C_TWO[0], d_sum)
    c_one = next_sum(c_one, ORDER_C_ONE[0], c_two)
    b_sum, _ = tie(b_sum, c_two)
    b_sum = next_sum(b_sum, ORDER_B[1])
    d_sum = next_sum(d_sum, ORDER_D[0], c_one)
    c_two = next_sum(c_two, ORDER_C_TWO[1], d_sum)
    grads_a = last_sum(a_sum, high)
    if code_share % 16 == 0:
        combined = sum_over_hi(swap_add(csend, ckeep, "lo"))
        summed = combined[:tail_rows].reshape(levels, code_share, latent)
        digits = combined[tail_rows:, :code_share]
        counted = 128.0 * digits[:levels] + digits[levels:]
    else:
        flat_res = jnp.concatenate(res_pieces, 1)
        used = part_code[:, :, None] == relative_codes[:, None, :]
        placed = part_place[:, :, None] == relative_frames[None]
        counts = jnp.sum(used.astype(f32), 2).reshape(levels, dp_count, code_share)
        selects = jnp.where(part_dead[:, :, None] == 1, placed, used).astype(bf16)
        sums = jnp.einsum("lct,ltd->lcd", selects, flat_res, preferred_element_type=f32)
        sums = sums.astype(bf16).reshape(levels, dp_count, code_share, latent)
        summed = lax.psum_scatter(sums, DP, scatter_dimension=1, tiled=False).astype(f32)
        counted = lax.psum_scatter(counts, DP, scatter_dimension=1, tiled=False)
    c_one = next_sum(c_one, ORDER_C_ONE[1])
    d_sum = next_sum(d_sum, ORDER_D[1])
    grads_b = next_sum(b_sum, ORDER_B[2]).astype(f32)
    edge, far_edge = c_one.shape[1], c_one.shape[1] + c_two.shape[1]
    together = last_sum(jnp.concatenate([c_one, c_two, d_sum], 1), high)
    grads_c, grads_c_two, grads_d = (
        together[:, :edge], together[:, edge:far_edge], together[:, far_edge:]
    )

    new_cluster_size = ema_decay * code_usage_average + (1.0 - ema_decay) * counted
    new_embed_sum = jnp.where(
        owner_flag[:, :, None],
        summed * new_cluster_size[:, :, None],
        ema_decay * code_latent_sum_average + (1.0 - ema_decay) * summed,
    )
    new_codebook = new_embed_sum / new_cluster_size[:, :, None]

    def columns(block, at, count):
        return block[:, at * width : (at + count) * width]

    def taps(block):
        return block.reshape(-1, 4, width).transpose(1, 0, 2)

    def unfold(block):
        return block.reshape(-1, 4, width).transpose(1, 0, 2).reshape(-1, width)

    vec = grads_d[:, 3 * width : 3 * width + 16].T
    return (
        output[None],
        activations_grad[None],
        vec[0],
        vec[1],
        columns(grads_d, 0, 3),
        columns(grads_c_two, 4, 1),
        vec[2],
        vec[3],
        vec[4],
        columns(grads_c, 4, 4),
        unfold(columns(grads_c, 0, 4)),
        vec[5],
        taps(columns(grads_c_two, 0, 4)),
        vec[6],
        grads_c_two[:, 5 * width :],
        grads_b[:, 7 * width :].T,
        taps(columns(grads_b, 3, 4)),
        vec[7],
        vec[8],
        vec[9],
        columns(grads_b, 0, 3),
        columns(grads_a, 8, 1),
        vec[10],
        vec[11],
        vec[12],
        columns(grads_a, 4, 4),
        unfold(columns(grads_a, 0, 4)),
        vec[13],
        new_cluster_size,
        new_embed_sum,
        new_codebook,
    )


def solution(mesh):
    grid = mesh.devices
    mesh = jax.sharding.Mesh(
        grid.reshape(grid.shape[0] // 2, 2, grid.shape[1] // 2, 2), ("hi", "lo", "x", "core")
    )
    placed = (
        P(DP, SEQ, None),
        P(SEQ),
        P(SEQ),
        P(SEQ, None),
        P(SEQ, None),
        P(SEQ),
        P(SEQ),
        P(SEQ),
        P(SEQ, None),
        P(SEQ, None),
        P(SEQ),
        P(None, SEQ, None),
        P(SEQ),
        P(SEQ, None),
        P(None, SEQ, None),
        P(None, SEQ),
        P(None, SEQ, None),
        P(SEQ),
        P(SEQ),
        P(SEQ),
        P(SEQ, None),
        P(SEQ, None),
        P(SEQ),
        P(SEQ),
        P(SEQ),
        P(SEQ, None),
        P(SEQ, None),
        P(SEQ),
        P(DP, SEQ, None),
        P(DP, None),
        P(DP, SEQ, None),
        P(),
        P(),
        P(None, DP + SEQ),
        P(None, DP + SEQ, None),
    )
    return jax.shard_map(
        local,
        mesh=mesh,
        in_specs=placed,
        out_specs=(
            P(DP, SEQ, None),
            P(DP, SEQ, None),
            P(DP + SEQ),
            P(DP + SEQ),
            P(DP + SEQ, None),
            P(DP + SEQ, None),
            P(DP + SEQ),
            P(DP + SEQ),
            P(DP + SEQ),
            P(DP + SEQ, None),
            P(DP + SEQ, None),
            P(DP + SEQ),
            P(None, DP + SEQ, None),
            P(DP + SEQ),
            P(DP + SEQ, None),
            P(None, DP + SEQ),
            P(None, DP + SEQ, None),
            P(DP + SEQ),
            P(DP + SEQ),
            P(DP + SEQ),
            P(DP + SEQ, None),
            P(DP + SEQ, None),
            P(DP + SEQ),
            P(DP + SEQ),
            P(DP + SEQ),
            P(DP + SEQ, None),
            P(DP + SEQ, None),
            P(DP + SEQ),
            P(None, DP + SEQ),
            P(None, DP + SEQ, None),
            P(None, DP + SEQ, None),
        ),
        check_vma=False,
    )
```

```python
from functools import partial

import jax
import jax.numpy as jnp
from jax import lax
from jax.experimental import pallas as pl
from jax.experimental.pallas import tpu as pltpu
from jax.sharding import PartitionSpec as P

HEADS = 8
HEAD_DIM = 64
CONTEXT = 250
HALO = 256
CODE_HALO = HALO // 2 + 16
EXTRA = 16
QUERIES = 64
GROUP = 4
WINDOW = HALO + QUERIES
VMEM_LIMIT = 26 * 1024 * 1024
ORDER_A = ("lo", "x", "hi")
ORDER_B = ("hi", "lo", "x")
ORDER_C_ONE = ("x", "lo", "hi")
ORDER_C_TWO = ("lo", "x", "hi")
ORDER_D = ("lo", "x", "hi")
DP = ("hi", "lo")
SEQ = ("x", "core")

norm_eps = 1e-05
ema_decay = 0.9
bf16 = jnp.bfloat16
f32 = jnp.float32


PIECES = 6


def fetch(sc_ref, pieces, at, width, dst, sems, first=0):
    copies = []
    for i, piece in enumerate(pieces):
        rows = piece.shape[0]
        row = pl.multiple_of(sc_ref[8 + i], 64)
        copies.append(
            pltpu.make_async_copy(
                piece.at[:, at : at + width], dst.at[pl.ds(row, rows), :], sems.at[first + i]
            )
        )
        copies[-1].start()
    return copies


def split_refs(refs, counts):
    groups = []
    for count in counts:
        groups.append(refs[:count])
        refs = refs[count:]
    return groups, refs


def wait_all(copies):
    for copy in copies:
        copy.wait()


def mm(a, b):
    return jnp.dot(a, b, preferred_element_type=f32)


def mm_nt(a, b):
    return lax.dot_general(a, b, (((1,), (1,)), ((), ())), preferred_element_type=f32)


def mm_tn(a, b):
    return lax.dot_general(a, b, (((0,), (0,)), ((), ())), preferred_element_type=f32)


def normalize(stream):
    center = stream - jnp.mean(stream, -1, keepdims=True)
    scaled = lax.rsqrt(jnp.mean(center * center, -1, keepdims=True) + norm_eps)
    return center * scaled, scaled


def norm_backward(upstream, normal, scaled, gain):
    inner = upstream * gain
    return scaled * (
        inner
        - jnp.mean(inner, -1, keepdims=True)
        - normal * jnp.mean(inner * normal, -1, keepdims=True)
    )


def column_sum(value):
    return jnp.sum(value, 0, keepdims=True)


def interleave(even, odd, scr):
    tiles, rows, _ = scr.shape
    for tile in range(tiles):
        cols = slice(tile * 128, (tile + 1) * 128)
        scr[tile, pl.ds(0, rows // 2, stride=2), :] = even[:, cols]
        scr[tile, pl.ds(1, rows // 2, stride=2), :] = odd[:, cols]
    return jnp.concatenate([scr[tile] for tile in range(tiles)], 1)


def split_rows(value, scr):
    tiles, rows, _ = scr.shape
    for tile in range(tiles):
        scr[tile] = value[:, tile * 128 : (tile + 1) * 128]
    even = [scr[tile, pl.ds(0, rows // 2, stride=2), :] for tile in range(tiles)]
    odd = [scr[tile, pl.ds(1, rows // 2, stride=2), :] for tile in range(tiles)]
    return jnp.concatenate(even, 1), jnp.concatenate(odd, 1)


def first_half():
    lane = lax.broadcasted_iota(jnp.int32, (1, 128), 1)
    return lane % HEAD_DIM < HEAD_DIM // 2


def rotate(tile, cos, sin):
    swapped = jnp.where(first_half(), pltpu.roll(tile, 96, 1), pltpu.roll(tile, 32, 1))
    return tile * cos + swapped * sin


def head_lanes():
    lane = lax.broadcasted_iota(jnp.int32, (1, GROUP * HEAD_DIM), 1) // HEAD_DIM
    return [(lane == head) for head in range(GROUP)]


def stack_heads(block, lanes):
    return jnp.concatenate([block * mask.astype(bf16) for mask in lanes], 0)


def unstack_heads(block, lanes):
    rows = block.shape[0] // GROUP
    out = block[:rows]
    for head in range(1, GROUP):
        out = jnp.where(lanes[head], block[head * rows : (head + 1) * rows], out)
    return out


def lowest_key(query, cut):
    low = jnp.maximum(query - (CONTEXT - 1), 0)
    return jnp.where(query >= cut, jnp.maximum(low, cut), low)


def attend(q_ref, k_ref, v_ref, att_ref, sc_ref, rows, first_query, first_key, keys, at_row):
    start, cut = sc_ref[0], sc_ref[1]
    query = start + first_query + lax.broadcasted_iota(jnp.int32, (rows, 1), 0)
    low = lowest_key(query, cut)
    key = start + first_key + lax.broadcasted_iota(jnp.int32, (rows, keys), 1)
    mask = (key <= query) & (key >= low)
    mask = jnp.concatenate([mask] * GROUP, 0)
    lanes = head_lanes()
    key_row = first_key + HALO
    for group in range(HEADS // GROUP):
        cols = slice(group * GROUP * HEAD_DIM, (group + 1) * GROUP * HEAD_DIM)
        stacked = stack_heads(q_ref[at_row : at_row + rows, cols], lanes)
        scores = mm_nt(stacked, k_ref[key_row : key_row + keys, cols]) * HEAD_DIM ** (-0.5)
        scores = jnp.where(mask, scores, -1e30)
        exponent = jnp.exp(scores - jnp.max(scores, -1, keepdims=True))
        weights = exponent * (1.0 / jnp.sum(exponent, -1, keepdims=True))
        mixed = mm(weights.astype(bf16), v_ref[key_row : key_row + keys, cols])
        att_ref[at_row : at_row + rows, cols] = unstack_heads(mixed, lanes).astype(bf16)


def front(x, vec_ref, base, w_in, cos_ref, sin_ref, sc_ref, n1_ref, q_ref, k_ref, v_ref, att_ref,
          extra):
    width = x.shape[1]
    normal, _ = normalize(x)
    low = (normal * vec_ref[base : base + 1] + vec_ref[base + 1 : base + 2]).astype(bf16)
    n1_ref[...] = low[HALO:]
    skip = HALO - extra
    queries = mm(low[skip:], w_in[:, :width])
    keys = mm(low, w_in[:, width : 2 * width])
    for at in range(0, width, 128):
        q_ref[:, at : at + 128] = rotate(
            queries[:, at : at + 128], cos_ref[skip:], sin_ref[skip:]
        ).astype(bf16)
        k_ref[:, at : at + 128] = rotate(keys[:, at : at + 128], cos_ref[...], sin_ref[...]).astype(
            bf16
        )
    v_ref[...] = mm(low, w_in[:, 2 * width :]).astype(bf16)
    frames = x.shape[0] - HALO
    if extra:
        attend(q_ref, k_ref, v_ref, att_ref, sc_ref, extra, -extra, -HALO, HALO, 0)
    for first in range(0, frames, QUERIES):
        attend(
            q_ref, k_ref, v_ref, att_ref, sc_ref, QUERIES, first, first - HALO, WINDOW,
            extra + first,
        )


def decoder_front_kernel(sc_ref, *refs):
    pieces, refs = refs[:PIECES], refs[PIECES:]
    (qz_ref, vec_ref, cos_ref, sin_ref, x_ref, restored_ref, n1_ref, q_ref, k_ref, v_ref, att_ref,
     w_vmem, x_scr, sems) = refs
    width = x_ref.shape[1]
    wait_all(fetch(sc_ref, pieces, 0, w_vmem.shape[1], w_vmem, sems))
    latent = qz_ref.shape[1]
    restored = mm_nt(qz_ref[...], w_vmem[:, :latent]).astype(bf16)
    restored_ref[...] = restored[CODE_HALO - 16 :]
    both = mm(restored, w_vmem[:, latent : latent + 4 * width])
    bias = vec_ref[7:8]
    now = both[16:, : 2 * width]
    before = pltpu.roll(both[:, 2 * width :], 1, 0)[16:]
    total = now + before
    x = interleave(total[:, :width] + bias, total[:, width:] + bias, x_scr)
    x_ref[...] = x[HALO:]
    w_in = w_vmem.at[:, latent + 4 * width :]
    front(x, vec_ref, 8, w_in, cos_ref, sin_ref, sc_ref, n1_ref, q_ref, k_ref, v_ref,
          att_ref, 0)


def encoder_front_kernel(sc_ref, *refs):
    (pieces,), refs = split_refs(refs, (PIECES,))
    (halo_ref, x_ref, vec_ref, cos_ref, sin_ref, n1_ref, q_ref, k_ref, v_ref, att_ref,
     w_vmem, sems) = refs
    width = x_ref.shape[1]
    copies = fetch(sc_ref, pieces, 0, 3 * width, w_vmem, sems)
    x = jnp.concatenate([halo_ref[...], x_ref[...]], 0).astype(f32)
    wait_all(copies)
    front(x, vec_ref, 0, w_vmem, cos_ref, sin_ref, sc_ref, n1_ref, q_ref, k_ref, v_ref, att_ref,
          EXTRA)


def gelu_both(hidden):
    share = 0.5 * (1.0 + lax.erf(hidden * 0.7071067811865476))
    density = jnp.exp(-0.5 * hidden * hidden) * 0.3989422804014327
    return hidden * share, share + hidden * density


def l2_rows(w, at, chunk, width):
    rows = width // 4
    return jnp.concatenate(
        [
            w[chunk * rows : (chunk + 1) * rows, at + g * width : at + (g + 1) * width]
            for g in range(4)
        ],
        0,
    )


def fetch_layer(sc_ref, groups, plan, width, w_vmem, sems):
    edges = (0, width, 5 * width, 9 * width)
    return [
        fetch(
            sc_ref, groups[plan[i][0]], plan[i][1], high - low, w_vmem.at[:, low:high], sems,
            PIECES * i,
        )
        for i, (low, high) in enumerate(zip(edges[:-1], edges[1:]))
    ]


def ff_forward(base, extra, copies, w_vmem, att_ref, stream, vec_ref, out_ref, n2_ref, active_ref,
               slope_ref, mid_ref, second_ref, h_scr, act_scr):
    rows, width = stream.shape
    scale_one = vec_ref[base + 2 : base + 3]
    gain_two = vec_ref[base + 3 : base + 4]
    bias_two = vec_ref[base + 4 : base + 5]
    scale_two = vec_ref[base + 5 : base + 6]
    wait_all(copies[0])
    middle = stream + scale_one * mm(att_ref[...], w_vmem[:, :width])
    mid_ref[...] = middle[extra:]
    normal, _ = normalize(middle)
    n2 = (normal * gain_two + bias_two).astype(bf16)
    n2_ref[...] = n2[extra:]
    wait_all(copies[1])
    l1_at, l2_at = width, 5 * width
    second = None
    for chunk in range(4):
        cols = slice(chunk * width, (chunk + 1) * width)
        h_scr[...] = mm(n2, w_vmem[:, l1_at + chunk * width : l1_at + (chunk + 1) * width])
        if extra:
            act, _ = gelu_both(h_scr[:extra, :])
            act_scr[:extra, cols] = act.astype(bf16)

        def body(i, _):
            at_row = pl.multiple_of(i * 16, 16)
            act, slope = gelu_both(h_scr[pl.ds(at_row + extra, 16), :])
            act_scr[pl.ds(at_row + extra, 16), cols] = act.astype(bf16)
            slope_ref[pl.ds(at_row, 16), cols] = slope
            return 0

        lax.fori_loop(0, (rows - extra) // 16, body, 0)
        if chunk == 0:
            wait_all(copies[2])
        part = mm(act_scr[:, cols], l2_rows(w_vmem, l2_at, chunk, width))
        second = part if second is None else second + part
    active_ref[...] = act_scr[extra:, :]
    second_ref[...] = second[extra:]
    out_ref[...] = (middle + scale_two * second).astype(bf16)


def ff_backward(base, extra, w_vmem, att_ref, g, vec_ref, slope_ref, mid_ref, second_ref, gmid_ref,
                dh_ref, dtwo_ref, done_ref, vg_ref, datt_scr):
    width = g.shape[1]
    scale_one = vec_ref[base + 2 : base + 3]
    gain_two = vec_ref[base + 3 : base + 4]
    scale_two = vec_ref[base + 5 : base + 6]
    l1_at, l2_at = width, 5 * width
    vg_ref[3:4, :] = column_sum(g * second_ref[...])
    d_two = (g * scale_two).astype(bf16)
    dtwo_ref[...] = d_two
    e = None
    for chunk in range(4):
        cols = slice(chunk * width, (chunk + 1) * width)
        d_active = mm_nt(d_two, l2_rows(w_vmem, l2_at, chunk, width))
        dh_ref[:, cols] = (d_active * slope_ref[:, cols]).astype(bf16)
        part = mm_nt(
            dh_ref[:, cols], w_vmem[:, l1_at + chunk * width : l1_at + (chunk + 1) * width]
        )
        e = part if e is None else e + part
    normal, scaled = normalize(mid_ref[...])
    vg_ref[1:2, :] = column_sum(e * normal)
    vg_ref[2:3, :] = column_sum(e)
    g_mid = g + norm_backward(e, normal, scaled, gain_two)
    gmid_ref[...] = g_mid
    vg_ref[0:1, :] = column_sum(g_mid * mm(att_ref[extra:, :], w_vmem[:, :width]))
    d_one = (g_mid * scale_one).astype(bf16)
    done_ref[...] = d_one
    datt_scr[...] = mm_nt(d_one, w_vmem[:, :width]).astype(bf16)


def decoder_layer_kernel(plan, sc_ref, *refs):
    (pieces,), refs = split_refs(refs, (PIECES,))
    (att_ref, x_ref, g_ref, vec_ref, q_ref, k_ref, v_ref,
     out_ref, n2_ref, active_ref, gmid_ref, dh_ref, dtwo_ref, done_ref, vg_ref,
     dq_ref, dk_ref, dv_ref, dkh_ref, dvh_ref,
     w_vmem, h_scr, act_scr, slope_scr, mid_scr, second_scr, datt_scr, dk_scr, dv_scr, sems) = refs
    width = x_ref.shape[1]
    copies = fetch_layer(sc_ref, (pieces,), plan, width, w_vmem, sems)
    ff_forward(8, 0, copies, w_vmem, att_ref, x_ref[...], vec_ref, out_ref, n2_ref, active_ref,
               slope_scr, mid_scr, second_scr, h_scr, act_scr)
    ff_backward(8, 0, w_vmem, att_ref, g_ref[...].astype(f32), vec_ref, slope_scr, mid_scr,
                second_scr, gmid_ref, dh_ref, dtwo_ref, done_ref, vg_ref, datt_scr)
    attention_backward(0, sc_ref, q_ref, k_ref, v_ref, datt_scr, dq_ref, dk_ref, dv_ref, dkh_ref,
                       dvh_ref, dk_scr, dv_scr)


def encoder_forward_kernel(plan, sc_ref, *refs):
    groups, refs = split_refs(refs, (PIECES, PIECES))
    (halo_ref, x_ref, att_ref, vec_ref,
     out_ref, n2_ref, active_ref, slope_ref, mid_ref, second_ref,
     w_vmem, h_scr, act_scr, sems) = refs
    width = x_ref.shape[1]
    copies = fetch_layer(sc_ref, groups, plan, width, w_vmem, sems)
    stream = jnp.concatenate([halo_ref[HALO - EXTRA :, :], x_ref[...]], 0).astype(f32)
    ff_forward(0, EXTRA, copies, w_vmem, att_ref, stream, vec_ref, out_ref, n2_ref, active_ref,
               slope_ref, mid_ref, second_ref, h_scr, act_scr)


def encoder_backward_kernel(plan, sc_ref, *refs):
    groups, refs = split_refs(refs, (PIECES, PIECES))
    (att_ref, g_ref, vec_ref, slope_ref, mid_ref, second_ref, q_ref, k_ref, v_ref,
     gmid_ref, dh_ref, dtwo_ref, done_ref, vg_ref, dq_ref, dk_ref, dv_ref, dkh_ref, dvh_ref,
     w_vmem, datt_scr, dk_scr, dv_scr, sems) = refs
    width = g_ref.shape[1]
    for copies in fetch_layer(sc_ref, groups, plan, width, w_vmem, sems):
        wait_all(copies)
    ff_backward(0, EXTRA, w_vmem, att_ref, g_ref[...], vec_ref, slope_ref, mid_ref, second_ref,
                gmid_ref, dh_ref, dtwo_ref, done_ref, vg_ref, datt_scr)
    attention_backward(EXTRA, sc_ref, q_ref, k_ref, v_ref, datt_scr, dq_ref, dk_ref, dv_ref,
                       dkh_ref, dvh_ref, dk_scr, dv_scr)


def attention_backward(extra, sc_ref, q_ref, k_ref, v_ref, do_ref,
                       dq_ref, dk_ref, dv_ref, dkh_ref, dvh_ref, dk_scr, dv_scr):
    start, cut = sc_ref[0], sc_ref[1]
    frames = do_ref.shape[0]
    lanes = head_lanes()
    scale = HEAD_DIM ** (-0.5)
    dk_scr[...] = jnp.zeros_like(dk_scr)
    dv_scr[...] = jnp.zeros_like(dv_scr)
    wide = GROUP * QUERIES
    for first in range(0, frames, QUERIES):
        lane = lax.broadcasted_iota(jnp.int32, (1, wide), 1) % QUERIES
        query = start + first + lane
        low = lowest_key(query, cut)
        key = start + first - HALO + lax.broadcasted_iota(jnp.int32, (WINDOW, wide), 0)
        mask = (key <= query) & (key >= low)
        for group in range(HEADS // GROUP):
            cols = slice(group * GROUP * HEAD_DIM, (group + 1) * GROUP * HEAD_DIM)
            qs = stack_heads(q_ref[extra + first : extra + first + QUERIES, cols], lanes)
            ds = stack_heads(do_ref[first : first + QUERIES, cols], lanes)
            kw = k_ref[first : first + WINDOW, cols]
            vw = v_ref[first : first + WINDOW, cols]
            scores = jnp.where(mask, mm_nt(kw, qs) * scale, -1e30)
            exponent = jnp.exp(scores - jnp.max(scores, 0, keepdims=True))
            probs = exponent * (1.0 / jnp.sum(exponent, 0, keepdims=True))
            d_probs = mm_nt(vw, ds)
            mean = jnp.sum(probs * d_probs, 0, keepdims=True)
            d_scores = (probs * (d_probs - mean)).astype(bf16)
            dk_scr[first : first + WINDOW, cols] += mm(d_scores, qs)
            dv_scr[first : first + WINDOW, cols] += mm(probs.astype(bf16), ds)
            dq_ref[first : first + QUERIES, cols] = (
                unstack_heads(mm_tn(d_scores, kw), lanes) * scale
            )
    dkh_ref[...] = (dk_scr[:HALO] * scale).astype(bf16)
    dvh_ref[...] = dv_scr[:HALO].astype(bf16)
    dk_ref[...] = dk_scr[HALO:] * scale
    dv_ref[...] = dv_scr[HALO:]


class Packer:
    def __init__(self, core, refs, shares, order):
        self.core, self.refs, self.shares, self.order = core, refs, shares, order

    def put(self, value, at, step=1, phase=0, block0=0):
        if len(self.refs) == 1:
            if step == 1:
                self.refs[0][:, at : at + value.shape[1]] = value.astype(bf16)
            return
        send, keep = self.refs
        cols = slice(at, at + value.shape[1])
        rows = 16
        hi = self.shares // 8
        blocks = value.shape[0] // (rows * step)
        for pair in range(blocks // 2):
            even = value[(2 * pair * step + phase) * rows :][:rows]
            odd = value[((2 * pair + 1) * step + phase) * rows :][:rows]
            block = (block0 + 2 * pair) // 2
            place = {"x": (block % 2, 2), "lo": (block // 2 % 2, 2), "hi": (block // 4, hi)}
            at_row = 0
            for axis in self.order:
                at_row = at_row * place[axis][1] + place[axis][0]
            at_row = at_row * rows
            first = self.core == 0
            keep[at_row : at_row + rows, cols] = jnp.where(first, even, odd).astype(bf16)
            send[at_row : at_row + rows, cols] = jnp.where(first, odd, even).astype(bf16)

    def put_l2(self, value, at, chunk, width):
        if len(self.refs) == 1:
            cols = slice(at + chunk * width, at + (chunk + 1) * width)
            self.refs[0][:, cols] = value.astype(bf16)
            return
        for phase in range(4):
            self.put(value, at + phase * width, 4, phase, chunk * width // 64)


def linear_gradients(pack, n2_ref, active_ref, dh_ref, dtwo_ref):
    width = n2_ref.shape[1]
    for chunk in range(4):
        cols = slice(chunk * width, (chunk + 1) * width)
        pack.put_l2(mm_tn(active_ref[:, cols], dtwo_ref[...]), 0, chunk, width)
        pack.put(mm_tn(n2_ref[...], dh_ref[:, cols]), (4 + chunk) * width)


def decoder_gradients_kernel(shares, sc_ref, n2_ref, active_ref, dh_ref, dtwo_ref, att_ref, done_ref,
                             *refs):
    pack = Packer(sc_ref[2], refs, shares, ORDER_A)
    linear_gradients(pack, n2_ref, active_ref, dh_ref, dtwo_ref)
    pack.put(mm_tn(att_ref[...], done_ref[...]), 8 * n2_ref.shape[1])


def encoder_gradients_kernel(shares, sc_ref, n2_ref, active_ref, dh_ref, dtwo_ref, att_ref, done_ref,
                             win_ref, dred_ref, red_ref, dlat_ref, *refs):
    width = n2_ref.shape[1]
    half = len(refs) // 2
    linear_gradients(
        Packer(sc_ref[2], refs[:half], shares, ORDER_C_ONE), n2_ref, active_ref, dh_ref, dtwo_ref
    )
    pack = Packer(sc_ref[2], refs[half:], shares, ORDER_C_TWO)
    d_reduced = dred_ref[...]
    for tap in range(4):
        pack.put(mm_tn(win_ref[tap], d_reduced), tap * width)
    pack.put(mm_tn(att_ref[EXTRA:, :], done_ref[...]), 4 * width)
    pack.put(mm_tn(red_ref[...], dlat_ref[...]), 5 * width)


def layer_input_gradient(extra_rows, base, dq_ref, dk_ref, dv_ref, dkh_ref, dvh_ref, x, gmid_ref,
                         w_in, vec_ref, cos_ref, sin_ref, dmix_ref, vg_ref):
    frames, width = dq_ref.shape
    later = frames - HALO
    cos, sin = cos_ref[HALO:], -sin_ref[HALO:]
    for at in range(0, width, 128):
        cols = slice(at, at + 128)
        dmix_ref[:, cols] = rotate(dq_ref[:, cols], cos, sin).astype(bf16)
        keys = dk_ref[:, cols]
        keys = jnp.concatenate([keys[:later], keys[later:] + dkh_ref[:, cols].astype(f32)], 0)
        dmix_ref[:, width + at : width + at + 128] = rotate(keys, cos, sin).astype(bf16)
        values = dv_ref[:, cols]
        values = jnp.concatenate([values[:later], values[later:] + dvh_ref[:, cols].astype(f32)], 0)
        dmix_ref[:, 2 * width + at : 2 * width + at + 128] = values.astype(bf16)
    d_normed = mm_nt(dmix_ref[...], w_in[...])
    normal, scaled = normalize(x)
    vg_ref[0:1, :] = column_sum(d_normed * normal)
    vg_ref[1:2, :] = column_sum(d_normed)
    return gmid_ref[...] + norm_backward(d_normed, normal, scaled, vec_ref[base : base + 1])


def decoder_back_kernel(at, sc_ref, *refs):
    pieces, refs = refs[:PIECES], refs[PIECES:]
    (dq_ref, dk_ref, dv_ref, dkh_ref, dvh_ref, x_ref, gmid_ref, vec_ref, cos_ref, sin_ref,
     dup_ref, dmix_ref, vg_ref, w_vmem, sems) = refs
    wait_all(fetch(sc_ref, pieces, at, w_vmem.shape[1], w_vmem, sems))
    grad = layer_input_gradient(
        0, 8, dq_ref, dk_ref, dv_ref, dkh_ref, dvh_ref, x_ref[...], gmid_ref, w_vmem, vec_ref,
        cos_ref, sin_ref, dmix_ref, vg_ref,
    )
    vg_ref[2:3, :] = column_sum(grad)
    dup_ref[...] = grad.astype(bf16)


def encoder_back_kernel(shares, sc_ref, *refs):
    (pieces,), refs = split_refs(refs, (PIECES,))
    (dq_ref, dk_ref, dv_ref, dkh_ref, dvh_ref, x_ref, gmid_ref, vec_ref, cos_ref, sin_ref, n1_ref,
     vgs_ref, grad_ref, *rest) = refs
    refs, (w_vmem, dmix_scr, vg_scr, all_scr, sems) = rest[:-5], rest[-5:]
    width = x_ref.shape[1]
    wait_all(fetch(sc_ref, pieces, 0, w_vmem.shape[1], w_vmem, sems))
    grad = layer_input_gradient(
        0, 0, dq_ref, dk_ref, dv_ref, dkh_ref, dvh_ref, x_ref[...].astype(f32), gmid_ref, w_vmem,
        vec_ref, cos_ref, sin_ref, dmix_scr, vg_scr,
    )
    grad_ref[...] = grad.astype(bf16)
    pack = Packer(sc_ref[2], refs, shares, ORDER_D)
    for part in range(3):
        cols = slice(part * width, (part + 1) * width)
        pack.put(mm_tn(n1_ref[...], dmix_scr[:, cols]), part * width)
    all_scr[...] = jnp.zeros_like(all_scr)
    all_scr[0:2, :] = vg_scr[0:2, :]
    all_scr[2:6, :] = vgs_ref[0:4, :]
    all_scr[6:7, :] = vgs_ref[16:17, :]
    all_scr[7:8, :] = vgs_ref[26:27, :]
    all_scr[8:10, :] = vgs_ref[24:26, :]
    all_scr[10:14, :] = vgs_ref[8:12, :]
    pack.put(all_scr[...].T, 3 * width)


def middle_kernel(shares, sc_ref, *refs):
    (pieces, more), refs = split_refs(refs, (PIECES, PIECES))
    (dup_ref, next_ref, dmix_ref, n1_ref, restored_ref, qz_ref,
     denc_ref, dred_ref, dlat_ref, vg_ref, *rest) = refs
    refs, (up_vmem, down_vmem, frame_scr, sems) = rest[:-4], rest[-4:]
    frames, width = dup_ref.shape
    latent = qz_ref.shape[1]
    codec = frames // 2
    copies = [
        fetch(sc_ref, pieces, 0, latent + 4 * width, up_vmem, sems),
        fetch(sc_ref, more, 4 * width, 4 * width + latent, down_vmem, sems, PIECES),
    ]
    pairs = codec + 16
    even, odd = split_rows(
        jnp.concatenate([dup_ref[...], next_ref[...]], 0).astype(f32), frame_scr
    )
    both = jnp.concatenate([even, odd], 1).astype(bf16)
    wait_all(copies[0])
    up = up_vmem[:, latent : latent + 4 * width]
    here = mm_nt(both, up[:, : 2 * width])
    later = mm_nt(both, up[:, 2 * width :])
    d_restored = (here + pltpu.roll(later, pairs - 1, 0)).astype(bf16)
    d_latent = mm(d_restored, up_vmem[:, :latent]).astype(bf16)
    wait_all(copies[1])
    d_reduced = mm_nt(d_latent, down_vmem[:, 4 * width :]).astype(bf16)
    dlat_ref[...] = d_latent[:codec]
    dred_ref[...] = d_reduced[:codec]
    vg_ref[0:1, :] = column_sum(d_reduced[:codec].astype(f32))
    taps = [mm_nt(d_reduced, down_vmem[:, tap * width : (tap + 1) * width]) for tap in range(4)]
    denc_ref[...] = interleave(
        taps[2] + pltpu.roll(taps[0], pairs - 1, 0),
        taps[3] + pltpu.roll(taps[1], pairs - 1, 0),
        frame_scr,
    )[:frames]

    pack = Packer(sc_ref[2], refs, shares, ORDER_B)
    for part in range(3):
        cols = slice(part * width, (part + 1) * width)
        pack.put(mm_tn(n1_ref[...], dmix_ref[:, cols]), part * width)
    restored = restored_ref[...]
    own_pairs = both[:codec]
    before = pltpu.roll(restored.astype(f32), 1, 0)[16:].astype(bf16)
    pack.put(mm_tn(restored[16:], own_pairs[:, :width]), 3 * width)
    pack.put(mm_tn(restored[16:], own_pairs[:, width:]), 4 * width)
    pack.put(mm_tn(before, own_pairs[:, :width]), 5 * width)
    pack.put(mm_tn(before, own_pairs[:, width:]), 6 * width)
    pack.put(mm_tn(d_restored[:codec], qz_ref[CODE_HALO:, :]), 7 * width)


def latent_kernel(sc_ref, *refs):
    (pieces,), refs = split_refs(refs, (PIECES,))
    (enc_ref, rows_ref, vec_ref, res_ref, win_ref, red_ref, w_vmem, frame_scr, sems) = refs
    total, width = enc_ref.shape
    copies = fetch(sc_ref, pieces, 4 * width, w_vmem.shape[1], w_vmem, sems)
    inside = (sc_ref[0] > 0).astype(f32)
    rim = enc_ref[:EXTRA].astype(f32) * inside
    skip = EXTRA // 2
    even, odd = split_rows(jnp.concatenate([rim, enc_ref[EXTRA:].astype(f32)], 0), frame_scr)
    win_ref[0] = pltpu.roll(even, 1, 0)[skip:].astype(bf16)
    win_ref[1] = pltpu.roll(odd, 1, 0)[skip:].astype(bf16)
    win_ref[2] = even[skip:].astype(bf16)
    win_ref[3] = odd[skip:].astype(bf16)
    wait_all(copies)
    reduced = vec_ref[6:7]
    for tap in range(4):
        reduced = reduced + mm(win_ref[tap], w_vmem[:, tap * width : (tap + 1) * width])
    reduced = reduced.astype(bf16)
    red_ref[...] = reduced
    remaining = mm(reduced, w_vmem[:, 4 * width :])
    for level in range(rows_ref.shape[0]):
        res_ref[level] = remaining.astype(bf16)
        remaining = remaining - rows_ref[level].astype(f32)


def lookup_kernel(sc_ref, codes_ref, book_ref, qsend_ref, qkeep_ref, rsend_ref, rkeep_ref, q_scr):
    levels, share, latent = book_ref.shape
    total = codes_ref.shape[0]
    codec = total // 4
    base = sc_ref[3]
    core = sc_ref[2]
    entry = lax.broadcasted_iota(jnp.int32, (1, share), 1)
    for level in range(levels):
        picks = (codes_ref[:, level : level + 1] - base == entry).astype(f32).astype(bf16)
        found = mm(picks, book_ref[level])
        q_scr[CODE_HALO:] = found if level == 0 else q_scr[CODE_HALO:] + found
        for x in range(2):
            even = found[(2 * x) * codec :][:codec]
            odd = found[(2 * x + 1) * codec :][:codec]
            rkeep_ref[x, level] = jnp.where(core == 0, even, odd).astype(bf16)
            rsend_ref[x, level] = jnp.where(core == 0, odd, even).astype(bf16)
    q_scr[:CODE_HALO] = jnp.zeros((CODE_HALO, latent), f32)
    for x in range(2):
        even = q_scr[(2 * x) * codec : (2 * x + 1) * codec + CODE_HALO]
        odd = q_scr[(2 * x + 1) * codec : (2 * x + 2) * codec + CODE_HALO]
        qkeep_ref[x] = jnp.where(core == 0, even, odd)
        qsend_ref[x] = jnp.where(core == 0, odd, even)


def collect_kernel(share, sc_ref, own_ref, x_ref, core_ref, far_ref, frame_ref, codes_ref, entry_ref,
                   dead_ref, place_ref, send_ref, keep_ref, cnt_scr):
    levels = codes_ref.shape[0]
    latent = own_ref.shape[2]
    total = codes_ref.shape[1]
    lo = sc_ref[4]
    high = send_ref.shape[0]
    frame = frame_ref[0:1, :]
    ones = jnp.ones((16, total), bf16)
    for level in range(levels):
        used = (entry_ref[:, level : level + 1] == codes_ref[level : level + 1, :]).astype(f32)
        placed = (place_ref[:, level : level + 1] == frame).astype(f32)
        select = jnp.where(dead_ref[:, level : level + 1] == 1, placed, used).astype(bf16)
        rows = jnp.concatenate([ref[level] for ref in (own_ref, x_ref, core_ref, far_ref)], 0)
        sums = mm(select, rows)
        cnt_scr[level : level + 1, :] = mm_nt(ones, used.astype(bf16))[0:1]
        at = slice(level * share, (level + 1) * share)
        for h in range(high):
            even = sums[(2 * h) * share :][:share]
            odd = sums[(2 * h + 1) * share :][:share]
            keep_ref[h, at, :] = jnp.where(lo == 0, even, odd).astype(bf16)
            send_ref[h, at, :] = jnp.where(lo == 0, odd, even).astype(bf16)
    counts = cnt_scr[...]
    upper = jnp.floor(counts * (1.0 / 128.0))
    digits = jnp.concatenate([upper, counts - 128.0 * upper], 0)
    tail = slice(levels * share, levels * share + 2 * levels)
    for h in range(high):
        even = digits[:, (2 * h) * share : (2 * h + 1) * share]
        odd = digits[:, (2 * h + 1) * share : (2 * h + 2) * share]
        keep_ref[h, tail, :] = jnp.zeros((2 * levels, latent), bf16)
        send_ref[h, tail, :] = jnp.zeros((2 * levels, latent), bf16)
        keep_ref[h, tail, :share] = jnp.where(lo == 0, even, odd).astype(bf16)
        send_ref[h, tail, :share] = jnp.where(lo == 0, odd, even).astype(bf16)


def call(kernel, outs, spaces, scratch, args, micros):
    where = {"s": pltpu.SMEM, "v": pltpu.VMEM, "h": pltpu.HBM}
    title = getattr(kernel, "func", kernel).__name__
    return pl.pallas_call(
        kernel,
        name=title,
        out_shape=outs,
        in_specs=[pl.BlockSpec(memory_space=where[space]) for space in spaces],
        out_specs=[pl.BlockSpec(memory_space=pltpu.VMEM) for _ in outs],
        scratch_shapes=scratch,
        compiler_params=pltpu.CompilerParams(vmem_limit_bytes=VMEM_LIMIT),
        cost_estimate=pl.CostEstimate(
            flops=int(micros * 1.1e9), bytes_accessed=1, transcendentals=0
        ),
    )(*args)


def shape(dims, dtype=f32):
    return jax.ShapeDtypeStruct(dims, dtype)


def pick(block, at):
    zero = jnp.zeros((), jnp.uint32)
    start = (at,) + (zero,) * (block.ndim - 1)
    return lax.dynamic_slice(block, start, (1,) + block.shape[1:])[0]


def halve(block, axis, index, after=None):
    sent = pick(block, index["other " + axis])
    kept = pick(block, index[axis])
    got = lax.ppermute(sent, axis, [(0, 1), (1, 0)])
    if after is not None:
        got, _ = tie(got, after)
    return (kept.astype(f32) + got.astype(f32)).astype(block.dtype)


def sum_by_permutes(block, index):
    count = block.shape[0]
    if count != 4:
        return sum_over_hi(block)
    total = pick(block, index["hi"]).astype(f32)
    for turn in range(1, count):
        sent = pick(block, index["hi ^ %d" % turn])
        got = lax.ppermute(sent, "hi", [(i, i ^ turn) for i in range(count)])
        total = total + got.astype(f32)
    return total


def swap_add(send, keep, axis):
    got = lax.ppermute(send, axis, [(0, 1), (1, 0)])
    return (keep.astype(f32) + got.astype(f32)).astype(keep.dtype)


def sum_over_hi(block):
    parts = lax.all_to_all(block, "hi", 0, 0, tiled=True)
    return jnp.sum(parts.astype(f32), 0)


def shifted(block, distance):
    devices = range(lax.axis_size(SEQ))
    route = [(i - distance, i) for i in devices if i - distance in devices]
    return lax.ppermute(block, SEQ, route)


def packed_outs(width_total, width, shares):
    if width // shares % 16 == 0:
        return [shape((width // 2, width_total), bf16)] * 2
    return [shape((width, width_total), bf16)]


def swap(block, axis):
    return lax.ppermute(block, axis, [(0, 1), (1, 0)])


def tie(*values):
    return lax.optimization_barrier(values)


def near_half(share, index):
    rows = share.shape[0] // 2
    zero = jnp.zeros((), jnp.uint32)
    return swap(lax.dynamic_slice(share, (index["lo"] * rows, zero), (rows, share.shape[1])), "x")


def unfolded_rows(block, shares, l2_at):
    width = block.shape[0]
    full = [block[:, l2_at + i * width : l2_at + (i + 1) * width] for i in range(4)]
    full = jnp.concatenate(full, 0).reshape(shares, 4, width // shares, width)
    full = full.transpose(0, 2, 1, 3).reshape(width, 4 * width)
    return jnp.concatenate([block[:, :l2_at], full, block[:, l2_at + 4 * width :]], 1)


def first_sum(parts, shares, order, index, l2_at=None):
    if len(parts) == 2:
        return swap_add(*parts, "core")
    (block,) = parts
    if l2_at is not None:
        block = unfolded_rows(block, shares, l2_at)
    width, total = block.shape
    block = block.reshape(shares // 8, 2, 2, 2, width // shares, total)
    block = halve(block.transpose(3, 0, 1, 2, 4, 5), "core", index)
    places = [("hi", "lo", "x").index(axis) for axis in order]
    return block.transpose(*places, 3, 4).reshape(width // 2, total)


def next_sum(block, axis, index, after=None):
    rows, total = block.shape
    return halve(block.reshape(2, rows // 2, total), axis, index, after)


def last_sum(block, high):
    return sum_over_hi(block.reshape(high, -1, block.shape[1]))


def local(
    activations,
    encoder_attention_norm_gain,
    encoder_attention_norm_bias,
    encoder_query_key_value_weight,
    encoder_attention_output_weight,
    encoder_attention_layer_scale,
    encoder_forward_norm_gain,
    encoder_forward_norm_bias,
    encoder_forward_input_weight,
    encoder_forward_output_weight,
    encoder_forward_layer_scale,
    strided_convolution_weight,
    strided_convolution_bias,
    quantizer_input_weight,
    codebook,
    quantizer_output_weight,
    transposed_convolution_weight,
    transposed_convolution_bias,
    decoder_attention_norm_gain,
    decoder_attention_norm_bias,
    decoder_query_key_value_weight,
    decoder_attention_output_weight,
    decoder_attention_layer_scale,
    decoder_forward_norm_gain,
    decoder_forward_norm_bias,
    decoder_forward_input_weight,
    decoder_forward_output_weight,
    decoder_forward_layer_scale,
    cotangent,
    frame_segment_index,
    frame_code_index,
    replace_code_mask,
    replacing_batch_position,
    code_usage_average,
    code_latent_sum_average,
):
    batch_rows, frames, width = activations.shape
    assert batch_rows == 1
    seq_index = lax.axis_index(SEQ)
    seq_count = lax.axis_size(SEQ)
    dp_index = lax.axis_index(DP)
    dp_count = lax.axis_size(DP)
    shares = dp_count * seq_count
    codec = frames // 2
    levels = frame_code_index.shape[2]
    latent = codebook.shape[2]
    book_share = codebook.shape[1]
    core_index = lax.axis_index("core")

    x_index, lo_index = lax.axis_index("x"), lax.axis_index("lo")
    rows_share = width // seq_count
    high = shares // 8
    total_frames = HALO + frames
    code_total = replace_code_mask.shape[1]
    code_share = code_usage_average.shape[1]
    row_frames = codec * seq_count

    vectors = jnp.stack(
        [
            encoder_attention_norm_gain,
            encoder_attention_norm_bias,
            encoder_attention_layer_scale,
            encoder_forward_norm_gain,
            encoder_forward_norm_bias,
            encoder_forward_layer_scale,
            strided_convolution_bias,
            transposed_convolution_bias,
            decoder_attention_norm_gain,
            decoder_attention_norm_bias,
            decoder_attention_layer_scale,
            decoder_forward_norm_gain,
            decoder_forward_norm_bias,
            decoder_forward_layer_scale,
        ]
    )
    vectors = jnp.pad(vectors, ((0, 2), (0, 0)))
    small = jnp.concatenate(
        [frame_code_index.reshape(-1).astype(f32), vectors.reshape(-1).astype(f32)]
    )
    small = lax.all_gather(small, SEQ, axis=0, tiled=False)
    index = {}
    unsigned = jnp.uint32
    for axis in ("x", "lo", "core"):
        index[axis] = lax.axis_index(axis).astype(unsigned)
        index["other " + axis] = (1 - lax.axis_index(axis)).astype(unsigned)
    index["hi"] = lax.axis_index("hi").astype(unsigned)
    for turn in range(1, 4):
        index["hi ^ %d" % turn] = lax.axis_index("hi").astype(unsigned) ^ unsigned(turn)
    names = sorted(index)
    *index_values, small = tie(*[index[name] for name in names], small)
    index = dict(zip(names, index_values))
    code_count = codec * levels
    row_codes = small[:, :code_count].astype(jnp.int32).reshape(seq_count, codec, levels)
    vectors = small[:, code_count:].reshape(seq_count, 16, -1).transpose(1, 0, 2).reshape(16, width)
    order = [2 * x_index + core_index, 2 * (1 - x_index) + core_index]
    order += [2 * x_index + 1 - core_index, 2 * (1 - x_index) + 1 - core_index]
    cut = jnp.sum((frame_segment_index[0] == 0).astype(jnp.int32))
    scalars = jnp.stack(
        [
            seq_index * frames,
            cut,
            core_index,
            seq_index * book_share,
            lo_index,
            seq_index,
            seq_index,
            seq_index,
        ]
        + [
            order[0] * rows_share,
            order[1] * rows_share + lo_index * (rows_share // 2),
            order[1] * rows_share + (1 - lo_index) * (rows_share // 2),
            order[2] * rows_share,
            order[3] * rows_share + lo_index * (rows_share // 2),
            order[3] * rows_share + (1 - lo_index) * (rows_share // 2),
        ]
    ).astype(jnp.int32)

    def flat_taps(taps):
        return taps.transpose(1, 0, 2).reshape(taps.shape[1], -1)

    def fold_l2(share):
        return share.reshape(4, -1, width).transpose(1, 0, 2).reshape(-1, 4 * width)

    dec_one = jnp.concatenate(
        [
            quantizer_output_weight.T,
            flat_taps(transposed_convolution_weight),
            decoder_query_key_value_weight,
        ],
        1,
    )
    dec_two = jnp.concatenate(
        [
            decoder_attention_output_weight,
            decoder_forward_input_weight,
            fold_l2(decoder_forward_output_weight),
        ],
        1,
    )
    enc_one = jnp.concatenate(
        [
            encoder_query_key_value_weight,
            encoder_attention_output_weight,
            flat_taps(strided_convolution_weight),
            quantizer_input_weight,
        ],
        1,
    )
    enc_two = jnp.concatenate(
        [encoder_forward_input_weight, fold_l2(encoder_forward_output_weight)], 1
    )
    dec_one, small = tie(dec_one, small)
    near_one = near_half(dec_one, index)
    activation_halo = shifted(activations[0, frames - HALO :], 1)

    window = codec + CODE_HALO
    qsend, qkeep, rsend, rkeep = call(
        lookup_kernel,
        [shape((2, window, latent))] * 2 + [shape((2, levels, codec, latent), bf16)] * 2,
        "svv",
        [pltpu.VMEM((CODE_HALO + codec * seq_count, latent), f32)],
        (scalars, row_codes.reshape(-1, levels), codebook),
        4,
    )
    q_sum = swap_add(qsend, qkeep, "core")
    code_rows = swap_add(rsend, rkeep, "core")
    q_sum, near_one, dec_two, replace_code_mask, replacing_batch_position, row_codes, rsend = tie(
        q_sum, near_one, dec_two, replace_code_mask, replacing_batch_position, row_codes, rsend
    )
    quantized = halve(q_sum, "x", index).astype(bf16)
    near_two = near_half(dec_two, index)
    far_one = swap(near_one, "lo")
    dec_one = [dec_one, near_one, far_one, swap(dec_one, "core"), swap(near_one, "core"),
               swap(far_one, "core")]

    positions = seq_index * frames - HALO + jnp.arange(total_frames, dtype=jnp.int32)
    half_dim = HEAD_DIM // 2
    frequency = jnp.power(10000.0, -jnp.arange(half_dim, dtype=f32) / half_dim)
    angles = positions.astype(f32)[:, None] * frequency[None, :]
    cos, sin = jnp.cos(angles), jnp.sin(angles)
    cos_table = jnp.concatenate([cos] * 4, 1)
    sin_table = jnp.concatenate([-sin, sin, -sin, sin], 1)
    dead_flag = replace_code_mask == 1

    def seq_part(array):
        return lax.dynamic_index_in_dim(
            array.reshape(levels, dp_count, seq_count, code_share), seq_index, 2, False
        ).reshape(levels, dp_count * code_share)

    part_dead = seq_part(replace_code_mask)
    part_place = seq_part(replacing_batch_position)
    part_place = jnp.where(part_place // row_frames == dp_index, part_place % row_frames, -1)
    part_code = seq_part(
        jnp.broadcast_to(jnp.arange(code_total, dtype=jnp.int32), (levels, code_total))
    )
    owner_flag = lax.dynamic_slice_in_dim(
        dead_flag, lax.axis_index(DP + SEQ) * code_share, code_share, 1
    )
    relative_codes = jnp.concatenate([row_codes[i] for i in order], 0).T
    relative_frames = jnp.concatenate(
        [i * codec + jnp.arange(codec, dtype=jnp.int32) for i in order]
    )[None]
    entry_t, dead_t, place_t = part_code.T, part_dead.T, part_place.T
    quantized, near_two, enc_one = tie(quantized, near_two, enc_one)
    far_two = swap(near_two, "lo")
    near_three = near_half(enc_one, index)

    d_x, restored, d_n1, d_q, d_k, d_v, d_att = call(
        decoder_front_kernel,
        [
            shape((frames, width)),
            shape((codec + 16, width), bf16),
            shape((frames, width), bf16),
            shape((frames, width), bf16),
            shape((total_frames, width), bf16),
            shape((total_frames, width), bf16),
            shape((frames, width), bf16),
        ],
        "s" + "h" * PIECES + "vvvv",
        [
            pltpu.VMEM((width, latent + 7 * width), bf16),
            pltpu.VMEM((width // 128, total_frames, 128), f32),
            pltpu.SemaphoreType.DMA((PIECES,)),
        ],
        (scalars, *dec_one, quantized, vectors, cos_table, sin_table),
        8,
    )
    (d_att, far_two, near_three, enc_two, entry_t, dead_t, place_t, relative_codes, relative_frames,
     owner_flag, code_rows) = tie(
        d_att, far_two, near_three, enc_two, entry_t, dead_t, place_t, relative_codes,
        relative_frames, owner_flag, code_rows,
    )
    dec_two = [dec_two, near_two, far_two, swap(dec_two, "core"), swap(near_two, "core"),
               swap(far_two, "core")]
    far_three = swap(near_three, "lo")
    near_four = near_half(enc_two, index)
    layer_scratch = [
        pltpu.VMEM((frames, width), bf16),
        pltpu.VMEM((total_frames, width), f32),
        pltpu.VMEM((total_frames, width), f32),
        pltpu.SemaphoreType.DMA((3 * PIECES,)),
    ]
    forward_outs = [shape((frames, width), bf16), shape((frames, 4 * width), bf16)]
    kept_outs = [shape((frames, 4 * width)), shape((frames, width)), shape((frames, width))]
    backward_outs = [
        shape((frames, width)),
        shape((frames, 4 * width), bf16),
        shape((frames, width), bf16),
        shape((frames, width), bf16),
        shape((8, width)),
        shape((frames, width)),
        shape((frames, width)),
        shape((frames, width)),
        shape((HALO, width), bf16),
        shape((HALO, width), bf16),
    ]
    weights_scratch = pltpu.VMEM((width, 9 * width), bf16)
    (output, d_n2, d_active, d_gmid, d_dh, d_dtwo, d_done, d_vg_two, d_dq, d_dk, d_dv, d_dkh,
     d_dvh) = call(
        partial(decoder_layer_kernel, ((0, 0), (0, width), (0, 5 * width))),
        [shape((frames, width), bf16)] + forward_outs + backward_outs,
        "s" + "h" * PIECES + "vvvvvvv",
        [
            weights_scratch,
            pltpu.VMEM((frames, width), f32),
            pltpu.VMEM((frames, 4 * width), bf16),
            pltpu.VMEM((frames, 4 * width), f32),
            pltpu.VMEM((frames, width), f32),
            pltpu.VMEM((frames, width), f32),
        ]
        + layer_scratch,
        (scalars, *dec_two, d_att, d_x, cotangent[0], vectors, d_q, d_k, d_v),
        14,
    )
    d_n2, far_three, near_four = tie(d_n2, far_three, near_four)
    enc_one = [enc_one, near_three, far_three, swap(enc_one, "core"), swap(near_three, "core"),
               swap(far_three, "core")]
    far_four = swap(near_four, "lo")
    d_dkh, d_dvh = shifted(d_dkh, -1), shifted(d_dvh, -1)
    group_a = call(
        partial(decoder_gradients_kernel, shares),
        packed_outs(9 * width, width, shares),
        "svvvvvv",
        [],
        (scalars, d_n2, d_active, d_dh, d_dtwo, d_att, d_done),
        5,
    )
    d_dq, *group_a = tie(d_dq, *group_a)
    a_sum = first_sum(group_a, shares, ORDER_A, index, 0)
    d_up, d_mixed, d_vg_one = call(
        partial(decoder_back_kernel, latent + 4 * width),
        [shape((frames, width), bf16), shape((frames, 3 * width), bf16), shape((8, width))],
        "s" + "h" * PIECES + "" + "v" * 10,
        [pltpu.VMEM((width, 3 * width), bf16), pltpu.SemaphoreType.DMA((PIECES,))],
        (
            scalars, *dec_one, d_dq, d_dk, d_dv, d_dkh, d_dvh, d_x, d_gmid, vectors, cos_table,
            sin_table,
        ),
        4,
    )
    d_up_next = shifted(d_up[:32], -1)

    code_rows, d_dkh = tie(code_rows, d_dkh)
    code_rows = halve(code_rows, "x", index)

    a_sum, d_up, e_input, far_four = tie(a_sum, d_up, activations[0], far_four)
    enc_two = [enc_two, near_four, far_four, swap(enc_two, "core"), swap(near_four, "core"),
               swap(far_four, "core")]
    e_n1, e_q, e_k, e_v, e_att = call(
        encoder_front_kernel,
        [
            shape((frames, width), bf16),
            shape((frames + EXTRA, width), bf16),
            shape((total_frames, width), bf16),
            shape((total_frames, width), bf16),
            shape((frames + EXTRA, width), bf16),
        ],
        "s" + "h" * PIECES + "vvvvv",
        [pltpu.VMEM((width, 3 * width), bf16), pltpu.SemaphoreType.DMA((PIECES,))],
        (scalars, *enc_one, activation_halo, e_input, vectors, cos_table, sin_table),
        7,
    )

    d_mixed, e_n1 = tie(d_mixed, e_n1)
    middle_outs = call(
        partial(middle_kernel, shares),
        [
            shape((frames, width)),
            shape((codec, width), bf16),
            shape((codec, latent), bf16),
            shape((8, width)),
        ]
        + packed_outs(7 * width + latent, width, shares),
        "s" + "h" * (2 * PIECES) + "" + "v" * 6,
        [
            pltpu.VMEM((width, latent + 4 * width), bf16),
            pltpu.VMEM((width, latent + 4 * width), bf16),
            pltpu.VMEM((width // 128, frames + 32, 128), f32),
            pltpu.SemaphoreType.DMA((2 * PIECES,)),
        ],
        (scalars, *dec_one, *enc_one, d_up, d_up_next, d_mixed, d_n1, restored, quantized),
        7,
    )
    d_encoded, d_reduced, d_latent, m_vg = middle_outs[:4]
    b_sum = first_sum(middle_outs[4:], shares, ORDER_B, index)

    e_att, d_encoded = tie(e_att, d_encoded)
    enc_plan = ((0, 3 * width), (1, 0), (1, 4 * width))
    rows = frames + EXTRA
    encoded, e_n2, e_active, e_slope, e_mid, e_second = call(
        partial(encoder_forward_kernel, enc_plan),
        [shape((rows, width), bf16)] + forward_outs + kept_outs,
        "s" + "h" * (2 * PIECES) + "vvvv",
        [
            weights_scratch,
            pltpu.VMEM((rows, width), f32),
            pltpu.VMEM((rows, 4 * width), bf16),
            pltpu.SemaphoreType.DMA((3 * PIECES,)),
        ],
        (scalars, *enc_one, *enc_two, activation_halo, e_input, e_att, vectors),
        6,
    )
    encoded, b_sum = tie(encoded, b_sum)
    a_sum = next_sum(a_sum, ORDER_A[0], index)
    b_sum = sum_by_permutes(b_sum.reshape(high, -1, b_sum.shape[1]), index).astype(bf16)
    residuals, windows, reduced = call(
        latent_kernel,
        [
            shape((levels, codec, latent), bf16),
            shape((4, codec, width), bf16),
            shape((codec, width), bf16),
        ],
        "s" + "h" * PIECES + "vvv",
        [
            pltpu.VMEM((width, 4 * width + latent), bf16),
            pltpu.VMEM((width // 128, frames + EXTRA, 128), f32),
            pltpu.SemaphoreType.DMA((PIECES,)),
        ],
        (scalars, *enc_one, encoded, code_rows, vectors),
        3,
    )
    near_res = swap(residuals, "x")
    res_pieces = [residuals, near_res, swap(residuals, "core"), swap(near_res, "core")]

    d_encoded, a_sum, _ = tie(d_encoded, a_sum, residuals)
    a_sum = next_sum(a_sum, ORDER_A[1], index)
    (e_gmid, e_dh, e_dtwo, e_done, e_vg_two, e_dq, e_dk, e_dv, e_dkh, e_dvh) = call(
        partial(encoder_backward_kernel, enc_plan),
        backward_outs,
        "s" + "h" * (2 * PIECES) + "" + "v" * 9,
        [weights_scratch] + layer_scratch,
        (
            scalars, *enc_one, *enc_two, e_att, d_encoded, vectors, e_slope, e_mid, e_second,
            e_q, e_k, e_v,
        ),
        11,
    )
    e_dkh, e_dvh = shifted(e_dkh, -1), shifted(e_dvh, -1)
    c_outs = packed_outs(8 * width, width, shares)
    group_c = call(
        partial(encoder_gradients_kernel, shares),
        c_outs + packed_outs(5 * width + latent, width, shares),
        "s" + "v" * 10,
        [],
        (
            scalars, e_n2, e_active, e_dh, e_dtwo, e_att, e_done, windows, d_reduced, reduced,
            d_latent,
        ),
        6,
    )
    c_one = first_sum(group_c[: len(c_outs)], shares, ORDER_C_ONE, index, 0)
    c_two = first_sum(group_c[len(c_outs) :], shares, ORDER_C_TWO, index)

    if code_share % 16 == 0:
        tail_rows = levels * code_share
        csend, ckeep = call(
            partial(collect_kernel, code_share),
            [shape((dp_count // 2, tail_rows + 2 * levels, latent), bf16)] * 2,
            "s" + "v" * 9,
            [pltpu.VMEM((levels, dp_count * code_share), f32)],
            (scalars, *res_pieces, relative_frames, relative_codes, entry_t, dead_t, place_t),
            6,
        )
        e_dq, csend, c_one, c_two, a_sum = tie(e_dq, csend, c_one, c_two, a_sum)
    vector_grads = jnp.concatenate([e_vg_two, d_vg_two, m_vg, d_vg_one], 0)
    grad_outs = call(
        partial(encoder_back_kernel, shares),
        [shape((frames, width), bf16)] + packed_outs(3 * width + 128, width, shares),
        "s" + "h" * PIECES + "" + "v" * 12,
        [
            pltpu.VMEM((width, 3 * width), bf16),
            pltpu.VMEM((frames, 3 * width), bf16),
            pltpu.VMEM((8, width), f32),
            pltpu.VMEM((128, width), f32),
            pltpu.SemaphoreType.DMA((PIECES,)),
        ],
        (
            scalars, *enc_one, e_dq, e_dk, e_dv, e_dkh, e_dvh, e_input, e_gmid, vectors,
            cos_table, sin_table, e_n1, vector_grads,
        ),
        5,
    )
    activations_grad = grad_outs[0]

    grads_a = sum_by_permutes(a_sum.reshape(high, -1, a_sum.shape[1]), index)
    d_sum = first_sum(grad_outs[1:], shares, ORDER_D, index)
    c_two = next_sum(c_two, ORDER_C_TWO[0], index, d_sum)
    c_one = next_sum(c_one, ORDER_C_ONE[0], index, c_two)
    b_sum, _ = tie(b_sum, c_two)
    b_sum = next_sum(b_sum, ORDER_B[1], index)
    d_sum = next_sum(d_sum, ORDER_D[0], index, c_one)
    c_two = next_sum(c_two, ORDER_C_TWO[1], index, d_sum)
    if code_share % 16 == 0:
        combined = sum_over_hi(swap_add(csend, ckeep, "lo"))
        summed = combined[:tail_rows].reshape(levels, code_share, latent)
        digits = combined[tail_rows:, :code_share]
        counted = 128.0 * digits[:levels] + digits[levels:]
    else:
        flat_res = jnp.concatenate(res_pieces, 1)
        used = part_code[:, :, None] == relative_codes[:, None, :]
        placed = part_place[:, :, None] == relative_frames[None]
        counts = jnp.sum(used.astype(f32), 2).reshape(levels, dp_count, code_share)
        selects = jnp.where(part_dead[:, :, None] == 1, placed, used).astype(bf16)
        sums = jnp.einsum("lct,ltd->lcd", selects, flat_res, preferred_element_type=f32)
        sums = sums.astype(bf16).reshape(levels, dp_count, code_share, latent)
        summed = lax.psum_scatter(sums, DP, scatter_dimension=1, tiled=False).astype(f32)
        counted = lax.psum_scatter(counts, DP, scatter_dimension=1, tiled=False)
    c_one = next_sum(c_one, ORDER_C_ONE[1], index)
    d_sum = next_sum(d_sum, ORDER_D[1], index)
    grads_b = next_sum(b_sum, ORDER_B[2], index).astype(f32)
    edge, far_edge = c_one.shape[1], c_one.shape[1] + c_two.shape[1]
    together = last_sum(jnp.concatenate([c_one, c_two, d_sum], 1), high)
    grads_c, grads_c_two, grads_d = (
        together[:, :edge], together[:, edge:far_edge], together[:, far_edge:]
    )

    new_cluster_size = ema_decay * code_usage_average + (1.0 - ema_decay) * counted
    new_embed_sum = jnp.where(
        owner_flag[:, :, None],
        summed * new_cluster_size[:, :, None],
        ema_decay * code_latent_sum_average + (1.0 - ema_decay) * summed,
    )
    new_codebook = new_embed_sum / new_cluster_size[:, :, None]

    def columns(block, at, count):
        return block[:, at * width : (at + count) * width]

    def taps(block):
        return block.reshape(-1, 4, width).transpose(1, 0, 2)

    def unfold(block):
        return block.reshape(-1, 4, width).transpose(1, 0, 2).reshape(-1, width)

    vec = grads_d[:, 3 * width : 3 * width + 16].T
    return (
        output[None],
        activations_grad[None],
        vec[0],
        vec[1],
        columns(grads_d, 0, 3),
        columns(grads_c_two, 4, 1),
        vec[2],
        vec[3],
        vec[4],
        columns(grads_c, 4, 4),
        unfold(columns(grads_c, 0, 4)),
        vec[5],
        taps(columns(grads_c_two, 0, 4)),
        vec[6],
        grads_c_two[:, 5 * width :],
        grads_b[:, 7 * width :].T,
        taps(columns(grads_b, 3, 4)),
        vec[7],
        vec[8],
        vec[9],
        columns(grads_b, 0, 3),
        columns(grads_a, 8, 1),
        vec[10],
        vec[11],
        vec[12],
        columns(grads_a, 4, 4),
        unfold(columns(grads_a, 0, 4)),
        vec[13],
        new_cluster_size,
        new_embed_sum,
        new_codebook,
    )


def solution(mesh):
    grid = mesh.devices
    mesh = jax.sharding.Mesh(
        grid.reshape(grid.shape[0] // 2, 2, grid.shape[1] // 2, 2), ("hi", "lo", "x", "core")
    )
    placed = (
        P(DP, SEQ, None),
        P(SEQ),
        P(SEQ),
        P(SEQ, None),
        P(SEQ, None),
        P(SEQ),
        P(SEQ),
        P(SEQ),
        P(SEQ, None),
        P(SEQ, None),
        P(SEQ),
        P(None, SEQ, None),
        P(SEQ),
        P(SEQ, None),
        P(None, SEQ, None),
        P(None, SEQ),
        P(None, SEQ, None),
        P(SEQ),
        P(SEQ),
        P(SEQ),
        P(SEQ, None),
        P(SEQ, None),
        P(SEQ),
        P(SEQ),
        P(SEQ),
        P(SEQ, None),
        P(SEQ, None),
        P(SEQ),
        P(DP, SEQ, None),
        P(DP, None),
        P(DP, SEQ, None),
        P(),
        P(),
        P(None, DP + SEQ),
        P(None, DP + SEQ, None),
    )
    return jax.shard_map(
        local,
        mesh=mesh,
        in_specs=placed,
        out_specs=(
            P(DP, SEQ, None),
            P(DP, SEQ, None),
            P(DP + SEQ),
            P(DP + SEQ),
            P(DP + SEQ, None),
            P(DP + SEQ, None),
            P(DP + SEQ),
            P(DP + SEQ),
            P(DP + SEQ),
            P(DP + SEQ, None),
            P(DP + SEQ, None),
            P(DP + SEQ),
            P(None, DP + SEQ, None),
            P(DP + SEQ),
            P(DP + SEQ, None),
            P(None, DP + SEQ),
            P(None, DP + SEQ, None),
            P(DP + SEQ),
            P(DP + SEQ),
            P(DP + SEQ),
            P(DP + SEQ, None),
            P(DP + SEQ, None),
            P(DP + SEQ),
            P(DP + SEQ),
            P(DP + SEQ),
            P(DP + SEQ, None),
            P(DP + SEQ, None),
            P(DP + SEQ),
            P(None, DP + SEQ),
            P(None, DP + SEQ, None),
            P(None, DP + SEQ, None),
        ),
        check_vma=False,
    )
```

```python
from functools import partial

import jax
import jax.numpy as jnp
from jax import lax
from jax.experimental import pallas as pl
from jax.experimental.pallas import tpu as pltpu
from jax.sharding import PartitionSpec as P

HEADS = 8
HEAD_DIM = 64
CONTEXT = 250
HALO = 256
CODE_HALO = HALO // 2 + 16
EXTRA = 16
QUERIES = 64
GROUP = 4
WINDOW = HALO + QUERIES
VMEM_LIMIT = 26 * 1024 * 1024
ORDER_A = ("lo", "x", "hi")
ORDER_B = ("hi", "lo", "x")
ORDER_C_ONE = ("x", "lo", "hi")
ORDER_C_TWO = ("x", "lo", "hi")
ORDER_D = ("x", "lo", "hi")
DP = ("hi", "lo")
SEQ = ("x", "core")

norm_eps = 1e-05
ema_decay = 0.9
bf16 = jnp.bfloat16
f32 = jnp.float32


PIECES = 6


def fetch(sc_ref, pieces, at, width, dst, sems, first=0):
    copies = []
    for i, piece in enumerate(pieces):
        rows = piece.shape[0]
        row = pl.multiple_of(sc_ref[8 + i], 64)
        copies.append(
            pltpu.make_async_copy(
                piece.at[:, at : at + width], dst.at[pl.ds(row, rows), :], sems.at[first + i]
            )
        )
        copies[-1].start()
    return copies


def split_refs(refs, counts):
    groups = []
    for count in counts:
        groups.append(refs[:count])
        refs = refs[count:]
    return groups, refs


def wait_all(copies):
    for copy in copies:
        copy.wait()


def mm(a, b):
    return jnp.dot(a, b, preferred_element_type=f32)


def mm_nt(a, b):
    return lax.dot_general(a, b, (((1,), (1,)), ((), ())), preferred_element_type=f32)


def mm_tn(a, b):
    return lax.dot_general(a, b, (((0,), (0,)), ((), ())), preferred_element_type=f32)


def normalize(stream):
    center = stream - jnp.mean(stream, -1, keepdims=True)
    scaled = lax.rsqrt(jnp.mean(center * center, -1, keepdims=True) + norm_eps)
    return center * scaled, scaled


def norm_backward(upstream, normal, scaled, gain):
    inner = upstream * gain
    return scaled * (
        inner
        - jnp.mean(inner, -1, keepdims=True)
        - normal * jnp.mean(inner * normal, -1, keepdims=True)
    )


def column_sum(value):
    return jnp.sum(value, 0, keepdims=True)


def interleave(even, odd, scr):
    tiles, rows, _ = scr.shape
    for tile in range(tiles):
        cols = slice(tile * 128, (tile + 1) * 128)
        scr[tile, pl.ds(0, rows // 2, stride=2), :] = even[:, cols]
        scr[tile, pl.ds(1, rows // 2, stride=2), :] = odd[:, cols]
    return jnp.concatenate([scr[tile] for tile in range(tiles)], 1)


def split_rows(value, scr):
    tiles, rows, _ = scr.shape
    for tile in range(tiles):
        scr[tile] = value[:, tile * 128 : (tile + 1) * 128]
    even = [scr[tile, pl.ds(0, rows // 2, stride=2), :] for tile in range(tiles)]
    odd = [scr[tile, pl.ds(1, rows // 2, stride=2), :] for tile in range(tiles)]
    return jnp.concatenate(even, 1), jnp.concatenate(odd, 1)


def first_half():
    lane = lax.broadcasted_iota(jnp.int32, (1, 128), 1)
    return lane % HEAD_DIM < HEAD_DIM // 2


def rotate(tile, cos, sin):
    swapped = jnp.where(first_half(), pltpu.roll(tile, 96, 1), pltpu.roll(tile, 32, 1))
    return tile * cos + swapped * sin


def head_lanes():
    lane = lax.broadcasted_iota(jnp.int32, (1, GROUP * HEAD_DIM), 1) // HEAD_DIM
    return [(lane == head) for head in range(GROUP)]


def stack_heads(block, lanes):
    return jnp.concatenate([block * mask.astype(bf16) for mask in lanes], 0)


def unstack_heads(block, lanes):
    rows = block.shape[0] // GROUP
    out = block[:rows]
    for head in range(1, GROUP):
        out = jnp.where(lanes[head], block[head * rows : (head + 1) * rows], out)
    return out


def lowest_key(query, cut):
    low = jnp.maximum(query - (CONTEXT - 1), 0)
    return jnp.where(query >= cut, jnp.maximum(low, cut), low)


def attend(q_ref, k_ref, v_ref, att_ref, sc_ref, rows, first_query, first_key, keys, at_row):
    start, cut = sc_ref[0], sc_ref[1]
    query = start + first_query + lax.broadcasted_iota(jnp.int32, (rows, 1), 0)
    low = lowest_key(query, cut)
    key = start + first_key + lax.broadcasted_iota(jnp.int32, (rows, keys), 1)
    mask = (key <= query) & (key >= low)
    mask = jnp.concatenate([mask] * GROUP, 0)
    lanes = head_lanes()
    key_row = first_key + HALO
    for group in range(HEADS // GROUP):
        cols = slice(group * GROUP * HEAD_DIM, (group + 1) * GROUP * HEAD_DIM)
        stacked = stack_heads(q_ref[at_row : at_row + rows, cols], lanes)
        scores = mm_nt(stacked, k_ref[key_row : key_row + keys, cols]) * HEAD_DIM ** (-0.5)
        scores = jnp.where(mask, scores, -1e30)
        exponent = jnp.exp(scores - jnp.max(scores, -1, keepdims=True))
        weights = exponent * (1.0 / jnp.sum(exponent, -1, keepdims=True))
        mixed = mm(weights.astype(bf16), v_ref[key_row : key_row + keys, cols])
        att_ref[at_row : at_row + rows, cols] = unstack_heads(mixed, lanes).astype(bf16)


def front(x, vec_ref, base, w_in, cos_ref, sin_ref, sc_ref, n1_ref, q_ref, k_ref, v_ref, att_ref,
          extra):
    width = x.shape[1]
    normal, _ = normalize(x)
    low = (normal * vec_ref[base : base + 1] + vec_ref[base + 1 : base + 2]).astype(bf16)
    n1_ref[...] = low[HALO:]
    skip = HALO - extra
    queries = mm(low[skip:], w_in[:, :width])
    keys = mm(low, w_in[:, width : 2 * width])
    for at in range(0, width, 128):
        q_ref[:, at : at + 128] = rotate(
            queries[:, at : at + 128], cos_ref[skip:], sin_ref[skip:]
        ).astype(bf16)
        k_ref[:, at : at + 128] = rotate(keys[:, at : at + 128], cos_ref[...], sin_ref[...]).astype(
            bf16
        )
    v_ref[...] = mm(low, w_in[:, 2 * width :]).astype(bf16)
    frames = x.shape[0] - HALO
    if extra:
        attend(q_ref, k_ref, v_ref, att_ref, sc_ref, extra, -extra, -HALO, HALO, 0)
    for first in range(0, frames, QUERIES):
        attend(
            q_ref, k_ref, v_ref, att_ref, sc_ref, QUERIES, first, first - HALO, WINDOW,
            extra + first,
        )


def decoder_front_kernel(sc_ref, *refs):
    pieces, refs = refs[:PIECES], refs[PIECES:]
    (qz_ref, vec_ref, cos_ref, sin_ref, x_ref, restored_ref, n1_ref, q_ref, k_ref, v_ref, att_ref,
     w_vmem, x_scr, sems) = refs
    width = x_ref.shape[1]
    wait_all(fetch(sc_ref, pieces, 0, w_vmem.shape[1], w_vmem, sems))
    latent = qz_ref.shape[1]
    restored = mm_nt(qz_ref[...], w_vmem[:, :latent]).astype(bf16)
    restored_ref[...] = restored[CODE_HALO - 16 :]
    both = mm(restored, w_vmem[:, latent : latent + 4 * width])
    bias = vec_ref[7:8]
    now = both[16:, : 2 * width]
    before = pltpu.roll(both[:, 2 * width :], 1, 0)[16:]
    total = now + before
    x = interleave(total[:, :width] + bias, total[:, width:] + bias, x_scr)
    x_ref[...] = x[HALO:]
    w_in = w_vmem.at[:, latent + 4 * width :]
    front(x, vec_ref, 8, w_in, cos_ref, sin_ref, sc_ref, n1_ref, q_ref, k_ref, v_ref,
          att_ref, 0)


def encoder_front_kernel(sc_ref, *refs):
    (pieces,), refs = split_refs(refs, (PIECES,))
    (halo_ref, x_ref, vec_ref, cos_ref, sin_ref, n1_ref, q_ref, k_ref, v_ref, att_ref,
     w_vmem, sems) = refs
    width = x_ref.shape[1]
    copies = fetch(sc_ref, pieces, 0, 3 * width, w_vmem, sems)
    x = jnp.concatenate([halo_ref[...], x_ref[...]], 0).astype(f32)
    wait_all(copies)
    front(x, vec_ref, 0, w_vmem, cos_ref, sin_ref, sc_ref, n1_ref, q_ref, k_ref, v_ref, att_ref,
          EXTRA)


def gelu_both(hidden):
    share = 0.5 * (1.0 + lax.erf(hidden * 0.7071067811865476))
    density = jnp.exp(-0.5 * hidden * hidden) * 0.3989422804014327
    return hidden * share, share + hidden * density


def l2_rows(w, at, chunk, width):
    rows = width // 4
    return jnp.concatenate(
        [
            w[chunk * rows : (chunk + 1) * rows, at + g * width : at + (g + 1) * width]
            for g in range(4)
        ],
        0,
    )


def fetch_layer(sc_ref, groups, plan, width, w_vmem, sems):
    edges = (0, width, 5 * width, 9 * width)
    return [
        fetch(
            sc_ref, groups[plan[i][0]], plan[i][1], high - low, w_vmem.at[:, low:high], sems,
            PIECES * i,
        )
        for i, (low, high) in enumerate(zip(edges[:-1], edges[1:]))
    ]


def ff_forward(base, extra, copies, w_vmem, att_ref, stream, vec_ref, out_ref, n2_ref, active_ref,
               slope_ref, mid_ref, second_ref, h_scr, act_scr):
    rows, width = stream.shape
    scale_one = vec_ref[base + 2 : base + 3]
    gain_two = vec_ref[base + 3 : base + 4]
    bias_two = vec_ref[base + 4 : base + 5]
    scale_two = vec_ref[base + 5 : base + 6]
    wait_all(copies[0])
    middle = stream + scale_one * mm(att_ref[...], w_vmem[:, :width])
    mid_ref[...] = middle[extra:]
    normal, _ = normalize(middle)
    n2 = (normal * gain_two + bias_two).astype(bf16)
    n2_ref[...] = n2[extra:]
    wait_all(copies[1])
    l1_at, l2_at = width, 5 * width
    second = None
    for chunk in range(4):
        cols = slice(chunk * width, (chunk + 1) * width)
        h_scr[...] = mm(n2, w_vmem[:, l1_at + chunk * width : l1_at + (chunk + 1) * width])
        if extra:
            act, _ = gelu_both(h_scr[:extra, :])
            act_scr[:extra, cols] = act.astype(bf16)

        def body(i, _):
            at_row = pl.multiple_of(i * 16, 16)
            act, slope = gelu_both(h_scr[pl.ds(at_row + extra, 16), :])
            act_scr[pl.ds(at_row + extra, 16), cols] = act.astype(bf16)
            slope_ref[pl.ds(at_row, 16), cols] = slope
            return 0

        lax.fori_loop(0, (rows - extra) // 16, body, 0)
        if chunk == 0:
            wait_all(copies[2])
        part = mm(act_scr[:, cols], l2_rows(w_vmem, l2_at, chunk, width))
        second = part if second is None else second + part
    active_ref[...] = act_scr[extra:, :]
    second_ref[...] = second[extra:]
    out_ref[...] = (middle + scale_two * second).astype(bf16)


def ff_backward(base, extra, w_vmem, att_ref, g, vec_ref, slope_ref, mid_ref, second_ref, gmid_ref,
                dh_ref, dtwo_ref, done_ref, vg_ref, datt_scr):
    width = g.shape[1]
    scale_one = vec_ref[base + 2 : base + 3]
    gain_two = vec_ref[base + 3 : base + 4]
    scale_two = vec_ref[base + 5 : base + 6]
    l1_at, l2_at = width, 5 * width
    vg_ref[3:4, :] = column_sum(g * second_ref[...])
    d_two = (g * scale_two).astype(bf16)
    dtwo_ref[...] = d_two
    e = None
    for chunk in range(4):
        cols = slice(chunk * width, (chunk + 1) * width)
        d_active = mm_nt(d_two, l2_rows(w_vmem, l2_at, chunk, width))
        dh_ref[:, cols] = (d_active * slope_ref[:, cols]).astype(bf16)
        part = mm_nt(
            dh_ref[:, cols], w_vmem[:, l1_at + chunk * width : l1_at + (chunk + 1) * width]
        )
        e = part if e is None else e + part
    normal, scaled = normalize(mid_ref[...])
    vg_ref[1:2, :] = column_sum(e * normal)
    vg_ref[2:3, :] = column_sum(e)
    g_mid = g + norm_backward(e, normal, scaled, gain_two)
    gmid_ref[...] = g_mid
    vg_ref[0:1, :] = column_sum(g_mid * mm(att_ref[extra:, :], w_vmem[:, :width]))
    d_one = (g_mid * scale_one).astype(bf16)
    done_ref[...] = d_one
    datt_scr[...] = mm_nt(d_one, w_vmem[:, :width]).astype(bf16)


def decoder_layer_kernel(plan, sc_ref, *refs):
    (pieces,), refs = split_refs(refs, (PIECES,))
    (att_ref, x_ref, g_ref, vec_ref, q_ref, k_ref, v_ref,
     out_ref, n2_ref, active_ref, gmid_ref, dh_ref, dtwo_ref, done_ref, vg_ref,
     dq_ref, dk_ref, dv_ref, dkv_ref,
     w_vmem, h_scr, act_scr, slope_scr, mid_scr, second_scr, datt_scr, dk_scr, dv_scr, sems) = refs
    width = x_ref.shape[1]
    copies = fetch_layer(sc_ref, (pieces,), plan, width, w_vmem, sems)
    ff_forward(8, 0, copies, w_vmem, att_ref, x_ref[...], vec_ref, out_ref, n2_ref, active_ref,
               slope_scr, mid_scr, second_scr, h_scr, act_scr)
    ff_backward(8, 0, w_vmem, att_ref, g_ref[...].astype(f32), vec_ref, slope_scr, mid_scr,
                second_scr, gmid_ref, dh_ref, dtwo_ref, done_ref, vg_ref, datt_scr)
    attention_backward(0, sc_ref, q_ref, k_ref, v_ref, datt_scr, dq_ref, dk_ref, dv_ref, dkv_ref,
                       dk_scr, dv_scr)


def encoder_forward_kernel(plan, sc_ref, *refs):
    groups, refs = split_refs(refs, (PIECES,))
    (halo_ref, x_ref, att_ref, vec_ref,
     out_ref, n2_ref, active_ref, slope_ref, mid_ref, second_ref,
     w_vmem, h_scr, act_scr, sems) = refs
    width = x_ref.shape[1]
    copies = fetch_layer(sc_ref, groups, plan, width, w_vmem, sems)
    stream = jnp.concatenate([halo_ref[HALO - EXTRA :, :], x_ref[...]], 0).astype(f32)
    ff_forward(0, EXTRA, copies, w_vmem, att_ref, stream, vec_ref, out_ref, n2_ref, active_ref,
               slope_ref, mid_ref, second_ref, h_scr, act_scr)


def encoder_backward_kernel(plan, sc_ref, *refs):
    groups, refs = split_refs(refs, (PIECES,))
    (att_ref, g_ref, vec_ref, slope_ref, mid_ref, second_ref, q_ref, k_ref, v_ref,
     gmid_ref, dh_ref, dtwo_ref, done_ref, vg_ref, dq_ref, dk_ref, dv_ref, dkv_ref,
     w_vmem, datt_scr, dk_scr, dv_scr, sems) = refs
    width = g_ref.shape[1]
    for copies in fetch_layer(sc_ref, groups, plan, width, w_vmem, sems):
        wait_all(copies)
    ff_backward(0, EXTRA, w_vmem, att_ref, g_ref[...], vec_ref, slope_ref, mid_ref, second_ref,
                gmid_ref, dh_ref, dtwo_ref, done_ref, vg_ref, datt_scr)
    attention_backward(EXTRA, sc_ref, q_ref, k_ref, v_ref, datt_scr, dq_ref, dk_ref, dv_ref,
                       dkv_ref, dk_scr, dv_scr)


def attention_backward(extra, sc_ref, q_ref, k_ref, v_ref, do_ref,
                       dq_ref, dk_ref, dv_ref, dkv_ref, dk_scr, dv_scr):
    start, cut = sc_ref[0], sc_ref[1]
    frames = do_ref.shape[0]
    lanes = head_lanes()
    scale = HEAD_DIM ** (-0.5)
    dk_scr[...] = jnp.zeros_like(dk_scr)
    dv_scr[...] = jnp.zeros_like(dv_scr)
    wide = GROUP * QUERIES
    for first in range(0, frames, QUERIES):
        lane = lax.broadcasted_iota(jnp.int32, (1, wide), 1) % QUERIES
        query = start + first + lane
        low = lowest_key(query, cut)
        key = start + first - HALO + lax.broadcasted_iota(jnp.int32, (WINDOW, wide), 0)
        mask = (key <= query) & (key >= low)
        for group in range(HEADS // GROUP):
            cols = slice(group * GROUP * HEAD_DIM, (group + 1) * GROUP * HEAD_DIM)
            qs = stack_heads(q_ref[extra + first : extra + first + QUERIES, cols], lanes)
            ds = stack_heads(do_ref[first : first + QUERIES, cols], lanes)
            kw = k_ref[first : first + WINDOW, cols]
            vw = v_ref[first : first + WINDOW, cols]
            scores = jnp.where(mask, mm_nt(kw, qs) * scale, -1e30)
            exponent = jnp.exp(scores - jnp.max(scores, 0, keepdims=True))
            probs = exponent * (1.0 / jnp.sum(exponent, 0, keepdims=True))
            d_probs = mm_nt(vw, ds)
            mean = jnp.sum(probs * d_probs, 0, keepdims=True)
            d_scores = (probs * (d_probs - mean)).astype(bf16)
            dk_scr[first : first + WINDOW, cols] += mm(d_scores, qs)
            dv_scr[first : first + WINDOW, cols] += mm(probs.astype(bf16), ds)
            dq_ref[first : first + QUERIES, cols] = (
                unstack_heads(mm_tn(d_scores, kw), lanes) * scale
            )
    width = dq_ref.shape[1]
    dkv_ref[:, :width] = (dk_scr[:HALO] * scale).astype(bf16)
    dkv_ref[:, width:] = dv_scr[:HALO].astype(bf16)
    dk_ref[...] = dk_scr[HALO:] * scale
    dv_ref[...] = dv_scr[HALO:]


class Packer:
    def __init__(self, core, refs, shares, order):
        self.core, self.refs, self.shares, self.order = core, refs, shares, order

    def put(self, value, at, step=1, phase=0, block0=0):
        if len(self.refs) == 1:
            if step == 1:
                self.refs[0][:, at : at + value.shape[1]] = value.astype(bf16)
            return
        send, keep = self.refs
        cols = slice(at, at + value.shape[1])
        rows = 16
        hi = self.shares // 8
        blocks = value.shape[0] // (rows * step)
        for pair in range(blocks // 2):
            even = value[(2 * pair * step + phase) * rows :][:rows]
            odd = value[((2 * pair + 1) * step + phase) * rows :][:rows]
            block = (block0 + 2 * pair) // 2
            place = {"x": (block % 2, 2), "lo": (block // 2 % 2, 2), "hi": (block // 4, hi)}
            at_row = 0
            for axis in self.order:
                at_row = at_row * place[axis][1] + place[axis][0]
            at_row = at_row * rows
            first = self.core == 0
            keep[at_row : at_row + rows, cols] = jnp.where(first, even, odd).astype(bf16)
            send[at_row : at_row + rows, cols] = jnp.where(first, odd, even).astype(bf16)

    def put_l2(self, value, at, chunk, width):
        if len(self.refs) == 1:
            cols = slice(at + chunk * width, at + (chunk + 1) * width)
            self.refs[0][:, cols] = value.astype(bf16)
            return
        for phase in range(4):
            self.put(value, at + phase * width, 4, phase, chunk * width // 64)


def linear_gradients(pack, n2_ref, active_ref, dh_ref, dtwo_ref):
    width = n2_ref.shape[1]
    for chunk in range(4):
        cols = slice(chunk * width, (chunk + 1) * width)
        pack.put_l2(mm_tn(active_ref[:, cols], dtwo_ref[...]), 0, chunk, width)
        pack.put(mm_tn(n2_ref[...], dh_ref[:, cols]), (4 + chunk) * width)


def decoder_gradients_kernel(shares, sc_ref, n2_ref, active_ref, dh_ref, dtwo_ref, att_ref, done_ref,
                             *refs):
    pack = Packer(sc_ref[2], refs, shares, ORDER_A)
    linear_gradients(pack, n2_ref, active_ref, dh_ref, dtwo_ref)
    pack.put(mm_tn(att_ref[...], done_ref[...]), 8 * n2_ref.shape[1])


def encoder_gradients_kernel(shares, sc_ref, n2_ref, active_ref, dh_ref, dtwo_ref, att_ref, done_ref,
                             win_ref, dred_ref, red_ref, dlat_ref, *refs):
    width = n2_ref.shape[1]
    half = len(refs) // 2
    linear_gradients(
        Packer(sc_ref[2], refs[:half], shares, ORDER_C_ONE), n2_ref, active_ref, dh_ref, dtwo_ref
    )
    pack = Packer(sc_ref[2], refs[half:], shares, ORDER_C_TWO)
    d_reduced = dred_ref[...]
    for tap in range(4):
        pack.put(mm_tn(win_ref[tap], d_reduced), tap * width)
    pack.put(mm_tn(att_ref[EXTRA:, :], done_ref[...]), 4 * width)
    pack.put(mm_tn(red_ref[...], dlat_ref[...]), 5 * width)


def layer_input_gradient(base, dq_ref, dk_ref, dv_ref, dkv_ref, x, gmid_ref,
                         w_in, vec_ref, cos_ref, sin_ref, dmix_ref, vg_ref):
    frames, width = dq_ref.shape
    later = frames - HALO
    cos, sin = cos_ref[HALO:], -sin_ref[HALO:]
    for at in range(0, width, 128):
        cols = slice(at, at + 128)
        dmix_ref[:, cols] = rotate(dq_ref[:, cols], cos, sin).astype(bf16)
        keys = dk_ref[:, cols]
        keys = jnp.concatenate([keys[:later], keys[later:] + dkv_ref[:, cols].astype(f32)], 0)
        dmix_ref[:, width + at : width + at + 128] = rotate(keys, cos, sin).astype(bf16)
        values = dv_ref[:, cols]
        moved = dkv_ref[:, width + at : width + at + 128].astype(f32)
        values = jnp.concatenate([values[:later], values[later:] + moved], 0)
        dmix_ref[:, 2 * width + at : 2 * width + at + 128] = values.astype(bf16)
    d_normed = mm_nt(dmix_ref[...], w_in[...])
    normal, scaled = normalize(x)
    vg_ref[0:1, :] = column_sum(d_normed * normal)
    vg_ref[1:2, :] = column_sum(d_normed)
    return gmid_ref[...] + norm_backward(d_normed, normal, scaled, vec_ref[base : base + 1])


def decoder_back_kernel(at, sc_ref, *refs):
    pieces, refs = refs[:PIECES], refs[PIECES:]
    (dq_ref, dk_ref, dv_ref, dkv_ref, x_ref, gmid_ref, vec_ref, cos_ref, sin_ref,
     dup_ref, dmix_ref, vg_ref, w_vmem, sems) = refs
    wait_all(fetch(sc_ref, pieces, at, w_vmem.shape[1], w_vmem, sems))
    grad = layer_input_gradient(
        8, dq_ref, dk_ref, dv_ref, dkv_ref, x_ref[...], gmid_ref, w_vmem, vec_ref,
        cos_ref, sin_ref, dmix_ref, vg_ref,
    )
    vg_ref[2:3, :] = column_sum(grad)
    dup_ref[...] = grad.astype(bf16)


def encoder_back_kernel(shares, sc_ref, *refs):
    (pieces,), refs = split_refs(refs, (PIECES,))
    (dq_ref, dk_ref, dv_ref, dkv_ref, x_ref, gmid_ref, vec_ref, cos_ref, sin_ref, n1_ref,
     vgs_ref, grad_ref, *rest) = refs
    refs, (w_vmem, dmix_scr, vg_scr, all_scr, sems) = rest[:-5], rest[-5:]
    width = x_ref.shape[1]
    wait_all(fetch(sc_ref, pieces, 0, w_vmem.shape[1], w_vmem, sems))
    grad = layer_input_gradient(
        0, dq_ref, dk_ref, dv_ref, dkv_ref, x_ref[...].astype(f32), gmid_ref, w_vmem,
        vec_ref, cos_ref, sin_ref, dmix_scr, vg_scr,
    )
    grad_ref[...] = grad.astype(bf16)
    pack = Packer(sc_ref[2], refs, shares, ORDER_D)
    for part in range(3):
        cols = slice(part * width, (part + 1) * width)
        pack.put(mm_tn(n1_ref[...], dmix_scr[:, cols]), part * width)
    all_scr[...] = jnp.zeros_like(all_scr)
    all_scr[0:2, :] = vg_scr[0:2, :]
    all_scr[2:6, :] = vgs_ref[0:4, :]
    all_scr[6:7, :] = vgs_ref[16:17, :]
    all_scr[7:8, :] = vgs_ref[26:27, :]
    all_scr[8:10, :] = vgs_ref[24:26, :]
    all_scr[10:14, :] = vgs_ref[8:12, :]
    pack.put(all_scr[...].T, 3 * width)


def middle_kernel(shares, sc_ref, *refs):
    (pieces, more), refs = split_refs(refs, (PIECES, PIECES))
    (dup_ref, next_ref, dmix_ref, n1_ref, restored_ref, qz_ref,
     denc_ref, dred_ref, dlat_ref, vg_ref, *rest) = refs
    refs, (up_vmem, down_vmem, frame_scr, sems) = rest[:-4], rest[-4:]
    frames, width = dup_ref.shape
    latent = qz_ref.shape[1]
    codec = frames // 2
    copies = [
        fetch(sc_ref, pieces, 0, latent + 4 * width, up_vmem, sems),
        fetch(sc_ref, more, 4 * width, 4 * width + latent, down_vmem, sems, PIECES),
    ]
    pairs = codec + 16
    even, odd = split_rows(
        jnp.concatenate([dup_ref[...], next_ref[...]], 0).astype(f32), frame_scr
    )
    both = jnp.concatenate([even, odd], 1).astype(bf16)
    wait_all(copies[0])
    up = up_vmem[:, latent : latent + 4 * width]
    here = mm_nt(both, up[:, : 2 * width])
    later = mm_nt(both, up[:, 2 * width :])
    d_restored = (here + pltpu.roll(later, pairs - 1, 0)).astype(bf16)
    d_latent = mm(d_restored, up_vmem[:, :latent]).astype(bf16)
    wait_all(copies[1])
    d_reduced = mm_nt(d_latent, down_vmem[:, 4 * width :]).astype(bf16)
    dlat_ref[...] = d_latent[:codec]
    dred_ref[...] = d_reduced[:codec]
    vg_ref[0:1, :] = column_sum(d_reduced[:codec].astype(f32))
    taps = [mm_nt(d_reduced, down_vmem[:, tap * width : (tap + 1) * width]) for tap in range(4)]
    denc_ref[...] = interleave(
        taps[2] + pltpu.roll(taps[0], pairs - 1, 0),
        taps[3] + pltpu.roll(taps[1], pairs - 1, 0),
        frame_scr,
    )[:frames]

    pack = Packer(sc_ref[2], refs, shares, ORDER_B)
    for part in range(3):
        cols = slice(part * width, (part + 1) * width)
        pack.put(mm_tn(n1_ref[...], dmix_ref[:, cols]), part * width)
    restored = restored_ref[...]
    own_pairs = both[:codec]
    before = pltpu.roll(restored.astype(f32), 1, 0)[16:].astype(bf16)
    pack.put(mm_tn(restored[16:], own_pairs[:, :width]), 3 * width)
    pack.put(mm_tn(restored[16:], own_pairs[:, width:]), 4 * width)
    pack.put(mm_tn(before, own_pairs[:, :width]), 5 * width)
    pack.put(mm_tn(before, own_pairs[:, width:]), 6 * width)
    pack.put(mm_tn(d_restored[:codec], qz_ref[CODE_HALO:, :]), 7 * width)


def latent_kernel(sc_ref, *refs):
    (pieces,), refs = split_refs(refs, (PIECES,))
    (enc_ref, rows_ref, vec_ref, res_ref, win_ref, red_ref, w_vmem, frame_scr, sems) = refs
    total, width = enc_ref.shape
    copies = fetch(sc_ref, pieces, 4 * width, w_vmem.shape[1], w_vmem, sems)
    inside = (sc_ref[0] > 0).astype(f32)
    rim = enc_ref[:EXTRA].astype(f32) * inside
    skip = EXTRA // 2
    even, odd = split_rows(jnp.concatenate([rim, enc_ref[EXTRA:].astype(f32)], 0), frame_scr)
    win_ref[0] = pltpu.roll(even, 1, 0)[skip:].astype(bf16)
    win_ref[1] = pltpu.roll(odd, 1, 0)[skip:].astype(bf16)
    win_ref[2] = even[skip:].astype(bf16)
    win_ref[3] = odd[skip:].astype(bf16)
    wait_all(copies)
    reduced = vec_ref[6:7]
    for tap in range(4):
        reduced = reduced + mm(win_ref[tap], w_vmem[:, tap * width : (tap + 1) * width])
    reduced = reduced.astype(bf16)
    red_ref[...] = reduced
    remaining = mm(reduced, w_vmem[:, 4 * width :])
    for level in range(rows_ref.shape[0]):
        res_ref[level] = remaining.astype(bf16)
        remaining = remaining - rows_ref[level].astype(f32)


def lookup_kernel(sc_ref, codes_ref, book_ref, qsend_ref, qkeep_ref, rsend_ref, rkeep_ref, q_scr):
    levels, share, latent = book_ref.shape
    total = codes_ref.shape[0]
    codec = total // 4
    base = sc_ref[3]
    core = sc_ref[2]
    entry = lax.broadcasted_iota(jnp.int32, (1, share), 1)
    for level in range(levels):
        picks = (codes_ref[:, level : level + 1] - base == entry).astype(f32).astype(bf16)
        found = mm(picks, book_ref[level])
        q_scr[CODE_HALO:] = found if level == 0 else q_scr[CODE_HALO:] + found
        for x in range(2):
            even = found[(2 * x) * codec :][:codec]
            odd = found[(2 * x + 1) * codec :][:codec]
            rkeep_ref[x, level] = jnp.where(core == 0, even, odd).astype(bf16)
            rsend_ref[x, level] = jnp.where(core == 0, odd, even).astype(bf16)
    q_scr[:CODE_HALO] = jnp.zeros((CODE_HALO, latent), f32)
    for x in range(2):
        even = q_scr[(2 * x) * codec : (2 * x + 1) * codec + CODE_HALO]
        odd = q_scr[(2 * x + 1) * codec : (2 * x + 2) * codec + CODE_HALO]
        qkeep_ref[x] = jnp.where(core == 0, even, odd)
        qsend_ref[x] = jnp.where(core == 0, odd, even)


def collect_kernel(share, seq_count, sc_ref, own_ref, x_ref, core_ref, far_ref, codes_ref,
                   marked_ref, send_ref, keep_ref, row_scr, cnt_scr):
    levels, codec, latent = own_ref.shape
    total = codes_ref.shape[1]
    lo = sc_ref[4]
    high = send_ref.shape[0]
    frame = lax.broadcasted_iota(jnp.int32, (1, total), 1) + sc_ref[6]
    row = lax.broadcasted_iota(jnp.int32, (2 * high * share, 1), 0)
    entry = (row // share * seq_count + sc_ref[5]) * share + row % share
    ones = jnp.ones((16, total), bf16)
    for level in range(levels):
        marked = marked_ref[:, level : level + 1]
        used = (entry == codes_ref[level : level + 1, :]).astype(f32)
        placed = (marked // 2 == frame).astype(f32)
        select = jnp.where(marked % 2 == 1, placed, used).astype(bf16)
        for place, ref in enumerate((own_ref, x_ref, core_ref, far_ref)):
            at_row = pl.multiple_of(sc_ref[14 + place], 32)
            row_scr[pl.ds(at_row, codec), :] = ref[level]
        sums = mm(select, row_scr[...])
        cnt_scr[level : level + 1, :] = mm_nt(ones, used.astype(bf16))[0:1]
        at = slice(level * share, (level + 1) * share)
        for h in range(high):
            even = sums[(2 * h) * share :][:share]
            odd = sums[(2 * h + 1) * share :][:share]
            keep_ref[h, at, :] = jnp.where(lo == 0, even, odd).astype(bf16)
            send_ref[h, at, :] = jnp.where(lo == 0, odd, even).astype(bf16)
    counts = cnt_scr[...]
    upper = jnp.floor(counts * (1.0 / 128.0))
    digits = jnp.concatenate([upper, counts - 128.0 * upper], 0)
    tail = slice(levels * share, levels * share + 2 * levels)
    for h in range(high):
        even = digits[:, (2 * h) * share : (2 * h + 1) * share]
        odd = digits[:, (2 * h + 1) * share : (2 * h + 2) * share]
        keep_ref[h, tail, :] = jnp.zeros((2 * levels, latent), bf16)
        send_ref[h, tail, :] = jnp.zeros((2 * levels, latent), bf16)
        keep_ref[h, tail, :share] = jnp.where(lo == 0, even, odd).astype(bf16)
        send_ref[h, tail, :share] = jnp.where(lo == 0, odd, even).astype(bf16)


def call(kernel, outs, spaces, scratch, args, micros):
    where = {"s": pltpu.SMEM, "v": pltpu.VMEM, "h": pltpu.HBM}
    title = getattr(kernel, "func", kernel).__name__
    return pl.pallas_call(
        kernel,
        name=title,
        out_shape=outs,
        in_specs=[pl.BlockSpec(memory_space=where[space]) for space in spaces],
        out_specs=[pl.BlockSpec(memory_space=pltpu.VMEM) for _ in outs],
        scratch_shapes=scratch,
        compiler_params=pltpu.CompilerParams(vmem_limit_bytes=VMEM_LIMIT),
        cost_estimate=pl.CostEstimate(
            flops=int(micros * 1.1e9), bytes_accessed=1, transcendentals=0
        ),
    )(*args)


def shape(dims, dtype=f32):
    return jax.ShapeDtypeStruct(dims, dtype)


def pick(block, at):
    zero = jnp.zeros((), jnp.uint32)
    start = (at,) + (zero,) * (block.ndim - 1)
    return lax.dynamic_slice(block, start, (1,) + block.shape[1:])[0]


def halve(block, axis, index, after=None):
    sent = pick(block, index["other " + axis])
    kept = pick(block, index[axis])
    got = lax.ppermute(sent, axis, [(0, 1), (1, 0)])
    if after is not None:
        got, _ = tie(got, after)
    return (kept.astype(f32) + got.astype(f32)).astype(block.dtype)


def sum_by_permutes(block, index, after=None):
    count = block.shape[0]
    if count != 4:
        return sum_over_hi(block)
    total = pick(block, index["hi"]).astype(f32)
    for turn in range(1, count):
        sent = pick(block, index["hi ^ %d" % turn])
        got = lax.ppermute(sent, "hi", [(i, i ^ turn) for i in range(count)])
        if after is not None:
            got, _ = tie(got, after)
        total = total + got.astype(f32)
    return total


def swap_add(send, keep, axis):
    got = lax.ppermute(send, axis, [(0, 1), (1, 0)])
    return (keep.astype(f32) + got.astype(f32)).astype(keep.dtype)


def sum_over_hi(block):
    parts = lax.all_to_all(block, "hi", 0, 0, tiled=True)
    return jnp.sum(parts.astype(f32), 0)


def shifted(block, distance):
    devices = range(lax.axis_size(SEQ))
    route = [(i - distance, i) for i in devices if i - distance in devices]
    return lax.ppermute(block, SEQ, route)


def packed_outs(width_total, width, shares):
    if width // shares % 16 == 0:
        return [shape((width // 2, width_total), bf16)] * 2
    return [shape((width, width_total), bf16)]


def swap(block, axis):
    return lax.ppermute(block, axis, [(0, 1), (1, 0)])


def tie(*values):
    return lax.optimization_barrier(values)


def half_of(share, index):
    rows = share.shape[0] // 2
    zero = jnp.zeros((), jnp.uint32)
    return lax.dynamic_slice(share, (index["lo"] * rows, zero), (rows, share.shape[1]))


def unfolded_rows(block, shares, l2_at):
    width = block.shape[0]
    full = [block[:, l2_at + i * width : l2_at + (i + 1) * width] for i in range(4)]
    full = jnp.concatenate(full, 0).reshape(shares, 4, width // shares, width)
    full = full.transpose(0, 2, 1, 3).reshape(width, 4 * width)
    return jnp.concatenate([block[:, :l2_at], full, block[:, l2_at + 4 * width :]], 1)


def first_sum(parts, shares, order, index, l2_at=None):
    if len(parts) == 2:
        return swap_add(*parts, "core")
    (block,) = parts
    if l2_at is not None:
        block = unfolded_rows(block, shares, l2_at)
    width, total = block.shape
    block = block.reshape(shares // 8, 2, 2, 2, width // shares, total)
    block = halve(block.transpose(3, 0, 1, 2, 4, 5), "core", index)
    places = [("hi", "lo", "x").index(axis) for axis in order]
    return block.transpose(*places, 3, 4).reshape(width // 2, total)


def next_sum(block, axis, index, after=None):
    rows, total = block.shape
    return halve(block.reshape(2, rows // 2, total), axis, index, after)


def last_sum(block, high):
    return sum_over_hi(block.reshape(high, -1, block.shape[1]))


def local(
    activations,
    encoder_attention_norm_gain,
    encoder_attention_norm_bias,
    encoder_query_key_value_weight,
    encoder_attention_output_weight,
    encoder_attention_layer_scale,
    encoder_forward_norm_gain,
    encoder_forward_norm_bias,
    encoder_forward_input_weight,
    encoder_forward_output_weight,
    encoder_forward_layer_scale,
    strided_convolution_weight,
    strided_convolution_bias,
    quantizer_input_weight,
    codebook,
    quantizer_output_weight,
    transposed_convolution_weight,
    transposed_convolution_bias,
    decoder_attention_norm_gain,
    decoder_attention_norm_bias,
    decoder_query_key_value_weight,
    decoder_attention_output_weight,
    decoder_attention_layer_scale,
    decoder_forward_norm_gain,
    decoder_forward_norm_bias,
    decoder_forward_input_weight,
    decoder_forward_output_weight,
    decoder_forward_layer_scale,
    cotangent,
    frame_segment_index,
    frame_code_index,
    replace_code_mask,
    replacing_batch_position,
    code_usage_average,
    code_latent_sum_average,
):
    batch_rows, frames, width = activations.shape
    assert batch_rows == 1
    seq_index = lax.axis_index(SEQ)
    seq_count = lax.axis_size(SEQ)
    dp_index = lax.axis_index(DP)
    dp_count = lax.axis_size(DP)
    shares = dp_count * seq_count
    codec = frames // 2
    levels = frame_code_index.shape[2]
    latent = codebook.shape[2]
    book_share = codebook.shape[1]
    core_index = lax.axis_index("core")

    x_index, lo_index = lax.axis_index("x"), lax.axis_index("lo")
    rows_share = width // seq_count
    high = shares // 8
    total_frames = HALO + frames
    code_total = replace_code_mask.shape[1]
    code_share = code_usage_average.shape[1]
    row_frames = codec * seq_count

    vectors = jnp.stack(
        [
            encoder_attention_norm_gain,
            encoder_attention_norm_bias,
            encoder_attention_layer_scale,
            encoder_forward_norm_gain,
            encoder_forward_norm_bias,
            encoder_forward_layer_scale,
            strided_convolution_bias,
            transposed_convolution_bias,
            decoder_attention_norm_gain,
            decoder_attention_norm_bias,
            decoder_attention_layer_scale,
            decoder_forward_norm_gain,
            decoder_forward_norm_bias,
            decoder_forward_layer_scale,
        ]
    )
    vectors = jnp.pad(vectors, ((0, 2), (0, 0)))
    small = jnp.concatenate(
        [frame_code_index.reshape(-1).astype(f32), vectors.reshape(-1).astype(f32)]
    )
    index = {}
    unsigned = jnp.uint32
    for axis in ("x", "lo", "core"):
        index[axis] = lax.axis_index(axis).astype(unsigned)
        index["other " + axis] = (1 - lax.axis_index(axis)).astype(unsigned)
    index["hi"] = lax.axis_index("hi").astype(unsigned)
    index["seq"] = lax.axis_index(SEQ).astype(unsigned)
    index["owner"] = (lax.axis_index(DP + SEQ) * code_share).astype(unsigned)
    for turn in range(1, 4):
        index["hi ^ %d" % turn] = lax.axis_index("hi").astype(unsigned) ^ unsigned(turn)
    def flat_taps(taps):
        return taps.transpose(1, 0, 2).reshape(taps.shape[1], -1)

    def fold_l2(share):
        return share.reshape(4, -1, width).transpose(1, 0, 2).reshape(-1, 4 * width)

    dec_one = jnp.concatenate(
        [
            quantizer_output_weight.T,
            flat_taps(transposed_convolution_weight),
            decoder_query_key_value_weight,
        ],
        1,
    )
    dec_two = jnp.concatenate(
        [
            decoder_attention_output_weight,
            decoder_forward_input_weight,
            fold_l2(decoder_forward_output_weight),
        ],
        1,
    )
    enc = jnp.concatenate(
        [
            encoder_query_key_value_weight,
            encoder_attention_output_weight,
            flat_taps(strided_convolution_weight),
            quantizer_input_weight,
            encoder_forward_input_weight,
            fold_l2(encoder_forward_output_weight),
        ],
        1,
    )
    half_one = half_of(dec_one, index)
    small, half_one = tie(small, half_one)
    small = lax.all_gather(small, SEQ, axis=0, tiled=False)
    names = sorted(index)
    *index_values, small = tie(*[index[name] for name in names], small)
    index = dict(zip(names, index_values))
    code_count = codec * levels
    row_codes = small[:, :code_count].astype(jnp.int32).reshape(seq_count, codec, levels)
    vectors = small[:, code_count:].reshape(seq_count, 16, -1).transpose(1, 0, 2).reshape(16, width)
    order = [2 * x_index + core_index, 2 * (1 - x_index) + core_index]
    order += [2 * x_index + 1 - core_index, 2 * (1 - x_index) + 1 - core_index]
    cut = jnp.sum((frame_segment_index[0] == 0).astype(jnp.int32))
    scalars = jnp.stack(
        [
            seq_index * frames,
            cut,
            core_index,
            seq_index * book_share,
            lo_index,
            seq_index,
            dp_index * row_frames,
            seq_index,
        ]
        + [
            order[0] * rows_share,
            order[1] * rows_share + lo_index * (rows_share // 2),
            order[1] * rows_share + (1 - lo_index) * (rows_share // 2),
            order[2] * rows_share,
            order[3] * rows_share + lo_index * (rows_share // 2),
            order[3] * rows_share + (1 - lo_index) * (rows_share // 2),
        ]
        + [place * codec for place in order]
    ).astype(jnp.int32)

    half_one, _ = tie(half_one, small)
    near_one = swap(half_one, "x")
    activation_halo = shifted(activations[0, frames - HALO :], 1)

    positions = seq_index * frames - HALO + jnp.arange(total_frames, dtype=jnp.int32)
    half_dim = HEAD_DIM // 2
    frequency = jnp.power(10000.0, -jnp.arange(half_dim, dtype=f32) / half_dim)

    def angle_tables(positions):
        angles = positions.astype(f32)[:, None] * frequency[None, :]
        cos, sin = jnp.cos(angles), jnp.sin(angles)
        return jnp.concatenate([cos] * 4, 1), jnp.concatenate([-sin, sin, -sin, sin], 1)

    window = codec + CODE_HALO
    qsend, qkeep, rsend, rkeep = call(
        lookup_kernel,
        [shape((2, window, latent))] * 2 + [shape((2, levels, codec, latent), bf16)] * 2,
        "svv",
        [pltpu.VMEM((CODE_HALO + codec * seq_count, latent), f32)],
        (scalars, row_codes.reshape(-1, levels), codebook),
        4,
    )
    q_sum = swap_add(qsend, qkeep, "core")
    code_rows = swap_add(rsend, rkeep, "core")
    q_sent = pick(q_sum, index["other x"])
    q_got = swap(q_sent, "x")
    near_one, dec_two, positions, _ = tie(near_one, dec_two, positions, q_sent)
    far_one = swap(near_one, "lo")
    dec_one = [dec_one, near_one, far_one, swap(dec_one, "core"), swap(near_one, "core"),
               swap(far_one, "core")]
    half_two = half_of(dec_two, index)
    cos_table, sin_table = angle_tables(positions)
    half_two, q_got = tie(half_two, q_got)
    near_two = swap(half_two, "x")
    quantized = (pick(q_sum, index["x"]) + q_got).astype(bf16)
    half_three = half_of(enc, index)
    quantized, near_two, half_three, activation_halo, cos_table, sin_table = tie(
        quantized, near_two, half_three, activation_halo, cos_table, sin_table
    )
    far_two = swap(near_two, "lo")
    near_three = swap(half_three, "x")

    d_x, restored, d_n1, d_q, d_k, d_v, d_att = call(
        decoder_front_kernel,
        [
            shape((frames, width)),
            shape((codec + 16, width), bf16),
            shape((frames, width), bf16),
            shape((frames, width), bf16),
            shape((total_frames, width), bf16),
            shape((total_frames, width), bf16),
            shape((frames, width), bf16),
        ],
        "s" + "h" * PIECES + "vvvv",
        [
            pltpu.VMEM((width, latent + 7 * width), bf16),
            pltpu.VMEM((width // 128, total_frames, 128), f32),
            pltpu.SemaphoreType.DMA((PIECES,)),
        ],
        (scalars, *dec_one, quantized, vectors, cos_table, sin_table),
        8,
    )
    d_att, far_two, code_rows, replace_code_mask, replacing_batch_position, row_codes = tie(
        d_att, far_two, code_rows, replace_code_mask, replacing_batch_position, row_codes
    )
    dec_two = [dec_two, near_two, far_two, swap(dec_two, "core"), swap(near_two, "core"),
               swap(far_two, "core")]
    marked = (replacing_batch_position * 2 + replace_code_mask).T
    marked = marked.reshape(dp_count, seq_count, code_share, levels).transpose(1, 0, 2, 3)
    marked = pick(marked, index["seq"]).reshape(dp_count * code_share, levels)
    row_codes = row_codes.reshape(row_frames, levels).T
    owner_flag = lax.dynamic_slice(
        replace_code_mask, (jnp.zeros((), unsigned), index["owner"]), (levels, code_share)
    ) == 1
    d_att, marked, row_codes, owner_flag, near_three = tie(
        d_att, marked, row_codes, owner_flag, near_three
    )
    far_three = swap(near_three, "lo")
    layer_scratch = [
        pltpu.VMEM((frames, width), bf16),
        pltpu.VMEM((total_frames, width), f32),
        pltpu.VMEM((total_frames, width), f32),
        pltpu.SemaphoreType.DMA((3 * PIECES,)),
    ]
    forward_outs = [shape((frames, width), bf16), shape((frames, 4 * width), bf16)]
    kept_outs = [shape((frames, 4 * width)), shape((frames, width)), shape((frames, width))]
    backward_outs = [
        shape((frames, width)),
        shape((frames, 4 * width), bf16),
        shape((frames, width), bf16),
        shape((frames, width), bf16),
        shape((8, width)),
        shape((frames, width)),
        shape((frames, width)),
        shape((frames, width)),
        shape((HALO, 2 * width), bf16),
    ]
    weights_scratch = pltpu.VMEM((width, 9 * width), bf16)
    (output, d_n2, d_active, d_gmid, d_dh, d_dtwo, d_done, d_vg_two, d_dq, d_dk, d_dv, d_dkv) = call(
        partial(decoder_layer_kernel, ((0, 0), (0, width), (0, 5 * width))),
        [shape((frames, width), bf16)] + forward_outs + backward_outs,
        "s" + "h" * PIECES + "vvvvvvv",
        [
            weights_scratch,
            pltpu.VMEM((frames, width), f32),
            pltpu.VMEM((frames, 4 * width), bf16),
            pltpu.VMEM((frames, 4 * width), f32),
            pltpu.VMEM((frames, width), f32),
            pltpu.VMEM((frames, width), f32),
        ]
        + layer_scratch,
        (scalars, *dec_two, d_att, d_x, cotangent[0], vectors, d_q, d_k, d_v),
        14,
    )
    d_dkv = shifted(d_dkv, -1)
    group_a = call(
        partial(decoder_gradients_kernel, shares),
        packed_outs(9 * width, width, shares),
        "svvvvvv",
        [],
        (scalars, d_n2, d_active, d_dh, d_dtwo, d_att, d_done),
        5,
    )
    d_dq, *group_a = tie(d_dq, *group_a)
    enc_core, enc_near_core = swap(enc, "core"), swap(near_three, "core")
    a_sum = first_sum(group_a, shares, ORDER_A, index, 0)
    d_up, d_mixed, d_vg_one = call(
        partial(decoder_back_kernel, latent + 4 * width),
        [shape((frames, width), bf16), shape((frames, 3 * width), bf16), shape((8, width))],
        "s" + "h" * PIECES + "v" * 9,
        [pltpu.VMEM((width, 3 * width), bf16), pltpu.SemaphoreType.DMA((PIECES,))],
        (
            scalars, *dec_one, d_dq, d_dk, d_dv, d_dkv, d_x, d_gmid, vectors, cos_table,
            sin_table,
        ),
        4,
    )
    d_up_next = shifted(d_up[:32], -1)

    code_rows, d_dkv = tie(code_rows, d_dkv)
    code_rows = halve(code_rows, "x", index)

    a_sum, d_up, e_input, far_three = tie(a_sum, d_up, activations[0], far_three)
    enc = [enc, near_three, far_three, enc_core, enc_near_core, swap(far_three, "core")]
    e_n1, e_q, e_k, e_v, e_att = call(
        encoder_front_kernel,
        [
            shape((frames, width), bf16),
            shape((frames + EXTRA, width), bf16),
            shape((total_frames, width), bf16),
            shape((total_frames, width), bf16),
            shape((frames + EXTRA, width), bf16),
        ],
        "s" + "h" * PIECES + "vvvvv",
        [pltpu.VMEM((width, 3 * width), bf16), pltpu.SemaphoreType.DMA((PIECES,))],
        (scalars, *enc, activation_halo, e_input, vectors, cos_table, sin_table),
        7,
    )

    d_mixed, e_n1 = tie(d_mixed, e_n1)
    middle_outs = call(
        partial(middle_kernel, shares),
        [
            shape((frames, width)),
            shape((codec, width), bf16),
            shape((codec, latent), bf16),
            shape((8, width)),
        ]
        + packed_outs(7 * width + latent, width, shares),
        "s" + "h" * (2 * PIECES) + "" + "v" * 6,
        [
            pltpu.VMEM((width, latent + 4 * width), bf16),
            pltpu.VMEM((width, latent + 4 * width), bf16),
            pltpu.VMEM((width // 128, frames + 32, 128), f32),
            pltpu.SemaphoreType.DMA((2 * PIECES,)),
        ],
        (scalars, *dec_one, *enc, d_up, d_up_next, d_mixed, d_n1, restored, quantized),
        7,
    )
    d_encoded, d_reduced, d_latent, m_vg = middle_outs[:4]
    b_sum = first_sum(middle_outs[4:], shares, ORDER_B, index)

    e_att, d_encoded = tie(e_att, d_encoded)
    enc_plan = ((0, 3 * width), (0, 8 * width + latent), (0, 12 * width + latent))
    rows = frames + EXTRA
    encoded, e_n2, e_active, e_slope, e_mid, e_second = call(
        partial(encoder_forward_kernel, enc_plan),
        [shape((rows, width), bf16)] + forward_outs + kept_outs,
        "s" + "h" * PIECES + "vvvv",
        [
            weights_scratch,
            pltpu.VMEM((rows, width), f32),
            pltpu.VMEM((rows, 4 * width), bf16),
            pltpu.SemaphoreType.DMA((3 * PIECES,)),
        ],
        (scalars, *enc, activation_halo, e_input, e_att, vectors),
        6,
    )
    encoded, b_sum = tie(encoded, b_sum)
    a_sum = next_sum(a_sum, ORDER_A[0], index)
    residuals, windows, reduced = call(
        latent_kernel,
        [
            shape((levels, codec, latent), bf16),
            shape((4, codec, width), bf16),
            shape((codec, width), bf16),
        ],
        "s" + "h" * PIECES + "vvv",
        [
            pltpu.VMEM((width, 4 * width + latent), bf16),
            pltpu.VMEM((width // 128, frames + EXTRA, 128), f32),
            pltpu.SemaphoreType.DMA((PIECES,)),
        ],
        (scalars, *enc, encoded, code_rows, vectors),
        3,
    )
    near_res = swap(residuals, "x")
    res_pieces = [residuals, near_res, swap(residuals, "core"), swap(near_res, "core")]

    d_encoded, a_sum, _ = tie(d_encoded, a_sum, residuals)
    a_sum = next_sum(a_sum, ORDER_A[1], index)
    (e_gmid, e_dh, e_dtwo, e_done, e_vg_two, e_dq, e_dk, e_dv, e_dkv) = call(
        partial(encoder_backward_kernel, enc_plan),
        backward_outs,
        "s" + "h" * PIECES + "v" * 9,
        [weights_scratch] + layer_scratch,
        (
            scalars, *enc, e_att, d_encoded, vectors, e_slope, e_mid, e_second,
            e_q, e_k, e_v,
        ),
        11,
    )
    e_dkv = shifted(e_dkv, -1)
    if code_share % 16 == 0:
        tail_rows = levels * code_share
        csend, ckeep = call(
            partial(collect_kernel, code_share, seq_count),
            [shape((dp_count // 2, tail_rows + 2 * levels, latent), bf16)] * 2,
            "svvvvvv",
            [
                pltpu.VMEM((row_frames, latent), bf16),
                pltpu.VMEM((levels, dp_count * code_share), f32),
            ],
            (scalars, *res_pieces, row_codes, marked),
            5,
        )
        e_n2, csend, e_gmid = tie(e_n2, csend, e_gmid)
    c_outs = packed_outs(8 * width, width, shares)
    group_c = call(
        partial(encoder_gradients_kernel, shares),
        c_outs + packed_outs(5 * width + latent, width, shares),
        "s" + "v" * 10,
        [],
        (
            scalars, e_n2, e_active, e_dh, e_dtwo, e_att, e_done, windows, d_reduced, reduced,
            d_latent,
        ),
        5,
    )
    e_dq, *group_c = tie(e_dq, *group_c)
    c_one = first_sum(group_c[: len(c_outs)], shares, ORDER_C_ONE, index, 0)
    c_two = first_sum(group_c[len(c_outs) :], shares, ORDER_C_TWO, index)
    e_dq, c_one, c_two, a_sum = tie(e_dq, c_one, c_two, a_sum)
    vector_grads = jnp.concatenate([e_vg_two, d_vg_two, m_vg, d_vg_one], 0)
    grad_outs = call(
        partial(encoder_back_kernel, shares),
        [shape((frames, width), bf16)] + packed_outs(3 * width + 128, width, shares),
        "s" + "h" * PIECES + "v" * 11,
        [
            pltpu.VMEM((width, 3 * width), bf16),
            pltpu.VMEM((frames, 3 * width), bf16),
            pltpu.VMEM((8, width), f32),
            pltpu.VMEM((128, width), f32),
            pltpu.SemaphoreType.DMA((PIECES,)),
        ],
        (
            scalars, *enc, e_dq, e_dk, e_dv, e_dkv, e_input, e_gmid, vectors,
            cos_table, sin_table, e_n1, vector_grads,
        ),
        5,
    )
    activations_grad = grad_outs[0]

    b_sum = sum_by_permutes(
        b_sum.reshape(high, -1, b_sum.shape[1]), index, activations_grad
    ).astype(bf16)
    grads_a = sum_by_permutes(a_sum.reshape(high, -1, a_sum.shape[1]), index, activations_grad)
    d_sum = first_sum(grad_outs[1:], shares, ORDER_D, index)
    c_one = next_sum(c_one, ORDER_C_ONE[0], index, d_sum)
    b_sum = next_sum(b_sum, ORDER_B[1], index)
    c_two = next_sum(c_two, ORDER_C_TWO[0], index, c_one)
    if code_share % 16 == 0:
        combined = sum_by_permutes(swap_add(csend, ckeep, "lo"), index)
        summed = combined[:tail_rows].reshape(levels, code_share, latent)
        digits = combined[tail_rows:, :code_share]
        counted = 128.0 * digits[:levels] + digits[levels:]
    else:
        entry = (
            jnp.arange(dp_count, dtype=jnp.int32)[:, None] * seq_count + seq_index
        ) * code_share + jnp.arange(code_share, dtype=jnp.int32)
        relative = [place * codec + jnp.arange(codec, dtype=jnp.int32) for place in order]
        relative = jnp.concatenate(relative)
        flat_res = jnp.concatenate(res_pieces, 1)
        used = entry.reshape(1, -1, 1) == row_codes[:, None, relative]
        placed = (marked.T // 2)[:, :, None] == dp_index * row_frames + relative
        counts = jnp.sum(used.astype(f32), 2).reshape(levels, dp_count, code_share)
        selects = jnp.where((marked.T % 2)[:, :, None] == 1, placed, used).astype(bf16)
        sums = jnp.einsum("lct,ltd->lcd", selects, flat_res, preferred_element_type=f32)
        sums = sums.astype(bf16).reshape(levels, dp_count, code_share, latent)
        summed = lax.psum_scatter(sums, DP, scatter_dimension=1, tiled=False).astype(f32)
        counted = lax.psum_scatter(counts, DP, scatter_dimension=1, tiled=False)
    d_sum = next_sum(d_sum, ORDER_D[0], index, c_two)
    c_one = next_sum(c_one, ORDER_C_ONE[1], index)
    c_two = next_sum(c_two, ORDER_C_TWO[1], index, d_sum)
    grads_b = next_sum(b_sum, ORDER_B[2], index).astype(f32)
    d_sum = next_sum(d_sum, ORDER_D[1], index, c_two)
    edge, far_edge = c_one.shape[1], c_one.shape[1] + c_two.shape[1]
    together = last_sum(jnp.concatenate([c_one, c_two, d_sum], 1), high)
    grads_c, grads_c_two, grads_d = (
        together[:, :edge], together[:, edge:far_edge], together[:, far_edge:]
    )

    new_cluster_size = ema_decay * code_usage_average + (1.0 - ema_decay) * counted
    new_embed_sum = jnp.where(
        owner_flag[:, :, None],
        summed * new_cluster_size[:, :, None],
        ema_decay * code_latent_sum_average + (1.0 - ema_decay) * summed,
    )
    new_codebook = new_embed_sum / new_cluster_size[:, :, None]

    def columns(block, at, count):
        return block[:, at * width : (at + count) * width]

    def taps(block):
        return block.reshape(-1, 4, width).transpose(1, 0, 2)

    def unfold(block):
        return block.reshape(-1, 4, width).transpose(1, 0, 2).reshape(-1, width)

    vec = grads_d[:, 3 * width : 3 * width + 16].T
    return (
        output[None],
        activations_grad[None],
        vec[0],
        vec[1],
        columns(grads_d, 0, 3),
        columns(grads_c_two, 4, 1),
        vec[2],
        vec[3],
        vec[4],
        columns(grads_c, 4, 4),
        unfold(columns(grads_c, 0, 4)),
        vec[5],
        taps(columns(grads_c_two, 0, 4)),
        vec[6],
        grads_c_two[:, 5 * width :],
        grads_b[:, 7 * width :].T,
        taps(columns(grads_b, 3, 4)),
        vec[7],
        vec[8],
        vec[9],
        columns(grads_b, 0, 3),
        columns(grads_a, 8, 1),
        vec[10],
        vec[11],
        vec[12],
        columns(grads_a, 4, 4),
        unfold(columns(grads_a, 0, 4)),
        vec[13],
        new_cluster_size,
        new_embed_sum,
        new_codebook,
    )


def solution(mesh):
    grid = mesh.devices
    mesh = jax.sharding.Mesh(
        grid.reshape(grid.shape[0] // 2, 2, grid.shape[1] // 2, 2), ("hi", "lo", "x", "core")
    )
    placed = (
        P(DP, SEQ, None),
        P(SEQ),
        P(SEQ),
        P(SEQ, None),
        P(SEQ, None),
        P(SEQ),
        P(SEQ),
        P(SEQ),
        P(SEQ, None),
        P(SEQ, None),
        P(SEQ),
        P(None, SEQ, None),
        P(SEQ),
        P(SEQ, None),
        P(None, SEQ, None),
        P(None, SEQ),
        P(None, SEQ, None),
        P(SEQ),
        P(SEQ),
        P(SEQ),
        P(SEQ, None),
        P(SEQ, None),
        P(SEQ),
        P(SEQ),
        P(SEQ),
        P(SEQ, None),
        P(SEQ, None),
        P(SEQ),
        P(DP, SEQ, None),
        P(DP, None),
        P(DP, SEQ, None),
        P(),
        P(),
        P(None, DP + SEQ),
        P(None, DP + SEQ, None),
    )
    return jax.shard_map(
        local,
        mesh=mesh,
        in_specs=placed,
        out_specs=(
            P(DP, SEQ, None),
            P(DP, SEQ, None),
            P(DP + SEQ),
            P(DP + SEQ),
            P(DP + SEQ, None),
            P(DP + SEQ, None),
            P(DP + SEQ),
            P(DP + SEQ),
            P(DP + SEQ),
            P(DP + SEQ, None),
            P(DP + SEQ, None),
            P(DP + SEQ),
            P(None, DP + SEQ, None),
            P(DP + SEQ),
            P(DP + SEQ, None),
            P(None, DP + SEQ),
            P(None, DP + SEQ, None),
            P(DP + SEQ),
            P(DP + SEQ),
            P(DP + SEQ),
            P(DP + SEQ, None),
            P(DP + SEQ, None),
            P(DP + SEQ),
            P(DP + SEQ),
            P(DP + SEQ),
            P(DP + SEQ, None),
            P(DP + SEQ, None),
            P(DP + SEQ),
            P(None, DP + SEQ),
            P(None, DP + SEQ, None),
            P(None, DP + SEQ, None),
        ),
        check_vma=False,
    )
```

```python
from functools import partial

import jax
import jax.numpy as jnp
from jax import lax
from jax.experimental import pallas as pl
from jax.experimental.pallas import tpu as pltpu
from jax.sharding import PartitionSpec as P

HEADS = 8
HEAD_DIM = 64
CONTEXT = 250
HALO = 256
CODE_HALO = HALO // 2 + 16
EXTRA = 16
QUERIES = 64
GROUP = 4
WINDOW = HALO + QUERIES
VMEM_LIMIT = 26 * 1024 * 1024
ORDER_A = ("lo", "x", "hi")
ORDER_B = ("lo", "x", "hi")
ORDER_C_ONE = ("x", "lo", "hi")
ORDER_C_TWO = ("lo", "x", "hi")
ORDER_D = ("lo", "x", "hi")
DP = ("hi", "lo")
SEQ = ("x", "core")

norm_eps = 1e-05
ema_decay = 0.9
bf16 = jnp.bfloat16
f32 = jnp.float32


PIECES = 6


def fetch(sc_ref, pieces, at, width, dst, sems, first=0):
    copies = []
    for i, piece in enumerate(pieces):
        rows = piece.shape[0]
        row = pl.multiple_of(sc_ref[8 + i], 64)
        copies.append(
            pltpu.make_async_copy(
                piece.at[:, at : at + width], dst.at[pl.ds(row, rows), :], sems.at[first + i]
            )
        )
        copies[-1].start()
    return copies


def split_refs(refs, counts):
    groups = []
    for count in counts:
        groups.append(refs[:count])
        refs = refs[count:]
    return groups, refs


def wait_all(copies):
    for copy in copies:
        copy.wait()


def mm(a, b):
    return jnp.dot(a, b, preferred_element_type=f32)


def mm_nt(a, b):
    return lax.dot_general(a, b, (((1,), (1,)), ((), ())), preferred_element_type=f32)


def mm_tn(a, b):
    return lax.dot_general(a, b, (((0,), (0,)), ((), ())), preferred_element_type=f32)


def normalize(stream):
    center = stream - jnp.mean(stream, -1, keepdims=True)
    scaled = lax.rsqrt(jnp.mean(center * center, -1, keepdims=True) + norm_eps)
    return center * scaled, scaled


def norm_backward(upstream, normal, scaled, gain):
    inner = upstream * gain
    return scaled * (
        inner
        - jnp.mean(inner, -1, keepdims=True)
        - normal * jnp.mean(inner * normal, -1, keepdims=True)
    )


def column_sum(value):
    return jnp.sum(value, 0, keepdims=True)


def interleave(even, odd, scr):
    tiles, rows, _ = scr.shape
    for tile in range(tiles):
        cols = slice(tile * 128, (tile + 1) * 128)
        scr[tile, pl.ds(0, rows // 2, stride=2), :] = even[:, cols]
        scr[tile, pl.ds(1, rows // 2, stride=2), :] = odd[:, cols]
    return jnp.concatenate([scr[tile] for tile in range(tiles)], 1)


def split_rows(value, scr):
    tiles, rows, _ = scr.shape
    for tile in range(tiles):
        scr[tile] = value[:, tile * 128 : (tile + 1) * 128]
    even = [scr[tile, pl.ds(0, rows // 2, stride=2), :] for tile in range(tiles)]
    odd = [scr[tile, pl.ds(1, rows // 2, stride=2), :] for tile in range(tiles)]
    return jnp.concatenate(even, 1), jnp.concatenate(odd, 1)


def first_half():
    lane = lax.broadcasted_iota(jnp.int32, (1, 128), 1)
    return lane % HEAD_DIM < HEAD_DIM // 2


def rotate(tile, cos, sin):
    swapped = jnp.where(first_half(), pltpu.roll(tile, 96, 1), pltpu.roll(tile, 32, 1))
    return tile * cos + swapped * sin


def head_lanes():
    lane = lax.broadcasted_iota(jnp.int32, (1, GROUP * HEAD_DIM), 1) // HEAD_DIM
    return [(lane == head) for head in range(GROUP)]


def stack_heads(block, lanes):
    return jnp.concatenate([block * mask.astype(bf16) for mask in lanes], 0)


def unstack_heads(block, lanes):
    rows = block.shape[0] // GROUP
    out = block[:rows]
    for head in range(1, GROUP):
        out = jnp.where(lanes[head], block[head * rows : (head + 1) * rows], out)
    return out


def lowest_key(query, cut):
    low = jnp.maximum(query - (CONTEXT - 1), 0)
    return jnp.where(query >= cut, jnp.maximum(low, cut), low)


def attend(q_ref, k_ref, v_ref, att_ref, sc_ref, rows, first_query, first_key, keys, at_row):
    start, cut = sc_ref[0], sc_ref[1]
    query = start + first_query + lax.broadcasted_iota(jnp.int32, (rows, 1), 0)
    low = lowest_key(query, cut)
    key = start + first_key + lax.broadcasted_iota(jnp.int32, (rows, keys), 1)
    mask = (key <= query) & (key >= low)
    mask = jnp.concatenate([mask] * GROUP, 0)
    lanes = head_lanes()
    key_row = first_key + HALO
    for group in range(HEADS // GROUP):
        cols = slice(group * GROUP * HEAD_DIM, (group + 1) * GROUP * HEAD_DIM)
        stacked = stack_heads(q_ref[at_row : at_row + rows, cols], lanes)
        scores = mm_nt(stacked, k_ref[key_row : key_row + keys, cols]) * HEAD_DIM ** (-0.5)
        scores = jnp.where(mask, scores, -1e30)
        exponent = jnp.exp(scores - jnp.max(scores, -1, keepdims=True))
        weights = exponent * (1.0 / jnp.sum(exponent, -1, keepdims=True))
        mixed = mm(weights.astype(bf16), v_ref[key_row : key_row + keys, cols])
        att_ref[at_row : at_row + rows, cols] = unstack_heads(mixed, lanes).astype(bf16)


def front(x, vec_ref, base, w_in, cos_ref, sin_ref, sc_ref, n1_ref, q_ref, k_ref, v_ref, att_ref,
          extra):
    width = x.shape[1]
    normal, _ = normalize(x)
    low = (normal * vec_ref[base : base + 1] + vec_ref[base + 1 : base + 2]).astype(bf16)
    n1_ref[...] = low[HALO:]
    skip = HALO - extra
    queries = mm(low[skip:], w_in[:, :width])
    keys = mm(low, w_in[:, width : 2 * width])
    for at in range(0, width, 128):
        q_ref[:, at : at + 128] = rotate(
            queries[:, at : at + 128], cos_ref[skip:], sin_ref[skip:]
        ).astype(bf16)
        k_ref[:, at : at + 128] = rotate(keys[:, at : at + 128], cos_ref[...], sin_ref[...]).astype(
            bf16
        )
    v_ref[...] = mm(low, w_in[:, 2 * width :]).astype(bf16)
    frames = x.shape[0] - HALO
    if extra:
        attend(q_ref, k_ref, v_ref, att_ref, sc_ref, extra, -extra, -HALO, HALO, 0)
    for first in range(0, frames, QUERIES):
        attend(
            q_ref, k_ref, v_ref, att_ref, sc_ref, QUERIES, first, first - HALO, WINDOW,
            extra + first,
        )


def decoder_front_kernel(sc_ref, *refs):
    pieces, refs = refs[:PIECES], refs[PIECES:]
    (qz_ref, vec_ref, cos_ref, sin_ref, x_ref, restored_ref, n1_ref, q_ref, k_ref, v_ref, att_ref,
     w_vmem, x_scr, sems) = refs
    width = x_ref.shape[1]
    wait_all(fetch(sc_ref, pieces, 0, w_vmem.shape[1], w_vmem, sems))
    latent = qz_ref.shape[1]
    restored = mm_nt(qz_ref[...], w_vmem[:, :latent]).astype(bf16)
    restored_ref[...] = restored[CODE_HALO - 16 :]
    both = mm(restored, w_vmem[:, latent : latent + 4 * width])
    bias = vec_ref[7:8]
    now = both[16:, : 2 * width]
    before = pltpu.roll(both[:, 2 * width :], 1, 0)[16:]
    total = now + before
    x = interleave(total[:, :width] + bias, total[:, width:] + bias, x_scr)
    x_ref[...] = x[HALO:]
    w_in = w_vmem.at[:, latent + 4 * width :]
    front(x, vec_ref, 8, w_in, cos_ref, sin_ref, sc_ref, n1_ref, q_ref, k_ref, v_ref,
          att_ref, 0)


def encoder_front_kernel(sc_ref, *refs):
    (pieces,), refs = split_refs(refs, (PIECES,))
    (halo_ref, x_ref, vec_ref, cos_ref, sin_ref, n1_ref, q_ref, k_ref, v_ref, att_ref,
     w_vmem, sems) = refs
    width = x_ref.shape[1]
    copies = fetch(sc_ref, pieces, 0, 3 * width, w_vmem, sems)
    x = jnp.concatenate([halo_ref[...], x_ref[...]], 0).astype(f32)
    wait_all(copies)
    front(x, vec_ref, 0, w_vmem, cos_ref, sin_ref, sc_ref, n1_ref, q_ref, k_ref, v_ref, att_ref,
          EXTRA)


def gelu_both(hidden):
    share = 0.5 * (1.0 + lax.erf(hidden * 0.7071067811865476))
    density = jnp.exp(-0.5 * hidden * hidden) * 0.3989422804014327
    return hidden * share, share + hidden * density


def l2_rows(w, at, chunk, width):
    rows = width // 4
    return jnp.concatenate(
        [
            w[chunk * rows : (chunk + 1) * rows, at + g * width : at + (g + 1) * width]
            for g in range(4)
        ],
        0,
    )


def fetch_layer(sc_ref, groups, plan, width, w_vmem, sems):
    edges = (0, width, 5 * width, 9 * width)
    return [
        fetch(
            sc_ref, groups[plan[i][0]], plan[i][1], high - low, w_vmem.at[:, low:high], sems,
            PIECES * i,
        )
        for i, (low, high) in enumerate(zip(edges[:-1], edges[1:]))
    ]


def ff_forward(base, extra, copies, w_vmem, att_ref, stream, vec_ref, out_ref, n2_ref, active_ref,
               slope_ref, mid_ref, second_ref, h_scr, act_scr):
    rows, width = stream.shape
    scale_one = vec_ref[base + 2 : base + 3]
    gain_two = vec_ref[base + 3 : base + 4]
    bias_two = vec_ref[base + 4 : base + 5]
    scale_two = vec_ref[base + 5 : base + 6]
    wait_all(copies[0])
    middle = stream + scale_one * mm(att_ref[...], w_vmem[:, :width])
    mid_ref[...] = middle[extra:]
    normal, _ = normalize(middle)
    n2 = (normal * gain_two + bias_two).astype(bf16)
    n2_ref[...] = n2[extra:]
    wait_all(copies[1])
    l1_at, l2_at = width, 5 * width
    second = None
    for chunk in range(4):
        cols = slice(chunk * width, (chunk + 1) * width)
        h_scr[...] = mm(n2, w_vmem[:, l1_at + chunk * width : l1_at + (chunk + 1) * width])
        if extra:
            act, _ = gelu_both(h_scr[:extra, :])
            act_scr[:extra, cols] = act.astype(bf16)

        def body(i, _):
            at_row = pl.multiple_of(i * 16, 16)
            act, slope = gelu_both(h_scr[pl.ds(at_row + extra, 16), :])
            act_scr[pl.ds(at_row + extra, 16), cols] = act.astype(bf16)
            slope_ref[pl.ds(at_row, 16), cols] = slope
            return 0

        lax.fori_loop(0, (rows - extra) // 16, body, 0)
        if chunk == 0:
            wait_all(copies[2])
        part = mm(act_scr[:, cols], l2_rows(w_vmem, l2_at, chunk, width))
        second = part if second is None else second + part
    active_ref[...] = act_scr[extra:, :]
    second_ref[...] = second[extra:]
    out_ref[...] = (middle + scale_two * second).astype(bf16)


def ff_backward(base, extra, w_vmem, att_ref, g, vec_ref, slope_ref, mid_ref, second_ref, gmid_ref,
                dh_ref, dtwo_ref, done_ref, vg_ref, datt_scr):
    width = g.shape[1]
    scale_one = vec_ref[base + 2 : base + 3]
    gain_two = vec_ref[base + 3 : base + 4]
    scale_two = vec_ref[base + 5 : base + 6]
    l1_at, l2_at = width, 5 * width
    vg_ref[3:4, :] = column_sum(g * second_ref[...])
    d_two = (g * scale_two).astype(bf16)
    dtwo_ref[...] = d_two
    e = None
    for chunk in range(4):
        cols = slice(chunk * width, (chunk + 1) * width)
        d_active = mm_nt(d_two, l2_rows(w_vmem, l2_at, chunk, width))
        dh_ref[:, cols] = (d_active * slope_ref[:, cols]).astype(bf16)
        part = mm_nt(
            dh_ref[:, cols], w_vmem[:, l1_at + chunk * width : l1_at + (chunk + 1) * width]
        )
        e = part if e is None else e + part
    normal, scaled = normalize(mid_ref[...])
    vg_ref[1:2, :] = column_sum(e * normal)
    vg_ref[2:3, :] = column_sum(e)
    g_mid = g + norm_backward(e, normal, scaled, gain_two)
    gmid_ref[...] = g_mid
    vg_ref[0:1, :] = column_sum(g_mid * mm(att_ref[extra:, :], w_vmem[:, :width]))
    d_one = (g_mid * scale_one).astype(bf16)
    done_ref[...] = d_one
    datt_scr[...] = mm_nt(d_one, w_vmem[:, :width]).astype(bf16)


def decoder_layer_kernel(plan, sc_ref, *refs):
    (pieces,), refs = split_refs(refs, (PIECES,))
    (att_ref, x_ref, g_ref, vec_ref, q_ref, k_ref, v_ref,
     out_ref, n2_ref, active_ref, gmid_ref, dh_ref, dtwo_ref, done_ref, vg_ref,
     dq_ref, dk_ref, dv_ref, dkv_ref,
     w_vmem, h_scr, act_scr, slope_scr, mid_scr, second_scr, datt_scr, dk_scr, dv_scr, sems) = refs
    width = x_ref.shape[1]
    copies = fetch_layer(sc_ref, (pieces,), plan, width, w_vmem, sems)
    ff_forward(8, 0, copies, w_vmem, att_ref, x_ref[...], vec_ref, out_ref, n2_ref, active_ref,
               slope_scr, mid_scr, second_scr, h_scr, act_scr)
    ff_backward(8, 0, w_vmem, att_ref, g_ref[...].astype(f32), vec_ref, slope_scr, mid_scr,
                second_scr, gmid_ref, dh_ref, dtwo_ref, done_ref, vg_ref, datt_scr)
    attention_backward(0, sc_ref, q_ref, k_ref, v_ref, datt_scr, dq_ref, dk_ref, dv_ref, dkv_ref,
                       dk_scr, dv_scr)


def encoder_forward_kernel(plan, sc_ref, *refs):
    groups, refs = split_refs(refs, (PIECES, PIECES))
    (halo_ref, x_ref, att_ref, vec_ref,
     out_ref, n2_ref, active_ref, slope_ref, mid_ref, second_ref,
     w_vmem, h_scr, act_scr, sems) = refs
    width = x_ref.shape[1]
    copies = fetch_layer(sc_ref, groups, plan, width, w_vmem, sems)
    stream = jnp.concatenate([halo_ref[HALO - EXTRA :, :], x_ref[...]], 0).astype(f32)
    ff_forward(0, EXTRA, copies, w_vmem, att_ref, stream, vec_ref, out_ref, n2_ref, active_ref,
               slope_ref, mid_ref, second_ref, h_scr, act_scr)


def encoder_backward_kernel(plan, sc_ref, *refs):
    groups, refs = split_refs(refs, (PIECES, PIECES))
    (att_ref, g_ref, vec_ref, slope_ref, mid_ref, second_ref, q_ref, k_ref, v_ref,
     gmid_ref, dh_ref, dtwo_ref, done_ref, vg_ref, dq_ref, dk_ref, dv_ref, dkv_ref,
     w_vmem, datt_scr, dk_scr, dv_scr, sems) = refs
    width = g_ref.shape[1]
    for copies in fetch_layer(sc_ref, groups, plan, width, w_vmem, sems):
        wait_all(copies)
    ff_backward(0, EXTRA, w_vmem, att_ref, g_ref[...], vec_ref, slope_ref, mid_ref, second_ref,
                gmid_ref, dh_ref, dtwo_ref, done_ref, vg_ref, datt_scr)
    attention_backward(EXTRA, sc_ref, q_ref, k_ref, v_ref, datt_scr, dq_ref, dk_ref, dv_ref,
                       dkv_ref, dk_scr, dv_scr)


def attention_backward(extra, sc_ref, q_ref, k_ref, v_ref, do_ref,
                       dq_ref, dk_ref, dv_ref, dkv_ref, dk_scr, dv_scr):
    start, cut = sc_ref[0], sc_ref[1]
    frames = do_ref.shape[0]
    lanes = head_lanes()
    scale = HEAD_DIM ** (-0.5)
    dk_scr[...] = jnp.zeros_like(dk_scr)
    dv_scr[...] = jnp.zeros_like(dv_scr)
    wide = GROUP * QUERIES
    for first in range(0, frames, QUERIES):
        lane = lax.broadcasted_iota(jnp.int32, (1, wide), 1) % QUERIES
        query = start + first + lane
        low = lowest_key(query, cut)
        key = start + first - HALO + lax.broadcasted_iota(jnp.int32, (WINDOW, wide), 0)
        mask = (key <= query) & (key >= low)
        for group in range(HEADS // GROUP):
            cols = slice(group * GROUP * HEAD_DIM, (group + 1) * GROUP * HEAD_DIM)
            qs = stack_heads(q_ref[extra + first : extra + first + QUERIES, cols], lanes)
            ds = stack_heads(do_ref[first : first + QUERIES, cols], lanes)
            kw = k_ref[first : first + WINDOW, cols]
            vw = v_ref[first : first + WINDOW, cols]
            scores = jnp.where(mask, mm_nt(kw, qs) * scale, -1e30)
            exponent = jnp.exp(scores - jnp.max(scores, 0, keepdims=True))
            probs = exponent * (1.0 / jnp.sum(exponent, 0, keepdims=True))
            d_probs = mm_nt(vw, ds)
            mean = jnp.sum(probs * d_probs, 0, keepdims=True)
            d_scores = (probs * (d_probs - mean)).astype(bf16)
            dk_scr[first : first + WINDOW, cols] += mm(d_scores, qs)
            dv_scr[first : first + WINDOW, cols] += mm(probs.astype(bf16), ds)
            dq_ref[first : first + QUERIES, cols] = (
                unstack_heads(mm_tn(d_scores, kw), lanes) * scale
            )
    width = dq_ref.shape[1]
    dkv_ref[:, :width] = (dk_scr[:HALO] * scale).astype(bf16)
    dkv_ref[:, width:] = dv_scr[:HALO].astype(bf16)
    dk_ref[...] = dk_scr[HALO:] * scale
    dv_ref[...] = dv_scr[HALO:]


class Packer:
    def __init__(self, core, refs, shares, order):
        self.core, self.refs, self.shares, self.order = core, refs, shares, order

    def put(self, value, at, step=1, phase=0, block0=0):
        if len(self.refs) == 1:
            if step == 1:
                self.refs[0][:, at : at + value.shape[1]] = value.astype(bf16)
            return
        send, keep = self.refs
        cols = slice(at, at + value.shape[1])
        rows = 16
        hi = self.shares // 8
        blocks = value.shape[0] // (rows * step)
        for pair in range(blocks // 2):
            even = value[(2 * pair * step + phase) * rows :][:rows]
            odd = value[((2 * pair + 1) * step + phase) * rows :][:rows]
            block = (block0 + 2 * pair) // 2
            place = {"x": (block % 2, 2), "lo": (block // 2 % 2, 2), "hi": (block // 4, hi)}
            at_row = 0
            for axis in self.order:
                at_row = at_row * place[axis][1] + place[axis][0]
            at_row = at_row * rows
            first = self.core == 0
            keep[at_row : at_row + rows, cols] = jnp.where(first, even, odd).astype(bf16)
            send[at_row : at_row + rows, cols] = jnp.where(first, odd, even).astype(bf16)

    def put_l2(self, value, at, chunk, width):
        if len(self.refs) == 1:
            cols = slice(at + chunk * width, at + (chunk + 1) * width)
            self.refs[0][:, cols] = value.astype(bf16)
            return
        for phase in range(4):
            self.put(value, at + phase * width, 4, phase, chunk * width // 64)


def linear_gradients(pack, n2_ref, active_ref, dh_ref, dtwo_ref):
    width = n2_ref.shape[1]
    for chunk in range(4):
        cols = slice(chunk * width, (chunk + 1) * width)
        pack.put_l2(mm_tn(active_ref[:, cols], dtwo_ref[...]), 0, chunk, width)
        pack.put(mm_tn(n2_ref[...], dh_ref[:, cols]), (4 + chunk) * width)


def decoder_gradients_kernel(shares, sc_ref, n2_ref, active_ref, dh_ref, dtwo_ref, att_ref, done_ref,
                             *refs):
    pack = Packer(sc_ref[2], refs, shares, ORDER_A)
    linear_gradients(pack, n2_ref, active_ref, dh_ref, dtwo_ref)
    pack.put(mm_tn(att_ref[...], done_ref[...]), 8 * n2_ref.shape[1])


def encoder_gradients_kernel(shares, sc_ref, n2_ref, active_ref, dh_ref, dtwo_ref, att_ref, done_ref,
                             win_ref, dred_ref, red_ref, dlat_ref, *refs):
    width = n2_ref.shape[1]
    half = len(refs) // 2
    linear_gradients(
        Packer(sc_ref[2], refs[:half], shares, ORDER_C_ONE), n2_ref, active_ref, dh_ref, dtwo_ref
    )
    pack = Packer(sc_ref[2], refs[half:], shares, ORDER_C_TWO)
    d_reduced = dred_ref[...]
    for tap in range(4):
        pack.put(mm_tn(win_ref[tap], d_reduced), tap * width)
    pack.put(mm_tn(att_ref[EXTRA:, :], done_ref[...]), 4 * width)
    pack.put(mm_tn(red_ref[...], dlat_ref[...]), 5 * width)


def layer_input_gradient(base, dq_ref, dk_ref, dv_ref, dkv_ref, x, gmid_ref,
                         w_in, vec_ref, cos_ref, sin_ref, dmix_ref, vg_ref):
    frames, width = dq_ref.shape
    later = frames - HALO
    cos, sin = cos_ref[HALO:], -sin_ref[HALO:]
    for at in range(0, width, 128):
        cols = slice(at, at + 128)
        dmix_ref[:, cols] = rotate(dq_ref[:, cols], cos, sin).astype(bf16)
        keys = dk_ref[:, cols]
        keys = jnp.concatenate([keys[:later], keys[later:] + dkv_ref[:, cols].astype(f32)], 0)
        dmix_ref[:, width + at : width + at + 128] = rotate(keys, cos, sin).astype(bf16)
        values = dv_ref[:, cols]
        moved = dkv_ref[:, width + at : width + at + 128].astype(f32)
        values = jnp.concatenate([values[:later], values[later:] + moved], 0)
        dmix_ref[:, 2 * width + at : 2 * width + at + 128] = values.astype(bf16)
    d_normed = mm_nt(dmix_ref[...], w_in[...])
    normal, scaled = normalize(x)
    vg_ref[0:1, :] = column_sum(d_normed * normal)
    vg_ref[1:2, :] = column_sum(d_normed)
    return gmid_ref[...] + norm_backward(d_normed, normal, scaled, vec_ref[base : base + 1])


def decoder_back_kernel(at, sc_ref, *refs):
    pieces, refs = refs[:PIECES], refs[PIECES:]
    (dq_ref, dk_ref, dv_ref, dkv_ref, x_ref, gmid_ref, vec_ref, cos_ref, sin_ref,
     dup_ref, dmix_ref, vg_ref, w_vmem, sems) = refs
    wait_all(fetch(sc_ref, pieces, at, w_vmem.shape[1], w_vmem, sems))
    grad = layer_input_gradient(
        8, dq_ref, dk_ref, dv_ref, dkv_ref, x_ref[...], gmid_ref, w_vmem, vec_ref,
        cos_ref, sin_ref, dmix_ref, vg_ref,
    )
    vg_ref[2:3, :] = column_sum(grad)
    dup_ref[...] = grad.astype(bf16)


def encoder_back_kernel(shares, sc_ref, *refs):
    (pieces,), refs = split_refs(refs, (PIECES,))
    (dq_ref, dk_ref, dv_ref, dkv_ref, x_ref, gmid_ref, vec_ref, cos_ref, sin_ref, n1_ref,
     vgs_ref, grad_ref, *rest) = refs
    refs, (w_vmem, dmix_scr, vg_scr, all_scr, sems) = rest[:-5], rest[-5:]
    width = x_ref.shape[1]
    wait_all(fetch(sc_ref, pieces, 0, w_vmem.shape[1], w_vmem, sems))
    grad = layer_input_gradient(
        0, dq_ref, dk_ref, dv_ref, dkv_ref, x_ref[...].astype(f32), gmid_ref, w_vmem,
        vec_ref, cos_ref, sin_ref, dmix_scr, vg_scr,
    )
    grad_ref[...] = grad.astype(bf16)
    pack = Packer(sc_ref[2], refs, shares, ORDER_D)
    for part in range(3):
        cols = slice(part * width, (part + 1) * width)
        pack.put(mm_tn(n1_ref[...], dmix_scr[:, cols]), part * width)
    all_scr[...] = jnp.zeros_like(all_scr)
    all_scr[0:2, :] = vg_scr[0:2, :]
    all_scr[2:6, :] = vgs_ref[0:4, :]
    all_scr[6:7, :] = vgs_ref[16:17, :]
    all_scr[7:8, :] = vgs_ref[26:27, :]
    all_scr[8:10, :] = vgs_ref[24:26, :]
    all_scr[10:14, :] = vgs_ref[8:12, :]
    pack.put(all_scr[...].T, 3 * width)


def middle_kernel(shares, sc_ref, *refs):
    (pieces, more), refs = split_refs(refs, (PIECES, PIECES))
    (dup_ref, next_ref, dmix_ref, n1_ref, restored_ref, qz_ref,
     denc_ref, dred_ref, dlat_ref, vg_ref, *rest) = refs
    refs, (up_vmem, down_vmem, frame_scr, sems) = rest[:-4], rest[-4:]
    frames, width = dup_ref.shape
    latent = qz_ref.shape[1]
    codec = frames // 2
    copies = [
        fetch(sc_ref, pieces, 0, latent + 4 * width, up_vmem, sems),
        fetch(sc_ref, more, 4 * width, 4 * width + latent, down_vmem, sems, PIECES),
    ]
    pairs = codec + 16
    even, odd = split_rows(
        jnp.concatenate([dup_ref[...], next_ref[...]], 0).astype(f32), frame_scr
    )
    both = jnp.concatenate([even, odd], 1).astype(bf16)
    wait_all(copies[0])
    up = up_vmem[:, latent : latent + 4 * width]
    here = mm_nt(both, up[:, : 2 * width])
    later = mm_nt(both, up[:, 2 * width :])
    d_restored = (here + pltpu.roll(later, pairs - 1, 0)).astype(bf16)
    d_latent = mm(d_restored, up_vmem[:, :latent]).astype(bf16)
    wait_all(copies[1])
    d_reduced = mm_nt(d_latent, down_vmem[:, 4 * width :]).astype(bf16)
    dlat_ref[...] = d_latent[:codec]
    dred_ref[...] = d_reduced[:codec]
    vg_ref[0:1, :] = column_sum(d_reduced[:codec].astype(f32))
    taps = [mm_nt(d_reduced, down_vmem[:, tap * width : (tap + 1) * width]) for tap in range(4)]
    denc_ref[...] = interleave(
        taps[2] + pltpu.roll(taps[0], pairs - 1, 0),
        taps[3] + pltpu.roll(taps[1], pairs - 1, 0),
        frame_scr,
    )[:frames]

    pack = Packer(sc_ref[2], refs, shares, ORDER_B)
    for part in range(3):
        cols = slice(part * width, (part + 1) * width)
        pack.put(mm_tn(n1_ref[...], dmix_ref[:, cols]), part * width)
    restored = restored_ref[...]
    own_pairs = both[:codec]
    before = pltpu.roll(restored.astype(f32), 1, 0)[16:].astype(bf16)
    pack.put(mm_tn(restored[16:], own_pairs[:, :width]), 3 * width)
    pack.put(mm_tn(restored[16:], own_pairs[:, width:]), 4 * width)
    pack.put(mm_tn(before, own_pairs[:, :width]), 5 * width)
    pack.put(mm_tn(before, own_pairs[:, width:]), 6 * width)
    pack.put(mm_tn(d_restored[:codec], qz_ref[CODE_HALO:, :]), 7 * width)


def latent_kernel(sc_ref, *refs):
    (pieces,), refs = split_refs(refs, (PIECES,))
    (enc_ref, rows_ref, vec_ref, res_ref, win_ref, red_ref, w_vmem, frame_scr, sems) = refs
    total, width = enc_ref.shape
    copies = fetch(sc_ref, pieces, 4 * width, w_vmem.shape[1], w_vmem, sems)
    inside = (sc_ref[0] > 0).astype(f32)
    rim = enc_ref[:EXTRA].astype(f32) * inside
    skip = EXTRA // 2
    even, odd = split_rows(jnp.concatenate([rim, enc_ref[EXTRA:].astype(f32)], 0), frame_scr)
    win_ref[0] = pltpu.roll(even, 1, 0)[skip:].astype(bf16)
    win_ref[1] = pltpu.roll(odd, 1, 0)[skip:].astype(bf16)
    win_ref[2] = even[skip:].astype(bf16)
    win_ref[3] = odd[skip:].astype(bf16)
    wait_all(copies)
    reduced = vec_ref[6:7]
    for tap in range(4):
        reduced = reduced + mm(win_ref[tap], w_vmem[:, tap * width : (tap + 1) * width])
    reduced = reduced.astype(bf16)
    red_ref[...] = reduced
    remaining = mm(reduced, w_vmem[:, 4 * width :])
    for level in range(rows_ref.shape[0]):
        res_ref[level] = remaining.astype(bf16)
        remaining = remaining - rows_ref[level].astype(f32)


def lookup_kernel(sc_ref, codes_ref, book_ref, qsend_ref, qkeep_ref, rsend_ref, rkeep_ref, q_scr):
    levels, share, latent = book_ref.shape
    total = codes_ref.shape[0]
    codec = total // 4
    base = sc_ref[3]
    core = sc_ref[2]
    entry = lax.broadcasted_iota(jnp.int32, (1, share), 1)
    for level in range(levels):
        picks = (codes_ref[:, level : level + 1] - base == entry).astype(f32).astype(bf16)
        found = mm(picks, book_ref[level])
        q_scr[CODE_HALO:] = found if level == 0 else q_scr[CODE_HALO:] + found
        for x in range(2):
            even = found[(2 * x) * codec :][:codec]
            odd = found[(2 * x + 1) * codec :][:codec]
            rkeep_ref[x, level] = jnp.where(core == 0, even, odd).astype(bf16)
            rsend_ref[x, level] = jnp.where(core == 0, odd, even).astype(bf16)
    q_scr[:CODE_HALO] = jnp.zeros((CODE_HALO, latent), f32)
    for x in range(2):
        even = q_scr[(2 * x) * codec : (2 * x + 1) * codec + CODE_HALO]
        odd = q_scr[(2 * x + 1) * codec : (2 * x + 2) * codec + CODE_HALO]
        qkeep_ref[x] = jnp.where(core == 0, even, odd)
        qsend_ref[x] = jnp.where(core == 0, odd, even)


def collect_kernel(share, seq_count, sc_ref, own_ref, x_ref, core_ref, far_ref, codes_ref,
                   marked_ref, send_ref, keep_ref, row_scr, cnt_scr):
    levels, codec, latent = own_ref.shape
    total = codes_ref.shape[1]
    lo = sc_ref[4]
    high = send_ref.shape[0]
    frame = lax.broadcasted_iota(jnp.int32, (1, total), 1) + sc_ref[6]
    row = lax.broadcasted_iota(jnp.int32, (2 * high * share, 1), 0)
    entry = (row // share * seq_count + sc_ref[5]) * share + row % share
    ones = jnp.ones((16, total), bf16)
    for level in range(levels):
        marked = marked_ref[:, level : level + 1]
        used = (entry == codes_ref[level : level + 1, :]).astype(f32)
        placed = (marked // 2 == frame).astype(f32)
        select = jnp.where(marked % 2 == 1, placed, used).astype(bf16)
        for place, ref in enumerate((own_ref, x_ref, core_ref, far_ref)):
            at_row = pl.multiple_of(sc_ref[14 + place], 32)
            row_scr[pl.ds(at_row, codec), :] = ref[level]
        sums = mm(select, row_scr[...])
        cnt_scr[level : level + 1, :] = mm_nt(ones, used.astype(bf16))[0:1]
        at = slice(level * share, (level + 1) * share)
        for h in range(high):
            even = sums[(2 * h) * share :][:share]
            odd = sums[(2 * h + 1) * share :][:share]
            keep_ref[h, at, :] = jnp.where(lo == 0, even, odd).astype(bf16)
            send_ref[h, at, :] = jnp.where(lo == 0, odd, even).astype(bf16)
    counts = cnt_scr[...]
    upper = jnp.floor(counts * (1.0 / 128.0))
    digits = jnp.concatenate([upper, counts - 128.0 * upper], 0)
    tail = slice(levels * share, levels * share + 2 * levels)
    for h in range(high):
        even = digits[:, (2 * h) * share : (2 * h + 1) * share]
        odd = digits[:, (2 * h + 1) * share : (2 * h + 2) * share]
        keep_ref[h, tail, :] = jnp.zeros((2 * levels, latent), bf16)
        send_ref[h, tail, :] = jnp.zeros((2 * levels, latent), bf16)
        keep_ref[h, tail, :share] = jnp.where(lo == 0, even, odd).astype(bf16)
        send_ref[h, tail, :share] = jnp.where(lo == 0, odd, even).astype(bf16)


def call(kernel, outs, spaces, scratch, args, micros):
    where = {"s": pltpu.SMEM, "v": pltpu.VMEM, "h": pltpu.HBM}
    title = getattr(kernel, "func", kernel).__name__
    return pl.pallas_call(
        kernel,
        name=title,
        out_shape=outs,
        in_specs=[pl.BlockSpec(memory_space=where[space]) for space in spaces],
        out_specs=[pl.BlockSpec(memory_space=pltpu.VMEM) for _ in outs],
        scratch_shapes=scratch,
        compiler_params=pltpu.CompilerParams(vmem_limit_bytes=VMEM_LIMIT),
        cost_estimate=pl.CostEstimate(
            flops=int(micros * 1e6), bytes_accessed=1, transcendentals=0
        ),
    )(*args)


def shape(dims, dtype=f32):
    return jax.ShapeDtypeStruct(dims, dtype)


def pick(block, at):
    zero = jnp.zeros((), jnp.uint32)
    start = (at,) + (zero,) * (block.ndim - 1)
    return lax.dynamic_slice(block, start, (1,) + block.shape[1:])[0]


def halve(block, axis, index, after=None):
    sent = pick(block, index["other " + axis])
    kept = pick(block, index[axis])
    got = lax.ppermute(sent, axis, [(0, 1), (1, 0)])
    if after is not None:
        got, _ = tie(got, after)
    return (kept.astype(f32) + got.astype(f32)).astype(block.dtype)


def sum_by_permutes(block, index, after=None):
    count = block.shape[0]
    if count != 4:
        return sum_over_hi(block)
    total = pick(block, index["hi"]).astype(f32)
    for turn in range(1, count):
        sent = pick(block, index["hi ^ %d" % turn])
        got = lax.ppermute(sent, "hi", [(i, i ^ turn) for i in range(count)])
        if after is not None:
            got, _ = tie(got, after)
        total = total + got.astype(f32)
    return total


def swap_add(send, keep, axis, after=None):
    got = lax.ppermute(send, axis, [(0, 1), (1, 0)])
    if after is not None:
        got, _ = tie(got, after)
    return (keep.astype(f32) + got.astype(f32)).astype(keep.dtype)


def sum_over_hi(block):
    parts = lax.all_to_all(block, "hi", 0, 0, tiled=True)
    return jnp.sum(parts.astype(f32), 0)


def shifted(block, distance):
    devices = range(lax.axis_size(SEQ))
    route = [(i - distance, i) for i in devices if i - distance in devices]
    return lax.ppermute(block, SEQ, route)


def packed_outs(width_total, width, shares):
    if width // shares % 16 == 0:
        return [shape((width // 2, width_total), bf16)] * 2
    return [shape((width, width_total), bf16)]


def swap(block, axis):
    return lax.ppermute(block, axis, [(0, 1), (1, 0)])


def tie(*values):
    return lax.optimization_barrier(values)


def half_of(share, index):
    rows = share.shape[0] // 2
    zero = jnp.zeros((), jnp.uint32)
    return lax.dynamic_slice(share, (index["lo"] * rows, zero), (rows, share.shape[1]))


def unfolded_rows(block, shares, l2_at):
    width = block.shape[0]
    full = [block[:, l2_at + i * width : l2_at + (i + 1) * width] for i in range(4)]
    full = jnp.concatenate(full, 0).reshape(shares, 4, width // shares, width)
    full = full.transpose(0, 2, 1, 3).reshape(width, 4 * width)
    return jnp.concatenate([block[:, :l2_at], full, block[:, l2_at + 4 * width :]], 1)


def first_sum(parts, shares, order, index, l2_at=None):
    if len(parts) == 2:
        return swap_add(*parts, "core")
    (block,) = parts
    if l2_at is not None:
        block = unfolded_rows(block, shares, l2_at)
    width, total = block.shape
    block = block.reshape(shares // 8, 2, 2, 2, width // shares, total)
    block = halve(block.transpose(3, 0, 1, 2, 4, 5), "core", index)
    places = [("hi", "lo", "x").index(axis) for axis in order]
    return block.transpose(*places, 3, 4).reshape(width // 2, total)


def next_sum(block, axis, index, after=None):
    rows, total = block.shape
    return halve(block.reshape(2, rows // 2, total), axis, index, after)


def last_sum(block, high):
    return sum_over_hi(block.reshape(high, -1, block.shape[1]))


def local(
    activations,
    encoder_attention_norm_gain,
    encoder_attention_norm_bias,
    encoder_query_key_value_weight,
    encoder_attention_output_weight,
    encoder_attention_layer_scale,
    encoder_forward_norm_gain,
    encoder_forward_norm_bias,
    encoder_forward_input_weight,
    encoder_forward_output_weight,
    encoder_forward_layer_scale,
    strided_convolution_weight,
    strided_convolution_bias,
    quantizer_input_weight,
    codebook,
    quantizer_output_weight,
    transposed_convolution_weight,
    transposed_convolution_bias,
    decoder_attention_norm_gain,
    decoder_attention_norm_bias,
    decoder_query_key_value_weight,
    decoder_attention_output_weight,
    decoder_attention_layer_scale,
    decoder_forward_norm_gain,
    decoder_forward_norm_bias,
    decoder_forward_input_weight,
    decoder_forward_output_weight,
    decoder_forward_layer_scale,
    cotangent,
    frame_segment_index,
    frame_code_index,
    replace_code_mask,
    replacing_batch_position,
    code_usage_average,
    code_latent_sum_average,
):
    batch_rows, frames, width = activations.shape
    assert batch_rows == 1
    seq_index = lax.axis_index(SEQ)
    seq_count = lax.axis_size(SEQ)
    dp_index = lax.axis_index(DP)
    dp_count = lax.axis_size(DP)
    shares = dp_count * seq_count
    codec = frames // 2
    levels = frame_code_index.shape[2]
    latent = codebook.shape[2]
    book_share = codebook.shape[1]
    core_index = lax.axis_index("core")

    x_index, lo_index = lax.axis_index("x"), lax.axis_index("lo")
    rows_share = width // seq_count
    high = shares // 8
    total_frames = HALO + frames
    code_total = replace_code_mask.shape[1]
    code_share = code_usage_average.shape[1]
    row_frames = codec * seq_count

    vectors = jnp.stack(
        [
            encoder_attention_norm_gain,
            encoder_attention_norm_bias,
            encoder_attention_layer_scale,
            encoder_forward_norm_gain,
            encoder_forward_norm_bias,
            encoder_forward_layer_scale,
            strided_convolution_bias,
            transposed_convolution_bias,
            decoder_attention_norm_gain,
            decoder_attention_norm_bias,
            decoder_attention_layer_scale,
            decoder_forward_norm_gain,
            decoder_forward_norm_bias,
            decoder_forward_layer_scale,
        ]
    )
    vectors = jnp.pad(vectors, ((0, 2), (0, 0)))
    small = jnp.concatenate(
        [frame_code_index.reshape(-1).astype(f32), vectors.reshape(-1).astype(f32)]
    )
    index = {}
    unsigned = jnp.uint32
    for axis in ("x", "lo", "core"):
        index[axis] = lax.axis_index(axis).astype(unsigned)
        index["other " + axis] = (1 - lax.axis_index(axis)).astype(unsigned)
    index["hi"] = lax.axis_index("hi").astype(unsigned)
    index["seq"] = lax.axis_index(SEQ).astype(unsigned)
    index["owner"] = (lax.axis_index(DP + SEQ) * code_share).astype(unsigned)
    for turn in range(1, 4):
        index["hi ^ %d" % turn] = lax.axis_index("hi").astype(unsigned) ^ unsigned(turn)
    def flat_taps(taps):
        return taps.transpose(1, 0, 2).reshape(taps.shape[1], -1)

    def fold_l2(share):
        return share.reshape(4, -1, width).transpose(1, 0, 2).reshape(-1, 4 * width)

    dec_one = jnp.concatenate(
        [
            quantizer_output_weight.T,
            flat_taps(transposed_convolution_weight),
            decoder_query_key_value_weight,
        ],
        1,
    )
    half_one = half_of(dec_one, index)
    small, half_one = tie(small, half_one)
    small = lax.all_gather(small, SEQ, axis=0, tiled=False)
    names = sorted(index)
    *index_values, small = tie(*[index[name] for name in names], small)
    index = dict(zip(names, index_values))
    code_count = codec * levels
    row_codes = small[:, :code_count].astype(jnp.int32).reshape(seq_count, codec, levels)
    vectors = small[:, code_count:].reshape(seq_count, 16, -1).transpose(1, 0, 2).reshape(16, width)
    order = [2 * x_index + core_index, 2 * (1 - x_index) + core_index]
    order += [2 * x_index + 1 - core_index, 2 * (1 - x_index) + 1 - core_index]
    cut = jnp.sum((frame_segment_index[0] == 0).astype(jnp.int32))
    scalars = jnp.stack(
        [
            seq_index * frames,
            cut,
            core_index,
            seq_index * book_share,
            lo_index,
            seq_index,
            dp_index * row_frames,
            seq_index,
        ]
        + [
            order[0] * rows_share,
            order[1] * rows_share + lo_index * (rows_share // 2),
            order[1] * rows_share + (1 - lo_index) * (rows_share // 2),
            order[2] * rows_share,
            order[3] * rows_share + lo_index * (rows_share // 2),
            order[3] * rows_share + (1 - lo_index) * (rows_share // 2),
        ]
        + [place * codec for place in order]
    ).astype(jnp.int32)

    half_one, _ = tie(half_one, small)
    near_one = swap(half_one, "x")
    activation_halo = shifted(activations[0, frames - HALO :], 1)

    positions = seq_index * frames - HALO + jnp.arange(total_frames, dtype=jnp.int32)
    half_dim = HEAD_DIM // 2
    frequency = jnp.power(10000.0, -jnp.arange(half_dim, dtype=f32) / half_dim)

    def angle_tables(positions):
        angles = positions.astype(f32)[:, None] * frequency[None, :]
        cos, sin = jnp.cos(angles), jnp.sin(angles)
        return jnp.concatenate([cos] * 4, 1), jnp.concatenate([-sin, sin, -sin, sin], 1)

    window = codec + CODE_HALO
    qsend, qkeep, rsend, rkeep = call(
        lookup_kernel,
        [shape((2, window, latent))] * 2 + [shape((2, levels, codec, latent), bf16)] * 2,
        "svv",
        [pltpu.VMEM((CODE_HALO + codec * seq_count, latent), f32)],
        (scalars, row_codes.reshape(-1, levels), codebook),
        4,
    )
    q_sum = swap_add(qsend, qkeep, "core")
    code_rows = swap_add(rsend, rkeep, "core")
    q_sent = pick(q_sum, index["other x"])
    q_got = swap(q_sent, "x")
    (near_one, positions, dec_l2, enc_in, enc_l2, down_share, replace_code_mask,
     replacing_batch_position, row_codes, _) = tie(
        near_one, positions, decoder_forward_output_weight, encoder_query_key_value_weight,
        encoder_forward_output_weight, strided_convolution_weight, replace_code_mask,
        replacing_batch_position, row_codes, q_sent,
    )
    dec_two = jnp.concatenate(
        [decoder_attention_output_weight, decoder_forward_input_weight, fold_l2(dec_l2)], 1
    )
    enc_one = jnp.concatenate(
        [
            enc_in,
            encoder_attention_output_weight,
            flat_taps(down_share),
            quantizer_input_weight,
        ],
        1,
    )
    enc_two = jnp.concatenate([encoder_forward_input_weight, fold_l2(enc_l2)], 1)
    marked = (replacing_batch_position * 2 + replace_code_mask).T
    marked = marked.reshape(dp_count, seq_count, code_share, levels).transpose(1, 0, 2, 3)
    marked = pick(marked, index["seq"]).reshape(dp_count * code_share, levels)
    code_columns = row_codes.reshape(row_frames, levels).T
    owner_flag = lax.dynamic_slice(
        replace_code_mask, (jnp.zeros((), unsigned), index["owner"]), (levels, code_share)
    ) == 1
    far_one = swap(near_one, "lo")
    dec_one = [dec_one, near_one, far_one, swap(dec_one, "core"), swap(near_one, "core"),
               swap(far_one, "core")]
    half_two = half_of(dec_two, index)
    cos_table, sin_table = angle_tables(positions)
    near_two = swap(half_two, "x")
    quantized = (pick(q_sum, index["x"]) + q_got).astype(bf16)
    half_three, half_four = half_of(enc_one, index), half_of(enc_two, index)
    (quantized, near_two, half_three, half_four, activation_halo, cos_table, sin_table, marked,
     code_columns, owner_flag, code_rows) = tie(
        quantized, near_two, half_three, half_four, activation_halo, cos_table, sin_table, marked,
        code_columns, owner_flag, code_rows,
    )
    far_two = swap(near_two, "lo")
    near_three = swap(half_three, "x")

    d_x, restored, d_n1, d_q, d_k, d_v, d_att = call(
        decoder_front_kernel,
        [
            shape((frames, width)),
            shape((codec + 16, width), bf16),
            shape((frames, width), bf16),
            shape((frames, width), bf16),
            shape((total_frames, width), bf16),
            shape((total_frames, width), bf16),
            shape((frames, width), bf16),
        ],
        "s" + "h" * PIECES + "vvvv",
        [
            pltpu.VMEM((width, latent + 7 * width), bf16),
            pltpu.VMEM((width // 128, total_frames, 128), f32),
            pltpu.SemaphoreType.DMA((PIECES,)),
        ],
        (scalars, *dec_one, quantized, vectors, cos_table, sin_table),
        8,
    )
    d_att, far_two, near_three, half_four = tie(d_att, far_two, near_three, half_four)
    dec_two = [dec_two, near_two, far_two, swap(dec_two, "core"), swap(near_two, "core"),
               swap(far_two, "core")]
    far_three = swap(near_three, "lo")
    near_four = swap(half_four, "x")
    layer_scratch = [
        pltpu.VMEM((frames, width), bf16),
        pltpu.VMEM((total_frames, width), f32),
        pltpu.VMEM((total_frames, width), f32),
        pltpu.SemaphoreType.DMA((3 * PIECES,)),
    ]
    forward_outs = [shape((frames, width), bf16), shape((frames, 4 * width), bf16)]
    kept_outs = [shape((frames, 4 * width)), shape((frames, width)), shape((frames, width))]
    backward_outs = [
        shape((frames, width)),
        shape((frames, 4 * width), bf16),
        shape((frames, width), bf16),
        shape((frames, width), bf16),
        shape((8, width)),
        shape((frames, width)),
        shape((frames, width)),
        shape((frames, width)),
        shape((HALO, 2 * width), bf16),
    ]
    weights_scratch = pltpu.VMEM((width, 9 * width), bf16)
    (output, d_n2, d_active, d_gmid, d_dh, d_dtwo, d_done, d_vg_two, d_dq, d_dk, d_dv, d_dkv) = call(
        partial(decoder_layer_kernel, ((0, 0), (0, width), (0, 5 * width))),
        [shape((frames, width), bf16)] + forward_outs + backward_outs,
        "s" + "h" * PIECES + "vvvvvvv",
        [
            weights_scratch,
            pltpu.VMEM((frames, width), f32),
            pltpu.VMEM((frames, 4 * width), bf16),
            pltpu.VMEM((frames, 4 * width), f32),
            pltpu.VMEM((frames, width), f32),
            pltpu.VMEM((frames, width), f32),
        ]
        + layer_scratch,
        (scalars, *dec_two, d_att, d_x, cotangent[0], vectors, d_q, d_k, d_v),
        14,
    )
    d_n2, far_three, near_four = tie(d_n2, far_three, near_four)
    enc_one = [enc_one, near_three, far_three, swap(enc_one, "core"), swap(near_three, "core"),
               swap(far_three, "core")]
    far_four = swap(near_four, "lo")
    d_dkv = shifted(d_dkv, -1)
    group_a = call(
        partial(decoder_gradients_kernel, shares),
        packed_outs(9 * width, width, shares),
        "svvvvvv",
        [],
        (scalars, d_n2, d_active, d_dh, d_dtwo, d_att, d_done),
        5,
    )
    d_dq, *group_a = tie(d_dq, *group_a)
    a_sum = first_sum(group_a, shares, ORDER_A, index, 0)
    d_up, d_mixed, d_vg_one = call(
        partial(decoder_back_kernel, latent + 4 * width),
        [shape((frames, width), bf16), shape((frames, 3 * width), bf16), shape((8, width))],
        "s" + "h" * PIECES + "v" * 9,
        [pltpu.VMEM((width, 3 * width), bf16), pltpu.SemaphoreType.DMA((PIECES,))],
        (
            scalars, *dec_one, d_dq, d_dk, d_dv, d_dkv, d_x, d_gmid, vectors, cos_table,
            sin_table,
        ),
        4,
    )
    d_up_next = shifted(d_up[:32], -1)

    code_rows, d_dkv = tie(code_rows, d_dkv)
    code_rows = halve(code_rows, "x", index)

    a_sum, d_up, e_input, far_four = tie(a_sum, d_up, activations[0], far_four)
    enc_two = [enc_two, near_four, far_four, swap(enc_two, "core"), swap(near_four, "core"),
               swap(far_four, "core")]
    a_sum = next_sum(a_sum, ORDER_A[0], index)
    e_n1, e_q, e_k, e_v, e_att = call(
        encoder_front_kernel,
        [
            shape((frames, width), bf16),
            shape((frames + EXTRA, width), bf16),
            shape((total_frames, width), bf16),
            shape((total_frames, width), bf16),
            shape((frames + EXTRA, width), bf16),
        ],
        "s" + "h" * PIECES + "vvvvv",
        [pltpu.VMEM((width, 3 * width), bf16), pltpu.SemaphoreType.DMA((PIECES,))],
        (scalars, *enc_one, activation_halo, e_input, vectors, cos_table, sin_table),
        7,
    )

    d_mixed, e_n1 = tie(d_mixed, e_n1)
    middle_outs = call(
        partial(middle_kernel, shares),
        [
            shape((frames, width)),
            shape((codec, width), bf16),
            shape((codec, latent), bf16),
            shape((8, width)),
        ]
        + packed_outs(7 * width + latent, width, shares),
        "s" + "h" * (2 * PIECES) + "" + "v" * 6,
        [
            pltpu.VMEM((width, latent + 4 * width), bf16),
            pltpu.VMEM((width, latent + 4 * width), bf16),
            pltpu.VMEM((width // 128, frames + 32, 128), f32),
            pltpu.SemaphoreType.DMA((2 * PIECES,)),
        ],
        (scalars, *dec_one, *enc_one, d_up, d_up_next, d_mixed, d_n1, restored, quantized),
        7,
    )
    d_encoded, d_reduced, d_latent, m_vg = middle_outs[:4]
    b_sum = first_sum(middle_outs[4:], shares, ORDER_B, index)

    e_att, d_encoded = tie(e_att, d_encoded)
    enc_plan = ((0, 3 * width), (1, 0), (1, 4 * width))
    rows = frames + EXTRA
    encoded, e_n2, e_active, e_slope, e_mid, e_second = call(
        partial(encoder_forward_kernel, enc_plan),
        [shape((rows, width), bf16)] + forward_outs + kept_outs,
        "s" + "h" * (2 * PIECES) + "vvvv",
        [
            weights_scratch,
            pltpu.VMEM((rows, width), f32),
            pltpu.VMEM((rows, 4 * width), bf16),
            pltpu.SemaphoreType.DMA((3 * PIECES,)),
        ],
        (scalars, *enc_one, *enc_two, activation_halo, e_input, e_att, vectors),
        6,
    )
    encoded, b_sum = tie(encoded, b_sum)
    b_sum = next_sum(b_sum, ORDER_B[0], index)
    residuals, windows, reduced = call(
        latent_kernel,
        [
            shape((levels, codec, latent), bf16),
            shape((4, codec, width), bf16),
            shape((codec, width), bf16),
        ],
        "s" + "h" * PIECES + "vvv",
        [
            pltpu.VMEM((width, 4 * width + latent), bf16),
            pltpu.VMEM((width // 128, frames + EXTRA, 128), f32),
            pltpu.SemaphoreType.DMA((PIECES,)),
        ],
        (scalars, *enc_one, encoded, code_rows, vectors),
        3,
    )
    near_res = swap(residuals, "x")
    res_pieces = [residuals, near_res, swap(residuals, "core"), swap(near_res, "core")]

    d_encoded, a_sum, _ = tie(d_encoded, a_sum, residuals)
    a_sum = next_sum(a_sum, ORDER_A[1], index)
    (e_gmid, e_dh, e_dtwo, e_done, e_vg_two, e_dq, e_dk, e_dv, e_dkv) = call(
        partial(encoder_backward_kernel, enc_plan),
        backward_outs,
        "s" + "h" * (2 * PIECES) + "v" * 9,
        [weights_scratch] + layer_scratch,
        (
            scalars, *enc_one, *enc_two, e_att, d_encoded, vectors, e_slope, e_mid, e_second,
            e_q, e_k, e_v,
        ),
        11,
    )
    e_dkv = shifted(e_dkv, -1)
    if code_share % 16 == 0:
        tail_rows = levels * code_share
        csend, ckeep = call(
            partial(collect_kernel, code_share, seq_count),
            [shape((dp_count // 2, tail_rows + 2 * levels, latent), bf16)] * 2,
            "svvvvvv",
            [
                pltpu.VMEM((row_frames, latent), bf16),
                pltpu.VMEM((levels, dp_count * code_share), f32),
            ],
            (scalars, *res_pieces, code_columns, marked),
            5,
        )
        e_n2, csend, e_gmid = tie(e_n2, csend, e_gmid)
    c_outs = packed_outs(8 * width, width, shares)
    group_c = call(
        partial(encoder_gradients_kernel, shares),
        c_outs + packed_outs(5 * width + latent, width, shares),
        "s" + "v" * 10,
        [],
        (
            scalars, e_n2, e_active, e_dh, e_dtwo, e_att, e_done, windows, d_reduced, reduced,
            d_latent,
        ),
        5,
    )
    e_dq, *group_c = tie(e_dq, *group_c)
    c_one = first_sum(group_c[: len(c_outs)], shares, ORDER_C_ONE, index, 0)
    c_two = first_sum(group_c[len(c_outs) :], shares, ORDER_C_TWO, index)
    e_dq, c_one, c_two, a_sum, b_sum = tie(e_dq, c_one, c_two, a_sum, b_sum)
    vector_grads = jnp.concatenate([e_vg_two, d_vg_two, m_vg, d_vg_one], 0)
    grad_outs = call(
        partial(encoder_back_kernel, shares),
        [shape((frames, width), bf16)] + packed_outs(3 * width + 128, width, shares),
        "s" + "h" * PIECES + "v" * 11,
        [
            pltpu.VMEM((width, 3 * width), bf16),
            pltpu.VMEM((frames, 3 * width), bf16),
            pltpu.VMEM((8, width), f32),
            pltpu.VMEM((128, width), f32),
            pltpu.SemaphoreType.DMA((PIECES,)),
        ],
        (
            scalars, *enc_one, e_dq, e_dk, e_dv, e_dkv, e_input, e_gmid, vectors,
            cos_table, sin_table, e_n1, vector_grads,
        ),
        5,
    )
    activations_grad = grad_outs[0]

    def z_sum(block):
        return sum_by_permutes(block.reshape(high, -1, block.shape[1]), index, activations_grad)

    grads_a = z_sum(a_sum)
    d_sum = first_sum(grad_outs[1:], shares, ORDER_D, index)
    b_sum = next_sum(b_sum, ORDER_B[1], index, d_sum)
    if code_share % 16 == 0:
        combined = swap_add(csend, ckeep, "lo", b_sum)
        c_two = next_sum(c_two, ORDER_C_TWO[0], index, combined)
        combined = sum_by_permutes(combined, index)
        summed = combined[:tail_rows].reshape(levels, code_share, latent)
        digits = combined[tail_rows:, :code_share]
        counted = 128.0 * digits[:levels] + digits[levels:]
    else:
        entry = (
            jnp.arange(dp_count, dtype=jnp.int32)[:, None] * seq_count + seq_index
        ) * code_share + jnp.arange(code_share, dtype=jnp.int32)
        relative = [place * codec + jnp.arange(codec, dtype=jnp.int32) for place in order]
        relative = jnp.concatenate(relative)
        flat_res = jnp.concatenate(res_pieces, 1)
        used = entry.reshape(1, -1, 1) == code_columns[:, None, relative]
        placed = (marked.T // 2)[:, :, None] == dp_index * row_frames + relative
        counts = jnp.sum(used.astype(f32), 2).reshape(levels, dp_count, code_share)
        selects = jnp.where((marked.T % 2)[:, :, None] == 1, placed, used).astype(bf16)
        sums = jnp.einsum("lct,ltd->lcd", selects, flat_res, preferred_element_type=f32)
        sums = sums.astype(bf16).reshape(levels, dp_count, code_share, latent)
        c_two = next_sum(c_two, ORDER_C_TWO[0], index)
        summed = lax.psum_scatter(sums, DP, scatter_dimension=1, tiled=False).astype(f32)
        counted = lax.psum_scatter(counts, DP, scatter_dimension=1, tiled=False)
    c_one = next_sum(c_one, ORDER_C_ONE[0], index, c_two)
    d_sum = next_sum(d_sum, ORDER_D[0], index, c_one)
    c_two = next_sum(c_two, ORDER_C_TWO[1], index, d_sum)
    grads_b = z_sum(b_sum)
    c_one = next_sum(c_one, ORDER_C_ONE[1], index, c_two)
    d_sum = next_sum(d_sum, ORDER_D[1], index, c_one)
    grads_c_two = z_sum(c_two)
    grads_c = z_sum(c_one)
    grads_d = z_sum(d_sum)

    new_cluster_size = ema_decay * code_usage_average + (1.0 - ema_decay) * counted
    new_embed_sum = jnp.where(
        owner_flag[:, :, None],
        summed * new_cluster_size[:, :, None],
        ema_decay * code_latent_sum_average + (1.0 - ema_decay) * summed,
    )
    new_codebook = new_embed_sum / new_cluster_size[:, :, None]

    def columns(block, at, count):
        return block[:, at * width : (at + count) * width]

    def taps(block):
        return block.reshape(-1, 4, width).transpose(1, 0, 2)

    def unfold(block):
        return block.reshape(-1, 4, width).transpose(1, 0, 2).reshape(-1, width)

    vec = grads_d[:, 3 * width : 3 * width + 16].T
    return (
        output[None],
        activations_grad[None],
        vec[0],
        vec[1],
        columns(grads_d, 0, 3),
        columns(grads_c_two, 4, 1),
        vec[2],
        vec[3],
        vec[4],
        columns(grads_c, 4, 4),
        unfold(columns(grads_c, 0, 4)),
        vec[5],
        taps(columns(grads_c_two, 0, 4)),
        vec[6],
        grads_c_two[:, 5 * width :],
        grads_b[:, 7 * width :].T,
        taps(columns(grads_b, 3, 4)),
        vec[7],
        vec[8],
        vec[9],
        columns(grads_b, 0, 3),
        columns(grads_a, 8, 1),
        vec[10],
        vec[11],
        vec[12],
        columns(grads_a, 4, 4),
        unfold(columns(grads_a, 0, 4)),
        vec[13],
        new_cluster_size,
        new_embed_sum,
        new_codebook,
    )


def solution(mesh):
    grid = mesh.devices
    mesh = jax.sharding.Mesh(
        grid.reshape(grid.shape[0] // 2, 2, grid.shape[1] // 2, 2), ("hi", "lo", "x", "core")
    )
    placed = (
        P(DP, SEQ, None),
        P(SEQ),
        P(SEQ),
        P(SEQ, None),
        P(SEQ, None),
        P(SEQ),
        P(SEQ),
        P(SEQ),
        P(SEQ, None),
        P(SEQ, None),
        P(SEQ),
        P(None, SEQ, None),
        P(SEQ),
        P(SEQ, None),
        P(None, SEQ, None),
        P(None, SEQ),
        P(None, SEQ, None),
        P(SEQ),
        P(SEQ),
        P(SEQ),
        P(SEQ, None),
        P(SEQ, None),
        P(SEQ),
        P(SEQ),
        P(SEQ),
        P(SEQ, None),
        P(SEQ, None),
        P(SEQ),
        P(DP, SEQ, None),
        P(DP, None),
        P(DP, SEQ, None),
        P(),
        P(),
        P(None, DP + SEQ),
        P(None, DP + SEQ, None),
    )
    return jax.shard_map(
        local,
        mesh=mesh,
        in_specs=placed,
        out_specs=(
            P(DP, SEQ, None),
            P(DP, SEQ, None),
            P(DP + SEQ),
            P(DP + SEQ),
            P(DP + SEQ, None),
            P(DP + SEQ, None),
            P(DP + SEQ),
            P(DP + SEQ),
            P(DP + SEQ),
            P(DP + SEQ, None),
            P(DP + SEQ, None),
            P(DP + SEQ),
            P(None, DP + SEQ, None),
            P(DP + SEQ),
            P(DP + SEQ, None),
            P(None, DP + SEQ),
            P(None, DP + SEQ, None),
            P(DP + SEQ),
            P(DP + SEQ),
            P(DP + SEQ),
            P(DP + SEQ, None),
            P(DP + SEQ, None),
            P(DP + SEQ),
            P(DP + SEQ),
            P(DP + SEQ),
            P(DP + SEQ, None),
            P(DP + SEQ, None),
            P(DP + SEQ),
            P(None, DP + SEQ),
            P(None, DP + SEQ, None),
            P(None, DP + SEQ, None),
        ),
        check_vma=False,
    )
```

```python
from functools import partial

import jax
import jax.numpy as jnp
from jax import lax
from jax.experimental import pallas as pl
from jax.experimental.pallas import tpu as pltpu
from jax.sharding import PartitionSpec as P

HEADS = 8
HEAD_DIM = 64
CONTEXT = 250
HALO = 256
CODE_HALO = HALO // 2 + 16
EXTRA = 16
QUERIES = 64
GROUP = 4
WINDOW = HALO + QUERIES
VMEM_LIMIT = 26 * 1024 * 1024
ORDER_A = ("lo", "x", "hi")
ORDER_B = ("lo", "x", "hi")
ORDER_C = ("x", "lo", "hi")
ORDER_D = ("lo", "x", "hi")
DP = ("hi", "lo")
SEQ = ("x", "core")

norm_eps = 1e-05
ema_decay = 0.9
bf16 = jnp.bfloat16
f32 = jnp.float32


PIECES = 4


def fetch(sc_ref, pieces, at, width, dst, sems, first=0):
    copies = []
    for i, piece in enumerate(pieces):
        rows = piece.shape[0]
        row = pl.multiple_of(sc_ref[8 + i], 128)
        copies.append(
            pltpu.make_async_copy(
                piece.at[:, at : at + width], dst.at[pl.ds(row, rows), :], sems.at[first + i]
            )
        )
        copies[-1].start()
    return copies


def split_refs(refs, counts):
    groups = []
    for count in counts:
        groups.append(refs[:count])
        refs = refs[count:]
    return groups, refs


def wait_all(copies):
    for copy in copies:
        copy.wait()


def mm(a, b):
    return jnp.dot(a, b, preferred_element_type=f32)


def mm_nt(a, b):
    return lax.dot_general(a, b, (((1,), (1,)), ((), ())), preferred_element_type=f32)


def mm_tn(a, b):
    return lax.dot_general(a, b, (((0,), (0,)), ((), ())), preferred_element_type=f32)


def normalize(stream):
    center = stream - jnp.mean(stream, -1, keepdims=True)
    scaled = lax.rsqrt(jnp.mean(center * center, -1, keepdims=True) + norm_eps)
    return center * scaled, scaled


def norm_backward(upstream, normal, scaled, gain):
    inner = upstream * gain
    return scaled * (
        inner
        - jnp.mean(inner, -1, keepdims=True)
        - normal * jnp.mean(inner * normal, -1, keepdims=True)
    )


def column_sum(value):
    return jnp.sum(value, 0, keepdims=True)


def interleave(even, odd, scr):
    tiles, rows, _ = scr.shape
    for tile in range(tiles):
        cols = slice(tile * 128, (tile + 1) * 128)
        scr[tile, pl.ds(0, rows // 2, stride=2), :] = even[:, cols]
        scr[tile, pl.ds(1, rows // 2, stride=2), :] = odd[:, cols]
    return jnp.concatenate([scr[tile] for tile in range(tiles)], 1)


def split_rows(value, scr):
    tiles, rows, _ = scr.shape
    for tile in range(tiles):
        scr[tile] = value[:, tile * 128 : (tile + 1) * 128]
    even = [scr[tile, pl.ds(0, rows // 2, stride=2), :] for tile in range(tiles)]
    odd = [scr[tile, pl.ds(1, rows // 2, stride=2), :] for tile in range(tiles)]
    return jnp.concatenate(even, 1), jnp.concatenate(odd, 1)


def first_half():
    lane = lax.broadcasted_iota(jnp.int32, (1, 128), 1)
    return lane % HEAD_DIM < HEAD_DIM // 2


def rotate(tile, cos, sin):
    swapped = jnp.where(first_half(), pltpu.roll(tile, 96, 1), pltpu.roll(tile, 32, 1))
    return tile * cos + swapped * sin


def head_lanes():
    lane = lax.broadcasted_iota(jnp.int32, (1, GROUP * HEAD_DIM), 1) // HEAD_DIM
    return [(lane == head) for head in range(GROUP)]


def stack_heads(block, lanes):
    return jnp.concatenate([block * mask.astype(bf16) for mask in lanes], 0)


def unstack_heads(block, lanes):
    rows = block.shape[0] // GROUP
    out = block[:rows]
    for head in range(1, GROUP):
        out = jnp.where(lanes[head], block[head * rows : (head + 1) * rows], out)
    return out


def lowest_key(query, cut):
    low = jnp.maximum(query - (CONTEXT - 1), 0)
    return jnp.where(query >= cut, jnp.maximum(low, cut), low)


def attend(q_ref, k_ref, v_ref, att_ref, sc_ref, rows, first_query, first_key, keys, at_row):
    start, cut = sc_ref[0], sc_ref[1]
    query = start + first_query + lax.broadcasted_iota(jnp.int32, (rows, 1), 0)
    low = lowest_key(query, cut)
    key = start + first_key + lax.broadcasted_iota(jnp.int32, (rows, keys), 1)
    mask = (key <= query) & (key >= low)
    mask = jnp.concatenate([mask] * GROUP, 0)
    lanes = head_lanes()
    key_row = first_key + HALO
    for group in range(HEADS // GROUP):
        cols = slice(group * GROUP * HEAD_DIM, (group + 1) * GROUP * HEAD_DIM)
        stacked = stack_heads(q_ref[at_row : at_row + rows, cols], lanes)
        scores = mm_nt(stacked, k_ref[key_row : key_row + keys, cols]) * HEAD_DIM ** (-0.5)
        scores = jnp.where(mask, scores, -1e30)
        exponent = jnp.exp(scores - jnp.max(scores, -1, keepdims=True))
        weights = exponent * (1.0 / jnp.sum(exponent, -1, keepdims=True))
        mixed = mm(weights.astype(bf16), v_ref[key_row : key_row + keys, cols])
        att_ref[at_row : at_row + rows, cols] = unstack_heads(mixed, lanes).astype(bf16)


def front(x, vec_ref, base, w_in, cos_ref, sin_ref, sc_ref, n1_ref, q_ref, k_ref, v_ref, att_ref,
          extra):
    width = x.shape[1]
    normal, _ = normalize(x)
    low = (normal * vec_ref[base : base + 1] + vec_ref[base + 1 : base + 2]).astype(bf16)
    n1_ref[...] = low[HALO:]
    skip = HALO - extra
    queries = mm(low[skip:], w_in[:, :width])
    keys = mm(low, w_in[:, width : 2 * width])
    for at in range(0, width, 128):
        q_ref[:, at : at + 128] = rotate(
            queries[:, at : at + 128], cos_ref[skip:], sin_ref[skip:]
        ).astype(bf16)
        k_ref[:, at : at + 128] = rotate(keys[:, at : at + 128], cos_ref[...], sin_ref[...]).astype(
            bf16
        )
    v_ref[...] = mm(low, w_in[:, 2 * width :]).astype(bf16)
    frames = x.shape[0] - HALO
    if extra:
        attend(q_ref, k_ref, v_ref, att_ref, sc_ref, extra, -extra, -HALO, HALO, 0)
    for first in range(0, frames, QUERIES):
        attend(
            q_ref, k_ref, v_ref, att_ref, sc_ref, QUERIES, first, first - HALO, WINDOW,
            extra + first,
        )


def decoder_front_kernel(sc_ref, *refs):
    pieces, refs = refs[:PIECES], refs[PIECES:]
    (qz_ref, vec_ref, cos_ref, sin_ref, x_ref, restored_ref, n1_ref, q_ref, k_ref, v_ref, att_ref,
     w_vmem, x_scr, sems) = refs
    width = x_ref.shape[1]
    wait_all(fetch(sc_ref, pieces, 0, w_vmem.shape[1], w_vmem, sems))
    latent = qz_ref.shape[1]
    restored = mm_nt(qz_ref[...], w_vmem[:, :latent]).astype(bf16)
    restored_ref[...] = restored[CODE_HALO - 16 :]
    both = mm(restored, w_vmem[:, latent : latent + 4 * width])
    bias = vec_ref[7:8]
    now = both[16:, : 2 * width]
    before = pltpu.roll(both[:, 2 * width :], 1, 0)[16:]
    total = now + before
    x = interleave(total[:, :width] + bias, total[:, width:] + bias, x_scr)
    x_ref[...] = x[HALO:]
    w_in = w_vmem.at[:, latent + 4 * width :]
    front(x, vec_ref, 8, w_in, cos_ref, sin_ref, sc_ref, n1_ref, q_ref, k_ref, v_ref,
          att_ref, 0)


def encoder_front_kernel(sc_ref, *refs):
    (pieces,), refs = split_refs(refs, (PIECES,))
    (halo_ref, x_ref, vec_ref, cos_ref, sin_ref, n1_ref, q_ref, k_ref, v_ref, att_ref,
     w_vmem, sems) = refs
    width = x_ref.shape[1]
    copies = fetch(sc_ref, pieces, 0, 3 * width, w_vmem, sems)
    x = jnp.concatenate([halo_ref[...], x_ref[...]], 0).astype(f32)
    wait_all(copies)
    front(x, vec_ref, 0, w_vmem, cos_ref, sin_ref, sc_ref, n1_ref, q_ref, k_ref, v_ref, att_ref,
          EXTRA)


def gelu_both(hidden):
    share = 0.5 * (1.0 + lax.erf(hidden * 0.7071067811865476))
    density = jnp.exp(-0.5 * hidden * hidden) * 0.3989422804014327
    return hidden * share, share + hidden * density


def l2_rows(w, at, chunk, width):
    rows = width // 4
    return jnp.concatenate(
        [
            w[chunk * rows : (chunk + 1) * rows, at + g * width : at + (g + 1) * width]
            for g in range(4)
        ],
        0,
    )


def fetch_layer(sc_ref, groups, plan, width, w_vmem, sems):
    edges = (0, width, 5 * width, 9 * width)
    return [
        fetch(
            sc_ref, groups[plan[i][0]], plan[i][1], high - low, w_vmem.at[:, low:high], sems,
            PIECES * i,
        )
        for i, (low, high) in enumerate(zip(edges[:-1], edges[1:]))
    ]


def ff_forward(base, extra, copies, w_vmem, att_ref, stream, vec_ref, out_ref, n2_ref, active_ref,
               slope_ref, mid_ref, second_ref, h_scr, act_scr):
    rows, width = stream.shape
    scale_one = vec_ref[base + 2 : base + 3]
    gain_two = vec_ref[base + 3 : base + 4]
    bias_two = vec_ref[base + 4 : base + 5]
    scale_two = vec_ref[base + 5 : base + 6]
    wait_all(copies[0])
    middle = stream + scale_one * mm(att_ref[...], w_vmem[:, :width])
    mid_ref[...] = middle[extra:]
    normal, _ = normalize(middle)
    n2 = (normal * gain_two + bias_two).astype(bf16)
    n2_ref[...] = n2[extra:]
    wait_all(copies[1])
    l1_at, l2_at = width, 5 * width
    second = None
    for chunk in range(4):
        cols = slice(chunk * width, (chunk + 1) * width)
        h_scr[...] = mm(n2, w_vmem[:, l1_at + chunk * width : l1_at + (chunk + 1) * width])
        if extra:
            act, _ = gelu_both(h_scr[:extra, :])
            act_scr[:extra, cols] = act.astype(bf16)

        def body(i, _):
            at_row = pl.multiple_of(i * 16, 16)
            act, slope = gelu_both(h_scr[pl.ds(at_row + extra, 16), :])
            act_scr[pl.ds(at_row + extra, 16), cols] = act.astype(bf16)
            slope_ref[pl.ds(at_row, 16), cols] = slope
            return 0

        lax.fori_loop(0, (rows - extra) // 16, body, 0)
        if chunk == 0:
            wait_all(copies[2])
        part = mm(act_scr[:, cols], l2_rows(w_vmem, l2_at, chunk, width))
        second = part if second is None else second + part
    active_ref[...] = act_scr[extra:, :]
    second_ref[...] = second[extra:]
    out_ref[...] = (middle + scale_two * second).astype(bf16)


def ff_backward(base, extra, w_vmem, att_ref, g, vec_ref, slope_ref, mid_ref, second_ref, gmid_ref,
                dh_ref, dtwo_ref, done_ref, vg_ref, datt_scr):
    width = g.shape[1]
    scale_one = vec_ref[base + 2 : base + 3]
    gain_two = vec_ref[base + 3 : base + 4]
    scale_two = vec_ref[base + 5 : base + 6]
    l1_at, l2_at = width, 5 * width
    vg_ref[3:4, :] = column_sum(g * second_ref[...])
    d_two = (g * scale_two).astype(bf16)
    dtwo_ref[...] = d_two
    e = None
    for chunk in range(4):
        cols = slice(chunk * width, (chunk + 1) * width)
        d_active = mm_nt(d_two, l2_rows(w_vmem, l2_at, chunk, width))
        dh_ref[:, cols] = (d_active * slope_ref[:, cols]).astype(bf16)
        part = mm_nt(
            dh_ref[:, cols], w_vmem[:, l1_at + chunk * width : l1_at + (chunk + 1) * width]
        )
        e = part if e is None else e + part
    normal, scaled = normalize(mid_ref[...])
    vg_ref[1:2, :] = column_sum(e * normal)
    vg_ref[2:3, :] = column_sum(e)
    g_mid = g + norm_backward(e, normal, scaled, gain_two)
    gmid_ref[...] = g_mid
    vg_ref[0:1, :] = column_sum(g_mid * mm(att_ref[extra:, :], w_vmem[:, :width]))
    d_one = (g_mid * scale_one).astype(bf16)
    done_ref[...] = d_one
    datt_scr[...] = mm_nt(d_one, w_vmem[:, :width]).astype(bf16)


def decoder_layer_kernel(plan, sc_ref, *refs):
    (pieces,), refs = split_refs(refs, (PIECES,))
    (att_ref, x_ref, g_ref, vec_ref, q_ref, k_ref, v_ref,
     out_ref, n2_ref, active_ref, gmid_ref, dh_ref, dtwo_ref, done_ref, vg_ref,
     dq_ref, dk_ref, dv_ref, dkv_ref,
     w_vmem, h_scr, act_scr, slope_scr, mid_scr, second_scr, datt_scr, dk_scr, dv_scr, sems) = refs
    width = x_ref.shape[1]
    copies = fetch_layer(sc_ref, (pieces,), plan, width, w_vmem, sems)
    ff_forward(8, 0, copies, w_vmem, att_ref, x_ref[...], vec_ref, out_ref, n2_ref, active_ref,
               slope_scr, mid_scr, second_scr, h_scr, act_scr)
    ff_backward(8, 0, w_vmem, att_ref, g_ref[...].astype(f32), vec_ref, slope_scr, mid_scr,
                second_scr, gmid_ref, dh_ref, dtwo_ref, done_ref, vg_ref, datt_scr)
    attention_backward(0, sc_ref, q_ref, k_ref, v_ref, datt_scr, dq_ref, dk_ref, dv_ref, dkv_ref,
                       dk_scr, dv_scr)


def encoder_forward_kernel(plan, sc_ref, *refs):
    groups, refs = split_refs(refs, (PIECES, PIECES))
    (halo_ref, x_ref, att_ref, vec_ref,
     out_ref, n2_ref, active_ref, slope_ref, mid_ref, second_ref,
     w_vmem, h_scr, act_scr, sems) = refs
    width = x_ref.shape[1]
    copies = fetch_layer(sc_ref, groups, plan, width, w_vmem, sems)
    stream = jnp.concatenate([halo_ref[HALO - EXTRA :, :], x_ref[...]], 0).astype(f32)
    ff_forward(0, EXTRA, copies, w_vmem, att_ref, stream, vec_ref, out_ref, n2_ref, active_ref,
               slope_ref, mid_ref, second_ref, h_scr, act_scr)


def encoder_backward_kernel(plan, sc_ref, *refs):
    groups, refs = split_refs(refs, (PIECES, PIECES))
    (att_ref, g_ref, vec_ref, slope_ref, mid_ref, second_ref, q_ref, k_ref, v_ref,
     gmid_ref, dh_ref, dtwo_ref, done_ref, vg_ref, dq_ref, dk_ref, dv_ref, dkv_ref,
     w_vmem, datt_scr, dk_scr, dv_scr, sems) = refs
    width = g_ref.shape[1]
    for copies in fetch_layer(sc_ref, groups, plan, width, w_vmem, sems):
        wait_all(copies)
    ff_backward(0, EXTRA, w_vmem, att_ref, g_ref[...], vec_ref, slope_ref, mid_ref, second_ref,
                gmid_ref, dh_ref, dtwo_ref, done_ref, vg_ref, datt_scr)
    attention_backward(EXTRA, sc_ref, q_ref, k_ref, v_ref, datt_scr, dq_ref, dk_ref, dv_ref,
                       dkv_ref, dk_scr, dv_scr)


def attention_backward(extra, sc_ref, q_ref, k_ref, v_ref, do_ref,
                       dq_ref, dk_ref, dv_ref, dkv_ref, dk_scr, dv_scr):
    start, cut = sc_ref[0], sc_ref[1]
    frames = do_ref.shape[0]
    lanes = head_lanes()
    scale = HEAD_DIM ** (-0.5)
    dk_scr[...] = jnp.zeros_like(dk_scr)
    dv_scr[...] = jnp.zeros_like(dv_scr)
    wide = GROUP * QUERIES
    for first in range(0, frames, QUERIES):
        lane = lax.broadcasted_iota(jnp.int32, (1, wide), 1) % QUERIES
        query = start + first + lane
        low = lowest_key(query, cut)
        key = start + first - HALO + lax.broadcasted_iota(jnp.int32, (WINDOW, wide), 0)
        mask = (key <= query) & (key >= low)
        for group in range(HEADS // GROUP):
            cols = slice(group * GROUP * HEAD_DIM, (group + 1) * GROUP * HEAD_DIM)
            qs = stack_heads(q_ref[extra + first : extra + first + QUERIES, cols], lanes)
            ds = stack_heads(do_ref[first : first + QUERIES, cols], lanes)
            kw = k_ref[first : first + WINDOW, cols]
            vw = v_ref[first : first + WINDOW, cols]
            scores = jnp.where(mask, mm_nt(kw, qs) * scale, -1e30)
            exponent = jnp.exp(scores - jnp.max(scores, 0, keepdims=True))
            probs = exponent * (1.0 / jnp.sum(exponent, 0, keepdims=True))
            d_probs = mm_nt(vw, ds)
            mean = jnp.sum(probs * d_probs, 0, keepdims=True)
            d_scores = (probs * (d_probs - mean)).astype(bf16)
            dk_scr[first : first + WINDOW, cols] += mm(d_scores, qs)
            dv_scr[first : first + WINDOW, cols] += mm(probs.astype(bf16), ds)
            dq_ref[first : first + QUERIES, cols] = (
                unstack_heads(mm_tn(d_scores, kw), lanes) * scale
            )
    width = dq_ref.shape[1]
    dkv_ref[:, :width] = (dk_scr[:HALO] * scale).astype(bf16)
    dkv_ref[:, width:] = dv_scr[:HALO].astype(bf16)
    dk_ref[...] = dk_scr[HALO:] * scale
    dv_ref[...] = dv_scr[HALO:]


class Packer:
    def __init__(self, core, refs, shares, order):
        self.core, self.refs, self.shares, self.order = core, refs, shares, order

    def put(self, value, at, step=1, phase=0, block0=0):
        if len(self.refs) == 1:
            if step == 1:
                self.refs[0][:, at : at + value.shape[1]] = value.astype(bf16)
            return
        send, keep = self.refs
        cols = slice(at, at + value.shape[1])
        rows = 16
        hi = self.shares // 8
        blocks = value.shape[0] // (rows * step)
        for pair in range(blocks // 2):
            even = value[(2 * pair * step + phase) * rows :][:rows]
            odd = value[((2 * pair + 1) * step + phase) * rows :][:rows]
            block = (block0 + 2 * pair) // 2
            place = {"x": (block % 2, 2), "lo": (block // 2 % 2, 2), "hi": (block // 4, hi)}
            at_row = 0
            for axis in self.order:
                at_row = at_row * place[axis][1] + place[axis][0]
            at_row = at_row * rows
            first = self.core == 0
            keep[at_row : at_row + rows, cols] = jnp.where(first, even, odd).astype(bf16)
            send[at_row : at_row + rows, cols] = jnp.where(first, odd, even).astype(bf16)

    def put_l2(self, value, at, chunk, width):
        if len(self.refs) == 1:
            cols = slice(at + chunk * width, at + (chunk + 1) * width)
            self.refs[0][:, cols] = value.astype(bf16)
            return
        for phase in range(4):
            self.put(value, at + phase * width, 4, phase, chunk * width // 64)


def linear_gradients(pack, n2_ref, active_ref, dh_ref, dtwo_ref):
    width = n2_ref.shape[1]
    for chunk in range(4):
        cols = slice(chunk * width, (chunk + 1) * width)
        pack.put_l2(mm_tn(active_ref[:, cols], dtwo_ref[...]), 0, chunk, width)
        pack.put(mm_tn(n2_ref[...], dh_ref[:, cols]), (4 + chunk) * width)


def decoder_gradients_kernel(shares, sc_ref, n2_ref, active_ref, dh_ref, dtwo_ref, att_ref, done_ref,
                             *refs):
    pack = Packer(sc_ref[2], refs, shares, ORDER_A)
    linear_gradients(pack, n2_ref, active_ref, dh_ref, dtwo_ref)
    pack.put(mm_tn(att_ref[...], done_ref[...]), 8 * n2_ref.shape[1])


def encoder_gradients_kernel(shares, sc_ref, n2_ref, active_ref, dh_ref, dtwo_ref, att_ref, done_ref,
                             win_ref, dred_ref, red_ref, dlat_ref, *refs):
    width = n2_ref.shape[1]
    pack = Packer(sc_ref[2], refs, shares, ORDER_C)
    linear_gradients(pack, n2_ref, active_ref, dh_ref, dtwo_ref)
    d_reduced = dred_ref[...]
    for tap in range(4):
        pack.put(mm_tn(win_ref[tap], d_reduced), (8 + tap) * width)
    pack.put(mm_tn(att_ref[EXTRA:, :], done_ref[...]), 12 * width)
    pack.put(mm_tn(red_ref[...], dlat_ref[...]), 13 * width)


def layer_input_gradient(base, dq_ref, dk_ref, dv_ref, dkv_ref, x, gmid_ref,
                         w_in, vec_ref, cos_ref, sin_ref, dmix_ref, vg_ref):
    frames, width = dq_ref.shape
    later = frames - HALO
    cos, sin = cos_ref[HALO:], -sin_ref[HALO:]
    for at in range(0, width, 128):
        cols = slice(at, at + 128)
        dmix_ref[:, cols] = rotate(dq_ref[:, cols], cos, sin).astype(bf16)
        keys = dk_ref[:, cols]
        keys = jnp.concatenate([keys[:later], keys[later:] + dkv_ref[:, cols].astype(f32)], 0)
        dmix_ref[:, width + at : width + at + 128] = rotate(keys, cos, sin).astype(bf16)
        values = dv_ref[:, cols]
        moved = dkv_ref[:, width + at : width + at + 128].astype(f32)
        values = jnp.concatenate([values[:later], values[later:] + moved], 0)
        dmix_ref[:, 2 * width + at : 2 * width + at + 128] = values.astype(bf16)
    d_normed = mm_nt(dmix_ref[...], w_in[...])
    normal, scaled = normalize(x)
    vg_ref[0:1, :] = column_sum(d_normed * normal)
    vg_ref[1:2, :] = column_sum(d_normed)
    return gmid_ref[...] + norm_backward(d_normed, normal, scaled, vec_ref[base : base + 1])


def decoder_back_kernel(at, sc_ref, *refs):
    pieces, refs = refs[:PIECES], refs[PIECES:]
    (dq_ref, dk_ref, dv_ref, dkv_ref, x_ref, gmid_ref, vec_ref, cos_ref, sin_ref,
     dup_ref, dmix_ref, vg_ref, w_vmem, sems) = refs
    wait_all(fetch(sc_ref, pieces, at, w_vmem.shape[1], w_vmem, sems))
    grad = layer_input_gradient(
        8, dq_ref, dk_ref, dv_ref, dkv_ref, x_ref[...], gmid_ref, w_vmem, vec_ref,
        cos_ref, sin_ref, dmix_ref, vg_ref,
    )
    vg_ref[2:3, :] = column_sum(grad)
    dup_ref[...] = grad.astype(bf16)


def encoder_back_kernel(shares, sc_ref, *refs):
    (pieces,), refs = split_refs(refs, (PIECES,))
    (dq_ref, dk_ref, dv_ref, dkv_ref, x_ref, gmid_ref, vec_ref, cos_ref, sin_ref, n1_ref,
     vgs_ref, grad_ref, *rest) = refs
    refs, (w_vmem, dmix_scr, vg_scr, all_scr, sems) = rest[:-5], rest[-5:]
    width = x_ref.shape[1]
    wait_all(fetch(sc_ref, pieces, 0, w_vmem.shape[1], w_vmem, sems))
    grad = layer_input_gradient(
        0, dq_ref, dk_ref, dv_ref, dkv_ref, x_ref[...].astype(f32), gmid_ref, w_vmem,
        vec_ref, cos_ref, sin_ref, dmix_scr, vg_scr,
    )
    grad_ref[...] = grad.astype(bf16)
    pack = Packer(sc_ref[2], refs, shares, ORDER_D)
    for part in range(3):
        cols = slice(part * width, (part + 1) * width)
        pack.put(mm_tn(n1_ref[...], dmix_scr[:, cols]), part * width)
    all_scr[...] = jnp.zeros_like(all_scr)
    all_scr[0:2, :] = vg_scr[0:2, :]
    all_scr[2:6, :] = vgs_ref[0:4, :]
    all_scr[6:7, :] = vgs_ref[16:17, :]
    all_scr[7:8, :] = vgs_ref[26:27, :]
    all_scr[8:10, :] = vgs_ref[24:26, :]
    all_scr[10:14, :] = vgs_ref[8:12, :]
    pack.put(all_scr[...].T, 3 * width)


def middle_kernel(shares, sc_ref, *refs):
    (pieces, more), refs = split_refs(refs, (PIECES, PIECES))
    (dup_ref, next_ref, dmix_ref, n1_ref, restored_ref, qz_ref,
     denc_ref, dred_ref, dlat_ref, vg_ref, *rest) = refs
    refs, (up_vmem, down_vmem, frame_scr, sems) = rest[:-4], rest[-4:]
    frames, width = dup_ref.shape
    latent = qz_ref.shape[1]
    codec = frames // 2
    copies = [
        fetch(sc_ref, pieces, 0, latent + 4 * width, up_vmem, sems),
        fetch(sc_ref, more, 4 * width, 4 * width + latent, down_vmem, sems, PIECES),
    ]
    pairs = codec + 16
    even, odd = split_rows(
        jnp.concatenate([dup_ref[...], next_ref[...]], 0).astype(f32), frame_scr
    )
    both = jnp.concatenate([even, odd], 1).astype(bf16)
    wait_all(copies[0])
    up = up_vmem[:, latent : latent + 4 * width]
    here = mm_nt(both, up[:, : 2 * width])
    later = mm_nt(both, up[:, 2 * width :])
    d_restored = (here + pltpu.roll(later, pairs - 1, 0)).astype(bf16)
    d_latent = mm(d_restored, up_vmem[:, :latent]).astype(bf16)
    wait_all(copies[1])
    d_reduced = mm_nt(d_latent, down_vmem[:, 4 * width :]).astype(bf16)
    dlat_ref[...] = d_latent[:codec]
    dred_ref[...] = d_reduced[:codec]
    vg_ref[0:1, :] = column_sum(d_reduced[:codec].astype(f32))
    taps = [mm_nt(d_reduced, down_vmem[:, tap * width : (tap + 1) * width]) for tap in range(4)]
    denc_ref[...] = interleave(
        taps[2] + pltpu.roll(taps[0], pairs - 1, 0),
        taps[3] + pltpu.roll(taps[1], pairs - 1, 0),
        frame_scr,
    )[:frames]

    pack = Packer(sc_ref[2], refs, shares, ORDER_B)
    for part in range(3):
        cols = slice(part * width, (part + 1) * width)
        pack.put(mm_tn(n1_ref[...], dmix_ref[:, cols]), part * width)
    restored = restored_ref[...]
    own_pairs = both[:codec]
    before = pltpu.roll(restored.astype(f32), 1, 0)[16:].astype(bf16)
    pack.put(mm_tn(restored[16:], own_pairs[:, :width]), 3 * width)
    pack.put(mm_tn(restored[16:], own_pairs[:, width:]), 4 * width)
    pack.put(mm_tn(before, own_pairs[:, :width]), 5 * width)
    pack.put(mm_tn(before, own_pairs[:, width:]), 6 * width)
    pack.put(mm_tn(d_restored[:codec], qz_ref[CODE_HALO:, :]), 7 * width)


def latent_kernel(sc_ref, *refs):
    (pieces,), refs = split_refs(refs, (PIECES,))
    (enc_ref, rows_ref, vec_ref, res_ref, win_ref, red_ref, w_vmem, frame_scr, sems) = refs
    total, width = enc_ref.shape
    copies = fetch(sc_ref, pieces, 4 * width, w_vmem.shape[1], w_vmem, sems)
    inside = (sc_ref[0] > 0).astype(f32)
    rim = enc_ref[:EXTRA].astype(f32) * inside
    skip = EXTRA // 2
    even, odd = split_rows(jnp.concatenate([rim, enc_ref[EXTRA:].astype(f32)], 0), frame_scr)
    win_ref[0] = pltpu.roll(even, 1, 0)[skip:].astype(bf16)
    win_ref[1] = pltpu.roll(odd, 1, 0)[skip:].astype(bf16)
    win_ref[2] = even[skip:].astype(bf16)
    win_ref[3] = odd[skip:].astype(bf16)
    wait_all(copies)
    reduced = vec_ref[6:7]
    for tap in range(4):
        reduced = reduced + mm(win_ref[tap], w_vmem[:, tap * width : (tap + 1) * width])
    reduced = reduced.astype(bf16)
    red_ref[...] = reduced
    remaining = mm(reduced, w_vmem[:, 4 * width :])
    for level in range(rows_ref.shape[0]):
        res_ref[level] = remaining.astype(bf16)
        remaining = remaining - rows_ref[level].astype(f32)


def lookup_kernel(sc_ref, codes_ref, book_ref, qsend_ref, qkeep_ref, rsend_ref, rkeep_ref, q_scr):
    levels, share, latent = book_ref.shape
    total = codes_ref.shape[0]
    codec = total // 4
    base = sc_ref[3]
    core = sc_ref[2]
    entry = lax.broadcasted_iota(jnp.int32, (1, share), 1)
    for level in range(levels):
        picks = (codes_ref[:, level : level + 1] - base == entry).astype(f32).astype(bf16)
        found = mm(picks, book_ref[level])
        q_scr[CODE_HALO:] = found if level == 0 else q_scr[CODE_HALO:] + found
        for x in range(2):
            even = found[(2 * x) * codec :][:codec]
            odd = found[(2 * x + 1) * codec :][:codec]
            rkeep_ref[x, level] = jnp.where(core == 0, even, odd).astype(bf16)
            rsend_ref[x, level] = jnp.where(core == 0, odd, even).astype(bf16)
    q_scr[:CODE_HALO] = jnp.zeros((CODE_HALO, latent), f32)
    for x in range(2):
        even = q_scr[(2 * x) * codec : (2 * x + 1) * codec + CODE_HALO]
        odd = q_scr[(2 * x + 1) * codec : (2 * x + 2) * codec + CODE_HALO]
        qkeep_ref[x] = jnp.where(core == 0, even, odd)
        qsend_ref[x] = jnp.where(core == 0, odd, even)


def collect_kernel(share, seq_count, sc_ref, own_ref, x_ref, core_ref, far_ref, codes_ref,
                   marked_ref, send_ref, keep_ref, row_scr, cnt_scr):
    levels, codec, latent = own_ref.shape
    total = codes_ref.shape[1]
    lo = sc_ref[4]
    high = send_ref.shape[0]
    frame = lax.broadcasted_iota(jnp.int32, (1, total), 1) + sc_ref[6]
    row = lax.broadcasted_iota(jnp.int32, (2 * high * share, 1), 0)
    entry = (row // share * seq_count + sc_ref[5]) * share + row % share
    ones = jnp.ones((16, total), bf16)
    for level in range(levels):
        marked = marked_ref[:, level : level + 1]
        used = (entry == codes_ref[level : level + 1, :]).astype(f32)
        placed = (marked // 2 == frame).astype(f32)
        select = jnp.where(marked % 2 == 1, placed, used).astype(bf16)
        for place, ref in enumerate((own_ref, x_ref, core_ref, far_ref)):
            at_row = pl.multiple_of(sc_ref[14 + place], 32)
            row_scr[pl.ds(at_row, codec), :] = ref[level]
        sums = mm(select, row_scr[...])
        cnt_scr[level : level + 1, :] = mm_nt(ones, used.astype(bf16))[0:1]
        at = slice(level * share, (level + 1) * share)
        for h in range(high):
            even = sums[(2 * h) * share :][:share]
            odd = sums[(2 * h + 1) * share :][:share]
            keep_ref[h, at, :] = jnp.where(lo == 0, even, odd).astype(bf16)
            send_ref[h, at, :] = jnp.where(lo == 0, odd, even).astype(bf16)
    counts = cnt_scr[...]
    upper = jnp.floor(counts * (1.0 / 128.0))
    digits = jnp.concatenate([upper, counts - 128.0 * upper], 0)
    tail = slice(levels * share, levels * share + 2 * levels)
    for h in range(high):
        even = digits[:, (2 * h) * share : (2 * h + 1) * share]
        odd = digits[:, (2 * h + 1) * share : (2 * h + 2) * share]
        keep_ref[h, tail, :] = jnp.zeros((2 * levels, latent), bf16)
        send_ref[h, tail, :] = jnp.zeros((2 * levels, latent), bf16)
        keep_ref[h, tail, :share] = jnp.where(lo == 0, even, odd).astype(bf16)
        send_ref[h, tail, :share] = jnp.where(lo == 0, odd, even).astype(bf16)


def call(kernel, outs, spaces, scratch, args, micros):
    where = {"s": pltpu.SMEM, "v": pltpu.VMEM, "h": pltpu.HBM}
    title = getattr(kernel, "func", kernel).__name__
    return pl.pallas_call(
        kernel,
        name=title,
        out_shape=outs,
        in_specs=[pl.BlockSpec(memory_space=where[space]) for space in spaces],
        out_specs=[pl.BlockSpec(memory_space=pltpu.VMEM) for _ in outs],
        scratch_shapes=scratch,
        compiler_params=pltpu.CompilerParams(vmem_limit_bytes=VMEM_LIMIT),
        cost_estimate=pl.CostEstimate(
            flops=int(micros * 1e6), bytes_accessed=1, transcendentals=0
        ),
    )(*args)


def shape(dims, dtype=f32):
    return jax.ShapeDtypeStruct(dims, dtype)


def pick(block, at):
    zero = jnp.zeros((), jnp.uint32)
    start = (at,) + (zero,) * (block.ndim - 1)
    return lax.dynamic_slice(block, start, (1,) + block.shape[1:])[0]


def halve(block, axis, index, after=None):
    sent = pick(block, index["other " + axis])
    kept = pick(block, index[axis])
    got = lax.ppermute(sent, axis, [(0, 1), (1, 0)])
    if after is not None:
        got, _ = tie(got, after)
    return (kept.astype(f32) + got.astype(f32)).astype(block.dtype)


def sum_by_permutes(block, index, after=None):
    count = block.shape[0]
    if count != 4:
        return sum_over_hi(block)
    total = pick(block, index["hi"]).astype(f32)
    for turn in range(1, count):
        sent = pick(block, index["hi ^ %d" % turn])
        got = lax.ppermute(sent, "hi", [(i, i ^ turn) for i in range(count)])
        if after is not None:
            got, _ = tie(got, after)
        total = total + got.astype(f32)
    return total


def halve_hi(block, bit, index):
    name = "hi bit %d" % bit
    sent = pick(block, index["other " + name])
    kept = pick(block, index[name])
    count = lax.axis_size("hi")
    got = lax.ppermute(sent, "hi", [(i, i ^ (1 << bit)) for i in range(count)])
    return kept.astype(f32) + got.astype(f32)


def swap_add(send, keep, axis, after=None):
    got = lax.ppermute(send, axis, [(0, 1), (1, 0)])
    if after is not None:
        got, _ = tie(got, after)
    return (keep.astype(f32) + got.astype(f32)).astype(keep.dtype)


def sum_over_hi(block):
    parts = lax.all_to_all(block, "hi", 0, 0, tiled=True)
    return jnp.sum(parts.astype(f32), 0)


def shifted(block, distance):
    devices = range(lax.axis_size(SEQ))
    route = [(i - distance, i) for i in devices if i - distance in devices]
    return lax.ppermute(block, SEQ, route)


def packed_outs(width_total, width, shares):
    if width // shares % 16 == 0:
        return [shape((width // 2, width_total), bf16)] * 2
    return [shape((width, width_total), bf16)]


def swap(block, axis):
    return lax.ppermute(block, axis, [(0, 1), (1, 0)])


def tie(*values):
    return lax.optimization_barrier(values)


def half_of(share, index):
    rows = share.shape[0] // 2
    zero = jnp.zeros((), jnp.uint32)
    return lax.dynamic_slice(share, (index["lo"] * rows, zero), (rows, share.shape[1]))


def both_halves(near, far, index):
    first = index["lo"] == 0
    return jnp.concatenate([jnp.where(first, near, far), jnp.where(first, far, near)], 0)


def unfolded_rows(block, shares, l2_at):
    width = block.shape[0]
    full = [block[:, l2_at + i * width : l2_at + (i + 1) * width] for i in range(4)]
    full = jnp.concatenate(full, 0).reshape(shares, 4, width // shares, width)
    full = full.transpose(0, 2, 1, 3).reshape(width, 4 * width)
    return jnp.concatenate([block[:, :l2_at], full, block[:, l2_at + 4 * width :]], 1)


def first_sum(parts, shares, order, index, l2_at=None):
    if len(parts) == 2:
        return swap_add(*parts, "core")
    (block,) = parts
    if l2_at is not None:
        block = unfolded_rows(block, shares, l2_at)
    width, total = block.shape
    block = block.reshape(shares // 8, 2, 2, 2, width // shares, total)
    block = halve(block.transpose(3, 0, 1, 2, 4, 5), "core", index)
    places = [("hi", "lo", "x").index(axis) for axis in order]
    return block.transpose(*places, 3, 4).reshape(width // 2, total)


def next_sum(block, axis, index, after=None):
    rows, total = block.shape
    return halve(block.reshape(2, rows // 2, total), axis, index, after)


def last_sum(block, high):
    return sum_over_hi(block.reshape(high, -1, block.shape[1]))


def local(
    activations,
    encoder_attention_norm_gain,
    encoder_attention_norm_bias,
    encoder_query_key_value_weight,
    encoder_attention_output_weight,
    encoder_attention_layer_scale,
    encoder_forward_norm_gain,
    encoder_forward_norm_bias,
    encoder_forward_input_weight,
    encoder_forward_output_weight,
    encoder_forward_layer_scale,
    strided_convolution_weight,
    strided_convolution_bias,
    quantizer_input_weight,
    codebook,
    quantizer_output_weight,
    transposed_convolution_weight,
    transposed_convolution_bias,
    decoder_attention_norm_gain,
    decoder_attention_norm_bias,
    decoder_query_key_value_weight,
    decoder_attention_output_weight,
    decoder_attention_layer_scale,
    decoder_forward_norm_gain,
    decoder_forward_norm_bias,
    decoder_forward_input_weight,
    decoder_forward_output_weight,
    decoder_forward_layer_scale,
    cotangent,
    frame_segment_index,
    frame_code_index,
    replace_code_mask,
    replacing_batch_position,
    code_usage_average,
    code_latent_sum_average,
):
    batch_rows, frames, width = activations.shape
    assert batch_rows == 1
    seq_index = lax.axis_index(SEQ)
    seq_count = lax.axis_size(SEQ)
    dp_index = lax.axis_index(DP)
    dp_count = lax.axis_size(DP)
    shares = dp_count * seq_count
    codec = frames // 2
    levels = frame_code_index.shape[2]
    latent = codebook.shape[2]
    book_share = codebook.shape[1]
    core_index = lax.axis_index("core")

    x_index, lo_index = lax.axis_index("x"), lax.axis_index("lo")
    rows_share = width // seq_count
    high = shares // 8
    total_frames = HALO + frames
    code_total = replace_code_mask.shape[1]
    code_share = code_usage_average.shape[1]
    row_frames = codec * seq_count

    vectors = jnp.stack(
        [
            encoder_attention_norm_gain,
            encoder_attention_norm_bias,
            encoder_attention_layer_scale,
            encoder_forward_norm_gain,
            encoder_forward_norm_bias,
            encoder_forward_layer_scale,
            strided_convolution_bias,
            transposed_convolution_bias,
            decoder_attention_norm_gain,
            decoder_attention_norm_bias,
            decoder_attention_layer_scale,
            decoder_forward_norm_gain,
            decoder_forward_norm_bias,
            decoder_forward_layer_scale,
        ]
    )
    vectors = jnp.pad(vectors, ((0, 2), (0, 0)))
    small = jnp.concatenate(
        [frame_code_index.reshape(-1).astype(f32), vectors.reshape(-1).astype(f32)]
    )
    index = {}
    unsigned = jnp.uint32
    for axis in ("x", "lo", "core"):
        index[axis] = lax.axis_index(axis).astype(unsigned)
        index["other " + axis] = (1 - lax.axis_index(axis)).astype(unsigned)
    index["hi"] = lax.axis_index("hi").astype(unsigned)
    index["seq"] = lax.axis_index(SEQ).astype(unsigned)
    index["owner"] = (lax.axis_index(DP + SEQ) * code_share).astype(unsigned)
    for bit in range(2):
        value = (lax.axis_index("hi") >> bit) & 1
        index["hi bit %d" % bit] = value.astype(unsigned)
        index["other hi bit %d" % bit] = (1 - value).astype(unsigned)
    for turn in range(1, 4):
        index["hi ^ %d" % turn] = lax.axis_index("hi").astype(unsigned) ^ unsigned(turn)
    def flat_taps(taps):
        return taps.transpose(1, 0, 2).reshape(taps.shape[1], -1)

    def fold_l2(share):
        return share.reshape(4, -1, width).transpose(1, 0, 2).reshape(-1, 4 * width)

    dec_one = jnp.concatenate(
        [
            quantizer_output_weight.T,
            flat_taps(transposed_convolution_weight),
            decoder_query_key_value_weight,
        ],
        1,
    )
    half_one = half_of(dec_one, index)
    small, half_one = tie(small, half_one)
    small = lax.all_gather(small, SEQ, axis=0, tiled=False)
    names = sorted(index)
    *index_values, small = tie(*[index[name] for name in names], small)
    index = dict(zip(names, index_values))
    code_count = codec * levels
    row_codes = small[:, :code_count].astype(jnp.int32).reshape(seq_count, codec, levels)
    vectors = small[:, code_count:].reshape(seq_count, 16, -1).transpose(1, 0, 2).reshape(16, width)
    order = [2 * x_index + core_index, 2 * (1 - x_index) + core_index]
    order += [2 * x_index + 1 - core_index, 2 * (1 - x_index) + 1 - core_index]
    cut = jnp.sum((frame_segment_index[0] == 0).astype(jnp.int32))
    scalars = jnp.stack(
        [
            seq_index * frames,
            cut,
            core_index,
            seq_index * book_share,
            lo_index,
            seq_index,
            dp_index * row_frames,
            seq_index,
        ]
        + [
            *[place * rows_share for place in order],
            seq_index,
            seq_index,
        ]
        + [place * codec for place in order]
    ).astype(jnp.int32)

    half_one, _ = tie(half_one, small)
    near_one = swap(half_one, "x")
    core_one = swap(dec_one, "core")
    activation_halo = shifted(activations[0, frames - HALO :], 1)

    positions = seq_index * frames - HALO + jnp.arange(total_frames, dtype=jnp.int32)
    half_dim = HEAD_DIM // 2
    frequency = jnp.power(10000.0, -jnp.arange(half_dim, dtype=f32) / half_dim)

    def angle_tables(positions):
        angles = positions.astype(f32)[:, None] * frequency[None, :]
        cos, sin = jnp.cos(angles), jnp.sin(angles)
        return jnp.concatenate([cos] * 4, 1), jnp.concatenate([-sin, sin, -sin, sin], 1)

    row_codes, activation_halo, core_one = tie(row_codes, activation_halo, core_one)

    window = codec + CODE_HALO
    qsend, qkeep, rsend, rkeep = call(
        lookup_kernel,
        [shape((2, window, latent))] * 2 + [shape((2, levels, codec, latent), bf16)] * 2,
        "svv",
        [pltpu.VMEM((CODE_HALO + codec * seq_count, latent), f32)],
        (scalars, row_codes.reshape(-1, levels), codebook),
        4,
    )
    q_sum = swap_add(qsend, qkeep, "core")
    q_sent = pick(q_sum, index["other x"])
    q_got = swap(q_sent, "x")
    (near_one, positions, dec_l2, enc_in, enc_l2, down_share, replace_code_mask,
     replacing_batch_position, row_codes, _) = tie(
        near_one, positions, decoder_forward_output_weight, encoder_query_key_value_weight,
        encoder_forward_output_weight, strided_convolution_weight, replace_code_mask,
        replacing_batch_position, row_codes, q_sent,
    )
    dec_two = jnp.concatenate(
        [decoder_attention_output_weight, decoder_forward_input_weight, fold_l2(dec_l2)], 1
    )
    enc_one = jnp.concatenate(
        [
            enc_in,
            encoder_attention_output_weight,
            flat_taps(down_share),
            quantizer_input_weight,
        ],
        1,
    )
    enc_two = jnp.concatenate([encoder_forward_input_weight, fold_l2(enc_l2)], 1)
    marked = (replacing_batch_position * 2 + replace_code_mask).T
    marked = marked.reshape(dp_count, seq_count, code_share, levels).transpose(1, 0, 2, 3)
    marked = pick(marked, index["seq"]).reshape(dp_count * code_share, levels)
    code_columns = row_codes.reshape(row_frames, levels).T
    owner_flag = lax.dynamic_slice(
        replace_code_mask, (jnp.zeros((), unsigned), index["owner"]), (levels, code_share)
    ) == 1
    far_one = swap(near_one, "lo")
    near_one = both_halves(near_one, far_one, index)
    dec_one = [dec_one, near_one, core_one, swap(near_one, "core")]
    half_two = half_of(dec_two, index)
    cos_table, sin_table = angle_tables(positions)
    near_two = swap(half_two, "x")
    quantized = (pick(q_sum, index["x"]) + q_got).astype(bf16)
    half_three, half_four = half_of(enc_one, index), half_of(enc_two, index)
    (quantized, near_two, half_three, half_four, activation_halo, cos_table, sin_table, marked,
     code_columns, owner_flag) = tie(
        quantized, near_two, half_three, half_four, activation_halo, cos_table, sin_table, marked,
        code_columns, owner_flag,
    )
    core_two = swap(dec_two, "core")
    far_two = swap(near_two, "lo")
    near_three = swap(half_three, "x")

    d_x, restored, d_n1, d_q, d_k, d_v, d_att = call(
        decoder_front_kernel,
        [
            shape((frames, width)),
            shape((codec + 16, width), bf16),
            shape((frames, width), bf16),
            shape((frames, width), bf16),
            shape((total_frames, width), bf16),
            shape((total_frames, width), bf16),
            shape((frames, width), bf16),
        ],
        "s" + "h" * PIECES + "vvvv",
        [
            pltpu.VMEM((width, latent + 7 * width), bf16),
            pltpu.VMEM((width // 128, total_frames, 128), f32),
            pltpu.SemaphoreType.DMA((PIECES,)),
        ],
        (scalars, *dec_one, quantized, vectors, cos_table, sin_table),
        8,
    )
    d_att, far_two, near_three, half_four, rsend = tie(
        d_att, far_two, near_three, half_four, rsend
    )
    code_rows = swap_add(rsend, rkeep, "core")
    near_two = both_halves(near_two, far_two, index)
    dec_two = [dec_two, near_two, core_two, swap(near_two, "core")]
    far_three = swap(near_three, "lo")
    near_four = swap(half_four, "x")
    layer_scratch = [
        pltpu.VMEM((frames, width), bf16),
        pltpu.VMEM((total_frames, width), f32),
        pltpu.VMEM((total_frames, width), f32),
        pltpu.SemaphoreType.DMA((3 * PIECES,)),
    ]
    forward_outs = [shape((frames, width), bf16), shape((frames, 4 * width), bf16)]
    kept_outs = [shape((frames, 4 * width)), shape((frames, width)), shape((frames, width))]
    backward_outs = [
        shape((frames, width)),
        shape((frames, 4 * width), bf16),
        shape((frames, width), bf16),
        shape((frames, width), bf16),
        shape((8, width)),
        shape((frames, width)),
        shape((frames, width)),
        shape((frames, width)),
        shape((HALO, 2 * width), bf16),
    ]
    weights_scratch = pltpu.VMEM((width, 9 * width), bf16)
    (output, d_n2, d_active, d_gmid, d_dh, d_dtwo, d_done, d_vg_two, d_dq, d_dk, d_dv, d_dkv) = call(
        partial(decoder_layer_kernel, ((0, 0), (0, width), (0, 5 * width))),
        [shape((frames, width), bf16)] + forward_outs + backward_outs,
        "s" + "h" * PIECES + "vvvvvvv",
        [
            weights_scratch,
            pltpu.VMEM((frames, width), f32),
            pltpu.VMEM((frames, 4 * width), bf16),
            pltpu.VMEM((frames, 4 * width), f32),
            pltpu.VMEM((frames, width), f32),
            pltpu.VMEM((frames, width), f32),
        ]
        + layer_scratch,
        (scalars, *dec_two, d_att, d_x, cotangent[0], vectors, d_q, d_k, d_v),
        14,
    )
    d_n2, far_three, near_four, code_rows = tie(d_n2, far_three, near_four, code_rows)
    near_three = both_halves(near_three, far_three, index)
    enc_one = [enc_one, near_three, swap(enc_one, "core"), swap(near_three, "core")]
    far_four = swap(near_four, "lo")
    d_dkv = shifted(d_dkv, -1)
    group_a = call(
        partial(decoder_gradients_kernel, shares),
        packed_outs(9 * width, width, shares),
        "svvvvvv",
        [],
        (scalars, d_n2, d_active, d_dh, d_dtwo, d_att, d_done),
        5,
    )
    d_dq, *group_a = tie(d_dq, *group_a)
    code_rows, d_dkv = tie(code_rows, d_dkv)
    code_rows = halve(code_rows, "x", index)
    a_sum = first_sum(group_a, shares, ORDER_A, index, 0)
    d_up, d_mixed, d_vg_one = call(
        partial(decoder_back_kernel, latent + 4 * width),
        [shape((frames, width), bf16), shape((frames, 3 * width), bf16), shape((8, width))],
        "s" + "h" * PIECES + "v" * 9,
        [pltpu.VMEM((width, 3 * width), bf16), pltpu.SemaphoreType.DMA((PIECES,))],
        (
            scalars, *dec_one, d_dq, d_dk, d_dv, d_dkv, d_x, d_gmid, vectors, cos_table,
            sin_table,
        ),
        4,
    )
    d_up_next = shifted(d_up[:32], -1)


    a_sum, d_up, e_input, far_four, code_rows = tie(
        a_sum, d_up, activations[0], far_four, code_rows
    )
    near_four = both_halves(near_four, far_four, index)
    enc_two = [enc_two, near_four, swap(enc_two, "core"), swap(near_four, "core")]
    a_sum = next_sum(a_sum, ORDER_A[0], index)
    e_n1, e_q, e_k, e_v, e_att = call(
        encoder_front_kernel,
        [
            shape((frames, width), bf16),
            shape((frames + EXTRA, width), bf16),
            shape((total_frames, width), bf16),
            shape((total_frames, width), bf16),
            shape((frames + EXTRA, width), bf16),
        ],
        "s" + "h" * PIECES + "vvvvv",
        [pltpu.VMEM((width, 3 * width), bf16), pltpu.SemaphoreType.DMA((PIECES,))],
        (scalars, *enc_one, activation_halo, e_input, vectors, cos_table, sin_table),
        7,
    )

    d_mixed, e_n1 = tie(d_mixed, e_n1)
    middle_outs = call(
        partial(middle_kernel, shares),
        [
            shape((frames, width)),
            shape((codec, width), bf16),
            shape((codec, latent), bf16),
            shape((8, width)),
        ]
        + packed_outs(7 * width + latent, width, shares),
        "s" + "h" * (2 * PIECES) + "" + "v" * 6,
        [
            pltpu.VMEM((width, latent + 4 * width), bf16),
            pltpu.VMEM((width, latent + 4 * width), bf16),
            pltpu.VMEM((width // 128, frames + 32, 128), f32),
            pltpu.SemaphoreType.DMA((2 * PIECES,)),
        ],
        (scalars, *dec_one, *enc_one, d_up, d_up_next, d_mixed, d_n1, restored, quantized),
        7,
    )
    d_encoded, d_reduced, d_latent, m_vg = middle_outs[:4]
    b_sum = first_sum(middle_outs[4:], shares, ORDER_B, index)

    e_att, d_encoded = tie(e_att, d_encoded)
    enc_plan = ((0, 3 * width), (1, 0), (1, 4 * width))
    rows = frames + EXTRA
    encoded, e_n2, e_active, e_slope, e_mid, e_second = call(
        partial(encoder_forward_kernel, enc_plan),
        [shape((rows, width), bf16)] + forward_outs + kept_outs,
        "s" + "h" * (2 * PIECES) + "vvvv",
        [
            weights_scratch,
            pltpu.VMEM((rows, width), f32),
            pltpu.VMEM((rows, 4 * width), bf16),
            pltpu.SemaphoreType.DMA((3 * PIECES,)),
        ],
        (scalars, *enc_one, *enc_two, activation_halo, e_input, e_att, vectors),
        6,
    )
    encoded, b_sum, a_sum = tie(encoded, b_sum, a_sum)
    residuals, windows, reduced = call(
        latent_kernel,
        [
            shape((levels, codec, latent), bf16),
            shape((4, codec, width), bf16),
            shape((codec, width), bf16),
        ],
        "s" + "h" * PIECES + "vvv",
        [
            pltpu.VMEM((width, 4 * width + latent), bf16),
            pltpu.VMEM((width // 128, frames + EXTRA, 128), f32),
            pltpu.SemaphoreType.DMA((PIECES,)),
        ],
        (scalars, *enc_one, encoded, code_rows, vectors),
        3,
    )
    near_res = swap(residuals, "x")
    core_res = swap(residuals, "core")

    d_encoded, _ = tie(d_encoded, residuals)
    (e_gmid, e_dh, e_dtwo, e_done, e_vg_two, e_dq, e_dk, e_dv, e_dkv) = call(
        partial(encoder_backward_kernel, enc_plan),
        backward_outs,
        "s" + "h" * (2 * PIECES) + "v" * 9,
        [weights_scratch] + layer_scratch,
        (
            scalars, *enc_one, *enc_two, e_att, d_encoded, vectors, e_slope, e_mid, e_second,
            e_q, e_k, e_v,
        ),
        11,
    )
    e_dkv = shifted(e_dkv, -1)
    near_res, core_res, _ = tie(near_res, core_res, e_gmid)
    res_pieces = [residuals, near_res, core_res, swap(near_res, "core")]

    b_sum = next_sum(b_sum, ORDER_B[0], index)
    a_sum = next_sum(a_sum, ORDER_A[1], index, e_gmid)

    if code_share % 16 == 0:
        tail_rows = levels * code_share
        csend, ckeep = call(
            partial(collect_kernel, code_share, seq_count),
            [shape((dp_count // 2, tail_rows + 2 * levels, latent), bf16)] * 2,
            "svvvvvv",
            [
                pltpu.VMEM((row_frames, latent), bf16),
                pltpu.VMEM((levels, dp_count * code_share), f32),
            ],
            (scalars, *res_pieces, code_columns, marked),
            5,
        )
        e_n2, csend, e_gmid, b_sum, a_sum, e_dkv = tie(
            e_n2, csend, e_gmid, b_sum, a_sum, e_dkv
        )
    group_c = call(
        partial(encoder_gradients_kernel, shares),
        packed_outs(13 * width + latent, width, shares),
        "s" + "v" * 10,
        [],
        (
            scalars, e_n2, e_active, e_dh, e_dtwo, e_att, e_done, windows, d_reduced, reduced,
            d_latent,
        ),
        5,
    )
    e_dq, *group_c = tie(e_dq, *group_c)
    c_sum = first_sum(group_c, shares, ORDER_C, index, 0)
    if high == 4:
        a_sum = halve_hi(a_sum.reshape(2, -1, a_sum.shape[1]), 1, index).astype(bf16)
    e_dq, c_sum, a_sum, b_sum = tie(e_dq, c_sum, a_sum, b_sum)
    vector_grads = jnp.concatenate([e_vg_two, d_vg_two, m_vg, d_vg_one], 0)
    grad_outs = call(
        partial(encoder_back_kernel, shares),
        [shape((frames, width), bf16)] + packed_outs(3 * width + 128, width, shares),
        "s" + "h" * PIECES + "v" * 11,
        [
            pltpu.VMEM((width, 3 * width), bf16),
            pltpu.VMEM((frames, 3 * width), bf16),
            pltpu.VMEM((8, width), f32),
            pltpu.VMEM((128, width), f32),
            pltpu.SemaphoreType.DMA((PIECES,)),
        ],
        (
            scalars, *enc_one, e_dq, e_dk, e_dv, e_dkv, e_input, e_gmid, vectors,
            cos_table, sin_table, e_n1, vector_grads,
        ),
        5,
    )
    activations_grad = grad_outs[0]

    d_sum = first_sum(grad_outs[1:], shares, ORDER_D, index)
    if code_share % 16 == 0:
        combined = swap_add(csend, ckeep, "lo", d_sum)
        b_sum = next_sum(b_sum, ORDER_B[1], index, combined)
    else:
        b_sum = next_sum(b_sum, ORDER_B[1], index, d_sum)
    if high == 4:
        grads_a = halve_hi(a_sum.reshape(2, -1, a_sum.shape[1]), 0, index)
    else:
        grads_a = last_sum(a_sum, high)
    grads_b = last_sum(b_sum, high)
    if code_share % 16 == 0:
        combined = sum_over_hi(combined)
        summed = combined[:tail_rows].reshape(levels, code_share, latent)
        digits = combined[tail_rows:, :code_share]
        counted = 128.0 * digits[:levels] + digits[levels:]
    else:
        entry = (
            jnp.arange(dp_count, dtype=jnp.int32)[:, None] * seq_count + seq_index
        ) * code_share + jnp.arange(code_share, dtype=jnp.int32)
        relative = [place * codec + jnp.arange(codec, dtype=jnp.int32) for place in order]
        relative = jnp.concatenate(relative)
        flat_res = jnp.concatenate(res_pieces, 1)
        used = entry.reshape(1, -1, 1) == code_columns[:, None, relative]
        placed = (marked.T // 2)[:, :, None] == dp_index * row_frames + relative
        counts = jnp.sum(used.astype(f32), 2).reshape(levels, dp_count, code_share)
        selects = jnp.where((marked.T % 2)[:, :, None] == 1, placed, used).astype(bf16)
        sums = jnp.einsum("lct,ltd->lcd", selects, flat_res, preferred_element_type=f32)
        sums = sums.astype(bf16).reshape(levels, dp_count, code_share, latent)
        summed = lax.psum_scatter(sums, DP, scatter_dimension=1, tiled=False).astype(f32)
        counted = lax.psum_scatter(counts, DP, scatter_dimension=1, tiled=False)
    d_sum = next_sum(d_sum, ORDER_D[0], index, b_sum)
    c_one, c_two = c_sum[:, : 8 * width], c_sum[:, 8 * width :]
    c_one = next_sum(c_one, ORDER_C[0], index, d_sum)
    d_sum = next_sum(d_sum, ORDER_D[1], index, c_one)
    c_two = next_sum(c_two, ORDER_C[0], index, d_sum)
    c_one = next_sum(c_one, ORDER_C[1], index, c_two)
    c_two = next_sum(c_two, ORDER_C[1], index, c_one)
    edge = 13 * width + latent
    together = last_sum(jnp.concatenate([c_one, c_two, d_sum], 1), high)
    grads_c, grads_d = together[:, :edge], together[:, edge:]

    new_cluster_size = ema_decay * code_usage_average + (1.0 - ema_decay) * counted
    new_embed_sum = jnp.where(
        owner_flag[:, :, None],
        summed * new_cluster_size[:, :, None],
        ema_decay * code_latent_sum_average + (1.0 - ema_decay) * summed,
    )
    new_codebook = new_embed_sum / new_cluster_size[:, :, None]

    def columns(block, at, count):
        return block[:, at * width : (at + count) * width]

    def taps(block):
        return block.reshape(-1, 4, width).transpose(1, 0, 2)

    def unfold(block):
        return block.reshape(-1, 4, width).transpose(1, 0, 2).reshape(-1, width)

    vec = grads_d[:, 3 * width : 3 * width + 16].T
    return (
        output[None],
        activations_grad[None],
        vec[0],
        vec[1],
        columns(grads_d, 0, 3),
        columns(grads_c, 12, 1),
        vec[2],
        vec[3],
        vec[4],
        columns(grads_c, 4, 4),
        unfold(columns(grads_c, 0, 4)),
        vec[5],
        taps(columns(grads_c, 8, 4)),
        vec[6],
        grads_c[:, 13 * width :],
        grads_b[:, 7 * width :].T,
        taps(columns(grads_b, 3, 4)),
        vec[7],
        vec[8],
        vec[9],
        columns(grads_b, 0, 3),
        columns(grads_a, 8, 1),
        vec[10],
        vec[11],
        vec[12],
        columns(grads_a, 4, 4),
        unfold(columns(grads_a, 0, 4)),
        vec[13],
        new_cluster_size,
        new_embed_sum,
        new_codebook,
    )


def solution(mesh):
    grid = mesh.devices
    mesh = jax.sharding.Mesh(
        grid.reshape(grid.shape[0] // 2, 2, grid.shape[1] // 2, 2), ("hi", "lo", "x", "core")
    )
    placed = (
        P(DP, SEQ, None),
        P(SEQ),
        P(SEQ),
        P(SEQ, None),
        P(SEQ, None),
        P(SEQ),
        P(SEQ),
        P(SEQ),
        P(SEQ, None),
        P(SEQ, None),
        P(SEQ),
        P(None, SEQ, None),
        P(SEQ),
        P(SEQ, None),
        P(None, SEQ, None),
        P(None, SEQ),
        P(None, SEQ, None),
        P(SEQ),
        P(SEQ),
        P(SEQ),
        P(SEQ, None),
        P(SEQ, None),
        P(SEQ),
        P(SEQ),
        P(SEQ),
        P(SEQ, None),
        P(SEQ, None),
        P(SEQ),
        P(DP, SEQ, None),
        P(DP, None),
        P(DP, SEQ, None),
        P(),
        P(),
        P(None, DP + SEQ),
        P(None, DP + SEQ, None),
    )
    return jax.shard_map(
        local,
        mesh=mesh,
        in_specs=placed,
        out_specs=(
            P(DP, SEQ, None),
            P(DP, SEQ, None),
            P(DP + SEQ),
            P(DP + SEQ),
            P(DP + SEQ, None),
            P(DP + SEQ, None),
            P(DP + SEQ),
            P(DP + SEQ),
            P(DP + SEQ),
            P(DP + SEQ, None),
            P(DP + SEQ, None),
            P(DP + SEQ),
            P(None, DP + SEQ, None),
            P(DP + SEQ),
            P(DP + SEQ, None),
            P(None, DP + SEQ),
            P(None, DP + SEQ, None),
            P(DP + SEQ),
            P(DP + SEQ),
            P(DP + SEQ),
            P(DP + SEQ, None),
            P(DP + SEQ, None),
            P(DP + SEQ),
            P(DP + SEQ),
            P(DP + SEQ),
            P(DP + SEQ, None),
            P(DP + SEQ, None),
            P(DP + SEQ),
            P(None, DP + SEQ),
            P(None, DP + SEQ, None),
            P(None, DP + SEQ, None),
        ),
        check_vma=False,
    )
```

```python
from functools import partial

import jax
import jax.numpy as jnp
from jax import lax
from jax.experimental import pallas as pl
from jax.experimental.pallas import tpu as pltpu
from jax.sharding import PartitionSpec as P

HEADS = 8
HEAD_DIM = 64
CONTEXT = 250
HALO = 256
CODE_HALO = HALO // 2 + 16
EXTRA = 16
QUERIES = 64
GROUP = 4
WINDOW = HALO + QUERIES
VMEM_LIMIT = 26 * 1024 * 1024
ORDER_A = ("lo", "x", "hi")
ORDER_B = ("lo", "x", "hi")
ORDER_C_ONE = ("x", "lo", "hi")
ORDER_C_TWO = ("lo", "x", "hi")
ORDER_D = ("lo", "x", "hi")
DP = ("hi", "lo")
SEQ = ("x", "core")

norm_eps = 1e-05
ema_decay = 0.9
bf16 = jnp.bfloat16
f32 = jnp.float32


PIECES = 4


def fetch(sc_ref, pieces, at, width, dst, sems, first=0):
    copies = []
    for i, piece in enumerate(pieces):
        rows = piece.shape[0]
        row = pl.multiple_of(sc_ref[8 + i], 128)
        copies.append(
            pltpu.make_async_copy(
                piece.at[:, at : at + width], dst.at[pl.ds(row, rows), :], sems.at[first + i]
            )
        )
        copies[-1].start()
    return copies


def split_refs(refs, counts):
    groups = []
    for count in counts:
        groups.append(refs[:count])
        refs = refs[count:]
    return groups, refs


def wait_all(copies):
    for copy in copies:
        copy.wait()


def mm(a, b):
    return jnp.dot(a, b, preferred_element_type=f32)


def mm_nt(a, b):
    return lax.dot_general(a, b, (((1,), (1,)), ((), ())), preferred_element_type=f32)


def mm_tn(a, b):
    return lax.dot_general(a, b, (((0,), (0,)), ((), ())), preferred_element_type=f32)


def normalize(stream):
    center = stream - jnp.mean(stream, -1, keepdims=True)
    scaled = lax.rsqrt(jnp.mean(center * center, -1, keepdims=True) + norm_eps)
    return center * scaled, scaled


def norm_backward(upstream, normal, scaled, gain):
    inner = upstream * gain
    return scaled * (
        inner
        - jnp.mean(inner, -1, keepdims=True)
        - normal * jnp.mean(inner * normal, -1, keepdims=True)
    )


def column_sum(value):
    return jnp.sum(value, 0, keepdims=True)


def interleave(even, odd, scr):
    tiles, rows, _ = scr.shape
    for tile in range(tiles):
        cols = slice(tile * 128, (tile + 1) * 128)
        scr[tile, pl.ds(0, rows // 2, stride=2), :] = even[:, cols]
        scr[tile, pl.ds(1, rows // 2, stride=2), :] = odd[:, cols]
    return jnp.concatenate([scr[tile] for tile in range(tiles)], 1)


def split_rows(value, scr):
    tiles, rows, _ = scr.shape
    for tile in range(tiles):
        scr[tile] = value[:, tile * 128 : (tile + 1) * 128]
    even = [scr[tile, pl.ds(0, rows // 2, stride=2), :] for tile in range(tiles)]
    odd = [scr[tile, pl.ds(1, rows // 2, stride=2), :] for tile in range(tiles)]
    return jnp.concatenate(even, 1), jnp.concatenate(odd, 1)


def first_half():
    lane = lax.broadcasted_iota(jnp.int32, (1, 128), 1)
    return lane % HEAD_DIM < HEAD_DIM // 2


def rotate(tile, cos, sin):
    swapped = jnp.where(first_half(), pltpu.roll(tile, 96, 1), pltpu.roll(tile, 32, 1))
    return tile * cos + swapped * sin


def head_lanes():
    lane = lax.broadcasted_iota(jnp.int32, (1, GROUP * HEAD_DIM), 1) // HEAD_DIM
    return [(lane == head) for head in range(GROUP)]


def stack_heads(block, lanes):
    return jnp.concatenate([block * mask.astype(bf16) for mask in lanes], 0)


def unstack_heads(block, lanes):
    rows = block.shape[0] // GROUP
    out = block[:rows]
    for head in range(1, GROUP):
        out = jnp.where(lanes[head], block[head * rows : (head + 1) * rows], out)
    return out


def lowest_key(query, cut):
    low = jnp.maximum(query - (CONTEXT - 1), 0)
    return jnp.where(query >= cut, jnp.maximum(low, cut), low)


def attend(q_ref, k_ref, v_ref, att_ref, sc_ref, rows, first_query, first_key, keys, at_row):
    start, cut = sc_ref[0], sc_ref[1]
    query = start + first_query + lax.broadcasted_iota(jnp.int32, (rows, 1), 0)
    low = lowest_key(query, cut)
    key = start + first_key + lax.broadcasted_iota(jnp.int32, (rows, keys), 1)
    mask = (key <= query) & (key >= low)
    mask = jnp.concatenate([mask] * GROUP, 0)
    lanes = head_lanes()
    key_row = first_key + HALO
    for group in range(HEADS // GROUP):
        cols = slice(group * GROUP * HEAD_DIM, (group + 1) * GROUP * HEAD_DIM)
        stacked = stack_heads(q_ref[at_row : at_row + rows, cols], lanes)
        scores = mm_nt(stacked, k_ref[key_row : key_row + keys, cols]) * HEAD_DIM ** (-0.5)
        scores = jnp.where(mask, scores, -1e30)
        exponent = jnp.exp(scores - jnp.max(scores, -1, keepdims=True))
        weights = exponent * (1.0 / jnp.sum(exponent, -1, keepdims=True))
        mixed = mm(weights.astype(bf16), v_ref[key_row : key_row + keys, cols])
        att_ref[at_row : at_row + rows, cols] = unstack_heads(mixed, lanes).astype(bf16)


def front(x, vec_ref, base, w_in, cos_ref, sin_ref, sc_ref, n1_ref, q_ref, k_ref, v_ref, att_ref,
          extra):
    width = x.shape[1]
    normal, _ = normalize(x)
    low = (normal * vec_ref[base : base + 1] + vec_ref[base + 1 : base + 2]).astype(bf16)
    n1_ref[...] = low[HALO:]
    skip = HALO - extra
    queries = mm(low[skip:], w_in[:, :width])
    keys = mm(low, w_in[:, width : 2 * width])
    for at in range(0, width, 128):
        q_ref[:, at : at + 128] = rotate(
            queries[:, at : at + 128], cos_ref[skip:], sin_ref[skip:]
        ).astype(bf16)
        k_ref[:, at : at + 128] = rotate(keys[:, at : at + 128], cos_ref[...], sin_ref[...]).astype(
            bf16
        )
    v_ref[...] = mm(low, w_in[:, 2 * width :]).astype(bf16)
    frames = x.shape[0] - HALO
    if extra:
        attend(q_ref, k_ref, v_ref, att_ref, sc_ref, extra, -extra, -HALO, HALO, 0)
    for first in range(0, frames, QUERIES):
        attend(
            q_ref, k_ref, v_ref, att_ref, sc_ref, QUERIES, first, first - HALO, WINDOW,
            extra + first,
        )


def decoder_front_kernel(sc_ref, *refs):
    pieces, refs = refs[:PIECES], refs[PIECES:]
    (qz_ref, vec_ref, cos_ref, sin_ref, x_ref, restored_ref, n1_ref, q_ref, k_ref, v_ref, att_ref,
     w_vmem, x_scr, sems) = refs
    width = x_ref.shape[1]
    wait_all(fetch(sc_ref, pieces, 0, w_vmem.shape[1], w_vmem, sems))
    latent = qz_ref.shape[1]
    restored = mm_nt(qz_ref[...], w_vmem[:, :latent]).astype(bf16)
    restored_ref[...] = restored[CODE_HALO - 16 :]
    both = mm(restored, w_vmem[:, latent : latent + 4 * width])
    bias = vec_ref[7:8]
    now = both[16:, : 2 * width]
    before = pltpu.roll(both[:, 2 * width :], 1, 0)[16:]
    total = now + before
    x = interleave(total[:, :width] + bias, total[:, width:] + bias, x_scr)
    x_ref[...] = x[HALO:]
    w_in = w_vmem.at[:, latent + 4 * width :]
    front(x, vec_ref, 8, w_in, cos_ref, sin_ref, sc_ref, n1_ref, q_ref, k_ref, v_ref,
          att_ref, 0)


def encoder_front_kernel(sc_ref, *refs):
    (pieces,), refs = split_refs(refs, (PIECES,))
    (halo_ref, x_ref, vec_ref, cos_ref, sin_ref, n1_ref, q_ref, k_ref, v_ref, att_ref,
     w_vmem, sems) = refs
    width = x_ref.shape[1]
    copies = fetch(sc_ref, pieces, 0, 3 * width, w_vmem, sems)
    x = jnp.concatenate([halo_ref[...], x_ref[...]], 0).astype(f32)
    wait_all(copies)
    front(x, vec_ref, 0, w_vmem, cos_ref, sin_ref, sc_ref, n1_ref, q_ref, k_ref, v_ref, att_ref,
          EXTRA)


def gelu_both(hidden):
    share = 0.5 * (1.0 + lax.erf(hidden * 0.7071067811865476))
    density = jnp.exp(-0.5 * hidden * hidden) * 0.3989422804014327
    return hidden * share, share + hidden * density


def l2_rows(w, at, chunk, width):
    rows = width // 4
    return jnp.concatenate(
        [
            w[chunk * rows : (chunk + 1) * rows, at + g * width : at + (g + 1) * width]
            for g in range(4)
        ],
        0,
    )


def fetch_layer(sc_ref, groups, plan, width, w_vmem, sems):
    edges = (0, width, 5 * width, 9 * width)
    return [
        fetch(
            sc_ref, groups[plan[i][0]], plan[i][1], high - low, w_vmem.at[:, low:high], sems,
            PIECES * i,
        )
        for i, (low, high) in enumerate(zip(edges[:-1], edges[1:]))
    ]


def ff_forward(base, extra, copies, w_vmem, att_ref, stream, vec_ref, out_ref, n2_ref, active_ref,
               slope_ref, mid_ref, second_ref, h_scr, act_scr):
    rows, width = stream.shape
    scale_one = vec_ref[base + 2 : base + 3]
    gain_two = vec_ref[base + 3 : base + 4]
    bias_two = vec_ref[base + 4 : base + 5]
    scale_two = vec_ref[base + 5 : base + 6]
    wait_all(copies[0])
    middle = stream + scale_one * mm(att_ref[...], w_vmem[:, :width])
    mid_ref[...] = middle[extra:]
    normal, _ = normalize(middle)
    n2 = (normal * gain_two + bias_two).astype(bf16)
    n2_ref[...] = n2[extra:]
    wait_all(copies[1])
    l1_at, l2_at = width, 5 * width
    second = None
    for chunk in range(4):
        cols = slice(chunk * width, (chunk + 1) * width)
        h_scr[...] = mm(n2, w_vmem[:, l1_at + chunk * width : l1_at + (chunk + 1) * width])
        if extra:
            act, _ = gelu_both(h_scr[:extra, :])
            act_scr[:extra, cols] = act.astype(bf16)

        def body(i, _):
            at_row = pl.multiple_of(i * 16, 16)
            act, slope = gelu_both(h_scr[pl.ds(at_row + extra, 16), :])
            act_scr[pl.ds(at_row + extra, 16), cols] = act.astype(bf16)
            slope_ref[pl.ds(at_row, 16), cols] = slope
            return 0

        lax.fori_loop(0, (rows - extra) // 16, body, 0)
        if chunk == 0:
            wait_all(copies[2])
        part = mm(act_scr[:, cols], l2_rows(w_vmem, l2_at, chunk, width))
        second = part if second is None else second + part
    active_ref[...] = act_scr[extra:, :]
    second_ref[...] = second[extra:]
    out_ref[...] = (middle + scale_two * second).astype(bf16)


def ff_backward(base, extra, w_vmem, att_ref, g, vec_ref, slope_ref, mid_ref, second_ref, gmid_ref,
                dh_ref, dtwo_ref, done_ref, vg_ref, datt_scr):
    width = g.shape[1]
    scale_one = vec_ref[base + 2 : base + 3]
    gain_two = vec_ref[base + 3 : base + 4]
    scale_two = vec_ref[base + 5 : base + 6]
    l1_at, l2_at = width, 5 * width
    vg_ref[3:4, :] = column_sum(g * second_ref[...])
    d_two = (g * scale_two).astype(bf16)
    dtwo_ref[...] = d_two
    e = None
    for chunk in range(4):
        cols = slice(chunk * width, (chunk + 1) * width)
        d_active = mm_nt(d_two, l2_rows(w_vmem, l2_at, chunk, width))
        dh_ref[:, cols] = (d_active * slope_ref[:, cols]).astype(bf16)
        part = mm_nt(
            dh_ref[:, cols], w_vmem[:, l1_at + chunk * width : l1_at + (chunk + 1) * width]
        )
        e = part if e is None else e + part
    normal, scaled = normalize(mid_ref[...])
    vg_ref[1:2, :] = column_sum(e * normal)
    vg_ref[2:3, :] = column_sum(e)
    g_mid = g + norm_backward(e, normal, scaled, gain_two)
    gmid_ref[...] = g_mid
    vg_ref[0:1, :] = column_sum(g_mid * mm(att_ref[extra:, :], w_vmem[:, :width]))
    d_one = (g_mid * scale_one).astype(bf16)
    done_ref[...] = d_one
    datt_scr[...] = mm_nt(d_one, w_vmem[:, :width]).astype(bf16)


def decoder_layer_kernel(plan, sc_ref, *refs):
    (pieces,), refs = split_refs(refs, (PIECES,))
    (att_ref, x_ref, g_ref, vec_ref, q_ref, k_ref, v_ref,
     out_ref, n2_ref, active_ref, gmid_ref, dh_ref, dtwo_ref, done_ref, vg_ref,
     dq_ref, dk_ref, dv_ref, dkv_ref,
     w_vmem, h_scr, act_scr, slope_scr, mid_scr, second_scr, datt_scr, dk_scr, dv_scr, sems) = refs
    width = x_ref.shape[1]
    copies = fetch_layer(sc_ref, (pieces,), plan, width, w_vmem, sems)
    ff_forward(8, 0, copies, w_vmem, att_ref, x_ref[...], vec_ref, out_ref, n2_ref, active_ref,
               slope_scr, mid_scr, second_scr, h_scr, act_scr)
    ff_backward(8, 0, w_vmem, att_ref, g_ref[...].astype(f32), vec_ref, slope_scr, mid_scr,
                second_scr, gmid_ref, dh_ref, dtwo_ref, done_ref, vg_ref, datt_scr)
    attention_backward(0, sc_ref, q_ref, k_ref, v_ref, datt_scr, dq_ref, dk_ref, dv_ref, dkv_ref,
                       dk_scr, dv_scr)


def encoder_forward_kernel(plan, sc_ref, *refs):
    groups, refs = split_refs(refs, (PIECES, PIECES))
    (halo_ref, x_ref, att_ref, vec_ref,
     out_ref, n2_ref, active_ref, slope_ref, mid_ref, second_ref,
     w_vmem, h_scr, act_scr, sems) = refs
    width = x_ref.shape[1]
    copies = fetch_layer(sc_ref, groups, plan, width, w_vmem, sems)
    stream = jnp.concatenate([halo_ref[HALO - EXTRA :, :], x_ref[...]], 0).astype(f32)
    ff_forward(0, EXTRA, copies, w_vmem, att_ref, stream, vec_ref, out_ref, n2_ref, active_ref,
               slope_ref, mid_ref, second_ref, h_scr, act_scr)


def encoder_backward_kernel(plan, sc_ref, *refs):
    groups, refs = split_refs(refs, (PIECES, PIECES))
    (att_ref, g_ref, vec_ref, slope_ref, mid_ref, second_ref, q_ref, k_ref, v_ref,
     gmid_ref, dh_ref, dtwo_ref, done_ref, vg_ref, dq_ref, dk_ref, dv_ref, dkv_ref,
     w_vmem, datt_scr, dk_scr, dv_scr, sems) = refs
    width = g_ref.shape[1]
    for copies in fetch_layer(sc_ref, groups, plan, width, w_vmem, sems):
        wait_all(copies)
    ff_backward(0, EXTRA, w_vmem, att_ref, g_ref[...], vec_ref, slope_ref, mid_ref, second_ref,
                gmid_ref, dh_ref, dtwo_ref, done_ref, vg_ref, datt_scr)
    attention_backward(EXTRA, sc_ref, q_ref, k_ref, v_ref, datt_scr, dq_ref, dk_ref, dv_ref,
                       dkv_ref, dk_scr, dv_scr)


def attention_backward(extra, sc_ref, q_ref, k_ref, v_ref, do_ref,
                       dq_ref, dk_ref, dv_ref, dkv_ref, dk_scr, dv_scr):
    start, cut = sc_ref[0], sc_ref[1]
    frames = do_ref.shape[0]
    lanes = head_lanes()
    scale = HEAD_DIM ** (-0.5)
    dk_scr[...] = jnp.zeros_like(dk_scr)
    dv_scr[...] = jnp.zeros_like(dv_scr)
    wide = GROUP * QUERIES
    for first in range(0, frames, QUERIES):
        lane = lax.broadcasted_iota(jnp.int32, (1, wide), 1) % QUERIES
        query = start + first + lane
        low = lowest_key(query, cut)
        key = start + first - HALO + lax.broadcasted_iota(jnp.int32, (WINDOW, wide), 0)
        mask = (key <= query) & (key >= low)
        for group in range(HEADS // GROUP):
            cols = slice(group * GROUP * HEAD_DIM, (group + 1) * GROUP * HEAD_DIM)
            qs = stack_heads(q_ref[extra + first : extra + first + QUERIES, cols], lanes)
            ds = stack_heads(do_ref[first : first + QUERIES, cols], lanes)
            kw = k_ref[first : first + WINDOW, cols]
            vw = v_ref[first : first + WINDOW, cols]
            scores = jnp.where(mask, mm_nt(kw, qs) * scale, -1e30)
            exponent = jnp.exp(scores - jnp.max(scores, 0, keepdims=True))
            probs = exponent * (1.0 / jnp.sum(exponent, 0, keepdims=True))
            d_probs = mm_nt(vw, ds)
            mean = jnp.sum(probs * d_probs, 0, keepdims=True)
            d_scores = (probs * (d_probs - mean)).astype(bf16)
            dk_scr[first : first + WINDOW, cols] += mm(d_scores, qs)
            dv_scr[first : first + WINDOW, cols] += mm(probs.astype(bf16), ds)
            dq_ref[first : first + QUERIES, cols] = (
                unstack_heads(mm_tn(d_scores, kw), lanes) * scale
            )
    width = dq_ref.shape[1]
    dkv_ref[:, :width] = (dk_scr[:HALO] * scale).astype(bf16)
    dkv_ref[:, width:] = dv_scr[:HALO].astype(bf16)
    dk_ref[...] = dk_scr[HALO:] * scale
    dv_ref[...] = dv_scr[HALO:]


class Packer:
    def __init__(self, core, refs, shares, order):
        self.core, self.refs, self.shares, self.order = core, refs, shares, order

    def put(self, value, at, step=1, phase=0, block0=0):
        if len(self.refs) == 1:
            if step == 1:
                self.refs[0][:, at : at + value.shape[1]] = value.astype(bf16)
            return
        send, keep = self.refs
        cols = slice(at, at + value.shape[1])
        rows = 16
        hi = self.shares // 8
        blocks = value.shape[0] // (rows * step)
        for pair in range(blocks // 2):
            even = value[(2 * pair * step + phase) * rows :][:rows]
            odd = value[((2 * pair + 1) * step + phase) * rows :][:rows]
            block = (block0 + 2 * pair) // 2
            place = {"x": (block % 2, 2), "lo": (block // 2 % 2, 2), "hi": (block // 4, hi)}
            at_row = 0
            for axis in self.order:
                at_row = at_row * place[axis][1] + place[axis][0]
            at_row = at_row * rows
            first = self.core == 0
            keep[at_row : at_row + rows, cols] = jnp.where(first, even, odd).astype(bf16)
            send[at_row : at_row + rows, cols] = jnp.where(first, odd, even).astype(bf16)

    def put_l2(self, value, at, chunk, width):
        if len(self.refs) == 1:
            cols = slice(at + chunk * width, at + (chunk + 1) * width)
            self.refs[0][:, cols] = value.astype(bf16)
            return
        for phase in range(4):
            self.put(value, at + phase * width, 4, phase, chunk * width // 64)


def linear_gradients(pack, n2_ref, active_ref, dh_ref, dtwo_ref):
    width = n2_ref.shape[1]
    for chunk in range(4):
        cols = slice(chunk * width, (chunk + 1) * width)
        pack.put_l2(mm_tn(active_ref[:, cols], dtwo_ref[...]), 0, chunk, width)
        pack.put(mm_tn(n2_ref[...], dh_ref[:, cols]), (4 + chunk) * width)


def decoder_gradients_kernel(shares, sc_ref, n2_ref, active_ref, dh_ref, dtwo_ref, att_ref, done_ref,
                             *refs):
    pack = Packer(sc_ref[2], refs, shares, ORDER_A)
    linear_gradients(pack, n2_ref, active_ref, dh_ref, dtwo_ref)
    pack.put(mm_tn(att_ref[...], done_ref[...]), 8 * n2_ref.shape[1])


def encoder_gradients_kernel(shares, sc_ref, n2_ref, active_ref, dh_ref, dtwo_ref, att_ref, done_ref,
                             win_ref, dred_ref, red_ref, dlat_ref, *refs):
    width = n2_ref.shape[1]
    half = len(refs) // 2
    linear_gradients(
        Packer(sc_ref[2], refs[:half], shares, ORDER_C_ONE), n2_ref, active_ref, dh_ref, dtwo_ref
    )
    pack = Packer(sc_ref[2], refs[half:], shares, ORDER_C_TWO)
    d_reduced = dred_ref[...]
    for tap in range(4):
        pack.put(mm_tn(win_ref[tap], d_reduced), tap * width)
    pack.put(mm_tn(att_ref[EXTRA:, :], done_ref[...]), 4 * width)
    pack.put(mm_tn(red_ref[...], dlat_ref[...]), 5 * width)


def layer_input_gradient(base, dq_ref, dk_ref, dv_ref, dkv_ref, x, gmid_ref,
                         w_in, vec_ref, cos_ref, sin_ref, dmix_ref, vg_ref):
    frames, width = dq_ref.shape
    later = frames - HALO
    cos, sin = cos_ref[HALO:], -sin_ref[HALO:]
    for at in range(0, width, 128):
        cols = slice(at, at + 128)
        dmix_ref[:, cols] = rotate(dq_ref[:, cols], cos, sin).astype(bf16)
        keys = dk_ref[:, cols]
        keys = jnp.concatenate([keys[:later], keys[later:] + dkv_ref[:, cols].astype(f32)], 0)
        dmix_ref[:, width + at : width + at + 128] = rotate(keys, cos, sin).astype(bf16)
        values = dv_ref[:, cols]
        moved = dkv_ref[:, width + at : width + at + 128].astype(f32)
        values = jnp.concatenate([values[:later], values[later:] + moved], 0)
        dmix_ref[:, 2 * width + at : 2 * width + at + 128] = values.astype(bf16)
    d_normed = mm_nt(dmix_ref[...], w_in[...])
    normal, scaled = normalize(x)
    vg_ref[0:1, :] = column_sum(d_normed * normal)
    vg_ref[1:2, :] = column_sum(d_normed)
    return gmid_ref[...] + norm_backward(d_normed, normal, scaled, vec_ref[base : base + 1])


def decoder_back_kernel(at, sc_ref, *refs):
    pieces, refs = refs[:PIECES], refs[PIECES:]
    (dq_ref, dk_ref, dv_ref, dkv_ref, x_ref, gmid_ref, vec_ref, cos_ref, sin_ref,
     dup_ref, dmix_ref, vg_ref, w_vmem, sems) = refs
    wait_all(fetch(sc_ref, pieces, at, w_vmem.shape[1], w_vmem, sems))
    grad = layer_input_gradient(
        8, dq_ref, dk_ref, dv_ref, dkv_ref, x_ref[...], gmid_ref, w_vmem, vec_ref,
        cos_ref, sin_ref, dmix_ref, vg_ref,
    )
    vg_ref[2:3, :] = column_sum(grad)
    dup_ref[...] = grad.astype(bf16)


def encoder_back_kernel(shares, sc_ref, *refs):
    (pieces,), refs = split_refs(refs, (PIECES,))
    (dq_ref, dk_ref, dv_ref, dkv_ref, x_ref, gmid_ref, vec_ref, cos_ref, sin_ref, n1_ref,
     vgs_ref, grad_ref, *rest) = refs
    refs, (w_vmem, dmix_scr, vg_scr, all_scr, sems) = rest[:-5], rest[-5:]
    width = x_ref.shape[1]
    wait_all(fetch(sc_ref, pieces, 0, w_vmem.shape[1], w_vmem, sems))
    grad = layer_input_gradient(
        0, dq_ref, dk_ref, dv_ref, dkv_ref, x_ref[...].astype(f32), gmid_ref, w_vmem,
        vec_ref, cos_ref, sin_ref, dmix_scr, vg_scr,
    )
    grad_ref[...] = grad.astype(bf16)
    pack = Packer(sc_ref[2], refs, shares, ORDER_D)
    for part in range(3):
        cols = slice(part * width, (part + 1) * width)
        pack.put(mm_tn(n1_ref[...], dmix_scr[:, cols]), part * width)
    all_scr[...] = jnp.zeros_like(all_scr)
    all_scr[0:2, :] = vg_scr[0:2, :]
    all_scr[2:6, :] = vgs_ref[0:4, :]
    all_scr[6:7, :] = vgs_ref[16:17, :]
    all_scr[7:8, :] = vgs_ref[26:27, :]
    all_scr[8:10, :] = vgs_ref[24:26, :]
    all_scr[10:14, :] = vgs_ref[8:12, :]
    pack.put(all_scr[...].T, 3 * width)


def middle_kernel(shares, sc_ref, *refs):
    (pieces, more), refs = split_refs(refs, (PIECES, PIECES))
    (dup_ref, next_ref, dmix_ref, n1_ref, restored_ref, qz_ref,
     denc_ref, dred_ref, dlat_ref, vg_ref, *rest) = refs
    refs, (up_vmem, down_vmem, frame_scr, sems) = rest[:-4], rest[-4:]
    frames, width = dup_ref.shape
    latent = qz_ref.shape[1]
    codec = frames // 2
    copies = [
        fetch(sc_ref, pieces, 0, latent + 4 * width, up_vmem, sems),
        fetch(sc_ref, more, 4 * width, 4 * width + latent, down_vmem, sems, PIECES),
    ]
    pairs = codec + 16
    even, odd = split_rows(
        jnp.concatenate([dup_ref[...], next_ref[...]], 0).astype(f32), frame_scr
    )
    both = jnp.concatenate([even, odd], 1).astype(bf16)
    wait_all(copies[0])
    up = up_vmem[:, latent : latent + 4 * width]
    here = mm_nt(both, up[:, : 2 * width])
    later = mm_nt(both, up[:, 2 * width :])
    d_restored = (here + pltpu.roll(later, pairs - 1, 0)).astype(bf16)
    d_latent = mm(d_restored, up_vmem[:, :latent]).astype(bf16)
    wait_all(copies[1])
    d_reduced = mm_nt(d_latent, down_vmem[:, 4 * width :]).astype(bf16)
    dlat_ref[...] = d_latent[:codec]
    dred_ref[...] = d_reduced[:codec]
    vg_ref[0:1, :] = column_sum(d_reduced[:codec].astype(f32))
    taps = [mm_nt(d_reduced, down_vmem[:, tap * width : (tap + 1) * width]) for tap in range(4)]
    denc_ref[...] = interleave(
        taps[2] + pltpu.roll(taps[0], pairs - 1, 0),
        taps[3] + pltpu.roll(taps[1], pairs - 1, 0),
        frame_scr,
    )[:frames]

    pack = Packer(sc_ref[2], refs, shares, ORDER_B)
    for part in range(3):
        cols = slice(part * width, (part + 1) * width)
        pack.put(mm_tn(n1_ref[...], dmix_ref[:, cols]), part * width)
    restored = restored_ref[...]
    own_pairs = both[:codec]
    before = pltpu.roll(restored.astype(f32), 1, 0)[16:].astype(bf16)
    pack.put(mm_tn(restored[16:], own_pairs[:, :width]), 3 * width)
    pack.put(mm_tn(restored[16:], own_pairs[:, width:]), 4 * width)
    pack.put(mm_tn(before, own_pairs[:, :width]), 5 * width)
    pack.put(mm_tn(before, own_pairs[:, width:]), 6 * width)
    pack.put(mm_tn(d_restored[:codec], qz_ref[CODE_HALO:, :]), 7 * width)


def latent_kernel(sc_ref, *refs):
    (pieces,), refs = split_refs(refs, (PIECES,))
    (enc_ref, rows_ref, vec_ref, res_ref, win_ref, red_ref, w_vmem, frame_scr, sems) = refs
    total, width = enc_ref.shape
    copies = fetch(sc_ref, pieces, 4 * width, w_vmem.shape[1], w_vmem, sems)
    inside = (sc_ref[0] > 0).astype(f32)
    rim = enc_ref[:EXTRA].astype(f32) * inside
    skip = EXTRA // 2
    even, odd = split_rows(jnp.concatenate([rim, enc_ref[EXTRA:].astype(f32)], 0), frame_scr)
    win_ref[0] = pltpu.roll(even, 1, 0)[skip:].astype(bf16)
    win_ref[1] = pltpu.roll(odd, 1, 0)[skip:].astype(bf16)
    win_ref[2] = even[skip:].astype(bf16)
    win_ref[3] = odd[skip:].astype(bf16)
    wait_all(copies)
    reduced = vec_ref[6:7]
    for tap in range(4):
        reduced = reduced + mm(win_ref[tap], w_vmem[:, tap * width : (tap + 1) * width])
    reduced = reduced.astype(bf16)
    red_ref[...] = reduced
    remaining = mm(reduced, w_vmem[:, 4 * width :])
    for level in range(rows_ref.shape[0]):
        res_ref[level] = remaining.astype(bf16)
        remaining = remaining - rows_ref[level].astype(f32)


def lookup_kernel(sc_ref, codes_ref, book_ref, qsend_ref, qkeep_ref, rsend_ref, rkeep_ref, q_scr):
    levels, share, latent = book_ref.shape
    total = codes_ref.shape[0]
    codec = total // 4
    base = sc_ref[3]
    core = sc_ref[2]
    entry = lax.broadcasted_iota(jnp.int32, (1, share), 1)
    for level in range(levels):
        picks = (codes_ref[:, level : level + 1] - base == entry).astype(f32).astype(bf16)
        found = mm(picks, book_ref[level])
        q_scr[CODE_HALO:] = found if level == 0 else q_scr[CODE_HALO:] + found
        for x in range(2):
            even = found[(2 * x) * codec :][:codec]
            odd = found[(2 * x + 1) * codec :][:codec]
            rkeep_ref[x, level] = jnp.where(core == 0, even, odd).astype(bf16)
            rsend_ref[x, level] = jnp.where(core == 0, odd, even).astype(bf16)
    q_scr[:CODE_HALO] = jnp.zeros((CODE_HALO, latent), f32)
    for x in range(2):
        even = q_scr[(2 * x) * codec : (2 * x + 1) * codec + CODE_HALO]
        odd = q_scr[(2 * x + 1) * codec : (2 * x + 2) * codec + CODE_HALO]
        qkeep_ref[x] = jnp.where(core == 0, even, odd)
        qsend_ref[x] = jnp.where(core == 0, odd, even)


def collect_kernel(share, seq_count, sc_ref, own_ref, x_ref, core_ref, far_ref, codes_ref,
                   marked_ref, send_ref, keep_ref, row_scr, cnt_scr):
    levels, codec, latent = own_ref.shape
    total = codes_ref.shape[1]
    lo = sc_ref[4]
    high = send_ref.shape[0]
    frame = lax.broadcasted_iota(jnp.int32, (1, total), 1) + sc_ref[6]
    row = lax.broadcasted_iota(jnp.int32, (2 * high * share, 1), 0)
    entry = (row // share * seq_count + sc_ref[5]) * share + row % share
    ones = jnp.ones((16, total), bf16)
    for level in range(levels):
        marked = marked_ref[:, level : level + 1]
        used = (entry == codes_ref[level : level + 1, :]).astype(f32)
        placed = (marked // 2 == frame).astype(f32)
        select = jnp.where(marked % 2 == 1, placed, used).astype(bf16)
        for place, ref in enumerate((own_ref, x_ref, core_ref, far_ref)):
            at_row = pl.multiple_of(sc_ref[14 + place], 32)
            row_scr[pl.ds(at_row, codec), :] = ref[level]
        sums = mm(select, row_scr[...])
        cnt_scr[level : level + 1, :] = mm_nt(ones, used.astype(bf16))[0:1]
        at = slice(level * share, (level + 1) * share)
        for h in range(high):
            even = sums[(2 * h) * share :][:share]
            odd = sums[(2 * h + 1) * share :][:share]
            keep_ref[h, at, :] = jnp.where(lo == 0, even, odd).astype(bf16)
            send_ref[h, at, :] = jnp.where(lo == 0, odd, even).astype(bf16)
    counts = cnt_scr[...]
    upper = jnp.floor(counts * (1.0 / 128.0))
    digits = jnp.concatenate([upper, counts - 128.0 * upper], 0)
    tail = slice(levels * share, levels * share + 2 * levels)
    for h in range(high):
        even = digits[:, (2 * h) * share : (2 * h + 1) * share]
        odd = digits[:, (2 * h + 1) * share : (2 * h + 2) * share]
        keep_ref[h, tail, :] = jnp.zeros((2 * levels, latent), bf16)
        send_ref[h, tail, :] = jnp.zeros((2 * levels, latent), bf16)
        keep_ref[h, tail, :share] = jnp.where(lo == 0, even, odd).astype(bf16)
        send_ref[h, tail, :share] = jnp.where(lo == 0, odd, even).astype(bf16)


def call(kernel, outs, spaces, scratch, args, micros):
    where = {"s": pltpu.SMEM, "v": pltpu.VMEM, "h": pltpu.HBM}
    title = getattr(kernel, "func", kernel).__name__
    return pl.pallas_call(
        kernel,
        name=title,
        out_shape=outs,
        in_specs=[pl.BlockSpec(memory_space=where[space]) for space in spaces],
        out_specs=[pl.BlockSpec(memory_space=pltpu.VMEM) for _ in outs],
        scratch_shapes=scratch,
        compiler_params=pltpu.CompilerParams(vmem_limit_bytes=VMEM_LIMIT),
        cost_estimate=pl.CostEstimate(
            flops=int(micros * 1e6), bytes_accessed=1, transcendentals=0
        ),
    )(*args)


def shape(dims, dtype=f32):
    return jax.ShapeDtypeStruct(dims, dtype)


def pick(block, at):
    zero = jnp.zeros((), jnp.uint32)
    start = (at,) + (zero,) * (block.ndim - 1)
    return lax.dynamic_slice(block, start, (1,) + block.shape[1:])[0]


def halve(block, axis, index, after=None):
    sent = pick(block, index["other " + axis])
    kept = pick(block, index[axis])
    got = lax.ppermute(sent, axis, [(0, 1), (1, 0)])
    if after is not None:
        got, _ = tie(got, after)
    return (kept.astype(f32) + got.astype(f32)).astype(block.dtype)


def sum_by_permutes(block, index, after=None):
    count = block.shape[0]
    if count != 4:
        return sum_over_hi(block)
    total = pick(block, index["hi"]).astype(f32)
    for turn in range(1, count):
        sent = pick(block, index["hi ^ %d" % turn])
        got = lax.ppermute(sent, "hi", [(i, i ^ turn) for i in range(count)])
        if after is not None:
            got, _ = tie(got, after)
        total = total + got.astype(f32)
    return total


def swap_add(send, keep, axis, after=None):
    got = lax.ppermute(send, axis, [(0, 1), (1, 0)])
    if after is not None:
        got, _ = tie(got, after)
    return (keep.astype(f32) + got.astype(f32)).astype(keep.dtype)


def sum_over_hi(block):
    parts = lax.all_to_all(block, "hi", 0, 0, tiled=True)
    return jnp.sum(parts.astype(f32), 0)


def shifted(block, distance):
    devices = range(lax.axis_size(SEQ))
    route = [(i - distance, i) for i in devices if i - distance in devices]
    return lax.ppermute(block, SEQ, route)


def packed_outs(width_total, width, shares):
    if width // shares % 16 == 0:
        return [shape((width // 2, width_total), bf16)] * 2
    return [shape((width, width_total), bf16)]


def swap(block, axis):
    return lax.ppermute(block, axis, [(0, 1), (1, 0)])


def tie(*values):
    return lax.optimization_barrier(values)


def half_of(share, index):
    rows = share.shape[0] // 2
    zero = jnp.zeros((), jnp.uint32)
    return lax.dynamic_slice(share, (index["lo"] * rows, zero), (rows, share.shape[1]))


def both_halves(near, far, index):
    first = index["lo"] == 0
    return jnp.concatenate([jnp.where(first, near, far), jnp.where(first, far, near)], 0)


def unfolded_rows(block, shares, l2_at):
    width = block.shape[0]
    full = [block[:, l2_at + i * width : l2_at + (i + 1) * width] for i in range(4)]
    full = jnp.concatenate(full, 0).reshape(shares, 4, width // shares, width)
    full = full.transpose(0, 2, 1, 3).reshape(width, 4 * width)
    return jnp.concatenate([block[:, :l2_at], full, block[:, l2_at + 4 * width :]], 1)


def first_sum(parts, shares, order, index, l2_at=None):
    if len(parts) == 2:
        return swap_add(*parts, "core")
    (block,) = parts
    if l2_at is not None:
        block = unfolded_rows(block, shares, l2_at)
    width, total = block.shape
    block = block.reshape(shares // 8, 2, 2, 2, width // shares, total)
    block = halve(block.transpose(3, 0, 1, 2, 4, 5), "core", index)
    places = [("hi", "lo", "x").index(axis) for axis in order]
    return block.transpose(*places, 3, 4).reshape(width // 2, total)


def next_sum(block, axis, index, after=None):
    rows, total = block.shape
    return halve(block.reshape(2, rows // 2, total), axis, index, after)


def last_sum(block, high):
    return sum_over_hi(block.reshape(high, -1, block.shape[1]))


def local(
    activations,
    encoder_attention_norm_gain,
    encoder_attention_norm_bias,
    encoder_query_key_value_weight,
    encoder_attention_output_weight,
    encoder_attention_layer_scale,
    encoder_forward_norm_gain,
    encoder_forward_norm_bias,
    encoder_forward_input_weight,
    encoder_forward_output_weight,
    encoder_forward_layer_scale,
    strided_convolution_weight,
    strided_convolution_bias,
    quantizer_input_weight,
    codebook,
    quantizer_output_weight,
    transposed_convolution_weight,
    transposed_convolution_bias,
    decoder_attention_norm_gain,
    decoder_attention_norm_bias,
    decoder_query_key_value_weight,
    decoder_attention_output_weight,
    decoder_attention_layer_scale,
    decoder_forward_norm_gain,
    decoder_forward_norm_bias,
    decoder_forward_input_weight,
    decoder_forward_output_weight,
    decoder_forward_layer_scale,
    cotangent,
    frame_segment_index,
    frame_code_index,
    replace_code_mask,
    replacing_batch_position,
    code_usage_average,
    code_latent_sum_average,
):
    batch_rows, frames, width = activations.shape
    assert batch_rows == 1
    seq_index = lax.axis_index(SEQ)
    seq_count = lax.axis_size(SEQ)
    dp_index = lax.axis_index(DP)
    dp_count = lax.axis_size(DP)
    shares = dp_count * seq_count
    codec = frames // 2
    levels = frame_code_index.shape[2]
    latent = codebook.shape[2]
    book_share = codebook.shape[1]
    core_index = lax.axis_index("core")

    x_index, lo_index = lax.axis_index("x"), lax.axis_index("lo")
    rows_share = width // seq_count
    high = shares // 8
    total_frames = HALO + frames
    code_total = replace_code_mask.shape[1]
    code_share = code_usage_average.shape[1]
    row_frames = codec * seq_count

    vectors = jnp.stack(
        [
            encoder_attention_norm_gain,
            encoder_attention_norm_bias,
            encoder_attention_layer_scale,
            encoder_forward_norm_gain,
            encoder_forward_norm_bias,
            encoder_forward_layer_scale,
            strided_convolution_bias,
            transposed_convolution_bias,
            decoder_attention_norm_gain,
            decoder_attention_norm_bias,
            decoder_attention_layer_scale,
            decoder_forward_norm_gain,
            decoder_forward_norm_bias,
            decoder_forward_layer_scale,
        ]
    )
    vectors = jnp.pad(vectors, ((0, 2), (0, 0)))
    small = jnp.concatenate(
        [frame_code_index.reshape(-1).astype(f32), vectors.reshape(-1).astype(f32)]
    )
    index = {}
    unsigned = jnp.uint32
    for axis in ("x", "lo", "core"):
        index[axis] = lax.axis_index(axis).astype(unsigned)
        index["other " + axis] = (1 - lax.axis_index(axis)).astype(unsigned)
    index["hi"] = lax.axis_index("hi").astype(unsigned)
    index["seq"] = lax.axis_index(SEQ).astype(unsigned)
    index["owner"] = (lax.axis_index(DP + SEQ) * code_share).astype(unsigned)
    for turn in range(1, 4):
        index["hi ^ %d" % turn] = lax.axis_index("hi").astype(unsigned) ^ unsigned(turn)
    def flat_taps(taps):
        return taps.transpose(1, 0, 2).reshape(taps.shape[1], -1)

    def fold_l2(share):
        return share.reshape(4, -1, width).transpose(1, 0, 2).reshape(-1, 4 * width)

    dec_one = jnp.concatenate(
        [
            quantizer_output_weight.T,
            flat_taps(transposed_convolution_weight),
            decoder_query_key_value_weight,
        ],
        1,
    )
    dec_two = jnp.concatenate(
        [
            decoder_attention_output_weight,
            decoder_forward_input_weight,
            fold_l2(decoder_forward_output_weight),
        ],
        1,
    )
    half_one, half_two = half_of(dec_one, index), half_of(dec_two, index)
    small, half_one, half_two = tie(small, half_one, half_two)
    small = lax.all_gather(small, SEQ, axis=0, tiled=False)
    names = sorted(index)
    *index_values, small = tie(*[index[name] for name in names], small)
    index = dict(zip(names, index_values))
    code_count = codec * levels
    row_codes = small[:, :code_count].astype(jnp.int32).reshape(seq_count, codec, levels)
    vectors = small[:, code_count:].reshape(seq_count, 16, -1).transpose(1, 0, 2).reshape(16, width)
    order = [2 * x_index + core_index, 2 * (1 - x_index) + core_index]
    order += [2 * x_index + 1 - core_index, 2 * (1 - x_index) + 1 - core_index]
    cut = jnp.sum((frame_segment_index[0] == 0).astype(jnp.int32))
    scalars = jnp.stack(
        [
            seq_index * frames,
            cut,
            core_index,
            seq_index * book_share,
            lo_index,
            seq_index,
            dp_index * row_frames,
            seq_index,
        ]
        + [
            *[place * rows_share for place in order],
            seq_index,
            seq_index,
        ]
        + [place * codec for place in order]
    ).astype(jnp.int32)

    half_one, _ = tie(half_one, small)
    near_one = swap(half_one, "x")
    core_one = swap(dec_one, "core")
    activation_halo = shifted(activations[0, frames - HALO :], 1)

    positions = seq_index * frames - HALO + jnp.arange(total_frames, dtype=jnp.int32)
    half_dim = HEAD_DIM // 2
    frequency = jnp.power(10000.0, -jnp.arange(half_dim, dtype=f32) / half_dim)

    def angle_tables(positions):
        angles = positions.astype(f32)[:, None] * frequency[None, :]
        cos, sin = jnp.cos(angles), jnp.sin(angles)
        return jnp.concatenate([cos] * 4, 1), jnp.concatenate([-sin, sin, -sin, sin], 1)

    row_codes, activation_halo, core_one = tie(row_codes, activation_halo, core_one)

    window = codec + CODE_HALO
    qsend, qkeep, rsend, rkeep = call(
        lookup_kernel,
        [shape((2, window, latent))] * 2 + [shape((2, levels, codec, latent), bf16)] * 2,
        "svv",
        [pltpu.VMEM((CODE_HALO + codec * seq_count, latent), f32)],
        (scalars, row_codes.reshape(-1, levels), codebook),
        4,
    )
    q_sum = swap_add(qsend, qkeep, "core")
    q_sent = pick(q_sum, index["other x"])
    q_got = swap(q_sent, "x")
    (near_one, positions, half_two, enc_in, enc_l2, down_share, replace_code_mask,
     replacing_batch_position, row_codes, _) = tie(
        near_one, positions, half_two, encoder_query_key_value_weight,
        encoder_forward_output_weight, strided_convolution_weight, replace_code_mask,
        replacing_batch_position, row_codes, q_sent,
    )
    enc_one = jnp.concatenate(
        [
            enc_in,
            encoder_attention_output_weight,
            flat_taps(down_share),
            quantizer_input_weight,
        ],
        1,
    )
    enc_two = jnp.concatenate([encoder_forward_input_weight, fold_l2(enc_l2)], 1)
    marked = (replacing_batch_position * 2 + replace_code_mask).T
    marked = marked.reshape(dp_count, seq_count, code_share, levels).transpose(1, 0, 2, 3)
    marked = pick(marked, index["seq"]).reshape(dp_count * code_share, levels)
    code_columns = row_codes.reshape(row_frames, levels).T
    owner_flag = lax.dynamic_slice(
        replace_code_mask, (jnp.zeros((), unsigned), index["owner"]), (levels, code_share)
    ) == 1
    far_one = swap(near_one, "lo")
    near_one = both_halves(near_one, far_one, index)
    dec_one = [dec_one, near_one, core_one, swap(near_one, "core")]
    cos_table, sin_table = angle_tables(positions)
    near_two = swap(half_two, "x")
    quantized = (pick(q_sum, index["x"]) + q_got).astype(bf16)
    half_three, half_four = half_of(enc_one, index), half_of(enc_two, index)
    (quantized, near_two, half_three, half_four, activation_halo, cos_table, sin_table, marked,
     code_columns, owner_flag) = tie(
        quantized, near_two, half_three, half_four, activation_halo, cos_table, sin_table, marked,
        code_columns, owner_flag,
    )
    core_two = swap(dec_two, "core")
    far_two = swap(near_two, "lo")
    near_three = swap(half_three, "x")

    d_x, restored, d_n1, d_q, d_k, d_v, d_att = call(
        decoder_front_kernel,
        [
            shape((frames, width)),
            shape((codec + 16, width), bf16),
            shape((frames, width), bf16),
            shape((frames, width), bf16),
            shape((total_frames, width), bf16),
            shape((total_frames, width), bf16),
            shape((frames, width), bf16),
        ],
        "s" + "h" * PIECES + "vvvv",
        [
            pltpu.VMEM((width, latent + 7 * width), bf16),
            pltpu.VMEM((width // 128, total_frames, 128), f32),
            pltpu.SemaphoreType.DMA((PIECES,)),
        ],
        (scalars, *dec_one, quantized, vectors, cos_table, sin_table),
        8,
    )
    d_att, far_two, near_three, half_four, rsend = tie(
        d_att, far_two, near_three, half_four, rsend
    )
    code_rows = swap_add(rsend, rkeep, "core")
    near_two = both_halves(near_two, far_two, index)
    dec_two = [dec_two, near_two, core_two, swap(near_two, "core")]
    far_three = swap(near_three, "lo")
    near_four = swap(half_four, "x")
    layer_scratch = [
        pltpu.VMEM((frames, width), bf16),
        pltpu.VMEM((total_frames, width), f32),
        pltpu.VMEM((total_frames, width), f32),
        pltpu.SemaphoreType.DMA((3 * PIECES,)),
    ]
    forward_outs = [shape((frames, width), bf16), shape((frames, 4 * width), bf16)]
    kept_outs = [shape((frames, 4 * width)), shape((frames, width)), shape((frames, width))]
    backward_outs = [
        shape((frames, width)),
        shape((frames, 4 * width), bf16),
        shape((frames, width), bf16),
        shape((frames, width), bf16),
        shape((8, width)),
        shape((frames, width)),
        shape((frames, width)),
        shape((frames, width)),
        shape((HALO, 2 * width), bf16),
    ]
    weights_scratch = pltpu.VMEM((width, 9 * width), bf16)
    (output, d_n2, d_active, d_gmid, d_dh, d_dtwo, d_done, d_vg_two, d_dq, d_dk, d_dv, d_dkv) = call(
        partial(decoder_layer_kernel, ((0, 0), (0, width), (0, 5 * width))),
        [shape((frames, width), bf16)] + forward_outs + backward_outs,
        "s" + "h" * PIECES + "vvvvvvv",
        [
            weights_scratch,
            pltpu.VMEM((frames, width), f32),
            pltpu.VMEM((frames, 4 * width), bf16),
            pltpu.VMEM((frames, 4 * width), f32),
            pltpu.VMEM((frames, width), f32),
            pltpu.VMEM((frames, width), f32),
        ]
        + layer_scratch,
        (scalars, *dec_two, d_att, d_x, cotangent[0], vectors, d_q, d_k, d_v),
        14,
    )
    d_n2, far_three, near_four, code_rows = tie(d_n2, far_three, near_four, code_rows)
    near_three = both_halves(near_three, far_three, index)
    enc_one = [enc_one, near_three, swap(enc_one, "core"), swap(near_three, "core")]
    far_four = swap(near_four, "lo")
    d_dkv = shifted(d_dkv, -1)
    group_a = call(
        partial(decoder_gradients_kernel, shares),
        packed_outs(9 * width, width, shares),
        "svvvvvv",
        [],
        (scalars, d_n2, d_active, d_dh, d_dtwo, d_att, d_done),
        5,
    )
    d_dq, *group_a = tie(d_dq, *group_a)
    code_rows, d_dkv = tie(code_rows, d_dkv)
    code_rows = halve(code_rows, "x", index)
    a_sum = first_sum(group_a, shares, ORDER_A, index, 0)
    d_up, d_mixed, d_vg_one = call(
        partial(decoder_back_kernel, latent + 4 * width),
        [shape((frames, width), bf16), shape((frames, 3 * width), bf16), shape((8, width))],
        "s" + "h" * PIECES + "v" * 9,
        [pltpu.VMEM((width, 3 * width), bf16), pltpu.SemaphoreType.DMA((PIECES,))],
        (
            scalars, *dec_one, d_dq, d_dk, d_dv, d_dkv, d_x, d_gmid, vectors, cos_table,
            sin_table,
        ),
        4,
    )
    d_up_next = shifted(d_up[:32], -1)


    a_sum, d_up, e_input, far_four, code_rows = tie(
        a_sum, d_up, activations[0], far_four, code_rows
    )
    near_four = both_halves(near_four, far_four, index)
    enc_two = [enc_two, near_four, swap(enc_two, "core"), swap(near_four, "core")]
    a_sum = next_sum(a_sum, ORDER_A[0], index)
    e_n1, e_q, e_k, e_v, e_att = call(
        encoder_front_kernel,
        [
            shape((frames, width), bf16),
            shape((frames + EXTRA, width), bf16),
            shape((total_frames, width), bf16),
            shape((total_frames, width), bf16),
            shape((frames + EXTRA, width), bf16),
        ],
        "s" + "h" * PIECES + "vvvvv",
        [pltpu.VMEM((width, 3 * width), bf16), pltpu.SemaphoreType.DMA((PIECES,))],
        (scalars, *enc_one, activation_halo, e_input, vectors, cos_table, sin_table),
        7,
    )

    d_mixed, e_n1 = tie(d_mixed, e_n1)
    middle_outs = call(
        partial(middle_kernel, shares),
        [
            shape((frames, width)),
            shape((codec, width), bf16),
            shape((codec, latent), bf16),
            shape((8, width)),
        ]
        + packed_outs(7 * width + latent, width, shares),
        "s" + "h" * (2 * PIECES) + "" + "v" * 6,
        [
            pltpu.VMEM((width, latent + 4 * width), bf16),
            pltpu.VMEM((width, latent + 4 * width), bf16),
            pltpu.VMEM((width // 128, frames + 32, 128), f32),
            pltpu.SemaphoreType.DMA((2 * PIECES,)),
        ],
        (scalars, *dec_one, *enc_one, d_up, d_up_next, d_mixed, d_n1, restored, quantized),
        7,
    )
    d_encoded, d_reduced, d_latent, m_vg = middle_outs[:4]
    b_sum = first_sum(middle_outs[4:], shares, ORDER_B, index)

    e_att, d_encoded = tie(e_att, d_encoded)
    enc_plan = ((0, 3 * width), (1, 0), (1, 4 * width))
    rows = frames + EXTRA
    encoded, e_n2, e_active, e_slope, e_mid, e_second = call(
        partial(encoder_forward_kernel, enc_plan),
        [shape((rows, width), bf16)] + forward_outs + kept_outs,
        "s" + "h" * (2 * PIECES) + "vvvv",
        [
            weights_scratch,
            pltpu.VMEM((rows, width), f32),
            pltpu.VMEM((rows, 4 * width), bf16),
            pltpu.SemaphoreType.DMA((3 * PIECES,)),
        ],
        (scalars, *enc_one, *enc_two, activation_halo, e_input, e_att, vectors),
        6,
    )
    encoded, b_sum, a_sum = tie(encoded, b_sum, a_sum)
    b_sum = next_sum(b_sum, ORDER_B[0], index)
    residuals, windows, reduced = call(
        latent_kernel,
        [
            shape((levels, codec, latent), bf16),
            shape((4, codec, width), bf16),
            shape((codec, width), bf16),
        ],
        "s" + "h" * PIECES + "vvv",
        [
            pltpu.VMEM((width, 4 * width + latent), bf16),
            pltpu.VMEM((width // 128, frames + EXTRA, 128), f32),
            pltpu.SemaphoreType.DMA((PIECES,)),
        ],
        (scalars, *enc_one, encoded, code_rows, vectors),
        3,
    )
    near_res = swap(residuals, "x")
    core_res = swap(residuals, "core")

    d_encoded, _ = tie(d_encoded, residuals)
    a_sum = next_sum(a_sum, ORDER_A[1], index)
    (e_gmid, e_dh, e_dtwo, e_done, e_vg_two, e_dq, e_dk, e_dv, e_dkv) = call(
        partial(encoder_backward_kernel, enc_plan),
        backward_outs,
        "s" + "h" * (2 * PIECES) + "v" * 9,
        [weights_scratch] + layer_scratch,
        (
            scalars, *enc_one, *enc_two, e_att, d_encoded, vectors, e_slope, e_mid, e_second,
            e_q, e_k, e_v,
        ),
        11,
    )
    e_dkv = shifted(e_dkv, -1)
    near_res, core_res, _ = tie(near_res, core_res, e_gmid)
    res_pieces = [residuals, near_res, core_res, swap(near_res, "core")]

    if code_share % 16 == 0:
        tail_rows = levels * code_share
        csend, ckeep = call(
            partial(collect_kernel, code_share, seq_count),
            [shape((dp_count // 2, tail_rows + 2 * levels, latent), bf16)] * 2,
            "svvvvvv",
            [
                pltpu.VMEM((row_frames, latent), bf16),
                pltpu.VMEM((levels, dp_count * code_share), f32),
            ],
            (scalars, *res_pieces, code_columns, marked),
            5,
        )
        e_n2, csend, e_gmid = tie(e_n2, csend, e_gmid)
    c_outs = packed_outs(8 * width, width, shares)
    group_c = call(
        partial(encoder_gradients_kernel, shares),
        c_outs + packed_outs(5 * width + latent, width, shares),
        "s" + "v" * 10,
        [],
        (
            scalars, e_n2, e_active, e_dh, e_dtwo, e_att, e_done, windows, d_reduced, reduced,
            d_latent,
        ),
        5,
    )
    e_dq, *group_c = tie(e_dq, *group_c)
    c_one = first_sum(group_c[: len(c_outs)], shares, ORDER_C_ONE, index, 0)
    c_two = first_sum(group_c[len(c_outs) :], shares, ORDER_C_TWO, index)
    e_dq, c_one, c_two, a_sum, b_sum = tie(e_dq, c_one, c_two, a_sum, b_sum)
    vector_grads = jnp.concatenate([e_vg_two, d_vg_two, m_vg, d_vg_one], 0)
    grad_outs = call(
        partial(encoder_back_kernel, shares),
        [shape((frames, width), bf16)] + packed_outs(3 * width + 128, width, shares),
        "s" + "h" * PIECES + "v" * 11,
        [
            pltpu.VMEM((width, 3 * width), bf16),
            pltpu.VMEM((frames, 3 * width), bf16),
            pltpu.VMEM((8, width), f32),
            pltpu.VMEM((128, width), f32),
            pltpu.SemaphoreType.DMA((PIECES,)),
        ],
        (
            scalars, *enc_one, e_dq, e_dk, e_dv, e_dkv, e_input, e_gmid, vectors,
            cos_table, sin_table, e_n1, vector_grads,
        ),
        5,
    )
    activations_grad = grad_outs[0]

    def z_sum(block):
        return sum_by_permutes(block.reshape(high, -1, block.shape[1]), index, activations_grad)

    grads_a = z_sum(a_sum)
    d_sum = first_sum(grad_outs[1:], shares, ORDER_D, index)
    b_sum = next_sum(b_sum, ORDER_B[1], index, d_sum)
    if code_share % 16 == 0:
        combined = swap_add(csend, ckeep, "lo", b_sum)
        c_one = next_sum(c_one, ORDER_C_ONE[0], index, combined)
        combined = sum_by_permutes(combined, index)
        summed = combined[:tail_rows].reshape(levels, code_share, latent)
        digits = combined[tail_rows:, :code_share]
        counted = 128.0 * digits[:levels] + digits[levels:]
    else:
        entry = (
            jnp.arange(dp_count, dtype=jnp.int32)[:, None] * seq_count + seq_index
        ) * code_share + jnp.arange(code_share, dtype=jnp.int32)
        relative = [place * codec + jnp.arange(codec, dtype=jnp.int32) for place in order]
        relative = jnp.concatenate(relative)
        flat_res = jnp.concatenate(res_pieces, 1)
        used = entry.reshape(1, -1, 1) == code_columns[:, None, relative]
        placed = (marked.T // 2)[:, :, None] == dp_index * row_frames + relative
        counts = jnp.sum(used.astype(f32), 2).reshape(levels, dp_count, code_share)
        selects = jnp.where((marked.T % 2)[:, :, None] == 1, placed, used).astype(bf16)
        sums = jnp.einsum("lct,ltd->lcd", selects, flat_res, preferred_element_type=f32)
        sums = sums.astype(bf16).reshape(levels, dp_count, code_share, latent)
        c_one = next_sum(c_one, ORDER_C_ONE[0], index)
        summed = lax.psum_scatter(sums, DP, scatter_dimension=1, tiled=False).astype(f32)
        counted = lax.psum_scatter(counts, DP, scatter_dimension=1, tiled=False)
    c_two = next_sum(c_two, ORDER_C_TWO[0], index, c_one)
    d_sum = next_sum(d_sum, ORDER_D[0], index, c_two)
    c_two = next_sum(c_two, ORDER_C_TWO[1], index, d_sum)
    d_sum = next_sum(d_sum, ORDER_D[1], index, c_two)
    c_one = next_sum(c_one, ORDER_C_ONE[1], index, d_sum)
    grads_b = last_sum(b_sum, high)
    edge, far_edge = c_one.shape[1], c_one.shape[1] + c_two.shape[1]
    together = last_sum(jnp.concatenate([c_one, c_two, d_sum], 1), high)
    grads_c, grads_c_two, grads_d = (
        together[:, :edge], together[:, edge:far_edge], together[:, far_edge:]
    )

    new_cluster_size = ema_decay * code_usage_average + (1.0 - ema_decay) * counted
    new_embed_sum = jnp.where(
        owner_flag[:, :, None],
        summed * new_cluster_size[:, :, None],
        ema_decay * code_latent_sum_average + (1.0 - ema_decay) * summed,
    )
    new_codebook = new_embed_sum / new_cluster_size[:, :, None]

    def columns(block, at, count):
        return block[:, at * width : (at + count) * width]

    def taps(block):
        return block.reshape(-1, 4, width).transpose(1, 0, 2)

    def unfold(block):
        return block.reshape(-1, 4, width).transpose(1, 0, 2).reshape(-1, width)

    vec = grads_d[:, 3 * width : 3 * width + 16].T
    return (
        output[None],
        activations_grad[None],
        vec[0],
        vec[1],
        columns(grads_d, 0, 3),
        columns(grads_c_two, 4, 1),
        vec[2],
        vec[3],
        vec[4],
        columns(grads_c, 4, 4),
        unfold(columns(grads_c, 0, 4)),
        vec[5],
        taps(columns(grads_c_two, 0, 4)),
        vec[6],
        grads_c_two[:, 5 * width :],
        grads_b[:, 7 * width :].T,
        taps(columns(grads_b, 3, 4)),
        vec[7],
        vec[8],
        vec[9],
        columns(grads_b, 0, 3),
        columns(grads_a, 8, 1),
        vec[10],
        vec[11],
        vec[12],
        columns(grads_a, 4, 4),
        unfold(columns(grads_a, 0, 4)),
        vec[13],
        new_cluster_size,
        new_embed_sum,
        new_codebook,
    )


def solution(mesh):
    grid = mesh.devices
    mesh = jax.sharding.Mesh(
        grid.reshape(grid.shape[0] // 2, 2, grid.shape[1] // 2, 2), ("hi", "lo", "x", "core")
    )
    placed = (
        P(DP, SEQ, None),
        P(SEQ),
        P(SEQ),
        P(SEQ, None),
        P(SEQ, None),
        P(SEQ),
        P(SEQ),
        P(SEQ),
        P(SEQ, None),
        P(SEQ, None),
        P(SEQ),
        P(None, SEQ, None),
        P(SEQ),
        P(SEQ, None),
        P(None, SEQ, None),
        P(None, SEQ),
        P(None, SEQ, None),
        P(SEQ),
        P(SEQ),
        P(SEQ),
        P(SEQ, None),
        P(SEQ, None),
        P(SEQ),
        P(SEQ),
        P(SEQ),
        P(SEQ, None),
        P(SEQ, None),
        P(SEQ),
        P(DP, SEQ, None),
        P(DP, None),
        P(DP, SEQ, None),
        P(),
        P(),
        P(None, DP + SEQ),
        P(None, DP + SEQ, None),
    )
    return jax.shard_map(
        local,
        mesh=mesh,
        in_specs=placed,
        out_specs=(
            P(DP, SEQ, None),
            P(DP, SEQ, None),
            P(DP + SEQ),
            P(DP + SEQ),
            P(DP + SEQ, None),
            P(DP + SEQ, None),
            P(DP + SEQ),
            P(DP + SEQ),
            P(DP + SEQ),
            P(DP + SEQ, None),
            P(DP + SEQ, None),
            P(DP + SEQ),
            P(None, DP + SEQ, None),
            P(DP + SEQ),
            P(DP + SEQ, None),
            P(None, DP + SEQ),
            P(None, DP + SEQ, None),
            P(DP + SEQ),
            P(DP + SEQ),
            P(DP + SEQ),
            P(DP + SEQ, None),
            P(DP + SEQ, None),
            P(DP + SEQ),
            P(DP + SEQ),
            P(DP + SEQ),
            P(DP + SEQ, None),
            P(DP + SEQ, None),
            P(DP + SEQ),
            P(None, DP + SEQ),
            P(None, DP + SEQ, None),
            P(None, DP + SEQ, None),
        ),
        check_vma=False,
    )
```

```python
from functools import partial

import jax
import jax.numpy as jnp
from jax import lax
from jax.experimental import pallas as pl
from jax.experimental.pallas import tpu as pltpu
from jax.sharding import PartitionSpec as P

HEADS = 8
HEAD_DIM = 64
CONTEXT = 250
HALO = 256
CODE_HALO = HALO // 2 + 16
EXTRA = 16
QUERIES = 64
GROUP = 4
WINDOW = HALO + QUERIES
VMEM_LIMIT = 26 * 1024 * 1024
ORDER_A = ("lo", "x", "hi")
ORDER_B = ("lo", "x", "hi")
ORDER_C_ONE = ("x", "lo", "hi")
ORDER_C_TWO = ("lo", "x", "hi")
ORDER_D = ("lo", "x", "hi")
DP = ("hi", "lo")
SEQ = ("x", "core")

norm_eps = 1e-05
ema_decay = 0.9
bf16 = jnp.bfloat16
f32 = jnp.float32


PIECES = 4


def fetch(sc_ref, pieces, at, width, dst, sems, first=0):
    copies = []
    for i, piece in enumerate(pieces):
        rows = piece.shape[0]
        row = pl.multiple_of(sc_ref[8 + i], 128)
        copies.append(
            pltpu.make_async_copy(
                piece.at[:, at : at + width], dst.at[pl.ds(row, rows), :], sems.at[first + i]
            )
        )
        copies[-1].start()
    return copies


def split_refs(refs, counts):
    groups = []
    for count in counts:
        groups.append(refs[:count])
        refs = refs[count:]
    return groups, refs


def wait_all(copies):
    for copy in copies:
        copy.wait()


def mm(a, b):
    return jnp.dot(a, b, preferred_element_type=f32)


def mm_nt(a, b):
    return lax.dot_general(a, b, (((1,), (1,)), ((), ())), preferred_element_type=f32)


def mm_tn(a, b):
    return lax.dot_general(a, b, (((0,), (0,)), ((), ())), preferred_element_type=f32)


def normalize(stream):
    center = stream - jnp.mean(stream, -1, keepdims=True)
    scaled = lax.rsqrt(jnp.mean(center * center, -1, keepdims=True) + norm_eps)
    return center * scaled, scaled


def norm_backward(upstream, normal, scaled, gain):
    inner = upstream * gain
    return scaled * (
        inner
        - jnp.mean(inner, -1, keepdims=True)
        - normal * jnp.mean(inner * normal, -1, keepdims=True)
    )


def column_sum(value):
    return jnp.sum(value, 0, keepdims=True)


def interleave(even, odd, scr):
    tiles, rows, _ = scr.shape
    for tile in range(tiles):
        cols = slice(tile * 128, (tile + 1) * 128)
        scr[tile, pl.ds(0, rows // 2, stride=2), :] = even[:, cols]
        scr[tile, pl.ds(1, rows // 2, stride=2), :] = odd[:, cols]
    return jnp.concatenate([scr[tile] for tile in range(tiles)], 1)


def split_rows(value, scr):
    tiles, rows, _ = scr.shape
    for tile in range(tiles):
        scr[tile] = value[:, tile * 128 : (tile + 1) * 128]
    even = [scr[tile, pl.ds(0, rows // 2, stride=2), :] for tile in range(tiles)]
    odd = [scr[tile, pl.ds(1, rows // 2, stride=2), :] for tile in range(tiles)]
    return jnp.concatenate(even, 1), jnp.concatenate(odd, 1)


def first_half():
    lane = lax.broadcasted_iota(jnp.int32, (1, 128), 1)
    return lane % HEAD_DIM < HEAD_DIM // 2


def rotate(tile, cos, sin):
    swapped = jnp.where(first_half(), pltpu.roll(tile, 96, 1), pltpu.roll(tile, 32, 1))
    return tile * cos + swapped * sin


def head_lanes():
    lane = lax.broadcasted_iota(jnp.int32, (1, GROUP * HEAD_DIM), 1) // HEAD_DIM
    return [(lane == head) for head in range(GROUP)]


def stack_heads(block, lanes):
    return jnp.concatenate([block * mask.astype(bf16) for mask in lanes], 0)


def unstack_heads(block, lanes):
    rows = block.shape[0] // GROUP
    out = block[:rows]
    for head in range(1, GROUP):
        out = jnp.where(lanes[head], block[head * rows : (head + 1) * rows], out)
    return out


def lowest_key(query, cut):
    low = jnp.maximum(query - (CONTEXT - 1), 0)
    return jnp.where(query >= cut, jnp.maximum(low, cut), low)


def attend(q_ref, k_ref, v_ref, att_ref, sc_ref, rows, first_query, first_key, keys, at_row):
    start, cut = sc_ref[0], sc_ref[1]
    query = start + first_query + lax.broadcasted_iota(jnp.int32, (rows, 1), 0)
    low = lowest_key(query, cut)
    key = start + first_key + lax.broadcasted_iota(jnp.int32, (rows, keys), 1)
    mask = (key <= query) & (key >= low)
    mask = jnp.concatenate([mask] * GROUP, 0)
    lanes = head_lanes()
    key_row = first_key + HALO
    for group in range(HEADS // GROUP):
        cols = slice(group * GROUP * HEAD_DIM, (group + 1) * GROUP * HEAD_DIM)
        stacked = stack_heads(q_ref[at_row : at_row + rows, cols], lanes)
        scores = mm_nt(stacked, k_ref[key_row : key_row + keys, cols]) * HEAD_DIM ** (-0.5)
        scores = jnp.where(mask, scores, -1e30)
        exponent = jnp.exp(scores - jnp.max(scores, -1, keepdims=True))
        weights = exponent * (1.0 / jnp.sum(exponent, -1, keepdims=True))
        mixed = mm(weights.astype(bf16), v_ref[key_row : key_row + keys, cols])
        att_ref[at_row : at_row + rows, cols] = unstack_heads(mixed, lanes).astype(bf16)


def front(x, vec_ref, base, w_in, cos_ref, sin_ref, sc_ref, n1_ref, q_ref, k_ref, v_ref, att_ref,
          extra):
    width = x.shape[1]
    normal, _ = normalize(x)
    low = (normal * vec_ref[base : base + 1] + vec_ref[base + 1 : base + 2]).astype(bf16)
    n1_ref[...] = low[HALO:]
    skip = HALO - extra
    queries = mm(low[skip:], w_in[:, :width])
    keys = mm(low, w_in[:, width : 2 * width])
    for at in range(0, width, 128):
        q_ref[:, at : at + 128] = rotate(
            queries[:, at : at + 128], cos_ref[skip:], sin_ref[skip:]
        ).astype(bf16)
        k_ref[:, at : at + 128] = rotate(keys[:, at : at + 128], cos_ref[...], sin_ref[...]).astype(
            bf16
        )
    v_ref[...] = mm(low, w_in[:, 2 * width :]).astype(bf16)
    frames = x.shape[0] - HALO
    if extra:
        attend(q_ref, k_ref, v_ref, att_ref, sc_ref, extra, -extra, -HALO, HALO, 0)
    for first in range(0, frames, QUERIES):
        attend(
            q_ref, k_ref, v_ref, att_ref, sc_ref, QUERIES, first, first - HALO, WINDOW,
            extra + first,
        )


def decoder_front_kernel(sc_ref, *refs):
    pieces, refs = refs[:PIECES], refs[PIECES:]
    (qz_ref, vec_ref, cos_ref, sin_ref, x_ref, restored_ref, n1_ref, q_ref, k_ref, v_ref, att_ref,
     w_vmem, x_scr, sems) = refs
    width = x_ref.shape[1]
    wait_all(fetch(sc_ref, pieces, 0, w_vmem.shape[1], w_vmem, sems))
    latent = qz_ref.shape[1]
    restored = mm_nt(qz_ref[...], w_vmem[:, :latent]).astype(bf16)
    restored_ref[...] = restored[CODE_HALO - 16 :]
    both = mm(restored, w_vmem[:, latent : latent + 4 * width])
    bias = vec_ref[7:8]
    now = both[16:, : 2 * width]
    before = pltpu.roll(both[:, 2 * width :], 1, 0)[16:]
    total = now + before
    x = interleave(total[:, :width] + bias, total[:, width:] + bias, x_scr)
    x_ref[...] = x[HALO:]
    w_in = w_vmem.at[:, latent + 4 * width :]
    front(x, vec_ref, 8, w_in, cos_ref, sin_ref, sc_ref, n1_ref, q_ref, k_ref, v_ref,
          att_ref, 0)


def encoder_front_kernel(sc_ref, *refs):
    (pieces,), refs = split_refs(refs, (PIECES,))
    (halo_ref, x_ref, vec_ref, cos_ref, sin_ref, n1_ref, q_ref, k_ref, v_ref, att_ref,
     w_vmem, sems) = refs
    width = x_ref.shape[1]
    copies = fetch(sc_ref, pieces, 0, 3 * width, w_vmem, sems)
    x = jnp.concatenate([halo_ref[...], x_ref[...]], 0).astype(f32)
    wait_all(copies)
    front(x, vec_ref, 0, w_vmem, cos_ref, sin_ref, sc_ref, n1_ref, q_ref, k_ref, v_ref, att_ref,
          EXTRA)


def gelu_both(hidden):
    share = 0.5 * (1.0 + lax.erf(hidden * 0.7071067811865476))
    density = jnp.exp(-0.5 * hidden * hidden) * 0.3989422804014327
    return hidden * share, share + hidden * density


def l2_rows(w, at, chunk, width):
    rows = width // 4
    return jnp.concatenate(
        [
            w[chunk * rows : (chunk + 1) * rows, at + g * width : at + (g + 1) * width]
            for g in range(4)
        ],
        0,
    )


def fetch_layer(sc_ref, groups, plan, width, w_vmem, sems):
    edges = (0, width, 5 * width, 9 * width)
    return [
        fetch(
            sc_ref, groups[plan[i][0]], plan[i][1], high - low, w_vmem.at[:, low:high], sems,
            PIECES * i,
        )
        for i, (low, high) in enumerate(zip(edges[:-1], edges[1:]))
    ]


def ff_forward(base, extra, copies, w_vmem, att_ref, stream, vec_ref, out_ref, n2_ref, active_ref,
               slope_ref, mid_ref, second_ref, h_scr, act_scr):
    rows, width = stream.shape
    scale_one = vec_ref[base + 2 : base + 3]
    gain_two = vec_ref[base + 3 : base + 4]
    bias_two = vec_ref[base + 4 : base + 5]
    scale_two = vec_ref[base + 5 : base + 6]
    wait_all(copies[0])
    middle = stream + scale_one * mm(att_ref[...], w_vmem[:, :width])
    mid_ref[...] = middle[extra:]
    normal, _ = normalize(middle)
    n2 = (normal * gain_two + bias_two).astype(bf16)
    n2_ref[...] = n2[extra:]
    wait_all(copies[1])
    l1_at, l2_at = width, 5 * width
    second = None
    for chunk in range(4):
        cols = slice(chunk * width, (chunk + 1) * width)
        h_scr[...] = mm(n2, w_vmem[:, l1_at + chunk * width : l1_at + (chunk + 1) * width])
        if extra:
            act, _ = gelu_both(h_scr[:extra, :])
            act_scr[:extra, cols] = act.astype(bf16)

        def body(i, _):
            at_row = pl.multiple_of(i * 16, 16)
            act, slope = gelu_both(h_scr[pl.ds(at_row + extra, 16), :])
            act_scr[pl.ds(at_row + extra, 16), cols] = act.astype(bf16)
            slope_ref[pl.ds(at_row, 16), cols] = slope
            return 0

        lax.fori_loop(0, (rows - extra) // 16, body, 0)
        if chunk == 0:
            wait_all(copies[2])
        part = mm(act_scr[:, cols], l2_rows(w_vmem, l2_at, chunk, width))
        second = part if second is None else second + part
    active_ref[...] = act_scr[extra:, :]
    second_ref[...] = second[extra:]
    out_ref[...] = (middle + scale_two * second).astype(bf16)


def ff_backward(base, extra, w_vmem, att_ref, g, vec_ref, slope_ref, mid_ref, second_ref, gmid_ref,
                dh_ref, dtwo_ref, done_ref, vg_ref, datt_scr):
    width = g.shape[1]
    scale_one = vec_ref[base + 2 : base + 3]
    gain_two = vec_ref[base + 3 : base + 4]
    scale_two = vec_ref[base + 5 : base + 6]
    l1_at, l2_at = width, 5 * width
    vg_ref[3:4, :] = column_sum(g * second_ref[...])
    d_two = (g * scale_two).astype(bf16)
    dtwo_ref[...] = d_two
    e = None
    for chunk in range(4):
        cols = slice(chunk * width, (chunk + 1) * width)
        d_active = mm_nt(d_two, l2_rows(w_vmem, l2_at, chunk, width))
        dh_ref[:, cols] = (d_active * slope_ref[:, cols]).astype(bf16)
        part = mm_nt(
            dh_ref[:, cols], w_vmem[:, l1_at + chunk * width : l1_at + (chunk + 1) * width]
        )
        e = part if e is None else e + part
    normal, scaled = normalize(mid_ref[...])
    vg_ref[1:2, :] = column_sum(e * normal)
    vg_ref[2:3, :] = column_sum(e)
    g_mid = g + norm_backward(e, normal, scaled, gain_two)
    gmid_ref[...] = g_mid
    vg_ref[0:1, :] = column_sum(g_mid * mm(att_ref[extra:, :], w_vmem[:, :width]))
    d_one = (g_mid * scale_one).astype(bf16)
    done_ref[...] = d_one
    datt_scr[...] = mm_nt(d_one, w_vmem[:, :width]).astype(bf16)


def decoder_layer_kernel(plan, sc_ref, *refs):
    (pieces,), refs = split_refs(refs, (PIECES,))
    (att_ref, x_ref, g_ref, vec_ref, q_ref, k_ref, v_ref,
     out_ref, n2_ref, active_ref, gmid_ref, dh_ref, dtwo_ref, done_ref, vg_ref,
     dq_ref, dk_ref, dv_ref, dkv_ref,
     w_vmem, h_scr, act_scr, slope_scr, mid_scr, second_scr, datt_scr, dk_scr, dv_scr, sems) = refs
    width = x_ref.shape[1]
    copies = fetch_layer(sc_ref, (pieces,), plan, width, w_vmem, sems)
    ff_forward(8, 0, copies, w_vmem, att_ref, x_ref[...], vec_ref, out_ref, n2_ref, active_ref,
               slope_scr, mid_scr, second_scr, h_scr, act_scr)
    ff_backward(8, 0, w_vmem, att_ref, g_ref[...].astype(f32), vec_ref, slope_scr, mid_scr,
                second_scr, gmid_ref, dh_ref, dtwo_ref, done_ref, vg_ref, datt_scr)
    attention_backward(0, sc_ref, q_ref, k_ref, v_ref, datt_scr, dq_ref, dk_ref, dv_ref, dkv_ref,
                       dk_scr, dv_scr)


def encoder_forward_kernel(plan, sc_ref, *refs):
    groups, refs = split_refs(refs, (PIECES, PIECES))
    (halo_ref, x_ref, att_ref, vec_ref,
     out_ref, n2_ref, active_ref, slope_ref, mid_ref, second_ref,
     w_vmem, h_scr, act_scr, sems) = refs
    width = x_ref.shape[1]
    copies = fetch_layer(sc_ref, groups, plan, width, w_vmem, sems)
    stream = jnp.concatenate([halo_ref[HALO - EXTRA :, :], x_ref[...]], 0).astype(f32)
    ff_forward(0, EXTRA, copies, w_vmem, att_ref, stream, vec_ref, out_ref, n2_ref, active_ref,
               slope_ref, mid_ref, second_ref, h_scr, act_scr)


def encoder_backward_kernel(plan, sc_ref, *refs):
    groups, refs = split_refs(refs, (PIECES, PIECES))
    (att_ref, g_ref, vec_ref, slope_ref, mid_ref, second_ref, q_ref, k_ref, v_ref,
     gmid_ref, dh_ref, dtwo_ref, done_ref, vg_ref, dq_ref, dk_ref, dv_ref, dkv_ref,
     w_vmem, datt_scr, dk_scr, dv_scr, sems) = refs
    width = g_ref.shape[1]
    for copies in fetch_layer(sc_ref, groups, plan, width, w_vmem, sems):
        wait_all(copies)
    ff_backward(0, EXTRA, w_vmem, att_ref, g_ref[...], vec_ref, slope_ref, mid_ref, second_ref,
                gmid_ref, dh_ref, dtwo_ref, done_ref, vg_ref, datt_scr)
    attention_backward(EXTRA, sc_ref, q_ref, k_ref, v_ref, datt_scr, dq_ref, dk_ref, dv_ref,
                       dkv_ref, dk_scr, dv_scr)


def attention_backward(extra, sc_ref, q_ref, k_ref, v_ref, do_ref,
                       dq_ref, dk_ref, dv_ref, dkv_ref, dk_scr, dv_scr):
    start, cut = sc_ref[0], sc_ref[1]
    frames = do_ref.shape[0]
    lanes = head_lanes()
    scale = HEAD_DIM ** (-0.5)
    dk_scr[...] = jnp.zeros_like(dk_scr)
    dv_scr[...] = jnp.zeros_like(dv_scr)
    wide = GROUP * QUERIES
    for first in range(0, frames, QUERIES):
        lane = lax.broadcasted_iota(jnp.int32, (1, wide), 1) % QUERIES
        query = start + first + lane
        low = lowest_key(query, cut)
        key = start + first - HALO + lax.broadcasted_iota(jnp.int32, (WINDOW, wide), 0)
        mask = (key <= query) & (key >= low)
        for group in range(HEADS // GROUP):
            cols = slice(group * GROUP * HEAD_DIM, (group + 1) * GROUP * HEAD_DIM)
            qs = stack_heads(q_ref[extra + first : extra + first + QUERIES, cols], lanes)
            ds = stack_heads(do_ref[first : first + QUERIES, cols], lanes)
            kw = k_ref[first : first + WINDOW, cols]
            vw = v_ref[first : first + WINDOW, cols]
            scores = jnp.where(mask, mm_nt(kw, qs) * scale, -1e30)
            exponent = jnp.exp(scores - jnp.max(scores, 0, keepdims=True))
            probs = exponent * (1.0 / jnp.sum(exponent, 0, keepdims=True))
            d_probs = mm_nt(vw, ds)
            mean = jnp.sum(probs * d_probs, 0, keepdims=True)
            d_scores = (probs * (d_probs - mean)).astype(bf16)
            dk_scr[first : first + WINDOW, cols] += mm(d_scores, qs)
            dv_scr[first : first + WINDOW, cols] += mm(probs.astype(bf16), ds)
            dq_ref[first : first + QUERIES, cols] = (
                unstack_heads(mm_tn(d_scores, kw), lanes) * scale
            )
    width = dq_ref.shape[1]
    dkv_ref[:, :width] = (dk_scr[:HALO] * scale).astype(bf16)
    dkv_ref[:, width:] = dv_scr[:HALO].astype(bf16)
    dk_ref[...] = dk_scr[HALO:] * scale
    dv_ref[...] = dv_scr[HALO:]


class Packer:
    def __init__(self, core, refs, shares, order):
        self.core, self.refs, self.shares, self.order = core, refs, shares, order

    def put(self, value, at, step=1, phase=0, block0=0):
        if len(self.refs) == 1:
            if step == 1:
                self.refs[0][:, at : at + value.shape[1]] = value.astype(bf16)
            return
        send, keep = self.refs
        cols = slice(at, at + value.shape[1])
        rows = 16
        hi = self.shares // 8
        blocks = value.shape[0] // (rows * step)
        for pair in range(blocks // 2):
            even = value[(2 * pair * step + phase) * rows :][:rows]
            odd = value[((2 * pair + 1) * step + phase) * rows :][:rows]
            block = (block0 + 2 * pair) // 2
            place = {"x": (block % 2, 2), "lo": (block // 2 % 2, 2), "hi": (block // 4, hi)}
            at_row = 0
            for axis in self.order:
                at_row = at_row * place[axis][1] + place[axis][0]
            at_row = at_row * rows
            first = self.core == 0
            keep[at_row : at_row + rows, cols] = jnp.where(first, even, odd).astype(bf16)
            send[at_row : at_row + rows, cols] = jnp.where(first, odd, even).astype(bf16)

    def put_l2(self, value, at, chunk, width):
        if len(self.refs) == 1:
            cols = slice(at + chunk * width, at + (chunk + 1) * width)
            self.refs[0][:, cols] = value.astype(bf16)
            return
        for phase in range(4):
            self.put(value, at + phase * width, 4, phase, chunk * width // 64)


def linear_gradients(pack, n2_ref, active_ref, dh_ref, dtwo_ref):
    width = n2_ref.shape[1]
    for chunk in range(4):
        cols = slice(chunk * width, (chunk + 1) * width)
        pack.put_l2(mm_tn(active_ref[:, cols], dtwo_ref[...]), 0, chunk, width)
        pack.put(mm_tn(n2_ref[...], dh_ref[:, cols]), (4 + chunk) * width)


def decoder_gradients_kernel(shares, sc_ref, n2_ref, active_ref, dh_ref, dtwo_ref, att_ref, done_ref,
                             *refs):
    pack = Packer(sc_ref[2], refs, shares, ORDER_A)
    linear_gradients(pack, n2_ref, active_ref, dh_ref, dtwo_ref)
    pack.put(mm_tn(att_ref[...], done_ref[...]), 8 * n2_ref.shape[1])


def encoder_gradients_kernel(shares, sc_ref, n2_ref, active_ref, dh_ref, dtwo_ref, att_ref, done_ref,
                             win_ref, dred_ref, red_ref, dlat_ref, *refs):
    width = n2_ref.shape[1]
    half = len(refs) // 2
    linear_gradients(
        Packer(sc_ref[2], refs[:half], shares, ORDER_C_ONE), n2_ref, active_ref, dh_ref, dtwo_ref
    )
    pack = Packer(sc_ref[2], refs[half:], shares, ORDER_C_TWO)
    d_reduced = dred_ref[...]
    for tap in range(4):
        pack.put(mm_tn(win_ref[tap], d_reduced), tap * width)
    pack.put(mm_tn(att_ref[EXTRA:, :], done_ref[...]), 4 * width)
    pack.put(mm_tn(red_ref[...], dlat_ref[...]), 5 * width)


def layer_input_gradient(base, dq_ref, dk_ref, dv_ref, dkv_ref, x, gmid_ref,
                         w_in, vec_ref, cos_ref, sin_ref, dmix_ref, vg_ref):
    frames, width = dq_ref.shape
    later = frames - HALO
    cos, sin = cos_ref[HALO:], -sin_ref[HALO:]
    for at in range(0, width, 128):
        cols = slice(at, at + 128)
        dmix_ref[:, cols] = rotate(dq_ref[:, cols], cos, sin).astype(bf16)
        keys = dk_ref[:, cols]
        keys = jnp.concatenate([keys[:later], keys[later:] + dkv_ref[:, cols].astype(f32)], 0)
        dmix_ref[:, width + at : width + at + 128] = rotate(keys, cos, sin).astype(bf16)
        values = dv_ref[:, cols]
        moved = dkv_ref[:, width + at : width + at + 128].astype(f32)
        values = jnp.concatenate([values[:later], values[later:] + moved], 0)
        dmix_ref[:, 2 * width + at : 2 * width + at + 128] = values.astype(bf16)
    d_normed = mm_nt(dmix_ref[...], w_in[...])
    normal, scaled = normalize(x)
    vg_ref[0:1, :] = column_sum(d_normed * normal)
    vg_ref[1:2, :] = column_sum(d_normed)
    return gmid_ref[...] + norm_backward(d_normed, normal, scaled, vec_ref[base : base + 1])


def decoder_back_kernel(at, sc_ref, *refs):
    pieces, refs = refs[:PIECES], refs[PIECES:]
    (dq_ref, dk_ref, dv_ref, dkv_ref, x_ref, gmid_ref, vec_ref, cos_ref, sin_ref,
     dup_ref, dmix_ref, vg_ref, w_vmem, sems) = refs
    wait_all(fetch(sc_ref, pieces, at, w_vmem.shape[1], w_vmem, sems))
    grad = layer_input_gradient(
        8, dq_ref, dk_ref, dv_ref, dkv_ref, x_ref[...], gmid_ref, w_vmem, vec_ref,
        cos_ref, sin_ref, dmix_ref, vg_ref,
    )
    vg_ref[2:3, :] = column_sum(grad)
    dup_ref[...] = grad.astype(bf16)


def encoder_back_kernel(shares, sc_ref, *refs):
    (pieces,), refs = split_refs(refs, (PIECES,))
    (dq_ref, dk_ref, dv_ref, dkv_ref, x_ref, gmid_ref, vec_ref, cos_ref, sin_ref, n1_ref,
     vgs_ref, grad_ref, *rest) = refs
    refs, (w_vmem, dmix_scr, vg_scr, all_scr, sems) = rest[:-5], rest[-5:]
    width = x_ref.shape[1]
    wait_all(fetch(sc_ref, pieces, 0, w_vmem.shape[1], w_vmem, sems))
    grad = layer_input_gradient(
        0, dq_ref, dk_ref, dv_ref, dkv_ref, x_ref[...].astype(f32), gmid_ref, w_vmem,
        vec_ref, cos_ref, sin_ref, dmix_scr, vg_scr,
    )
    grad_ref[...] = grad.astype(bf16)
    pack = Packer(sc_ref[2], refs, shares, ORDER_D)
    for part in range(3):
        cols = slice(part * width, (part + 1) * width)
        pack.put(mm_tn(n1_ref[...], dmix_scr[:, cols]), part * width)
    all_scr[...] = jnp.zeros_like(all_scr)
    all_scr[0:2, :] = vg_scr[0:2, :]
    all_scr[2:6, :] = vgs_ref[0:4, :]
    all_scr[6:7, :] = vgs_ref[16:17, :]
    all_scr[7:8, :] = vgs_ref[26:27, :]
    all_scr[8:10, :] = vgs_ref[24:26, :]
    all_scr[10:14, :] = vgs_ref[8:12, :]
    pack.put(all_scr[...].T, 3 * width)


def middle_kernel(shares, sc_ref, *refs):
    (pieces, more), refs = split_refs(refs, (PIECES, PIECES))
    (dup_ref, next_ref, dmix_ref, n1_ref, restored_ref, qz_ref,
     denc_ref, dred_ref, dlat_ref, vg_ref, *rest) = refs
    refs, (up_vmem, down_vmem, frame_scr, sems) = rest[:-4], rest[-4:]
    frames, width = dup_ref.shape
    latent = qz_ref.shape[1]
    codec = frames // 2
    copies = [
        fetch(sc_ref, pieces, 0, latent + 4 * width, up_vmem, sems),
        fetch(sc_ref, more, 4 * width, 4 * width + latent, down_vmem, sems, PIECES),
    ]
    pairs = codec + 16
    even, odd = split_rows(
        jnp.concatenate([dup_ref[...], next_ref[...]], 0).astype(f32), frame_scr
    )
    both = jnp.concatenate([even, odd], 1).astype(bf16)
    wait_all(copies[0])
    up = up_vmem[:, latent : latent + 4 * width]
    here = mm_nt(both, up[:, : 2 * width])
    later = mm_nt(both, up[:, 2 * width :])
    d_restored = (here + pltpu.roll(later, pairs - 1, 0)).astype(bf16)
    d_latent = mm(d_restored, up_vmem[:, :latent]).astype(bf16)
    wait_all(copies[1])
    d_reduced = mm_nt(d_latent, down_vmem[:, 4 * width :]).astype(bf16)
    dlat_ref[...] = d_latent[:codec]
    dred_ref[...] = d_reduced[:codec]
    vg_ref[0:1, :] = column_sum(d_reduced[:codec].astype(f32))
    taps = [mm_nt(d_reduced, down_vmem[:, tap * width : (tap + 1) * width]) for tap in range(4)]
    denc_ref[...] = interleave(
        taps[2] + pltpu.roll(taps[0], pairs - 1, 0),
        taps[3] + pltpu.roll(taps[1], pairs - 1, 0),
        frame_scr,
    )[:frames]

    pack = Packer(sc_ref[2], refs, shares, ORDER_B)
    for part in range(3):
        cols = slice(part * width, (part + 1) * width)
        pack.put(mm_tn(n1_ref[...], dmix_ref[:, cols]), part * width)
    restored = restored_ref[...]
    own_pairs = both[:codec]
    before = pltpu.roll(restored.astype(f32), 1, 0)[16:].astype(bf16)
    pack.put(mm_tn(restored[16:], own_pairs[:, :width]), 3 * width)
    pack.put(mm_tn(restored[16:], own_pairs[:, width:]), 4 * width)
    pack.put(mm_tn(before, own_pairs[:, :width]), 5 * width)
    pack.put(mm_tn(before, own_pairs[:, width:]), 6 * width)
    pack.put(mm_tn(d_restored[:codec], qz_ref[CODE_HALO:, :]), 7 * width)


def latent_kernel(sc_ref, *refs):
    (pieces,), refs = split_refs(refs, (PIECES,))
    (enc_ref, rows_ref, vec_ref, res_ref, win_ref, red_ref, w_vmem, frame_scr, sems) = refs
    total, width = enc_ref.shape
    copies = fetch(sc_ref, pieces, 4 * width, w_vmem.shape[1], w_vmem, sems)
    inside = (sc_ref[0] > 0).astype(f32)
    rim = enc_ref[:EXTRA].astype(f32) * inside
    skip = EXTRA // 2
    even, odd = split_rows(jnp.concatenate([rim, enc_ref[EXTRA:].astype(f32)], 0), frame_scr)
    win_ref[0] = pltpu.roll(even, 1, 0)[skip:].astype(bf16)
    win_ref[1] = pltpu.roll(odd, 1, 0)[skip:].astype(bf16)
    win_ref[2] = even[skip:].astype(bf16)
    win_ref[3] = odd[skip:].astype(bf16)
    wait_all(copies)
    reduced = vec_ref[6:7]
    for tap in range(4):
        reduced = reduced + mm(win_ref[tap], w_vmem[:, tap * width : (tap + 1) * width])
    reduced = reduced.astype(bf16)
    red_ref[...] = reduced
    remaining = mm(reduced, w_vmem[:, 4 * width :])
    for level in range(rows_ref.shape[0]):
        res_ref[level] = remaining.astype(bf16)
        remaining = remaining - rows_ref[level].astype(f32)


def lookup_kernel(sc_ref, codes_ref, book_ref, qsend_ref, qkeep_ref, rsend_ref, rkeep_ref, q_scr):
    levels, share, latent = book_ref.shape
    total = codes_ref.shape[0]
    codec = total // 4
    base = sc_ref[3]
    core = sc_ref[2]
    entry = lax.broadcasted_iota(jnp.int32, (1, share), 1)
    for level in range(levels):
        picks = (codes_ref[:, level : level + 1] - base == entry).astype(f32).astype(bf16)
        found = mm(picks, book_ref[level])
        q_scr[CODE_HALO:] = found if level == 0 else q_scr[CODE_HALO:] + found
        for x in range(2):
            even = found[(2 * x) * codec :][:codec]
            odd = found[(2 * x + 1) * codec :][:codec]
            rkeep_ref[x, level] = jnp.where(core == 0, even, odd).astype(bf16)
            rsend_ref[x, level] = jnp.where(core == 0, odd, even).astype(bf16)
    q_scr[:CODE_HALO] = jnp.zeros((CODE_HALO, latent), f32)
    for x in range(2):
        even = q_scr[(2 * x) * codec : (2 * x + 1) * codec + CODE_HALO]
        odd = q_scr[(2 * x + 1) * codec : (2 * x + 2) * codec + CODE_HALO]
        qkeep_ref[x] = jnp.where(core == 0, even, odd)
        qsend_ref[x] = jnp.where(core == 0, odd, even)


def collect_kernel(share, seq_count, sc_ref, own_ref, x_ref, core_ref, far_ref, codes_ref,
                   marked_ref, send_ref, keep_ref, row_scr, cnt_scr):
    levels, codec, latent = own_ref.shape
    total = codes_ref.shape[1]
    lo = sc_ref[4]
    high = send_ref.shape[0]
    frame = lax.broadcasted_iota(jnp.int32, (1, total), 1) + sc_ref[6]
    row = lax.broadcasted_iota(jnp.int32, (2 * high * share, 1), 0)
    entry = (row // share * seq_count + sc_ref[5]) * share + row % share
    ones = jnp.ones((16, total), bf16)
    for level in range(levels):
        marked = marked_ref[:, level : level + 1]
        used = (entry == codes_ref[level : level + 1, :]).astype(f32)
        placed = (marked // 2 == frame).astype(f32)
        select = jnp.where(marked % 2 == 1, placed, used).astype(bf16)
        for place, ref in enumerate((own_ref, x_ref, core_ref, far_ref)):
            at_row = pl.multiple_of(sc_ref[14 + place], 32)
            row_scr[pl.ds(at_row, codec), :] = ref[level]
        sums = mm(select, row_scr[...])
        cnt_scr[level : level + 1, :] = mm_nt(ones, used.astype(bf16))[0:1]
        at = slice(level * share, (level + 1) * share)
        for h in range(high):
            even = sums[(2 * h) * share :][:share]
            odd = sums[(2 * h + 1) * share :][:share]
            keep_ref[h, at, :] = jnp.where(lo == 0, even, odd).astype(bf16)
            send_ref[h, at, :] = jnp.where(lo == 0, odd, even).astype(bf16)
    counts = cnt_scr[...]
    upper = jnp.floor(counts * (1.0 / 128.0))
    digits = jnp.concatenate([upper, counts - 128.0 * upper], 0)
    tail = slice(levels * share, levels * share + 2 * levels)
    for h in range(high):
        even = digits[:, (2 * h) * share : (2 * h + 1) * share]
        odd = digits[:, (2 * h + 1) * share : (2 * h + 2) * share]
        keep_ref[h, tail, :] = jnp.zeros((2 * levels, latent), bf16)
        send_ref[h, tail, :] = jnp.zeros((2 * levels, latent), bf16)
        keep_ref[h, tail, :share] = jnp.where(lo == 0, even, odd).astype(bf16)
        send_ref[h, tail, :share] = jnp.where(lo == 0, odd, even).astype(bf16)


def call(kernel, outs, spaces, scratch, args, micros):
    where = {"s": pltpu.SMEM, "v": pltpu.VMEM, "h": pltpu.HBM}
    title = getattr(kernel, "func", kernel).__name__
    return pl.pallas_call(
        kernel,
        name=title,
        out_shape=outs,
        in_specs=[pl.BlockSpec(memory_space=where[space]) for space in spaces],
        out_specs=[pl.BlockSpec(memory_space=pltpu.VMEM) for _ in outs],
        scratch_shapes=scratch,
        compiler_params=pltpu.CompilerParams(vmem_limit_bytes=VMEM_LIMIT),
        cost_estimate=pl.CostEstimate(
            flops=int(micros * 1e6), bytes_accessed=1, transcendentals=0
        ),
    )(*args)


def shape(dims, dtype=f32):
    return jax.ShapeDtypeStruct(dims, dtype)


def pick(block, at):
    zero = jnp.zeros((), jnp.uint32)
    start = (at,) + (zero,) * (block.ndim - 1)
    return lax.dynamic_slice(block, start, (1,) + block.shape[1:])[0]


def halve(block, axis, index, after=None):
    sent = pick(block, index["other " + axis])
    kept = pick(block, index[axis])
    got = lax.ppermute(sent, axis, [(0, 1), (1, 0)])
    if after is not None:
        got, _ = tie(got, after)
    return (kept.astype(f32) + got.astype(f32)).astype(block.dtype)


def sum_by_permutes(block, index, after=None):
    count = block.shape[0]
    if count != 4:
        return sum_over_hi(block)
    total = pick(block, index["hi"]).astype(f32)
    for turn in range(1, count):
        sent = pick(block, index["hi ^ %d" % turn])
        got = lax.ppermute(sent, "hi", [(i, i ^ turn) for i in range(count)])
        if after is not None:
            got, _ = tie(got, after)
        total = total + got.astype(f32)
    return total


def swap_add(send, keep, axis, after=None):
    got = lax.ppermute(send, axis, [(0, 1), (1, 0)])
    if after is not None:
        got, _ = tie(got, after)
    return (keep.astype(f32) + got.astype(f32)).astype(keep.dtype)


def sum_over_hi(block):
    parts = lax.all_to_all(block, "hi", 0, 0, tiled=True)
    return jnp.sum(parts.astype(f32), 0)


def shifted(block, distance):
    devices = range(lax.axis_size(SEQ))
    route = [(i - distance, i) for i in devices if i - distance in devices]
    return lax.ppermute(block, SEQ, route)


def packed_outs(width_total, width, shares):
    if width // shares % 16 == 0:
        return [shape((width // 2, width_total), bf16)] * 2
    return [shape((width, width_total), bf16)]


def swap(block, axis):
    return lax.ppermute(block, axis, [(0, 1), (1, 0)])


def tie(*values):
    return lax.optimization_barrier(values)


def half_of(share, index):
    rows = share.shape[0] // 2
    zero = jnp.zeros((), jnp.uint32)
    return lax.dynamic_slice(share, (index["lo"] * rows, zero), (rows, share.shape[1]))


def both_halves(near, far, index):
    first = index["lo"] == 0
    return jnp.concatenate([jnp.where(first, near, far), jnp.where(first, far, near)], 0)


def unfolded_rows(block, shares, l2_at):
    width = block.shape[0]
    full = [block[:, l2_at + i * width : l2_at + (i + 1) * width] for i in range(4)]
    full = jnp.concatenate(full, 0).reshape(shares, 4, width // shares, width)
    full = full.transpose(0, 2, 1, 3).reshape(width, 4 * width)
    return jnp.concatenate([block[:, :l2_at], full, block[:, l2_at + 4 * width :]], 1)


def first_sum(parts, shares, order, index, l2_at=None):
    if len(parts) == 2:
        return swap_add(*parts, "core")
    (block,) = parts
    if l2_at is not None:
        block = unfolded_rows(block, shares, l2_at)
    width, total = block.shape
    block = block.reshape(shares // 8, 2, 2, 2, width // shares, total)
    block = halve(block.transpose(3, 0, 1, 2, 4, 5), "core", index)
    places = [("hi", "lo", "x").index(axis) for axis in order]
    return block.transpose(*places, 3, 4).reshape(width // 2, total)


def next_sum(block, axis, index, after=None):
    rows, total = block.shape
    return halve(block.reshape(2, rows // 2, total), axis, index, after)


def last_sum(block, high):
    return sum_over_hi(block.reshape(high, -1, block.shape[1]))


def local(
    activations,
    encoder_attention_norm_gain,
    encoder_attention_norm_bias,
    encoder_query_key_value_weight,
    encoder_attention_output_weight,
    encoder_attention_layer_scale,
    encoder_forward_norm_gain,
    encoder_forward_norm_bias,
    encoder_forward_input_weight,
    encoder_forward_output_weight,
    encoder_forward_layer_scale,
    strided_convolution_weight,
    strided_convolution_bias,
    quantizer_input_weight,
    codebook,
    quantizer_output_weight,
    transposed_convolution_weight,
    transposed_convolution_bias,
    decoder_attention_norm_gain,
    decoder_attention_norm_bias,
    decoder_query_key_value_weight,
    decoder_attention_output_weight,
    decoder_attention_layer_scale,
    decoder_forward_norm_gain,
    decoder_forward_norm_bias,
    decoder_forward_input_weight,
    decoder_forward_output_weight,
    decoder_forward_layer_scale,
    cotangent,
    frame_segment_index,
    frame_code_index,
    replace_code_mask,
    replacing_batch_position,
    code_usage_average,
    code_latent_sum_average,
):
    batch_rows, frames, width = activations.shape
    assert batch_rows == 1
    seq_index = lax.axis_index(SEQ)
    seq_count = lax.axis_size(SEQ)
    dp_index = lax.axis_index(DP)
    dp_count = lax.axis_size(DP)
    shares = dp_count * seq_count
    codec = frames // 2
    levels = frame_code_index.shape[2]
    latent = codebook.shape[2]
    book_share = codebook.shape[1]
    core_index = lax.axis_index("core")

    x_index, lo_index = lax.axis_index("x"), lax.axis_index("lo")
    rows_share = width // seq_count
    high = shares // 8
    total_frames = HALO + frames
    code_total = replace_code_mask.shape[1]
    code_share = code_usage_average.shape[1]
    row_frames = codec * seq_count

    vectors = jnp.stack(
        [
            encoder_attention_norm_gain,
            encoder_attention_norm_bias,
            encoder_attention_layer_scale,
            encoder_forward_norm_gain,
            encoder_forward_norm_bias,
            encoder_forward_layer_scale,
            strided_convolution_bias,
            transposed_convolution_bias,
            decoder_attention_norm_gain,
            decoder_attention_norm_bias,
            decoder_attention_layer_scale,
            decoder_forward_norm_gain,
            decoder_forward_norm_bias,
            decoder_forward_layer_scale,
        ]
    )
    vectors = jnp.pad(vectors, ((0, 2), (0, 0)))
    small = jnp.concatenate(
        [frame_code_index.reshape(-1).astype(f32), vectors.reshape(-1).astype(f32)]
    )
    index = {}
    unsigned = jnp.uint32
    for axis in ("x", "lo", "core"):
        index[axis] = lax.axis_index(axis).astype(unsigned)
        index["other " + axis] = (1 - lax.axis_index(axis)).astype(unsigned)
    index["hi"] = lax.axis_index("hi").astype(unsigned)
    index["seq"] = lax.axis_index(SEQ).astype(unsigned)
    index["owner"] = (lax.axis_index(DP + SEQ) * code_share).astype(unsigned)
    for turn in range(1, 4):
        index["hi ^ %d" % turn] = lax.axis_index("hi").astype(unsigned) ^ unsigned(turn)
    def flat_taps(taps):
        return taps.transpose(1, 0, 2).reshape(taps.shape[1], -1)

    def fold_l2(share):
        return share.reshape(4, -1, width).transpose(1, 0, 2).reshape(-1, 4 * width)

    dec_one = jnp.concatenate(
        [
            quantizer_output_weight.T,
            flat_taps(transposed_convolution_weight),
            decoder_query_key_value_weight,
        ],
        1,
    )
    half_one = half_of(dec_one, index)
    small, half_one = tie(small, half_one)
    small = lax.all_gather(small, SEQ, axis=0, tiled=False)
    names = sorted(index)
    *index_values, small = tie(*[index[name] for name in names], small)
    index = dict(zip(names, index_values))
    code_count = codec * levels
    row_codes = small[:, :code_count].astype(jnp.int32).reshape(seq_count, codec, levels)
    vectors = small[:, code_count:].reshape(seq_count, 16, -1).transpose(1, 0, 2).reshape(16, width)
    order = [2 * x_index + core_index, 2 * (1 - x_index) + core_index]
    order += [2 * x_index + 1 - core_index, 2 * (1 - x_index) + 1 - core_index]
    cut = jnp.sum((frame_segment_index[0] == 0).astype(jnp.int32))
    scalars = jnp.stack(
        [
            seq_index * frames,
            cut,
            core_index,
            seq_index * book_share,
            lo_index,
            seq_index,
            dp_index * row_frames,
            seq_index,
        ]
        + [
            *[place * rows_share for place in order],
            seq_index,
            seq_index,
        ]
        + [place * codec for place in order]
    ).astype(jnp.int32)

    half_one, _ = tie(half_one, small)
    near_one = swap(half_one, "x")
    core_one = swap(dec_one, "core")
    activation_halo = shifted(activations[0, frames - HALO :], 1)

    positions = seq_index * frames - HALO + jnp.arange(total_frames, dtype=jnp.int32)
    half_dim = HEAD_DIM // 2
    frequency = jnp.power(10000.0, -jnp.arange(half_dim, dtype=f32) / half_dim)

    def angle_tables(positions):
        angles = positions.astype(f32)[:, None] * frequency[None, :]
        cos, sin = jnp.cos(angles), jnp.sin(angles)
        return jnp.concatenate([cos] * 4, 1), jnp.concatenate([-sin, sin, -sin, sin], 1)

    row_codes, activation_halo, core_one = tie(row_codes, activation_halo, core_one)

    window = codec + CODE_HALO
    qsend, qkeep, rsend, rkeep = call(
        lookup_kernel,
        [shape((2, window, latent))] * 2 + [shape((2, levels, codec, latent), bf16)] * 2,
        "svv",
        [pltpu.VMEM((CODE_HALO + codec * seq_count, latent), f32)],
        (scalars, row_codes.reshape(-1, levels), codebook),
        4,
    )
    q_sum = swap_add(qsend, qkeep, "core")
    q_sent = pick(q_sum, index["other x"])
    q_got = swap(q_sent, "x")
    (near_one, positions, dec_l2, enc_in, enc_l2, down_share, replace_code_mask,
     replacing_batch_position, row_codes, _) = tie(
        near_one, positions, decoder_forward_output_weight, encoder_query_key_value_weight,
        encoder_forward_output_weight, strided_convolution_weight, replace_code_mask,
        replacing_batch_position, row_codes, q_sent,
    )
    dec_two = jnp.concatenate(
        [decoder_attention_output_weight, decoder_forward_input_weight, fold_l2(dec_l2)], 1
    )
    enc_one = jnp.concatenate(
        [
            enc_in,
            encoder_attention_output_weight,
            flat_taps(down_share),
            quantizer_input_weight,
        ],
        1,
    )
    marked = (replacing_batch_position * 2 + replace_code_mask).T
    marked = marked.reshape(dp_count, seq_count, code_share, levels).transpose(1, 0, 2, 3)
    marked = pick(marked, index["seq"]).reshape(dp_count * code_share, levels)
    code_columns = row_codes.reshape(row_frames, levels).T
    owner_flag = lax.dynamic_slice(
        replace_code_mask, (jnp.zeros((), unsigned), index["owner"]), (levels, code_share)
    ) == 1
    far_one = swap(near_one, "lo")
    near_one = both_halves(near_one, far_one, index)
    dec_one = [dec_one, near_one, core_one, swap(near_one, "core")]
    half_two = half_of(dec_two, index)
    cos_table, sin_table = angle_tables(positions)
    near_two = swap(half_two, "x")
    quantized = (pick(q_sum, index["x"]) + q_got).astype(bf16)
    half_three = half_of(enc_one, index)
    (quantized, near_two, half_three, activation_halo, cos_table, sin_table, marked,
     code_columns, owner_flag) = tie(
        quantized, near_two, half_three, activation_halo, cos_table, sin_table, marked,
        code_columns, owner_flag,
    )
    core_two = swap(dec_two, "core")
    far_two = swap(near_two, "lo")
    near_three = swap(half_three, "x")

    d_x, restored, d_n1, d_q, d_k, d_v, d_att = call(
        decoder_front_kernel,
        [
            shape((frames, width)),
            shape((codec + 16, width), bf16),
            shape((frames, width), bf16),
            shape((frames, width), bf16),
            shape((total_frames, width), bf16),
            shape((total_frames, width), bf16),
            shape((frames, width), bf16),
        ],
        "s" + "h" * PIECES + "vvvv",
        [
            pltpu.VMEM((width, latent + 7 * width), bf16),
            pltpu.VMEM((width // 128, total_frames, 128), f32),
            pltpu.SemaphoreType.DMA((PIECES,)),
        ],
        (scalars, *dec_one, quantized, vectors, cos_table, sin_table),
        8,
    )
    d_att, far_two, near_three, enc_l2, rsend = tie(d_att, far_two, near_three, enc_l2, rsend)
    enc_two = jnp.concatenate([encoder_forward_input_weight, fold_l2(enc_l2)], 1)
    half_four = half_of(enc_two, index)
    code_rows = swap_add(rsend, rkeep, "core")
    near_two = both_halves(near_two, far_two, index)
    dec_two = [dec_two, near_two, core_two, swap(near_two, "core")]
    far_three = swap(near_three, "lo")
    near_four = swap(half_four, "x")
    layer_scratch = [
        pltpu.VMEM((frames, width), bf16),
        pltpu.VMEM((total_frames, width), f32),
        pltpu.VMEM((total_frames, width), f32),
        pltpu.SemaphoreType.DMA((3 * PIECES,)),
    ]
    forward_outs = [shape((frames, width), bf16), shape((frames, 4 * width), bf16)]
    kept_outs = [shape((frames, 4 * width)), shape((frames, width)), shape((frames, width))]
    backward_outs = [
        shape((frames, width)),
        shape((frames, 4 * width), bf16),
        shape((frames, width), bf16),
        shape((frames, width), bf16),
        shape((8, width)),
        shape((frames, width)),
        shape((frames, width)),
        shape((frames, width)),
        shape((HALO, 2 * width), bf16),
    ]
    weights_scratch = pltpu.VMEM((width, 9 * width), bf16)
    (output, d_n2, d_active, d_gmid, d_dh, d_dtwo, d_done, d_vg_two, d_dq, d_dk, d_dv, d_dkv) = call(
        partial(decoder_layer_kernel, ((0, 0), (0, width), (0, 5 * width))),
        [shape((frames, width), bf16)] + forward_outs + backward_outs,
        "s" + "h" * PIECES + "vvvvvvv",
        [
            weights_scratch,
            pltpu.VMEM((frames, width), f32),
            pltpu.VMEM((frames, 4 * width), bf16),
            pltpu.VMEM((frames, 4 * width), f32),
            pltpu.VMEM((frames, width), f32),
            pltpu.VMEM((frames, width), f32),
        ]
        + layer_scratch,
        (scalars, *dec_two, d_att, d_x, cotangent[0], vectors, d_q, d_k, d_v),
        14,
    )
    d_n2, far_three, near_four, code_rows = tie(d_n2, far_three, near_four, code_rows)
    near_three = both_halves(near_three, far_three, index)
    enc_one = [enc_one, near_three, swap(enc_one, "core"), swap(near_three, "core")]
    far_four = swap(near_four, "lo")
    d_dkv = shifted(d_dkv, -1)
    group_a = call(
        partial(decoder_gradients_kernel, shares),
        packed_outs(9 * width, width, shares),
        "svvvvvv",
        [],
        (scalars, d_n2, d_active, d_dh, d_dtwo, d_att, d_done),
        5,
    )
    d_dq, *group_a = tie(d_dq, *group_a)
    code_rows, d_dkv = tie(code_rows, d_dkv)
    code_rows = halve(code_rows, "x", index)
    a_sum = first_sum(group_a, shares, ORDER_A, index, 0)
    d_up, d_mixed, d_vg_one = call(
        partial(decoder_back_kernel, latent + 4 * width),
        [shape((frames, width), bf16), shape((frames, 3 * width), bf16), shape((8, width))],
        "s" + "h" * PIECES + "v" * 9,
        [pltpu.VMEM((width, 3 * width), bf16), pltpu.SemaphoreType.DMA((PIECES,))],
        (
            scalars, *dec_one, d_dq, d_dk, d_dv, d_dkv, d_x, d_gmid, vectors, cos_table,
            sin_table,
        ),
        4,
    )
    d_up_next = shifted(d_up[:32], -1)


    a_sum, d_up, e_input, far_four, code_rows = tie(
        a_sum, d_up, activations[0], far_four, code_rows
    )
    near_four = both_halves(near_four, far_four, index)
    enc_two = [enc_two, near_four, swap(enc_two, "core"), swap(near_four, "core")]
    a_sum = next_sum(a_sum, ORDER_A[0], index)
    e_n1, e_q, e_k, e_v, e_att = call(
        encoder_front_kernel,
        [
            shape((frames, width), bf16),
            shape((frames + EXTRA, width), bf16),
            shape((total_frames, width), bf16),
            shape((total_frames, width), bf16),
            shape((frames + EXTRA, width), bf16),
        ],
        "s" + "h" * PIECES + "vvvvv",
        [pltpu.VMEM((width, 3 * width), bf16), pltpu.SemaphoreType.DMA((PIECES,))],
        (scalars, *enc_one, activation_halo, e_input, vectors, cos_table, sin_table),
        7,
    )

    d_mixed, e_n1 = tie(d_mixed, e_n1)
    middle_outs = call(
        partial(middle_kernel, shares),
        [
            shape((frames, width)),
            shape((codec, width), bf16),
            shape((codec, latent), bf16),
            shape((8, width)),
        ]
        + packed_outs(7 * width + latent, width, shares),
        "s" + "h" * (2 * PIECES) + "" + "v" * 6,
        [
            pltpu.VMEM((width, latent + 4 * width), bf16),
            pltpu.VMEM((width, latent + 4 * width), bf16),
            pltpu.VMEM((width // 128, frames + 32, 128), f32),
            pltpu.SemaphoreType.DMA((2 * PIECES,)),
        ],
        (scalars, *dec_one, *enc_one, d_up, d_up_next, d_mixed, d_n1, restored, quantized),
        7,
    )
    d_encoded, d_reduced, d_latent, m_vg = middle_outs[:4]
    b_sum = first_sum(middle_outs[4:], shares, ORDER_B, index)

    e_att, d_encoded = tie(e_att, d_encoded)
    enc_plan = ((0, 3 * width), (1, 0), (1, 4 * width))
    rows = frames + EXTRA
    encoded, e_n2, e_active, e_slope, e_mid, e_second = call(
        partial(encoder_forward_kernel, enc_plan),
        [shape((rows, width), bf16)] + forward_outs + kept_outs,
        "s" + "h" * (2 * PIECES) + "vvvv",
        [
            weights_scratch,
            pltpu.VMEM((rows, width), f32),
            pltpu.VMEM((rows, 4 * width), bf16),
            pltpu.SemaphoreType.DMA((3 * PIECES,)),
        ],
        (scalars, *enc_one, *enc_two, activation_halo, e_input, e_att, vectors),
        6,
    )
    encoded, b_sum, a_sum = tie(encoded, b_sum, a_sum)
    b_sum = next_sum(b_sum, ORDER_B[0], index)
    residuals, windows, reduced = call(
        latent_kernel,
        [
            shape((levels, codec, latent), bf16),
            shape((4, codec, width), bf16),
            shape((codec, width), bf16),
        ],
        "s" + "h" * PIECES + "vvv",
        [
            pltpu.VMEM((width, 4 * width + latent), bf16),
            pltpu.VMEM((width // 128, frames + EXTRA, 128), f32),
            pltpu.SemaphoreType.DMA((PIECES,)),
        ],
        (scalars, *enc_one, encoded, code_rows, vectors),
        3,
    )
    near_res = swap(residuals, "x")
    core_res = swap(residuals, "core")

    d_encoded, _ = tie(d_encoded, residuals)
    a_sum = next_sum(a_sum, ORDER_A[1], index)
    (e_gmid, e_dh, e_dtwo, e_done, e_vg_two, e_dq, e_dk, e_dv, e_dkv) = call(
        partial(encoder_backward_kernel, enc_plan),
        backward_outs,
        "s" + "h" * (2 * PIECES) + "v" * 9,
        [weights_scratch] + layer_scratch,
        (
            scalars, *enc_one, *enc_two, e_att, d_encoded, vectors, e_slope, e_mid, e_second,
            e_q, e_k, e_v,
        ),
        11,
    )
    e_dkv = shifted(e_dkv, -1)
    near_res, core_res, _ = tie(near_res, core_res, e_gmid)
    res_pieces = [residuals, near_res, core_res, swap(near_res, "core")]

    code_columns, b_sum = tie(code_columns, b_sum)
    if code_share % 16 == 0:
        tail_rows = levels * code_share
        csend, ckeep = call(
            partial(collect_kernel, code_share, seq_count),
            [shape((dp_count // 2, tail_rows + 2 * levels, latent), bf16)] * 2,
            "svvvvvv",
            [
                pltpu.VMEM((row_frames, latent), bf16),
                pltpu.VMEM((levels, dp_count * code_share), f32),
            ],
            (scalars, *res_pieces, code_columns, marked),
            5,
        )
        e_n2, csend, e_gmid, e_dkv = tie(e_n2, csend, e_gmid, e_dkv)
    c_outs = packed_outs(8 * width, width, shares)
    group_c = call(
        partial(encoder_gradients_kernel, shares),
        c_outs + packed_outs(5 * width + latent, width, shares),
        "s" + "v" * 10,
        [],
        (
            scalars, e_n2, e_active, e_dh, e_dtwo, e_att, e_done, windows, d_reduced, reduced,
            d_latent,
        ),
        5,
    )
    e_dq, *group_c = tie(e_dq, *group_c)
    c_one = first_sum(group_c[: len(c_outs)], shares, ORDER_C_ONE, index, 0)
    c_two = first_sum(group_c[len(c_outs) :], shares, ORDER_C_TWO, index)
    e_dq, c_one, c_two, a_sum, b_sum = tie(e_dq, c_one, c_two, a_sum, b_sum)
    vector_grads = jnp.concatenate([e_vg_two, d_vg_two, m_vg, d_vg_one], 0)
    grad_outs = call(
        partial(encoder_back_kernel, shares),
        [shape((frames, width), bf16)] + packed_outs(3 * width + 128, width, shares),
        "s" + "h" * PIECES + "v" * 11,
        [
            pltpu.VMEM((width, 3 * width), bf16),
            pltpu.VMEM((frames, 3 * width), bf16),
            pltpu.VMEM((8, width), f32),
            pltpu.VMEM((128, width), f32),
            pltpu.SemaphoreType.DMA((PIECES,)),
        ],
        (
            scalars, *enc_one, e_dq, e_dk, e_dv, e_dkv, e_input, e_gmid, vectors,
            cos_table, sin_table, e_n1, vector_grads,
        ),
        5,
    )
    activations_grad = grad_outs[0]

    def z_sum(block):
        return sum_by_permutes(block.reshape(high, -1, block.shape[1]), index, activations_grad)

    d_sum = first_sum(grad_outs[1:], shares, ORDER_D, index)
    b_sum = next_sum(b_sum, ORDER_B[1], index, d_sum)
    if code_share % 16 == 0:
        combined = swap_add(csend, ckeep, "lo", b_sum)
        c_one = next_sum(c_one, ORDER_C_ONE[0], index, combined)
        together = last_sum(jnp.concatenate([a_sum, b_sum], 1), high)
        combined, together = tie(combined, together)
        combined = sum_over_hi(combined)
        summed = combined[:tail_rows].reshape(levels, code_share, latent)
        digits = combined[tail_rows:, :code_share]
        counted = 128.0 * digits[:levels] + digits[levels:]
    else:
        entry = (
            jnp.arange(dp_count, dtype=jnp.int32)[:, None] * seq_count + seq_index
        ) * code_share + jnp.arange(code_share, dtype=jnp.int32)
        relative = [place * codec + jnp.arange(codec, dtype=jnp.int32) for place in order]
        relative = jnp.concatenate(relative)
        flat_res = jnp.concatenate(res_pieces, 1)
        used = entry.reshape(1, -1, 1) == code_columns[:, None, relative]
        placed = (marked.T // 2)[:, :, None] == dp_index * row_frames + relative
        counts = jnp.sum(used.astype(f32), 2).reshape(levels, dp_count, code_share)
        selects = jnp.where((marked.T % 2)[:, :, None] == 1, placed, used).astype(bf16)
        sums = jnp.einsum("lct,ltd->lcd", selects, flat_res, preferred_element_type=f32)
        sums = sums.astype(bf16).reshape(levels, dp_count, code_share, latent)
        together = last_sum(jnp.concatenate([a_sum, b_sum], 1), high)
        c_one = next_sum(c_one, ORDER_C_ONE[0], index)
        summed = lax.psum_scatter(sums, DP, scatter_dimension=1, tiled=False).astype(f32)
        counted = lax.psum_scatter(counts, DP, scatter_dimension=1, tiled=False)
    c_two = next_sum(c_two, ORDER_C_TWO[0], index, c_one)
    d_sum = next_sum(d_sum, ORDER_D[0], index, c_two)
    c_two = next_sum(c_two, ORDER_C_TWO[1], index, d_sum)
    d_sum = next_sum(d_sum, ORDER_D[1], index, c_two)
    c_one = next_sum(c_one, ORDER_C_ONE[1], index, d_sum)
    grads_a, grads_b = together[:, : a_sum.shape[1]], together[:, a_sum.shape[1] :]
    edge, far_edge = c_one.shape[1], c_one.shape[1] + c_two.shape[1]
    together = last_sum(jnp.concatenate([c_one, c_two, d_sum], 1), high)
    grads_c, grads_c_two, grads_d = (
        together[:, :edge], together[:, edge:far_edge], together[:, far_edge:]
    )

    new_cluster_size = ema_decay * code_usage_average + (1.0 - ema_decay) * counted
    new_embed_sum = jnp.where(
        owner_flag[:, :, None],
        summed * new_cluster_size[:, :, None],
        ema_decay * code_latent_sum_average + (1.0 - ema_decay) * summed,
    )
    new_codebook = new_embed_sum / new_cluster_size[:, :, None]

    def columns(block, at, count):
        return block[:, at * width : (at + count) * width]

    def taps(block):
        return block.reshape(-1, 4, width).transpose(1, 0, 2)

    def unfold(block):
        return block.reshape(-1, 4, width).transpose(1, 0, 2).reshape(-1, width)

    vec = grads_d[:, 3 * width : 3 * width + 16].T
    return (
        output[None],
        activations_grad[None],
        vec[0],
        vec[1],
        columns(grads_d, 0, 3),
        columns(grads_c_two, 4, 1),
        vec[2],
        vec[3],
        vec[4],
        columns(grads_c, 4, 4),
        unfold(columns(grads_c, 0, 4)),
        vec[5],
        taps(columns(grads_c_two, 0, 4)),
        vec[6],
        grads_c_two[:, 5 * width :],
        grads_b[:, 7 * width :].T,
        taps(columns(grads_b, 3, 4)),
        vec[7],
        vec[8],
        vec[9],
        columns(grads_b, 0, 3),
        columns(grads_a, 8, 1),
        vec[10],
        vec[11],
        vec[12],
        columns(grads_a, 4, 4),
        unfold(columns(grads_a, 0, 4)),
        vec[13],
        new_cluster_size,
        new_embed_sum,
        new_codebook,
    )


def solution(mesh):
    grid = mesh.devices
    mesh = jax.sharding.Mesh(
        grid.reshape(grid.shape[0] // 2, 2, grid.shape[1] // 2, 2), ("hi", "lo", "x", "core")
    )
    placed = (
        P(DP, SEQ, None),
        P(SEQ),
        P(SEQ),
        P(SEQ, None),
        P(SEQ, None),
        P(SEQ),
        P(SEQ),
        P(SEQ),
        P(SEQ, None),
        P(SEQ, None),
        P(SEQ),
        P(None, SEQ, None),
        P(SEQ),
        P(SEQ, None),
        P(None, SEQ, None),
        P(None, SEQ),
        P(None, SEQ, None),
        P(SEQ),
        P(SEQ),
        P(SEQ),
        P(SEQ, None),
        P(SEQ, None),
        P(SEQ),
        P(SEQ),
        P(SEQ),
        P(SEQ, None),
        P(SEQ, None),
        P(SEQ),
        P(DP, SEQ, None),
        P(DP, None),
        P(DP, SEQ, None),
        P(),
        P(),
        P(None, DP + SEQ),
        P(None, DP + SEQ, None),
    )
    return jax.shard_map(
        local,
        mesh=mesh,
        in_specs=placed,
        out_specs=(
            P(DP, SEQ, None),
            P(DP, SEQ, None),
            P(DP + SEQ),
            P(DP + SEQ),
            P(DP + SEQ, None),
            P(DP + SEQ, None),
            P(DP + SEQ),
            P(DP + SEQ),
            P(DP + SEQ),
            P(DP + SEQ, None),
            P(DP + SEQ, None),
            P(DP + SEQ),
            P(None, DP + SEQ, None),
            P(DP + SEQ),
            P(DP + SEQ, None),
            P(None, DP + SEQ),
            P(None, DP + SEQ, None),
            P(DP + SEQ),
            P(DP + SEQ),
            P(DP + SEQ),
            P(DP + SEQ, None),
            P(DP + SEQ, None),
            P(DP + SEQ),
            P(DP + SEQ),
            P(DP + SEQ),
            P(DP + SEQ, None),
            P(DP + SEQ, None),
            P(DP + SEQ),
            P(None, DP + SEQ),
            P(None, DP + SEQ, None),
            P(None, DP + SEQ, None),
        ),
        check_vma=False,
    )
```

```python
from functools import partial

import jax
import jax.numpy as jnp
from jax import lax
from jax.experimental import pallas as pl
from jax.experimental.pallas import tpu as pltpu
from jax.sharding import PartitionSpec as P

HEADS = 8
HEAD_DIM = 64
CONTEXT = 250
HALO = 256
CODE_HALO = HALO // 2 + 16
EXTRA = 16
QUERIES = 64
GROUP = 4
WINDOW = HALO + QUERIES
VMEM_LIMIT = 26 * 1024 * 1024
ORDER_A = ("lo", "x", "hi")
ORDER_B = ("lo", "x", "hi")
ORDER_C_ONE = ("x", "lo", "hi")
ORDER_C_TWO = ("lo", "x", "hi")
ORDER_D = ("lo", "x", "hi")
DP = ("hi", "lo")
SEQ = ("x", "core")

norm_eps = 1e-05
ema_decay = 0.9
bf16 = jnp.bfloat16
f32 = jnp.float32


PIECES = 4


def fetch(sc_ref, pieces, at, width, dst, sems, first=0):
    copies = []
    for i, piece in enumerate(pieces):
        rows = piece.shape[0]
        row = pl.multiple_of(sc_ref[8 + i], 128)
        copies.append(
            pltpu.make_async_copy(
                piece.at[:, at : at + width], dst.at[pl.ds(row, rows), :], sems.at[first + i]
            )
        )
        copies[-1].start()
    return copies


def split_refs(refs, counts):
    groups = []
    for count in counts:
        groups.append(refs[:count])
        refs = refs[count:]
    return groups, refs


def wait_all(copies):
    for copy in copies:
        copy.wait()


def mm(a, b):
    return jnp.dot(a, b, preferred_element_type=f32)


def mm_nt(a, b):
    return lax.dot_general(a, b, (((1,), (1,)), ((), ())), preferred_element_type=f32)


def mm_tn(a, b):
    return lax.dot_general(a, b, (((0,), (0,)), ((), ())), preferred_element_type=f32)


def normalize(stream):
    center = stream - jnp.mean(stream, -1, keepdims=True)
    scaled = lax.rsqrt(jnp.mean(center * center, -1, keepdims=True) + norm_eps)
    return center * scaled, scaled


def norm_backward(upstream, normal, scaled, gain):
    inner = upstream * gain
    return scaled * (
        inner
        - jnp.mean(inner, -1, keepdims=True)
        - normal * jnp.mean(inner * normal, -1, keepdims=True)
    )


def column_sum(value):
    return jnp.sum(value, 0, keepdims=True)


def interleave(even, odd, scr):
    tiles, rows, _ = scr.shape
    for tile in range(tiles):
        cols = slice(tile * 128, (tile + 1) * 128)
        scr[tile, pl.ds(0, rows // 2, stride=2), :] = even[:, cols]
        scr[tile, pl.ds(1, rows // 2, stride=2), :] = odd[:, cols]
    return jnp.concatenate([scr[tile] for tile in range(tiles)], 1)


def split_rows(value, scr):
    tiles, rows, _ = scr.shape
    for tile in range(tiles):
        scr[tile] = value[:, tile * 128 : (tile + 1) * 128]
    even = [scr[tile, pl.ds(0, rows // 2, stride=2), :] for tile in range(tiles)]
    odd = [scr[tile, pl.ds(1, rows // 2, stride=2), :] for tile in range(tiles)]
    return jnp.concatenate(even, 1), jnp.concatenate(odd, 1)


def first_half():
    lane = lax.broadcasted_iota(jnp.int32, (1, 128), 1)
    return lane % HEAD_DIM < HEAD_DIM // 2


def rotate(tile, cos, sin):
    swapped = jnp.where(first_half(), pltpu.roll(tile, 96, 1), pltpu.roll(tile, 32, 1))
    return tile * cos + swapped * sin


def head_lanes():
    lane = lax.broadcasted_iota(jnp.int32, (1, GROUP * HEAD_DIM), 1) // HEAD_DIM
    return [(lane == head) for head in range(GROUP)]


def stack_heads(block, lanes):
    return jnp.concatenate([block * mask.astype(bf16) for mask in lanes], 0)


def unstack_heads(block, lanes):
    rows = block.shape[0] // GROUP
    out = block[:rows]
    for head in range(1, GROUP):
        out = jnp.where(lanes[head], block[head * rows : (head + 1) * rows], out)
    return out


def lowest_key(query, cut):
    low = jnp.maximum(query - (CONTEXT - 1), 0)
    return jnp.where(query >= cut, jnp.maximum(low, cut), low)


def attend(q_ref, k_ref, v_ref, att_ref, sc_ref, rows, first_query, first_key, keys, at_row):
    start, cut = sc_ref[0], sc_ref[1]
    query = start + first_query + lax.broadcasted_iota(jnp.int32, (rows, 1), 0)
    low = lowest_key(query, cut)
    key = start + first_key + lax.broadcasted_iota(jnp.int32, (rows, keys), 1)
    mask = (key <= query) & (key >= low)
    mask = jnp.concatenate([mask] * GROUP, 0)
    lanes = head_lanes()
    key_row = first_key + HALO
    for group in range(HEADS // GROUP):
        cols = slice(group * GROUP * HEAD_DIM, (group + 1) * GROUP * HEAD_DIM)
        stacked = stack_heads(q_ref[at_row : at_row + rows, cols], lanes)
        scores = mm_nt(stacked, k_ref[key_row : key_row + keys, cols]) * HEAD_DIM ** (-0.5)
        scores = jnp.where(mask, scores, -1e30)
        exponent = jnp.exp(scores - jnp.max(scores, -1, keepdims=True))
        weights = exponent * (1.0 / jnp.sum(exponent, -1, keepdims=True))
        mixed = mm(weights.astype(bf16), v_ref[key_row : key_row + keys, cols])
        att_ref[at_row : at_row + rows, cols] = unstack_heads(mixed, lanes).astype(bf16)


def front(x, vec_ref, base, w_in, cos_ref, sin_ref, sc_ref, n1_ref, q_ref, k_ref, v_ref, att_ref,
          extra):
    width = x.shape[1]
    normal, _ = normalize(x)
    low = (normal * vec_ref[base : base + 1] + vec_ref[base + 1 : base + 2]).astype(bf16)
    n1_ref[...] = low[HALO:]
    skip = HALO - extra
    queries = mm(low[skip:], w_in[:, :width])
    keys = mm(low, w_in[:, width : 2 * width])
    for at in range(0, width, 128):
        q_ref[:, at : at + 128] = rotate(
            queries[:, at : at + 128], cos_ref[skip:], sin_ref[skip:]
        ).astype(bf16)
        k_ref[:, at : at + 128] = rotate(keys[:, at : at + 128], cos_ref[...], sin_ref[...]).astype(
            bf16
        )
    v_ref[...] = mm(low, w_in[:, 2 * width :]).astype(bf16)
    frames = x.shape[0] - HALO
    if extra:
        attend(q_ref, k_ref, v_ref, att_ref, sc_ref, extra, -extra, -HALO, HALO, 0)
    for first in range(0, frames, QUERIES):
        attend(
            q_ref, k_ref, v_ref, att_ref, sc_ref, QUERIES, first, first - HALO, WINDOW,
            extra + first,
        )


def decoder_front_kernel(sc_ref, *refs):
    pieces, refs = refs[:PIECES], refs[PIECES:]
    (qz_ref, vec_ref, cos_ref, sin_ref, x_ref, restored_ref, n1_ref, q_ref, k_ref, v_ref, att_ref,
     w_vmem, x_scr, sems) = refs
    width = x_ref.shape[1]
    wait_all(fetch(sc_ref, pieces, 0, w_vmem.shape[1], w_vmem, sems))
    latent = qz_ref.shape[1]
    restored = mm_nt(qz_ref[...], w_vmem[:, :latent]).astype(bf16)
    restored_ref[...] = restored[CODE_HALO - 16 :]
    both = mm(restored, w_vmem[:, latent : latent + 4 * width])
    bias = vec_ref[7:8]
    now = both[16:, : 2 * width]
    before = pltpu.roll(both[:, 2 * width :], 1, 0)[16:]
    total = now + before
    x = interleave(total[:, :width] + bias, total[:, width:] + bias, x_scr)
    x_ref[...] = x[HALO:]
    w_in = w_vmem.at[:, latent + 4 * width :]
    front(x, vec_ref, 8, w_in, cos_ref, sin_ref, sc_ref, n1_ref, q_ref, k_ref, v_ref,
          att_ref, 0)


def encoder_front_kernel(sc_ref, *refs):
    (pieces,), refs = split_refs(refs, (PIECES,))
    (halo_ref, x_ref, vec_ref, cos_ref, sin_ref, n1_ref, q_ref, k_ref, v_ref, att_ref,
     w_vmem, sems) = refs
    width = x_ref.shape[1]
    copies = fetch(sc_ref, pieces, 0, 3 * width, w_vmem, sems)
    x = jnp.concatenate([halo_ref[...], x_ref[...]], 0).astype(f32)
    wait_all(copies)
    front(x, vec_ref, 0, w_vmem, cos_ref, sin_ref, sc_ref, n1_ref, q_ref, k_ref, v_ref, att_ref,
          EXTRA)


def gelu_both(hidden):
    share = 0.5 * (1.0 + lax.erf(hidden * 0.7071067811865476))
    density = jnp.exp(-0.5 * hidden * hidden) * 0.3989422804014327
    return hidden * share, share + hidden * density


def l2_rows(w, at, chunk, width):
    rows = width // 4
    return jnp.concatenate(
        [
            w[chunk * rows : (chunk + 1) * rows, at + g * width : at + (g + 1) * width]
            for g in range(4)
        ],
        0,
    )


def fetch_layer(sc_ref, groups, plan, width, w_vmem, sems):
    edges = (0, width, 5 * width, 9 * width)
    return [
        fetch(
            sc_ref, groups[plan[i][0]], plan[i][1], high - low, w_vmem.at[:, low:high], sems,
            PIECES * i,
        )
        for i, (low, high) in enumerate(zip(edges[:-1], edges[1:]))
    ]


def ff_forward(base, extra, copies, w_vmem, att_ref, stream, vec_ref, out_ref, n2_ref, active_ref,
               slope_ref, mid_ref, second_ref, h_scr, act_scr):
    rows, width = stream.shape
    scale_one = vec_ref[base + 2 : base + 3]
    gain_two = vec_ref[base + 3 : base + 4]
    bias_two = vec_ref[base + 4 : base + 5]
    scale_two = vec_ref[base + 5 : base + 6]
    wait_all(copies[0])
    middle = stream + scale_one * mm(att_ref[...], w_vmem[:, :width])
    mid_ref[...] = middle[extra:]
    normal, _ = normalize(middle)
    n2 = (normal * gain_two + bias_two).astype(bf16)
    n2_ref[...] = n2[extra:]
    wait_all(copies[1])
    l1_at, l2_at = width, 5 * width
    second = None
    for chunk in range(4):
        cols = slice(chunk * width, (chunk + 1) * width)
        h_scr[...] = mm(n2, w_vmem[:, l1_at + chunk * width : l1_at + (chunk + 1) * width])
        if extra:
            act, _ = gelu_both(h_scr[:extra, :])
            act_scr[:extra, cols] = act.astype(bf16)

        def body(i, _):
            at_row = pl.multiple_of(i * 16, 16)
            act, slope = gelu_both(h_scr[pl.ds(at_row + extra, 16), :])
            act_scr[pl.ds(at_row + extra, 16), cols] = act.astype(bf16)
            slope_ref[pl.ds(at_row, 16), cols] = slope
            return 0

        lax.fori_loop(0, (rows - extra) // 16, body, 0)
        if chunk == 0:
            wait_all(copies[2])
        part = mm(act_scr[:, cols], l2_rows(w_vmem, l2_at, chunk, width))
        second = part if second is None else second + part
    active_ref[...] = act_scr[extra:, :]
    second_ref[...] = second[extra:]
    out_ref[...] = (middle + scale_two * second).astype(bf16)


def ff_backward(base, extra, w_vmem, att_ref, g, vec_ref, slope_ref, mid_ref, second_ref, gmid_ref,
                dh_ref, dtwo_ref, done_ref, vg_ref, datt_scr):
    width = g.shape[1]
    scale_one = vec_ref[base + 2 : base + 3]
    gain_two = vec_ref[base + 3 : base + 4]
    scale_two = vec_ref[base + 5 : base + 6]
    l1_at, l2_at = width, 5 * width
    vg_ref[3:4, :] = column_sum(g * second_ref[...])
    d_two = (g * scale_two).astype(bf16)
    dtwo_ref[...] = d_two
    e = None
    for chunk in range(4):
        cols = slice(chunk * width, (chunk + 1) * width)
        d_active = mm_nt(d_two, l2_rows(w_vmem, l2_at, chunk, width))
        dh_ref[:, cols] = (d_active * slope_ref[:, cols]).astype(bf16)
        part = mm_nt(
            dh_ref[:, cols], w_vmem[:, l1_at + chunk * width : l1_at + (chunk + 1) * width]
        )
        e = part if e is None else e + part
    normal, scaled = normalize(mid_ref[...])
    vg_ref[1:2, :] = column_sum(e * normal)
    vg_ref[2:3, :] = column_sum(e)
    g_mid = g + norm_backward(e, normal, scaled, gain_two)
    gmid_ref[...] = g_mid
    vg_ref[0:1, :] = column_sum(g_mid * mm(att_ref[extra:, :], w_vmem[:, :width]))
    d_one = (g_mid * scale_one).astype(bf16)
    done_ref[...] = d_one
    datt_scr[...] = mm_nt(d_one, w_vmem[:, :width]).astype(bf16)


def decoder_layer_kernel(plan, sc_ref, *refs):
    (pieces,), refs = split_refs(refs, (PIECES,))
    (att_ref, x_ref, g_ref, vec_ref, q_ref, k_ref, v_ref,
     out_ref, n2_ref, active_ref, gmid_ref, dh_ref, dtwo_ref, done_ref, vg_ref,
     dq_ref, dk_ref, dv_ref, dkv_ref,
     w_vmem, h_scr, act_scr, slope_scr, mid_scr, second_scr, datt_scr, dk_scr, dv_scr, sems) = refs
    width = x_ref.shape[1]
    copies = fetch_layer(sc_ref, (pieces,), plan, width, w_vmem, sems)
    ff_forward(8, 0, copies, w_vmem, att_ref, x_ref[...], vec_ref, out_ref, n2_ref, active_ref,
               slope_scr, mid_scr, second_scr, h_scr, act_scr)
    ff_backward(8, 0, w_vmem, att_ref, g_ref[...].astype(f32), vec_ref, slope_scr, mid_scr,
                second_scr, gmid_ref, dh_ref, dtwo_ref, done_ref, vg_ref, datt_scr)
    attention_backward(0, sc_ref, q_ref, k_ref, v_ref, datt_scr, dq_ref, dk_ref, dv_ref, dkv_ref,
                       dk_scr, dv_scr)


def encoder_forward_kernel(plan, sc_ref, *refs):
    groups, refs = split_refs(refs, (PIECES, PIECES))
    (halo_ref, x_ref, att_ref, vec_ref,
     out_ref, n2_ref, active_ref, slope_ref, mid_ref, second_ref,
     w_vmem, h_scr, act_scr, sems) = refs
    width = x_ref.shape[1]
    copies = fetch_layer(sc_ref, groups, plan, width, w_vmem, sems)
    stream = jnp.concatenate([halo_ref[HALO - EXTRA :, :], x_ref[...]], 0).astype(f32)
    ff_forward(0, EXTRA, copies, w_vmem, att_ref, stream, vec_ref, out_ref, n2_ref, active_ref,
               slope_ref, mid_ref, second_ref, h_scr, act_scr)


def encoder_backward_kernel(plan, sc_ref, *refs):
    groups, refs = split_refs(refs, (PIECES, PIECES))
    (att_ref, g_ref, vec_ref, slope_ref, mid_ref, second_ref, q_ref, k_ref, v_ref,
     gmid_ref, dh_ref, dtwo_ref, done_ref, vg_ref, dq_ref, dk_ref, dv_ref, dkv_ref,
     w_vmem, datt_scr, dk_scr, dv_scr, sems) = refs
    width = g_ref.shape[1]
    for copies in fetch_layer(sc_ref, groups, plan, width, w_vmem, sems):
        wait_all(copies)
    ff_backward(0, EXTRA, w_vmem, att_ref, g_ref[...], vec_ref, slope_ref, mid_ref, second_ref,
                gmid_ref, dh_ref, dtwo_ref, done_ref, vg_ref, datt_scr)
    attention_backward(EXTRA, sc_ref, q_ref, k_ref, v_ref, datt_scr, dq_ref, dk_ref, dv_ref,
                       dkv_ref, dk_scr, dv_scr)


def attention_backward(extra, sc_ref, q_ref, k_ref, v_ref, do_ref,
                       dq_ref, dk_ref, dv_ref, dkv_ref, dk_scr, dv_scr):
    start, cut = sc_ref[0], sc_ref[1]
    frames = do_ref.shape[0]
    lanes = head_lanes()
    scale = HEAD_DIM ** (-0.5)
    dk_scr[...] = jnp.zeros_like(dk_scr)
    dv_scr[...] = jnp.zeros_like(dv_scr)
    wide = GROUP * QUERIES
    for first in range(0, frames, QUERIES):
        lane = lax.broadcasted_iota(jnp.int32, (1, wide), 1) % QUERIES
        query = start + first + lane
        low = lowest_key(query, cut)
        key = start + first - HALO + lax.broadcasted_iota(jnp.int32, (WINDOW, wide), 0)
        mask = (key <= query) & (key >= low)
        for group in range(HEADS // GROUP):
            cols = slice(group * GROUP * HEAD_DIM, (group + 1) * GROUP * HEAD_DIM)
            qs = stack_heads(q_ref[extra + first : extra + first + QUERIES, cols], lanes)
            ds = stack_heads(do_ref[first : first + QUERIES, cols], lanes)
            kw = k_ref[first : first + WINDOW, cols]
            vw = v_ref[first : first + WINDOW, cols]
            scores = jnp.where(mask, mm_nt(kw, qs) * scale, -1e30)
            exponent = jnp.exp(scores - jnp.max(scores, 0, keepdims=True))
            probs = exponent * (1.0 / jnp.sum(exponent, 0, keepdims=True))
            d_probs = mm_nt(vw, ds)
            mean = jnp.sum(probs * d_probs, 0, keepdims=True)
            d_scores = (probs * (d_probs - mean)).astype(bf16)
            dk_scr[first : first + WINDOW, cols] += mm(d_scores, qs)
            dv_scr[first : first + WINDOW, cols] += mm(probs.astype(bf16), ds)
            dq_ref[first : first + QUERIES, cols] = (
                unstack_heads(mm_tn(d_scores, kw), lanes) * scale
            )
    width = dq_ref.shape[1]
    dkv_ref[:, :width] = (dk_scr[:HALO] * scale).astype(bf16)
    dkv_ref[:, width:] = dv_scr[:HALO].astype(bf16)
    dk_ref[...] = dk_scr[HALO:] * scale
    dv_ref[...] = dv_scr[HALO:]


class Packer:
    def __init__(self, core, refs, shares, order):
        self.core, self.refs, self.shares, self.order = core, refs, shares, order

    def put(self, value, at, step=1, phase=0, block0=0):
        if len(self.refs) == 1:
            if step == 1:
                self.refs[0][:, at : at + value.shape[1]] = value.astype(bf16)
            return
        send, keep = self.refs
        cols = slice(at, at + value.shape[1])
        rows = 16
        hi = self.shares // 8
        blocks = value.shape[0] // (rows * step)
        for pair in range(blocks // 2):
            even = value[(2 * pair * step + phase) * rows :][:rows]
            odd = value[((2 * pair + 1) * step + phase) * rows :][:rows]
            block = (block0 + 2 * pair) // 2
            place = {"x": (block % 2, 2), "lo": (block // 2 % 2, 2), "hi": (block // 4, hi)}
            at_row = 0
            for axis in self.order:
                at_row = at_row * place[axis][1] + place[axis][0]
            at_row = at_row * rows
            first = self.core == 0
            keep[at_row : at_row + rows, cols] = jnp.where(first, even, odd).astype(bf16)
            send[at_row : at_row + rows, cols] = jnp.where(first, odd, even).astype(bf16)

    def put_l2(self, value, at, chunk, width):
        if len(self.refs) == 1:
            cols = slice(at + chunk * width, at + (chunk + 1) * width)
            self.refs[0][:, cols] = value.astype(bf16)
            return
        for phase in range(4):
            self.put(value, at + phase * width, 4, phase, chunk * width // 64)


def linear_gradients(pack, n2_ref, active_ref, dh_ref, dtwo_ref):
    width = n2_ref.shape[1]
    for chunk in range(4):
        cols = slice(chunk * width, (chunk + 1) * width)
        pack.put_l2(mm_tn(active_ref[:, cols], dtwo_ref[...]), 0, chunk, width)
        pack.put(mm_tn(n2_ref[...], dh_ref[:, cols]), (4 + chunk) * width)


def decoder_gradients_kernel(shares, sc_ref, n2_ref, active_ref, dh_ref, dtwo_ref, att_ref, done_ref,
                             *refs):
    pack = Packer(sc_ref[2], refs, shares, ORDER_A)
    linear_gradients(pack, n2_ref, active_ref, dh_ref, dtwo_ref)
    pack.put(mm_tn(att_ref[...], done_ref[...]), 8 * n2_ref.shape[1])


def encoder_gradients_kernel(shares, sc_ref, n2_ref, active_ref, dh_ref, dtwo_ref, att_ref, done_ref,
                             win_ref, dred_ref, red_ref, dlat_ref, *refs):
    width = n2_ref.shape[1]
    half = len(refs) // 2
    linear_gradients(
        Packer(sc_ref[2], refs[:half], shares, ORDER_C_ONE), n2_ref, active_ref, dh_ref, dtwo_ref
    )
    pack = Packer(sc_ref[2], refs[half:], shares, ORDER_C_TWO)
    d_reduced = dred_ref[...]
    for tap in range(4):
        pack.put(mm_tn(win_ref[tap], d_reduced), tap * width)
    pack.put(mm_tn(att_ref[EXTRA:, :], done_ref[...]), 4 * width)
    pack.put(mm_tn(red_ref[...], dlat_ref[...]), 5 * width)


def layer_input_gradient(base, dq_ref, dk_ref, dv_ref, dkv_ref, x, gmid_ref,
                         w_in, vec_ref, cos_ref, sin_ref, dmix_ref, vg_ref):
    frames, width = dq_ref.shape
    later = frames - HALO
    cos, sin = cos_ref[HALO:], -sin_ref[HALO:]
    for at in range(0, width, 128):
        cols = slice(at, at + 128)
        dmix_ref[:, cols] = rotate(dq_ref[:, cols], cos, sin).astype(bf16)
        keys = dk_ref[:, cols]
        keys = jnp.concatenate([keys[:later], keys[later:] + dkv_ref[:, cols].astype(f32)], 0)
        dmix_ref[:, width + at : width + at + 128] = rotate(keys, cos, sin).astype(bf16)
        values = dv_ref[:, cols]
        moved = dkv_ref[:, width + at : width + at + 128].astype(f32)
        values = jnp.concatenate([values[:later], values[later:] + moved], 0)
        dmix_ref[:, 2 * width + at : 2 * width + at + 128] = values.astype(bf16)
    d_normed = mm_nt(dmix_ref[...], w_in[...])
    normal, scaled = normalize(x)
    vg_ref[0:1, :] = column_sum(d_normed * normal)
    vg_ref[1:2, :] = column_sum(d_normed)
    return gmid_ref[...] + norm_backward(d_normed, normal, scaled, vec_ref[base : base + 1])


def decoder_back_kernel(at, sc_ref, *refs):
    pieces, refs = refs[:PIECES], refs[PIECES:]
    (dq_ref, dk_ref, dv_ref, dkv_ref, x_ref, gmid_ref, vec_ref, cos_ref, sin_ref,
     dup_ref, dmix_ref, vg_ref, w_vmem, sems) = refs
    wait_all(fetch(sc_ref, pieces, at, w_vmem.shape[1], w_vmem, sems))
    grad = layer_input_gradient(
        8, dq_ref, dk_ref, dv_ref, dkv_ref, x_ref[...], gmid_ref, w_vmem, vec_ref,
        cos_ref, sin_ref, dmix_ref, vg_ref,
    )
    vg_ref[2:3, :] = column_sum(grad)
    dup_ref[...] = grad.astype(bf16)


def encoder_back_kernel(shares, sc_ref, *refs):
    (pieces,), refs = split_refs(refs, (PIECES,))
    (dq_ref, dk_ref, dv_ref, dkv_ref, x_ref, gmid_ref, vec_ref, cos_ref, sin_ref, n1_ref,
     vgs_ref, grad_ref, *rest) = refs
    refs, (w_vmem, dmix_scr, vg_scr, all_scr, sems) = rest[:-5], rest[-5:]
    width = x_ref.shape[1]
    wait_all(fetch(sc_ref, pieces, 0, w_vmem.shape[1], w_vmem, sems))
    grad = layer_input_gradient(
        0, dq_ref, dk_ref, dv_ref, dkv_ref, x_ref[...].astype(f32), gmid_ref, w_vmem,
        vec_ref, cos_ref, sin_ref, dmix_scr, vg_scr,
    )
    grad_ref[...] = grad.astype(bf16)
    pack = Packer(sc_ref[2], refs, shares, ORDER_D)
    for part in range(3):
        cols = slice(part * width, (part + 1) * width)
        pack.put(mm_tn(n1_ref[...], dmix_scr[:, cols]), part * width)
    all_scr[...] = jnp.zeros_like(all_scr)
    all_scr[0:2, :] = vg_scr[0:2, :]
    all_scr[2:6, :] = vgs_ref[0:4, :]
    all_scr[6:7, :] = vgs_ref[16:17, :]
    all_scr[7:8, :] = vgs_ref[26:27, :]
    all_scr[8:10, :] = vgs_ref[24:26, :]
    all_scr[10:14, :] = vgs_ref[8:12, :]
    pack.put(all_scr[...].T, 3 * width)


def middle_kernel(shares, sc_ref, *refs):
    (pieces, more), refs = split_refs(refs, (PIECES, PIECES))
    (dup_ref, next_ref, dmix_ref, n1_ref, restored_ref, qz_ref,
     denc_ref, dred_ref, dlat_ref, vg_ref, *rest) = refs
    refs, (up_vmem, down_vmem, frame_scr, sems) = rest[:-4], rest[-4:]
    frames, width = dup_ref.shape
    latent = qz_ref.shape[1]
    codec = frames // 2
    copies = [
        fetch(sc_ref, pieces, 0, latent + 4 * width, up_vmem, sems),
        fetch(sc_ref, more, 4 * width, 4 * width + latent, down_vmem, sems, PIECES),
    ]
    pairs = codec + 16
    even, odd = split_rows(
        jnp.concatenate([dup_ref[...], next_ref[...]], 0).astype(f32), frame_scr
    )
    both = jnp.concatenate([even, odd], 1).astype(bf16)
    wait_all(copies[0])
    up = up_vmem[:, latent : latent + 4 * width]
    here = mm_nt(both, up[:, : 2 * width])
    later = mm_nt(both, up[:, 2 * width :])
    d_restored = (here + pltpu.roll(later, pairs - 1, 0)).astype(bf16)
    d_latent = mm(d_restored, up_vmem[:, :latent]).astype(bf16)
    wait_all(copies[1])
    d_reduced = mm_nt(d_latent, down_vmem[:, 4 * width :]).astype(bf16)
    dlat_ref[...] = d_latent[:codec]
    dred_ref[...] = d_reduced[:codec]
    vg_ref[0:1, :] = column_sum(d_reduced[:codec].astype(f32))
    taps = [mm_nt(d_reduced, down_vmem[:, tap * width : (tap + 1) * width]) for tap in range(4)]
    denc_ref[...] = interleave(
        taps[2] + pltpu.roll(taps[0], pairs - 1, 0),
        taps[3] + pltpu.roll(taps[1], pairs - 1, 0),
        frame_scr,
    )[:frames]

    pack = Packer(sc_ref[2], refs, shares, ORDER_B)
    for part in range(3):
        cols = slice(part * width, (part + 1) * width)
        pack.put(mm_tn(n1_ref[...], dmix_ref[:, cols]), part * width)
    restored = restored_ref[...]
    own_pairs = both[:codec]
    before = pltpu.roll(restored.astype(f32), 1, 0)[16:].astype(bf16)
    pack.put(mm_tn(restored[16:], own_pairs[:, :width]), 3 * width)
    pack.put(mm_tn(restored[16:], own_pairs[:, width:]), 4 * width)
    pack.put(mm_tn(before, own_pairs[:, :width]), 5 * width)
    pack.put(mm_tn(before, own_pairs[:, width:]), 6 * width)
    pack.put(mm_tn(d_restored[:codec], qz_ref[CODE_HALO:, :]), 7 * width)


def latent_kernel(sc_ref, *refs):
    (pieces,), refs = split_refs(refs, (PIECES,))
    (enc_ref, rows_ref, vec_ref, res_ref, win_ref, red_ref, w_vmem, frame_scr, sems) = refs
    total, width = enc_ref.shape
    copies = fetch(sc_ref, pieces, 4 * width, w_vmem.shape[1], w_vmem, sems)
    inside = (sc_ref[0] > 0).astype(f32)
    rim = enc_ref[:EXTRA].astype(f32) * inside
    skip = EXTRA // 2
    even, odd = split_rows(jnp.concatenate([rim, enc_ref[EXTRA:].astype(f32)], 0), frame_scr)
    win_ref[0] = pltpu.roll(even, 1, 0)[skip:].astype(bf16)
    win_ref[1] = pltpu.roll(odd, 1, 0)[skip:].astype(bf16)
    win_ref[2] = even[skip:].astype(bf16)
    win_ref[3] = odd[skip:].astype(bf16)
    wait_all(copies)
    reduced = vec_ref[6:7]
    for tap in range(4):
        reduced = reduced + mm(win_ref[tap], w_vmem[:, tap * width : (tap + 1) * width])
    reduced = reduced.astype(bf16)
    red_ref[...] = reduced
    remaining = mm(reduced, w_vmem[:, 4 * width :])
    for level in range(rows_ref.shape[0]):
        res_ref[level] = remaining.astype(bf16)
        remaining = remaining - rows_ref[level].astype(f32)


def lookup_kernel(sc_ref, codes_ref, book_ref, qsend_ref, qkeep_ref, rsend_ref, rkeep_ref, q_scr):
    levels, share, latent = book_ref.shape
    total = codes_ref.shape[0]
    codec = total // 4
    base = sc_ref[3]
    core = sc_ref[2]
    entry = lax.broadcasted_iota(jnp.int32, (1, share), 1)
    for level in range(levels):
        picks = (codes_ref[:, level : level + 1] - base == entry).astype(f32).astype(bf16)
        found = mm(picks, book_ref[level])
        q_scr[CODE_HALO:] = found if level == 0 else q_scr[CODE_HALO:] + found
        for x in range(2):
            even = found[(2 * x) * codec :][:codec]
            odd = found[(2 * x + 1) * codec :][:codec]
            rkeep_ref[x, level] = jnp.where(core == 0, even, odd).astype(bf16)
            rsend_ref[x, level] = jnp.where(core == 0, odd, even).astype(bf16)
    q_scr[:CODE_HALO] = jnp.zeros((CODE_HALO, latent), f32)
    for x in range(2):
        even = q_scr[(2 * x) * codec : (2 * x + 1) * codec + CODE_HALO]
        odd = q_scr[(2 * x + 1) * codec : (2 * x + 2) * codec + CODE_HALO]
        qkeep_ref[x] = jnp.where(core == 0, even, odd)
        qsend_ref[x] = jnp.where(core == 0, odd, even)


def collect_kernel(share, seq_count, sc_ref, own_ref, x_ref, core_ref, far_ref, codes_ref,
                   marked_ref, send_ref, keep_ref, row_scr, cnt_scr):
    levels, codec, latent = own_ref.shape
    total = codes_ref.shape[1]
    lo = sc_ref[4]
    high = send_ref.shape[0]
    frame = lax.broadcasted_iota(jnp.int32, (1, total), 1) + sc_ref[6]
    row = lax.broadcasted_iota(jnp.int32, (2 * high * share, 1), 0)
    entry = (row // share * seq_count + sc_ref[5]) * share + row % share
    ones = jnp.ones((16, total), bf16)
    for level in range(levels):
        marked = marked_ref[:, level : level + 1]
        used = (entry == codes_ref[level : level + 1, :]).astype(f32)
        placed = (marked // 2 == frame).astype(f32)
        select = jnp.where(marked % 2 == 1, placed, used).astype(bf16)
        for place, ref in enumerate((own_ref, x_ref, core_ref, far_ref)):
            at_row = pl.multiple_of(sc_ref[14 + place], 32)
            row_scr[pl.ds(at_row, codec), :] = ref[level]
        sums = mm(select, row_scr[...])
        cnt_scr[level : level + 1, :] = mm_nt(ones, used.astype(bf16))[0:1]
        at = slice(level * share, (level + 1) * share)
        for h in range(high):
            even = sums[(2 * h) * share :][:share]
            odd = sums[(2 * h + 1) * share :][:share]
            keep_ref[h, at, :] = jnp.where(lo == 0, even, odd).astype(bf16)
            send_ref[h, at, :] = jnp.where(lo == 0, odd, even).astype(bf16)
    counts = cnt_scr[...]
    upper = jnp.floor(counts * (1.0 / 128.0))
    digits = jnp.concatenate([upper, counts - 128.0 * upper], 0)
    tail = slice(levels * share, levels * share + 2 * levels)
    for h in range(high):
        even = digits[:, (2 * h) * share : (2 * h + 1) * share]
        odd = digits[:, (2 * h + 1) * share : (2 * h + 2) * share]
        keep_ref[h, tail, :] = jnp.zeros((2 * levels, latent), bf16)
        send_ref[h, tail, :] = jnp.zeros((2 * levels, latent), bf16)
        keep_ref[h, tail, :share] = jnp.where(lo == 0, even, odd).astype(bf16)
        send_ref[h, tail, :share] = jnp.where(lo == 0, odd, even).astype(bf16)


def call(kernel, outs, spaces, scratch, args, micros):
    where = {"s": pltpu.SMEM, "v": pltpu.VMEM, "h": pltpu.HBM}
    title = getattr(kernel, "func", kernel).__name__
    return pl.pallas_call(
        kernel,
        name=title,
        out_shape=outs,
        in_specs=[pl.BlockSpec(memory_space=where[space]) for space in spaces],
        out_specs=[pl.BlockSpec(memory_space=pltpu.VMEM) for _ in outs],
        scratch_shapes=scratch,
        compiler_params=pltpu.CompilerParams(vmem_limit_bytes=VMEM_LIMIT),
        cost_estimate=pl.CostEstimate(
            flops=int(micros * 1e6), bytes_accessed=1, transcendentals=0
        ),
    )(*args)


def shape(dims, dtype=f32):
    return jax.ShapeDtypeStruct(dims, dtype)


def pick(block, at):
    zero = jnp.zeros((), jnp.uint32)
    start = (at,) + (zero,) * (block.ndim - 1)
    return lax.dynamic_slice(block, start, (1,) + block.shape[1:])[0]


def halve(block, axis, index, after=None):
    sent = pick(block, index["other " + axis])
    kept = pick(block, index[axis])
    got = lax.ppermute(sent, axis, [(0, 1), (1, 0)])
    if after is not None:
        got, _ = tie(got, after)
    return (kept.astype(f32) + got.astype(f32)).astype(block.dtype)


def sum_by_permutes(block, index, after=None):
    count = block.shape[0]
    if count != 4:
        return sum_over_hi(block)
    total = pick(block, index["hi"]).astype(f32)
    for turn in range(1, count):
        sent = pick(block, index["hi ^ %d" % turn])
        got = lax.ppermute(sent, "hi", [(i, i ^ turn) for i in range(count)])
        if after is not None:
            got, _ = tie(got, after)
        total = total + got.astype(f32)
    return total


def swap_add(send, keep, axis, after=None):
    got = lax.ppermute(send, axis, [(0, 1), (1, 0)])
    if after is not None:
        got, _ = tie(got, after)
    return (keep.astype(f32) + got.astype(f32)).astype(keep.dtype)


def sum_over_hi(block):
    parts = lax.all_to_all(block, "hi", 0, 0, tiled=True)
    return jnp.sum(parts.astype(f32), 0)


def shifted(block, distance):
    devices = range(lax.axis_size(SEQ))
    route = [(i - distance, i) for i in devices if i - distance in devices]
    return lax.ppermute(block, SEQ, route)


def packed_outs(width_total, width, shares):
    if width // shares % 16 == 0:
        return [shape((width // 2, width_total), bf16)] * 2
    return [shape((width, width_total), bf16)]


def swap(block, axis):
    return lax.ppermute(block, axis, [(0, 1), (1, 0)])


def tie(*values):
    return lax.optimization_barrier(values)


def half_of(share, index):
    rows = share.shape[0] // 2
    zero = jnp.zeros((), jnp.uint32)
    return lax.dynamic_slice(share, (index["lo"] * rows, zero), (rows, share.shape[1]))


def both_halves(near, far, index):
    first = index["lo"] == 0
    return jnp.concatenate([jnp.where(first, near, far), jnp.where(first, far, near)], 0)


def unfolded_rows(block, shares, l2_at):
    width = block.shape[0]
    full = [block[:, l2_at + i * width : l2_at + (i + 1) * width] for i in range(4)]
    full = jnp.concatenate(full, 0).reshape(shares, 4, width // shares, width)
    full = full.transpose(0, 2, 1, 3).reshape(width, 4 * width)
    return jnp.concatenate([block[:, :l2_at], full, block[:, l2_at + 4 * width :]], 1)


def first_sum(parts, shares, order, index, l2_at=None):
    if len(parts) == 2:
        return swap_add(*parts, "core")
    (block,) = parts
    if l2_at is not None:
        block = unfolded_rows(block, shares, l2_at)
    width, total = block.shape
    block = block.reshape(shares // 8, 2, 2, 2, width // shares, total)
    block = halve(block.transpose(3, 0, 1, 2, 4, 5), "core", index)
    places = [("hi", "lo", "x").index(axis) for axis in order]
    return block.transpose(*places, 3, 4).reshape(width // 2, total)


def next_sum(block, axis, index, after=None):
    rows, total = block.shape
    return halve(block.reshape(2, rows // 2, total), axis, index, after)


def last_sum(block, high):
    return sum_over_hi(block.reshape(high, -1, block.shape[1]))


def local(
    activations,
    encoder_attention_norm_gain,
    encoder_attention_norm_bias,
    encoder_query_key_value_weight,
    encoder_attention_output_weight,
    encoder_attention_layer_scale,
    encoder_forward_norm_gain,
    encoder_forward_norm_bias,
    encoder_forward_input_weight,
    encoder_forward_output_weight,
    encoder_forward_layer_scale,
    strided_convolution_weight,
    strided_convolution_bias,
    quantizer_input_weight,
    codebook,
    quantizer_output_weight,
    transposed_convolution_weight,
    transposed_convolution_bias,
    decoder_attention_norm_gain,
    decoder_attention_norm_bias,
    decoder_query_key_value_weight,
    decoder_attention_output_weight,
    decoder_attention_layer_scale,
    decoder_forward_norm_gain,
    decoder_forward_norm_bias,
    decoder_forward_input_weight,
    decoder_forward_output_weight,
    decoder_forward_layer_scale,
    cotangent,
    frame_segment_index,
    frame_code_index,
    replace_code_mask,
    replacing_batch_position,
    code_usage_average,
    code_latent_sum_average,
):
    batch_rows, frames, width = activations.shape
    assert batch_rows == 1
    seq_index = lax.axis_index(SEQ)
    seq_count = lax.axis_size(SEQ)
    dp_index = lax.axis_index(DP)
    dp_count = lax.axis_size(DP)
    shares = dp_count * seq_count
    codec = frames // 2
    levels = frame_code_index.shape[2]
    latent = codebook.shape[2]
    book_share = codebook.shape[1]
    core_index = lax.axis_index("core")

    x_index, lo_index = lax.axis_index("x"), lax.axis_index("lo")
    rows_share = width // seq_count
    high = shares // 8
    total_frames = HALO + frames
    code_total = replace_code_mask.shape[1]
    code_share = code_usage_average.shape[1]
    row_frames = codec * seq_count

    vectors = jnp.stack(
        [
            encoder_attention_norm_gain,
            encoder_attention_norm_bias,
            encoder_attention_layer_scale,
            encoder_forward_norm_gain,
            encoder_forward_norm_bias,
            encoder_forward_layer_scale,
            strided_convolution_bias,
            transposed_convolution_bias,
            decoder_attention_norm_gain,
            decoder_attention_norm_bias,
            decoder_attention_layer_scale,
            decoder_forward_norm_gain,
            decoder_forward_norm_bias,
            decoder_forward_layer_scale,
        ]
    )
    vectors = jnp.pad(vectors, ((0, 2), (0, 0)))
    small = jnp.concatenate(
        [frame_code_index.reshape(-1).astype(f32), vectors.reshape(-1).astype(f32)]
    )
    index = {}
    unsigned = jnp.uint32
    for axis in ("x", "lo", "core"):
        index[axis] = lax.axis_index(axis).astype(unsigned)
        index["other " + axis] = (1 - lax.axis_index(axis)).astype(unsigned)
    index["hi"] = lax.axis_index("hi").astype(unsigned)
    index["seq"] = lax.axis_index(SEQ).astype(unsigned)
    index["owner"] = (lax.axis_index(DP + SEQ) * code_share).astype(unsigned)
    for turn in range(1, 4):
        index["hi ^ %d" % turn] = lax.axis_index("hi").astype(unsigned) ^ unsigned(turn)
    def flat_taps(taps):
        return taps.transpose(1, 0, 2).reshape(taps.shape[1], -1)

    def fold_l2(share):
        return share.reshape(4, -1, width).transpose(1, 0, 2).reshape(-1, 4 * width)

    dec_one = jnp.concatenate(
        [
            quantizer_output_weight.T,
            flat_taps(transposed_convolution_weight),
            decoder_query_key_value_weight,
        ],
        1,
    )
    half_one = half_of(dec_one, index)
    small, half_one = tie(small, half_one)
    small = lax.all_gather(small, SEQ, axis=0, tiled=False)
    names = sorted(index)
    *index_values, small = tie(*[index[name] for name in names], small)
    index = dict(zip(names, index_values))
    code_count = codec * levels
    row_codes = small[:, :code_count].astype(jnp.int32).reshape(seq_count, codec, levels)
    vectors = small[:, code_count:].reshape(seq_count, 16, -1).transpose(1, 0, 2).reshape(16, width)
    order = [2 * x_index + core_index, 2 * (1 - x_index) + core_index]
    order += [2 * x_index + 1 - core_index, 2 * (1 - x_index) + 1 - core_index]
    cut = jnp.sum((frame_segment_index[0] == 0).astype(jnp.int32))
    scalars = jnp.stack(
        [
            seq_index * frames,
            cut,
            core_index,
            seq_index * book_share,
            lo_index,
            seq_index,
            dp_index * row_frames,
            seq_index,
        ]
        + [
            *[place * rows_share for place in order],
            seq_index,
            seq_index,
        ]
        + [place * codec for place in order]
    ).astype(jnp.int32)

    half_one, _ = tie(half_one, small)
    near_one = swap(half_one, "x")
    core_one = swap(dec_one, "core")
    activation_halo = shifted(activations[0, frames - HALO :], 1)

    positions = seq_index * frames - HALO + jnp.arange(total_frames, dtype=jnp.int32)
    half_dim = HEAD_DIM // 2
    frequency = jnp.power(10000.0, -jnp.arange(half_dim, dtype=f32) / half_dim)

    def angle_tables(positions):
        angles = positions.astype(f32)[:, None] * frequency[None, :]
        cos, sin = jnp.cos(angles), jnp.sin(angles)
        return jnp.concatenate([cos] * 4, 1), jnp.concatenate([-sin, sin, -sin, sin], 1)

    row_codes, activation_halo, core_one = tie(row_codes, activation_halo, core_one)

    window = codec + CODE_HALO
    qsend, qkeep, rsend, rkeep = call(
        lookup_kernel,
        [shape((2, window, latent))] * 2 + [shape((2, levels, codec, latent), bf16)] * 2,
        "svv",
        [pltpu.VMEM((CODE_HALO + codec * seq_count, latent), f32)],
        (scalars, row_codes.reshape(-1, levels), codebook),
        4,
    )
    q_sum = swap_add(qsend, qkeep, "core")
    q_sent = pick(q_sum, index["other x"])
    q_got = swap(q_sent, "x")
    (near_one, positions, dec_l2, enc_in, enc_l2, down_share, replace_code_mask,
     replacing_batch_position, row_codes, _) = tie(
        near_one, positions, decoder_forward_output_weight, encoder_query_key_value_weight,
        encoder_forward_output_weight, strided_convolution_weight, replace_code_mask,
        replacing_batch_position, row_codes, q_sent,
    )
    dec_two = jnp.concatenate(
        [decoder_attention_output_weight, decoder_forward_input_weight, fold_l2(dec_l2)], 1
    )
    enc_one = jnp.concatenate(
        [
            enc_in,
            encoder_attention_output_weight,
            flat_taps(down_share),
            quantizer_input_weight,
        ],
        1,
    )
    marked = (replacing_batch_position * 2 + replace_code_mask).T
    marked = marked.reshape(dp_count, seq_count, code_share, levels).transpose(1, 0, 2, 3)
    marked = pick(marked, index["seq"]).reshape(dp_count * code_share, levels)
    code_columns = row_codes.reshape(row_frames, levels).T
    owner_flag = lax.dynamic_slice(
        replace_code_mask, (jnp.zeros((), unsigned), index["owner"]), (levels, code_share)
    ) == 1
    far_one = swap(near_one, "lo")
    near_one = both_halves(near_one, far_one, index)
    dec_one = [dec_one, near_one, core_one, swap(near_one, "core")]
    half_two = half_of(dec_two, index)
    cos_table, sin_table = angle_tables(positions)
    near_two = swap(half_two, "x")
    quantized = (pick(q_sum, index["x"]) + q_got).astype(bf16)
    half_three = half_of(enc_one, index)
    (quantized, near_two, half_three, activation_halo, cos_table, sin_table, marked,
     code_columns, owner_flag) = tie(
        quantized, near_two, half_three, activation_halo, cos_table, sin_table, marked,
        code_columns, owner_flag,
    )
    core_two = swap(dec_two, "core")
    far_two = swap(near_two, "lo")
    near_three = swap(half_three, "x")

    d_x, restored, d_n1, d_q, d_k, d_v, d_att = call(
        decoder_front_kernel,
        [
            shape((frames, width)),
            shape((codec + 16, width), bf16),
            shape((frames, width), bf16),
            shape((frames, width), bf16),
            shape((total_frames, width), bf16),
            shape((total_frames, width), bf16),
            shape((frames, width), bf16),
        ],
        "s" + "h" * PIECES + "vvvv",
        [
            pltpu.VMEM((width, latent + 7 * width), bf16),
            pltpu.VMEM((width // 128, total_frames, 128), f32),
            pltpu.SemaphoreType.DMA((PIECES,)),
        ],
        (scalars, *dec_one, quantized, vectors, cos_table, sin_table),
        8,
    )
    d_att, far_two, near_three, enc_l2, rsend = tie(d_att, far_two, near_three, enc_l2, rsend)
    enc_two = jnp.concatenate([encoder_forward_input_weight, fold_l2(enc_l2)], 1)
    half_four = half_of(enc_two, index)
    code_rows = swap_add(rsend, rkeep, "core")
    near_two = both_halves(near_two, far_two, index)
    dec_two = [dec_two, near_two, core_two, swap(near_two, "core")]
    far_three = swap(near_three, "lo")
    near_four = swap(half_four, "x")
    layer_scratch = [
        pltpu.VMEM((frames, width), bf16),
        pltpu.VMEM((total_frames, width), f32),
        pltpu.VMEM((total_frames, width), f32),
        pltpu.SemaphoreType.DMA((3 * PIECES,)),
    ]
    forward_outs = [shape((frames, width), bf16), shape((frames, 4 * width), bf16)]
    kept_outs = [shape((frames, 4 * width)), shape((frames, width)), shape((frames, width))]
    backward_outs = [
        shape((frames, width)),
        shape((frames, 4 * width), bf16),
        shape((frames, width), bf16),
        shape((frames, width), bf16),
        shape((8, width)),
        shape((frames, width)),
        shape((frames, width)),
        shape((frames, width)),
        shape((HALO, 2 * width), bf16),
    ]
    weights_scratch = pltpu.VMEM((width, 9 * width), bf16)
    (output, d_n2, d_active, d_gmid, d_dh, d_dtwo, d_done, d_vg_two, d_dq, d_dk, d_dv, d_dkv) = call(
        partial(decoder_layer_kernel, ((0, 0), (0, width), (0, 5 * width))),
        [shape((frames, width), bf16)] + forward_outs + backward_outs,
        "s" + "h" * PIECES + "vvvvvvv",
        [
            weights_scratch,
            pltpu.VMEM((frames, width), f32),
            pltpu.VMEM((frames, 4 * width), bf16),
            pltpu.VMEM((frames, 4 * width), f32),
            pltpu.VMEM((frames, width), f32),
            pltpu.VMEM((frames, width), f32),
        ]
        + layer_scratch,
        (scalars, *dec_two, d_att, d_x, cotangent[0], vectors, d_q, d_k, d_v),
        14,
    )
    d_n2, far_three, near_four, code_rows = tie(d_n2, far_three, near_four, code_rows)
    near_three = both_halves(near_three, far_three, index)
    enc_one = [enc_one, near_three, swap(enc_one, "core"), swap(near_three, "core")]
    far_four = swap(near_four, "lo")
    d_dkv = shifted(d_dkv, -1)
    group_a = call(
        partial(decoder_gradients_kernel, shares),
        packed_outs(9 * width, width, shares),
        "svvvvvv",
        [],
        (scalars, d_n2, d_active, d_dh, d_dtwo, d_att, d_done),
        5,
    )
    d_dq, *group_a = tie(d_dq, *group_a)
    code_rows, d_dkv = tie(code_rows, d_dkv)
    code_rows = halve(code_rows, "x", index)
    a_sum = first_sum(group_a, shares, ORDER_A, index, 0)
    d_dq, a_sum = tie(d_dq, a_sum)
    d_up, d_mixed, d_vg_one = call(
        partial(decoder_back_kernel, latent + 4 * width),
        [shape((frames, width), bf16), shape((frames, 3 * width), bf16), shape((8, width))],
        "s" + "h" * PIECES + "v" * 9,
        [pltpu.VMEM((width, 3 * width), bf16), pltpu.SemaphoreType.DMA((PIECES,))],
        (
            scalars, *dec_one, d_dq, d_dk, d_dv, d_dkv, d_x, d_gmid, vectors, cos_table,
            sin_table,
        ),
        4,
    )
    d_up_next = shifted(d_up[:32], -1)


    a_sum, d_up, e_input, far_four, code_rows = tie(
        a_sum, d_up, activations[0], far_four, code_rows
    )
    near_four = both_halves(near_four, far_four, index)
    enc_two = [enc_two, near_four, swap(enc_two, "core"), swap(near_four, "core")]
    a_sum = next_sum(a_sum, ORDER_A[0], index)
    e_n1, e_q, e_k, e_v, e_att = call(
        encoder_front_kernel,
        [
            shape((frames, width), bf16),
            shape((frames + EXTRA, width), bf16),
            shape((total_frames, width), bf16),
            shape((total_frames, width), bf16),
            shape((frames + EXTRA, width), bf16),
        ],
        "s" + "h" * PIECES + "vvvvv",
        [pltpu.VMEM((width, 3 * width), bf16), pltpu.SemaphoreType.DMA((PIECES,))],
        (scalars, *enc_one, activation_halo, e_input, vectors, cos_table, sin_table),
        7,
    )

    d_mixed, e_n1 = tie(d_mixed, e_n1)
    middle_outs = call(
        partial(middle_kernel, shares),
        [
            shape((frames, width)),
            shape((codec, width), bf16),
            shape((codec, latent), bf16),
            shape((8, width)),
        ]
        + packed_outs(7 * width + latent, width, shares),
        "s" + "h" * (2 * PIECES) + "" + "v" * 6,
        [
            pltpu.VMEM((width, latent + 4 * width), bf16),
            pltpu.VMEM((width, latent + 4 * width), bf16),
            pltpu.VMEM((width // 128, frames + 32, 128), f32),
            pltpu.SemaphoreType.DMA((2 * PIECES,)),
        ],
        (scalars, *dec_one, *enc_one, d_up, d_up_next, d_mixed, d_n1, restored, quantized),
        7,
    )
    d_encoded, d_reduced, d_latent, m_vg = middle_outs[:4]
    b_sum = first_sum(middle_outs[4:], shares, ORDER_B, index)

    e_att, d_encoded = tie(e_att, d_encoded)
    enc_plan = ((0, 3 * width), (1, 0), (1, 4 * width))
    rows = frames + EXTRA
    encoded, e_n2, e_active, e_slope, e_mid, e_second = call(
        partial(encoder_forward_kernel, enc_plan),
        [shape((rows, width), bf16)] + forward_outs + kept_outs,
        "s" + "h" * (2 * PIECES) + "vvvv",
        [
            weights_scratch,
            pltpu.VMEM((rows, width), f32),
            pltpu.VMEM((rows, 4 * width), bf16),
            pltpu.SemaphoreType.DMA((3 * PIECES,)),
        ],
        (scalars, *enc_one, *enc_two, activation_halo, e_input, e_att, vectors),
        6,
    )
    encoded, b_sum, a_sum = tie(encoded, b_sum, a_sum)
    b_sum = next_sum(b_sum, ORDER_B[0], index)
    residuals, windows, reduced = call(
        latent_kernel,
        [
            shape((levels, codec, latent), bf16),
            shape((4, codec, width), bf16),
            shape((codec, width), bf16),
        ],
        "s" + "h" * PIECES + "vvv",
        [
            pltpu.VMEM((width, 4 * width + latent), bf16),
            pltpu.VMEM((width // 128, frames + EXTRA, 128), f32),
            pltpu.SemaphoreType.DMA((PIECES,)),
        ],
        (scalars, *enc_one, encoded, code_rows, vectors),
        3,
    )
    near_res = swap(residuals, "x")
    core_res = swap(residuals, "core")

    d_encoded, _ = tie(d_encoded, residuals)
    a_sum = next_sum(a_sum, ORDER_A[1], index)
    (e_gmid, e_dh, e_dtwo, e_done, e_vg_two, e_dq, e_dk, e_dv, e_dkv) = call(
        partial(encoder_backward_kernel, enc_plan),
        backward_outs,
        "s" + "h" * (2 * PIECES) + "v" * 9,
        [weights_scratch] + layer_scratch,
        (
            scalars, *enc_one, *enc_two, e_att, d_encoded, vectors, e_slope, e_mid, e_second,
            e_q, e_k, e_v,
        ),
        11,
    )
    e_dkv = shifted(e_dkv, -1)
    near_res, core_res, _ = tie(near_res, core_res, e_gmid)
    res_pieces = [residuals, near_res, core_res, swap(near_res, "core")]

    code_columns, b_sum = tie(code_columns, b_sum)
    if code_share % 16 == 0:
        tail_rows = levels * code_share
        csend, ckeep = call(
            partial(collect_kernel, code_share, seq_count),
            [shape((dp_count // 2, tail_rows + 2 * levels, latent), bf16)] * 2,
            "svvvvvv",
            [
                pltpu.VMEM((row_frames, latent), bf16),
                pltpu.VMEM((levels, dp_count * code_share), f32),
            ],
            (scalars, *res_pieces, code_columns, marked),
            5,
        )
        e_n2, csend, e_gmid, e_dkv = tie(e_n2, csend, e_gmid, e_dkv)
    c_outs = packed_outs(8 * width, width, shares)
    group_c = call(
        partial(encoder_gradients_kernel, shares),
        c_outs + packed_outs(5 * width + latent, width, shares),
        "s" + "v" * 10,
        [],
        (
            scalars, e_n2, e_active, e_dh, e_dtwo, e_att, e_done, windows, d_reduced, reduced,
            d_latent,
        ),
        5,
    )
    e_dq, *group_c = tie(e_dq, *group_c)
    c_one = first_sum(group_c[: len(c_outs)], shares, ORDER_C_ONE, index, 0)
    c_two = first_sum(group_c[len(c_outs) :], shares, ORDER_C_TWO, index)
    e_dq, c_one, c_two, a_sum, b_sum = tie(e_dq, c_one, c_two, a_sum, b_sum)
    vector_grads = jnp.concatenate([e_vg_two, d_vg_two, m_vg, d_vg_one], 0)
    grad_outs = call(
        partial(encoder_back_kernel, shares),
        [shape((frames, width), bf16)] + packed_outs(3 * width + 128, width, shares),
        "s" + "h" * PIECES + "v" * 11,
        [
            pltpu.VMEM((width, 3 * width), bf16),
            pltpu.VMEM((frames, 3 * width), bf16),
            pltpu.VMEM((8, width), f32),
            pltpu.VMEM((128, width), f32),
            pltpu.SemaphoreType.DMA((PIECES,)),
        ],
        (
            scalars, *enc_one, e_dq, e_dk, e_dv, e_dkv, e_input, e_gmid, vectors,
            cos_table, sin_table, e_n1, vector_grads,
        ),
        5,
    )
    activations_grad = grad_outs[0]

    def z_sum(block):
        return sum_by_permutes(block.reshape(high, -1, block.shape[1]), index, activations_grad)

    d_sum = first_sum(grad_outs[1:], shares, ORDER_D, index)
    b_sum = next_sum(b_sum, ORDER_B[1], index, d_sum)
    if code_share % 16 == 0:
        combined = swap_add(csend, ckeep, "lo", b_sum)
        c_one = next_sum(c_one, ORDER_C_ONE[0], index, combined)
        a_sum, _ = tie(a_sum, activations_grad)
        grads_a = last_sum(a_sum, high)
        b_sum, grads_a = tie(b_sum, grads_a)
        grads_b = last_sum(b_sum, high)
        combined, grads_b = tie(combined, grads_b)
        combined = sum_over_hi(combined)
    else:
        entry = (
            jnp.arange(dp_count, dtype=jnp.int32)[:, None] * seq_count + seq_index
        ) * code_share + jnp.arange(code_share, dtype=jnp.int32)
        relative = [place * codec + jnp.arange(codec, dtype=jnp.int32) for place in order]
        relative = jnp.concatenate(relative)
        flat_res = jnp.concatenate(res_pieces, 1)
        used = entry.reshape(1, -1, 1) == code_columns[:, None, relative]
        placed = (marked.T // 2)[:, :, None] == dp_index * row_frames + relative
        counts = jnp.sum(used.astype(f32), 2).reshape(levels, dp_count, code_share)
        selects = jnp.where((marked.T % 2)[:, :, None] == 1, placed, used).astype(bf16)
        sums = jnp.einsum("lct,ltd->lcd", selects, flat_res, preferred_element_type=f32)
        sums = sums.astype(bf16).reshape(levels, dp_count, code_share, latent)
        grads_a, grads_b = last_sum(a_sum, high), last_sum(b_sum, high)
        c_one = next_sum(c_one, ORDER_C_ONE[0], index)
        summed = lax.psum_scatter(sums, DP, scatter_dimension=1, tiled=False).astype(f32)
        counted = lax.psum_scatter(counts, DP, scatter_dimension=1, tiled=False)
    c_two = next_sum(c_two, ORDER_C_TWO[0], index, c_one)
    d_sum = next_sum(d_sum, ORDER_D[0], index, c_two)
    c_two = next_sum(c_two, ORDER_C_TWO[1], index, d_sum)
    d_sum = next_sum(d_sum, ORDER_D[1], index, c_two)
    c_one = next_sum(c_one, ORDER_C_ONE[1], index, d_sum)
    if code_share % 16 == 0:
        d_sum, combined = tie(d_sum, combined)
        summed = combined[:tail_rows].reshape(levels, code_share, latent)
        digits = combined[tail_rows:, :code_share]
        counted = 128.0 * digits[:levels] + digits[levels:]
    edge, far_edge = c_one.shape[1], c_one.shape[1] + c_two.shape[1]
    together = last_sum(jnp.concatenate([c_one, c_two, d_sum], 1), high)
    grads_c, grads_c_two, grads_d = (
        together[:, :edge], together[:, edge:far_edge], together[:, far_edge:]
    )

    new_cluster_size = ema_decay * code_usage_average + (1.0 - ema_decay) * counted
    new_embed_sum = jnp.where(
        owner_flag[:, :, None],
        summed * new_cluster_size[:, :, None],
        ema_decay * code_latent_sum_average + (1.0 - ema_decay) * summed,
    )
    new_codebook = new_embed_sum / new_cluster_size[:, :, None]

    def columns(block, at, count):
        return block[:, at * width : (at + count) * width]

    def taps(block):
        return block.reshape(-1, 4, width).transpose(1, 0, 2)

    def unfold(block):
        return block.reshape(-1, 4, width).transpose(1, 0, 2).reshape(-1, width)

    vec = grads_d[:, 3 * width : 3 * width + 16].T
    return (
        output[None],
        activations_grad[None],
        vec[0],
        vec[1],
        columns(grads_d, 0, 3),
        columns(grads_c_two, 4, 1),
        vec[2],
        vec[3],
        vec[4],
        columns(grads_c, 4, 4),
        unfold(columns(grads_c, 0, 4)),
        vec[5],
        taps(columns(grads_c_two, 0, 4)),
        vec[6],
        grads_c_two[:, 5 * width :],
        grads_b[:, 7 * width :].T,
        taps(columns(grads_b, 3, 4)),
        vec[7],
        vec[8],
        vec[9],
        columns(grads_b, 0, 3),
        columns(grads_a, 8, 1),
        vec[10],
        vec[11],
        vec[12],
        columns(grads_a, 4, 4),
        unfold(columns(grads_a, 0, 4)),
        vec[13],
        new_cluster_size,
        new_embed_sum,
        new_codebook,
    )


def solution(mesh):
    grid = mesh.devices
    mesh = jax.sharding.Mesh(
        grid.reshape(grid.shape[0] // 2, 2, grid.shape[1] // 2, 2), ("hi", "lo", "x", "core")
    )
    placed = (
        P(DP, SEQ, None),
        P(SEQ),
        P(SEQ),
        P(SEQ, None),
        P(SEQ, None),
        P(SEQ),
        P(SEQ),
        P(SEQ),
        P(SEQ, None),
        P(SEQ, None),
        P(SEQ),
        P(None, SEQ, None),
        P(SEQ),
        P(SEQ, None),
        P(None, SEQ, None),
        P(None, SEQ),
        P(None, SEQ, None),
        P(SEQ),
        P(SEQ),
        P(SEQ),
        P(SEQ, None),
        P(SEQ, None),
        P(SEQ),
        P(SEQ),
        P(SEQ),
        P(SEQ, None),
        P(SEQ, None),
        P(SEQ),
        P(DP, SEQ, None),
        P(DP, None),
        P(DP, SEQ, None),
        P(),
        P(),
        P(None, DP + SEQ),
        P(None, DP + SEQ, None),
    )
    return jax.shard_map(
        local,
        mesh=mesh,
        in_specs=placed,
        out_specs=(
            P(DP, SEQ, None),
            P(DP, SEQ, None),
            P(DP + SEQ),
            P(DP + SEQ),
            P(DP + SEQ, None),
            P(DP + SEQ, None),
            P(DP + SEQ),
            P(DP + SEQ),
            P(DP + SEQ),
            P(DP + SEQ, None),
            P(DP + SEQ, None),
            P(DP + SEQ),
            P(None, DP + SEQ, None),
            P(DP + SEQ),
            P(DP + SEQ, None),
            P(None, DP + SEQ),
            P(None, DP + SEQ, None),
            P(DP + SEQ),
            P(DP + SEQ),
            P(DP + SEQ),
            P(DP + SEQ, None),
            P(DP + SEQ, None),
            P(DP + SEQ),
            P(DP + SEQ),
            P(DP + SEQ),
            P(DP + SEQ, None),
            P(DP + SEQ, None),
            P(DP + SEQ),
            P(None, DP + SEQ),
            P(None, DP + SEQ, None),
            P(None, DP + SEQ, None),
        ),
        check_vma=False,
    )
```

```python
from functools import partial

import jax
import jax.numpy as jnp
from jax import lax
from jax.experimental import pallas as pl
from jax.experimental.pallas import tpu as pltpu
from jax.sharding import PartitionSpec as P

HEADS = 8
HEAD_DIM = 64
CONTEXT = 250
HALO = 256
CODE_HALO = HALO // 2 + 16
EXTRA = 16
QUERIES = 64
GROUP = 4
WINDOW = HALO + QUERIES
VMEM_LIMIT = 26 * 1024 * 1024
ORDER_A = ("lo", "x", "hi")
ORDER_B = ("lo", "x", "hi")
ORDER_C_ONE = ("x", "lo", "hi")
ORDER_C_TWO = ("lo", "x", "hi")
ORDER_D = ("lo", "x", "hi")
DP = ("hi", "lo")
SEQ = ("x", "core")

norm_eps = 1e-05
ema_decay = 0.9
bf16 = jnp.bfloat16
f32 = jnp.float32


PIECES = 4


def fetch(sc_ref, pieces, at, width, dst, sems, first=0):
    copies = []
    for i, piece in enumerate(pieces):
        rows = piece.shape[0]
        row = pl.multiple_of(sc_ref[8 + i], 128)
        copies.append(
            pltpu.make_async_copy(
                piece.at[:, at : at + width], dst.at[pl.ds(row, rows), :], sems.at[first + i]
            )
        )
        copies[-1].start()
    return copies


def split_refs(refs, counts):
    groups = []
    for count in counts:
        groups.append(refs[:count])
        refs = refs[count:]
    return groups, refs


def wait_all(copies):
    for copy in copies:
        copy.wait()


def mm(a, b):
    return jnp.dot(a, b, preferred_element_type=f32)


def mm_nt(a, b):
    return lax.dot_general(a, b, (((1,), (1,)), ((), ())), preferred_element_type=f32)


def mm_tn(a, b):
    return lax.dot_general(a, b, (((0,), (0,)), ((), ())), preferred_element_type=f32)


def normalize(stream):
    center = stream - jnp.mean(stream, -1, keepdims=True)
    scaled = lax.rsqrt(jnp.mean(center * center, -1, keepdims=True) + norm_eps)
    return center * scaled, scaled


def norm_backward(upstream, normal, scaled, gain):
    inner = upstream * gain
    return scaled * (
        inner
        - jnp.mean(inner, -1, keepdims=True)
        - normal * jnp.mean(inner * normal, -1, keepdims=True)
    )


def column_sum(value):
    return jnp.sum(value, 0, keepdims=True)


def interleave(even, odd, scr):
    tiles, rows, _ = scr.shape
    for tile in range(tiles):
        cols = slice(tile * 128, (tile + 1) * 128)
        scr[tile, pl.ds(0, rows // 2, stride=2), :] = even[:, cols]
        scr[tile, pl.ds(1, rows // 2, stride=2), :] = odd[:, cols]
    return jnp.concatenate([scr[tile] for tile in range(tiles)], 1)


def split_rows(value, scr):
    tiles, rows, _ = scr.shape
    for tile in range(tiles):
        scr[tile] = value[:, tile * 128 : (tile + 1) * 128]
    even = [scr[tile, pl.ds(0, rows // 2, stride=2), :] for tile in range(tiles)]
    odd = [scr[tile, pl.ds(1, rows // 2, stride=2), :] for tile in range(tiles)]
    return jnp.concatenate(even, 1), jnp.concatenate(odd, 1)


def first_half():
    lane = lax.broadcasted_iota(jnp.int32, (1, 128), 1)
    return lane % HEAD_DIM < HEAD_DIM // 2


def rotate(tile, cos, sin):
    swapped = jnp.where(first_half(), pltpu.roll(tile, 96, 1), pltpu.roll(tile, 32, 1))
    return tile * cos + swapped * sin


def head_lanes():
    lane = lax.broadcasted_iota(jnp.int32, (1, GROUP * HEAD_DIM), 1) // HEAD_DIM
    return [(lane == head) for head in range(GROUP)]


def stack_heads(block, lanes):
    return jnp.concatenate([block * mask.astype(bf16) for mask in lanes], 0)


def unstack_heads(block, lanes):
    rows = block.shape[0] // GROUP
    out = block[:rows]
    for head in range(1, GROUP):
        out = jnp.where(lanes[head], block[head * rows : (head + 1) * rows], out)
    return out


def lowest_key(query, cut):
    low = jnp.maximum(query - (CONTEXT - 1), 0)
    return jnp.where(query >= cut, jnp.maximum(low, cut), low)


def attend(q_ref, k_ref, v_ref, att_ref, sc_ref, rows, first_query, first_key, keys, at_row):
    start, cut = sc_ref[0], sc_ref[1]
    query = start + first_query + lax.broadcasted_iota(jnp.int32, (rows, 1), 0)
    low = lowest_key(query, cut)
    key = start + first_key + lax.broadcasted_iota(jnp.int32, (rows, keys), 1)
    mask = (key <= query) & (key >= low)
    mask = jnp.concatenate([mask] * GROUP, 0)
    lanes = head_lanes()
    key_row = first_key + HALO
    for group in range(HEADS // GROUP):
        cols = slice(group * GROUP * HEAD_DIM, (group + 1) * GROUP * HEAD_DIM)
        stacked = stack_heads(q_ref[at_row : at_row + rows, cols], lanes)
        scores = mm_nt(stacked, k_ref[key_row : key_row + keys, cols]) * HEAD_DIM ** (-0.5)
        scores = jnp.where(mask, scores, -1e30)
        exponent = jnp.exp(scores - jnp.max(scores, -1, keepdims=True))
        weights = exponent * (1.0 / jnp.sum(exponent, -1, keepdims=True))
        mixed = mm(weights.astype(bf16), v_ref[key_row : key_row + keys, cols])
        att_ref[at_row : at_row + rows, cols] = unstack_heads(mixed, lanes).astype(bf16)


def front(x, vec_ref, base, w_in, cos_ref, sin_ref, sc_ref, n1_ref, q_ref, k_ref, v_ref, att_ref,
          extra):
    width = x.shape[1]
    normal, _ = normalize(x)
    low = (normal * vec_ref[base : base + 1] + vec_ref[base + 1 : base + 2]).astype(bf16)
    n1_ref[...] = low[HALO:]
    skip = HALO - extra
    queries = mm(low[skip:], w_in[:, :width])
    keys = mm(low, w_in[:, width : 2 * width])
    for at in range(0, width, 128):
        q_ref[:, at : at + 128] = rotate(
            queries[:, at : at + 128], cos_ref[skip:], sin_ref[skip:]
        ).astype(bf16)
        k_ref[:, at : at + 128] = rotate(keys[:, at : at + 128], cos_ref[...], sin_ref[...]).astype(
            bf16
        )
    v_ref[...] = mm(low, w_in[:, 2 * width :]).astype(bf16)
    frames = x.shape[0] - HALO
    if extra:
        attend(q_ref, k_ref, v_ref, att_ref, sc_ref, extra, -extra, -HALO, HALO, 0)
    for first in range(0, frames, QUERIES):
        attend(
            q_ref, k_ref, v_ref, att_ref, sc_ref, QUERIES, first, first - HALO, WINDOW,
            extra + first,
        )


def decoder_front_kernel(sc_ref, *refs):
    pieces, refs = refs[:PIECES], refs[PIECES:]
    (qz_ref, vec_ref, cos_ref, sin_ref, x_ref, restored_ref, n1_ref, q_ref, k_ref, v_ref, att_ref,
     w_vmem, x_scr, sems) = refs
    width = x_ref.shape[1]
    wait_all(fetch(sc_ref, pieces, 0, w_vmem.shape[1], w_vmem, sems))
    latent = qz_ref.shape[1]
    restored = mm_nt(qz_ref[...], w_vmem[:, :latent]).astype(bf16)
    restored_ref[...] = restored[CODE_HALO - 16 :]
    both = mm(restored, w_vmem[:, latent : latent + 4 * width])
    bias = vec_ref[7:8]
    now = both[16:, : 2 * width]
    before = pltpu.roll(both[:, 2 * width :], 1, 0)[16:]
    total = now + before
    x = interleave(total[:, :width] + bias, total[:, width:] + bias, x_scr)
    x_ref[...] = x[HALO:]
    w_in = w_vmem.at[:, latent + 4 * width :]
    front(x, vec_ref, 8, w_in, cos_ref, sin_ref, sc_ref, n1_ref, q_ref, k_ref, v_ref,
          att_ref, 0)


def encoder_front_kernel(sc_ref, *refs):
    (pieces,), refs = split_refs(refs, (PIECES,))
    (halo_ref, x_ref, vec_ref, cos_ref, sin_ref, n1_ref, q_ref, k_ref, v_ref, att_ref,
     w_vmem, sems) = refs
    width = x_ref.shape[1]
    copies = fetch(sc_ref, pieces, 0, 3 * width, w_vmem, sems)
    x = jnp.concatenate([halo_ref[...], x_ref[...]], 0).astype(f32)
    wait_all(copies)
    front(x, vec_ref, 0, w_vmem, cos_ref, sin_ref, sc_ref, n1_ref, q_ref, k_ref, v_ref, att_ref,
          EXTRA)


def gelu_both(hidden):
    share = 0.5 * (1.0 + lax.erf(hidden * 0.7071067811865476))
    density = jnp.exp(-0.5 * hidden * hidden) * 0.3989422804014327
    return hidden * share, share + hidden * density


def l2_rows(w, at, chunk, width):
    rows = width // 4
    return jnp.concatenate(
        [
            w[chunk * rows : (chunk + 1) * rows, at + g * width : at + (g + 1) * width]
            for g in range(4)
        ],
        0,
    )


def fetch_layer(sc_ref, groups, plan, width, w_vmem, sems):
    edges = (0, width, 5 * width, 9 * width)
    return [
        fetch(
            sc_ref, groups[plan[i][0]], plan[i][1], high - low, w_vmem.at[:, low:high], sems,
            PIECES * i,
        )
        for i, (low, high) in enumerate(zip(edges[:-1], edges[1:]))
    ]


def ff_forward(base, extra, copies, w_vmem, att_ref, stream, vec_ref, out_ref, n2_ref, active_ref,
               slope_ref, mid_ref, second_ref, h_scr, act_scr):
    rows, width = stream.shape
    scale_one = vec_ref[base + 2 : base + 3]
    gain_two = vec_ref[base + 3 : base + 4]
    bias_two = vec_ref[base + 4 : base + 5]
    scale_two = vec_ref[base + 5 : base + 6]
    wait_all(copies[0])
    middle = stream + scale_one * mm(att_ref[...], w_vmem[:, :width])
    mid_ref[...] = middle[extra:]
    normal, _ = normalize(middle)
    n2 = (normal * gain_two + bias_two).astype(bf16)
    n2_ref[...] = n2[extra:]
    wait_all(copies[1])
    l1_at, l2_at = width, 5 * width
    second = None
    for chunk in range(4):
        cols = slice(chunk * width, (chunk + 1) * width)
        h_scr[...] = mm(n2, w_vmem[:, l1_at + chunk * width : l1_at + (chunk + 1) * width])
        if extra:
            act, _ = gelu_both(h_scr[:extra, :])
            act_scr[:extra, cols] = act.astype(bf16)

        def body(i, _):
            at_row = pl.multiple_of(i * 16, 16)
            act, slope = gelu_both(h_scr[pl.ds(at_row + extra, 16), :])
            act_scr[pl.ds(at_row + extra, 16), cols] = act.astype(bf16)
            slope_ref[pl.ds(at_row, 16), cols] = slope
            return 0

        lax.fori_loop(0, (rows - extra) // 16, body, 0)
        if chunk == 0:
            wait_all(copies[2])
        part = mm(act_scr[:, cols], l2_rows(w_vmem, l2_at, chunk, width))
        second = part if second is None else second + part
    active_ref[...] = act_scr[extra:, :]
    second_ref[...] = second[extra:]
    out_ref[...] = (middle + scale_two * second).astype(bf16)


def ff_backward(base, extra, w_vmem, att_ref, g, vec_ref, slope_ref, mid_ref, second_ref, gmid_ref,
                dh_ref, dtwo_ref, done_ref, vg_ref, datt_scr):
    width = g.shape[1]
    scale_one = vec_ref[base + 2 : base + 3]
    gain_two = vec_ref[base + 3 : base + 4]
    scale_two = vec_ref[base + 5 : base + 6]
    l1_at, l2_at = width, 5 * width
    vg_ref[3:4, :] = column_sum(g * second_ref[...])
    d_two = (g * scale_two).astype(bf16)
    dtwo_ref[...] = d_two
    e = None
    for chunk in range(4):
        cols = slice(chunk * width, (chunk + 1) * width)
        d_active = mm_nt(d_two, l2_rows(w_vmem, l2_at, chunk, width))
        dh_ref[:, cols] = (d_active * slope_ref[:, cols]).astype(bf16)
        part = mm_nt(
            dh_ref[:, cols], w_vmem[:, l1_at + chunk * width : l1_at + (chunk + 1) * width]
        )
        e = part if e is None else e + part
    normal, scaled = normalize(mid_ref[...])
    vg_ref[1:2, :] = column_sum(e * normal)
    vg_ref[2:3, :] = column_sum(e)
    g_mid = g + norm_backward(e, normal, scaled, gain_two)
    gmid_ref[...] = g_mid
    vg_ref[0:1, :] = column_sum(g_mid * mm(att_ref[extra:, :], w_vmem[:, :width]))
    d_one = (g_mid * scale_one).astype(bf16)
    done_ref[...] = d_one
    datt_scr[...] = mm_nt(d_one, w_vmem[:, :width]).astype(bf16)


def decoder_layer_kernel(plan, sc_ref, *refs):
    (pieces,), refs = split_refs(refs, (PIECES,))
    (att_ref, x_ref, g_ref, vec_ref, q_ref, k_ref, v_ref,
     out_ref, n2_ref, active_ref, gmid_ref, dh_ref, dtwo_ref, done_ref, vg_ref,
     dq_ref, dk_ref, dv_ref, dkv_ref,
     w_vmem, h_scr, act_scr, slope_scr, mid_scr, second_scr, datt_scr, dk_scr, dv_scr, sems) = refs
    width = x_ref.shape[1]
    copies = fetch_layer(sc_ref, (pieces,), plan, width, w_vmem, sems)
    ff_forward(8, 0, copies, w_vmem, att_ref, x_ref[...], vec_ref, out_ref, n2_ref, active_ref,
               slope_scr, mid_scr, second_scr, h_scr, act_scr)
    ff_backward(8, 0, w_vmem, att_ref, g_ref[...].astype(f32), vec_ref, slope_scr, mid_scr,
                second_scr, gmid_ref, dh_ref, dtwo_ref, done_ref, vg_ref, datt_scr)
    attention_backward(0, sc_ref, q_ref, k_ref, v_ref, datt_scr, dq_ref, dk_ref, dv_ref, dkv_ref,
                       dk_scr, dv_scr)


def encoder_forward_kernel(plan, sc_ref, *refs):
    groups, refs = split_refs(refs, (PIECES, PIECES))
    (halo_ref, x_ref, att_ref, vec_ref,
     out_ref, n2_ref, active_ref, slope_ref, mid_ref, second_ref,
     w_vmem, h_scr, act_scr, sems) = refs
    width = x_ref.shape[1]
    copies = fetch_layer(sc_ref, groups, plan, width, w_vmem, sems)
    stream = jnp.concatenate([halo_ref[HALO - EXTRA :, :], x_ref[...]], 0).astype(f32)
    ff_forward(0, EXTRA, copies, w_vmem, att_ref, stream, vec_ref, out_ref, n2_ref, active_ref,
               slope_ref, mid_ref, second_ref, h_scr, act_scr)


def encoder_backward_kernel(plan, sc_ref, *refs):
    groups, refs = split_refs(refs, (PIECES, PIECES))
    (att_ref, g_ref, vec_ref, slope_ref, mid_ref, second_ref, q_ref, k_ref, v_ref,
     gmid_ref, dh_ref, dtwo_ref, done_ref, vg_ref, dq_ref, dk_ref, dv_ref, dkv_ref,
     w_vmem, datt_scr, dk_scr, dv_scr, sems) = refs
    width = g_ref.shape[1]
    for copies in fetch_layer(sc_ref, groups, plan, width, w_vmem, sems):
        wait_all(copies)
    ff_backward(0, EXTRA, w_vmem, att_ref, g_ref[...], vec_ref, slope_ref, mid_ref, second_ref,
                gmid_ref, dh_ref, dtwo_ref, done_ref, vg_ref, datt_scr)
    attention_backward(EXTRA, sc_ref, q_ref, k_ref, v_ref, datt_scr, dq_ref, dk_ref, dv_ref,
                       dkv_ref, dk_scr, dv_scr)


def attention_backward(extra, sc_ref, q_ref, k_ref, v_ref, do_ref,
                       dq_ref, dk_ref, dv_ref, dkv_ref, dk_scr, dv_scr):
    start, cut = sc_ref[0], sc_ref[1]
    frames = do_ref.shape[0]
    lanes = head_lanes()
    scale = HEAD_DIM ** (-0.5)
    dk_scr[...] = jnp.zeros_like(dk_scr)
    dv_scr[...] = jnp.zeros_like(dv_scr)
    wide = GROUP * QUERIES
    for first in range(0, frames, QUERIES):
        lane = lax.broadcasted_iota(jnp.int32, (1, wide), 1) % QUERIES
        query = start + first + lane
        low = lowest_key(query, cut)
        key = start + first - HALO + lax.broadcasted_iota(jnp.int32, (WINDOW, wide), 0)
        mask = (key <= query) & (key >= low)
        for group in range(HEADS // GROUP):
            cols = slice(group * GROUP * HEAD_DIM, (group + 1) * GROUP * HEAD_DIM)
            qs = stack_heads(q_ref[extra + first : extra + first + QUERIES, cols], lanes)
            ds = stack_heads(do_ref[first : first + QUERIES, cols], lanes)
            kw = k_ref[first : first + WINDOW, cols]
            vw = v_ref[first : first + WINDOW, cols]
            scores = jnp.where(mask, mm_nt(kw, qs) * scale, -1e30)
            exponent = jnp.exp(scores - jnp.max(scores, 0, keepdims=True))
            probs = exponent * (1.0 / jnp.sum(exponent, 0, keepdims=True))
            d_probs = mm_nt(vw, ds)
            mean = jnp.sum(probs * d_probs, 0, keepdims=True)
            d_scores = (probs * (d_probs - mean)).astype(bf16)
            dk_scr[first : first + WINDOW, cols] += mm(d_scores, qs)
            dv_scr[first : first + WINDOW, cols] += mm(probs.astype(bf16), ds)
            dq_ref[first : first + QUERIES, cols] = (
                unstack_heads(mm_tn(d_scores, kw), lanes) * scale
            )
    width = dq_ref.shape[1]
    dkv_ref[:, :width] = (dk_scr[:HALO] * scale).astype(bf16)
    dkv_ref[:, width:] = dv_scr[:HALO].astype(bf16)
    dk_ref[...] = dk_scr[HALO:] * scale
    dv_ref[...] = dv_scr[HALO:]


class Packer:
    def __init__(self, core, refs, shares, order):
        self.core, self.refs, self.shares, self.order = core, refs, shares, order

    def put(self, value, at, step=1, phase=0, block0=0):
        if len(self.refs) == 1:
            if step == 1:
                self.refs[0][:, at : at + value.shape[1]] = value.astype(bf16)
            return
        send, keep = self.refs
        cols = slice(at, at + value.shape[1])
        rows = 16
        hi = self.shares // 8
        blocks = value.shape[0] // (rows * step)
        for pair in range(blocks // 2):
            even = value[(2 * pair * step + phase) * rows :][:rows]
            odd = value[((2 * pair + 1) * step + phase) * rows :][:rows]
            block = (block0 + 2 * pair) // 2
            place = {"x": (block % 2, 2), "lo": (block // 2 % 2, 2), "hi": (block // 4, hi)}
            at_row = 0
            for axis in self.order:
                at_row = at_row * place[axis][1] + place[axis][0]
            at_row = at_row * rows
            first = self.core == 0
            keep[at_row : at_row + rows, cols] = jnp.where(first, even, odd).astype(bf16)
            send[at_row : at_row + rows, cols] = jnp.where(first, odd, even).astype(bf16)

    def put_l2(self, value, at, chunk, width):
        if len(self.refs) == 1:
            cols = slice(at + chunk * width, at + (chunk + 1) * width)
            self.refs[0][:, cols] = value.astype(bf16)
            return
        for phase in range(4):
            self.put(value, at + phase * width, 4, phase, chunk * width // 64)


def linear_gradients(pack, n2_ref, active_ref, dh_ref, dtwo_ref):
    width = n2_ref.shape[1]
    for chunk in range(4):
        cols = slice(chunk * width, (chunk + 1) * width)
        pack.put_l2(mm_tn(active_ref[:, cols], dtwo_ref[...]), 0, chunk, width)
        pack.put(mm_tn(n2_ref[...], dh_ref[:, cols]), (4 + chunk) * width)


def decoder_gradients_kernel(shares, sc_ref, n2_ref, active_ref, dh_ref, dtwo_ref, att_ref, done_ref,
                             *refs):
    pack = Packer(sc_ref[2], refs, shares, ORDER_A)
    linear_gradients(pack, n2_ref, active_ref, dh_ref, dtwo_ref)
    pack.put(mm_tn(att_ref[...], done_ref[...]), 8 * n2_ref.shape[1])


def encoder_gradients_kernel(shares, sc_ref, n2_ref, active_ref, dh_ref, dtwo_ref, att_ref, done_ref,
                             win_ref, dred_ref, red_ref, dlat_ref, *refs):
    width = n2_ref.shape[1]
    half = len(refs) // 2
    linear_gradients(
        Packer(sc_ref[2], refs[:half], shares, ORDER_C_ONE), n2_ref, active_ref, dh_ref, dtwo_ref
    )
    pack = Packer(sc_ref[2], refs[half:], shares, ORDER_C_TWO)
    d_reduced = dred_ref[...]
    for tap in range(4):
        pack.put(mm_tn(win_ref[tap], d_reduced), tap * width)
    pack.put(mm_tn(att_ref[EXTRA:, :], done_ref[...]), 4 * width)
    pack.put(mm_tn(red_ref[...], dlat_ref[...]), 5 * width)


def layer_input_gradient(base, dq_ref, dk_ref, dv_ref, dkv_ref, x, gmid_ref,
                         w_in, vec_ref, cos_ref, sin_ref, dmix_ref, vg_ref):
    frames, width = dq_ref.shape
    later = frames - HALO
    cos, sin = cos_ref[HALO:], -sin_ref[HALO:]
    for at in range(0, width, 128):
        cols = slice(at, at + 128)
        dmix_ref[:, cols] = rotate(dq_ref[:, cols], cos, sin).astype(bf16)
        keys = dk_ref[:, cols]
        keys = jnp.concatenate([keys[:later], keys[later:] + dkv_ref[:, cols].astype(f32)], 0)
        dmix_ref[:, width + at : width + at + 128] = rotate(keys, cos, sin).astype(bf16)
        values = dv_ref[:, cols]
        moved = dkv_ref[:, width + at : width + at + 128].astype(f32)
        values = jnp.concatenate([values[:later], values[later:] + moved], 0)
        dmix_ref[:, 2 * width + at : 2 * width + at + 128] = values.astype(bf16)
    d_normed = mm_nt(dmix_ref[...], w_in[...])
    normal, scaled = normalize(x)
    vg_ref[0:1, :] = column_sum(d_normed * normal)
    vg_ref[1:2, :] = column_sum(d_normed)
    return gmid_ref[...] + norm_backward(d_normed, normal, scaled, vec_ref[base : base + 1])


def decoder_back_kernel(at, sc_ref, *refs):
    pieces, refs = refs[:PIECES], refs[PIECES:]
    (dq_ref, dk_ref, dv_ref, dkv_ref, x_ref, gmid_ref, vec_ref, cos_ref, sin_ref,
     dup_ref, dmix_ref, vg_ref, w_vmem, sems) = refs
    wait_all(fetch(sc_ref, pieces, at, w_vmem.shape[1], w_vmem, sems))
    grad = layer_input_gradient(
        8, dq_ref, dk_ref, dv_ref, dkv_ref, x_ref[...], gmid_ref, w_vmem, vec_ref,
        cos_ref, sin_ref, dmix_ref, vg_ref,
    )
    vg_ref[2:3, :] = column_sum(grad)
    dup_ref[...] = grad.astype(bf16)


def encoder_back_kernel(shares, sc_ref, *refs):
    (pieces,), refs = split_refs(refs, (PIECES,))
    (dq_ref, dk_ref, dv_ref, dkv_ref, x_ref, gmid_ref, vec_ref, cos_ref, sin_ref, n1_ref,
     vgs_ref, grad_ref, *rest) = refs
    refs, (w_vmem, dmix_scr, vg_scr, all_scr, sems) = rest[:-5], rest[-5:]
    width = x_ref.shape[1]
    wait_all(fetch(sc_ref, pieces, 0, w_vmem.shape[1], w_vmem, sems))
    grad = layer_input_gradient(
        0, dq_ref, dk_ref, dv_ref, dkv_ref, x_ref[...].astype(f32), gmid_ref, w_vmem,
        vec_ref, cos_ref, sin_ref, dmix_scr, vg_scr,
    )
    grad_ref[...] = grad.astype(bf16)
    pack = Packer(sc_ref[2], refs, shares, ORDER_D)
    for part in range(3):
        cols = slice(part * width, (part + 1) * width)
        pack.put(mm_tn(n1_ref[...], dmix_scr[:, cols]), part * width)
    all_scr[...] = jnp.zeros_like(all_scr)
    all_scr[0:2, :] = vg_scr[0:2, :]
    all_scr[2:6, :] = vgs_ref[0:4, :]
    all_scr[6:7, :] = vgs_ref[16:17, :]
    all_scr[7:8, :] = vgs_ref[26:27, :]
    all_scr[8:10, :] = vgs_ref[24:26, :]
    all_scr[10:14, :] = vgs_ref[8:12, :]
    pack.put(all_scr[...].T, 3 * width)


def middle_kernel(shares, sc_ref, *refs):
    (pieces, more), refs = split_refs(refs, (PIECES, PIECES))
    (dup_ref, next_ref, dmix_ref, n1_ref, restored_ref, qz_ref,
     denc_ref, dred_ref, dlat_ref, vg_ref, *rest) = refs
    refs, (up_vmem, down_vmem, frame_scr, sems) = rest[:-4], rest[-4:]
    frames, width = dup_ref.shape
    latent = qz_ref.shape[1]
    codec = frames // 2
    copies = [
        fetch(sc_ref, pieces, 0, latent + 4 * width, up_vmem, sems),
        fetch(sc_ref, more, 4 * width, 4 * width + latent, down_vmem, sems, PIECES),
    ]
    pairs = codec + 16
    even, odd = split_rows(
        jnp.concatenate([dup_ref[...], next_ref[...]], 0).astype(f32), frame_scr
    )
    both = jnp.concatenate([even, odd], 1).astype(bf16)
    wait_all(copies[0])
    up = up_vmem[:, latent : latent + 4 * width]
    here = mm_nt(both, up[:, : 2 * width])
    later = mm_nt(both, up[:, 2 * width :])
    d_restored = (here + pltpu.roll(later, pairs - 1, 0)).astype(bf16)
    d_latent = mm(d_restored, up_vmem[:, :latent]).astype(bf16)
    wait_all(copies[1])
    d_reduced = mm_nt(d_latent, down_vmem[:, 4 * width :]).astype(bf16)
    dlat_ref[...] = d_latent[:codec]
    dred_ref[...] = d_reduced[:codec]
    vg_ref[0:1, :] = column_sum(d_reduced[:codec].astype(f32))
    taps = [mm_nt(d_reduced, down_vmem[:, tap * width : (tap + 1) * width]) for tap in range(4)]
    denc_ref[...] = interleave(
        taps[2] + pltpu.roll(taps[0], pairs - 1, 0),
        taps[3] + pltpu.roll(taps[1], pairs - 1, 0),
        frame_scr,
    )[:frames]

    pack = Packer(sc_ref[2], refs, shares, ORDER_B)
    for part in range(3):
        cols = slice(part * width, (part + 1) * width)
        pack.put(mm_tn(n1_ref[...], dmix_ref[:, cols]), part * width)
    restored = restored_ref[...]
    own_pairs = both[:codec]
    before = pltpu.roll(restored.astype(f32), 1, 0)[16:].astype(bf16)
    pack.put(mm_tn(restored[16:], own_pairs[:, :width]), 3 * width)
    pack.put(mm_tn(restored[16:], own_pairs[:, width:]), 4 * width)
    pack.put(mm_tn(before, own_pairs[:, :width]), 5 * width)
    pack.put(mm_tn(before, own_pairs[:, width:]), 6 * width)
    pack.put(mm_tn(d_restored[:codec], qz_ref[CODE_HALO:, :]), 7 * width)


def latent_kernel(sc_ref, *refs):
    (pieces,), refs = split_refs(refs, (PIECES,))
    (enc_ref, rows_ref, vec_ref, res_ref, win_ref, red_ref, w_vmem, frame_scr, sems) = refs
    total, width = enc_ref.shape
    copies = fetch(sc_ref, pieces, 4 * width, w_vmem.shape[1], w_vmem, sems)
    inside = (sc_ref[0] > 0).astype(f32)
    rim = enc_ref[:EXTRA].astype(f32) * inside
    skip = EXTRA // 2
    even, odd = split_rows(jnp.concatenate([rim, enc_ref[EXTRA:].astype(f32)], 0), frame_scr)
    win_ref[0] = pltpu.roll(even, 1, 0)[skip:].astype(bf16)
    win_ref[1] = pltpu.roll(odd, 1, 0)[skip:].astype(bf16)
    win_ref[2] = even[skip:].astype(bf16)
    win_ref[3] = odd[skip:].astype(bf16)
    wait_all(copies)
    reduced = vec_ref[6:7]
    for tap in range(4):
        reduced = reduced + mm(win_ref[tap], w_vmem[:, tap * width : (tap + 1) * width])
    reduced = reduced.astype(bf16)
    red_ref[...] = reduced
    remaining = mm(reduced, w_vmem[:, 4 * width :])
    for level in range(rows_ref.shape[0]):
        res_ref[level] = remaining.astype(bf16)
        remaining = remaining - rows_ref[level].astype(f32)


def lookup_kernel(sc_ref, codes_ref, book_ref, qsend_ref, qkeep_ref, rsend_ref, rkeep_ref, q_scr):
    levels, share, latent = book_ref.shape
    total = codes_ref.shape[0]
    codec = total // 4
    base = sc_ref[3]
    core = sc_ref[2]
    entry = lax.broadcasted_iota(jnp.int32, (1, share), 1)
    for level in range(levels):
        picks = (codes_ref[:, level : level + 1] - base == entry).astype(f32).astype(bf16)
        found = mm(picks, book_ref[level])
        q_scr[CODE_HALO:] = found if level == 0 else q_scr[CODE_HALO:] + found
        for x in range(2):
            even = found[(2 * x) * codec :][:codec]
            odd = found[(2 * x + 1) * codec :][:codec]
            rkeep_ref[x, level] = jnp.where(core == 0, even, odd).astype(bf16)
            rsend_ref[x, level] = jnp.where(core == 0, odd, even).astype(bf16)
    q_scr[:CODE_HALO] = jnp.zeros((CODE_HALO, latent), f32)
    for x in range(2):
        even = q_scr[(2 * x) * codec : (2 * x + 1) * codec + CODE_HALO]
        odd = q_scr[(2 * x + 1) * codec : (2 * x + 2) * codec + CODE_HALO]
        qkeep_ref[x] = jnp.where(core == 0, even, odd)
        qsend_ref[x] = jnp.where(core == 0, odd, even)


def collect_kernel(share, seq_count, sc_ref, own_ref, x_ref, core_ref, far_ref, codes_ref,
                   marked_ref, send_ref, keep_ref, row_scr, cnt_scr):
    levels, codec, latent = own_ref.shape
    total = codes_ref.shape[1]
    lo = sc_ref[4]
    high = send_ref.shape[0]
    frame = lax.broadcasted_iota(jnp.int32, (1, total), 1) + sc_ref[6]
    row = lax.broadcasted_iota(jnp.int32, (2 * high * share, 1), 0)
    entry = (row // share * seq_count + sc_ref[5]) * share + row % share
    ones = jnp.ones((16, total), bf16)
    for level in range(levels):
        marked = marked_ref[:, level : level + 1]
        used = (entry == codes_ref[level : level + 1, :]).astype(f32)
        placed = (marked // 2 == frame).astype(f32)
        select = jnp.where(marked % 2 == 1, placed, used).astype(bf16)
        for place, ref in enumerate((own_ref, x_ref, core_ref, far_ref)):
            at_row = pl.multiple_of(sc_ref[14 + place], 32)
            row_scr[pl.ds(at_row, codec), :] = ref[level]
        sums = mm(select, row_scr[...])
        cnt_scr[level : level + 1, :] = mm_nt(ones, used.astype(bf16))[0:1]
        at = slice(level * share, (level + 1) * share)
        for h in range(high):
            even = sums[(2 * h) * share :][:share]
            odd = sums[(2 * h + 1) * share :][:share]
            keep_ref[h, at, :] = jnp.where(lo == 0, even, odd).astype(bf16)
            send_ref[h, at, :] = jnp.where(lo == 0, odd, even).astype(bf16)
    counts = cnt_scr[...]
    upper = jnp.floor(counts * (1.0 / 128.0))
    digits = jnp.concatenate([upper, counts - 128.0 * upper], 0)
    tail = slice(levels * share, levels * share + 2 * levels)
    for h in range(high):
        even = digits[:, (2 * h) * share : (2 * h + 1) * share]
        odd = digits[:, (2 * h + 1) * share : (2 * h + 2) * share]
        keep_ref[h, tail, :] = jnp.zeros((2 * levels, latent), bf16)
        send_ref[h, tail, :] = jnp.zeros((2 * levels, latent), bf16)
        keep_ref[h, tail, :share] = jnp.where(lo == 0, even, odd).astype(bf16)
        send_ref[h, tail, :share] = jnp.where(lo == 0, odd, even).astype(bf16)


def call(kernel, outs, spaces, scratch, args, micros):
    where = {"s": pltpu.SMEM, "v": pltpu.VMEM, "h": pltpu.HBM}
    title = getattr(kernel, "func", kernel).__name__
    return pl.pallas_call(
        kernel,
        name=title,
        out_shape=outs,
        in_specs=[pl.BlockSpec(memory_space=where[space]) for space in spaces],
        out_specs=[pl.BlockSpec(memory_space=pltpu.VMEM) for _ in outs],
        scratch_shapes=scratch,
        compiler_params=pltpu.CompilerParams(vmem_limit_bytes=VMEM_LIMIT),
        cost_estimate=pl.CostEstimate(
            flops=int(micros * 1e6), bytes_accessed=1, transcendentals=0
        ),
    )(*args)


def shape(dims, dtype=f32):
    return jax.ShapeDtypeStruct(dims, dtype)


def pick(block, at):
    zero = jnp.zeros((), jnp.uint32)
    start = (at,) + (zero,) * (block.ndim - 1)
    return lax.dynamic_slice(block, start, (1,) + block.shape[1:])[0]


def halve(block, axis, index, after=None):
    sent = pick(block, index["other " + axis])
    kept = pick(block, index[axis])
    got = lax.ppermute(sent, axis, [(0, 1), (1, 0)])
    if after is not None:
        got, _ = tie(got, after)
    return (kept.astype(f32) + got.astype(f32)).astype(block.dtype)


def sum_by_permutes(block, index, after=None):
    count = block.shape[0]
    if count != 4:
        return sum_over_hi(block)
    total = pick(block, index["hi"]).astype(f32)
    for turn in range(1, count):
        sent = pick(block, index["hi ^ %d" % turn])
        got = lax.ppermute(sent, "hi", [(i, i ^ turn) for i in range(count)])
        if after is not None:
            got, _ = tie(got, after)
        total = total + got.astype(f32)
    return total


def swap_add(send, keep, axis, after=None):
    got = lax.ppermute(send, axis, [(0, 1), (1, 0)])
    if after is not None:
        got, _ = tie(got, after)
    return (keep.astype(f32) + got.astype(f32)).astype(keep.dtype)


def sum_over_hi(block):
    parts = lax.all_to_all(block, "hi", 0, 0, tiled=True)
    return jnp.sum(parts.astype(f32), 0)


def shifted(block, distance):
    devices = range(lax.axis_size(SEQ))
    route = [(i - distance, i) for i in devices if i - distance in devices]
    return lax.ppermute(block, SEQ, route)


def packed_outs(width_total, width, shares):
    if width // shares % 16 == 0:
        return [shape((width // 2, width_total), bf16)] * 2
    return [shape((width, width_total), bf16)]


def swap(block, axis):
    return lax.ppermute(block, axis, [(0, 1), (1, 0)])


def tie(*values):
    return lax.optimization_barrier(values)


def half_of(share, index):
    rows = share.shape[0] // 2
    zero = jnp.zeros((), jnp.uint32)
    return lax.dynamic_slice(share, (index["lo"] * rows, zero), (rows, share.shape[1]))


def both_halves(near, far, index):
    first = index["lo"] == 0
    return jnp.concatenate([jnp.where(first, near, far), jnp.where(first, far, near)], 0)


def unfolded_rows(block, shares, l2_at):
    width = block.shape[0]
    full = [block[:, l2_at + i * width : l2_at + (i + 1) * width] for i in range(4)]
    full = jnp.concatenate(full, 0).reshape(shares, 4, width // shares, width)
    full = full.transpose(0, 2, 1, 3).reshape(width, 4 * width)
    return jnp.concatenate([block[:, :l2_at], full, block[:, l2_at + 4 * width :]], 1)


def first_sum(parts, shares, order, index, l2_at=None):
    if len(parts) == 2:
        return swap_add(*parts, "core")
    (block,) = parts
    if l2_at is not None:
        block = unfolded_rows(block, shares, l2_at)
    width, total = block.shape
    block = block.reshape(shares // 8, 2, 2, 2, width // shares, total)
    block = halve(block.transpose(3, 0, 1, 2, 4, 5), "core", index)
    places = [("hi", "lo", "x").index(axis) for axis in order]
    return block.transpose(*places, 3, 4).reshape(width // 2, total)


def next_sum(block, axis, index, after=None):
    rows, total = block.shape
    return halve(block.reshape(2, rows // 2, total), axis, index, after)


def last_sum(block, high):
    return sum_over_hi(block.reshape(high, -1, block.shape[1]))


def local(
    activations,
    encoder_attention_norm_gain,
    encoder_attention_norm_bias,
    encoder_query_key_value_weight,
    encoder_attention_output_weight,
    encoder_attention_layer_scale,
    encoder_forward_norm_gain,
    encoder_forward_norm_bias,
    encoder_forward_input_weight,
    encoder_forward_output_weight,
    encoder_forward_layer_scale,
    strided_convolution_weight,
    strided_convolution_bias,
    quantizer_input_weight,
    codebook,
    quantizer_output_weight,
    transposed_convolution_weight,
    transposed_convolution_bias,
    decoder_attention_norm_gain,
    decoder_attention_norm_bias,
    decoder_query_key_value_weight,
    decoder_attention_output_weight,
    decoder_attention_layer_scale,
    decoder_forward_norm_gain,
    decoder_forward_norm_bias,
    decoder_forward_input_weight,
    decoder_forward_output_weight,
    decoder_forward_layer_scale,
    cotangent,
    frame_segment_index,
    frame_code_index,
    replace_code_mask,
    replacing_batch_position,
    code_usage_average,
    code_latent_sum_average,
):
    batch_rows, frames, width = activations.shape
    assert batch_rows == 1
    seq_index = lax.axis_index(SEQ)
    seq_count = lax.axis_size(SEQ)
    dp_index = lax.axis_index(DP)
    dp_count = lax.axis_size(DP)
    shares = dp_count * seq_count
    codec = frames // 2
    levels = frame_code_index.shape[2]
    latent = codebook.shape[2]
    book_share = codebook.shape[1]
    core_index = lax.axis_index("core")

    x_index, lo_index = lax.axis_index("x"), lax.axis_index("lo")
    rows_share = width // seq_count
    high = shares // 8
    total_frames = HALO + frames
    code_total = replace_code_mask.shape[1]
    code_share = code_usage_average.shape[1]
    row_frames = codec * seq_count

    vectors = jnp.stack(
        [
            encoder_attention_norm_gain,
            encoder_attention_norm_bias,
            encoder_attention_layer_scale,
            encoder_forward_norm_gain,
            encoder_forward_norm_bias,
            encoder_forward_layer_scale,
            strided_convolution_bias,
            transposed_convolution_bias,
            decoder_attention_norm_gain,
            decoder_attention_norm_bias,
            decoder_attention_layer_scale,
            decoder_forward_norm_gain,
            decoder_forward_norm_bias,
            decoder_forward_layer_scale,
        ]
    )
    vectors = jnp.pad(vectors, ((0, 2), (0, 0)))
    small = jnp.concatenate(
        [frame_code_index.reshape(-1).astype(f32), vectors.reshape(-1).astype(f32)]
    )
    index = {}
    unsigned = jnp.uint32
    for axis in ("x", "lo", "core"):
        index[axis] = lax.axis_index(axis).astype(unsigned)
        index["other " + axis] = (1 - lax.axis_index(axis)).astype(unsigned)
    index["hi"] = lax.axis_index("hi").astype(unsigned)
    index["seq"] = lax.axis_index(SEQ).astype(unsigned)
    index["owner"] = (lax.axis_index(DP + SEQ) * code_share).astype(unsigned)
    for turn in range(1, 4):
        index["hi ^ %d" % turn] = lax.axis_index("hi").astype(unsigned) ^ unsigned(turn)
    def flat_taps(taps):
        return taps.transpose(1, 0, 2).reshape(taps.shape[1], -1)

    def fold_l2(share):
        return share.reshape(4, -1, width).transpose(1, 0, 2).reshape(-1, 4 * width)

    dec_one = jnp.concatenate(
        [
            quantizer_output_weight.T,
            flat_taps(transposed_convolution_weight),
            decoder_query_key_value_weight,
        ],
        1,
    )
    half_one = half_of(dec_one, index)
    small, half_one = tie(small, half_one)
    small = lax.all_gather(small, SEQ, axis=0, tiled=False)
    names = sorted(index)
    *index_values, small = tie(*[index[name] for name in names], small)
    index = dict(zip(names, index_values))
    code_count = codec * levels
    row_codes = small[:, :code_count].astype(jnp.int32).reshape(seq_count, codec, levels)
    vectors = small[:, code_count:].reshape(seq_count, 16, -1).transpose(1, 0, 2).reshape(16, width)
    order = [2 * x_index + core_index, 2 * (1 - x_index) + core_index]
    order += [2 * x_index + 1 - core_index, 2 * (1 - x_index) + 1 - core_index]
    cut = jnp.sum((frame_segment_index[0] == 0).astype(jnp.int32))
    scalars = jnp.stack(
        [
            seq_index * frames,
            cut,
            core_index,
            seq_index * book_share,
            lo_index,
            seq_index,
            dp_index * row_frames,
            seq_index,
        ]
        + [
            *[place * rows_share for place in order],
            seq_index,
            seq_index,
        ]
        + [place * codec for place in order]
    ).astype(jnp.int32)

    half_one, _ = tie(half_one, small)
    near_one = swap(half_one, "x")
    core_one = swap(dec_one, "core")
    activation_halo = shifted(activations[0, frames - HALO :], 1)

    positions = seq_index * frames - HALO + jnp.arange(total_frames, dtype=jnp.int32)
    half_dim = HEAD_DIM // 2
    frequency = jnp.power(10000.0, -jnp.arange(half_dim, dtype=f32) / half_dim)

    def angle_tables(positions):
        angles = positions.astype(f32)[:, None] * frequency[None, :]
        cos, sin = jnp.cos(angles), jnp.sin(angles)
        return jnp.concatenate([cos] * 4, 1), jnp.concatenate([-sin, sin, -sin, sin], 1)

    row_codes, activation_halo, core_one = tie(row_codes, activation_halo, core_one)

    window = codec + CODE_HALO
    qsend, qkeep, rsend, rkeep = call(
        lookup_kernel,
        [shape((2, window, latent))] * 2 + [shape((2, levels, codec, latent), bf16)] * 2,
        "svv",
        [pltpu.VMEM((CODE_HALO + codec * seq_count, latent), f32)],
        (scalars, row_codes.reshape(-1, levels), codebook),
        4,
    )
    q_sum = swap_add(qsend, qkeep, "core")
    q_sent = pick(q_sum, index["other x"])
    q_got = swap(q_sent, "x")
    (near_one, positions, dec_l2, enc_in, enc_l2, down_share, replace_code_mask,
     replacing_batch_position, row_codes, _) = tie(
        near_one, positions, decoder_forward_output_weight, encoder_query_key_value_weight,
        encoder_forward_output_weight, strided_convolution_weight, replace_code_mask,
        replacing_batch_position, row_codes, q_sent,
    )
    dec_two = jnp.concatenate(
        [decoder_attention_output_weight, decoder_forward_input_weight, fold_l2(dec_l2)], 1
    )
    enc_one = jnp.concatenate(
        [
            enc_in,
            encoder_attention_output_weight,
            flat_taps(down_share),
            quantizer_input_weight,
        ],
        1,
    )
    marked = (replacing_batch_position * 2 + replace_code_mask).T
    marked = marked.reshape(dp_count, seq_count, code_share, levels).transpose(1, 0, 2, 3)
    marked = pick(marked, index["seq"]).reshape(dp_count * code_share, levels)
    code_columns = row_codes.reshape(row_frames, levels).T
    owner_flag = lax.dynamic_slice(
        replace_code_mask, (jnp.zeros((), unsigned), index["owner"]), (levels, code_share)
    ) == 1
    far_one = swap(near_one, "lo")
    near_one = both_halves(near_one, far_one, index)
    dec_one = [dec_one, near_one, core_one, swap(near_one, "core")]
    half_two = half_of(dec_two, index)
    cos_table, sin_table = angle_tables(positions)
    near_two = swap(half_two, "x")
    quantized = (pick(q_sum, index["x"]) + q_got).astype(bf16)
    half_three = half_of(enc_one, index)
    (quantized, near_two, half_three, activation_halo, cos_table, sin_table, marked,
     code_columns, owner_flag) = tie(
        quantized, near_two, half_three, activation_halo, cos_table, sin_table, marked,
        code_columns, owner_flag,
    )
    core_two = swap(dec_two, "core")
    far_two = swap(near_two, "lo")
    near_three = swap(half_three, "x")

    d_x, restored, d_n1, d_q, d_k, d_v, d_att = call(
        decoder_front_kernel,
        [
            shape((frames, width)),
            shape((codec + 16, width), bf16),
            shape((frames, width), bf16),
            shape((frames, width), bf16),
            shape((total_frames, width), bf16),
            shape((total_frames, width), bf16),
            shape((frames, width), bf16),
        ],
        "s" + "h" * PIECES + "vvvv",
        [
            pltpu.VMEM((width, latent + 7 * width), bf16),
            pltpu.VMEM((width // 128, total_frames, 128), f32),
            pltpu.SemaphoreType.DMA((PIECES,)),
        ],
        (scalars, *dec_one, quantized, vectors, cos_table, sin_table),
        8,
    )
    d_att, far_two, near_three, enc_l2, rsend = tie(d_att, far_two, near_three, enc_l2, rsend)
    enc_two = jnp.concatenate([encoder_forward_input_weight, fold_l2(enc_l2)], 1)
    half_four = half_of(enc_two, index)
    code_rows = swap_add(rsend, rkeep, "core")
    near_two = both_halves(near_two, far_two, index)
    dec_two = [dec_two, near_two, core_two, swap(near_two, "core")]
    far_three = swap(near_three, "lo")
    near_four = swap(half_four, "x")
    layer_scratch = [
        pltpu.VMEM((frames, width), bf16),
        pltpu.VMEM((total_frames, width), f32),
        pltpu.VMEM((total_frames, width), f32),
        pltpu.SemaphoreType.DMA((3 * PIECES,)),
    ]
    forward_outs = [shape((frames, width), bf16), shape((frames, 4 * width), bf16)]
    kept_outs = [shape((frames, 4 * width)), shape((frames, width)), shape((frames, width))]
    backward_outs = [
        shape((frames, width)),
        shape((frames, 4 * width), bf16),
        shape((frames, width), bf16),
        shape((frames, width), bf16),
        shape((8, width)),
        shape((frames, width)),
        shape((frames, width)),
        shape((frames, width)),
        shape((HALO, 2 * width), bf16),
    ]
    weights_scratch = pltpu.VMEM((width, 9 * width), bf16)
    (output, d_n2, d_active, d_gmid, d_dh, d_dtwo, d_done, d_vg_two, d_dq, d_dk, d_dv, d_dkv) = call(
        partial(decoder_layer_kernel, ((0, 0), (0, width), (0, 5 * width))),
        [shape((frames, width), bf16)] + forward_outs + backward_outs,
        "s" + "h" * PIECES + "vvvvvvv",
        [
            weights_scratch,
            pltpu.VMEM((frames, width), f32),
            pltpu.VMEM((frames, 4 * width), bf16),
            pltpu.VMEM((frames, 4 * width), f32),
            pltpu.VMEM((frames, width), f32),
            pltpu.VMEM((frames, width), f32),
        ]
        + layer_scratch,
        (scalars, *dec_two, d_att, d_x, cotangent[0], vectors, d_q, d_k, d_v),
        14,
    )
    d_n2, far_three, near_four, code_rows = tie(d_n2, far_three, near_four, code_rows)
    near_three = both_halves(near_three, far_three, index)
    enc_one = [enc_one, near_three, swap(enc_one, "core"), swap(near_three, "core")]
    far_four = swap(near_four, "lo")
    d_dkv = shifted(d_dkv, -1)
    group_a = call(
        partial(decoder_gradients_kernel, shares),
        packed_outs(9 * width, width, shares),
        "svvvvvv",
        [],
        (scalars, d_n2, d_active, d_dh, d_dtwo, d_att, d_done),
        5,
    )
    d_dq, *group_a = tie(d_dq, *group_a)
    code_rows, d_dkv = tie(code_rows, d_dkv)
    code_rows = halve(code_rows, "x", index)
    a_sum = first_sum(group_a, shares, ORDER_A, index, 0)
    d_up, d_mixed, d_vg_one = call(
        partial(decoder_back_kernel, latent + 4 * width),
        [shape((frames, width), bf16), shape((frames, 3 * width), bf16), shape((8, width))],
        "s" + "h" * PIECES + "v" * 9,
        [pltpu.VMEM((width, 3 * width), bf16), pltpu.SemaphoreType.DMA((PIECES,))],
        (
            scalars, *dec_one, d_dq, d_dk, d_dv, d_dkv, d_x, d_gmid, vectors, cos_table,
            sin_table,
        ),
        4,
    )
    d_up_next = shifted(d_up[:32], -1)


    a_sum, d_up, e_input, far_four, code_rows = tie(
        a_sum, d_up, activations[0], far_four, code_rows
    )
    near_four = both_halves(near_four, far_four, index)
    enc_two = [enc_two, near_four, swap(enc_two, "core"), swap(near_four, "core")]
    a_sum = next_sum(a_sum, ORDER_A[0], index)
    e_n1, e_q, e_k, e_v, e_att = call(
        encoder_front_kernel,
        [
            shape((frames, width), bf16),
            shape((frames + EXTRA, width), bf16),
            shape((total_frames, width), bf16),
            shape((total_frames, width), bf16),
            shape((frames + EXTRA, width), bf16),
        ],
        "s" + "h" * PIECES + "vvvvv",
        [pltpu.VMEM((width, 3 * width), bf16), pltpu.SemaphoreType.DMA((PIECES,))],
        (scalars, *enc_one, activation_halo, e_input, vectors, cos_table, sin_table),
        7,
    )

    d_mixed, e_n1 = tie(d_mixed, e_n1)
    middle_outs = call(
        partial(middle_kernel, shares),
        [
            shape((frames, width)),
            shape((codec, width), bf16),
            shape((codec, latent), bf16),
            shape((8, width)),
        ]
        + packed_outs(7 * width + latent, width, shares),
        "s" + "h" * (2 * PIECES) + "" + "v" * 6,
        [
            pltpu.VMEM((width, latent + 4 * width), bf16),
            pltpu.VMEM((width, latent + 4 * width), bf16),
            pltpu.VMEM((width // 128, frames + 32, 128), f32),
            pltpu.SemaphoreType.DMA((2 * PIECES,)),
        ],
        (scalars, *dec_one, *enc_one, d_up, d_up_next, d_mixed, d_n1, restored, quantized),
        7,
    )
    d_encoded, d_reduced, d_latent, m_vg = middle_outs[:4]
    b_sum = first_sum(middle_outs[4:], shares, ORDER_B, index)

    e_att, d_encoded = tie(e_att, d_encoded)
    enc_plan = ((0, 3 * width), (1, 0), (1, 4 * width))
    rows = frames + EXTRA
    encoded, e_n2, e_active, e_slope, e_mid, e_second = call(
        partial(encoder_forward_kernel, enc_plan),
        [shape((rows, width), bf16)] + forward_outs + kept_outs,
        "s" + "h" * (2 * PIECES) + "vvvv",
        [
            weights_scratch,
            pltpu.VMEM((rows, width), f32),
            pltpu.VMEM((rows, 4 * width), bf16),
            pltpu.SemaphoreType.DMA((3 * PIECES,)),
        ],
        (scalars, *enc_one, *enc_two, activation_halo, e_input, e_att, vectors),
        6,
    )
    encoded, b_sum, a_sum = tie(encoded, b_sum, a_sum)
    b_sum = next_sum(b_sum, ORDER_B[0], index)
    residuals, windows, reduced = call(
        latent_kernel,
        [
            shape((levels, codec, latent), bf16),
            shape((4, codec, width), bf16),
            shape((codec, width), bf16),
        ],
        "s" + "h" * PIECES + "vvv",
        [
            pltpu.VMEM((width, 4 * width + latent), bf16),
            pltpu.VMEM((width // 128, frames + EXTRA, 128), f32),
            pltpu.SemaphoreType.DMA((PIECES,)),
        ],
        (scalars, *enc_one, encoded, code_rows, vectors),
        3,
    )
    near_res = swap(residuals, "x")
    core_res = swap(residuals, "core")

    d_encoded, _ = tie(d_encoded, residuals)
    a_sum = next_sum(a_sum, ORDER_A[1], index)
    (e_gmid, e_dh, e_dtwo, e_done, e_vg_two, e_dq, e_dk, e_dv, e_dkv) = call(
        partial(encoder_backward_kernel, enc_plan),
        backward_outs,
        "s" + "h" * (2 * PIECES) + "v" * 9,
        [weights_scratch] + layer_scratch,
        (
            scalars, *enc_one, *enc_two, e_att, d_encoded, vectors, e_slope, e_mid, e_second,
            e_q, e_k, e_v,
        ),
        11,
    )
    e_dkv = shifted(e_dkv, -1)
    near_res, core_res, _ = tie(near_res, core_res, e_gmid)
    res_pieces = [residuals, near_res, core_res, swap(near_res, "core")]

    code_columns, b_sum = tie(code_columns, b_sum)
    if code_share % 16 == 0:
        tail_rows = levels * code_share
        csend, ckeep = call(
            partial(collect_kernel, code_share, seq_count),
            [shape((dp_count // 2, tail_rows + 2 * levels, latent), bf16)] * 2,
            "svvvvvv",
            [
                pltpu.VMEM((row_frames, latent), bf16),
                pltpu.VMEM((levels, dp_count * code_share), f32),
            ],
            (scalars, *res_pieces, code_columns, marked),
            5,
        )
        e_n2, csend, e_gmid, e_dkv = tie(e_n2, csend, e_gmid, e_dkv)
    c_outs = packed_outs(8 * width, width, shares)
    group_c = call(
        partial(encoder_gradients_kernel, shares),
        c_outs + packed_outs(5 * width + latent, width, shares),
        "s" + "v" * 10,
        [],
        (
            scalars, e_n2, e_active, e_dh, e_dtwo, e_att, e_done, windows, d_reduced, reduced,
            d_latent,
        ),
        5,
    )
    e_dq, *group_c = tie(e_dq, *group_c)
    c_one = first_sum(group_c[: len(c_outs)], shares, ORDER_C_ONE, index, 0)
    c_two = first_sum(group_c[len(c_outs) :], shares, ORDER_C_TWO, index)
    e_dq, c_one, c_two, a_sum, b_sum = tie(e_dq, c_one, c_two, a_sum, b_sum)
    vector_grads = jnp.concatenate([e_vg_two, d_vg_two, m_vg, d_vg_one], 0)
    grad_outs = call(
        partial(encoder_back_kernel, shares),
        [shape((frames, width), bf16)] + packed_outs(3 * width + 128, width, shares),
        "s" + "h" * PIECES + "v" * 11,
        [
            pltpu.VMEM((width, 3 * width), bf16),
            pltpu.VMEM((frames, 3 * width), bf16),
            pltpu.VMEM((8, width), f32),
            pltpu.VMEM((128, width), f32),
            pltpu.SemaphoreType.DMA((PIECES,)),
        ],
        (
            scalars, *enc_one, e_dq, e_dk, e_dv, e_dkv, e_input, e_gmid, vectors,
            cos_table, sin_table, e_n1, vector_grads,
        ),
        5,
    )
    activations_grad = grad_outs[0]

    def z_sum(block):
        return sum_by_permutes(block.reshape(high, -1, block.shape[1]), index, activations_grad)

    d_sum = first_sum(grad_outs[1:], shares, ORDER_D, index)
    b_sum = next_sum(b_sum, ORDER_B[1], index, d_sum)
    if code_share % 16 == 0:
        combined = swap_add(csend, ckeep, "lo", b_sum)
        c_one = next_sum(c_one, ORDER_C_ONE[0], index, combined)
        together = last_sum(jnp.concatenate([a_sum, b_sum], 1), high)
        combined = sum_by_permutes(combined, index)
        summed = combined[:tail_rows].reshape(levels, code_share, latent)
        digits = combined[tail_rows:, :code_share]
        counted = 128.0 * digits[:levels] + digits[levels:]
    else:
        entry = (
            jnp.arange(dp_count, dtype=jnp.int32)[:, None] * seq_count + seq_index
        ) * code_share + jnp.arange(code_share, dtype=jnp.int32)
        relative = [place * codec + jnp.arange(codec, dtype=jnp.int32) for place in order]
        relative = jnp.concatenate(relative)
        flat_res = jnp.concatenate(res_pieces, 1)
        used = entry.reshape(1, -1, 1) == code_columns[:, None, relative]
        placed = (marked.T // 2)[:, :, None] == dp_index * row_frames + relative
        counts = jnp.sum(used.astype(f32), 2).reshape(levels, dp_count, code_share)
        selects = jnp.where((marked.T % 2)[:, :, None] == 1, placed, used).astype(bf16)
        sums = jnp.einsum("lct,ltd->lcd", selects, flat_res, preferred_element_type=f32)
        sums = sums.astype(bf16).reshape(levels, dp_count, code_share, latent)
        together = last_sum(jnp.concatenate([a_sum, b_sum], 1), high)
        c_one = next_sum(c_one, ORDER_C_ONE[0], index)
        summed = lax.psum_scatter(sums, DP, scatter_dimension=1, tiled=False).astype(f32)
        counted = lax.psum_scatter(counts, DP, scatter_dimension=1, tiled=False)
    c_two = next_sum(c_two, ORDER_C_TWO[0], index, c_one)
    d_sum = next_sum(d_sum, ORDER_D[0], index, c_two)
    c_two = next_sum(
        c_two, ORDER_C_TWO[1], index, combined if code_share % 16 == 0 else d_sum
    )
    d_sum = next_sum(d_sum, ORDER_D[1], index, c_two)
    c_one = next_sum(c_one, ORDER_C_ONE[1], index, d_sum)
    grads_a, grads_b = together[:, : a_sum.shape[1]], together[:, a_sum.shape[1] :]
    edge, far_edge = c_one.shape[1], c_one.shape[1] + c_two.shape[1]
    together = last_sum(jnp.concatenate([c_one, c_two, d_sum], 1), high)
    grads_c, grads_c_two, grads_d = (
        together[:, :edge], together[:, edge:far_edge], together[:, far_edge:]
    )

    new_cluster_size = ema_decay * code_usage_average + (1.0 - ema_decay) * counted
    new_embed_sum = jnp.where(
        owner_flag[:, :, None],
        summed * new_cluster_size[:, :, None],
        ema_decay * code_latent_sum_average + (1.0 - ema_decay) * summed,
    )
    new_codebook = new_embed_sum / new_cluster_size[:, :, None]

    def columns(block, at, count):
        return block[:, at * width : (at + count) * width]

    def taps(block):
        return block.reshape(-1, 4, width).transpose(1, 0, 2)

    def unfold(block):
        return block.reshape(-1, 4, width).transpose(1, 0, 2).reshape(-1, width)

    vec = grads_d[:, 3 * width : 3 * width + 16].T
    return (
        output[None],
        activations_grad[None],
        vec[0],
        vec[1],
        columns(grads_d, 0, 3),
        columns(grads_c_two, 4, 1),
        vec[2],
        vec[3],
        vec[4],
        columns(grads_c, 4, 4),
        unfold(columns(grads_c, 0, 4)),
        vec[5],
        taps(columns(grads_c_two, 0, 4)),
        vec[6],
        grads_c_two[:, 5 * width :],
        grads_b[:, 7 * width :].T,
        taps(columns(grads_b, 3, 4)),
        vec[7],
        vec[8],
        vec[9],
        columns(grads_b, 0, 3),
        columns(grads_a, 8, 1),
        vec[10],
        vec[11],
        vec[12],
        columns(grads_a, 4, 4),
        unfold(columns(grads_a, 0, 4)),
        vec[13],
        new_cluster_size,
        new_embed_sum,
        new_codebook,
    )


def solution(mesh):
    grid = mesh.devices
    mesh = jax.sharding.Mesh(
        grid.reshape(grid.shape[0] // 2, 2, grid.shape[1] // 2, 2), ("hi", "lo", "x", "core")
    )
    placed = (
        P(DP, SEQ, None),
        P(SEQ),
        P(SEQ),
        P(SEQ, None),
        P(SEQ, None),
        P(SEQ),
        P(SEQ),
        P(SEQ),
        P(SEQ, None),
        P(SEQ, None),
        P(SEQ),
        P(None, SEQ, None),
        P(SEQ),
        P(SEQ, None),
        P(None, SEQ, None),
        P(None, SEQ),
        P(None, SEQ, None),
        P(SEQ),
        P(SEQ),
        P(SEQ),
        P(SEQ, None),
        P(SEQ, None),
        P(SEQ),
        P(SEQ),
        P(SEQ),
        P(SEQ, None),
        P(SEQ, None),
        P(SEQ),
        P(DP, SEQ, None),
        P(DP, None),
        P(DP, SEQ, None),
        P(),
        P(),
        P(None, DP + SEQ),
        P(None, DP + SEQ, None),
    )
    return jax.shard_map(
        local,
        mesh=mesh,
        in_specs=placed,
        out_specs=(
            P(DP, SEQ, None),
            P(DP, SEQ, None),
            P(DP + SEQ),
            P(DP + SEQ),
            P(DP + SEQ, None),
            P(DP + SEQ, None),
            P(DP + SEQ),
            P(DP + SEQ),
            P(DP + SEQ),
            P(DP + SEQ, None),
            P(DP + SEQ, None),
            P(DP + SEQ),
            P(None, DP + SEQ, None),
            P(DP + SEQ),
            P(DP + SEQ, None),
            P(None, DP + SEQ),
            P(None, DP + SEQ, None),
            P(DP + SEQ),
            P(DP + SEQ),
            P(DP + SEQ),
            P(DP + SEQ, None),
            P(DP + SEQ, None),
            P(DP + SEQ),
            P(DP + SEQ),
            P(DP + SEQ),
            P(DP + SEQ, None),
            P(DP + SEQ, None),
            P(DP + SEQ),
            P(None, DP + SEQ),
            P(None, DP + SEQ, None),
            P(None, DP + SEQ, None),
        ),
        check_vma=False,
    )
```
